32 devices in a mesh: wide: 8 (over z, x), seq: 4 (over y, core).
Axes of the slice: x: 2, y: 2, z: 4, core: 2. Of those that a mesh axis runs over, the one named last changes fastest.
Arguments:
- tokens: bfloat16 [8, 2048, 2304], P('seq', 'wide'), may hold values from -6 to 6
- cotangent: bfloat16 [8, 2048, 2304], P('seq', 'wide'), may hold values from -6 to 6
- widths: int32 [8], P('seq'), may hold values from 0 to 2
- attn_codes: int32 [2304, 6144], P('wide'), may hold values from -128 to 127
- attn_exps: int32 [4096], replicated, may hold values from 11 to 13
- out_exps: int32 [2304], replicated, may hold values from 11 to 13
- mlp_codes: int32 [3, 9216, 2304], P(None, 'wide'), may hold values from -128 to 127
- gate_exps: int32 [2, 9216], replicated, may hold values from 11 to 13
- down_exps: int32 [2304], replicated, may hold values from 12 to 14
- gain_attn: float32 [2304], replicated, may hold values from 0.25 to 1.75
- gain_post_attn: float32 [2304], replicated, may hold values from 0.25 to 1.75
- gain_mlp: float32 [2304], replicated, may hold values from 0.25 to 1.75
- gain_post_mlp: float32 [2304], replicated, may hold values from 0.25 to 1.75
Outputs:
- layer_out: bfloat16 [8, 2048, 2304], P('seq', 'wide')
- grad_tokens: bfloat16 [8, 2048, 2304], P('seq', 'wide')
- grad_attn_weights: float32 [2304, 6144], P('wide')
- grad_mlp_weights: float32 [3, 9216, 2304], P(None, 'wide')
- grad_gain_attn: float32 [2304], replicated
- grad_gain_post_attn: float32 [2304], replicated
- grad_gain_mlp: float32 [2304], replicated
- grad_gain_post_mlp: float32 [2304], replicated
The draws below stay inside these ranges and needn't reach their ends.
All inputs are finite; a program needn't handle non-finite values.
Results may differ from the reference program's by a relative error of at most 0.024.
The reference program's roundings to bfloat16 on the way count: a program that leaves them out, or rounds other values in their place, can miss the bound.
Values may be sent and summed in bfloat16 or wider, within the bound.
No kernel may reach another device: no remote copies, remote signals or barrier semaphores. Data moves between devices by JAX's collectives and lax.ppermute only.
A program may use at most 576 MiB of HBM per device.

```python
import math
import jax
import jax.numpy as jnp
from jax import lax

D = 2304
QUERY_HEADS = 8
KEY_VALUE_HEADS = 4
HEAD_SIZE = 256
FF = 9216
SEQUENCE_LENGTH = 2048
SEQS = 8
QKV = 4096
QKVO = 6144


def plant(entries, key, low, high):
    index_at = [jax.random.randint(jax.random.fold_in(key, axis), (), 0, length) for axis, length in enumerate(entries.shape)]
    longest = entries.shape.index(max(entries.shape))
    next_to = index_at[:longest] + [(index_at[longest] + 1) % entries.shape[longest]] + index_at[longest + 1:]
    return entries.at[tuple(index_at)].set(low).at[tuple(next_to)].set(high)


def level_of(own_key, dims, cuts, low, largest):
    def one(dim, blocks):
        draws = jax.random.uniform(jax.random.fold_in(jax.random.fold_in(own_key, 6), dim), (blocks,), jnp.float32, low / len(cuts), largest / len(cuts))
        return jnp.repeat(jnp.exp(draws), dims[dim] // blocks).reshape((-1,) + (1,) * (len(dims) - dim - 1))

    factor_of = one(*cuts[0])
    for cut in cuts[1:]:
        factor_of = factor_of * one(*cut)
    return factor_of


def normal_values(stream_key, shape, deviation, limit, split=(), held_as=jnp.bfloat16):
    factor_of = level_of(stream_key, shape, split, -0.22, 0.18) if split else 1.0
    result = jax.random.normal(stream_key, shape, jnp.float32) * deviation * factor_of
    return jnp.minimum(jnp.maximum(result, -limit), limit).astype(held_as)


def setup_inputs(seed: int = 0) -> dict:
    keys = jax.random.split(jax.random.key(seed), 14)
    tokens = normal_values(keys[0], (SEQS, SEQUENCE_LENGTH, D), 1.0, 6.0, ((0, 4), (1, 8)))
    cotangent = normal_values(keys[1], (SEQS, SEQUENCE_LENGTH, D), 1.0, 6.0, ((0, 4), (1, 8)))
    widths = plant(jax.random.randint(keys[2], (SEQS,), 0, 3), jax.random.fold_in(keys[2], 1), 0, 2).astype(jnp.int32)
    attn_codes = plant(jax.random.randint(keys[3], (D, QKVO), -128, 128), jax.random.fold_in(keys[3], 1), -128, 127).astype(jnp.int32)
    attn_exps = plant(jax.random.randint(keys[4], (QKV,), 11, 14), jax.random.fold_in(keys[4], 1), 11, 13).astype(jnp.int32)
    out_exps = plant(jax.random.randint(keys[5], (D,), 11, 14), jax.random.fold_in(keys[5], 1), 11, 13).astype(jnp.int32)
    mlp_codes = plant(jax.random.randint(keys[6], (3, FF, D), -128, 128), jax.random.fold_in(keys[6], 1), -128, 127).astype(jnp.int32)
    gate_exps = plant(jax.random.randint(keys[7], (2, FF), 11, 14), jax.random.fold_in(keys[7], 1), 11, 13).astype(jnp.int32)
    down_exps = plant(jax.random.randint(keys[8], (D,), 12, 15), jax.random.fold_in(keys[8], 1), 12, 14).astype(jnp.int32)
    gain_attn = jnp.clip(1.0 + 0.15 * jax.random.normal(keys[9], (D,), jnp.float32), 0.25, 1.75)
    gain_post_attn = jnp.clip(1.0 + 0.15 * jax.random.normal(keys[10], (D,), jnp.float32), 0.25, 1.75)
    gain_mlp = jnp.clip(1.0 + 0.15 * jax.random.normal(keys[11], (D,), jnp.float32), 0.25, 1.75)
    gain_post_mlp = jnp.clip(1.0 + 0.15 * jax.random.normal(keys[12], (D,), jnp.float32), 0.25, 1.75)
    return dict(tokens=tokens, cotangent=cotangent, widths=widths, attn_codes=attn_codes, attn_exps=attn_exps, out_exps=out_exps, mlp_codes=mlp_codes, gate_exps=gate_exps, down_exps=down_exps, gain_attn=gain_attn, gain_post_attn=gain_post_attn, gain_mlp=gain_mlp, gain_post_mlp=gain_post_mlp)


@jax.custom_vjp
def low(v):
    return lax.optimization_barrier(v.astype(jnp.bfloat16)).astype(jnp.float32)

@jax.custom_vjp
def low_back(v):
    return v

def low_keep(v):
    return (low(v), None)

def low_pass(kept, grad):
    return (grad,)

def back_keep(v):
    return (v, None)

def back_low(kept, grad):
    return (low(grad),)
low.defvjp(low_keep, low_pass)
low_back.defvjp(back_keep, back_low)
eps_norm = 1e-06
soft_cap = 50.0
rope_base = 10000.0
masked_score = -1e+30
gelu_coeff = math.sqrt(2.0 / math.pi)
highest_precision = lax.Precision.HIGHEST

def integer_slice_codes(code_values, width_id):
    four_bit = jnp.clip(jnp.floor_divide(code_values + 8, 16), -8, 7) * 16
    two_bit = jnp.clip(jnp.floor_divide(code_values + 32, 64), -2, 1) * 64
    return jnp.where(width_id == 0, code_values, jnp.where(width_id == 1, four_bit, two_bit))

def powers(exponents):
    return jnp.left_shift(jnp.ones_like(exponents), exponents).astype(jnp.float32)

def rms_norm(values, gain):
    factor = lax.rsqrt(lax.optimization_barrier(jnp.mean(values * values, axis=-1, keepdims=True)) + eps_norm)
    return values * factor * gain

def gelu_tanh(values):
    return 0.5 * values * (1.0 + jnp.tanh(gelu_coeff * (values + 0.044715 * values * values * values)))

def rotary_tables(length, head_dim):
    half_dim = head_dim // 2
    frequency = jnp.exp(jnp.arange(half_dim, dtype=jnp.float32) * (-2.0 * math.log(rope_base) / head_dim))
    angles = jnp.arange(length, dtype=jnp.float32)[:, None] * frequency[None, :]
    return (jnp.cos(angles)[:, None, :], jnp.sin(angles)[:, None, :])

def rotate(values, cosine, sine_table):
    half_dim = values.shape[-1] // 2
    first_half = values[..., :half_dim]
    second_half = values[..., half_dim:]
    return jnp.concatenate([first_half * cosine - second_half * sine_table, second_half * cosine + first_half * sine_table], axis=-1)

def attention_weights(attn_codes, width_id, attn_exps, out_exps):
    sliced = integer_slice_codes(attn_codes, width_id).astype(jnp.float32)
    column_total = attn_exps.shape[0]
    return (sliced[:, :column_total] / powers(attn_exps)[None, :], sliced[:, column_total:] / powers(out_exps)[:, None])

def mlp_weights(mlp_codes, width_id, gate_exps, down_exps):
    sliced = integer_slice_codes(mlp_codes, width_id).astype(jnp.float32)
    return (sliced[:2] / powers(gate_exps)[:, :, None], sliced[2] / powers(down_exps)[None, :])

def head_block(head_items):
    query_head, key_head, value_head = head_items
    length = key_head.shape[0]
    raw_scores = low_back(jnp.einsum('tgd,sd->gts', query_head, key_head, precision=highest_precision))
    capped = soft_cap * jnp.tanh(raw_scores / soft_cap)
    position = jnp.arange(length)
    allowed = position[None, :] <= position[:, None]
    capped = jnp.where(allowed[None], capped, masked_score)
    top_score = lax.optimization_barrier(jnp.max(capped, axis=-1, keepdims=True))
    exp_scores = jnp.exp(capped - top_score)
    attn_probs = low(exp_scores / lax.optimization_barrier(jnp.sum(exp_scores, axis=-1, keepdims=True)))
    return low(low_back(jnp.einsum('gts,sd->tgd', attn_probs, value_head, precision=highest_precision)))

def reference(tokens, cotangent, widths, attn_codes, attn_exps, out_exps, mlp_codes, gate_exps, down_exps, gain_attn, gain_post_attn, gain_mlp, gain_post_mlp):
    column_total = attn_exps.shape[0]
    cosine, sine_table = rotary_tables(SEQUENCE_LENGTH, HEAD_SIZE)
    query_scale = HEAD_SIZE ** (-0.5)
    query_group_width = QUERY_HEADS // KEY_VALUE_HEADS

    def layer(inputs, width_id, attention_change, mlp_delta, gain_set):
        qkv_weight, out_weight = attention_weights(attn_codes, width_id, attn_exps, out_exps)
        qkv_weight = qkv_weight + attention_change[:, :column_total]
        out_weight = out_weight + attention_change[:, column_total:]
        pair_weight, down_weight = mlp_weights(mlp_codes, width_id, gate_exps, down_exps)
        pair_weight = pair_weight + mlp_delta[:2]
        down_weight = down_weight + mlp_delta[2]
        normalized_input = low(rms_norm(inputs, gain_set[0]))
        projected_output = low_back(jnp.dot(normalized_input, qkv_weight, precision=highest_precision))
        gathered_queries = projected_output[:, :QUERY_HEADS * HEAD_SIZE].reshape(SEQUENCE_LENGTH, QUERY_HEADS, HEAD_SIZE)
        gathered_keys = projected_output[:, QUERY_HEADS * HEAD_SIZE:(QUERY_HEADS + KEY_VALUE_HEADS) * HEAD_SIZE].reshape(SEQUENCE_LENGTH, KEY_VALUE_HEADS, HEAD_SIZE)
        gathered_values = projected_output[:, (QUERY_HEADS + KEY_VALUE_HEADS) * HEAD_SIZE:].reshape(SEQUENCE_LENGTH, KEY_VALUE_HEADS, HEAD_SIZE)
        gathered_queries = low(rotate(gathered_queries, cosine, sine_table) * query_scale)
        gathered_keys = low(rotate(gathered_keys, cosine, sine_table))
        gathered_values = low(gathered_values)
        query_head_tensor = jnp.transpose(gathered_queries.reshape(SEQUENCE_LENGTH, KEY_VALUE_HEADS, query_group_width, HEAD_SIZE), (1, 0, 2, 3))
        key_heads = jnp.transpose(gathered_keys, (1, 0, 2))
        value_heads = jnp.transpose(gathered_values, (1, 0, 2))
        attended = lax.map(jax.checkpoint(head_block), (query_head_tensor, key_heads, value_heads))
        attended = jnp.transpose(attended, (1, 0, 2, 3)).reshape(SEQUENCE_LENGTH, QUERY_HEADS * HEAD_SIZE)
        branch = low_back(jnp.dot(attended, out_weight.T, precision=highest_precision))
        middle = inputs + rms_norm(branch, gain_set[1])
        normalized_feedforward = low(rms_norm(middle, gain_set[2]))
        gate_act = low_back(jnp.dot(normalized_feedforward, pair_weight[0].T, precision=highest_precision))
        up_projection = low_back(jnp.dot(normalized_feedforward, pair_weight[1].T, precision=highest_precision))
        hidden_state = low(gelu_tanh(gate_act) * up_projection)
        mixed_out = low_back(jnp.dot(hidden_state, down_weight, precision=highest_precision))
        return middle + rms_norm(mixed_out, gain_set[3])

    def forward(inputs_all, attention_change, mlp_delta, gain_set):

        def step(carry_zero, item_pair):
            seq_inputs, width_id = item_pair
            return (carry_zero, layer(seq_inputs, width_id, attention_change, mlp_delta, gain_set))
        carry_last, outputs = lax.scan(jax.checkpoint(step), jnp.zeros((), jnp.float32), (inputs_all, widths))
        return outputs
    tokens_float = tokens.astype(jnp.float32)
    attn_zero = jnp.zeros(attn_codes.shape, jnp.float32)
    mlp_zero = jnp.zeros(mlp_codes.shape, jnp.float32)
    gain_set = jnp.stack([gain_attn, gain_post_attn, gain_mlp, gain_post_mlp]).astype(jnp.float32)
    outputs, pullback = jax.vjp(forward, tokens_float, attn_zero, mlp_zero, gain_set)
    grad_inputs, grad_attn, grad_mlp, grad_gains = pullback(cotangent.astype(jnp.float32))
    return (outputs.astype(jnp.bfloat16), grad_inputs.astype(jnp.bfloat16), grad_attn, grad_mlp, grad_gains[0], grad_gains[1], grad_gains[2], grad_gains[3])
```

```python
import functools
import math

import jax
import jax.numpy as jnp
from jax import lax
from jax.experimental import pallas as pl
from jax.experimental.pallas import tpu as pltpu
from jax.sharding import PartitionSpec as P

QUERY_HEADS = 8
KEY_VALUE_HEADS = 4
HEAD_SIZE = 256
PAIRED = QUERY_HEADS // KEY_VALUE_HEADS

eps_norm = 1e-06
soft_cap = 50.0
rope_base = 10000.0
gelu_coeff = math.sqrt(2.0 / math.pi)
f32 = jnp.float32
bf16 = jnp.bfloat16
VMEM_LIMIT = 56 * 1024 * 1024


def dot(a, b, dims):
    return lax.dot_general(a, b, (dims, ((), ())), preferred_element_type=f32)


NN = ((1,), (0,))
NT = ((1,), (1,))
TN = ((0,), (0,))


def inverse_powers(exponents):
    return 1.0 / jnp.left_shift(jnp.ones_like(exponents), exponents).astype(f32)


def norm_factor(values):
    return lax.rsqrt(jnp.mean(values * values, axis=-1, keepdims=True) + eps_norm)


def norm_back(values, factor, gain, grad):
    scaled = grad * gain
    inner = jnp.mean(values * scaled, axis=-1, keepdims=True)
    grad_values = factor * scaled - values * (factor * factor * factor * inner)
    return grad_values, jnp.sum(grad * values * factor, axis=0)


def gelu_parts(values):
    inner = gelu_coeff * (values + 0.044715 * values * values * values)
    return jnp.tanh(inner)


def rotary_rows(positions):
    half_dim = HEAD_SIZE // 2
    frequency = jnp.exp(
        jnp.arange(half_dim, dtype=f32) * (-2.0 * math.log(rope_base) / HEAD_SIZE)
    )
    angles = positions.astype(f32)[:, None] * frequency[None, :]
    return jnp.cos(angles)[:, None, :], jnp.sin(angles)[:, None, :]


def rotate(values, cosine, sine):
    half_dim = values.shape[-1] // 2
    a = values[..., :half_dim]
    b = values[..., half_dim:]
    return jnp.concatenate([a * cosine - b * sine, b * cosine + a * sine], axis=-1)


def ring_place(index, size):
    return jnp.where(index % 2 == 0, index // 2, size - 1 - index // 2)


def ring_index(place, size):
    return jnp.where(place < size // 2, 2 * place, 2 * (size - 1 - place) + 1)


def ring_perms(size):
    order = list(range(0, size, 2)) + list(range(size - 1, 0, -2))
    up = [(order[i], order[(i + 1) % size]) for i in range(size)]
    down = [(b, a) for a, b in up]
    return up, down


def ring_offsets(size):
    out = [0]
    for k in range(1, size // 2):
        out += [-k, k]
    return out + [size // 2]


def ring_gather(value, size):
    up, down = ring_perms(size)
    half = value.shape[0] // 2
    a = b = value
    out = [value]
    for _ in range(1, size // 2):
        a = lax.ppermute(a, "wide", up)
        b = lax.ppermute(b, "wide", down)
        out += [a, b]
    a = lax.ppermute(a[:half], "wide", up)
    b = lax.ppermute(b[half:], "wide", down)
    return out + [a, b]


def ring_scatter(part_of, rows, size):
    up, down = ring_perms(size)
    half = rows // 2
    far = part_of(size // 2)
    a = lax.ppermute(far[:half].astype(bf16), "wide", up)
    b = lax.ppermute(far[half:].astype(bf16), "wide", down)
    first = True
    for k in range(size // 2 - 1, 0, -1):
        own_a = part_of(k).astype(f32)
        own_b = part_of(-k).astype(f32)
        if first:
            a = jnp.concatenate([own_a[:half] + a.astype(f32), own_a[half:]], axis=0)
            b = jnp.concatenate([own_b[:half], own_b[half:] + b.astype(f32)], axis=0)
            first = False
        else:
            a = own_a + a.astype(f32)
            b = own_b + b.astype(f32)
        a = lax.ppermute(a.astype(bf16), "wide", up)
        b = lax.ppermute(b.astype(bf16), "wide", down)
    return part_of(0).astype(f32) + a.astype(f32) + b.astype(f32)


def swap(value, axis, bit):
    size = lax.axis_size(axis)
    return lax.ppermute(value, axis, [(i, i ^ bit) for i in range(size)])


def all_to_all(value):
    return lax.all_to_all(value, "wide", split_axis=0, concat_axis=0, tiled=True)


def slice_values(codes, width):
    add = jnp.where(width == 0, 0.0, jnp.where(width == 1, 8.0, 32.0)).astype(f32)
    inverse = jnp.where(width == 0, 1.0, jnp.where(width == 1, 1.0 / 16, 1.0 / 64)).astype(f32)
    step = jnp.where(width == 0, 1.0, jnp.where(width == 1, 16.0, 64.0)).astype(f32)
    top = jnp.where(width == 0, 127.0, jnp.where(width == 1, 112.0, 64.0)).astype(f32)
    low = jnp.where(width == 2, -128.0, -128.0).astype(f32)
    return jnp.maximum(jnp.minimum(jnp.floor((codes + add) * inverse) * step, top), low)


def attn_slice_kernel(places, info, own_ref, other_ref, col_ref, row_ref, *out_refs):
    mine = pl.program_id(1) == info[0]
    codes = jnp.where(mine, own_ref[0], other_ref[0]).astype(f32)
    scale = col_ref[...] * row_ref[...]
    for s, out_ref in enumerate(out_refs):
        out_ref[...] = (slice_values(codes, info[1 + s]) * scale).astype(bf16)


def attn_slices(own, other, places, info, col_scale, row_scale, count):
    blocks, rows, cols = own.shape
    grid_spec = pltpu.PrefetchScalarGridSpec(
        num_scalar_prefetch=2,
        grid=(blocks, 2),
        in_specs=[
            pl.BlockSpec((1, rows, cols), lambda k, j, p, i: (k, 0, 0)),
            pl.BlockSpec((1, rows, cols), lambda k, j, p, i: (k, 0, 0)),
            pl.BlockSpec((1, cols), lambda k, j, p, i: (0, j)),
            pl.BlockSpec((rows, 1), lambda k, j, p, i: (p[k], 0)),
        ],
        out_specs=[pl.BlockSpec((rows, cols), lambda k, j, p, i: (p[k], j))] * count,
    )
    return pl.pallas_call(
        attn_slice_kernel,
        grid_spec=grid_spec,
        out_shape=[jax.ShapeDtypeStruct((blocks * rows, 2 * cols), bf16)] * count,
        compiler_params=pltpu.CompilerParams(vmem_limit_bytes=VMEM_LIMIT),
        name="attn_slices",
    )(places, info, own, other, col_scale, row_scale)


def mlp_slice_kernel(info, code_ref, col_ref, row_ref, *out_refs):
    codes = code_ref[0].astype(f32)
    scale = col_ref[0] * row_ref[0]
    for s, out_ref in enumerate(out_refs):
        out_ref[0] = (slice_values(codes, info[1 + s]) * scale).astype(bf16)


def mlp_slices(codes, info, col_scale, row_scale, count):
    three, rows, cols = codes.shape
    block = 288 if rows % 288 == 0 else rows
    grid_spec = pltpu.PrefetchScalarGridSpec(
        num_scalar_prefetch=1,
        grid=(three, rows // block),
        in_specs=[
            pl.BlockSpec((1, block, cols), lambda k, j, i: (k, j, 0)),
            pl.BlockSpec((1, 1, cols), lambda k, j, i: (k, 0, 0)),
            pl.BlockSpec((1, block, 1), lambda k, j, i: (k, j, 0)),
        ],
        out_specs=[pl.BlockSpec((1, block, cols), lambda k, j, i: (k, j, 0))] * count,
    )
    return pl.pallas_call(
        mlp_slice_kernel,
        grid_spec=grid_spec,
        out_shape=[jax.ShapeDtypeStruct((three, rows, cols), bf16)] * count,
        compiler_params=pltpu.CompilerParams(vmem_limit_bytes=VMEM_LIMIT),
        name="mlp_slices",
    )(info, codes, col_scale, row_scale)


def tile_positions(tile, count, start, class_index, class_rows, rows):
    index = lax.broadcasted_iota(jnp.int32, (count, 1), 0)
    place = start + jnp.bitwise_and(index, tile - 1)
    shift = class_rows.bit_length() - 1
    return (
        jnp.right_shift(place, shift) * rows
        + class_index * class_rows
        + jnp.bitwise_and(place, class_rows - 1)
    )


def stack_heads(block):
    return jnp.concatenate(
        [block[:, j * HEAD_SIZE : (j + 1) * HEAD_SIZE] for j in range(PAIRED)], axis=0
    )


def key_ranges(start, tile, key_block, class_rows, rows):
    free = (start // class_rows) * rows // key_block
    last = (start + tile - 1) // class_rows
    total = ((last + 1) * rows + key_block - 1) // key_block
    return free, total


def attn_forward_kernel(
    info, q_ref, kv_ref, att_ref, exact_ref, lse_ref, *, tile, key_block, class_rows, rows
):
    start = pl.program_id(0) * tile
    free, total = key_ranges(start, tile, key_block, class_rows, rows)
    queries = stack_heads(q_ref[...])
    count = queries.shape[0]
    position = tile_positions(tile, count, start, info[0], class_rows, rows)

    def step(b, carry, masked):
        acc, row_sum = carry
        base = pl.multiple_of(b * key_block, key_block)
        keys = kv_ref[pl.ds(base, key_block), :HEAD_SIZE]
        values = kv_ref[pl.ds(base, key_block), HEAD_SIZE:]
        raw = dot(queries, keys, NT)
        weight = jnp.exp(soft_cap * jnp.tanh(raw * (1.0 / soft_cap)))
        if masked:
            key_place = base + lax.broadcasted_iota(jnp.int32, (1, key_block), 1)
            weight = jnp.where(key_place <= position, weight, 0.0)
        row_sum = row_sum + jnp.sum(weight, axis=-1, keepdims=True)
        acc = acc + dot(weight.astype(bf16), values, NN)
        return acc, row_sum

    carry = (jnp.zeros((count, HEAD_SIZE), f32), jnp.zeros((count, 1), f32))
    carry = lax.fori_loop(0, free, functools.partial(step, masked=False), carry)
    acc, row_sum = lax.fori_loop(free, total, functools.partial(step, masked=True), carry)
    exact = acc / row_sum
    lse = jnp.log(row_sum)
    for j in range(PAIRED):
        cols = slice(j * HEAD_SIZE, (j + 1) * HEAD_SIZE)
        exact_ref[:, cols] = exact[j * tile : (j + 1) * tile]
        att_ref[:, cols] = exact[j * tile : (j + 1) * tile].astype(bf16)
        lse_ref[:, j * 128 : (j + 1) * 128] = jnp.broadcast_to(
            lse[j * tile : (j + 1) * tile], (tile, 128)
        )


def attn_forward(info, queries, pairs, class_rows, rows):
    count, cols = queries.shape
    length = pairs.shape[0]
    tile = min(256, count)
    key_block = min(512, length)
    grid_spec = pltpu.PrefetchScalarGridSpec(
        num_scalar_prefetch=1,
        grid=(count // tile,),
        in_specs=[
            pl.BlockSpec((tile, cols), lambda i, c: (i, 0)),
            pl.BlockSpec((length, 2 * HEAD_SIZE), lambda i, c: (0, 0)),
        ],
        out_specs=[
            pl.BlockSpec((tile, cols), lambda i, c: (i, 0)),
            pl.BlockSpec((tile, cols), lambda i, c: (i, 0)),
            pl.BlockSpec((tile, PAIRED * 128), lambda i, c: (i, 0)),
        ],
    )
    return pl.pallas_call(
        functools.partial(
            attn_forward_kernel, tile=tile, key_block=key_block, class_rows=class_rows, rows=rows
        ),
        grid_spec=grid_spec,
        out_shape=[
            jax.ShapeDtypeStruct((count, cols), bf16),
            jax.ShapeDtypeStruct((count, cols), f32),
            jax.ShapeDtypeStruct((count, PAIRED * 128), f32),
        ],
        compiler_params=pltpu.CompilerParams(vmem_limit_bytes=VMEM_LIMIT),
        name="attn_forward",
    )(info, queries, pairs)


def attn_backward_kernel(
    info,
    q_ref,
    kv_ref,
    grad_ref,
    exact_ref,
    lse_ref,
    dq_ref,
    dkv_ref,
    sum_ref,
    *,
    tile,
    key_block,
    class_rows,
    rows,
):
    @pl.when(pl.program_id(0) == 0)
    def _():
        sum_ref[...] = jnp.zeros_like(sum_ref)

    start = pl.program_id(0) * tile
    free, total = key_ranges(start, tile, key_block, class_rows, rows)
    queries = stack_heads(q_ref[...])
    grads = stack_heads(grad_ref[...])
    count = queries.shape[0]
    delta = jnp.sum(grads.astype(f32) * stack_heads(exact_ref[...]), axis=-1, keepdims=True)
    lse = jnp.concatenate([lse_ref[:, j * 128 : j * 128 + 1] for j in range(PAIRED)], axis=0)
    position = tile_positions(tile, count, start, info[0], class_rows, rows)

    def step(b, acc, masked):
        base = pl.multiple_of(b * key_block, key_block)
        span = pl.ds(base, key_block)
        keys = kv_ref[span, :HEAD_SIZE]
        values = kv_ref[span, HEAD_SIZE:]
        bounded = jnp.tanh(dot(queries, keys, NT) * (1.0 / soft_cap))
        probs = jnp.exp(soft_cap * bounded - lse)
        if masked:
            key_place = base + lax.broadcasted_iota(jnp.int32, (1, key_block), 1)
            probs = jnp.where(key_place <= position, probs, 0.0)
        grad_probs = dot(grads, values, NT)
        grad_raw = (probs * (grad_probs - delta) * (1.0 - bounded * bounded)).astype(bf16)
        sum_ref[span, HEAD_SIZE:] += dot(probs.astype(bf16), grads, TN)
        sum_ref[span, :HEAD_SIZE] += dot(grad_raw, queries, TN)
        return acc + dot(grad_raw, keys, NN)

    acc = jnp.zeros((count, HEAD_SIZE), f32)
    acc = lax.fori_loop(0, free, functools.partial(step, masked=False), acc)
    acc = lax.fori_loop(free, total, functools.partial(step, masked=True), acc)
    for j in range(PAIRED):
        dq_ref[:, j * HEAD_SIZE : (j + 1) * HEAD_SIZE] = acc[j * tile : (j + 1) * tile].astype(bf16)

    @pl.when(pl.program_id(0) == pl.num_programs(0) - 1)
    def _():
        dkv_ref[...] = sum_ref[...].astype(bf16)


def attn_backward(info, queries, pairs, grads, exact, lse, class_rows, rows):
    count, cols = queries.shape
    length = pairs.shape[0]
    tile = min(256, count)
    key_block = min(512, length)
    row_spec = pl.BlockSpec((tile, cols), lambda i, c: (i, 0))
    whole_spec = pl.BlockSpec((length, 2 * HEAD_SIZE), lambda i, c: (0, 0))
    grid_spec = pltpu.PrefetchScalarGridSpec(
        num_scalar_prefetch=1,
        grid=(count // tile,),
        in_specs=[
            row_spec,
            whole_spec,
            row_spec,
            row_spec,
            pl.BlockSpec((tile, PAIRED * 128), lambda i, c: (i, 0)),
        ],
        out_specs=[row_spec, whole_spec],
        scratch_shapes=[pltpu.VMEM((length, 2 * HEAD_SIZE), f32)],
    )
    return pl.pallas_call(
        functools.partial(
            attn_backward_kernel, tile=tile, key_block=key_block, class_rows=class_rows, rows=rows
        ),
        grid_spec=grid_spec,
        out_shape=[
            jax.ShapeDtypeStruct((count, cols), bf16),
            jax.ShapeDtypeStruct((length, 2 * HEAD_SIZE), bf16),
        ],
        compiler_params=pltpu.CompilerParams(vmem_limit_bytes=VMEM_LIMIT),
        name="attn_backward",
    )(info, queries, pairs, grads, exact, lse)


def per_device(
    tokens,
    cotangent,
    widths,
    attn_codes,
    attn_exps,
    out_exps,
    mlp_codes,
    gate_exps,
    down_exps,
    gain_attn,
    gain_post_attn,
    gain_mlp,
    gain_post_mlp,
):
    wide = lax.axis_size("wide")
    seq_size = lax.axis_size("seq")
    wide_index = lax.axis_index("wide")
    side = lax.axis_index("seq") % 2
    is_low = side == 0
    place = ring_place(wide_index, wide)
    count, rows, model_dim = tokens.shape
    length = rows * wide
    classes = wide // KEY_VALUE_HEADS
    class_rows = rows // classes
    class_index = wide_index % classes
    query_cols = QUERY_HEADS * HEAD_SIZE
    key_cols = KEY_VALUE_HEADS * HEAD_SIZE
    head_cols = PAIRED * HEAD_SIZE
    proj_cols = attn_exps.shape[0]
    half_proj = proj_cols // 2
    half_out = (attn_codes.shape[1] - proj_cols) // 2
    query_scale = HEAD_SIZE ** (-0.5)
    attn_rows = attn_codes.shape[0]
    hidden = mlp_codes.shape[1]
    offsets = ring_offsets(wide)
    seqs = range(count)

    def index_at(offset):
        return ring_index(jnp.mod(place + offset, wide), wide)

    places = jnp.stack([index_at(o) for o in offsets]).astype(jnp.int32)
    info = jnp.concatenate([side[None].astype(jnp.int32), widths])
    class_info = class_index[None].astype(jnp.int32)

    def gather_columns(first, size):
        mine = lax.dynamic_slice_in_dim(attn_codes, first + side * size, size, 1).astype(bf16)
        own = jnp.concatenate(ring_gather(mine, wide), axis=0)
        own = own.reshape(wide, attn_rows, size)
        return own, swap(own, "seq", 1)

    column_scale = inverse_powers(attn_exps)[None, :]
    output_scale = inverse_powers(out_exps)[:, None]
    proj_own, proj_other = gather_columns(0, half_proj)
    proj_weights = attn_slices(
        proj_own,
        proj_other,
        places,
        info,
        column_scale,
        jnp.ones((model_dim, 1), f32),
        count,
    )
    out_own, out_other = gather_columns(proj_cols, half_out)
    out_weights = attn_slices(
        out_own,
        out_other,
        places,
        info,
        jnp.ones((1, 2 * half_out), f32),
        output_scale,
        count,
    )
    own_gate_scale = lax.dynamic_slice_in_dim(
        inverse_powers(gate_exps), wide_index * hidden, hidden, 1
    )
    down_scale = inverse_powers(down_exps)
    mlp_weights = mlp_slices(
        mlp_codes,
        info,
        jnp.concatenate([jnp.ones((2, 1, model_dim), f32), down_scale[None, None]], axis=0),
        jnp.concatenate([own_gate_scale, jnp.ones((1, hidden), f32)], axis=0)[:, :, None],
        count,
    )
    pair_weights = [w[:2].reshape(2 * hidden, model_dim) for w in mlp_weights]
    down_weights = [w[2] for w in mlp_weights]

    cosine, sine = rotary_rows(wide_index * rows + jnp.arange(rows))

    def rows_to_heads(values):
        split = values.reshape(classes, class_rows, KEY_VALUE_HEADS, head_cols)
        return jnp.transpose(split, (2, 0, 1, 3)).reshape(wide, class_rows, head_cols)

    def heads_to_rows(blocks):
        split = blocks.reshape(KEY_VALUE_HEADS, classes, class_rows, head_cols)
        return jnp.transpose(split, (1, 2, 0, 3)).reshape(rows, KEY_VALUE_HEADS * head_cols)

    inputs = [tokens[s].astype(f32) for s in seqs]
    grad_out = [cotangent[s].astype(f32) for s in seqs]
    input_factor = [norm_factor(v) for v in inputs]
    normed = [(inputs[s] * input_factor[s] * gain_attn).astype(bf16) for s in seqs]

    queries, pairs = [], []
    for s in seqs:
        projected = dot(normed[s], proj_weights[s], NN)
        query = rotate(
            projected[:, :query_cols].reshape(rows, QUERY_HEADS, HEAD_SIZE), cosine, sine
        )
        query = (query * query_scale).astype(bf16).reshape(rows, query_cols)
        key = rotate(
            projected[:, query_cols : query_cols + key_cols].reshape(
                rows, KEY_VALUE_HEADS, HEAD_SIZE
            ),
            cosine,
            sine,
        ).astype(bf16)
        value = (
            projected[:, query_cols + key_cols :]
            .reshape(rows, KEY_VALUE_HEADS, HEAD_SIZE)
            .astype(bf16)
        )
        pair = jnp.transpose(jnp.concatenate([key, value], axis=-1), (1, 0, 2))
        pair = jnp.broadcast_to(
            pair[:, None], (KEY_VALUE_HEADS, classes, rows, 2 * HEAD_SIZE)
        ).reshape(wide, rows, 2 * HEAD_SIZE)
        queries.append(all_to_all(rows_to_heads(query)).reshape(wide * class_rows, head_cols))
        pairs.append(all_to_all(pair).reshape(length, 2 * HEAD_SIZE))

    attended, exact, lse = [], [], []
    for s in seqs:
        out, full, log_sum = attn_forward(class_info, queries[s], pairs[s], class_rows, rows)
        exact.append(full)
        lse.append(log_sum)
        back = all_to_all(out.reshape(wide, class_rows, head_cols))
        attended.append(heads_to_rows(back))

    branch, branch_factor, middle, middle_factor, normed_mlp = [], [], [], [], []
    for s in seqs:
        value = dot(attended[s], out_weights[s], NT)
        factor = norm_factor(value)
        mid = inputs[s] + value * factor * gain_post_attn
        mid_factor = norm_factor(mid)
        branch.append(value)
        branch_factor.append(factor)
        middle.append(mid)
        middle_factor.append(mid_factor)
        normed_mlp.append((mid * mid_factor * gain_mlp).astype(bf16))

    gathered, gate, up, tanh_gate, hidden_rows, mixed = [], [], [], [], [], []
    for s in seqs:
        group = jnp.concatenate(ring_gather(normed_mlp[s], wide), axis=0)
        both = dot(group, pair_weights[s], NT)
        gate_s, up_s = both[:, :hidden], both[:, hidden:]
        bounded = gelu_parts(gate_s)
        hidden_s = (0.5 * gate_s * (1.0 + bounded) * up_s).astype(bf16)
        part = dot(hidden_s, down_weights[s], NN).astype(bf16)
        order = {o: i for i, o in enumerate(offsets)}
        mixed.append(
            ring_scatter(
                lambda o, part=part: part[order[o] * rows : (order[o] + 1) * rows], rows, wide
            )
        )
        gathered.append(group)
        gate.append(gate_s)
        up.append(up_s)
        hidden_rows.append(hidden_s)

    layer_out, grad_mixed, gain_fourth = [], [], 0.0
    for s in seqs:
        factor = norm_factor(mixed[s])
        layer_out.append((middle[s] + mixed[s] * factor * gain_post_mlp).astype(bf16))
        grad, gain = norm_back(mixed[s], factor, gain_post_mlp, grad_out[s])
        grad_mixed.append(grad.astype(bf16))
        gain_fourth = gain_fourth + gain

    grad_group, grad_pair, grad_normed_mlp = [], [], []
    for s in seqs:
        group = jnp.concatenate(ring_gather(grad_mixed[s], wide), axis=0)
        grad_hidden = dot(group, down_weights[s], NT)
        bounded = gelu_parts(gate[s])
        gelu_value = 0.5 * gate[s] * (1.0 + bounded)
        slope = 0.5 * (1.0 + bounded) + 0.5 * gate[s] * (1.0 - bounded * bounded) * gelu_coeff * (
            1.0 + 3.0 * 0.044715 * gate[s] * gate[s]
        )
        pair = jnp.concatenate(
            [
                (grad_hidden * up[s] * slope).astype(bf16),
                (grad_hidden * gelu_value).astype(bf16),
            ],
            axis=1,
        )
        part = dot(pair, pair_weights[s], NN).astype(bf16)
        order = {o: i for i, o in enumerate(offsets)}
        grad_normed_mlp.append(
            ring_scatter(
                lambda o, part=part: part[order[o] * rows : (order[o] + 1) * rows], rows, wide
            )
        )
        grad_group.append(group)
        grad_pair.append(pair)

    pair_term = sum(dot(grad_pair[s], gathered[s], TN) for s in seqs)
    down_term = sum(dot(hidden_rows[s], grad_group[s], TN) for s in seqs)
    half_hidden = hidden // 2
    mlp_part = jnp.concatenate(
        [pair_term.reshape(2, hidden, model_dim).astype(bf16), down_term[None].astype(bf16)], axis=0
    )
    keep = lax.dynamic_slice_in_dim(mlp_part, side * half_hidden, half_hidden, 1)
    send = lax.dynamic_slice_in_dim(mlp_part, (1 - side) * half_hidden, half_hidden, 1)
    total = keep.astype(f32) + swap(send, "seq", 1).astype(f32)
    bit = 2
    while bit < seq_size:
        low = total.astype(bf16)
        total = low.astype(f32) + swap(low, "seq", bit).astype(f32)
        bit *= 2
    low = total.astype(bf16)
    other = swap(low, "seq", 1)
    mlp_grad = jnp.concatenate(
        [jnp.where(is_low, low, other).astype(f32), jnp.where(is_low, other, low).astype(f32)],
        axis=1,
    )

    grad_middle, grad_branch, grad_heads = [], [], []
    gain_third = gain_second = 0.0
    for s in seqs:
        grad, gain = norm_back(middle[s], middle_factor[s], gain_mlp, grad_normed_mlp[s])
        gain_third = gain_third + gain
        grad_mid = grad_out[s] + grad
        grad_middle.append(grad_mid)
        grad, gain = norm_back(branch[s], branch_factor[s], gain_post_attn, grad_mid)
        gain_second = gain_second + gain
        grad_branch.append(grad.astype(bf16))
        grad_attended = dot(grad_branch[s], out_weights[s], NN).astype(bf16)
        grad_heads.append(
            all_to_all(rows_to_heads(grad_attended)).reshape(wide * class_rows, head_cols)
        )

    grad_query, grad_key_value = [], []
    for s in seqs:
        dq, dkv = attn_backward(
            class_info, queries[s], pairs[s], grad_heads[s], exact[s], lse[s], class_rows, rows
        )
        dq = heads_to_rows(all_to_all(dq.reshape(wide, class_rows, head_cols)))
        dq = rotate(
            dq.astype(f32).reshape(rows, QUERY_HEADS, HEAD_SIZE) * query_scale, cosine, -sine
        )
        dkv = all_to_all(dkv.reshape(wide, rows, 2 * HEAD_SIZE)).reshape(
            KEY_VALUE_HEADS, classes, rows, 2 * HEAD_SIZE
        )
        dkv = jnp.transpose(jnp.sum(dkv.astype(f32), axis=1), (1, 0, 2))
        dk = rotate(dkv[..., :HEAD_SIZE], cosine, -sine)
        grad_query.append(dq.reshape(rows, query_cols).astype(bf16))
        grad_key_value.append(
            jnp.concatenate(
                [dk.reshape(rows, key_cols), dkv[..., HEAD_SIZE:].reshape(rows, key_cols)], axis=1
            ).astype(bf16)
        )

    grad_tokens, gain_first = [], 0.0
    for s in seqs:
        grad_proj = jnp.concatenate([grad_query[s], grad_key_value[s]], axis=1)
        grad_normed = dot(grad_proj, proj_weights[s], NT)
        grad, gain = norm_back(inputs[s], input_factor[s], gain_attn, grad_normed)
        gain_first = gain_first + gain
        grad_tokens.append((grad_middle[s] + grad).astype(bf16))

    def scatter_columns(left, first_half, second_half):
        keep = jnp.where(is_low, first_half, second_half)
        send = jnp.where(is_low, second_half, first_half)
        received = swap(dot(left, send, TN).astype(bf16), "seq", 1)
        part = (dot(left, keep, TN) + received.astype(f32)).astype(bf16)
        own = ring_scatter(
            lambda o: lax.dynamic_slice_in_dim(part, index_at(o) * attn_rows, attn_rows, 0),
            attn_rows,
            wide,
        )
        bit = 2
        while bit < seq_size:
            low = own.astype(bf16)
            own = low.astype(f32) + swap(low, "seq", bit).astype(f32)
            bit *= 2
        low = own.astype(bf16)
        other = swap(low, "seq", 1)
        return [
            jnp.where(is_low, low, other).astype(f32),
            jnp.where(is_low, other, low).astype(f32),
        ]

    all_attended = jnp.concatenate(attended, axis=0)
    out_parts = scatter_columns(
        jnp.concatenate(grad_branch, axis=0), all_attended[:, :half_out], all_attended[:, half_out:]
    )
    proj_parts = scatter_columns(
        jnp.concatenate(normed, axis=0),
        jnp.concatenate(grad_query, axis=0),
        jnp.concatenate(grad_key_value, axis=0),
    )
    attn_grad = jnp.concatenate(proj_parts + out_parts, axis=1)

    gains = jnp.stack([gain_first, gain_second, gain_third, gain_fourth])
    for axis, size in (("seq", seq_size), ("wide", wide)):
        bit = 1
        while bit < size:
            gains = gains + swap(gains, axis, bit)
            bit *= 2
    return (
        jnp.stack(layer_out),
        jnp.stack(grad_tokens),
        attn_grad,
        mlp_grad,
        gains[0],
        gains[1],
        gains[2],
        gains[3],
    )


def solution(mesh):
    placed = (
        P("seq", "wide", None),
        P("seq", "wide", None),
        P("seq"),
        P("wide", None),
        P(),
        P(),
        P(None, "wide", None),
        P(),
        P(),
        P(),
        P(),
        P(),
        P(),
    )
    return jax.shard_map(
        per_device,
        mesh=mesh,
        in_specs=placed,
        out_specs=(
            P("seq", "wide", None),
            P("seq", "wide", None),
            P("wide", None),
            P(None, "wide", None),
            P(),
            P(),
            P(),
            P(),
        ),
        check_vma=False,
    )
```

```python
import functools
import math

import jax
import jax.numpy as jnp
from jax import lax
from jax.experimental import pallas as pl
from jax.experimental.pallas import tpu as pltpu
from jax.sharding import PartitionSpec as P

QUERY_HEADS = 8
KEY_VALUE_HEADS = 4
HEAD_SIZE = 256
PAIRED = QUERY_HEADS // KEY_VALUE_HEADS

eps_norm = 1e-06
soft_cap = 50.0
rope_base = 10000.0
gelu_coeff = math.sqrt(2.0 / math.pi)
f32 = jnp.float32
bf16 = jnp.bfloat16
VMEM_LIMIT = 56 * 1024 * 1024


def dot(a, b, dims):
    return lax.dot_general(a, b, (dims, ((), ())), preferred_element_type=f32)


NN = ((1,), (0,))
NT = ((1,), (1,))
TN = ((0,), (0,))


def inverse_powers(exponents):
    return 1.0 / jnp.left_shift(jnp.ones_like(exponents), exponents).astype(f32)


def norm_factor(values):
    return lax.rsqrt(jnp.mean(values * values, axis=-1, keepdims=True) + eps_norm)


def norm_back(values, factor, gain, grad):
    scaled = grad * gain
    inner = jnp.mean(values * scaled, axis=-1, keepdims=True)
    grad_values = factor * scaled - values * (factor * factor * factor * inner)
    return grad_values, jnp.sum(grad * values * factor, axis=0)


def gelu_parts(values):
    inner = gelu_coeff * (values + 0.044715 * values * values * values)
    return jnp.tanh(inner)


def rotary_rows(positions):
    half_dim = HEAD_SIZE // 2
    frequency = jnp.exp(
        jnp.arange(half_dim, dtype=f32) * (-2.0 * math.log(rope_base) / HEAD_SIZE)
    )
    angles = positions.astype(f32)[:, None] * frequency[None, :]
    return jnp.cos(angles)[:, None, :], jnp.sin(angles)[:, None, :]


def rotate(values, cosine, sine):
    half_dim = values.shape[-1] // 2
    a = values[..., :half_dim]
    b = values[..., half_dim:]
    return jnp.concatenate([a * cosine - b * sine, b * cosine + a * sine], axis=-1)


def ring_place(index, size):
    return jnp.where(index % 2 == 0, index // 2, size - 1 - index // 2)


def ring_index(place, size):
    return jnp.where(place < size // 2, 2 * place, 2 * (size - 1 - place) + 1)


def ring_perms(size):
    order = list(range(0, size, 2)) + list(range(size - 1, 0, -2))
    up = [
        (base + order[i], base + order[(i + 1) % size])
        for base in range(0, lax.axis_size("wide"), size)
        for i in range(size)
    ]
    return up, [(b, a) for a, b in up]


def ring_offsets(size):
    out = [0]
    for k in range(1, size // 2):
        out += [-k, k]
    return out + [size // 2]


def after(value, *earlier):
    return lax.optimization_barrier((value,) + earlier)[0]


def ring_gather(value, size, visit=lambda block: block):
    up, down = ring_perms(size)
    half = value.shape[0] // 2
    a = b = value
    out = [visit(value)]
    for _ in range(1, size // 2):
        a = lax.ppermute(a, "wide", up)
        b = lax.ppermute(b, "wide", down)
        out += [visit(a), visit(b)]
    tokens = (a, b)
    a = lax.ppermute(a[:half], "wide", up)
    b = lax.ppermute(b[half:], "wide", down)
    return out + [visit(a), visit(b)], tokens


def ring_scatter(part_of, rows, size, earlier=()):
    up, down = ring_perms(size)
    half = rows // 2
    far = part_of(size // 2).astype(bf16)
    if earlier:
        far = after(far, *earlier)
    a = lax.ppermute(far[:half], "wide", up)
    b = lax.ppermute(far[half:], "wide", down)
    tokens = (a, b)
    for k in range(size // 2 - 1, 0, -1):
        own_a = part_of(k).astype(f32)
        own_b = part_of(-k).astype(f32)
        if k == size // 2 - 1:
            a = jnp.concatenate([own_a[:half] + a.astype(f32), own_a[half:]], axis=0)
            b = jnp.concatenate([own_b[:half], own_b[half:] + b.astype(f32)], axis=0)
        else:
            a = own_a + a.astype(f32)
            b = own_b + b.astype(f32)
        if k > 1 or size == 4:
            tokens = (a, b)
        a = lax.ppermute(a.astype(bf16), "wide", up)
        b = lax.ppermute(b.astype(bf16), "wide", down)
    return part_of(0).astype(f32) + a.astype(f32) + b.astype(f32), tokens


def swap(value, axis, bit):
    size = lax.axis_size(axis)
    return lax.ppermute(value, axis, [(i, i ^ bit) for i in range(size)])


def all_to_all(value):
    return lax.all_to_all(value, "wide", split_axis=0, concat_axis=0, tiled=True)


def heads_all_to_all(value):
    size = lax.axis_size("wide")
    classes = size // KEY_VALUE_HEADS
    groups = [list(range(c, size, classes)) for c in range(classes)]
    return lax.all_to_all(
        value, "wide", split_axis=0, concat_axis=0, axis_index_groups=groups, tiled=True
    )


def class_ring(value):
    size = lax.axis_size("wide")
    classes = size // KEY_VALUE_HEADS
    perm = [(i, i // classes * classes + (i + 1) % classes) for i in range(size)]
    return lax.ppermute(value, "wide", perm)


def slice_values(codes, width):
    lift = jnp.where(width == 0, 0.0, 0.5).astype(bf16)
    large = jnp.where(width == 0, 0.0, jnp.where(width == 1, 1.5 * 2**11, 1.5 * 2**13)).astype(bf16)
    top = jnp.where(width == 0, 127.0, jnp.where(width == 1, 112.0, 64.0)).astype(bf16)
    return jnp.minimum(((codes + lift) + large) - large, top)


def attn_slice_kernel(places, info, own_ref, other_ref, scale_ref, *out_refs):
    def write(code_ref):
        codes = code_ref[0]
        scale = scale_ref[...].astype(bf16)
        for s, out_ref in enumerate(out_refs):
            out_ref[...] = slice_values(codes, info[1 + s]) * scale

    mine = pl.program_id(1) == info[0]
    pl.when(mine)(lambda: write(own_ref))
    pl.when(jnp.logical_not(mine))(lambda: write(other_ref))


def attn_slices(own, other, places, info, scale, by_column, count):
    blocks, rows, cols = own.shape
    if by_column:
        scale_spec = pl.BlockSpec((1, cols), lambda k, j, p, i: (0, j))
    else:
        scale_spec = pl.BlockSpec((rows, 1), lambda k, j, p, i: (p[k], 0))
    grid_spec = pltpu.PrefetchScalarGridSpec(
        num_scalar_prefetch=2,
        grid=(blocks, 2),
        in_specs=[
            pl.BlockSpec((1, rows, cols), lambda k, j, p, i: (k, 0, 0)),
            pl.BlockSpec((1, rows, cols), lambda k, j, p, i: (k, 0, 0)),
            scale_spec,
        ],
        out_specs=[pl.BlockSpec((rows, cols), lambda k, j, p, i: (p[k], j))] * count,
    )
    return pl.pallas_call(
        attn_slice_kernel,
        grid_spec=grid_spec,
        out_shape=[jax.ShapeDtypeStruct((blocks * rows, 2 * cols), bf16)] * count,
        compiler_params=pltpu.CompilerParams(vmem_limit_bytes=VMEM_LIMIT),
        cost_estimate=pl.CostEstimate(
            flops=10 * count * own.size,
            bytes_accessed=4 * own.size * (1 + count),
            transcendentals=0,
        ),
        name="attn_slices",
    )(places, info, own, other, scale)


def own_slice_kernel(pieces, info, code_ref, row_ref, col_ref, *out_refs):
    count = len(out_refs) // 3
    for m in range(3):
        codes = code_ref[m].astype(f32).astype(bf16)
        scale = (row_ref[m] if m < 2 else col_ref[...]).astype(bf16)
        for s in range(count):
            out_refs[m * count + s][...] = slice_values(codes, info[1 + s]) * scale


def own_slices(codes, pieces, info, row_scale, col_scale, count):
    three, rows, cols = codes.shape
    steps = pieces.shape[0]
    piece = rows // steps
    grid_spec = pltpu.PrefetchScalarGridSpec(
        num_scalar_prefetch=2,
        grid=(steps,),
        in_specs=[
            pl.BlockSpec((three, piece, cols), lambda j, p, i: (0, p[j], 0)),
            pl.BlockSpec((2, piece, 1), lambda j, p, i: (0, j, 0)),
            pl.BlockSpec((1, cols), lambda j, p, i: (0, 0)),
        ],
        out_specs=[pl.BlockSpec((piece, cols), lambda j, p, i: (j, 0))] * (three * count),
    )
    return pl.pallas_call(
        own_slice_kernel,
        grid_spec=grid_spec,
        out_shape=[jax.ShapeDtypeStruct((2 * rows, cols), bf16)] * (three * count),
        compiler_params=pltpu.CompilerParams(vmem_limit_bytes=VMEM_LIMIT),
        cost_estimate=pl.CostEstimate(
            flops=10 * count * codes.size,
            bytes_accessed=codes.size * (4 + 2 * count),
            transcendentals=0,
        ),
        name="own_slices",
    )(pieces, info, codes, row_scale, col_scale)


def partner_slice_kernel(info, *refs, steps, count):
    piece_refs, scale_ref, out_refs = refs[:steps], refs[steps], refs[steps + 1 + count :]
    for j in range(steps):

        @pl.when(pl.program_id(0) == j)
        def _():
            codes = piece_refs[j][...]
            scale = scale_ref[...].astype(bf16)
            for s, out_ref in enumerate(out_refs):
                out_ref[...] = slice_values(codes, info[1 + s]) * scale


def partner_slices(pieces, info, scale, by_column, weights):
    steps = len(pieces)
    count = len(weights)
    piece, cols = pieces[0].shape
    if by_column:
        scale_spec = pl.BlockSpec((1, cols), lambda j, i: (0, 0))
    else:
        scale_spec = pl.BlockSpec((piece, 1), lambda j, i: (steps + j, 0))
    grid_spec = pltpu.PrefetchScalarGridSpec(
        num_scalar_prefetch=1,
        grid=(steps,),
        in_specs=[pl.BlockSpec((piece, cols), lambda j, i: (0, 0))] * steps
        + [scale_spec]
        + [pl.BlockSpec(memory_space=pl.ANY)] * count,
        out_specs=[pl.BlockSpec((piece, cols), lambda j, i: (steps + j, 0))] * count,
    )
    return pl.pallas_call(
        functools.partial(partner_slice_kernel, steps=steps, count=count),
        grid_spec=grid_spec,
        out_shape=[jax.ShapeDtypeStruct(w.shape, bf16) for w in weights],
        input_output_aliases={2 + steps + s: s for s in range(count)},
        compiler_params=pltpu.CompilerParams(vmem_limit_bytes=VMEM_LIMIT),
        cost_estimate=pl.CostEstimate(
            flops=10 * count * steps * piece * cols,
            bytes_accessed=2 * (1 + count) * steps * piece * cols,
            transcendentals=0,
        ),
        name="partner_slices",
    )(info, *pieces, scale, *weights)


def unpack_kernel(pieces, *refs):
    out_ref = refs[-1]
    for m, ref in enumerate(refs[:-1]):
        out_ref[m] = ref[...].astype(f32)


def unpack(grads, pieces):
    steps = pieces.shape[0]
    rows, cols = grads[0].shape
    piece = rows // steps
    grid_spec = pltpu.PrefetchScalarGridSpec(
        num_scalar_prefetch=1,
        grid=(steps,),
        in_specs=[pl.BlockSpec((piece, cols), lambda j, p: (j, 0))] * len(grads),
        out_specs=pl.BlockSpec((len(grads), piece, cols), lambda j, p: (0, p[j], 0)),
    )
    return pl.pallas_call(
        unpack_kernel,
        grid_spec=grid_spec,
        out_shape=jax.ShapeDtypeStruct((len(grads), rows, cols), f32),
        compiler_params=pltpu.CompilerParams(vmem_limit_bytes=VMEM_LIMIT),
        cost_estimate=pl.CostEstimate(
            flops=rows * cols, bytes_accessed=6 * len(grads) * rows * cols, transcendentals=0
        ),
        name="unpack",
    )(pieces, *grads)


def tile_positions(tile, count, start, class_index, class_rows, rows):
    index = lax.broadcasted_iota(jnp.int32, (count, 1), 0)
    place = start + jnp.bitwise_and(index, tile - 1)
    shift = class_rows.bit_length() - 1
    return (
        jnp.right_shift(place, shift) * rows
        + class_index * class_rows
        + jnp.bitwise_and(place, class_rows - 1)
    )


def stack_heads(block):
    return jnp.concatenate(
        [block[:, j * HEAD_SIZE : (j + 1) * HEAD_SIZE] for j in range(PAIRED)], axis=0
    )


def key_ranges(start, tile, key_block, class_rows, rows):
    free = (start // class_rows) * rows // key_block
    last = (start + tile - 1) // class_rows
    total = ((last + 1) * rows + key_block - 1) // key_block
    return free, total


def attn_forward_kernel(
    info, q_ref, kv_ref, att_ref, exact_ref, lse_ref, *, tile, key_block, class_rows, rows
):
    start = pl.program_id(0) * tile
    free, total = key_ranges(start, tile, key_block, class_rows, rows)
    queries = stack_heads(q_ref[...])
    count = queries.shape[0]
    position = tile_positions(tile, count, start, info[0], class_rows, rows)

    def step(b, carry, masked):
        acc, row_sum = carry
        base = pl.multiple_of(b * key_block, key_block)
        keys = kv_ref[pl.ds(base, key_block), :HEAD_SIZE]
        values = kv_ref[pl.ds(base, key_block), HEAD_SIZE:]
        raw = dot(queries, keys, NT)
        weight = jnp.exp(soft_cap * jnp.tanh(raw * (1.0 / soft_cap)))
        if masked:
            key_place = base + lax.broadcasted_iota(jnp.int32, (1, key_block), 1)
            weight = jnp.where(key_place <= position, weight, 0.0)
        row_sum = row_sum + jnp.sum(weight, axis=-1, keepdims=True)
        acc = acc + dot(weight.astype(bf16), values, NN)
        return acc, row_sum

    carry = (jnp.zeros((count, HEAD_SIZE), f32), jnp.zeros((count, 1), f32))
    carry = lax.fori_loop(0, free, functools.partial(step, masked=False), carry)
    acc, row_sum = lax.fori_loop(free, total, functools.partial(step, masked=True), carry)
    exact = acc / row_sum
    lse = jnp.log(row_sum)
    for j in range(PAIRED):
        cols = slice(j * HEAD_SIZE, (j + 1) * HEAD_SIZE)
        exact_ref[:, cols] = exact[j * tile : (j + 1) * tile]
        att_ref[:, cols] = exact[j * tile : (j + 1) * tile].astype(bf16)
        lse_ref[:, j * 128 : (j + 1) * 128] = jnp.broadcast_to(
            lse[j * tile : (j + 1) * tile], (tile, 128)
        )


def attn_forward(info, queries, pairs, class_rows, rows):
    count, cols = queries.shape
    length = pairs.shape[0]
    tile = min(256, count)
    key_block = min(512, length)
    grid_spec = pltpu.PrefetchScalarGridSpec(
        num_scalar_prefetch=1,
        grid=(count // tile,),
        in_specs=[
            pl.BlockSpec((tile, cols), lambda i, c: (i, 0)),
            pl.BlockSpec((length, 2 * HEAD_SIZE), lambda i, c: (0, 0)),
        ],
        out_specs=[
            pl.BlockSpec((tile, cols), lambda i, c: (i, 0)),
            pl.BlockSpec((tile, cols), lambda i, c: (i, 0)),
            pl.BlockSpec((tile, PAIRED * 128), lambda i, c: (i, 0)),
        ],
    )
    return pl.pallas_call(
        functools.partial(
            attn_forward_kernel, tile=tile, key_block=key_block, class_rows=class_rows, rows=rows
        ),
        grid_spec=grid_spec,
        out_shape=[
            jax.ShapeDtypeStruct((count, cols), bf16),
            jax.ShapeDtypeStruct((count, cols), f32),
            jax.ShapeDtypeStruct((count, PAIRED * 128), f32),
        ],
        compiler_params=pltpu.CompilerParams(vmem_limit_bytes=VMEM_LIMIT),
        cost_estimate=pl.CostEstimate(
            flops=2 * count * PAIRED * length * 2 * HEAD_SIZE, bytes_accessed=8 * count * cols + 4 * length * HEAD_SIZE, transcendentals=2 * count * PAIRED * length
        ),
        name="attn_forward",
    )(info, queries, pairs)


def attn_backward_kernel(
    info,
    q_ref,
    kv_ref,
    grad_ref,
    exact_ref,
    lse_ref,
    dq_ref,
    dkv_ref,
    sum_ref,
    *,
    tile,
    key_block,
    class_rows,
    rows,
):
    @pl.when(pl.program_id(0) == 0)
    def _():
        sum_ref[...] = jnp.zeros_like(sum_ref)

    start = pl.program_id(0) * tile
    free, total = key_ranges(start, tile, key_block, class_rows, rows)
    queries = stack_heads(q_ref[...])
    grads = stack_heads(grad_ref[...])
    count = queries.shape[0]
    delta = jnp.sum(grads.astype(f32) * stack_heads(exact_ref[...]), axis=-1, keepdims=True)
    lse = jnp.concatenate([lse_ref[:, j * 128 : j * 128 + 1] for j in range(PAIRED)], axis=0)
    position = tile_positions(tile, count, start, info[0], class_rows, rows)

    def step(b, acc, masked):
        base = pl.multiple_of(b * key_block, key_block)
        span = pl.ds(base, key_block)
        keys = kv_ref[span, :HEAD_SIZE]
        values = kv_ref[span, HEAD_SIZE:]
        bounded = jnp.tanh(dot(queries, keys, NT) * (1.0 / soft_cap))
        probs = jnp.exp(soft_cap * bounded - lse)
        if masked:
            key_place = base + lax.broadcasted_iota(jnp.int32, (1, key_block), 1)
            probs = jnp.where(key_place <= position, probs, 0.0)
        grad_probs = dot(grads, values, NT)
        grad_raw = (probs * (grad_probs - delta) * (1.0 - bounded * bounded)).astype(bf16)
        sum_ref[span, HEAD_SIZE:] += dot(probs.astype(bf16), grads, TN)
        sum_ref[span, :HEAD_SIZE] += dot(grad_raw, queries, TN)
        return acc + dot(grad_raw, keys, NN)

    acc = jnp.zeros((count, HEAD_SIZE), f32)
    acc = lax.fori_loop(0, free, functools.partial(step, masked=False), acc)
    acc = lax.fori_loop(free, total, functools.partial(step, masked=True), acc)
    for j in range(PAIRED):
        dq_ref[:, j * HEAD_SIZE : (j + 1) * HEAD_SIZE] = acc[j * tile : (j + 1) * tile].astype(bf16)

    @pl.when(pl.program_id(0) == pl.num_programs(0) - 1)
    def _():
        dkv_ref[...] = sum_ref[...].astype(bf16)


def attn_backward(info, queries, pairs, grads, exact, lse, class_rows, rows):
    count, cols = queries.shape
    length = pairs.shape[0]
    tile = min(256, count)
    key_block = min(512, length)
    row_spec = pl.BlockSpec((tile, cols), lambda i, c: (i, 0))
    whole_spec = pl.BlockSpec((length, 2 * HEAD_SIZE), lambda i, c: (0, 0))
    grid_spec = pltpu.PrefetchScalarGridSpec(
        num_scalar_prefetch=1,
        grid=(count // tile,),
        in_specs=[
            row_spec,
            whole_spec,
            row_spec,
            row_spec,
            pl.BlockSpec((tile, PAIRED * 128), lambda i, c: (i, 0)),
        ],
        out_specs=[row_spec, whole_spec],
        scratch_shapes=[pltpu.VMEM((length, 2 * HEAD_SIZE), f32)],
    )
    return pl.pallas_call(
        functools.partial(
            attn_backward_kernel, tile=tile, key_block=key_block, class_rows=class_rows, rows=rows
        ),
        grid_spec=grid_spec,
        out_shape=[
            jax.ShapeDtypeStruct((count, cols), bf16),
            jax.ShapeDtypeStruct((length, 2 * HEAD_SIZE), bf16),
        ],
        compiler_params=pltpu.CompilerParams(vmem_limit_bytes=VMEM_LIMIT),
        cost_estimate=pl.CostEstimate(
            flops=5 * count * PAIRED * length * 2 * HEAD_SIZE, bytes_accessed=10 * count * cols + 8 * length * HEAD_SIZE, transcendentals=2 * count * PAIRED * length
        ),
        name="attn_backward",
    )(info, queries, pairs, grads, exact, lse)


def per_device(
    tokens,
    cotangent,
    widths,
    attn_codes,
    attn_exps,
    out_exps,
    mlp_codes,
    gate_exps,
    down_exps,
    gain_attn,
    gain_post_attn,
    gain_mlp,
    gain_post_mlp,
):
    wide = lax.axis_size("wide")
    seq_size = lax.axis_size("seq")
    wide_index = lax.axis_index("wide")
    seq_index = lax.axis_index("seq")
    side = seq_index % 2
    half_wide = wide // 2
    is_low = side == 0
    place = ring_place(wide_index, wide)
    count, rows, model_dim = tokens.shape
    length = rows * wide
    classes = wide // KEY_VALUE_HEADS
    class_rows = rows // classes
    class_index = wide_index % classes
    query_cols = QUERY_HEADS * HEAD_SIZE
    key_cols = KEY_VALUE_HEADS * HEAD_SIZE
    head_cols = PAIRED * HEAD_SIZE
    proj_cols = attn_exps.shape[0]
    half_proj = proj_cols // 2
    half_out = (attn_codes.shape[1] - proj_cols) // 2
    query_scale = HEAD_SIZE ** (-0.5)
    attn_rows = attn_codes.shape[0]
    hidden = mlp_codes.shape[1]
    offsets = ring_offsets(wide)
    order = {o: i for i, o in enumerate(ring_offsets(half_wide))}
    seqs = range(count)

    def index_at(offset):
        return ring_index(jnp.mod(place + offset, wide), wide)

    places = jnp.stack([index_at(o) for o in offsets]).astype(jnp.int32)
    info = jnp.concatenate([side[None].astype(jnp.int32), widths])
    class_info = class_index[None].astype(jnp.int32)

    def gather_columns(first, size, earlier=()):
        mine = lax.dynamic_slice_in_dim(attn_codes, first + side * size, size, 1).astype(bf16)
        if earlier:
            mine = after(mine, *earlier)
        blocks, tokens = ring_gather(mine, wide, lambda block: (block, swap(block, "seq", 1)))
        own = jnp.concatenate([block[0] for block in blocks], axis=0)
        other = jnp.concatenate([block[1] for block in blocks], axis=0)
        shape = (wide, attn_rows, size)
        return own.reshape(shape), other.reshape(shape), tokens

    column_scale = inverse_powers(attn_exps)[None, :]
    output_scale = inverse_powers(out_exps)[:, None]
    proj_own, proj_other, ring_tokens = gather_columns(0, half_proj)
    out_own, out_other, out_tokens = gather_columns(proj_cols, half_out, ring_tokens)
    seq_bits = [1 << i for i in range(seq_size.bit_length() - 1)]
    relative = [0]
    for bit in reversed(seq_bits):
        relative = relative + [r | bit for r in relative]
    pieces = jnp.stack([jnp.bitwise_xor(seq_index, r) for r in relative]).astype(jnp.int32)
    piece_rows = hidden // seq_size
    partner = jnp.bitwise_xor(wide_index, half_wide)
    gate_scale = inverse_powers(gate_exps)
    row_scale = jnp.concatenate(
        [
            lax.dynamic_slice_in_dim(
                gate_scale, block * hidden + pieces[j] * piece_rows, piece_rows, 1
            )
            for block in (wide_index, partner)
            for j in range(seq_size)
        ],
        axis=1,
    )[:, :, None]
    down_scale = inverse_powers(down_exps)[None, :]
    own_weights = own_slices(mlp_codes, pieces, info, row_scale, down_scale, count)
    mlp_weights = []
    token = ring_tokens
    for m in range(3):
        sent = lax.dynamic_slice_in_dim(mlp_codes[m], seq_index * piece_rows, piece_rows, 0)
        sent = after(sent.astype(bf16), *token)
        held = [swap(sent, "wide", half_wide)]
        token = (held[0],)
        for bit in reversed(seq_bits):
            held = held + [swap(block, "seq", bit) for block in held]
        mlp_weights.append(
            partner_slices(
                held,
                info,
                row_scale[m] if m < 2 else down_scale,
                m == 2,
                own_weights[m * count : (m + 1) * count],
            )
        )
    gate_weights, up_weights, down_weights = mlp_weights
    proj_own = after(proj_own, *own_weights)
    proj_weights = attn_slices(proj_own, proj_other, places, info, column_scale, True, count)
    out_weights = attn_slices(out_own, out_other, places, info, output_scale, False, count)

    cosine, sine = rotary_rows(wide_index * rows + jnp.arange(rows))

    def rows_to_heads(values):
        split = values.reshape(classes, class_rows, KEY_VALUE_HEADS, head_cols)
        return jnp.transpose(split, (2, 0, 1, 3)).reshape(wide, class_rows, head_cols)

    def heads_to_rows(blocks):
        split = blocks.reshape(KEY_VALUE_HEADS, classes, class_rows, head_cols)
        return jnp.transpose(split, (1, 2, 0, 3)).reshape(rows, KEY_VALUE_HEADS * head_cols)

    inputs = [tokens[s].astype(f32) for s in seqs]
    grad_out = [cotangent[s].astype(f32) for s in seqs]
    input_factor = [norm_factor(v) for v in inputs]
    normed = [(inputs[s] * input_factor[s] * gain_attn).astype(bf16) for s in seqs]

    queries, pairs = [], []
    for s in seqs:
        projected = dot(normed[s], proj_weights[s], NN)
        query = rotate(
            projected[:, :query_cols].reshape(rows, QUERY_HEADS, HEAD_SIZE), cosine, sine
        )
        query = (query * query_scale).astype(bf16).reshape(rows, query_cols)
        key = rotate(
            projected[:, query_cols : query_cols + key_cols].reshape(
                rows, KEY_VALUE_HEADS, HEAD_SIZE
            ),
            cosine,
            sine,
        ).astype(bf16)
        value = (
            projected[:, query_cols + key_cols :]
            .reshape(rows, KEY_VALUE_HEADS, HEAD_SIZE)
            .astype(bf16)
        )
        pair = jnp.transpose(jnp.concatenate([key, value], axis=-1), (1, 0, 2))
        pair = heads_all_to_all(pair)
        held = [pair]
        for _ in range(classes - 1):
            held.append(class_ring(held[-1]))
        held = jnp.stack(held)
        held = [
            lax.dynamic_index_in_dim(held, jnp.mod(class_index - c, classes), 0, keepdims=False)
            for c in range(classes)
        ]
        pairs.append(jnp.stack(held, axis=1).reshape(length, 2 * HEAD_SIZE))
        queries.append(all_to_all(rows_to_heads(query)).reshape(wide * class_rows, head_cols))

    attended, exact, lse = [], [], []
    for s in seqs:
        out, full, log_sum = attn_forward(class_info, queries[s], pairs[s], class_rows, rows)
        exact.append(full)
        lse.append(log_sum)
        back = all_to_all(out.reshape(wide, class_rows, head_cols))
        attended.append(heads_to_rows(back))

    branch, branch_factor, middle, middle_factor, normed_mlp = [], [], [], [], []
    for s in seqs:
        value = dot(attended[s], out_weights[s], NT)
        factor = norm_factor(value)
        mid = inputs[s] + value * factor * gain_post_attn
        mid_factor = norm_factor(mid)
        branch.append(value)
        branch_factor.append(factor)
        middle.append(mid)
        middle_factor.append(mid_factor)
        normed_mlp.append((mid * mid_factor * gain_mlp).astype(bf16))

    def blocks_of(part):
        return lambda o: part[order[o] * rows : (order[o] + 1) * rows]

    gathered, gate, up, hidden_rows, mixed = [], [], [], [], []
    for s in seqs:
        blocks, ring_tokens = ring_gather(
            after(normed_mlp[s], *ring_tokens) if s else normed_mlp[s], half_wide
        )
        gathered.append(jnp.concatenate(blocks, axis=0))
    for s in seqs:
        gate_s = dot(gathered[s], gate_weights[s], NT)
        up_s = dot(gathered[s], up_weights[s], NT)
        bounded = gelu_parts(gate_s)
        hidden_s = (0.5 * gate_s * (1.0 + bounded) * up_s).astype(bf16)
        part = dot(hidden_s, down_weights[s], NN).astype(bf16)
        total, ring_tokens = ring_scatter(blocks_of(part), rows, half_wide)
        mixed.append(total)
        gate.append(gate_s)
        up.append(up_s)
        hidden_rows.append(hidden_s)

    layer_out, grad_mixed, gain_fourth = [], [], 0.0
    for s in seqs:
        factor = norm_factor(mixed[s])
        layer_out.append((middle[s] + mixed[s] * factor * gain_post_mlp).astype(bf16))
        grad, gain = norm_back(mixed[s], factor, gain_post_mlp, grad_out[s])
        grad_mixed.append(grad.astype(bf16))
        gain_fourth = gain_fourth + gain

    grad_group, grad_gate, grad_up, grad_normed_mlp = [], [], [], []
    for s in seqs:
        blocks, ring_tokens = ring_gather(
            after(grad_mixed[s], *ring_tokens) if s else grad_mixed[s], half_wide
        )
        grad_group.append(jnp.concatenate(blocks, axis=0))
    for s in seqs:
        grad_hidden = dot(grad_group[s], down_weights[s], NT)
        bounded = gelu_parts(gate[s])
        gelu_value = 0.5 * gate[s] * (1.0 + bounded)
        slope = 0.5 * (1.0 + bounded) + 0.5 * gate[s] * (1.0 - bounded * bounded) * gelu_coeff * (
            1.0 + 3.0 * 0.044715 * gate[s] * gate[s]
        )
        grad_gate.append((grad_hidden * up[s] * slope).astype(bf16))
        grad_up.append((grad_hidden * gelu_value).astype(bf16))
        part = dot(grad_gate[s], gate_weights[s], NN) + dot(grad_up[s], up_weights[s], NN)
        total, ring_tokens = ring_scatter(blocks_of(part.astype(bf16)), rows, half_wide)
        grad_normed_mlp.append(total)

    def mlp_gradient(lefts, rights):
        grad = sum(dot(lefts[s], rights[s], TN) for s in seqs).astype(bf16)
        grad = grad.reshape(2, hidden, model_dim)
        for bit in seq_bits:
            split = grad.reshape(2, 2, grad.shape[1] // 2, model_dim)
            received = swap(split[:, 1], "seq", bit)
            grad = (split[:, 0].astype(f32) + received.astype(f32)).astype(bf16)
        received = swap(grad[1], "wide", half_wide)
        grad = (grad[0].astype(f32) + received.astype(f32)).astype(bf16)
        for bit in reversed(seq_bits):
            grad = jnp.concatenate([grad, swap(grad, "seq", bit)], axis=0)
        return grad

    down_grad = mlp_gradient(hidden_rows, grad_group)
    up_grad = mlp_gradient(grad_up, gathered)
    gate_grad = mlp_gradient(grad_gate, gathered)
    mlp_grad = unpack([gate_grad, up_grad, down_grad], pieces)

    grad_middle, grad_branch, grad_heads = [], [], []
    gain_third = gain_second = 0.0
    for s in seqs:
        grad, gain = norm_back(middle[s], middle_factor[s], gain_mlp, grad_normed_mlp[s])
        gain_third = gain_third + gain
        grad_mid = grad_out[s] + grad
        grad_middle.append(grad_mid)
        grad, gain = norm_back(branch[s], branch_factor[s], gain_post_attn, grad_mid)
        gain_second = gain_second + gain
        grad_branch.append(grad.astype(bf16))
        grad_attended = dot(grad_branch[s], out_weights[s], NN).astype(bf16)
        grad_heads.append(
            all_to_all(rows_to_heads(grad_attended)).reshape(wide * class_rows, head_cols)
        )

    grad_query, grad_key_value = [], []
    for s in seqs:
        dq, dkv = attn_backward(
            class_info, queries[s], pairs[s], grad_heads[s], exact[s], lse[s], class_rows, rows
        )
        dq = heads_to_rows(all_to_all(dq.reshape(wide, class_rows, head_cols)))
        dq = rotate(
            dq.astype(f32).reshape(rows, QUERY_HEADS, HEAD_SIZE) * query_scale, cosine, -sine
        )
        dkv = dkv.reshape(KEY_VALUE_HEADS, classes, rows, 2 * HEAD_SIZE)
        total = None
        for step in range(1, classes + 1):
            own = lax.dynamic_index_in_dim(
                dkv, jnp.mod(class_index - step, classes), 1, keepdims=False
            )
            total = own if total is None else own.astype(f32) + class_ring(total).astype(f32)
            total = total.astype(bf16)
        dkv = heads_all_to_all(total)
        dkv = jnp.transpose(dkv.astype(f32), (1, 0, 2))
        dk = rotate(dkv[..., :HEAD_SIZE], cosine, -sine)
        grad_query.append(dq.reshape(rows, query_cols).astype(bf16))
        grad_key_value.append(
            jnp.concatenate(
                [dk.reshape(rows, key_cols), dkv[..., HEAD_SIZE:].reshape(rows, key_cols)], axis=1
            ).astype(bf16)
        )

    grad_tokens, gain_first = [], 0.0
    for s in seqs:
        grad_proj = jnp.concatenate([grad_query[s], grad_key_value[s]], axis=1)
        grad_normed = dot(grad_proj, proj_weights[s], NT)
        grad, gain = norm_back(inputs[s], input_factor[s], gain_attn, grad_normed)
        gain_first = gain_first + gain
        grad_tokens.append((grad_middle[s] + grad).astype(bf16))

    def scatter_columns(left, first_half, second_half, earlier=()):
        keep = jnp.where(is_low, first_half, second_half)
        send = jnp.where(is_low, second_half, first_half)
        received = swap(dot(left, send, TN).astype(bf16), "seq", 1)
        part = (dot(left, keep, TN) + received.astype(f32)).astype(bf16)
        own, tokens = ring_scatter(
            lambda o: lax.dynamic_slice_in_dim(part, index_at(o) * attn_rows, attn_rows, 0),
            attn_rows,
            wide,
            earlier,
        )
        bit = 2
        while bit < seq_size:
            low = own.astype(bf16)
            own = low.astype(f32) + swap(low, "seq", bit).astype(f32)
            bit *= 2
        low = own.astype(bf16)
        other = swap(low, "seq", 1)
        return [
            jnp.where(is_low, low, other).astype(f32),
            jnp.where(is_low, other, low).astype(f32),
        ], tokens

    gains = jnp.stack([gain_first, gain_second, gain_third, gain_fourth])
    for axis, size in (("seq", seq_size), ("wide", wide)):
        bit = 1
        while bit < size:
            gains = gains + swap(gains, axis, bit)
            bit *= 2

    all_attended = jnp.concatenate(attended, axis=0)
    out_parts, ring_tokens = scatter_columns(
        jnp.concatenate(grad_branch, axis=0), all_attended[:, :half_out], all_attended[:, half_out:]
    )
    proj_parts, ring_tokens = scatter_columns(
        jnp.concatenate(normed, axis=0),
        jnp.concatenate(grad_query, axis=0),
        jnp.concatenate(grad_key_value, axis=0),
        ring_tokens,
    )
    attn_grad = jnp.concatenate(proj_parts + out_parts, axis=1)
    return (
        jnp.stack(layer_out),
        jnp.stack(grad_tokens),
        attn_grad,
        mlp_grad,
        gains[0],
        gains[1],
        gains[2],
        gains[3],
    )


def solution(mesh):
    placed = (
        P("seq", "wide", None),
        P("seq", "wide", None),
        P("seq"),
        P("wide", None),
        P(),
        P(),
        P(None, "wide", None),
        P(),
        P(),
        P(),
        P(),
        P(),
        P(),
    )
    return jax.shard_map(
        per_device,
        mesh=mesh,
        in_specs=placed,
        out_specs=(
            P("seq", "wide", None),
            P("seq", "wide", None),
            P("wide", None),
            P(None, "wide", None),
            P(),
            P(),
            P(),
            P(),
        ),
        check_vma=False,
    )
```

```python
import functools
import math

import jax
import jax.numpy as jnp
from jax import lax
from jax.experimental import pallas as pl
from jax.experimental.pallas import tpu as pltpu
from jax.sharding import PartitionSpec as P

QUERY_HEADS = 8
KEY_VALUE_HEADS = 4
HEAD_SIZE = 256
PAIRED = QUERY_HEADS // KEY_VALUE_HEADS

eps_norm = 1e-06
soft_cap = 50.0
rope_base = 10000.0
gelu_coeff = math.sqrt(2.0 / math.pi)
f32 = jnp.float32
bf16 = jnp.bfloat16
VMEM_LIMIT = 56 * 1024 * 1024


def dot(a, b, dims):
    return lax.dot_general(a, b, (dims, ((), ())), preferred_element_type=f32)


NN = ((1,), (0,))
NT = ((1,), (1,))
TN = ((0,), (0,))


def inverse_powers(exponents):
    return 1.0 / jnp.left_shift(jnp.ones_like(exponents), exponents).astype(f32)


def norm_factor(values):
    return lax.rsqrt(jnp.mean(values * values, axis=-1, keepdims=True) + eps_norm)


def norm_back(values, factor, gain, grad):
    scaled = grad * gain
    inner = jnp.mean(values * scaled, axis=-1, keepdims=True)
    grad_values = factor * scaled - values * (factor * factor * factor * inner)
    return grad_values, jnp.sum(grad * values * factor, axis=0)


def gelu_parts(values):
    inner = gelu_coeff * (values + 0.044715 * values * values * values)
    return jnp.tanh(inner)


def rotary_rows(positions):
    half_dim = HEAD_SIZE // 2
    frequency = jnp.exp(
        jnp.arange(half_dim, dtype=f32) * (-2.0 * math.log(rope_base) / HEAD_SIZE)
    )
    angles = positions.astype(f32)[:, None] * frequency[None, :]
    return jnp.cos(angles)[:, None, :], jnp.sin(angles)[:, None, :]


def rotate(values, cosine, sine):
    half_dim = values.shape[-1] // 2
    a = values[..., :half_dim]
    b = values[..., half_dim:]
    return jnp.concatenate([a * cosine - b * sine, b * cosine + a * sine], axis=-1)


def ring_place(index, size):
    return jnp.where(index % 2 == 0, index // 2, size - 1 - index // 2)


def ring_index(place, size):
    return jnp.where(place < size // 2, 2 * place, 2 * (size - 1 - place) + 1)


def ring_perms(size):
    order = list(range(0, size, 2)) + list(range(size - 1, 0, -2))
    up = [
        (base + order[i], base + order[(i + 1) % size])
        for base in range(0, lax.axis_size("wide"), size)
        for i in range(size)
    ]
    return up, [(b, a) for a, b in up]


def ring_offsets(size):
    out = [0]
    for k in range(1, size // 2):
        out += [-k, k]
    return out + [size // 2]


class Clock:
    def __init__(self, token):
        self.token = token

    def sync(self, *arrays):
        *arrays, self.token = lax.optimization_barrier(tuple(arrays) + (self.token,))
        return arrays

    def hold(self, value):
        return lax.optimization_barrier((value, self.token))[0]


def hop(a, b, size):
    up, down = ring_perms(size)
    return lax.ppermute(a, "wide", up), lax.ppermute(b, "wide", down)


def low_sum(*terms):
    return sum(t.astype(f32) for t in terms).astype(bf16)


def halves(value):
    half = value.shape[0] // 2
    return value[:half], value[half:]


def add_first(whole, part):
    count = part.shape[0]
    return jnp.concatenate([low_sum(whole[:count], part), whole[count:].astype(bf16)], axis=0)


def add_last(whole, part):
    count = whole.shape[0] - part.shape[0]
    return jnp.concatenate([whole[:count].astype(bf16), low_sum(whole[count:], part)], axis=0)


def ring_gather(clock, value, size, beside=lambda step: ()):
    a = b = clock.hold(value)
    out, other = [a], []
    for k in range(1, size // 2 + 1):
        if k == size // 2:
            a, b = halves(a)[0], halves(b)[1]
        work = beside(k - 1)
        a, b = hop(a, b, size)
        a, b, *work = clock.sync(a, b, *work)
        out += [a, b]
        other.append(work)
    return out, other


def ring_scatter(clock, part_of, rows, size, beside=lambda step: ()):
    a, b = halves(clock.hold(part_of(size // 2).astype(bf16)))
    other = []
    for k in range(size // 2 - 1, -1, -1):
        work = beside(size // 2 - 1 - k)
        a, b = hop(a, b, size)
        a, b, *work = clock.sync(a, b, *work)
        other.append(work)
        if k == size // 2 - 1 and k > 0:
            a = add_first(part_of(k), a)
            b = add_last(part_of(-k), b)
        elif k > 0:
            a = low_sum(part_of(k), a)
            b = low_sum(part_of(-k), b)
    return part_of(0).astype(f32) + a.astype(f32) + b.astype(f32), other


def swap(value, axis, bit):
    size = lax.axis_size(axis)
    return lax.ppermute(value, axis, [(i, i ^ bit) for i in range(size)])


def all_to_all(value):
    return lax.all_to_all(value, "wide", split_axis=0, concat_axis=0, tiled=True)


def heads_all_to_all(value):
    size = lax.axis_size("wide")
    classes = size // KEY_VALUE_HEADS
    groups = [list(range(c, size, classes)) for c in range(classes)]
    return lax.all_to_all(
        value, "wide", split_axis=0, concat_axis=0, axis_index_groups=groups, tiled=True
    )


def class_ring(value):
    size = lax.axis_size("wide")
    classes = size // KEY_VALUE_HEADS
    perm = [(i, i // classes * classes + (i + 1) % classes) for i in range(size)]
    return lax.ppermute(value, "wide", perm)


def slice_values(codes, width):
    lift = jnp.where(width == 0, 0.0, 0.5).astype(bf16)
    large = jnp.where(width == 0, 0.0, jnp.where(width == 1, 1.5 * 2**11, 1.5 * 2**13)).astype(bf16)
    top = jnp.where(width == 0, 127.0, jnp.where(width == 1, 112.0, 64.0)).astype(bf16)
    return jnp.minimum(((codes + lift) + large) - large, top)


def attn_slice_kernel(places, info, *refs, fixed, split, by_column, count):
    inputs = refs[: len(refs) - 1 - count]
    scale_ref = refs[len(refs) - 1 - count]
    out_refs = refs[len(refs) - count :]
    per_side = len(inputs) // 2
    member = info[1 + count]

    def write(code_refs):
        def put(codes, columns):
            scale = (scale_ref[:, columns] if by_column else scale_ref[...]).astype(bf16)
            for s, out_ref in enumerate(out_refs):
                out_ref[:, columns] = slice_values(codes, info[1 + s]) * scale

        if fixed:
            put(code_refs[0][0][:, :fixed], slice(0, fixed))
        for t in range(per_side):
            first = fixed + jnp.bitwise_xor(member, t) * split
            codes = code_refs[t][0][:, fixed:] if t == 0 and fixed else code_refs[t][0]
            put(codes, pl.ds(pl.multiple_of(first, 128), split))

    mine = pl.program_id(1) == info[0]
    pl.when(mine)(lambda: write(inputs[:per_side]))
    pl.when(jnp.logical_not(mine))(lambda: write(inputs[per_side:]))


def attn_slices(own, other, places, info, scale, fixed, by_column, count):
    blocks, rows, cols = own[0].shape
    split = cols - fixed
    width = fixed + split * len(own)
    if by_column:
        scale_spec = pl.BlockSpec((1, width), lambda k, j, p, i: (0, j))
    else:
        scale_spec = pl.BlockSpec((rows, 1), lambda k, j, p, i: (p[k], 0))
    inputs = list(own) + list(other)
    grid_spec = pltpu.PrefetchScalarGridSpec(
        num_scalar_prefetch=2,
        grid=(blocks, 2),
        in_specs=[
            pl.BlockSpec((1, rows, v.shape[2]), lambda k, j, p, i: (k, 0, 0)) for v in inputs
        ]
        + [scale_spec],
        out_specs=[pl.BlockSpec((rows, width), lambda k, j, p, i: (p[k], j))] * count,
    )
    return pl.pallas_call(
        functools.partial(
            attn_slice_kernel, fixed=fixed, split=split, by_column=by_column, count=count
        ),
        grid_spec=grid_spec,
        out_shape=[jax.ShapeDtypeStruct((blocks * rows, 2 * width), bf16)] * count,
        compiler_params=pltpu.CompilerParams(vmem_limit_bytes=VMEM_LIMIT),
        cost_estimate=pl.CostEstimate(
            flops=20 * count * blocks * rows * width,
            bytes_accessed=4 * blocks * rows * width * (1 + count),
            transcendentals=0,
        ),
        name="attn_slices",
    )(places, info, *inputs, scale)


def own_slice_kernel(pieces, info, code_ref, row_ref, col_ref, *out_refs):
    count = len(out_refs) // 3
    for m in range(3):
        codes = code_ref[m].astype(f32).astype(bf16)
        scale = (row_ref[m] if m < 2 else col_ref[...]).astype(bf16)
        for s in range(count):
            out_refs[m * count + s][...] = slice_values(codes, info[1 + s]) * scale


def own_slices(codes, pieces, info, row_scale, col_scale, count):
    three, rows, cols = codes.shape
    steps = pieces.shape[0]
    piece = rows // steps
    grid_spec = pltpu.PrefetchScalarGridSpec(
        num_scalar_prefetch=2,
        grid=(steps,),
        in_specs=[
            pl.BlockSpec((three, piece, cols), lambda j, p, i: (0, p[j], 0)),
            pl.BlockSpec((2, piece, 1), lambda j, p, i: (0, j, 0)),
            pl.BlockSpec((1, cols), lambda j, p, i: (0, 0)),
        ],
        out_specs=[pl.BlockSpec((piece, cols), lambda j, p, i: (j, 0))] * (three * count),
    )
    return pl.pallas_call(
        own_slice_kernel,
        grid_spec=grid_spec,
        out_shape=[jax.ShapeDtypeStruct((2 * rows, cols), bf16)] * (three * count),
        compiler_params=pltpu.CompilerParams(vmem_limit_bytes=VMEM_LIMIT),
        cost_estimate=pl.CostEstimate(
            flops=10 * count * codes.size,
            bytes_accessed=codes.size * (4 + 2 * count),
            transcendentals=0,
        ),
        name="own_slices",
    )(pieces, info, codes, row_scale, col_scale)


def partner_slice_kernel(info, *refs, steps, count):
    piece_refs, scale_ref, out_refs = refs[:steps], refs[steps], refs[steps + 1 + count :]
    for j in range(steps):

        @pl.when(pl.program_id(0) == j)
        def _():
            codes = piece_refs[j][...]
            scale = scale_ref[...].astype(bf16)
            for s, out_ref in enumerate(out_refs):
                out_ref[...] = slice_values(codes, info[1 + s]) * scale


def partner_slices(pieces, info, scale, by_column, weights):
    steps = len(pieces)
    count = len(weights)
    piece, cols = pieces[0].shape
    if by_column:
        scale_spec = pl.BlockSpec((1, cols), lambda j, i: (0, 0))
    else:
        scale_spec = pl.BlockSpec((piece, 1), lambda j, i: (steps + j, 0))
    grid_spec = pltpu.PrefetchScalarGridSpec(
        num_scalar_prefetch=1,
        grid=(steps,),
        in_specs=[pl.BlockSpec((piece, cols), lambda j, i: (0, 0))] * steps
        + [scale_spec]
        + [pl.BlockSpec(memory_space=pl.ANY)] * count,
        out_specs=[pl.BlockSpec((piece, cols), lambda j, i: (steps + j, 0))] * count,
    )
    return pl.pallas_call(
        functools.partial(partner_slice_kernel, steps=steps, count=count),
        grid_spec=grid_spec,
        out_shape=[jax.ShapeDtypeStruct(w.shape, bf16) for w in weights],
        input_output_aliases={2 + steps + s: s for s in range(count)},
        compiler_params=pltpu.CompilerParams(vmem_limit_bytes=VMEM_LIMIT),
        cost_estimate=pl.CostEstimate(
            flops=10 * count * steps * piece * cols,
            bytes_accessed=2 * (1 + count) * steps * piece * cols,
            transcendentals=0,
        ),
        name="partner_slices",
    )(info, *pieces, scale, *weights)


def unpack_kernel(pieces, *refs):
    out_ref = refs[-1]
    for m, ref in enumerate(refs[:-1]):
        out_ref[m] = ref[...].astype(f32)


def unpack(grads, pieces):
    steps = pieces.shape[0]
    rows, cols = grads[0].shape
    piece = rows // steps
    grid_spec = pltpu.PrefetchScalarGridSpec(
        num_scalar_prefetch=1,
        grid=(steps,),
        in_specs=[pl.BlockSpec((piece, cols), lambda j, p: (j, 0))] * len(grads),
        out_specs=pl.BlockSpec((len(grads), piece, cols), lambda j, p: (0, p[j], 0)),
    )
    return pl.pallas_call(
        unpack_kernel,
        grid_spec=grid_spec,
        out_shape=jax.ShapeDtypeStruct((len(grads), rows, cols), f32),
        compiler_params=pltpu.CompilerParams(vmem_limit_bytes=VMEM_LIMIT),
        cost_estimate=pl.CostEstimate(
            flops=rows * cols, bytes_accessed=6 * len(grads) * rows * cols, transcendentals=0
        ),
        name="unpack",
    )(pieces, *grads)


def tile_positions(tile, count, start, class_index, class_rows, rows):
    index = lax.broadcasted_iota(jnp.int32, (count, 1), 0)
    place = start + jnp.bitwise_and(index, tile - 1)
    shift = class_rows.bit_length() - 1
    return (
        jnp.right_shift(place, shift) * rows
        + class_index * class_rows
        + jnp.bitwise_and(place, class_rows - 1)
    )


def stack_heads(block):
    return jnp.concatenate(
        [block[:, j * HEAD_SIZE : (j + 1) * HEAD_SIZE] for j in range(PAIRED)], axis=0
    )


def key_ranges(start, tile, key_block, class_rows, rows):
    free = (start // class_rows) * rows // key_block
    last = (start + tile - 1) // class_rows
    total = ((last + 1) * rows + key_block - 1) // key_block
    return free, total


def attn_forward_kernel(
    info, q_ref, kv_ref, att_ref, exact_ref, lse_ref, *, tile, key_block, class_rows, rows
):
    start = pl.program_id(0) * tile
    free, total = key_ranges(start, tile, key_block, class_rows, rows)
    queries = stack_heads(q_ref[...])
    count = queries.shape[0]
    position = tile_positions(tile, count, start, info[0], class_rows, rows)

    def step(b, carry, masked):
        acc, row_sum = carry
        base = pl.multiple_of(b * key_block, key_block)
        keys = kv_ref[pl.ds(base, key_block), :HEAD_SIZE]
        values = kv_ref[pl.ds(base, key_block), HEAD_SIZE:]
        raw = dot(queries, keys, NT)
        weight = jnp.exp(soft_cap * jnp.tanh(raw * (1.0 / soft_cap)))
        if masked:
            key_place = base + lax.broadcasted_iota(jnp.int32, (1, key_block), 1)
            weight = jnp.where(key_place <= position, weight, 0.0)
        row_sum = row_sum + jnp.sum(weight, axis=-1, keepdims=True)
        acc = acc + dot(weight.astype(bf16), values, NN)
        return acc, row_sum

    carry = (jnp.zeros((count, HEAD_SIZE), f32), jnp.zeros((count, 1), f32))
    carry = lax.fori_loop(0, free, functools.partial(step, masked=False), carry)
    acc, row_sum = lax.fori_loop(free, total, functools.partial(step, masked=True), carry)
    exact = acc / row_sum
    lse = jnp.log(row_sum)
    for j in range(PAIRED):
        cols = slice(j * HEAD_SIZE, (j + 1) * HEAD_SIZE)
        exact_ref[:, cols] = exact[j * tile : (j + 1) * tile]
        att_ref[:, cols] = exact[j * tile : (j + 1) * tile].astype(bf16)
        lse_ref[:, j * 128 : (j + 1) * 128] = jnp.broadcast_to(
            lse[j * tile : (j + 1) * tile], (tile, 128)
        )


def attn_forward(info, queries, pairs, class_rows, rows):
    count, cols = queries.shape
    length = pairs.shape[0]
    tile = min(256, count)
    key_block = min(512, length)
    grid_spec = pltpu.PrefetchScalarGridSpec(
        num_scalar_prefetch=1,
        grid=(count // tile,),
        in_specs=[
            pl.BlockSpec((tile, cols), lambda i, c: (i, 0)),
            pl.BlockSpec((length, 2 * HEAD_SIZE), lambda i, c: (0, 0)),
        ],
        out_specs=[
            pl.BlockSpec((tile, cols), lambda i, c: (i, 0)),
            pl.BlockSpec((tile, cols), lambda i, c: (i, 0)),
            pl.BlockSpec((tile, PAIRED * 128), lambda i, c: (i, 0)),
        ],
    )
    return pl.pallas_call(
        functools.partial(
            attn_forward_kernel, tile=tile, key_block=key_block, class_rows=class_rows, rows=rows
        ),
        grid_spec=grid_spec,
        out_shape=[
            jax.ShapeDtypeStruct((count, cols), bf16),
            jax.ShapeDtypeStruct((count, cols), f32),
            jax.ShapeDtypeStruct((count, PAIRED * 128), f32),
        ],
        compiler_params=pltpu.CompilerParams(vmem_limit_bytes=VMEM_LIMIT),
        cost_estimate=pl.CostEstimate(
            flops=2 * count * PAIRED * length * 2 * HEAD_SIZE, bytes_accessed=8 * count * cols + 4 * length * HEAD_SIZE, transcendentals=2 * count * PAIRED * length
        ),
        name="attn_forward",
    )(info, queries, pairs)


def attn_backward_kernel(
    info,
    q_ref,
    kv_ref,
    grad_ref,
    exact_ref,
    lse_ref,
    dq_ref,
    dkv_ref,
    sum_ref,
    *,
    tile,
    key_block,
    class_rows,
    rows,
):
    @pl.when(pl.program_id(0) == 0)
    def _():
        sum_ref[...] = jnp.zeros_like(sum_ref)

    start = pl.program_id(0) * tile
    free, total = key_ranges(start, tile, key_block, class_rows, rows)
    queries = stack_heads(q_ref[...])
    grads = stack_heads(grad_ref[...])
    count = queries.shape[0]
    delta = jnp.sum(grads.astype(f32) * stack_heads(exact_ref[...]), axis=-1, keepdims=True)
    lse = jnp.concatenate([lse_ref[:, j * 128 : j * 128 + 1] for j in range(PAIRED)], axis=0)
    position = tile_positions(tile, count, start, info[0], class_rows, rows)

    def step(b, acc, masked):
        base = pl.multiple_of(b * key_block, key_block)
        span = pl.ds(base, key_block)
        keys = kv_ref[span, :HEAD_SIZE]
        values = kv_ref[span, HEAD_SIZE:]
        bounded = jnp.tanh(dot(queries, keys, NT) * (1.0 / soft_cap))
        probs = jnp.exp(soft_cap * bounded - lse)
        if masked:
            key_place = base + lax.broadcasted_iota(jnp.int32, (1, key_block), 1)
            probs = jnp.where(key_place <= position, probs, 0.0)
        grad_probs = dot(grads, values, NT)
        grad_raw = (probs * (grad_probs - delta) * (1.0 - bounded * bounded)).astype(bf16)
        sum_ref[span, HEAD_SIZE:] += dot(probs.astype(bf16), grads, TN)
        sum_ref[span, :HEAD_SIZE] += dot(grad_raw, queries, TN)
        return acc + dot(grad_raw, keys, NN)

    acc = jnp.zeros((count, HEAD_SIZE), f32)
    acc = lax.fori_loop(0, free, functools.partial(step, masked=False), acc)
    acc = lax.fori_loop(free, total, functools.partial(step, masked=True), acc)
    for j in range(PAIRED):
        dq_ref[:, j * HEAD_SIZE : (j + 1) * HEAD_SIZE] = acc[j * tile : (j + 1) * tile].astype(bf16)

    @pl.when(pl.program_id(0) == pl.num_programs(0) - 1)
    def _():
        dkv_ref[...] = sum_ref[...].astype(bf16)


def attn_backward(info, queries, pairs, grads, exact, lse, class_rows, rows):
    count, cols = queries.shape
    length = pairs.shape[0]
    tile = min(256, count)
    key_block = min(512, length)
    row_spec = pl.BlockSpec((tile, cols), lambda i, c: (i, 0))
    whole_spec = pl.BlockSpec((length, 2 * HEAD_SIZE), lambda i, c: (0, 0))
    grid_spec = pltpu.PrefetchScalarGridSpec(
        num_scalar_prefetch=1,
        grid=(count // tile,),
        in_specs=[
            row_spec,
            whole_spec,
            row_spec,
            row_spec,
            pl.BlockSpec((tile, PAIRED * 128), lambda i, c: (i, 0)),
        ],
        out_specs=[row_spec, whole_spec],
        scratch_shapes=[pltpu.VMEM((length, 2 * HEAD_SIZE), f32)],
    )
    return pl.pallas_call(
        functools.partial(
            attn_backward_kernel, tile=tile, key_block=key_block, class_rows=class_rows, rows=rows
        ),
        grid_spec=grid_spec,
        out_shape=[
            jax.ShapeDtypeStruct((count, cols), bf16),
            jax.ShapeDtypeStruct((length, 2 * HEAD_SIZE), bf16),
        ],
        compiler_params=pltpu.CompilerParams(vmem_limit_bytes=VMEM_LIMIT),
        cost_estimate=pl.CostEstimate(
            flops=5 * count * PAIRED * length * 2 * HEAD_SIZE, bytes_accessed=10 * count * cols + 8 * length * HEAD_SIZE, transcendentals=2 * count * PAIRED * length
        ),
        name="attn_backward",
    )(info, queries, pairs, grads, exact, lse)


def per_device(
    tokens,
    cotangent,
    widths,
    attn_codes,
    attn_exps,
    out_exps,
    mlp_codes,
    gate_exps,
    down_exps,
    gain_attn,
    gain_post_attn,
    gain_mlp,
    gain_post_mlp,
):
    wide = lax.axis_size("wide")
    seq_size = lax.axis_size("seq")
    wide_index = lax.axis_index("wide")
    seq_index = lax.axis_index("seq")
    side = seq_index % 2
    is_low = side == 0
    members = seq_size // 2
    member = seq_index // 2
    half_wide = wide // 2
    place = ring_place(wide_index, wide)
    count, rows, model_dim = tokens.shape
    length = rows * wide
    classes = wide // KEY_VALUE_HEADS
    class_rows = rows // classes
    class_index = wide_index % classes
    query_cols = QUERY_HEADS * HEAD_SIZE
    key_cols = KEY_VALUE_HEADS * HEAD_SIZE
    head_cols = PAIRED * HEAD_SIZE
    proj_cols = attn_exps.shape[0]
    half_proj = proj_cols // 2
    half_out = (attn_codes.shape[1] - proj_cols) // 2
    query_scale = HEAD_SIZE ** (-0.5)
    attn_rows = attn_codes.shape[0]
    hidden = mlp_codes.shape[1]
    offsets = ring_offsets(wide)
    order = {o: i for i, o in enumerate(ring_offsets(half_wide))}
    seqs = range(count)
    seq_bits = [1 << i for i in range(seq_size.bit_length() - 1)]
    clock = Clock(widths)

    def index_at(offset):
        return ring_index(jnp.mod(place + offset, wide), wide)

    places = jnp.stack([index_at(o) for o in offsets]).astype(jnp.int32)
    info = jnp.concatenate(
        [side[None].astype(jnp.int32), widths, member[None].astype(jnp.int32)]
    )
    class_info = class_index[None].astype(jnp.int32)
    column_scale = inverse_powers(attn_exps)[None, :]
    output_scale = inverse_powers(out_exps)[:, None]

    relative = [0]
    for bit in reversed(seq_bits):
        relative = relative + [r | bit for r in relative]
    pieces = jnp.stack([jnp.bitwise_xor(seq_index, r) for r in relative]).astype(jnp.int32)
    piece_rows = hidden // seq_size
    partner = jnp.bitwise_xor(wide_index, half_wide)
    gate_scale = inverse_powers(gate_exps)
    row_scale = jnp.concatenate(
        [
            lax.dynamic_slice_in_dim(
                gate_scale, block * hidden + pieces[j] * piece_rows, piece_rows, 1
            )
            for block in (wide_index, partner)
            for j in range(seq_size)
        ],
        axis=1,
    )[:, :, None]
    down_scale = inverse_powers(down_exps)[None, :]

    fixed = half_proj // 2
    split_proj = (half_proj - fixed) // members
    split_out = half_out // members

    def columns(first, size):
        return lax.dynamic_slice_in_dim(attn_codes, first, size, 1)

    payload = jnp.concatenate(
        [
            columns(side * half_proj, fixed),
            columns(side * half_proj + fixed + member * split_proj, split_proj),
            columns(proj_cols + side * half_out + member * split_out, split_out),
        ],
        axis=1,
    ).astype(bf16)
    piece_codes = lax.dynamic_slice_in_dim(mlp_codes, seq_index * piece_rows, piece_rows, 1)
    inputs = [tokens[s].astype(f32) for s in seqs]
    grad_out = [cotangent[s].astype(f32) for s in seqs]

    def early(step):
        if step == 0:
            return own_slices(mlp_codes, pieces, info, row_scale, down_scale, count)
        if step == 1:
            out = [piece_codes[m].astype(bf16) for m in range(3)]
            for s in seqs:
                factor = norm_factor(clock.hold(inputs[s]))
                out += [factor, (inputs[s] * factor * gain_attn).astype(bf16)]
            return out
        return ()

    blocks, work = ring_gather(clock, payload, wide, early)
    work = sum((list(w) for w in work), [])
    own_weights, work = work[: 3 * count], work[3 * count :]
    sends, work = work[:3], work[3:]
    input_factor, normed = work[0::2], work[1::2]

    stacks = {}
    for block in blocks:
        shared = [block] + [None] * (members - 1)
        for bit in seq_bits[1:]:
            for t in range(bit // 2):
                value = shared[t][:, fixed:] if t == 0 else shared[t]
                shared[t + bit // 2] = swap(value, "seq", bit)
        for t, value in enumerate(shared):
            stacks.setdefault((0, t), []).append(value)
            stacks.setdefault((1, t), []).append(swap(value, "seq", 1))
    proj_in, out_in = [], []
    for core in range(2):
        for t in range(members):
            values = jnp.concatenate(stacks[core, t], axis=0).reshape(wide, attn_rows, -1)
            cut = values.shape[2] - split_out
            proj_in.append(values[:, :, :cut])
            out_in.append(values[:, :, cut:])

    def exchange(m):
        return swap(clock.hold(sends[m]), "wide", half_wide)

    def share(block):
        held = [block]
        for bit in reversed(seq_bits):
            held = held + [swap(value, "seq", bit) for value in held]
        return held

    def partner_weights(m, held):
        scale = row_scale[m] if m < 2 else down_scale
        return partner_slices(
            held, info, scale, m == 2, own_weights[m * count : (m + 1) * count]
        )

    cosine, sine = rotary_rows(wide_index * rows + jnp.arange(rows))

    def rows_to_heads(values):
        split = values.reshape(classes, class_rows, KEY_VALUE_HEADS, head_cols)
        return jnp.transpose(split, (2, 0, 1, 3)).reshape(wide, class_rows, head_cols)

    def heads_to_rows(blocks):
        split = blocks.reshape(KEY_VALUE_HEADS, classes, class_rows, head_cols)
        return jnp.transpose(split, (1, 2, 0, 3)).reshape(rows, KEY_VALUE_HEADS * head_cols)

    received = exchange(0)
    proj_weights = attn_slices(
        proj_in[:members], proj_in[members:], places, info, column_scale, fixed, True, count
    )
    query_send, pair_send = [], []
    for s in seqs:
        projected = dot(normed[s], proj_weights[s], NN)
        query = rotate(
            projected[:, :query_cols].reshape(rows, QUERY_HEADS, HEAD_SIZE), cosine, sine
        )
        query = (query * query_scale).astype(bf16).reshape(rows, query_cols)
        key = rotate(
            projected[:, query_cols : query_cols + key_cols].reshape(
                rows, KEY_VALUE_HEADS, HEAD_SIZE
            ),
            cosine,
            sine,
        ).astype(bf16)
        value = (
            projected[:, query_cols + key_cols :]
            .reshape(rows, KEY_VALUE_HEADS, HEAD_SIZE)
            .astype(bf16)
        )
        pair_send.append(jnp.transpose(jnp.concatenate([key, value], axis=-1), (1, 0, 2)))
        query_send.append(rows_to_heads(query))
    received, *sent = clock.sync(received, *query_send, *pair_send)
    query_send, pair_send = sent[:count], sent[count:]

    def spread_pairs(pair):
        held = [pair]
        for _ in range(classes - 1):
            held.append(class_ring(held[-1]))
        held = jnp.stack(held)
        held = [
            lax.dynamic_index_in_dim(held, jnp.mod(class_index - c, classes), 0, keepdims=False)
            for c in range(classes)
        ]
        return jnp.stack(held, axis=1).reshape(length, 2 * HEAD_SIZE)

    attended_send, exact, lse, queries, pairs = [], [], [], [], []

    def attend(s):
        out, full, log_sum = attn_forward(class_info, queries[s], pairs[s], class_rows, rows)
        return [out.reshape(wide, class_rows, head_cols), full, log_sum]

    def keep_attend(work):
        attended_send.append(work[0])
        exact.append(work[1])
        lse.append(work[2])

    gate_held = share(received)
    for s in seqs:
        pair = heads_all_to_all(clock.hold(pair_send[s]))
        if s:
            pair, *work = clock.sync(pair, *attend(s - 1))
            keep_attend(work)
        else:
            pair, *gate_held = clock.sync(pair, *gate_held)
        query = all_to_all(clock.hold(query_send[s]))
        pair = spread_pairs(pair)
        if s == 0:
            gate_weights = partner_weights(0, [clock.hold(v) for v in gate_held])
            query, pair, *gate_weights = clock.sync(query, pair, *gate_weights)
        elif s == 1:
            out_weights = attn_slices(
                [clock.hold(v) for v in out_in[:members]],
                out_in[members:],
                places,
                info,
                output_scale,
                0,
                False,
                count,
            )
            query, pair, *out_weights = clock.sync(query, pair, *out_weights)
        else:
            query, pair = clock.sync(query, pair)
        queries.append(query.reshape(wide * class_rows, head_cols))
        pairs.append(pair)

    attended, branch, branch_factor, middle, middle_factor, normed_mlp = [], [], [], [], [], []

    def join(s):
        value = dot(attended[s], out_weights[s], NT)
        factor = norm_factor(value)
        mid = inputs[s] + value * factor * gain_post_attn
        mid_factor = norm_factor(mid)
        return [value, factor, mid, mid_factor, (mid * mid_factor * gain_mlp).astype(bf16)]

    def keep_join(work):
        for held, value in zip((branch, branch_factor, middle, middle_factor, normed_mlp), work):
            held.append(value)

    for s in seqs:
        back = all_to_all(clock.hold(attended_send[s]))
        work = []
        if s == count - 2 or count == 1:
            work = attend(count - 1)
        if s:
            joined = join(s - 1)
            back, *joined = clock.sync(back, *joined)
            keep_join(joined)
        if work:
            back, *work = clock.sync(back, *work)
            keep_attend(work)
        attended.append(heads_to_rows(back))

    received, *joined = clock.sync(exchange(1), *join(count - 1))
    keep_join(joined)
    up_held = share(received)

    def blocks_of(part):
        return lambda o: part[order[o] * rows : (order[o] + 1) * rows]

    gathered, gate, up, hidden_rows, mixed, parts = [], [], [], [], [], []

    def open_gate(s):
        return dot(clock.hold(gathered[s]), gate_weights[s], NT)

    def open_up(s):
        up_s = dot(clock.hold(gathered[s]), up_weights[s], NT)
        hidden_s = (0.5 * gate[s] * (1.0 + gelu_parts(gate[s])) * up_s).astype(bf16)
        return [up_s, hidden_s]

    def keep_up(work):
        up.append(work[0])
        hidden_rows.append(work[1])

    def mix(s):
        return dot(clock.hold(hidden_rows[s]), down_weights[s], NN).astype(bf16)

    blocks, work = ring_gather(
        clock, normed_mlp[0], half_wide, lambda k: tuple(up_held) if k == half_wide // 2 - 1 else ()
    )
    up_held = work[-1]
    gathered.append(jnp.concatenate(blocks, axis=0))
    received = exchange(2)
    up_weights = partner_weights(1, up_held)
    gate.append(open_gate(0))
    received, *work = clock.sync(received, *open_up(0), *up_weights, gate[0])
    keep_up(work[:2])
    up_weights = work[2 : 2 + count]
    gate[0] = work[-1]
    down_held = share(received)
    for s in seqs[1:]:
        blocks, _ = ring_gather(clock, normed_mlp[s], half_wide)
        gathered.append(jnp.concatenate(blocks, axis=0))
    down_weights = partner_weights(2, down_held)
    parts.append(clock.sync(mix(0))[0])

    layer_out, grad_mixed, gain_fourth = [], [], 0.0

    def finish(s):
        nonlocal gain_fourth
        factor = norm_factor(mixed[s])
        layer_out.append((middle[s] + mixed[s] * factor * gain_post_mlp).astype(bf16))
        grad, gain = norm_back(mixed[s], factor, gain_post_mlp, grad_out[s])
        grad_mixed.append(grad.astype(bf16))
        gain_fourth = gain_fourth + gain

    def next_forward(s):
        def beside(step):
            if s + 1 >= count:
                return ()
            if step == 0:
                return (open_gate(s + 1),)
            return ()

        return beside

    grad_group, grad_gate, grad_up, grad_parts, grad_normed_mlp = [], [], [], [], []

    def back_hidden(s):
        grad_hidden = dot(clock.hold(grad_group[s]), down_weights[s], NT)
        bounded = gelu_parts(gate[s])
        gelu_value = 0.5 * gate[s] * (1.0 + bounded)
        slope = 0.5 * (1.0 + bounded) + 0.5 * gate[s] * (1.0 - bounded * bounded) * gelu_coeff * (
            1.0 + 3.0 * 0.044715 * gate[s] * gate[s]
        )
        return [(grad_hidden * up[s] * slope).astype(bf16), (grad_hidden * gelu_value).astype(bf16)]

    def back_input(s):
        return (
            dot(clock.hold(grad_gate[s]), gate_weights[s], NN)
            + dot(grad_up[s], up_weights[s], NN)
        ).astype(bf16)

    def keep_back(work):
        grad_gate.append(work[0])
        grad_up.append(work[1])

    def first_sum(part):
        a, b = hop(*halves(clock.hold(blocks_of(part)(half_wide // 2))), half_wide)
        return a, b

    def rest_sum(part, a, b, beside=lambda step: ()):
        part_of = blocks_of(part)
        other = []
        for k in range(half_wide // 2 - 1, 0, -1):
            if k == half_wide // 2 - 1:
                a = add_first(part_of(k), a)
                b = add_last(part_of(-k), b)
            else:
                a = low_sum(part_of(k), a)
                b = low_sum(part_of(-k), b)
            work = beside(half_wide // 2 - 1 - k)
            a, b = hop(a, b, half_wide)
            a, b, *work = clock.sync(a, b, *work)
            other.append(work)
        return part_of(0).astype(f32) + a.astype(f32) + b.astype(f32), other

    for s in seqs:
        a, b = first_sum(parts[s])
        if s + 1 < count:
            a, b, value = clock.sync(a, b, open_gate(s + 1))
            gate.append(value)
        elif s:
            a, b, *work = clock.sync(a, b, *back_hidden(0))
            keep_back(work)
        else:
            a, b = clock.sync(a, b)

        def beside(step, s=s):
            if step:
                return ()
            if s + 1 < count:
                return tuple(open_up(s + 1))
            return (back_input(0),) if s else ()

        total, work = rest_sum(parts[s], a, b, beside)
        if s + 1 < count:
            keep_up(work[0])
        elif s:
            grad_parts.append(work[0][0])
        mixed.append(total)
        finish(s)
        if s + 1 < count:
            parts.append(mix(s + 1))
            parts[-1], grad_mixed[s] = clock.sync(parts[-1], grad_mixed[s])
        if s == 0:
            blocks, _ = ring_gather(clock, grad_mixed[0], half_wide)
            grad_group.append(jnp.concatenate(blocks, axis=0))
    if count == 1:
        keep_back(back_hidden(0))
        grad_parts.append(back_input(0))

    def weight_first(left, right):
        return dot(clock.hold(left), right, TN)

    def weight_rest(first, lefts, rights):
        total = first + sum(dot(clock.hold(lefts[s]), rights[s], TN) for s in seqs[1:])
        return total.astype(bf16).reshape(2, hidden, model_dim)

    def core_half(grad):
        split = grad.reshape(2, 2, grad.shape[1] // 2, model_dim)
        return split[:, 0], split[:, 1]

    def seq_sum(grad, bits):
        for bit in bits:
            keep, send = core_half(grad)
            grad = low_sum(keep, swap(send, "seq", bit))
        return grad

    def seq_share(grad):
        for bit in reversed(seq_bits):
            grad = jnp.concatenate([grad, swap(grad, "seq", bit)], axis=0)
        return grad

    grad_middle, grad_branch, grad_send = [], [], []
    gain_third = gain_second = 0.0

    def back_branch(s):
        nonlocal gain_third, gain_second
        grad, gain = norm_back(middle[s], middle_factor[s], gain_mlp, grad_normed_mlp[s])
        gain_third = gain_third + gain
        grad_mid = grad_out[s] + grad
        grad, gain = norm_back(branch[s], branch_factor[s], gain_post_attn, grad_mid)
        gain_second = gain_second + gain
        grad = grad.astype(bf16)
        send = rows_to_heads(dot(grad, out_weights[s], NN).astype(bf16))
        return [grad_mid, grad, send]

    def keep_branch(work):
        grad_middle.append(work[0])
        grad_branch.append(work[1])
        grad_send.append(work[2])

    for s in seqs[1:]:
        blocks, work = ring_gather(
            clock,
            grad_mixed[s],
            half_wide,
            lambda k: (weight_first(hidden_rows[0], grad_group[0]),) if k == 0 and s == 1 else (),
        )
        if s == 1:
            down_first = work[0][0]
        grad_group.append(jnp.concatenate(blocks, axis=0))
    if count == 1:
        down_first = weight_first(hidden_rows[0], grad_group[0])
    for s in seqs:
        a, b = first_sum(grad_parts[s])
        if s + 1 < count:
            a, b, *work = clock.sync(a, b, *back_hidden(s + 1))
            keep_back(work)
        elif s:
            a, b, *work = clock.sync(a, b, *back_branch(s - 1))
            keep_branch(work)
        else:
            a, b = clock.sync(a, b)

        def beside(step, s=s):
            if step:
                return ()
            if s + 1 < count:
                return (back_input(s + 1),)
            return (weight_rest(down_first, hidden_rows, grad_group),)

        total, work = rest_sum(grad_parts[s], a, b, beside)
        if s + 1 < count:
            grad_parts.append(work[0][0])
        else:
            down_grad = work[0][0]
        grad_normed_mlp.append(total)

    down_grad = seq_sum(down_grad, seq_bits[:1])
    last = back_branch(count - 1) if count > 1 else back_branch(0)
    grad_heads = []
    for s in seqs:
        if s == count - 1 and count == 1:
            keep_branch(clock.sync(*last))
        back = all_to_all(clock.hold(grad_send[s]))
        work = []
        if s == count - 2:
            work = last
        if s:
            pass
        if work:
            back, down_grad, *work = clock.sync(back, down_grad, *work)
            keep_branch(work)
            down_grad = seq_sum(down_grad, seq_bits[1:])
        elif s == count - 1:
            up_first = weight_first(grad_up[0], gathered[0])
            dq_dkv = attn_backward(
                class_info,
                queries[0],
                pairs[0],
                clock.hold(grad_heads[0]) if s else back.reshape(wide * class_rows, head_cols),
                exact[0],
                lse[0],
                class_rows,
                rows,
            )
            back, up_first, *dq_dkv = clock.sync(back, up_first, *dq_dkv)
        else:
            (back,) = clock.sync(back)
        grad_heads.append(back.reshape(wide * class_rows, head_cols))

    def class_sum(dkv):
        dkv = dkv.reshape(KEY_VALUE_HEADS, classes, rows, 2 * HEAD_SIZE)
        total = None
        for step in range(1, classes + 1):
            own = lax.dynamic_index_in_dim(
                dkv, jnp.mod(class_index - step, classes), 1, keepdims=False
            )
            total = own if total is None else low_sum(own, class_ring(total))
        return total

    query_back, pair_back = [], []
    beside_query = {}
    for s in seqs:
        dq, dkv = dq_dkv
        query = all_to_all(clock.hold(dq.reshape(wide, class_rows, head_cols)))
        pair = class_sum(dkv)
        if s + 1 < count:
            dq_dkv = attn_backward(
                class_info,
                queries[s + 1],
                pairs[s + 1],
                clock.hold(grad_heads[s + 1]),
                exact[s + 1],
                lse[s + 1],
                class_rows,
                rows,
            )
            query, pair, *dq_dkv = clock.sync(query, pair, *dq_dkv)
        elif s:
            gate_first = weight_first(grad_gate[0], gathered[0])
            query, pair, gate_first = clock.sync(query, pair, gate_first)
        else:
            query, pair = clock.sync(query, pair)
        pair = heads_all_to_all(clock.hold(pair))
        if s == 0:
            up_grad = weight_rest(up_first, grad_up, gathered)
            pair, up_grad = clock.sync(pair, up_grad)
            up_grad = seq_sum(up_grad, seq_bits)
        elif s == 1:
            gate_grad = weight_rest(gate_first, grad_gate, gathered)
            pair, gate_grad = clock.sync(pair, gate_grad)
            gate_grad = seq_sum(gate_grad, seq_bits)
        else:
            (pair,) = clock.sync(pair)
        query_back.append(query)
        pair_back.append(pair)
    if count == 1:
        gate_grad = weight_rest(weight_first(grad_gate[0], gathered[0]), grad_gate, gathered)
        gate_grad = seq_sum(gate_grad, seq_bits)

    def owner_sum(grad):
        return low_sum(grad[0], swap(clock.hold(grad[1]), "wide", half_wide))

    down_grad = owner_sum(down_grad)
    grad_query, grad_key_value, grad_tokens, gain_first = [], [], [], 0.0
    for s in seqs:
        dq = rotate(
            heads_to_rows(query_back[s]).astype(f32).reshape(rows, QUERY_HEADS, HEAD_SIZE)
            * query_scale,
            cosine,
            -sine,
        )
        dkv = jnp.transpose(pair_back[s].astype(f32), (1, 0, 2))
        dk = rotate(dkv[..., :HEAD_SIZE], cosine, -sine)
        grad_query.append(dq.reshape(rows, query_cols).astype(bf16))
        grad_key_value.append(
            jnp.concatenate(
                [dk.reshape(rows, key_cols), dkv[..., HEAD_SIZE:].reshape(rows, key_cols)], axis=1
            ).astype(bf16)
        )
    first_half = jnp.concatenate(grad_query, axis=0)
    second_half = jnp.concatenate(grad_key_value, axis=0)
    all_normed = jnp.concatenate(normed, axis=0)
    all_attended = jnp.concatenate(attended, axis=0)
    all_branch = jnp.concatenate(grad_branch, axis=0)
    keep_left = jnp.where(is_low, first_half, second_half)
    send_right = jnp.where(is_low, second_half, first_half)
    proj_sent = swap(dot(all_normed, send_right, TN).astype(bf16), "seq", 1)
    low_out, high_out = all_attended[:, :half_out], all_attended[:, half_out:]
    out_sent = swap(
        dot(all_branch, jnp.where(is_low, high_out, low_out), TN).astype(bf16), "seq", 1
    )
    out_part = low_sum(dot(all_branch, jnp.where(is_low, low_out, high_out), TN), out_sent)
    proj_part = low_sum(dot(all_normed, keep_left, TN), proj_sent)
    for s in seqs:
        grad_proj = jnp.concatenate([grad_query[s], grad_key_value[s]], axis=1)
        grad_normed = dot(grad_proj, proj_weights[s], NT)
        grad, gain = norm_back(inputs[s], input_factor[s], gain_attn, grad_normed)
        gain_first = gain_first + gain
        grad_tokens.append((grad_middle[s] + grad).astype(bf16))
    gains = jnp.stack([gain_first, gain_second, gain_third, gain_fourth])
    down_grad, proj_part, out_part, gains = clock.sync(down_grad, proj_part, out_part, gains)
    for axis, size in (("seq", seq_size), ("wide", wide)):
        bit = 1
        while bit < size:
            gains = gains + swap(gains, axis, bit)
            bit *= 2
    gains, *grad_tokens = clock.sync(gains, *grad_tokens)

    def part_of(o):
        first = index_at(o) * attn_rows
        return jnp.concatenate(
            [
                lax.dynamic_slice_in_dim(proj_part, first, attn_rows, 0),
                lax.dynamic_slice_in_dim(out_part, first, attn_rows, 0),
            ],
            axis=1,
        )

    total, _ = ring_scatter(clock, part_of, attn_rows, wide)
    up_grad = owner_sum(up_grad)
    for bit in seq_bits[1:]:
        low = total.astype(bf16)
        total = low.astype(f32) + swap(low, "seq", bit).astype(f32)
    low = total.astype(bf16)
    other = swap(low, "seq", 1)
    (up_grad,) = clock.sync(up_grad)
    gate_grad = owner_sum(gate_grad)
    mlp_grad = unpack([seq_share(gate_grad), seq_share(up_grad), seq_share(down_grad)], pieces)
    left, right = jnp.where(is_low, low, other), jnp.where(is_low, other, low)
    attn_grad = jnp.concatenate(
        [left[:, :half_proj], right[:, :half_proj], left[:, half_proj:], right[:, half_proj:]],
        axis=1,
    ).astype(f32)
    return (
        jnp.stack(layer_out),
        jnp.stack(grad_tokens),
        attn_grad,
        mlp_grad,
        gains[0],
        gains[1],
        gains[2],
        gains[3],
    )


def solution(mesh):
    placed = (
        P("seq", "wide", None),
        P("seq", "wide", None),
        P("seq"),
        P("wide", None),
        P(),
        P(),
        P(None, "wide", None),
        P(),
        P(),
        P(),
        P(),
        P(),
        P(),
    )
    return jax.shard_map(
        per_device,
        mesh=mesh,
        in_specs=placed,
        out_specs=(
            P("seq", "wide", None),
            P("seq", "wide", None),
            P("wide", None),
            P(None, "wide", None),
            P(),
            P(),
            P(),
            P(),
        ),
        check_vma=False,
    )
```

```python
import functools
import math

import jax
import jax.numpy as jnp
from jax import lax
from jax.experimental import pallas as pl
from jax.experimental.pallas import tpu as pltpu
from jax.sharding import PartitionSpec as P

QUERY_HEADS = 8
KEY_VALUE_HEADS = 4
HEAD_SIZE = 256
PAIRED = QUERY_HEADS // KEY_VALUE_HEADS

eps_norm = 1e-06
soft_cap = 50.0
rope_base = 10000.0
gelu_coeff = math.sqrt(2.0 / math.pi)
f32 = jnp.float32
bf16 = jnp.bfloat16
VMEM_LIMIT = 56 * 1024 * 1024


def dot(a, b, dims):
    return lax.dot_general(a, b, (dims, ((), ())), preferred_element_type=f32)


NN = ((1,), (0,))
NT = ((1,), (1,))
TN = ((0,), (0,))


def inverse_powers(exponents):
    return 1.0 / jnp.left_shift(jnp.ones_like(exponents), exponents).astype(f32)


def norm_factor(values):
    return lax.rsqrt(jnp.mean(values * values, axis=-1, keepdims=True) + eps_norm)


def norm_back(values, factor, gain, grad):
    scaled = grad * gain
    inner = jnp.mean(values * scaled, axis=-1, keepdims=True)
    grad_values = factor * scaled - values * (factor * factor * factor * inner)
    return grad_values, jnp.sum(grad * values * factor, axis=0)


def gelu_parts(values):
    inner = gelu_coeff * (values + 0.044715 * values * values * values)
    return jnp.tanh(inner)


def rotary_rows(positions):
    half_dim = HEAD_SIZE // 2
    frequency = jnp.exp(
        jnp.arange(half_dim, dtype=f32) * (-2.0 * math.log(rope_base) / HEAD_SIZE)
    )
    angles = positions.astype(f32)[:, None] * frequency[None, :]
    return jnp.cos(angles), jnp.sin(angles)


def ring_place(index, size):
    return jnp.where(index % 2 == 0, index // 2, size - 1 - index // 2)


def ring_index(place, size):
    return jnp.where(place < size // 2, 2 * place, 2 * (size - 1 - place) + 1)


def ring_perms(size):
    order = list(range(0, size, 2)) + list(range(size - 1, 0, -2))
    up = [
        (base + order[i], base + order[(i + 1) % size])
        for base in range(0, lax.axis_size("wide"), size)
        for i in range(size)
    ]
    return up, [(b, a) for a, b in up]


def ring_offsets(size):
    out = [0]
    for k in range(1, size // 2):
        out += [-k, k]
    return out + [size // 2]


class Clock:
    def __init__(self, token):
        self.token = token

    def sync(self, *arrays):
        *arrays, self.token = lax.optimization_barrier(tuple(arrays) + (self.token,))
        return arrays

    def hold(self, value):
        return lax.optimization_barrier((value, self.token))[0]


def hop(a, b, size):
    up, down = ring_perms(size)
    return lax.ppermute(a, "wide", up), lax.ppermute(b, "wide", down)


def low_sum(*terms):
    return sum(t.astype(f32) for t in terms).astype(bf16)


def halves(value):
    half = value.shape[0] // 2
    return value[:half], value[half:]


def add_first(whole, part):
    count = part.shape[0]
    return jnp.concatenate([low_sum(whole[:count], part), whole[count:].astype(bf16)], axis=0)


def add_last(whole, part):
    count = whole.shape[0] - part.shape[0]
    return jnp.concatenate([whole[:count].astype(bf16), low_sum(whole[count:], part)], axis=0)


def ring_gather(clock, value, size, beside=lambda step: ()):
    a = b = clock.hold(value)
    out, other = [a], []
    for k in range(1, size // 2 + 1):
        if k == size // 2:
            a, b = halves(a)[0], halves(b)[1]
        work = beside(k - 1)
        a, b = hop(a, b, size)
        a, b, *work = clock.sync(a, b, *work)
        out += [a, b]
        other.append(work)
    return out, other


def ring_scatter(clock, part_of, rows, size, beside=lambda step: ()):
    a, b = halves(clock.hold(part_of(size // 2).astype(bf16)))
    other = []
    for k in range(size // 2 - 1, -1, -1):
        work = beside(size // 2 - 1 - k)
        a, b = hop(a, b, size)
        a, b, *work = clock.sync(a, b, *work)
        other.append(work)
        if k == size // 2 - 1 and k > 0:
            a = add_first(part_of(k), a)
            b = add_last(part_of(-k), b)
        elif k > 0:
            a = low_sum(part_of(k), a)
            b = low_sum(part_of(-k), b)
    return part_of(0).astype(f32) + a.astype(f32) + b.astype(f32), other


def swap(value, axis, bit):
    size = lax.axis_size(axis)
    return lax.ppermute(value, axis, [(i, i ^ bit) for i in range(size)])


def all_to_all(value):
    return lax.all_to_all(value, "wide", split_axis=0, concat_axis=0, tiled=True)


def heads_all_to_all(value):
    size = lax.axis_size("wide")
    classes = size // KEY_VALUE_HEADS
    groups = [list(range(c, size, classes)) for c in range(classes)]
    return lax.all_to_all(
        value, "wide", split_axis=0, concat_axis=0, axis_index_groups=groups, tiled=True
    )


def class_ring(value):
    size = lax.axis_size("wide")
    classes = size // KEY_VALUE_HEADS
    perm = [(i, i // classes * classes + (i + 1) % classes) for i in range(size)]
    return lax.ppermute(value, "wide", perm)


def slice_values(codes, width):
    lift = jnp.where(width == 0, 0.0, 0.5).astype(bf16)
    large = jnp.where(width == 0, 0.0, jnp.where(width == 1, 1.5 * 2**11, 1.5 * 2**13)).astype(bf16)
    top = jnp.where(width == 0, 127.0, jnp.where(width == 1, 112.0, 64.0)).astype(bf16)
    return jnp.minimum(((codes + lift) + large) - large, top)


def proj_slice_kernel(places, info, *refs, blocks, count):
    code_refs, scale_ref, out_refs = refs[: 2 * blocks], refs[2 * blocks], refs[len(refs) - count :]
    mine = pl.program_id(1) == info[0]

    def write(code_ref):
        codes = code_ref[...]
        scale = scale_ref[...].astype(bf16)
        for s, out_ref in enumerate(out_refs):
            out_ref[...] = slice_values(codes, info[1 + s]) * scale

    for k in range(blocks):
        here = pl.program_id(0) == k
        pl.when(jnp.logical_and(here, mine))(functools.partial(write, code_refs[2 * k]))
        pl.when(jnp.logical_and(here, jnp.logical_not(mine)))(
            functools.partial(write, code_refs[2 * k + 1])
        )


def proj_slices(own, other, places, info, scale, width, weights, total, count):
    blocks = len(own)
    rows = own[0].shape[0]
    inputs = [block for pair in zip(own, other) for block in pair] + [scale]
    grid_spec = pltpu.PrefetchScalarGridSpec(
        num_scalar_prefetch=2,
        grid=(blocks, 2),
        in_specs=[pl.BlockSpec((rows, width), lambda k, j, p, i: (0, 0))] * (2 * blocks)
        + [pl.BlockSpec((1, width), lambda k, j, p, i: (0, j))]
        + [pl.BlockSpec(memory_space=pl.ANY)] * len(weights),
        out_specs=[pl.BlockSpec((rows, width), lambda k, j, p, i: (p[k], j))] * count,
    )
    return pl.pallas_call(
        functools.partial(proj_slice_kernel, blocks=blocks, count=count),
        grid_spec=grid_spec,
        out_shape=[jax.ShapeDtypeStruct((total * rows, 2 * width), bf16)] * count,
        input_output_aliases={2 + len(inputs) + s: s for s in range(len(weights))},
        compiler_params=pltpu.CompilerParams(vmem_limit_bytes=VMEM_LIMIT),
        cost_estimate=pl.CostEstimate(
            flops=20 * count * blocks * rows * width,
            bytes_accessed=4 * blocks * rows * width * (1 + count),
            transcendentals=0,
        ),
        name="proj_slices",
    )(places, info, *inputs, *weights)


def out_slice_kernel(places, info, *refs, split, count):
    inputs, scale_ref, out_refs = refs[: -1 - count], refs[-1 - count], refs[-count:]
    members = len(inputs) // 2
    member = info[1 + count]
    mine = pl.program_id(1) == info[0]

    def write(code_refs):
        scale = scale_ref[...].astype(bf16)
        for t, code_ref in enumerate(code_refs):
            first = pl.multiple_of(jnp.bitwise_xor(member, t) * split, 128)
            for s, out_ref in enumerate(out_refs):
                out_ref[:, pl.ds(first, split)] = slice_values(code_ref[0], info[1 + s]) * scale

    pl.when(mine)(lambda: write(inputs[:members]))
    pl.when(jnp.logical_not(mine))(lambda: write(inputs[members:]))


def out_slices(own, other, places, info, scale, count):
    blocks, rows, split = own[0].shape
    width = split * len(own)
    inputs = list(own) + list(other)
    grid_spec = pltpu.PrefetchScalarGridSpec(
        num_scalar_prefetch=2,
        grid=(blocks, 2),
        in_specs=[pl.BlockSpec((1, rows, split), lambda k, j, p, i: (k, 0, 0))] * len(inputs)
        + [pl.BlockSpec((rows, 1), lambda k, j, p, i: (p[k], 0))],
        out_specs=[pl.BlockSpec((rows, width), lambda k, j, p, i: (p[k], j))] * count,
    )
    return pl.pallas_call(
        functools.partial(out_slice_kernel, split=split, count=count),
        grid_spec=grid_spec,
        out_shape=[jax.ShapeDtypeStruct((blocks * rows, 2 * width), bf16)] * count,
        compiler_params=pltpu.CompilerParams(vmem_limit_bytes=VMEM_LIMIT),
        cost_estimate=pl.CostEstimate(
            flops=20 * count * blocks * rows * width,
            bytes_accessed=4 * blocks * rows * width * (1 + count),
            transcendentals=0,
        ),
        name="out_slices",
    )(places, info, *inputs, scale)


def own_slice_kernel(pieces, info, code_ref, row_ref, col_ref, *out_refs):
    count = len(out_refs) // 3
    for m in range(3):
        codes = code_ref[m].astype(f32).astype(bf16)
        scale = (row_ref[m] if m < 2 else col_ref[...]).astype(bf16)
        for s in range(count):
            out_refs[m * count + s][...] = slice_values(codes, info[1 + s]) * scale


def own_slices(codes, pieces, info, row_scale, col_scale, count):
    three, rows, cols = codes.shape
    steps = pieces.shape[0]
    piece = rows // steps
    grid_spec = pltpu.PrefetchScalarGridSpec(
        num_scalar_prefetch=2,
        grid=(steps,),
        in_specs=[
            pl.BlockSpec((three, piece, cols), lambda j, p, i: (0, p[j], 0)),
            pl.BlockSpec((2, piece, 1), lambda j, p, i: (0, j, 0)),
            pl.BlockSpec((1, cols), lambda j, p, i: (0, 0)),
        ],
        out_specs=[pl.BlockSpec((piece, cols), lambda j, p, i: (j, 0))] * (three * count),
    )
    return pl.pallas_call(
        own_slice_kernel,
        grid_spec=grid_spec,
        out_shape=[jax.ShapeDtypeStruct((2 * rows, cols), bf16)] * (three * count),
        compiler_params=pltpu.CompilerParams(vmem_limit_bytes=VMEM_LIMIT),
        cost_estimate=pl.CostEstimate(
            flops=10 * count * codes.size,
            bytes_accessed=codes.size * (4 + 2 * count),
            transcendentals=0,
        ),
        name="own_slices",
    )(pieces, info, codes, row_scale, col_scale)


def partner_slice_kernel(info, *refs, steps, count):
    piece_refs, scale_ref, out_refs = refs[:steps], refs[steps], refs[steps + 1 + count :]
    for j in range(steps):

        @pl.when(pl.program_id(0) == j)
        def _():
            codes = piece_refs[j][...]
            scale = scale_ref[...].astype(bf16)
            for s, out_ref in enumerate(out_refs):
                out_ref[...] = slice_values(codes, info[1 + s]) * scale


def partner_slices(pieces, info, scale, by_column, weights):
    steps = len(pieces)
    count = len(weights)
    piece, cols = pieces[0].shape
    if by_column:
        scale_spec = pl.BlockSpec((1, cols), lambda j, i: (0, 0))
    else:
        scale_spec = pl.BlockSpec((piece, 1), lambda j, i: (steps + j, 0))
    grid_spec = pltpu.PrefetchScalarGridSpec(
        num_scalar_prefetch=1,
        grid=(steps,),
        in_specs=[pl.BlockSpec((piece, cols), lambda j, i: (0, 0))] * steps
        + [scale_spec]
        + [pl.BlockSpec(memory_space=pl.ANY)] * count,
        out_specs=[pl.BlockSpec((piece, cols), lambda j, i: (steps + j, 0))] * count,
    )
    return pl.pallas_call(
        functools.partial(partner_slice_kernel, steps=steps, count=count),
        grid_spec=grid_spec,
        out_shape=[jax.ShapeDtypeStruct(w.shape, bf16) for w in weights],
        input_output_aliases={2 + steps + s: s for s in range(count)},
        compiler_params=pltpu.CompilerParams(vmem_limit_bytes=VMEM_LIMIT),
        cost_estimate=pl.CostEstimate(
            flops=10 * count * steps * piece * cols,
            bytes_accessed=2 * (1 + count) * steps * piece * cols,
            transcendentals=0,
        ),
        name="partner_slices",
    )(info, *pieces, scale, *weights)


def unpack_kernel(pieces, grad_ref, *refs):
    refs[-1][0] = grad_ref[...].astype(f32)


def unpack(grad, pieces, matrix, held):
    steps = pieces.shape[0]
    rows, cols = grad.shape
    piece = rows // steps
    grid_spec = pltpu.PrefetchScalarGridSpec(
        num_scalar_prefetch=1,
        grid=(steps,),
        in_specs=[pl.BlockSpec((piece, cols), lambda j, p: (j, 0))]
        + [pl.BlockSpec(memory_space=pl.ANY)] * len(held),
        out_specs=pl.BlockSpec((1, piece, cols), lambda j, p: (matrix, p[j], 0)),
    )
    return pl.pallas_call(
        unpack_kernel,
        grid_spec=grid_spec,
        out_shape=jax.ShapeDtypeStruct((3, rows, cols), f32),
        input_output_aliases={2: 0} if held else {},
        compiler_params=pltpu.CompilerParams(vmem_limit_bytes=VMEM_LIMIT),
        cost_estimate=pl.CostEstimate(
            flops=rows * cols, bytes_accessed=6 * rows * cols, transcendentals=0
        ),
        name="unpack",
    )(pieces, grad, *held)


def turn(values, cosine, sine):
    half = HEAD_SIZE // 2
    out = []
    for j in range(values.shape[1] // HEAD_SIZE):
        a = values[:, j * HEAD_SIZE : j * HEAD_SIZE + half]
        b = values[:, j * HEAD_SIZE + half : (j + 1) * HEAD_SIZE]
        out += [a * cosine - b * sine, b * cosine + a * sine]
    return jnp.concatenate(out, axis=1)


def project_kernel(x_ref, wq_ref, wk_ref, wv_ref, cos_ref, sin_ref, q_ref, kv_ref):
    x = x_ref[...]
    cosine, sine = cos_ref[...], sin_ref[...]
    scale = HEAD_SIZE ** (-0.5)
    q_ref[0] = (turn(dot(x, wq_ref[...], NN), cosine, sine) * scale).astype(bf16)
    kv_ref[0, :, :HEAD_SIZE] = turn(dot(x, wk_ref[...], NN), cosine, sine).astype(bf16)
    kv_ref[0, :, HEAD_SIZE:] = dot(x, wv_ref[...], NN).astype(bf16)


def project(normed, weights, cosine, sine):
    rows, depth = normed.shape
    cols = PAIRED * HEAD_SIZE
    first_key = QUERY_HEADS
    first_value = QUERY_HEADS + KEY_VALUE_HEADS
    whole = lambda shape: pl.BlockSpec(shape, lambda h: (0, 0))
    return pl.pallas_call(
        project_kernel,
        grid=(KEY_VALUE_HEADS,),
        in_specs=[
            whole((rows, depth)),
            pl.BlockSpec((depth, cols), lambda h: (0, h)),
            pl.BlockSpec((depth, HEAD_SIZE), lambda h: (0, first_key + h)),
            pl.BlockSpec((depth, HEAD_SIZE), lambda h: (0, first_value + h)),
            whole(cosine.shape),
            whole(sine.shape),
        ],
        out_specs=[
            pl.BlockSpec((1, rows, cols), lambda h: (h, 0, 0)),
            pl.BlockSpec((1, rows, 2 * HEAD_SIZE), lambda h: (h, 0, 0)),
        ],
        out_shape=[
            jax.ShapeDtypeStruct((KEY_VALUE_HEADS, rows, cols), bf16),
            jax.ShapeDtypeStruct((KEY_VALUE_HEADS, rows, 2 * HEAD_SIZE), bf16),
        ],
        compiler_params=pltpu.CompilerParams(vmem_limit_bytes=VMEM_LIMIT),
        cost_estimate=pl.CostEstimate(
            flops=2 * rows * weights.size, bytes_accessed=2 * weights.size, transcendentals=0
        ),
        name="project",
    )(normed, weights, weights, weights, cosine, sine)


def turn_back_kernel(*refs, count):
    q_refs, kv_refs = refs[:count], refs[count : 2 * count]
    cos_ref, sin_ref, out_ref = refs[2 * count :]
    j = pl.program_id(1)
    scale = HEAD_SIZE ** (-0.5)
    keys = KEY_VALUE_HEADS // PAIRED
    for s in range(count):
        here = pl.program_id(0) == s

        @pl.when(jnp.logical_and(here, j < KEY_VALUE_HEADS))
        def _():
            grad = q_refs[s][0].astype(f32) * scale
            out_ref[...] = turn(grad, cos_ref[...], -sin_ref[...]).astype(bf16)

        @pl.when(jnp.logical_and(here, jnp.logical_and(j >= KEY_VALUE_HEADS, j < KEY_VALUE_HEADS + keys)))
        def _():
            grad = jnp.concatenate([kv_refs[s][i, :, :HEAD_SIZE] for i in range(PAIRED)], axis=1)
            out_ref[...] = turn(grad.astype(f32), cos_ref[...], -sin_ref[...]).astype(bf16)

        @pl.when(jnp.logical_and(here, j >= KEY_VALUE_HEADS + keys))
        def _():
            out_ref[...] = jnp.concatenate(
                [kv_refs[s][i, :, HEAD_SIZE:] for i in range(PAIRED)], axis=1
            )


def turn_back(queries, pairs, cosine, sine):
    count = len(queries)
    heads, rows, cols = queries[0].shape
    keys = heads // PAIRED
    grid = (count, heads + 2 * keys)
    whole = pl.BlockSpec(cosine.shape, lambda s, j: (0, 0))
    return pl.pallas_call(
        functools.partial(turn_back_kernel, count=count),
        grid=grid,
        in_specs=[
            pl.BlockSpec((1, rows, cols), lambda s, j: (jnp.minimum(j, heads - 1), 0, 0))
        ]
        * count
        + [
            pl.BlockSpec(
                (PAIRED, rows, cols), lambda s, j: (jnp.maximum(j - heads, 0) % keys, 0, 0)
            )
        ]
        * count
        + [whole, whole],
        out_specs=pl.BlockSpec((rows, cols), lambda s, j: (s, j)),
        out_shape=jax.ShapeDtypeStruct((count * rows, grid[1] * cols), bf16),
        compiler_params=pltpu.CompilerParams(vmem_limit_bytes=VMEM_LIMIT),
        cost_estimate=pl.CostEstimate(
            flops=4 * count * rows * grid[1] * cols,
            bytes_accessed=4 * count * rows * grid[1] * cols,
            transcendentals=0,
        ),
        name="turn_back",
    )(*queries, *pairs, cosine, sine)


def tile_positions(tile, count, start, class_index, class_rows, rows):
    index = lax.broadcasted_iota(jnp.int32, (count, 1), 0)
    place = start + jnp.bitwise_and(index, tile - 1)
    shift = class_rows.bit_length() - 1
    return (
        jnp.right_shift(place, shift) * rows
        + class_index * class_rows
        + jnp.bitwise_and(place, class_rows - 1)
    )


def stack_heads(block):
    return jnp.concatenate(
        [block[:, j * HEAD_SIZE : (j + 1) * HEAD_SIZE] for j in range(PAIRED)], axis=0
    )


def key_places(group, class_index, classes, rows):
    index = lax.broadcasted_iota(jnp.int32, (1, classes * rows), 1)
    shift = rows.bit_length() - 1
    back = jnp.bitwise_and(class_index - jnp.right_shift(index, shift), classes - 1)
    return (group * classes + back) * rows + jnp.bitwise_and(index, rows - 1)


def held_block(refs, group, cols):
    return jnp.concatenate([ref[group, :, cols] for ref in refs], axis=0)


def group_range(start, tile, class_rows, classes):
    return start // class_rows // classes, (start + tile - 1) // class_rows // classes + 1


def attn_forward_kernel(info, q_ref, *refs, tile, class_rows, rows, classes):
    kv_refs = refs[:classes]
    att_ref, exact_ref, lse_ref = refs[classes:]
    start = pl.program_id(0) * tile
    free, total = group_range(start, tile, class_rows, classes)
    queries = stack_heads(q_ref[...])
    count = queries.shape[0]
    position = tile_positions(tile, count, start, info[0], class_rows, rows)

    def step(group, carry, masked):
        acc, row_sum = carry
        keys = held_block(kv_refs, group, slice(0, HEAD_SIZE))
        values = held_block(kv_refs, group, slice(HEAD_SIZE, 2 * HEAD_SIZE))
        raw = dot(queries, keys, NT)
        weight = jnp.exp(soft_cap * jnp.tanh(raw * (1.0 / soft_cap)))
        if masked:
            weight = jnp.where(
                key_places(group, info[0], classes, rows) <= position, weight, 0.0
            )
        row_sum = row_sum + jnp.sum(weight, axis=-1, keepdims=True)
        acc = acc + dot(weight.astype(bf16), values, NN)
        return acc, row_sum

    carry = (jnp.zeros((count, HEAD_SIZE), f32), jnp.zeros((count, 1), f32))
    carry = lax.fori_loop(0, free, functools.partial(step, masked=False), carry)
    acc, row_sum = lax.fori_loop(free, total, functools.partial(step, masked=True), carry)
    exact = acc / row_sum
    lse = jnp.log(row_sum)
    for j in range(PAIRED):
        cols = slice(j * HEAD_SIZE, (j + 1) * HEAD_SIZE)
        exact_ref[:, cols] = exact[j * tile : (j + 1) * tile]
        att_ref[:, cols] = exact[j * tile : (j + 1) * tile].astype(bf16)
        lse_ref[:, j * 128 : (j + 1) * 128] = jnp.broadcast_to(
            lse[j * tile : (j + 1) * tile], (tile, 128)
        )


def attn_forward(info, queries, pairs, class_rows, rows):
    count, cols = queries.shape
    classes = len(pairs)
    length = classes * pairs[0].shape[0] * rows
    tile = min(256, count)
    grid_spec = pltpu.PrefetchScalarGridSpec(
        num_scalar_prefetch=1,
        grid=(count // tile,),
        in_specs=[pl.BlockSpec((tile, cols), lambda i, c: (i, 0))]
        + [pl.BlockSpec(p.shape, lambda i, c: (0, 0, 0)) for p in pairs],
        out_specs=[
            pl.BlockSpec((tile, cols), lambda i, c: (i, 0)),
            pl.BlockSpec((tile, cols), lambda i, c: (i, 0)),
            pl.BlockSpec((tile, PAIRED * 128), lambda i, c: (i, 0)),
        ],
    )
    return pl.pallas_call(
        functools.partial(
            attn_forward_kernel, tile=tile, class_rows=class_rows, rows=rows, classes=classes
        ),
        grid_spec=grid_spec,
        out_shape=[
            jax.ShapeDtypeStruct((count, cols), bf16),
            jax.ShapeDtypeStruct((count, cols), f32),
            jax.ShapeDtypeStruct((count, PAIRED * 128), f32),
        ],
        compiler_params=pltpu.CompilerParams(vmem_limit_bytes=VMEM_LIMIT),
        cost_estimate=pl.CostEstimate(
            flops=2 * count * PAIRED * length * 2 * HEAD_SIZE,
            bytes_accessed=8 * count * cols + 4 * length * HEAD_SIZE,
            transcendentals=2 * count * PAIRED * length,
        ),
        name="attn_forward",
    )(info, queries, *pairs)


def attn_backward_kernel(info, q_ref, grad_ref, exact_ref, lse_ref, *refs, tile, class_rows, rows, classes):
    kv_refs, dq_ref = refs[:classes], refs[classes]
    dkv_refs, sum_ref = refs[classes + 1 : 2 * classes + 1], refs[2 * classes + 1]

    @pl.when(pl.program_id(0) == 0)
    def _():
        sum_ref[...] = jnp.zeros_like(sum_ref)

    start = pl.program_id(0) * tile
    free, total = group_range(start, tile, class_rows, classes)
    queries = stack_heads(q_ref[...])
    grads = stack_heads(grad_ref[...])
    count = queries.shape[0]
    delta = jnp.sum(grads.astype(f32) * stack_heads(exact_ref[...]), axis=-1, keepdims=True)
    lse = jnp.concatenate([lse_ref[:, j * 128 : j * 128 + 1] for j in range(PAIRED)], axis=0)
    position = tile_positions(tile, count, start, info[0], class_rows, rows)

    def step(group, acc, masked):
        keys = held_block(kv_refs, group, slice(0, HEAD_SIZE))
        values = held_block(kv_refs, group, slice(HEAD_SIZE, 2 * HEAD_SIZE))
        bounded = jnp.tanh(dot(queries, keys, NT) * (1.0 / soft_cap))
        probs = jnp.exp(soft_cap * bounded - lse)
        if masked:
            probs = jnp.where(key_places(group, info[0], classes, rows) <= position, probs, 0.0)
        grad_probs = dot(grads, values, NT)
        grad_raw = (probs * (grad_probs - delta) * (1.0 - bounded * bounded)).astype(bf16)
        sum_ref[group, :, HEAD_SIZE:] += dot(probs.astype(bf16), grads, TN)
        sum_ref[group, :, :HEAD_SIZE] += dot(grad_raw, queries, TN)
        return acc + dot(grad_raw, keys, NN)

    acc = jnp.zeros((count, HEAD_SIZE), f32)
    acc = lax.fori_loop(0, free, functools.partial(step, masked=False), acc)
    acc = lax.fori_loop(free, total, functools.partial(step, masked=True), acc)
    for j in range(PAIRED):
        dq_ref[:, j * HEAD_SIZE : (j + 1) * HEAD_SIZE] = acc[j * tile : (j + 1) * tile].astype(bf16)

    @pl.when(pl.program_id(0) == pl.num_programs(0) - 1)
    def _():
        for h, ref in enumerate(dkv_refs):
            ref[...] = sum_ref[:, h * rows : (h + 1) * rows, :].astype(bf16)


def attn_backward(info, queries, pairs, grads, exact, lse, class_rows, rows):
    count, cols = queries.shape
    classes = len(pairs)
    groups = pairs[0].shape[0]
    length = classes * groups * rows
    tile = min(256, count)
    row_spec = pl.BlockSpec((tile, cols), lambda i, c: (i, 0))
    pair_specs = [pl.BlockSpec(p.shape, lambda i, c: (0, 0, 0)) for p in pairs]
    grid_spec = pltpu.PrefetchScalarGridSpec(
        num_scalar_prefetch=1,
        grid=(count // tile,),
        in_specs=[
            row_spec,
            row_spec,
            row_spec,
            pl.BlockSpec((tile, PAIRED * 128), lambda i, c: (i, 0)),
        ]
        + pair_specs,
        out_specs=[row_spec] + pair_specs,
        scratch_shapes=[pltpu.VMEM((groups, classes * rows, 2 * HEAD_SIZE), f32)],
    )
    return pl.pallas_call(
        functools.partial(
            attn_backward_kernel, tile=tile, class_rows=class_rows, rows=rows, classes=classes
        ),
        grid_spec=grid_spec,
        out_shape=[jax.ShapeDtypeStruct((count, cols), bf16)]
        + [jax.ShapeDtypeStruct(p.shape, bf16) for p in pairs],
        compiler_params=pltpu.CompilerParams(vmem_limit_bytes=VMEM_LIMIT),
        cost_estimate=pl.CostEstimate(
            flops=5 * count * PAIRED * length * 2 * HEAD_SIZE,
            bytes_accessed=10 * count * cols + 8 * length * HEAD_SIZE,
            transcendentals=2 * count * PAIRED * length,
        ),
        name="attn_backward",
    )(info, queries, grads, exact, lse, *pairs)


def per_device(
    tokens,
    cotangent,
    widths,
    attn_codes,
    attn_exps,
    out_exps,
    mlp_codes,
    gate_exps,
    down_exps,
    gain_attn,
    gain_post_attn,
    gain_mlp,
    gain_post_mlp,
):
    wide = lax.axis_size("wide")
    seq_size = lax.axis_size("seq")
    wide_index = lax.axis_index("wide")
    seq_index = lax.axis_index("seq")
    side = seq_index % 2
    is_low = side == 0
    members = seq_size // 2
    member = seq_index // 2
    half_wide = wide // 2
    place = ring_place(wide_index, wide)
    count, rows, model_dim = tokens.shape
    classes = wide // KEY_VALUE_HEADS
    class_rows = rows // classes
    class_index = wide_index % classes
    head_cols = PAIRED * HEAD_SIZE
    proj_cols = attn_exps.shape[0]
    half_proj = proj_cols // 2
    half_out = (attn_codes.shape[1] - proj_cols) // 2
    split_out = half_out // members
    attn_rows = attn_codes.shape[0]
    hidden = mlp_codes.shape[1]
    offsets = ring_offsets(wide)
    order = {o: i for i, o in enumerate(ring_offsets(half_wide))}
    seqs = range(count)
    seq_bits = [1 << i for i in range(seq_size.bit_length() - 1)]
    far_bits = list(reversed(seq_bits[1:]))
    clock = Clock(widths)

    def index_at(offset):
        return ring_index(jnp.mod(place + offset, wide), wide)

    places = jnp.stack([index_at(o) for o in offsets]).astype(jnp.int32)
    info = jnp.concatenate(
        [side[None].astype(jnp.int32), widths, member[None].astype(jnp.int32)]
    )
    class_info = class_index[None].astype(jnp.int32)
    column_scale = inverse_powers(attn_exps)[None, :]
    output_scale = inverse_powers(out_exps)[:, None]

    relative = [0]
    for bit in reversed(seq_bits):
        relative = relative + [r | bit for r in relative]
    pieces = jnp.stack([jnp.bitwise_xor(seq_index, r) for r in relative]).astype(jnp.int32)
    piece_rows = hidden // seq_size
    partner = jnp.bitwise_xor(wide_index, half_wide)
    gate_scale = inverse_powers(gate_exps)
    row_scale = jnp.concatenate(
        [
            lax.dynamic_slice_in_dim(
                gate_scale, block * hidden + pieces[j] * piece_rows, piece_rows, 1
            )
            for block in (wide_index, partner)
            for j in range(seq_size)
        ],
        axis=1,
    )[:, :, None]
    down_scale = inverse_powers(down_exps)[None, :]

    def columns(first, size):
        return lax.dynamic_slice_in_dim(attn_codes, first, size, 1)

    payload = jnp.concatenate(
        [
            columns(side * half_proj, half_proj),
            columns(proj_cols + side * half_out + member * split_out, split_out),
        ],
        axis=1,
    ).astype(bf16)
    piece_codes = lax.dynamic_slice_in_dim(mlp_codes, seq_index * piece_rows, piece_rows, 1)
    inputs = [tokens[s].astype(f32) for s in seqs]
    grad_out = [cotangent[s].astype(f32) for s in seqs]
    cosine, sine = rotary_rows(wide_index * rows + jnp.arange(rows))

    blocks, others = [clock.hold(payload)], []
    proj_weights = []

    def slice_more(first, last):
        return proj_slices(
            blocks[first:last],
            others[first:last],
            places[first:last],
            info,
            column_scale,
            half_proj,
            proj_weights,
            wide,
            count,
        )

    a = b = blocks[0]
    sliced = 0
    steps = half_wide
    for k in range(1, steps + 1):
        if k == steps:
            a, b = halves(a)[0], halves(b)[1]
        passed = [swap(v, "seq", 1) for v in blocks[len(others) :]]
        a, b = hop(a, b, wide)
        work = []
        if k == 1:
            work = own_slices(mlp_codes, pieces, info, row_scale, down_scale, count)
            a, b, *work = clock.sync(a, b, *passed, *work)
            passed, own_weights = work[: len(passed)], work[len(passed) :]
        elif k == 2:
            work = [piece_codes[m].astype(bf16) for m in range(3)]
            for s in seqs:
                factor = norm_factor(clock.hold(inputs[s]))
                work += [factor, (inputs[s] * factor * gain_attn).astype(bf16)]
            a, b, *work = clock.sync(a, b, *passed, *work)
            passed, work = work[: len(passed)], work[len(passed) :]
            sends, work = work[:3], work[3:]
            input_factor, normed = work[0::2], work[1::2]
        else:
            more = len(others)
            work = slice_more(sliced, more) if more > sliced else []
            a, b, *work = clock.sync(a, b, *passed, *work)
            passed, work = work[: len(passed)], work[len(passed) :]
            if work:
                proj_weights, sliced = list(work), more
        others += passed
        blocks += [a, b] if k < steps else [jnp.concatenate([a, b], axis=0)]

    def exchange(m):
        return swap(clock.hold(sends[m]), "wide", half_wide)

    def share(held, bits):
        for bit in bits:
            held = held + [swap(value, "seq", bit) for value in held]
        return held

    def partner_weights(m, held):
        scale = row_scale[m] if m < 2 else down_scale
        return partner_slices(
            held, info, scale, m == 2, own_weights[m * count : (m + 1) * count]
        )

    received = exchange(0)
    others += [swap(clock.hold(v), "seq", 1) for v in blocks[len(others) :]]
    proj_weights = slice_more(sliced, wide)
    query_send, pair_send = [], []
    for s in seqs:
        query, pair = project(normed[s], proj_weights[s], cosine, sine)
        query_send.append(query.reshape(wide, class_rows, head_cols))
        pair_send.append(pair)
    own_out = jnp.stack([clock.hold(v)[:, half_proj:] for v in blocks])
    other_out = jnp.stack([v[:, half_proj:] for v in others])
    out_own = share([own_out], far_bits)
    sent = clock.sync(received, *query_send, *pair_send, *out_own)
    received, sent = sent[0], sent[1:]
    query_send, pair_send, out_own = sent[:count], sent[count : 2 * count], sent[2 * count :]

    def start_spread(pair):
        held = [pair]
        for _ in range(classes - 1):
            held.append(class_ring(held[-1]))
        return held

    attended_send, exact, lse, queries, pairs = [], [], [], [], []

    def attend(s):
        out, full, log_sum = attn_forward(class_info, queries[s], pairs[s], class_rows, rows)
        return [out.reshape(wide, class_rows, head_cols), full, log_sum]

    def keep_attend(work):
        attended_send.append(work[0])
        exact.append(work[1])
        lse.append(work[2])

    out_other = [other_out] + [swap(v, "seq", 1) for v in out_own[1:]]
    pair = heads_all_to_all(clock.hold(pair_send[0]))
    gate_held = share([clock.hold(received)], far_bits)
    pair, *work = clock.sync(pair, *gate_held, *out_other)
    gate_held, out_other = work[: len(gate_held)], work[len(gate_held) :]
    for s in seqs[1:]:
        spread = start_spread(pair)
        pair = heads_all_to_all(clock.hold(pair_send[s]))
        work = []
        if s == 1:
            gate_held = share(gate_held, seq_bits[:1])
            work = out_slices(out_own, out_other, places, info, output_scale, count)
        pair, *rest = clock.sync(pair, *spread, *work, *gate_held)
        pairs.append(rest[:classes])
        if s == 1:
            out_weights = rest[classes : classes + count]
            gate_held = rest[classes + count :]
    spread = start_spread(pair)
    for s in seqs:
        query = all_to_all(clock.hold(query_send[s]))
        if s == 0:
            query, *rest = clock.sync(query, *spread)
            pairs.append(rest)
        else:
            query, *rest = clock.sync(query, *attend(s - 1))
            keep_attend(rest)
        queries.append(query.reshape(wide * class_rows, head_cols))

    attended, branch, branch_factor, middle, middle_factor, normed_mlp = [], [], [], [], [], []

    def heads_to_rows(values):
        split = values.reshape(KEY_VALUE_HEADS, rows, head_cols)
        return jnp.transpose(split, (1, 0, 2)).reshape(rows, KEY_VALUE_HEADS * head_cols)

    def join(s):
        value = dot(attended[s], out_weights[s], NT)
        factor = norm_factor(value)
        mid = inputs[s] + value * factor * gain_post_attn
        mid_factor = norm_factor(mid)
        return [value, factor, mid, mid_factor, (mid * mid_factor * gain_mlp).astype(bf16)]

    def keep_join(work):
        for held, value in zip((branch, branch_factor, middle, middle_factor, normed_mlp), work):
            held.append(value)

    for s in seqs:
        back = all_to_all(clock.hold(attended_send[s]))
        if s == 0:
            gate_weights = partner_weights(0, [clock.hold(v) for v in gate_held])
            back, *work = clock.sync(back, *attend(count - 1), *gate_weights)
            keep_attend(work[:3])
            gate_weights = work[3:]
        else:
            back, *work = clock.sync(back, *join(s - 1))
            keep_join(work)
        attended.append(heads_to_rows(back))

    received, *work = clock.sync(exchange(1), *join(count - 1))
    keep_join(work)

    def blocks_of(part):
        return lambda o: part[order[o] * rows : (order[o] + 1) * rows]

    gathered, gate, up, hidden_rows, mixed, parts = [], [], [], [], [], []

    def open_gate(s):
        return dot(clock.hold(gathered[s]), gate_weights[s], NT)

    def open_up(s):
        up_s = dot(clock.hold(gathered[s]), up_weights[s], NT)
        hidden_s = (0.5 * gate[s] * (1.0 + gelu_parts(gate[s])) * up_s).astype(bf16)
        return [up_s, hidden_s]

    def keep_up(work):
        up.append(work[0])
        hidden_rows.append(work[1])

    def mix(s):
        return dot(clock.hold(hidden_rows[s]), down_weights[s], NN).astype(bf16)

    def staged_share(received):
        held = [received]

        def beside(step):
            nonlocal held
            if step == 0:
                held = share([clock.hold(held[0])], far_bits)
            elif step == 1:
                held = share(held, seq_bits[:1])
            return tuple(held)

        def keep(work):
            nonlocal held
            held = work

        return beside, keep, lambda: held

    def shared_gather(value, received):
        beside, keep, result = staged_share(received)
        a = b = clock.hold(value)
        out = [a]
        for k in range(1, half_wide // 2 + 1):
            if k == half_wide // 2:
                a, b = halves(a)[0], halves(b)[1]
            work = beside(k - 1) if k <= 2 else ()
            a, b = hop(a, b, half_wide)
            a, b, *work = clock.sync(a, b, *work)
            if work:
                keep(work)
            out += [a, b]
        return jnp.concatenate(out, axis=0), result()

    group, up_held = shared_gather(normed_mlp[0], received)
    gathered.append(group)
    received = exchange(2)
    gate.append(open_gate(0))
    up_weights = partner_weights(1, up_held)
    received, *work = clock.sync(received, *open_up(0), *up_weights, gate[0])
    keep_up(work[:2])
    up_weights = work[2 : 2 + count]
    gate[0] = work[-1]
    for s in seqs[1:]:
        group, down_held = shared_gather(normed_mlp[s], received)
        gathered.append(group)
    down_weights = partner_weights(2, down_held)
    parts.append(clock.sync(mix(0))[0])

    layer_out, grad_mixed, gain_fourth = [], [], 0.0

    def finish(s):
        nonlocal gain_fourth
        factor = norm_factor(mixed[s])
        layer_out.append((middle[s] + mixed[s] * factor * gain_post_mlp).astype(bf16))
        grad, gain = norm_back(mixed[s], factor, gain_post_mlp, grad_out[s])
        grad_mixed.append(grad.astype(bf16))
        gain_fourth = gain_fourth + gain

    grad_group, grad_gate, grad_up, grad_parts, grad_normed_mlp = [], [], [], [], []

    def back_hidden(s):
        grad_hidden = dot(clock.hold(grad_group[s]), down_weights[s], NT)
        bounded = gelu_parts(gate[s])
        gelu_value = 0.5 * gate[s] * (1.0 + bounded)
        slope = 0.5 * (1.0 + bounded) + 0.5 * gate[s] * (1.0 - bounded * bounded) * gelu_coeff * (
            1.0 + 3.0 * 0.044715 * gate[s] * gate[s]
        )
        return [(grad_hidden * up[s] * slope).astype(bf16), (grad_hidden * gelu_value).astype(bf16)]

    def back_input(s):
        return (
            dot(clock.hold(grad_gate[s]), gate_weights[s], NN)
            + dot(grad_up[s], up_weights[s], NN)
        ).astype(bf16)

    def keep_back(work):
        grad_gate.append(work[0])
        grad_up.append(work[1])

    def first_sum(part):
        a, b = hop(*halves(clock.hold(blocks_of(part)(half_wide // 2))), half_wide)
        return a, b

    def rest_sum(part, a, b, beside=lambda step: ()):
        part_of = blocks_of(part)
        other = []
        for k in range(half_wide // 2 - 1, 0, -1):
            if k == half_wide // 2 - 1:
                a = add_first(part_of(k), a)
                b = add_last(part_of(-k), b)
            else:
                a = low_sum(part_of(k), a)
                b = low_sum(part_of(-k), b)
            work = beside(half_wide // 2 - 1 - k)
            a, b = hop(a, b, half_wide)
            a, b, *work = clock.sync(a, b, *work)
            other.append(work)
        return part_of(0).astype(f32) + a.astype(f32) + b.astype(f32), other

    for s in seqs:
        a, b = first_sum(parts[s])
        if s + 1 < count:
            a, b, value = clock.sync(a, b, open_gate(s + 1))
            gate.append(value)
        else:
            a, b, *work = clock.sync(a, b, *back_hidden(0))
            keep_back(work)

        def beside(step, s=s):
            if step:
                return ()
            return tuple(open_up(s + 1)) if s + 1 < count else (back_input(0),)

        total, work = rest_sum(parts[s], a, b, beside)
        if s + 1 < count:
            keep_up(work[0])
        else:
            grad_parts.append(work[0][0])
        mixed.append(total)
        finish(s)
        if s + 1 < count:
            parts.append(mix(s + 1))
        if s == 0:
            blocks, work = ring_gather(
                clock, grad_mixed[0], half_wide, lambda k: (parts[-1],) if k == 0 else ()
            )
            parts[-1] = work[0][0]
            grad_group.append(jnp.concatenate(blocks, axis=0))

    def weight_first(left, right):
        return dot(clock.hold(left), right, TN)

    def weight_rest(first, lefts, rights):
        for s in seqs[1:]:
            first = first + dot(clock.hold(lefts[s]), rights[s], TN)
        return first.astype(bf16).reshape(2, hidden, model_dim)

    def part_sum(grad, bit):
        split = grad.reshape(2, 2, grad.shape[1] // 2, model_dim)
        return low_sum(split[:, 0], swap(split[:, 1], "seq", bit))

    grad_middle, grad_branch, grad_send = [], [], []
    gain_third = gain_second = 0.0

    def back_branch(s):
        nonlocal gain_third, gain_second
        grad, gain = norm_back(middle[s], middle_factor[s], gain_mlp, grad_normed_mlp[s])
        gain_third = gain_third + gain
        grad_mid = grad_out[s] + grad
        grad, gain = norm_back(branch[s], branch_factor[s], gain_post_attn, grad_mid)
        gain_second = gain_second + gain
        grad = grad.astype(bf16)
        send = dot(grad, out_weights[s], NN).astype(bf16)
        send = jnp.transpose(send.reshape(rows, KEY_VALUE_HEADS, head_cols), (1, 0, 2))
        return [grad_mid, grad, send.reshape(wide, class_rows, head_cols)]

    def keep_branch(work):
        grad_middle.append(work[0])
        grad_branch.append(work[1])
        grad_send.append(work[2])

    for s in seqs[1:]:
        blocks, work = ring_gather(
            clock,
            grad_mixed[s],
            half_wide,
            lambda k: (weight_first(hidden_rows[0], grad_group[0]),) if k == 0 and s == 1 else (),
        )
        if s == 1:
            down_first = work[0][0]
        grad_group.append(jnp.concatenate(blocks, axis=0))
    for s in seqs:
        a, b = first_sum(grad_parts[s])
        if s + 1 < count:
            a, b, *work = clock.sync(a, b, *back_hidden(s + 1))
            keep_back(work)
        else:
            a, b, *work = clock.sync(a, b, *back_branch(s - 1))
            keep_branch(work)

        def beside(step, s=s):
            if step:
                return ()
            if s + 1 < count:
                return (back_input(s + 1),)
            return (weight_rest(down_first, hidden_rows, grad_group),)

        total, work = rest_sum(grad_parts[s], a, b, beside)
        if s + 1 < count:
            grad_parts.append(work[0][0])
        else:
            down_grad = work[0][0]
        grad_normed_mlp.append(total)

    def attend_back(s):
        dq, *dkv = attn_backward(
            class_info,
            queries[s],
            pairs[s],
            clock.hold(grad_heads[s]),
            exact[s],
            lse[s],
            class_rows,
            rows,
        )
        return [dq.reshape(wide, class_rows, head_cols)] + dkv

    def class_sum(dkv):
        total = dkv[1 % classes]
        for step in range(2, classes + 1):
            total = low_sum(dkv[step % classes], class_ring(total))
        return total

    grad_heads, grad_attend = [], []
    for s in seqs:
        back = all_to_all(clock.hold(grad_send[s]))
        if s == 0:
            work = back_branch(count - 1)
            down_grad = part_sum(down_grad, 1)
            back, down_grad, *work = clock.sync(back, down_grad, *work)
            keep_branch(work)
        else:
            back, *work = clock.sync(back, *attend_back(s - 1))
            grad_attend.append(work)
        grad_heads.append(back.reshape(wide * class_rows, head_cols))

    def far_sum_start(grad):
        split = grad.reshape(2, 2, grad.shape[1] // 2, model_dim)
        return split[:, 0], swap(clock.hold(split[:, 1]), "seq", seq_bits[1])

    down_keep, down_move = far_sum_start(down_grad)

    query_back, pair_back, pair_sum = [], [], []
    for s in seqs:
        dq, *dkv = grad_attend[s]
        query = all_to_all(clock.hold(dq))
        pair = class_sum(dkv)
        if s + 1 < count:
            query, pair, *work = clock.sync(query, pair, *attend_back(s + 1))
            grad_attend.append(work)
        else:
            up_first = weight_first(grad_up[0], gathered[0])
            up_grad = weight_rest(up_first, grad_up, gathered)
            query, pair, up_grad = clock.sync(query, pair, up_grad)
        query_back.append(query)
        pair_sum.append(pair)
    for s in seqs:
        pair = heads_all_to_all(clock.hold(pair_sum[s]))
        if s == 0:
            gate_first = weight_first(grad_gate[0], gathered[0])
            up_grad = part_sum(up_grad, 1)
            down_grad = low_sum(down_keep, down_move)
            pair, gate_first, up_grad, down_grad = clock.sync(pair, gate_first, up_grad, down_grad)
            up_keep, up_move = far_sum_start(up_grad)
        elif s == 1:
            gate_grad = weight_rest(gate_first, grad_gate, gathered)
            pair, gate_grad = clock.sync(pair, gate_grad)
        else:
            (pair,) = clock.sync(pair)
        pair_back.append(pair)

    def owner_start(grad):
        return grad[0], swap(clock.hold(grad[1]), "wide", half_wide)

    def last_sums(grad):
        for bit in seq_bits[2:]:
            grad = part_sum(grad, bit)
        return grad

    down_grad = last_sums(down_grad)
    down_own, down_other = owner_start(down_grad)
    grad_proj = turn_back(
        [v.reshape(KEY_VALUE_HEADS, rows, head_cols) for v in query_back], pair_back, cosine, sine
    )
    all_normed = jnp.concatenate(normed, axis=0)
    all_attended = jnp.concatenate(attended, axis=0)
    all_branch = jnp.concatenate(grad_branch, axis=0)

    def half_dot(left, right, which, size):
        return dot(left, lax.dynamic_slice_in_dim(right, which * size, size, 1), TN)

    proj_sent = swap(half_dot(all_normed, grad_proj, 1 - side, half_proj).astype(bf16), "seq", 1)
    out_sent = swap(half_dot(all_branch, all_attended, 1 - side, half_out).astype(bf16), "seq", 1)
    gate_grad = part_sum(gate_grad, 1)
    grad_tokens, gain_first = [], 0.0
    for s in seqs:
        grad_normed = dot(grad_proj[s * rows : (s + 1) * rows], proj_weights[s], NT)
        grad, gain = norm_back(inputs[s], input_factor[s], gain_attn, grad_normed)
        gain_first = gain_first + gain
        grad_tokens.append((grad_middle[s] + grad).astype(bf16))
    gains = jnp.stack([gain_first, gain_second, gain_third, gain_fourth])
    out_part = low_sum(half_dot(all_branch, all_attended, side, half_out), out_sent)
    proj_part = low_sum(half_dot(all_normed, grad_proj, side, half_proj), proj_sent)
    up_grad = low_sum(up_keep, up_move)
    down_other, proj_part, out_part, gains, gate_grad, up_grad, *grad_tokens = clock.sync(
        down_other, proj_part, out_part, gains, gate_grad, up_grad, *grad_tokens
    )
    gate_keep, gate_move = far_sum_start(gate_grad)

    def part_of(o):
        first = index_at(o) * attn_rows
        return jnp.concatenate(
            [
                lax.dynamic_slice_in_dim(proj_part, first, attn_rows, 0),
                lax.dynamic_slice_in_dim(out_part, first, attn_rows, 0),
            ],
            axis=1,
        )

    def spread_grad(grad, bits):
        for bit in bits:
            grad = jnp.concatenate([grad, swap(grad, "seq", bit)], axis=0)
        return grad

    for axis, size in (("seq", seq_size), ("wide", wide)):
        bit = 1
        while bit < size:
            gains = gains + swap(gains, axis, bit)
            bit *= 2
    down_grad = low_sum(down_own, down_other)

    def beside_ring(step):
        if step == 0:
            return (gains,)
        if step == 1:
            return (gate_move,)
        if step == 2:
            return (spread_grad(clock.hold(down_grad), far_bits),)
        return ()

    total, work = ring_scatter(clock, part_of, attn_rows, wide, beside_ring)
    gains, gate_move, down_grad = work[0][0], work[1][0], work[2][0]
    gate_grad = last_sums(low_sum(gate_keep, gate_move))

    up_own, up_other = owner_start(last_sums(up_grad))
    attn_low = total.astype(bf16)
    attn_move = swap(clock.hold(attn_low), "seq", seq_bits[1])
    mlp_grad = unpack(spread_grad(clock.hold(down_grad), seq_bits[:1]), pieces, 2, [])
    up_other, attn_move, mlp_grad = clock.sync(up_other, attn_move, mlp_grad)
    gate_own, gate_other = owner_start(gate_grad)
    for bit in seq_bits[2:]:
        attn_low = low_sum(attn_low, attn_move)
        attn_move = swap(attn_low, "seq", bit)
    low = low_sum(attn_low, attn_move)
    other = swap(low, "seq", 1)
    left, right = jnp.where(is_low, low, other), jnp.where(is_low, other, low)
    attn_grad = jnp.concatenate(
        [left[:, :half_proj], right[:, :half_proj], left[:, half_proj:], right[:, half_proj:]],
        axis=1,
    ).astype(f32)
    up_grad = spread_grad(low_sum(up_own, up_other), reversed(seq_bits))
    mlp_grad = unpack(up_grad, pieces, 1, [mlp_grad])
    gate_other, attn_grad, mlp_grad = clock.sync(gate_other, attn_grad, mlp_grad)
    gate_grad = spread_grad(low_sum(gate_own, gate_other), reversed(seq_bits))
    mlp_grad = unpack(gate_grad, pieces, 0, [mlp_grad])
    return (
        jnp.stack(layer_out),
        jnp.stack(grad_tokens),
        attn_grad,
        mlp_grad,
        gains[0],
        gains[1],
        gains[2],
        gains[3],
    )


def solution(mesh):
    placed = (
        P("seq", "wide", None),
        P("seq", "wide", None),
        P("seq"),
        P("wide", None),
        P(),
        P(),
        P(None, "wide", None),
        P(),
        P(),
        P(),
        P(),
        P(),
        P(),
    )
    return jax.shard_map(
        per_device,
        mesh=mesh,
        in_specs=placed,
        out_specs=(
            P("seq", "wide", None),
            P("seq", "wide", None),
            P("wide", None),
            P(None, "wide", None),
            P(),
            P(),
            P(),
            P(),
        ),
        check_vma=False,
    )
```

```python
import functools
import math

import jax
import jax.numpy as jnp
from jax import lax
from jax.experimental import pallas as pl
from jax.experimental.pallas import tpu as pltpu
from jax.sharding import PartitionSpec as P

QUERY_HEADS = 8
KEY_VALUE_HEADS = 4
HEAD_SIZE = 256
PAIRED = QUERY_HEADS // KEY_VALUE_HEADS

eps_norm = 1e-06
soft_cap = 50.0
rope_base = 10000.0
gelu_coeff = math.sqrt(2.0 / math.pi)
f32 = jnp.float32
bf16 = jnp.bfloat16
VMEM_LIMIT = 56 * 1024 * 1024


def dot(a, b, dims):
    return lax.dot_general(a, b, (dims, ((), ())), preferred_element_type=f32)


NN = ((1,), (0,))
NT = ((1,), (1,))
TN = ((0,), (0,))


def inverse_powers(exponents):
    return 1.0 / jnp.left_shift(jnp.ones_like(exponents), exponents).astype(f32)


def norm_factor(values):
    return lax.rsqrt(jnp.mean(values * values, axis=-1, keepdims=True) + eps_norm)


def norm_back(values, factor, gain, grad):
    scaled = grad * gain
    inner = jnp.mean(values * scaled, axis=-1, keepdims=True)
    grad_values = factor * scaled - values * (factor * factor * factor * inner)
    return grad_values, jnp.sum(grad * values * factor, axis=0)


def gelu_parts(values):
    inner = gelu_coeff * (values + 0.044715 * values * values * values)
    return jnp.tanh(inner)


def rotary_rows(positions):
    half_dim = HEAD_SIZE // 2
    frequency = jnp.exp(
        jnp.arange(half_dim, dtype=f32) * (-2.0 * math.log(rope_base) / HEAD_SIZE)
    )
    angles = positions.astype(f32)[:, None] * frequency[None, :]
    return jnp.cos(angles), jnp.sin(angles)


def ring_place(index, size):
    return jnp.where(index % 2 == 0, index // 2, size - 1 - index // 2)


def ring_index(place, size):
    return jnp.where(place < size // 2, 2 * place, 2 * (size - 1 - place) + 1)


def ring_perms(size):
    order = list(range(0, size, 2)) + list(range(size - 1, 0, -2))
    up = [
        (base + order[i], base + order[(i + 1) % size])
        for base in range(0, lax.axis_size("wide"), size)
        for i in range(size)
    ]
    return up, [(b, a) for a, b in up]


def ring_offsets(size):
    out = [0]
    for k in range(1, size // 2):
        out += [-k, k]
    return out + [size // 2]


class Clock:
    def __init__(self, token):
        self.token = token

    def sync(self, *arrays):
        *arrays, self.token = lax.optimization_barrier(tuple(arrays) + (self.token,))
        return arrays

    def hold(self, value):
        return lax.optimization_barrier((value, self.token))[0]


def hop(a, b, size):
    up, down = ring_perms(size)
    return lax.ppermute(a, "wide", up), lax.ppermute(b, "wide", down)


def low_sum(*terms):
    return sum(t.astype(f32) for t in terms).astype(bf16)


def halves(value):
    half = value.shape[0] // 2
    return value[:half], value[half:]


def add_first(whole, part):
    count = part.shape[0]
    return jnp.concatenate([low_sum(whole[:count], part), whole[count:].astype(bf16)], axis=0)


def add_last(whole, part):
    count = whole.shape[0] - part.shape[0]
    return jnp.concatenate([whole[:count].astype(bf16), low_sum(whole[count:], part)], axis=0)


def ring_gather(clock, value, size, beside=lambda step: ()):
    a = b = clock.hold(value)
    out, other = [a], []
    for k in range(1, size // 2 + 1):
        if k == size // 2:
            a, b = halves(a)[0], halves(b)[1]
        work = beside(k - 1)
        a, b = hop(a, b, size)
        a, b, *work = clock.sync(a, b, *work)
        out += [a, b]
        other.append(work)
    return out, other


def ring_scatter(clock, part_of, rows, size, beside=lambda step: ()):
    a, b = halves(clock.hold(part_of(size // 2).astype(bf16)))
    other = []
    for k in range(size // 2 - 1, -1, -1):
        work = beside(size // 2 - 1 - k)
        a, b = hop(a, b, size)
        a, b, *work = clock.sync(a, b, *work)
        other.append(work)
        if k == size // 2 - 1 and k > 0:
            a = add_first(part_of(k), a)
            b = add_last(part_of(-k), b)
        elif k > 0:
            a = low_sum(part_of(k), a)
            b = low_sum(part_of(-k), b)
    return part_of(0).astype(f32) + a.astype(f32) + b.astype(f32), other


def swap(value, axis, bit):
    size = lax.axis_size(axis)
    return lax.ppermute(value, axis, [(i, i ^ bit) for i in range(size)])


def all_to_all(value):
    return lax.all_to_all(value, "wide", split_axis=0, concat_axis=0, tiled=True)


def heads_all_to_all(value):
    size = lax.axis_size("wide")
    classes = size // KEY_VALUE_HEADS
    groups = [list(range(c, size, classes)) for c in range(classes)]
    return lax.all_to_all(
        value, "wide", split_axis=0, concat_axis=0, axis_index_groups=groups, tiled=True
    )


def class_ring(value):
    size = lax.axis_size("wide")
    classes = size // KEY_VALUE_HEADS
    perm = [(i, i // classes * classes + (i + 1) % classes) for i in range(size)]
    return lax.ppermute(value, "wide", perm)


def slice_values(codes, width):
    lift = jnp.where(width == 0, 0.0, 0.5).astype(bf16)
    large = jnp.where(width == 0, 0.0, jnp.where(width == 1, 1.5 * 2**11, 1.5 * 2**13)).astype(bf16)
    top = jnp.where(width == 0, 127.0, jnp.where(width == 1, 112.0, 64.0)).astype(bf16)
    return jnp.minimum(((codes + lift) + large) - large, top)


def proj_slice_kernel(places, info, *refs, blocks, count):
    code_refs, scale_ref, out_refs = refs[: 2 * blocks], refs[2 * blocks], refs[len(refs) - count :]
    mine = pl.program_id(1) == info[0]

    def write(code_ref):
        codes = code_ref[...]
        scale = scale_ref[...].astype(bf16)
        for s, out_ref in enumerate(out_refs):
            out_ref[...] = slice_values(codes, info[1 + s]) * scale

    for k in range(blocks):
        here = pl.program_id(0) == k
        pl.when(jnp.logical_and(here, mine))(functools.partial(write, code_refs[2 * k]))
        pl.when(jnp.logical_and(here, jnp.logical_not(mine)))(
            functools.partial(write, code_refs[2 * k + 1])
        )


def proj_slices(own, other, places, info, scale, width, weights, total, count):
    blocks = len(own)
    rows = own[0].shape[0]
    inputs = [block for pair in zip(own, other) for block in pair] + [scale]
    grid_spec = pltpu.PrefetchScalarGridSpec(
        num_scalar_prefetch=2,
        grid=(blocks, 2),
        in_specs=[pl.BlockSpec((rows, width), lambda k, j, p, i: (0, 0))] * (2 * blocks)
        + [pl.BlockSpec((1, width), lambda k, j, p, i: (0, j))]
        + [pl.BlockSpec(memory_space=pl.ANY)] * len(weights),
        out_specs=[pl.BlockSpec((rows, width), lambda k, j, p, i: (p[k], j))] * count,
    )
    return pl.pallas_call(
        functools.partial(proj_slice_kernel, blocks=blocks, count=count),
        grid_spec=grid_spec,
        out_shape=[jax.ShapeDtypeStruct((total * rows, 2 * width), bf16)] * count,
        input_output_aliases={2 + len(inputs) + s: s for s in range(len(weights))},
        compiler_params=pltpu.CompilerParams(vmem_limit_bytes=VMEM_LIMIT),
        cost_estimate=pl.CostEstimate(
            flops=20 * count * blocks * rows * width,
            bytes_accessed=4 * blocks * rows * width * (1 + count),
            transcendentals=0,
        ),
        name="proj_slices",
    )(places, info, *inputs, *weights)


def out_slice_kernel(places, info, *refs, split, count):
    inputs, scale_ref, out_refs = refs[: -1 - count], refs[-1 - count], refs[-count:]
    members = len(inputs) // 2
    member = info[1 + count]
    mine = pl.program_id(1) == info[0]

    def write(code_refs):
        scale = scale_ref[...].astype(bf16)
        for t, code_ref in enumerate(code_refs):
            first = pl.multiple_of(jnp.bitwise_xor(member, t) * split, 128)
            for s, out_ref in enumerate(out_refs):
                out_ref[:, pl.ds(first, split)] = slice_values(code_ref[0], info[1 + s]) * scale

    pl.when(mine)(lambda: write(inputs[:members]))
    pl.when(jnp.logical_not(mine))(lambda: write(inputs[members:]))


def out_slices(own, other, places, info, scale, count):
    blocks, rows, split = own[0].shape
    width = split * len(own)
    inputs = list(own) + list(other)
    grid_spec = pltpu.PrefetchScalarGridSpec(
        num_scalar_prefetch=2,
        grid=(blocks, 2),
        in_specs=[pl.BlockSpec((1, rows, split), lambda k, j, p, i: (k, 0, 0))] * len(inputs)
        + [pl.BlockSpec((rows, 1), lambda k, j, p, i: (p[k], 0))],
        out_specs=[pl.BlockSpec((rows, width), lambda k, j, p, i: (p[k], j))] * count,
    )
    return pl.pallas_call(
        functools.partial(out_slice_kernel, split=split, count=count),
        grid_spec=grid_spec,
        out_shape=[jax.ShapeDtypeStruct((blocks * rows, 2 * width), bf16)] * count,
        compiler_params=pltpu.CompilerParams(vmem_limit_bytes=VMEM_LIMIT),
        cost_estimate=pl.CostEstimate(
            flops=20 * count * blocks * rows * width,
            bytes_accessed=4 * blocks * rows * width * (1 + count),
            transcendentals=0,
        ),
        name="out_slices",
    )(places, info, *inputs, scale)


def own_slice_kernel(pieces, info, code_ref, row_ref, col_ref, *out_refs):
    count = len(out_refs) // 3
    for m in range(3):
        codes = code_ref[m].astype(f32).astype(bf16)
        scale = (row_ref[m] if m < 2 else col_ref[...]).astype(bf16)
        for s in range(count):
            out_refs[m * count + s][...] = slice_values(codes, info[1 + s]) * scale


def own_slices(codes, pieces, info, row_scale, col_scale, count):
    three, rows, cols = codes.shape
    steps = pieces.shape[0]
    piece = rows // steps
    grid_spec = pltpu.PrefetchScalarGridSpec(
        num_scalar_prefetch=2,
        grid=(steps,),
        in_specs=[
            pl.BlockSpec((three, piece, cols), lambda j, p, i: (0, p[j], 0)),
            pl.BlockSpec((2, piece, 1), lambda j, p, i: (0, j, 0)),
            pl.BlockSpec((1, cols), lambda j, p, i: (0, 0)),
        ],
        out_specs=[pl.BlockSpec((piece, cols), lambda j, p, i: (j, 0))] * (three * count),
    )
    return pl.pallas_call(
        own_slice_kernel,
        grid_spec=grid_spec,
        out_shape=[jax.ShapeDtypeStruct((2 * rows, cols), bf16)] * (three * count),
        compiler_params=pltpu.CompilerParams(vmem_limit_bytes=VMEM_LIMIT),
        cost_estimate=pl.CostEstimate(
            flops=10 * count * codes.size,
            bytes_accessed=codes.size * (4 + 2 * count),
            transcendentals=0,
        ),
        name="own_slices",
    )(pieces, info, codes, row_scale, col_scale)


def partner_slice_kernel(info, *refs, steps, count):
    piece_refs, scale_ref, out_refs = refs[:steps], refs[steps], refs[steps + 1 + count :]
    for j in range(steps):

        @pl.when(pl.program_id(0) == j)
        def _():
            codes = piece_refs[j][...]
            scale = scale_ref[...].astype(bf16)
            for s, out_ref in enumerate(out_refs):
                out_ref[...] = slice_values(codes, info[1 + s]) * scale


def partner_slices(pieces, info, scale, by_column, weights):
    steps = len(pieces)
    count = len(weights)
    piece, cols = pieces[0].shape
    if by_column:
        scale_spec = pl.BlockSpec((1, cols), lambda j, i: (0, 0))
    else:
        scale_spec = pl.BlockSpec((piece, 1), lambda j, i: (steps + j, 0))
    grid_spec = pltpu.PrefetchScalarGridSpec(
        num_scalar_prefetch=1,
        grid=(steps,),
        in_specs=[pl.BlockSpec((piece, cols), lambda j, i: (0, 0))] * steps
        + [scale_spec]
        + [pl.BlockSpec(memory_space=pl.ANY)] * count,
        out_specs=[pl.BlockSpec((piece, cols), lambda j, i: (steps + j, 0))] * count,
    )
    return pl.pallas_call(
        functools.partial(partner_slice_kernel, steps=steps, count=count),
        grid_spec=grid_spec,
        out_shape=[jax.ShapeDtypeStruct(w.shape, bf16) for w in weights],
        input_output_aliases={2 + steps + s: s for s in range(count)},
        compiler_params=pltpu.CompilerParams(vmem_limit_bytes=VMEM_LIMIT),
        cost_estimate=pl.CostEstimate(
            flops=10 * count * steps * piece * cols,
            bytes_accessed=2 * (1 + count) * steps * piece * cols,
            transcendentals=0,
        ),
        name="partner_slices",
    )(info, *pieces, scale, *weights)


def unpack_kernel(pieces, grad_ref, *refs):
    refs[-1][0] = grad_ref[...].astype(f32)


def unpack(grad, pieces, matrix, held):
    steps = pieces.shape[0]
    rows, cols = grad.shape
    piece = rows // steps
    grid_spec = pltpu.PrefetchScalarGridSpec(
        num_scalar_prefetch=1,
        grid=(steps,),
        in_specs=[pl.BlockSpec((piece, cols), lambda j, p: (j, 0))]
        + [pl.BlockSpec(memory_space=pl.ANY)] * len(held),
        out_specs=pl.BlockSpec((1, piece, cols), lambda j, p: (matrix, p[j], 0)),
    )
    return pl.pallas_call(
        unpack_kernel,
        grid_spec=grid_spec,
        out_shape=jax.ShapeDtypeStruct((3, rows, cols), f32),
        input_output_aliases={2: 0} if held else {},
        compiler_params=pltpu.CompilerParams(vmem_limit_bytes=VMEM_LIMIT),
        cost_estimate=pl.CostEstimate(
            flops=rows * cols, bytes_accessed=6 * rows * cols, transcendentals=0
        ),
        name="unpack",
    )(pieces, grad, *held)


def turn(values, cosine, sine):
    half = HEAD_SIZE // 2
    out = []
    for j in range(values.shape[1] // HEAD_SIZE):
        a = values[:, j * HEAD_SIZE : j * HEAD_SIZE + half]
        b = values[:, j * HEAD_SIZE + half : (j + 1) * HEAD_SIZE]
        out += [a * cosine - b * sine, b * cosine + a * sine]
    return jnp.concatenate(out, axis=1)


def project_kernel(x_ref, wq_ref, wk_ref, wv_ref, cos_ref, sin_ref, q_ref, kv_ref):
    x = x_ref[...]
    cosine, sine = cos_ref[...], sin_ref[...]
    scale = HEAD_SIZE ** (-0.5)
    q_ref[0] = (turn(dot(x, wq_ref[...], NN), cosine, sine) * scale).astype(bf16)
    kv_ref[0, :, :HEAD_SIZE] = turn(dot(x, wk_ref[...], NN), cosine, sine).astype(bf16)
    kv_ref[0, :, HEAD_SIZE:] = dot(x, wv_ref[...], NN).astype(bf16)


def project(normed, weights, cosine, sine):
    rows, depth = normed.shape
    cols = PAIRED * HEAD_SIZE
    first_key = QUERY_HEADS
    first_value = QUERY_HEADS + KEY_VALUE_HEADS
    whole = lambda shape: pl.BlockSpec(shape, lambda h: (0, 0))
    return pl.pallas_call(
        project_kernel,
        grid=(KEY_VALUE_HEADS,),
        in_specs=[
            whole((rows, depth)),
            pl.BlockSpec((depth, cols), lambda h: (0, h)),
            pl.BlockSpec((depth, HEAD_SIZE), lambda h: (0, first_key + h)),
            pl.BlockSpec((depth, HEAD_SIZE), lambda h: (0, first_value + h)),
            whole(cosine.shape),
            whole(sine.shape),
        ],
        out_specs=[
            pl.BlockSpec((1, rows, cols), lambda h: (h, 0, 0)),
            pl.BlockSpec((1, rows, 2 * HEAD_SIZE), lambda h: (h, 0, 0)),
        ],
        out_shape=[
            jax.ShapeDtypeStruct((KEY_VALUE_HEADS, rows, cols), bf16),
            jax.ShapeDtypeStruct((KEY_VALUE_HEADS, rows, 2 * HEAD_SIZE), bf16),
        ],
        compiler_params=pltpu.CompilerParams(vmem_limit_bytes=VMEM_LIMIT),
        cost_estimate=pl.CostEstimate(
            flops=2 * rows * weights.size, bytes_accessed=2 * weights.size, transcendentals=0
        ),
        name="project",
    )(normed, weights, weights, weights, cosine, sine)


def turn_back_kernel(*refs, count):
    q_refs, kv_refs = refs[:count], refs[count : 2 * count]
    cos_ref, sin_ref, out_ref = refs[2 * count :]
    j = pl.program_id(1)
    scale = HEAD_SIZE ** (-0.5)
    keys = KEY_VALUE_HEADS // PAIRED
    for s in range(count):
        here = pl.program_id(0) == s

        @pl.when(jnp.logical_and(here, j < KEY_VALUE_HEADS))
        def _():
            grad = q_refs[s][0].astype(f32) * scale
            out_ref[...] = turn(grad, cos_ref[...], -sin_ref[...]).astype(bf16)

        @pl.when(jnp.logical_and(here, jnp.logical_and(j >= KEY_VALUE_HEADS, j < KEY_VALUE_HEADS + keys)))
        def _():
            grad = jnp.concatenate([kv_refs[s][i, :, :HEAD_SIZE] for i in range(PAIRED)], axis=1)
            out_ref[...] = turn(grad.astype(f32), cos_ref[...], -sin_ref[...]).astype(bf16)

        @pl.when(jnp.logical_and(here, j >= KEY_VALUE_HEADS + keys))
        def _():
            out_ref[...] = jnp.concatenate(
                [kv_refs[s][i, :, HEAD_SIZE:] for i in range(PAIRED)], axis=1
            )


def turn_back(queries, pairs, cosine, sine):
    count = len(queries)
    heads, rows, cols = queries[0].shape
    keys = heads // PAIRED
    grid = (count, heads + 2 * keys)
    whole = pl.BlockSpec(cosine.shape, lambda s, j: (0, 0))
    return pl.pallas_call(
        functools.partial(turn_back_kernel, count=count),
        grid=grid,
        in_specs=[
            pl.BlockSpec((1, rows, cols), lambda s, j: (jnp.minimum(j, heads - 1), 0, 0))
        ]
        * count
        + [
            pl.BlockSpec(
                (PAIRED, rows, cols), lambda s, j: (jnp.maximum(j - heads, 0) % keys, 0, 0)
            )
        ]
        * count
        + [whole, whole],
        out_specs=pl.BlockSpec((rows, cols), lambda s, j: (s, j)),
        out_shape=jax.ShapeDtypeStruct((count * rows, grid[1] * cols), bf16),
        compiler_params=pltpu.CompilerParams(vmem_limit_bytes=VMEM_LIMIT),
        cost_estimate=pl.CostEstimate(
            flops=4 * count * rows * grid[1] * cols,
            bytes_accessed=4 * count * rows * grid[1] * cols,
            transcendentals=0,
        ),
        name="turn_back",
    )(*queries, *pairs, cosine, sine)


def tile_positions(tile, count, start, class_index, class_rows, rows):
    index = lax.broadcasted_iota(jnp.int32, (count, 1), 0)
    place = start + jnp.bitwise_and(index, tile - 1)
    shift = class_rows.bit_length() - 1
    return (
        jnp.right_shift(place, shift) * rows
        + class_index * class_rows
        + jnp.bitwise_and(place, class_rows - 1)
    )


def stack_heads(block):
    return jnp.concatenate(
        [block[:, j * HEAD_SIZE : (j + 1) * HEAD_SIZE] for j in range(PAIRED)], axis=0
    )


def key_places(group, class_index, classes, rows):
    index = lax.broadcasted_iota(jnp.int32, (1, classes * rows), 1)
    shift = rows.bit_length() - 1
    back = jnp.bitwise_and(class_index - jnp.right_shift(index, shift), classes - 1)
    return (group * classes + back) * rows + jnp.bitwise_and(index, rows - 1)


def held_block(refs, group, cols):
    return jnp.concatenate([ref[group, :, cols] for ref in refs], axis=0)


def group_range(start, tile, class_rows, classes):
    return start // class_rows // classes, (start + tile - 1) // class_rows // classes + 1


def attn_forward_kernel(info, q_ref, *refs, tile, class_rows, rows, classes):
    kv_refs = refs[:classes]
    att_ref, exact_ref, lse_ref = refs[classes:]
    start = pl.program_id(0) * tile
    free, total = group_range(start, tile, class_rows, classes)
    queries = stack_heads(q_ref[...])
    count = queries.shape[0]
    position = tile_positions(tile, count, start, info[0], class_rows, rows)

    def step(group, carry, masked):
        acc, row_sum = carry
        keys = held_block(kv_refs, group, slice(0, HEAD_SIZE))
        values = held_block(kv_refs, group, slice(HEAD_SIZE, 2 * HEAD_SIZE))
        raw = dot(queries, keys, NT)
        weight = jnp.exp(soft_cap * jnp.tanh(raw * (1.0 / soft_cap)))
        if masked:
            weight = jnp.where(
                key_places(group, info[0], classes, rows) <= position, weight, 0.0
            )
        row_sum = row_sum + jnp.sum(weight, axis=-1, keepdims=True)
        acc = acc + dot(weight.astype(bf16), values, NN)
        return acc, row_sum

    carry = (jnp.zeros((count, HEAD_SIZE), f32), jnp.zeros((count, 1), f32))
    carry = lax.fori_loop(0, free, functools.partial(step, masked=False), carry)
    acc, row_sum = lax.fori_loop(free, total, functools.partial(step, masked=True), carry)
    exact = acc / row_sum
    lse = jnp.log(row_sum)
    for j in range(PAIRED):
        cols = slice(j * HEAD_SIZE, (j + 1) * HEAD_SIZE)
        exact_ref[:, cols] = exact[j * tile : (j + 1) * tile]
        att_ref[:, cols] = exact[j * tile : (j + 1) * tile].astype(bf16)
        lse_ref[:, j * 128 : (j + 1) * 128] = jnp.broadcast_to(
            lse[j * tile : (j + 1) * tile], (tile, 128)
        )


def attn_forward(info, queries, pairs, class_rows, rows):
    count, cols = queries.shape
    classes = len(pairs)
    length = classes * pairs[0].shape[0] * rows
    tile = min(256, count)
    grid_spec = pltpu.PrefetchScalarGridSpec(
        num_scalar_prefetch=1,
        grid=(count // tile,),
        in_specs=[pl.BlockSpec((tile, cols), lambda i, c: (i, 0))]
        + [pl.BlockSpec(p.shape, lambda i, c: (0, 0, 0)) for p in pairs],
        out_specs=[
            pl.BlockSpec((tile, cols), lambda i, c: (i, 0)),
            pl.BlockSpec((tile, cols), lambda i, c: (i, 0)),
            pl.BlockSpec((tile, PAIRED * 128), lambda i, c: (i, 0)),
        ],
    )
    return pl.pallas_call(
        functools.partial(
            attn_forward_kernel, tile=tile, class_rows=class_rows, rows=rows, classes=classes
        ),
        grid_spec=grid_spec,
        out_shape=[
            jax.ShapeDtypeStruct((count, cols), bf16),
            jax.ShapeDtypeStruct((count, cols), f32),
            jax.ShapeDtypeStruct((count, PAIRED * 128), f32),
        ],
        compiler_params=pltpu.CompilerParams(vmem_limit_bytes=VMEM_LIMIT),
        cost_estimate=pl.CostEstimate(
            flops=2 * count * PAIRED * length * 2 * HEAD_SIZE,
            bytes_accessed=8 * count * cols + 4 * length * HEAD_SIZE,
            transcendentals=2 * count * PAIRED * length,
        ),
        name="attn_forward",
    )(info, queries, *pairs)


def attn_backward_kernel(info, q_ref, grad_ref, exact_ref, lse_ref, *refs, tile, class_rows, rows, classes):
    kv_refs, dq_ref = refs[:classes], refs[classes]
    dkv_refs, sum_ref = refs[classes + 1 : 2 * classes + 1], refs[2 * classes + 1]

    @pl.when(pl.program_id(0) == 0)
    def _():
        sum_ref[...] = jnp.zeros_like(sum_ref)

    start = pl.program_id(0) * tile
    free, total = group_range(start, tile, class_rows, classes)
    queries = stack_heads(q_ref[...])
    grads = stack_heads(grad_ref[...])
    count = queries.shape[0]
    delta = jnp.sum(grads.astype(f32) * stack_heads(exact_ref[...]), axis=-1, keepdims=True)
    lse = jnp.concatenate([lse_ref[:, j * 128 : j * 128 + 1] for j in range(PAIRED)], axis=0)
    position = tile_positions(tile, count, start, info[0], class_rows, rows)

    def step(group, acc, masked):
        keys = held_block(kv_refs, group, slice(0, HEAD_SIZE))
        values = held_block(kv_refs, group, slice(HEAD_SIZE, 2 * HEAD_SIZE))
        bounded = jnp.tanh(dot(queries, keys, NT) * (1.0 / soft_cap))
        probs = jnp.exp(soft_cap * bounded - lse)
        if masked:
            probs = jnp.where(key_places(group, info[0], classes, rows) <= position, probs, 0.0)
        grad_probs = dot(grads, values, NT)
        grad_raw = (probs * (grad_probs - delta) * (1.0 - bounded * bounded)).astype(bf16)
        sum_ref[group, :, HEAD_SIZE:] += dot(probs.astype(bf16), grads, TN)
        sum_ref[group, :, :HEAD_SIZE] += dot(grad_raw, queries, TN)
        return acc + dot(grad_raw, keys, NN)

    acc = jnp.zeros((count, HEAD_SIZE), f32)
    acc = lax.fori_loop(0, free, functools.partial(step, masked=False), acc)
    acc = lax.fori_loop(free, total, functools.partial(step, masked=True), acc)
    for j in range(PAIRED):
        dq_ref[:, j * HEAD_SIZE : (j + 1) * HEAD_SIZE] = acc[j * tile : (j + 1) * tile].astype(bf16)

    @pl.when(pl.program_id(0) == pl.num_programs(0) - 1)
    def _():
        for h, ref in enumerate(dkv_refs):
            ref[...] = sum_ref[:, h * rows : (h + 1) * rows, :].astype(bf16)


def attn_backward(info, queries, pairs, grads, exact, lse, class_rows, rows):
    count, cols = queries.shape
    classes = len(pairs)
    groups = pairs[0].shape[0]
    length = classes * groups * rows
    tile = min(256, count)
    row_spec = pl.BlockSpec((tile, cols), lambda i, c: (i, 0))
    pair_specs = [pl.BlockSpec(p.shape, lambda i, c: (0, 0, 0)) for p in pairs]
    grid_spec = pltpu.PrefetchScalarGridSpec(
        num_scalar_prefetch=1,
        grid=(count // tile,),
        in_specs=[
            row_spec,
            row_spec,
            row_spec,
            pl.BlockSpec((tile, PAIRED * 128), lambda i, c: (i, 0)),
        ]
        + pair_specs,
        out_specs=[row_spec] + pair_specs,
        scratch_shapes=[pltpu.VMEM((groups, classes * rows, 2 * HEAD_SIZE), f32)],
    )
    return pl.pallas_call(
        functools.partial(
            attn_backward_kernel, tile=tile, class_rows=class_rows, rows=rows, classes=classes
        ),
        grid_spec=grid_spec,
        out_shape=[jax.ShapeDtypeStruct((count, cols), bf16)]
        + [jax.ShapeDtypeStruct(p.shape, bf16) for p in pairs],
        compiler_params=pltpu.CompilerParams(vmem_limit_bytes=VMEM_LIMIT),
        cost_estimate=pl.CostEstimate(
            flops=5 * count * PAIRED * length * 2 * HEAD_SIZE,
            bytes_accessed=10 * count * cols + 8 * length * HEAD_SIZE,
            transcendentals=2 * count * PAIRED * length,
        ),
        name="attn_backward",
    )(info, queries, grads, exact, lse, *pairs)


def per_device(
    tokens,
    cotangent,
    widths,
    attn_codes,
    attn_exps,
    out_exps,
    mlp_codes,
    gate_exps,
    down_exps,
    gain_attn,
    gain_post_attn,
    gain_mlp,
    gain_post_mlp,
):
    wide = lax.axis_size("wide")
    seq_size = lax.axis_size("seq")
    wide_index = lax.axis_index("wide")
    seq_index = lax.axis_index("seq")
    side = seq_index % 2
    is_low = side == 0
    members = seq_size // 2
    member = seq_index // 2
    half_wide = wide // 2
    place = ring_place(wide_index, wide)
    count, rows, model_dim = tokens.shape
    classes = wide // KEY_VALUE_HEADS
    class_rows = rows // classes
    class_index = wide_index % classes
    head_cols = PAIRED * HEAD_SIZE
    proj_cols = attn_exps.shape[0]
    half_proj = proj_cols // 2
    half_out = (attn_codes.shape[1] - proj_cols) // 2
    split_out = half_out // members
    attn_rows = attn_codes.shape[0]
    hidden = mlp_codes.shape[1]
    offsets = ring_offsets(wide)
    order = {o: i for i, o in enumerate(ring_offsets(half_wide))}
    seqs = range(count)
    seq_bits = [1 << i for i in range(seq_size.bit_length() - 1)]
    far_bits = list(reversed(seq_bits[1:]))
    clock = Clock(widths)

    def index_at(offset):
        return ring_index(jnp.mod(place + offset, wide), wide)

    places = jnp.stack([index_at(o) for o in offsets]).astype(jnp.int32)
    info = jnp.concatenate(
        [side[None].astype(jnp.int32), widths, member[None].astype(jnp.int32)]
    )
    class_info = class_index[None].astype(jnp.int32)
    column_scale = inverse_powers(attn_exps)[None, :]
    output_scale = inverse_powers(out_exps)[:, None]

    relative = [0]
    for bit in reversed(seq_bits):
        relative = relative + [r | bit for r in relative]
    pieces = jnp.stack([jnp.bitwise_xor(seq_index, r) for r in relative]).astype(jnp.int32)
    piece_rows = hidden // seq_size
    partner = jnp.bitwise_xor(wide_index, half_wide)
    gate_scale = inverse_powers(gate_exps)
    row_scale = jnp.concatenate(
        [
            lax.dynamic_slice_in_dim(
                gate_scale, block * hidden + pieces[j] * piece_rows, piece_rows, 1
            )
            for block in (wide_index, partner)
            for j in range(seq_size)
        ],
        axis=1,
    )[:, :, None]
    down_scale = inverse_powers(down_exps)[None, :]

    def columns(first, size):
        return lax.dynamic_slice_in_dim(attn_codes, first, size, 1)

    payload = jnp.concatenate(
        [
            columns(side * half_proj, half_proj),
            columns(proj_cols + side * half_out + member * split_out, split_out),
        ],
        axis=1,
    ).astype(bf16)
    piece_codes = lax.dynamic_slice_in_dim(mlp_codes, seq_index * piece_rows, piece_rows, 1)
    inputs = [tokens[s].astype(f32) for s in seqs]
    grad_out = [cotangent[s].astype(f32) for s in seqs]
    cosine, sine = rotary_rows(wide_index * rows + jnp.arange(rows))

    blocks, others = [clock.hold(payload)], []
    proj_weights = []

    def slice_more(first, last):
        return proj_slices(
            blocks[first:last],
            others[first:last],
            places[first:last],
            info,
            column_scale,
            half_proj,
            proj_weights,
            wide,
            count,
        )

    a = b = blocks[0]
    sliced = 0
    steps = half_wide
    for k in range(1, steps + 1):
        if k == steps:
            a, b = halves(a)[0], halves(b)[1]
        passed = [swap(v, "seq", 1) for v in blocks[len(others) :]]
        a, b = hop(a, b, wide)
        work = []
        if k == 1:
            work = own_slices(mlp_codes, pieces, info, row_scale, down_scale, count)
            a, b, *work = clock.sync(a, b, *passed, *work)
            passed, own_weights = work[: len(passed)], work[len(passed) :]
        elif k == 2:
            work = [piece_codes[m].astype(bf16) for m in range(3)]
            for s in seqs:
                factor = norm_factor(clock.hold(inputs[s]))
                work += [factor, (inputs[s] * factor * gain_attn).astype(bf16)]
            a, b, *work = clock.sync(a, b, *passed, *work)
            passed, work = work[: len(passed)], work[len(passed) :]
            sends, work = work[:3], work[3:]
            input_factor, normed = work[0::2], work[1::2]
        else:
            more = len(others)
            work = slice_more(sliced, more) if more > sliced else []
            a, b, *work = clock.sync(a, b, *passed, *work)
            passed, work = work[: len(passed)], work[len(passed) :]
            if work:
                proj_weights, sliced = list(work), more
        others += passed
        blocks += [a, b] if k < steps else [jnp.concatenate([a, b], axis=0)]

    def exchange(m):
        return swap(clock.hold(sends[m]), "wide", half_wide)

    def share(held, bits):
        for bit in bits:
            held = held + [swap(value, "seq", bit) for value in held]
        return held

    def partner_weights(m, held):
        scale = row_scale[m] if m < 2 else down_scale
        return partner_slices(
            held, info, scale, m == 2, own_weights[m * count : (m + 1) * count]
        )

    received = exchange(0)
    others += [swap(clock.hold(v), "seq", 1) for v in blocks[len(others) :]]
    proj_weights = slice_more(sliced, wide)
    query_send, pair_send = [], []
    for s in seqs:
        query, pair = project(normed[s], proj_weights[s], cosine, sine)
        query_send.append(query.reshape(wide, class_rows, head_cols))
        pair_send.append(pair)
    own_out = jnp.stack([clock.hold(v)[:, half_proj:] for v in blocks])
    other_out = jnp.stack([v[:, half_proj:] for v in others])
    out_own = share([own_out], far_bits)
    sent = clock.sync(received, *query_send, *pair_send, *out_own)
    received, sent = sent[0], sent[1:]
    query_send, pair_send, out_own = sent[:count], sent[count : 2 * count], sent[2 * count :]

    def spread(pair):
        held = [pair]
        for _ in range(classes - 1):
            held.append(class_ring(held[-1]))
        return held[1:]

    def two_parts(value):
        cut = value.shape[0] // 2
        return value[:cut], value[cut:]

    attended_send, exact, lse, queries, pairs = [], [], [], [], []

    def attend(s):
        out, full, log_sum = attn_forward(class_info, queries[s], pairs[s], class_rows, rows)
        return [out.reshape(wide, class_rows, head_cols), full, log_sum]

    def keep_attend(work):
        attended_send.append(work[0])
        exact.append(work[1])
        lse.append(work[2])

    out_other = [other_out] + [swap(v, "seq", 1) for v in out_own[1:]]
    pair_first, *out_other = clock.sync(heads_all_to_all(clock.hold(pair_send[0])), *out_other)
    gate_held = share([clock.hold(received)], far_bits)
    moved = spread(pair_first)
    pair_last = heads_all_to_all(clock.hold(pair_send[1]))
    out_weights = out_slices(out_own, out_other, places, info, output_scale, count)
    work = clock.sync(pair_last, *moved, *out_weights, *gate_held)
    pair_last, work = work[0], work[1:]
    pairs.append([pair_first] + work[: classes - 1])
    out_weights = work[classes - 1 : classes - 1 + count]
    gate_held = share(work[classes - 1 + count :], seq_bits[:1])
    part_a, part_b = two_parts(pair_last)
    query = all_to_all(clock.hold(query_send[0]))
    query, *work = clock.sync(query, *spread(part_a), *gate_held)
    moved_a, gate_held = work[: classes - 1], work[classes - 1 :]
    queries.append(query.reshape(wide * class_rows, head_cols))
    moved_b = spread(clock.hold(part_b))
    query = all_to_all(clock.hold(query_send[1]))
    query, *work = clock.sync(query, *moved_b, *attend(0))
    moved_b = work[: classes - 1]
    keep_attend(work[classes - 1 :])
    queries.append(query.reshape(wide * class_rows, head_cols))
    pairs.append(
        [pair_last] + [jnp.concatenate([x, y], axis=0) for x, y in zip(moved_a, moved_b)]
    )

    attended, branch, branch_factor, middle, middle_factor, normed_mlp = [], [], [], [], [], []

    def heads_to_rows(values):
        split = values.reshape(KEY_VALUE_HEADS, rows, head_cols)
        return jnp.transpose(split, (1, 0, 2)).reshape(rows, KEY_VALUE_HEADS * head_cols)

    def join(s):
        value = dot(attended[s], out_weights[s], NT)
        factor = norm_factor(value)
        mid = inputs[s] + value * factor * gain_post_attn
        mid_factor = norm_factor(mid)
        return [value, factor, mid, mid_factor, (mid * mid_factor * gain_mlp).astype(bf16)]

    def keep_join(work):
        for held, value in zip((branch, branch_factor, middle, middle_factor, normed_mlp), work):
            held.append(value)

    for s in seqs:
        back = all_to_all(clock.hold(attended_send[s]))
        if s == 0:
            gate_weights = partner_weights(0, [clock.hold(v) for v in gate_held])
            back, *work = clock.sync(back, *attend(count - 1), *gate_weights)
            keep_attend(work[:3])
            gate_weights = work[3:]
        else:
            back, *work = clock.sync(back, *join(s - 1))
            keep_join(work)
        attended.append(heads_to_rows(back))

    received, *work = clock.sync(exchange(1), *join(count - 1))
    keep_join(work)

    def blocks_of(part):
        return lambda o: part[order[o] * rows : (order[o] + 1) * rows]

    gathered, gate, up, hidden_rows, mixed, parts = [], [], [], [], [], []

    def open_gate(s):
        return dot(clock.hold(gathered[s]), gate_weights[s], NT)

    def open_up(s):
        up_s = dot(clock.hold(gathered[s]), up_weights[s], NT)
        hidden_s = (0.5 * gate[s] * (1.0 + gelu_parts(gate[s])) * up_s).astype(bf16)
        return [up_s, hidden_s]

    def keep_up(work):
        up.append(work[0])
        hidden_rows.append(work[1])

    def mix(s):
        return dot(clock.hold(hidden_rows[s]), down_weights[s], NN).astype(bf16)

    up_held = share([clock.hold(received)], far_bits)
    received, *up_held = clock.sync(exchange(2), *up_held)

    def beside_first(step):
        nonlocal up_held
        if step == 0:
            up_held = share(up_held, seq_bits[:1])
            return tuple(up_held) + tuple(share([clock.hold(received)], far_bits))
        if step == 1:
            return tuple(partner_weights(1, [clock.hold(v) for v in up_held]))
        return ()

    a = b = clock.hold(normed_mlp[0])
    blocks = [a]
    for k in range(1, half_wide // 2 + 1):
        if k == half_wide // 2:
            a, b = halves(a)[0], halves(b)[1]
        if k == 2:
            down_held = share(down_held, seq_bits[:1])
        work = beside_first(k - 1) + (tuple(down_held) if k == 2 else ())
        a, b = hop(a, b, half_wide)
        a, b, *work = clock.sync(a, b, *work)
        if k == 1:
            up_held, down_held = work[: len(up_held)], work[len(up_held) :]
        elif k == 2:
            up_weights, down_held = work[:count], work[count:]
        blocks += [a, b]
    gathered.append(jnp.concatenate(blocks, axis=0))

    def beside_second(step):
        if step == 0:
            return [open_gate(0)] + list(partner_weights(2, [clock.hold(v) for v in down_held]))
        if step == 1:
            return open_up(0)
        return ()

    a = b = clock.hold(normed_mlp[1])
    blocks = [a]
    for k in range(1, half_wide // 2 + 1):
        if k == half_wide // 2:
            a, b = halves(a)[0], halves(b)[1]
        work = beside_second(k - 1)
        a, b = hop(a, b, half_wide)
        a, b, *work = clock.sync(a, b, *work)
        if k == 1:
            gate.append(work[0])
            down_weights = work[1:]
        elif k == 2:
            keep_up(work)
        blocks += [a, b]
    gathered.append(jnp.concatenate(blocks, axis=0))
    parts.append(clock.sync(mix(0))[0])

    layer_out, grad_mixed, gain_fourth = [], [], 0.0

    def finish(s):
        nonlocal gain_fourth
        factor = norm_factor(mixed[s])
        layer_out.append((middle[s] + mixed[s] * factor * gain_post_mlp).astype(bf16))
        grad, gain = norm_back(mixed[s], factor, gain_post_mlp, grad_out[s])
        grad_mixed.append(grad.astype(bf16))
        gain_fourth = gain_fourth + gain

    grad_group, grad_gate, grad_up, grad_parts, grad_normed_mlp = [], [], [], [], []

    def back_hidden(s):
        grad_hidden = dot(clock.hold(grad_group[s]), down_weights[s], NT)
        bounded = gelu_parts(gate[s])
        gelu_value = 0.5 * gate[s] * (1.0 + bounded)
        slope = 0.5 * (1.0 + bounded) + 0.5 * gate[s] * (1.0 - bounded * bounded) * gelu_coeff * (
            1.0 + 3.0 * 0.044715 * gate[s] * gate[s]
        )
        return [(grad_hidden * up[s] * slope).astype(bf16), (grad_hidden * gelu_value).astype(bf16)]

    def back_input(s):
        return (
            dot(clock.hold(grad_gate[s]), gate_weights[s], NN)
            + dot(grad_up[s], up_weights[s], NN)
        ).astype(bf16)

    def keep_back(work):
        grad_gate.append(work[0])
        grad_up.append(work[1])

    def first_sum(part):
        a, b = hop(*halves(clock.hold(blocks_of(part)(half_wide // 2))), half_wide)
        return a, b

    def rest_sum(part, a, b, beside=lambda step: ()):
        part_of = blocks_of(part)
        other = []
        for k in range(half_wide // 2 - 1, 0, -1):
            if k == half_wide // 2 - 1:
                a = add_first(part_of(k), a)
                b = add_last(part_of(-k), b)
            else:
                a = low_sum(part_of(k), a)
                b = low_sum(part_of(-k), b)
            work = beside(half_wide // 2 - 1 - k)
            a, b = hop(a, b, half_wide)
            a, b, *work = clock.sync(a, b, *work)
            other.append(work)
        return part_of(0).astype(f32) + a.astype(f32) + b.astype(f32), other

    for s in seqs:
        a, b = first_sum(parts[s])
        if s + 1 < count:
            a, b, value = clock.sync(a, b, open_gate(s + 1))
            gate.append(value)
        else:
            a, b, *work = clock.sync(a, b, *back_hidden(0))
            keep_back(work)

        def beside(step, s=s):
            if step:
                return ()
            return tuple(open_up(s + 1)) if s + 1 < count else (back_input(0),)

        total, work = rest_sum(parts[s], a, b, beside)
        if s + 1 < count:
            keep_up(work[0])
        else:
            grad_parts.append(work[0][0])
        mixed.append(total)
        finish(s)
        if s + 1 < count:
            parts.append(mix(s + 1))
        if s == 0:
            blocks, work = ring_gather(
                clock, grad_mixed[0], half_wide, lambda k: (parts[-1],) if k == 0 else ()
            )
            parts[-1] = work[0][0]
            grad_group.append(jnp.concatenate(blocks, axis=0))

    def weight_first(left, right):
        return dot(clock.hold(left), right, TN)

    def weight_rest(first, lefts, rights):
        for s in seqs[1:]:
            first = first + dot(clock.hold(lefts[s]), rights[s], TN)
        return first.astype(bf16).reshape(2, hidden, model_dim)

    def part_sum(grad, bit):
        split = grad.reshape(2, 2, grad.shape[1] // 2, model_dim)
        return low_sum(split[:, 0], swap(split[:, 1], "seq", bit))

    grad_middle, grad_branch, grad_send = [], [], []
    gain_third = gain_second = 0.0

    def back_branch(s):
        nonlocal gain_third, gain_second
        grad, gain = norm_back(middle[s], middle_factor[s], gain_mlp, grad_normed_mlp[s])
        gain_third = gain_third + gain
        grad_mid = grad_out[s] + grad
        grad, gain = norm_back(branch[s], branch_factor[s], gain_post_attn, grad_mid)
        gain_second = gain_second + gain
        grad = grad.astype(bf16)
        send = dot(grad, out_weights[s], NN).astype(bf16)
        send = jnp.transpose(send.reshape(rows, KEY_VALUE_HEADS, head_cols), (1, 0, 2))
        return [grad_mid, grad, send.reshape(wide, class_rows, head_cols)]

    def keep_branch(work):
        grad_middle.append(work[0])
        grad_branch.append(work[1])
        grad_send.append(work[2])

    for s in seqs[1:]:
        blocks, work = ring_gather(
            clock,
            grad_mixed[s],
            half_wide,
            lambda k: (weight_first(hidden_rows[0], grad_group[0]),) if k == 0 and s == 1 else (),
        )
        if s == 1:
            down_first = work[0][0]
        grad_group.append(jnp.concatenate(blocks, axis=0))
    for s in seqs:
        a, b = first_sum(grad_parts[s])
        if s + 1 < count:
            a, b, *work = clock.sync(a, b, *back_hidden(s + 1))
            keep_back(work)
        else:
            a, b, *work = clock.sync(a, b, *back_branch(s - 1))
            keep_branch(work)

        def beside(step, s=s):
            if step:
                return ()
            if s + 1 < count:
                return (back_input(s + 1),)
            return (weight_rest(down_first, hidden_rows, grad_group),)

        total, work = rest_sum(grad_parts[s], a, b, beside)
        if s + 1 < count:
            grad_parts.append(work[0][0])
        else:
            down_grad = work[0][0]
        grad_normed_mlp.append(total)

    def attend_back(s):
        dq, *dkv = attn_backward(
            class_info,
            queries[s],
            pairs[s],
            clock.hold(grad_heads[s]),
            exact[s],
            lse[s],
            class_rows,
            rows,
        )
        return [dq.reshape(wide, class_rows, head_cols)] + dkv

    def class_sum(dkv):
        total = dkv[1 % classes]
        for step in range(2, classes + 1):
            total = low_sum(dkv[step % classes], class_ring(total))
        return total

    def far_start(grad):
        split = grad.reshape(2, 2, grad.shape[1] // 2, model_dim)
        return split[:, 0], swap(clock.hold(split[:, 1]), "seq", seq_bits[1])

    def far_end(kept, moved):
        grad = low_sum(kept, moved)
        for bit in seq_bits[2:]:
            grad = part_sum(grad, bit)
        return grad

    grad_heads, grad_attend = [], []
    query_back, pair_back = [], []

    def heads_of(value):
        return value.reshape(wide * class_rows, head_cols)

    back = all_to_all(clock.hold(grad_send[0]))
    down_grad = part_sum(down_grad, 1)
    back, down_grad, *work = clock.sync(back, down_grad, *back_branch(1))
    keep_branch(work)
    grad_heads.append(heads_of(back))
    all_normed = jnp.concatenate(normed, axis=0)
    all_attended = jnp.concatenate(attended, axis=0)
    all_branch = jnp.concatenate(grad_branch, axis=0)

    def half_dot(left, right, which, size):
        return dot(left, lax.dynamic_slice_in_dim(right, which * size, size, 1), TN)

    down_keep, down_move = far_start(down_grad)
    back = all_to_all(clock.hold(grad_send[1]))
    out_send = half_dot(all_branch, clock.hold(all_attended), 1 - side, half_out).astype(bf16)
    back, out_send, *work = clock.sync(back, out_send, *attend_back(0))
    grad_heads.append(heads_of(back))
    grad_attend.append(work)

    dq, *dkv = grad_attend[0]
    parts_of_pair = [two_parts(v) for v in dkv]
    out_sent = swap(out_send, "seq", 1)
    query = all_to_all(clock.hold(dq))
    pair_a = class_sum([v[0] for v in parts_of_pair])
    out_part = low_sum(
        half_dot(all_branch, clock.hold(all_attended), side, half_out), out_sent
    )
    query, pair_a, out_part, *work = clock.sync(query, pair_a, out_part, *attend_back(1))
    query_back.append(query)
    grad_attend.append(work)
    dq, *dkv = grad_attend[1]
    query = all_to_all(clock.hold(dq))
    pair_b = class_sum([clock.hold(v[1]) for v in parts_of_pair])
    up_first = weight_first(grad_up[0], gathered[0])
    query, pair_b, up_first = clock.sync(query, pair_b, up_first)
    query_back.append(query)

    out_pieces = {
        t: lax.dynamic_slice_in_dim(
            out_part, jnp.bitwise_xor(member, t) * split_out, split_out, 1
        )
        for t in range(members)
    }

    pair = heads_all_to_all(clock.hold(jnp.concatenate([pair_a, pair_b], axis=0)))
    pair_sum = class_sum(dkv)
    up_grad = weight_rest(up_first, grad_up, gathered)
    pair, pair_sum, up_grad, down_move = clock.sync(pair, pair_sum, up_grad, down_move)
    pair_back.append(pair)
    down_grad = far_end(down_keep, down_move)
    for bit in seq_bits[1:]:
        for t in range(members):
            if not t & (bit // 2) and t in out_pieces and t | (bit // 2) in out_pieces:
                out_pieces[t] = low_sum(
                    out_pieces[t], swap(clock.hold(out_pieces.pop(t | (bit // 2))), "seq", bit)
                )
    pair = heads_all_to_all(clock.hold(pair_sum))
    up_grad = part_sum(up_grad, 1)
    pair, up_grad, down_grad = clock.sync(pair, up_grad, down_grad)
    pair_back.append(pair)
    up_keep, up_move = far_start(up_grad)

    def owner_start(grad):
        return grad[0], swap(clock.hold(grad[1]), "wide", half_wide)

    down_own, down_other = owner_start(down_grad)
    grad_proj = turn_back(
        [v.reshape(KEY_VALUE_HEADS, rows, head_cols) for v in query_back], pair_back, cosine, sine
    )
    proj_sent = swap(half_dot(all_normed, grad_proj, 1 - side, half_proj).astype(bf16), "seq", 1)
    gate_first = weight_first(grad_gate[0], gathered[0])
    proj_part = low_sum(half_dot(all_normed, grad_proj, side, half_proj), proj_sent)
    down_other, proj_part, out_piece, gate_first, up_move = clock.sync(
        down_other, proj_part, out_pieces[0], gate_first, up_move
    )
    up_grad = far_end(up_keep, up_move)

    def part_of(o):
        first = index_at(o) * attn_rows
        return jnp.concatenate(
            [
                lax.dynamic_slice_in_dim(proj_part, first, attn_rows, 0),
                lax.dynamic_slice_in_dim(out_piece, first, attn_rows, 0),
            ],
            axis=1,
        )

    def spread_grad(grad, bits):
        for bit in bits:
            grad = jnp.concatenate([grad, swap(grad, "seq", bit)], axis=0)
        return grad

    grad_tokens, gain_first = [], 0.0

    def back_tokens(s):
        grad_normed = dot(clock.hold(grad_proj[s * rows : (s + 1) * rows]), proj_weights[s], NT)
        grad, gain = norm_back(inputs[s], input_factor[s], gain_attn, grad_normed)
        return [(grad_middle[s] + grad).astype(bf16), gain]

    down_grad = low_sum(down_own, down_other)
    ring_work = {}

    def beside_ring(step):
        if step == 0:
            return (weight_rest(gate_first, grad_gate, gathered),)
        if step == 1:
            ring_work["down"] = spread_grad(clock.hold(down_grad), far_bits)
            return (part_sum(ring_work["gate"], 1), *back_tokens(0))
        if step == 2:
            ring_work["move"] = far_start(ring_work["gate"])
            return (ring_work["down"], *back_tokens(1))
        if step == half_wide - 1:
            return tuple(ring_work["move"])
        return ()

    a, b = halves(clock.hold(part_of(wide // 2)))
    for k in range(wide // 2 - 1, -1, -1):
        step = wide // 2 - 1 - k
        work = beside_ring(step)
        a, b = hop(a, b, wide)
        a, b, *work = clock.sync(a, b, *work)
        if step == 0:
            ring_work["gate"] = work[0]
        elif step == 1:
            ring_work["gate"] = work[0]
            grad_tokens.append(work[1])
            gain_first = work[2]
        elif step == 2:
            down_grad = work[0]
            grad_tokens.append(work[1])
            gain_first = gain_first + work[2]
        elif step == half_wide - 1:
            gate_grad = far_end(*work)
        if step == 0:
            a, b = add_first(part_of(k), a), add_last(part_of(-k), b)
        elif k > 0:
            a, b = low_sum(part_of(k), a), low_sum(part_of(-k), b)
    total = low_sum(part_of(0), a, b)

    def add_swapped(gains, axis, bits):
        for bit in bits:
            gains = gains + swap(gains, axis, bit)
        return gains

    gains = jnp.stack([gain_first, gain_second, gain_third, gain_fourth])
    wide_bits = [1 << i for i in range(wide.bit_length() - 1)]
    (gains,) = clock.sync(add_swapped(clock.hold(gains), "wide", wide_bits[1:]))

    up_own, up_other = owner_start(up_grad)
    gains = add_swapped(add_swapped(gains, "wide", wide_bits[:1]), "seq", seq_bits)
    proj_total = total[:, :half_proj]
    out_totals = {0: total[:, half_proj:]}
    for bit in seq_bits[1:]:
        sent = jnp.concatenate([proj_total] + [out_totals[t] for t in sorted(out_totals)], axis=1)
        moved = swap(clock.hold(sent), "seq", bit)
        proj_total = low_sum(proj_total, moved[:, :half_proj])
        for i, t in enumerate(sorted(out_totals)):
            first = half_proj + i * split_out
            out_totals[t | (bit // 2)] = moved[:, first : first + split_out]
    out_totals = jnp.stack([out_totals[t] for t in range(members)])
    low = jnp.concatenate(
        [proj_total]
        + [
            lax.dynamic_index_in_dim(out_totals, jnp.bitwise_xor(member, j), 0, keepdims=False)
            for j in range(members)
        ],
        axis=1,
    )
    up_other, low, gains = clock.sync(up_other, low, gains)
    up_grad = low_sum(up_own, up_other)
    gate_own, gate_other = owner_start(gate_grad)
    up_grad = spread_grad(clock.hold(up_grad), far_bits)
    other = swap(low, "seq", 1)
    left, right = jnp.where(is_low, low, other), jnp.where(is_low, other, low)
    attn_grad = jnp.concatenate(
        [left[:, :half_proj], right[:, :half_proj], left[:, half_proj:], right[:, half_proj:]],
        axis=1,
    ).astype(f32)
    mlp_grad = unpack(spread_grad(clock.hold(down_grad), seq_bits[:1]), pieces, 2, [])
    gate_other, up_grad, attn_grad, mlp_grad = clock.sync(gate_other, up_grad, attn_grad, mlp_grad)
    gate_grad = spread_grad(low_sum(gate_own, gate_other), far_bits)
    mlp_grad = unpack(spread_grad(clock.hold(up_grad), seq_bits[:1]), pieces, 1, [mlp_grad])
    gate_grad, mlp_grad = clock.sync(gate_grad, mlp_grad)
    mlp_grad = unpack(spread_grad(gate_grad, seq_bits[:1]), pieces, 0, [mlp_grad])
    return (
        jnp.stack(layer_out),
        jnp.stack(grad_tokens),
        attn_grad,
        mlp_grad,
        gains[0],
        gains[1],
        gains[2],
        gains[3],
    )


def solution(mesh):
    placed = (
        P("seq", "wide", None),
        P("seq", "wide", None),
        P("seq"),
        P("wide", None),
        P(),
        P(),
        P(None, "wide", None),
        P(),
        P(),
        P(),
        P(),
        P(),
        P(),
    )
    return jax.shard_map(
        per_device,
        mesh=mesh,
        in_specs=placed,
        out_specs=(
            P("seq", "wide", None),
            P("seq", "wide", None),
            P("wide", None),
            P(None, "wide", None),
            P(),
            P(),
            P(),
            P(),
        ),
        check_vma=False,
    )
```

```python
import functools
import math

import jax
import jax.numpy as jnp
from jax import lax
from jax.experimental import pallas as pl
from jax.experimental.pallas import tpu as pltpu
from jax.sharding import PartitionSpec as P

QUERY_HEADS = 8
KEY_VALUE_HEADS = 4
HEAD_SIZE = 256
PAIRED = QUERY_HEADS // KEY_VALUE_HEADS

eps_norm = 1e-06
soft_cap = 50.0
rope_base = 10000.0
gelu_coeff = math.sqrt(2.0 / math.pi)
f32 = jnp.float32
bf16 = jnp.bfloat16
VMEM_LIMIT = 56 * 1024 * 1024


def dot(a, b, dims):
    return lax.dot_general(a, b, (dims, ((), ())), preferred_element_type=f32)


NN = ((1,), (0,))
NT = ((1,), (1,))
TN = ((0,), (0,))


def inverse_powers(exponents):
    return 1.0 / jnp.left_shift(jnp.ones_like(exponents), exponents).astype(f32)


def norm_factor(values):
    return lax.rsqrt(jnp.mean(values * values, axis=-1, keepdims=True) + eps_norm)


def norm_back(values, factor, gain, grad):
    scaled = grad * gain
    inner = jnp.mean(values * scaled, axis=-1, keepdims=True)
    grad_values = factor * scaled - values * (factor * factor * factor * inner)
    return grad_values, jnp.sum(grad * values * factor, axis=0)


def gelu_parts(values):
    inner = gelu_coeff * (values + 0.044715 * values * values * values)
    return jnp.tanh(inner)


def rotary_rows(positions):
    half_dim = HEAD_SIZE // 2
    frequency = jnp.exp(
        jnp.arange(half_dim, dtype=f32) * (-2.0 * math.log(rope_base) / HEAD_SIZE)
    )
    angles = positions.astype(f32)[:, None] * frequency[None, :]
    return jnp.cos(angles), jnp.sin(angles)


def ring_place(index, size):
    return jnp.where(index % 2 == 0, index // 2, size - 1 - index // 2)


def ring_index(place, size):
    return jnp.where(place < size // 2, 2 * place, 2 * (size - 1 - place) + 1)


def ring_perms(size):
    order = list(range(0, size, 2)) + list(range(size - 1, 0, -2))
    up = [
        (base + order[i], base + order[(i + 1) % size])
        for base in range(0, lax.axis_size("wide"), size)
        for i in range(size)
    ]
    return up, [(b, a) for a, b in up]


def ring_offsets(size):
    out = [0]
    for k in range(1, size // 2):
        out += [-k, k]
    return out + [size // 2]


class Clock:
    def __init__(self, token):
        self.token = token

    def sync(self, *arrays):
        *arrays, self.token = lax.optimization_barrier(tuple(arrays) + (self.token,))
        return arrays

    def hold(self, value):
        return lax.optimization_barrier((value, self.token))[0]


def hop(a, b, size):
    up, down = ring_perms(size)
    return lax.ppermute(a, "wide", up), lax.ppermute(b, "wide", down)


def low_sum(*terms):
    return sum(t.astype(f32) for t in terms).astype(bf16)


def halves(value):
    half = value.shape[0] // 2
    return value[:half], value[half:]


def add_first(whole, part):
    count = part.shape[0]
    return jnp.concatenate([low_sum(whole[:count], part), whole[count:].astype(bf16)], axis=0)


def add_last(whole, part):
    count = whole.shape[0] - part.shape[0]
    return jnp.concatenate([whole[:count].astype(bf16), low_sum(whole[count:], part)], axis=0)


def ring_gather(clock, value, size, beside=lambda step: ()):
    a = b = clock.hold(value)
    out, other = [a], []
    for k in range(1, size // 2 + 1):
        if k == size // 2:
            a, b = halves(a)[0], halves(b)[1]
        work = beside(k - 1)
        a, b = hop(a, b, size)
        a, b, *work = clock.sync(a, b, *work)
        out += [a, b]
        other.append(work)
    return out, other


def ring_scatter(clock, part_of, rows, size, beside=lambda step: ()):
    a, b = halves(clock.hold(part_of(size // 2).astype(bf16)))
    other = []
    for k in range(size // 2 - 1, -1, -1):
        work = beside(size // 2 - 1 - k)
        a, b = hop(a, b, size)
        a, b, *work = clock.sync(a, b, *work)
        other.append(work)
        if k == size // 2 - 1 and k > 0:
            a = add_first(part_of(k), a)
            b = add_last(part_of(-k), b)
        elif k > 0:
            a = low_sum(part_of(k), a)
            b = low_sum(part_of(-k), b)
    return part_of(0).astype(f32) + a.astype(f32) + b.astype(f32), other


def swap(value, axis, bit):
    size = lax.axis_size(axis)
    return lax.ppermute(value, axis, [(i, i ^ bit) for i in range(size)])


def all_to_all(value):
    return lax.all_to_all(value, "wide", split_axis=0, concat_axis=0, tiled=True)


def heads_all_to_all(value):
    size = lax.axis_size("wide")
    classes = size // KEY_VALUE_HEADS
    groups = [list(range(c, size, classes)) for c in range(classes)]
    return lax.all_to_all(
        value, "wide", split_axis=0, concat_axis=0, axis_index_groups=groups, tiled=True
    )


def class_ring(value):
    size = lax.axis_size("wide")
    classes = size // KEY_VALUE_HEADS
    perm = [(i, i // classes * classes + (i + 1) % classes) for i in range(size)]
    return lax.ppermute(value, "wide", perm)


def slice_values(codes, width):
    lift = jnp.where(width == 0, 0.0, 0.5).astype(bf16)
    large = jnp.where(width == 0, 0.0, jnp.where(width == 1, 1.5 * 2**11, 1.5 * 2**13)).astype(bf16)
    top = jnp.where(width == 0, 127.0, jnp.where(width == 1, 112.0, 64.0)).astype(bf16)
    return jnp.minimum(((codes + lift) + large) - large, top)


def proj_slice_kernel(places, info, *refs, blocks, count):
    code_refs, scale_ref, out_refs = refs[: 2 * blocks], refs[2 * blocks], refs[len(refs) - count :]
    mine = pl.program_id(1) == info[0]

    def write(code_ref):
        codes = code_ref[...]
        scale = scale_ref[...].astype(bf16)
        for s, out_ref in enumerate(out_refs):
            out_ref[...] = slice_values(codes, info[1 + s]) * scale

    for k in range(blocks):
        here = pl.program_id(0) == k
        pl.when(jnp.logical_and(here, mine))(functools.partial(write, code_refs[2 * k]))
        pl.when(jnp.logical_and(here, jnp.logical_not(mine)))(
            functools.partial(write, code_refs[2 * k + 1])
        )


def proj_slices(own, other, places, info, scale, width, weights, total, count):
    blocks = len(own)
    rows = own[0].shape[0]
    inputs = [block for pair in zip(own, other) for block in pair] + [scale]
    grid_spec = pltpu.PrefetchScalarGridSpec(
        num_scalar_prefetch=2,
        grid=(blocks, 2),
        in_specs=[pl.BlockSpec((rows, width), lambda k, j, p, i: (0, 0))] * (2 * blocks)
        + [pl.BlockSpec((1, width), lambda k, j, p, i: (0, j))]
        + [pl.BlockSpec(memory_space=pl.ANY)] * len(weights),
        out_specs=[pl.BlockSpec((rows, width), lambda k, j, p, i: (p[k], j))] * count,
    )
    return pl.pallas_call(
        functools.partial(proj_slice_kernel, blocks=blocks, count=count),
        grid_spec=grid_spec,
        out_shape=[jax.ShapeDtypeStruct((total * rows, 2 * width), bf16)] * count,
        input_output_aliases={2 + len(inputs) + s: s for s in range(len(weights))},
        compiler_params=pltpu.CompilerParams(vmem_limit_bytes=VMEM_LIMIT),
        cost_estimate=pl.CostEstimate(
            flops=20 * count * blocks * rows * width,
            bytes_accessed=4 * blocks * rows * width * (1 + count),
            transcendentals=0,
        ),
        name="proj_slices",
    )(places, info, *inputs, *weights)


def out_slice_kernel(places, info, *refs, split, count):
    inputs, scale_ref, out_refs = refs[: -1 - count], refs[-1 - count], refs[-count:]
    members = len(inputs) // 2
    member = info[1 + count]
    mine = pl.program_id(1) == info[0]

    def write(code_refs):
        scale = scale_ref[...].astype(bf16)
        for t, code_ref in enumerate(code_refs):
            first = pl.multiple_of(jnp.bitwise_xor(member, t) * split, 128)
            for s, out_ref in enumerate(out_refs):
                out_ref[:, pl.ds(first, split)] = slice_values(code_ref[0], info[1 + s]) * scale

    pl.when(mine)(lambda: write(inputs[:members]))
    pl.when(jnp.logical_not(mine))(lambda: write(inputs[members:]))


def out_slices(own, other, places, info, scale, count):
    blocks, rows, split = own[0].shape
    width = split * len(own)
    inputs = list(own) + list(other)
    grid_spec = pltpu.PrefetchScalarGridSpec(
        num_scalar_prefetch=2,
        grid=(blocks, 2),
        in_specs=[pl.BlockSpec((1, rows, split), lambda k, j, p, i: (k, 0, 0))] * len(inputs)
        + [pl.BlockSpec((rows, 1), lambda k, j, p, i: (p[k], 0))],
        out_specs=[pl.BlockSpec((rows, width), lambda k, j, p, i: (p[k], j))] * count,
    )
    return pl.pallas_call(
        functools.partial(out_slice_kernel, split=split, count=count),
        grid_spec=grid_spec,
        out_shape=[jax.ShapeDtypeStruct((blocks * rows, 2 * width), bf16)] * count,
        compiler_params=pltpu.CompilerParams(vmem_limit_bytes=VMEM_LIMIT),
        cost_estimate=pl.CostEstimate(
            flops=20 * count * blocks * rows * width,
            bytes_accessed=4 * blocks * rows * width * (1 + count),
            transcendentals=0,
        ),
        name="out_slices",
    )(places, info, *inputs, scale)


def own_slice_kernel(pieces, info, code_ref, row_ref, col_ref, *out_refs):
    count = len(out_refs) // 3
    for m in range(3):
        codes = code_ref[m].astype(f32).astype(bf16)
        scale = (row_ref[m] if m < 2 else col_ref[...]).astype(bf16)
        for s in range(count):
            out_refs[m * count + s][...] = slice_values(codes, info[1 + s]) * scale


def own_slices(codes, pieces, info, row_scale, col_scale, count):
    three, rows, cols = codes.shape
    steps = pieces.shape[0]
    piece = rows // steps
    grid_spec = pltpu.PrefetchScalarGridSpec(
        num_scalar_prefetch=2,
        grid=(steps,),
        in_specs=[
            pl.BlockSpec((three, piece, cols), lambda j, p, i: (0, p[j], 0)),
            pl.BlockSpec((2, piece, 1), lambda j, p, i: (0, j, 0)),
            pl.BlockSpec((1, cols), lambda j, p, i: (0, 0)),
        ],
        out_specs=[pl.BlockSpec((piece, cols), lambda j, p, i: (j, 0))] * (three * count),
    )
    return pl.pallas_call(
        own_slice_kernel,
        grid_spec=grid_spec,
        out_shape=[jax.ShapeDtypeStruct((2 * rows, cols), bf16)] * (three * count),
        compiler_params=pltpu.CompilerParams(vmem_limit_bytes=VMEM_LIMIT),
        cost_estimate=pl.CostEstimate(
            flops=10 * count * codes.size,
            bytes_accessed=codes.size * (4 + 2 * count),
            transcendentals=0,
        ),
        name="own_slices",
    )(pieces, info, codes, row_scale, col_scale)


def partner_slice_kernel(info, *refs, steps, count):
    piece_refs, scale_ref, out_refs = refs[:steps], refs[steps], refs[steps + 1 + count :]
    for j in range(steps):

        @pl.when(pl.program_id(0) == j)
        def _():
            codes = piece_refs[j][...]
            scale = scale_ref[...].astype(bf16)
            for s, out_ref in enumerate(out_refs):
                out_ref[...] = slice_values(codes, info[1 + s]) * scale


def partner_slices(pieces, info, scale, by_column, weights):
    steps = len(pieces)
    count = len(weights)
    piece, cols = pieces[0].shape
    if by_column:
        scale_spec = pl.BlockSpec((1, cols), lambda j, i: (0, 0))
    else:
        scale_spec = pl.BlockSpec((piece, 1), lambda j, i: (steps + j, 0))
    grid_spec = pltpu.PrefetchScalarGridSpec(
        num_scalar_prefetch=1,
        grid=(steps,),
        in_specs=[pl.BlockSpec((piece, cols), lambda j, i: (0, 0))] * steps
        + [scale_spec]
        + [pl.BlockSpec(memory_space=pl.ANY)] * count,
        out_specs=[pl.BlockSpec((piece, cols), lambda j, i: (steps + j, 0))] * count,
    )
    return pl.pallas_call(
        functools.partial(partner_slice_kernel, steps=steps, count=count),
        grid_spec=grid_spec,
        out_shape=[jax.ShapeDtypeStruct(w.shape, bf16) for w in weights],
        input_output_aliases={2 + steps + s: s for s in range(count)},
        compiler_params=pltpu.CompilerParams(vmem_limit_bytes=VMEM_LIMIT),
        cost_estimate=pl.CostEstimate(
            flops=10 * count * steps * piece * cols,
            bytes_accessed=2 * (1 + count) * steps * piece * cols,
            transcendentals=0,
        ),
        name="partner_slices",
    )(info, *pieces, scale, *weights)


def unpack_kernel(pieces, grad_ref, *refs):
    refs[-1][0] = grad_ref[...].astype(f32)


def unpack(grad, pieces, matrix, held):
    steps = pieces.shape[0]
    rows, cols = grad.shape
    piece = rows // steps
    grid_spec = pltpu.PrefetchScalarGridSpec(
        num_scalar_prefetch=1,
        grid=(steps,),
        in_specs=[pl.BlockSpec((piece, cols), lambda j, p: (j, 0))]
        + [pl.BlockSpec(memory_space=pl.ANY)] * len(held),
        out_specs=pl.BlockSpec((1, piece, cols), lambda j, p: (matrix, p[j], 0)),
    )
    return pl.pallas_call(
        unpack_kernel,
        grid_spec=grid_spec,
        out_shape=jax.ShapeDtypeStruct((3, rows, cols), f32),
        input_output_aliases={2: 0} if held else {},
        compiler_params=pltpu.CompilerParams(vmem_limit_bytes=VMEM_LIMIT),
        cost_estimate=pl.CostEstimate(
            flops=rows * cols, bytes_accessed=6 * rows * cols, transcendentals=0
        ),
        name="unpack",
    )(pieces, grad, *held)


def tile_of(size):
    return 256 if size % 256 == 0 else size


def tiles_of(size, part):
    tile = tile_of(size)
    tiles = size // tile
    first_part = (tiles + 1) // 2
    if part is None or tiles == 1:
        return tile, 0, tiles
    return (tile, 0, first_part) if part == 0 else (tile, first_part, tiles - first_part)


def whole_spec(shape):
    return pl.BlockSpec(shape, lambda i: (0, 0))


def column_spec(rows, tile, first=0):
    return pl.BlockSpec((rows, tile), lambda i: (0, first + i))


def row_spec(tile, cols, first=0):
    return pl.BlockSpec((tile, cols), lambda i: (first + i, 0))


def kernel_call(kernel, grid, in_specs, out_specs, out_shape, flops, moved, name, held=()):
    inputs = len(in_specs)
    return pl.pallas_call(
        lambda *refs: kernel(*refs[:inputs], *refs[inputs + len(held) :]),
        grid=(grid,),
        in_specs=in_specs + [pl.BlockSpec(memory_space=pl.ANY)] * len(held),
        out_specs=out_specs,
        out_shape=out_shape,
        input_output_aliases={inputs + i: i for i in range(len(held))},
        compiler_params=pltpu.CompilerParams(vmem_limit_bytes=VMEM_LIMIT),
        cost_estimate=pl.CostEstimate(flops=flops, bytes_accessed=moved, transcendentals=0),
        name=name,
    )


def row_parts(rows):
    part = 512 if rows % 512 == 0 else rows
    return [slice(first, first + part) for first in range(0, rows, part)]


def open_kernel(x_ref, wg_ref, wu_ref, gate_ref, up_ref, hidden_ref):
    for part in row_parts(x_ref.shape[0]):
        x = x_ref[part]
        gate = dot(x, wg_ref[...], NT)
        up = dot(x, wu_ref[...], NT)
        gate_ref[part] = gate
        up_ref[part] = up
        hidden_ref[part] = (gate * (0.5 + 0.5 * gelu_parts(gate)) * up).astype(bf16)


def open_forward(x, gate_weights, up_weights, part, held=()):
    rows, depth = x.shape
    hidden = gate_weights.shape[0]
    tile, first, tiles = tiles_of(hidden, part)
    if held and tiles * tile == hidden:
        return list(held)
    return kernel_call(
        open_kernel,
        tiles,
        [whole_spec(x.shape)] + [row_spec(tile, depth, first)] * 2,
        [column_spec(rows, tile, first)] * 3,
        [jax.ShapeDtypeStruct((rows, hidden), t) for t in (f32, f32, bf16)],
        4 * rows * depth * tile * tiles,
        2 * rows * depth + tiles * tile * (4 * depth + 10 * rows),
        "open_forward",
        held,
    )(x, gate_weights, up_weights, *held)


def open_back_kernel(x_ref, wd_ref, gate_ref, up_ref, grad_gate_ref, grad_up_ref):
    for part in row_parts(x_ref.shape[0]):
        grad = dot(x_ref[part], wd_ref[...], NT)
        gate = gate_ref[part]
        square = gate * gate
        bounded = jnp.tanh(gate * (gelu_coeff + (0.044715 * gelu_coeff) * square))
        half = 0.5 + 0.5 * bounded
        steep = (0.5 * gelu_coeff) + (1.5 * 0.044715 * gelu_coeff) * square
        slope = half + gate * (1.0 - bounded * bounded) * steep
        grad_gate_ref[part] = (grad * up_ref[part] * slope).astype(bf16)
        grad_up_ref[part] = (grad * (gate * half)).astype(bf16)


def open_back(x, down_weights, gate, up, part, held=()):
    rows, depth = x.shape
    hidden = down_weights.shape[0]
    tile, first, tiles = tiles_of(hidden, part)
    if held and tiles * tile == hidden:
        return list(held)
    return kernel_call(
        open_back_kernel,
        tiles,
        [whole_spec(x.shape), row_spec(tile, depth, first)] + [column_spec(rows, tile, first)] * 2,
        [column_spec(rows, tile, first)] * 2,
        [jax.ShapeDtypeStruct((rows, hidden), bf16)] * 2,
        2 * rows * depth * tile * tiles,
        2 * rows * depth + tiles * tile * (2 * depth + 12 * rows),
        "open_back",
        held,
    )(x, down_weights, gate, up, *held)


def input_back_kernel(gate_ref, up_ref, wg_ref, wu_ref, out_ref):
    out_ref[...] = (
        dot(gate_ref[...], wg_ref[...], NN) + dot(up_ref[...], wu_ref[...], NN)
    ).astype(bf16)


def input_back(grad_gate, grad_up, gate_weights, up_weights, part, held=()):
    rows, hidden = grad_gate.shape
    depth = gate_weights.shape[1]
    tile, first, tiles = tiles_of(depth, part)
    if held and tiles * tile == depth:
        return list(held)
    return kernel_call(
        input_back_kernel,
        tiles,
        [whole_spec(grad_gate.shape)] * 2 + [column_spec(hidden, tile, first)] * 2,
        [column_spec(rows, tile, first)],
        [jax.ShapeDtypeStruct((rows, depth), bf16)],
        4 * rows * hidden * tile * tiles,
        4 * rows * hidden + tiles * tile * (4 * hidden + 2 * rows),
        "input_back",
        held,
    )(grad_gate, grad_up, gate_weights, up_weights, *held)


def weight_kernel(*refs, count):
    out_ref = refs[-1]
    total = dot(refs[0][...], refs[count][...], TN)
    for s in range(1, count):
        total = total + dot(refs[s][...], refs[count + s][...], TN)
    out_ref[...] = total.astype(bf16)


def weight_back(lefts, rights):
    count = len(lefts)
    rows, hidden = lefts[0].shape
    depth = rights[0].shape[1]
    tile = tile_of(hidden)
    return kernel_call(
        functools.partial(weight_kernel, count=count),
        hidden // tile,
        [column_spec(rows, tile)] * count + [whole_spec((rows, depth))] * count,
        row_spec(tile, depth),
        jax.ShapeDtypeStruct((hidden, depth), bf16),
        2 * count * rows * depth * hidden,
        2 * count * rows * (hidden + depth) + 2 * hidden * depth,
        "weight_back",
    )(*lefts, *rights)


def turn(values, cosine, sine):
    half = HEAD_SIZE // 2
    out = []
    for j in range(values.shape[1] // HEAD_SIZE):
        a = values[:, j * HEAD_SIZE : j * HEAD_SIZE + half]
        b = values[:, j * HEAD_SIZE + half : (j + 1) * HEAD_SIZE]
        out += [a * cosine - b * sine, b * cosine + a * sine]
    return jnp.concatenate(out, axis=1)


def project_kernel(x_ref, wq_ref, wk_ref, wv_ref, cos_ref, sin_ref, q_ref, kv_ref):
    x = x_ref[...]
    cosine, sine = cos_ref[...], sin_ref[...]
    scale = HEAD_SIZE ** (-0.5)
    q_ref[0] = (turn(dot(x, wq_ref[...], NN), cosine, sine) * scale).astype(bf16)
    kv_ref[0, :, :HEAD_SIZE] = turn(dot(x, wk_ref[...], NN), cosine, sine).astype(bf16)
    kv_ref[0, :, HEAD_SIZE:] = dot(x, wv_ref[...], NN).astype(bf16)


def project(normed, weights, cosine, sine):
    rows, depth = normed.shape
    cols = PAIRED * HEAD_SIZE
    first_key = QUERY_HEADS
    first_value = QUERY_HEADS + KEY_VALUE_HEADS
    whole = lambda shape: pl.BlockSpec(shape, lambda h: (0, 0))
    return pl.pallas_call(
        project_kernel,
        grid=(KEY_VALUE_HEADS,),
        in_specs=[
            whole((rows, depth)),
            pl.BlockSpec((depth, cols), lambda h: (0, h)),
            pl.BlockSpec((depth, HEAD_SIZE), lambda h: (0, first_key + h)),
            pl.BlockSpec((depth, HEAD_SIZE), lambda h: (0, first_value + h)),
            whole(cosine.shape),
            whole(sine.shape),
        ],
        out_specs=[
            pl.BlockSpec((1, rows, cols), lambda h: (h, 0, 0)),
            pl.BlockSpec((1, rows, 2 * HEAD_SIZE), lambda h: (h, 0, 0)),
        ],
        out_shape=[
            jax.ShapeDtypeStruct((KEY_VALUE_HEADS, rows, cols), bf16),
            jax.ShapeDtypeStruct((KEY_VALUE_HEADS, rows, 2 * HEAD_SIZE), bf16),
        ],
        compiler_params=pltpu.CompilerParams(vmem_limit_bytes=VMEM_LIMIT),
        cost_estimate=pl.CostEstimate(
            flops=2 * rows * weights.size, bytes_accessed=2 * weights.size, transcendentals=0
        ),
        name="project",
    )(normed, weights, weights, weights, cosine, sine)


def turn_back_kernel(*refs, count):
    q_refs, kv_refs = refs[:count], refs[count : 2 * count]
    cos_ref, sin_ref, out_ref = refs[2 * count :]
    j = pl.program_id(1)
    scale = HEAD_SIZE ** (-0.5)
    keys = KEY_VALUE_HEADS // PAIRED
    for s in range(count):
        here = pl.program_id(0) == s

        @pl.when(jnp.logical_and(here, j < KEY_VALUE_HEADS))
        def _():
            grad = q_refs[s][0].astype(f32) * scale
            out_ref[...] = turn(grad, cos_ref[...], -sin_ref[...]).astype(bf16)

        @pl.when(jnp.logical_and(here, jnp.logical_and(j >= KEY_VALUE_HEADS, j < KEY_VALUE_HEADS + keys)))
        def _():
            grad = jnp.concatenate([kv_refs[s][i, :, :HEAD_SIZE] for i in range(PAIRED)], axis=1)
            out_ref[...] = turn(grad.astype(f32), cos_ref[...], -sin_ref[...]).astype(bf16)

        @pl.when(jnp.logical_and(here, j >= KEY_VALUE_HEADS + keys))
        def _():
            out_ref[...] = jnp.concatenate(
                [kv_refs[s][i, :, HEAD_SIZE:] for i in range(PAIRED)], axis=1
            )


def turn_back(queries, pairs, cosine, sine):
    count = len(queries)
    heads, rows, cols = queries[0].shape
    keys = heads // PAIRED
    grid = (count, heads + 2 * keys)
    whole = pl.BlockSpec(cosine.shape, lambda s, j: (0, 0))
    return pl.pallas_call(
        functools.partial(turn_back_kernel, count=count),
        grid=grid,
        in_specs=[
            pl.BlockSpec((1, rows, cols), lambda s, j: (jnp.minimum(j, heads - 1), 0, 0))
        ]
        * count
        + [
            pl.BlockSpec(
                (PAIRED, rows, cols), lambda s, j: (jnp.maximum(j - heads, 0) % keys, 0, 0)
            )
        ]
        * count
        + [whole, whole],
        out_specs=pl.BlockSpec((rows, cols), lambda s, j: (s, j)),
        out_shape=jax.ShapeDtypeStruct((count * rows, grid[1] * cols), bf16),
        compiler_params=pltpu.CompilerParams(vmem_limit_bytes=VMEM_LIMIT),
        cost_estimate=pl.CostEstimate(
            flops=4 * count * rows * grid[1] * cols,
            bytes_accessed=4 * count * rows * grid[1] * cols,
            transcendentals=0,
        ),
        name="turn_back",
    )(*queries, *pairs, cosine, sine)


def tile_positions(tile, count, start, class_index, class_rows, rows):
    index = lax.broadcasted_iota(jnp.int32, (count, 1), 0)
    place = start + jnp.bitwise_and(index, tile - 1)
    shift = class_rows.bit_length() - 1
    return (
        jnp.right_shift(place, shift) * rows
        + class_index * class_rows
        + jnp.bitwise_and(place, class_rows - 1)
    )


def stack_heads(block):
    return jnp.concatenate(
        [block[:, j * HEAD_SIZE : (j + 1) * HEAD_SIZE] for j in range(PAIRED)], axis=0
    )


def key_places(group, class_index, classes, rows):
    index = lax.broadcasted_iota(jnp.int32, (1, classes * rows), 1)
    shift = rows.bit_length() - 1
    back = jnp.bitwise_and(class_index - jnp.right_shift(index, shift), classes - 1)
    return (group * classes + back) * rows + jnp.bitwise_and(index, rows - 1)


def held_block(refs, group, cols):
    return jnp.concatenate([ref[group, :, cols] for ref in refs], axis=0)


def group_range(start, tile, class_rows, classes):
    return start // class_rows // classes, (start + tile - 1) // class_rows // classes + 1


def attn_forward_kernel(info, q_ref, *refs, tile, class_rows, rows, classes):
    kv_refs = refs[:classes]
    att_ref, exact_ref, lse_ref = refs[classes:]
    start = pl.program_id(0) * tile
    free, total = group_range(start, tile, class_rows, classes)
    queries = stack_heads(q_ref[...])
    count = queries.shape[0]
    position = tile_positions(tile, count, start, info[0], class_rows, rows)

    def step(group, carry, masked):
        acc, row_sum = carry
        keys = held_block(kv_refs, group, slice(0, HEAD_SIZE))
        values = held_block(kv_refs, group, slice(HEAD_SIZE, 2 * HEAD_SIZE))
        raw = dot(queries, keys, NT)
        weight = jnp.exp(soft_cap * jnp.tanh(raw * (1.0 / soft_cap)))
        if masked:
            weight = jnp.where(
                key_places(group, info[0], classes, rows) <= position, weight, 0.0
            )
        row_sum = row_sum + jnp.sum(weight, axis=-1, keepdims=True)
        acc = acc + dot(weight.astype(bf16), values, NN)
        return acc, row_sum

    carry = (jnp.zeros((count, HEAD_SIZE), f32), jnp.zeros((count, 1), f32))
    carry = lax.fori_loop(0, free, functools.partial(step, masked=False), carry)
    acc, row_sum = lax.fori_loop(free, total, functools.partial(step, masked=True), carry)
    exact = acc / row_sum
    lse = jnp.log(row_sum)
    for j in range(PAIRED):
        cols = slice(j * HEAD_SIZE, (j + 1) * HEAD_SIZE)
        exact_ref[:, cols] = exact[j * tile : (j + 1) * tile]
        att_ref[:, cols] = exact[j * tile : (j + 1) * tile].astype(bf16)
        lse_ref[:, j * 128 : (j + 1) * 128] = jnp.broadcast_to(
            lse[j * tile : (j + 1) * tile], (tile, 128)
        )


def attn_forward(info, queries, pairs, class_rows, rows):
    count, cols = queries.shape
    classes = len(pairs)
    length = classes * pairs[0].shape[0] * rows
    tile = min(256, count)
    grid_spec = pltpu.PrefetchScalarGridSpec(
        num_scalar_prefetch=1,
        grid=(count // tile,),
        in_specs=[pl.BlockSpec((tile, cols), lambda i, c: (i, 0))]
        + [pl.BlockSpec(p.shape, lambda i, c: (0, 0, 0)) for p in pairs],
        out_specs=[
            pl.BlockSpec((tile, cols), lambda i, c: (i, 0)),
            pl.BlockSpec((tile, cols), lambda i, c: (i, 0)),
            pl.BlockSpec((tile, PAIRED * 128), lambda i, c: (i, 0)),
        ],
    )
    return pl.pallas_call(
        functools.partial(
            attn_forward_kernel, tile=tile, class_rows=class_rows, rows=rows, classes=classes
        ),
        grid_spec=grid_spec,
        out_shape=[
            jax.ShapeDtypeStruct((count, cols), bf16),
            jax.ShapeDtypeStruct((count, cols), f32),
            jax.ShapeDtypeStruct((count, PAIRED * 128), f32),
        ],
        compiler_params=pltpu.CompilerParams(vmem_limit_bytes=VMEM_LIMIT),
        cost_estimate=pl.CostEstimate(
            flops=2 * count * PAIRED * length * 2 * HEAD_SIZE,
            bytes_accessed=8 * count * cols + 4 * length * HEAD_SIZE,
            transcendentals=2 * count * PAIRED * length,
        ),
        name="attn_forward",
    )(info, queries, *pairs)


def attn_backward_kernel(info, q_ref, grad_ref, exact_ref, lse_ref, *refs, tile, class_rows, rows, classes):
    kv_refs, dq_ref = refs[:classes], refs[classes]
    dkv_refs, sum_ref = refs[classes + 1 : 2 * classes + 1], refs[2 * classes + 1]

    @pl.when(pl.program_id(0) == 0)
    def _():
        sum_ref[...] = jnp.zeros_like(sum_ref)

    start = pl.program_id(0) * tile
    free, total = group_range(start, tile, class_rows, classes)
    queries = stack_heads(q_ref[...])
    grads = stack_heads(grad_ref[...])
    count = queries.shape[0]
    delta = jnp.sum(grads.astype(f32) * stack_heads(exact_ref[...]), axis=-1, keepdims=True)
    lse = jnp.concatenate([lse_ref[:, j * 128 : j * 128 + 1] for j in range(PAIRED)], axis=0)
    position = tile_positions(tile, count, start, info[0], class_rows, rows)

    def step(group, acc, masked):
        keys = held_block(kv_refs, group, slice(0, HEAD_SIZE))
        values = held_block(kv_refs, group, slice(HEAD_SIZE, 2 * HEAD_SIZE))
        bounded = jnp.tanh(dot(queries, keys, NT) * (1.0 / soft_cap))
        probs = jnp.exp(soft_cap * bounded - lse)
        if masked:
            probs = jnp.where(key_places(group, info[0], classes, rows) <= position, probs, 0.0)
        grad_probs = dot(grads, values, NT)
        grad_raw = (probs * (grad_probs - delta) * (1.0 - bounded * bounded)).astype(bf16)
        sum_ref[group, :, HEAD_SIZE:] += dot(probs.astype(bf16), grads, TN)
        sum_ref[group, :, :HEAD_SIZE] += dot(grad_raw, queries, TN)
        return acc + dot(grad_raw, keys, NN)

    acc = jnp.zeros((count, HEAD_SIZE), f32)
    acc = lax.fori_loop(0, free, functools.partial(step, masked=False), acc)
    acc = lax.fori_loop(free, total, functools.partial(step, masked=True), acc)
    for j in range(PAIRED):
        dq_ref[:, j * HEAD_SIZE : (j + 1) * HEAD_SIZE] = acc[j * tile : (j + 1) * tile].astype(bf16)

    @pl.when(pl.program_id(0) == pl.num_programs(0) - 1)
    def _():
        for h, ref in enumerate(dkv_refs):
            ref[...] = sum_ref[:, h * rows : (h + 1) * rows, :].astype(bf16)


def attn_backward(info, queries, pairs, grads, exact, lse, class_rows, rows):
    count, cols = queries.shape
    classes = len(pairs)
    groups = pairs[0].shape[0]
    length = classes * groups * rows
    tile = min(256, count)
    row_spec = pl.BlockSpec((tile, cols), lambda i, c: (i, 0))
    pair_specs = [pl.BlockSpec(p.shape, lambda i, c: (0, 0, 0)) for p in pairs]
    grid_spec = pltpu.PrefetchScalarGridSpec(
        num_scalar_prefetch=1,
        grid=(count // tile,),
        in_specs=[
            row_spec,
            row_spec,
            row_spec,
            pl.BlockSpec((tile, PAIRED * 128), lambda i, c: (i, 0)),
        ]
        + pair_specs,
        out_specs=[row_spec] + pair_specs,
        scratch_shapes=[pltpu.VMEM((groups, classes * rows, 2 * HEAD_SIZE), f32)],
    )
    return pl.pallas_call(
        functools.partial(
            attn_backward_kernel, tile=tile, class_rows=class_rows, rows=rows, classes=classes
        ),
        grid_spec=grid_spec,
        out_shape=[jax.ShapeDtypeStruct((count, cols), bf16)]
        + [jax.ShapeDtypeStruct(p.shape, bf16) for p in pairs],
        compiler_params=pltpu.CompilerParams(vmem_limit_bytes=VMEM_LIMIT),
        cost_estimate=pl.CostEstimate(
            flops=5 * count * PAIRED * length * 2 * HEAD_SIZE,
            bytes_accessed=10 * count * cols + 8 * length * HEAD_SIZE,
            transcendentals=2 * count * PAIRED * length,
        ),
        name="attn_backward",
    )(info, queries, grads, exact, lse, *pairs)


def per_device(
    tokens,
    cotangent,
    widths,
    attn_codes,
    attn_exps,
    out_exps,
    mlp_codes,
    gate_exps,
    down_exps,
    gain_attn,
    gain_post_attn,
    gain_mlp,
    gain_post_mlp,
):
    wide = lax.axis_size("wide")
    seq_size = lax.axis_size("seq")
    wide_index = lax.axis_index("wide")
    seq_index = lax.axis_index("seq")
    side = seq_index % 2
    is_low = side == 0
    members = seq_size // 2
    member = seq_index // 2
    half_wide = wide // 2
    place = ring_place(wide_index, wide)
    count, rows, model_dim = tokens.shape
    classes = wide // KEY_VALUE_HEADS
    class_rows = rows // classes
    class_index = wide_index % classes
    head_cols = PAIRED * HEAD_SIZE
    proj_cols = attn_exps.shape[0]
    half_proj = proj_cols // 2
    half_out = (attn_codes.shape[1] - proj_cols) // 2
    split_out = half_out // members
    attn_rows = attn_codes.shape[0]
    hidden = mlp_codes.shape[1]
    offsets = ring_offsets(wide)
    order = {o: i for i, o in enumerate(ring_offsets(half_wide))}
    seqs = range(count)
    seq_bits = [1 << i for i in range(seq_size.bit_length() - 1)]
    far_bits = list(reversed(seq_bits[1:]))
    clock = Clock(widths)

    def index_at(offset):
        return ring_index(jnp.mod(place + offset, wide), wide)

    places = jnp.stack([index_at(o) for o in offsets]).astype(jnp.int32)
    info = jnp.concatenate(
        [side[None].astype(jnp.int32), widths, member[None].astype(jnp.int32)]
    )
    class_info = class_index[None].astype(jnp.int32)
    column_scale = inverse_powers(attn_exps)[None, :]
    output_scale = inverse_powers(out_exps)[:, None]

    relative = [0]
    for bit in reversed(seq_bits):
        relative = relative + [r | bit for r in relative]
    pieces = jnp.stack([jnp.bitwise_xor(seq_index, r) for r in relative]).astype(jnp.int32)
    piece_rows = hidden // seq_size
    partner = jnp.bitwise_xor(wide_index, half_wide)
    gate_scale = inverse_powers(gate_exps)
    row_scale = jnp.concatenate(
        [
            lax.dynamic_slice_in_dim(
                gate_scale, block * hidden + pieces[j] * piece_rows, piece_rows, 1
            )
            for block in (wide_index, partner)
            for j in range(seq_size)
        ],
        axis=1,
    )[:, :, None]
    down_scale = inverse_powers(down_exps)[None, :]

    def columns(first, size):
        return lax.dynamic_slice_in_dim(attn_codes, first, size, 1)

    payload = jnp.concatenate(
        [
            columns(side * half_proj, half_proj),
            columns(proj_cols + side * half_out + member * split_out, split_out),
        ],
        axis=1,
    ).astype(bf16)
    piece_codes = lax.dynamic_slice_in_dim(mlp_codes, seq_index * piece_rows, piece_rows, 1)
    inputs = [tokens[s].astype(f32) for s in seqs]
    grad_out = [cotangent[s].astype(f32) for s in seqs]
    cosine, sine = rotary_rows(wide_index * rows + jnp.arange(rows))

    blocks, others = [clock.hold(payload)], []
    proj_weights = []

    def slice_more(first, last):
        return proj_slices(
            blocks[first:last],
            others[first:last],
            places[first:last],
            info,
            column_scale,
            half_proj,
            proj_weights,
            wide,
            count,
        )

    a = b = blocks[0]
    sliced = 0
    steps = half_wide
    for k in range(1, steps + 1):
        if k == steps:
            a, b = halves(a)[0], halves(b)[1]
        passed = [swap(v, "seq", 1) for v in blocks[len(others) :]]
        a, b = hop(a, b, wide)
        work = []
        if k == 1:
            work = own_slices(mlp_codes, pieces, info, row_scale, down_scale, count)
            a, b, *work = clock.sync(a, b, *passed, *work)
            passed, own_weights = work[: len(passed)], work[len(passed) :]
        elif k == 2:
            work = [piece_codes[m].astype(bf16) for m in range(3)]
            for s in seqs:
                factor = norm_factor(clock.hold(inputs[s]))
                work += [factor, (inputs[s] * factor * gain_attn).astype(bf16)]
            a, b, *work = clock.sync(a, b, *passed, *work)
            passed, work = work[: len(passed)], work[len(passed) :]
            sends, work = work[:3], work[3:]
            input_factor, normed = work[0::2], work[1::2]
        else:
            more = len(others)
            work = slice_more(sliced, more) if more > sliced else []
            a, b, *work = clock.sync(a, b, *passed, *work)
            passed, work = work[: len(passed)], work[len(passed) :]
            if work:
                proj_weights, sliced = list(work), more
        others += passed
        blocks += [a, b] if k < steps else [jnp.concatenate([a, b], axis=0)]

    def exchange(m):
        return swap(clock.hold(sends[m]), "wide", half_wide)

    def share(held, bits):
        for bit in bits:
            held = held + [swap(value, "seq", bit) for value in held]
        return held

    def partner_weights(m, held):
        scale = row_scale[m] if m < 2 else down_scale
        return partner_slices(
            held, info, scale, m == 2, own_weights[m * count : (m + 1) * count]
        )

    received = exchange(0)
    others += [swap(clock.hold(v), "seq", 1) for v in blocks[len(others) :]]
    proj_weights = slice_more(sliced, wide)
    query_send, pair_send = [], []
    for s in seqs:
        query, pair = project(normed[s], proj_weights[s], cosine, sine)
        query_send.append(query.reshape(wide, class_rows, head_cols))
        pair_send.append(pair)
    own_out = jnp.stack([clock.hold(v)[:, half_proj:] for v in blocks])
    other_out = jnp.stack([v[:, half_proj:] for v in others])
    out_own = share([own_out], far_bits)
    sent = clock.sync(received, *query_send, *pair_send, *out_own)
    received, sent = sent[0], sent[1:]
    query_send, pair_send, out_own = sent[:count], sent[count : 2 * count], sent[2 * count :]

    def spread(pair):
        held = [pair]
        for _ in range(classes - 1):
            held.append(class_ring(held[-1]))
        return held[1:]

    def two_parts(value):
        cut = value.shape[0] // 2
        return value[:cut], value[cut:]

    attended_send, exact, lse, queries, pairs = [], [], [], [], []

    def attend(s):
        out, full, log_sum = attn_forward(class_info, queries[s], pairs[s], class_rows, rows)
        return [out.reshape(wide, class_rows, head_cols), full, log_sum]

    def keep_attend(work):
        attended_send.append(work[0])
        exact.append(work[1])
        lse.append(work[2])

    out_other = [other_out] + [swap(v, "seq", 1) for v in out_own[1:]]
    pair_first, *out_other = clock.sync(heads_all_to_all(clock.hold(pair_send[0])), *out_other)
    gate_held = share([clock.hold(received)], far_bits)
    moved = spread(pair_first)
    pair_last = heads_all_to_all(clock.hold(pair_send[1]))
    out_weights = out_slices(out_own, out_other, places, info, output_scale, count)
    work = clock.sync(pair_last, *moved, *out_weights, *gate_held)
    pair_last, work = work[0], work[1:]
    pairs.append([pair_first] + work[: classes - 1])
    out_weights = work[classes - 1 : classes - 1 + count]
    gate_held = share(work[classes - 1 + count :], seq_bits[:1])
    part_a, part_b = two_parts(pair_last)
    query = all_to_all(clock.hold(query_send[0]))
    query, *work = clock.sync(query, *spread(part_a), *gate_held)
    moved_a, gate_held = work[: classes - 1], work[classes - 1 :]
    queries.append(query.reshape(wide * class_rows, head_cols))
    moved_b = spread(clock.hold(part_b))
    query = all_to_all(clock.hold(query_send[1]))
    query, *work = clock.sync(query, *moved_b, *attend(0))
    moved_b = work[: classes - 1]
    keep_attend(work[classes - 1 :])
    queries.append(query.reshape(wide * class_rows, head_cols))
    pairs.append(
        [pair_last] + [jnp.concatenate([x, y], axis=0) for x, y in zip(moved_a, moved_b)]
    )

    attended, branch, branch_factor, middle, middle_factor, normed_mlp = [], [], [], [], [], []

    def heads_to_rows(values):
        split = values.reshape(KEY_VALUE_HEADS, rows, head_cols)
        return jnp.transpose(split, (1, 0, 2)).reshape(rows, KEY_VALUE_HEADS * head_cols)

    def join(s):
        value = dot(attended[s], out_weights[s], NT)
        factor = norm_factor(value)
        mid = inputs[s] + value * factor * gain_post_attn
        mid_factor = norm_factor(mid)
        return [value, factor, mid, mid_factor, (mid * mid_factor * gain_mlp).astype(bf16)]

    def keep_join(work):
        for held, value in zip((branch, branch_factor, middle, middle_factor, normed_mlp), work):
            held.append(value)

    for s in seqs:
        back = all_to_all(clock.hold(attended_send[s]))
        if s == 0:
            gate_weights = partner_weights(0, [clock.hold(v) for v in gate_held])
            back, *work = clock.sync(back, *attend(count - 1), *gate_weights)
            keep_attend(work[:3])
            gate_weights = work[3:]
        else:
            back, *work = clock.sync(back, *join(s - 1))
            keep_join(work)
        attended.append(heads_to_rows(back))

    received, *work = clock.sync(exchange(1), *join(count - 1))
    keep_join(work)

    def blocks_of(part):
        return lambda o: part[order[o] * rows : (order[o] + 1) * rows]

    gathered, gate, up, hidden_rows, mixed, parts = [], [], [], [], [], []

    def open_part(s, part, held=()):
        group = clock.hold(gathered[s])
        return open_forward(group, gate_weights[s], up_weights[s], part, held)

    def keep_open(work):
        gate.append(work[0])
        up.append(work[1])
        hidden_rows.append(work[2])

    def mix(s):
        return dot(clock.hold(hidden_rows[s]), down_weights[s], NN).astype(bf16)

    up_held = share([clock.hold(received)], far_bits)
    received, *up_held = clock.sync(exchange(2), *up_held)

    def beside_first(step):
        nonlocal up_held
        if step == 0:
            up_held = share(up_held, seq_bits[:1])
            return tuple(up_held) + tuple(share([clock.hold(received)], far_bits))
        if step == 1:
            return tuple(partner_weights(1, [clock.hold(v) for v in up_held]))
        return ()

    a = b = clock.hold(normed_mlp[0])
    blocks = [a]
    for k in range(1, half_wide // 2 + 1):
        if k == half_wide // 2:
            a, b = halves(a)[0], halves(b)[1]
        if k == 2:
            down_held = share(down_held, seq_bits[:1])
        work = beside_first(k - 1) + (tuple(down_held) if k == 2 else ())
        a, b = hop(a, b, half_wide)
        a, b, *work = clock.sync(a, b, *work)
        if k == 1:
            up_held, down_held = work[: len(up_held)], work[len(up_held) :]
        elif k == 2:
            up_weights, down_held = work[:count], work[count:]
        blocks += [a, b]
    gathered.append(jnp.concatenate(blocks, axis=0))

    def beside_second(step):
        if step == 0:
            return open_part(0, None)
        if step == 1:
            return partner_weights(2, [clock.hold(v) for v in down_held])
        return ()

    a = b = clock.hold(normed_mlp[1])
    blocks = [a]
    for k in range(1, half_wide // 2 + 1):
        if k == half_wide // 2:
            a, b = halves(a)[0], halves(b)[1]
        work = beside_second(k - 1)
        a, b = hop(a, b, half_wide)
        a, b, *work = clock.sync(a, b, *work)
        if k == 1:
            keep_open(work)
        elif k == 2:
            down_weights = work
        blocks += [a, b]
    gathered.append(jnp.concatenate(blocks, axis=0))
    parts.append(clock.sync(mix(0))[0])

    layer_out, grad_mixed, gain_fourth = [], [], 0.0

    def finish(s):
        nonlocal gain_fourth
        factor = norm_factor(mixed[s])
        layer_out.append((middle[s] + mixed[s] * factor * gain_post_mlp).astype(bf16))
        grad, gain = norm_back(mixed[s], factor, gain_post_mlp, grad_out[s])
        grad_mixed.append(grad.astype(bf16))
        gain_fourth = gain_fourth + gain

    grad_group, grad_gate, grad_up, grad_parts, grad_normed_mlp = [], [], [], [], []

    def back_hidden(s, part, held=()):
        group = clock.hold(grad_group[s])
        return open_back(group, down_weights[s], gate[s], up[s], part, held)

    def back_input(s, part, held=()):
        grad = clock.hold(grad_gate[s])
        return input_back(grad, grad_up[s], gate_weights[s], up_weights[s], part, held)

    def keep_back(work):
        grad_gate.append(work[0])
        grad_up.append(work[1])

    def first_sum(part):
        a, b = hop(*halves(clock.hold(blocks_of(part)(half_wide // 2))), half_wide)
        return a, b

    def rest_sum(part, a, b, beside=lambda step: ()):
        part_of = blocks_of(part)
        other = []
        for k in range(half_wide // 2 - 1, 0, -1):
            if k == half_wide // 2 - 1:
                a = add_first(part_of(k), a)
                b = add_last(part_of(-k), b)
            else:
                a = low_sum(part_of(k), a)
                b = low_sum(part_of(-k), b)
            work = beside(half_wide // 2 - 1 - k)
            a, b = hop(a, b, half_wide)
            a, b, *work = clock.sync(a, b, *work)
            other.append(work)
        return part_of(0).astype(f32) + a.astype(f32) + b.astype(f32), other

    a, b = first_sum(parts[0])
    a, b, *opened = clock.sync(a, b, *open_part(1, 0))
    total, work = rest_sum(
        parts[0], a, b, lambda step: () if step else tuple(open_part(1, 1, opened))
    )
    keep_open(work[0])
    mixed.append(total)
    finish(0)
    parts.append(mix(1))
    blocks, work = ring_gather(
        clock, grad_mixed[0], half_wide, lambda k: (parts[1],) if k == 0 else ()
    )
    parts[1] = work[0][0]
    grad_group.append(jnp.concatenate(blocks, axis=0))
    a, b = first_sum(parts[1])
    a, b, *opened = clock.sync(a, b, *back_hidden(0, 0))

    def beside_last(step):
        if step:
            return ()
        keep_back(back_hidden(0, 1, opened))
        return (grad_gate[0], grad_up[0], *input_back(
            grad_gate[0], grad_up[0], gate_weights[0], up_weights[0], 0, ()
        ))

    total, work = rest_sum(parts[1], a, b, beside_last)
    grad_gate[0], grad_up[0], opened = work[0][0], work[0][1], work[0][2:]
    mixed.append(total)
    finish(1)
    blocks, work = ring_gather(
        clock, grad_mixed[1], half_wide, lambda k: () if k else tuple(back_input(0, 1, opened))
    )
    grad_parts.append(work[0][0])
    grad_group.append(jnp.concatenate(blocks, axis=0))

    def weight_sum(lefts, rights):
        lefts = [clock.hold(v) for v in lefts]
        return weight_back(lefts, rights).reshape(2, hidden, model_dim)

    def part_sum(grad, bit):
        split = grad.reshape(2, 2, grad.shape[1] // 2, model_dim)
        return low_sum(split[:, 0], swap(split[:, 1], "seq", bit))

    grad_middle, grad_branch, grad_send = [], [], []
    gain_third = gain_second = 0.0

    def back_branch(s):
        nonlocal gain_third, gain_second
        grad, gain = norm_back(middle[s], middle_factor[s], gain_mlp, grad_normed_mlp[s])
        gain_third = gain_third + gain
        grad_mid = grad_out[s] + grad
        grad, gain = norm_back(branch[s], branch_factor[s], gain_post_attn, grad_mid)
        gain_second = gain_second + gain
        grad = grad.astype(bf16)
        send = dot(grad, out_weights[s], NN).astype(bf16)
        send = jnp.transpose(send.reshape(rows, KEY_VALUE_HEADS, head_cols), (1, 0, 2))
        return [grad_mid, grad, send.reshape(wide, class_rows, head_cols)]

    def keep_branch(work):
        grad_middle.append(work[0])
        grad_branch.append(work[1])
        grad_send.append(work[2])

    a, b = first_sum(grad_parts[0])
    a, b, *opened = clock.sync(a, b, *back_hidden(1, 0))

    def beside_back(step):
        if step:
            return ()
        keep_back(back_hidden(1, 1, opened))
        return (grad_gate[1], grad_up[1], *input_back(
            grad_gate[1], grad_up[1], gate_weights[1], up_weights[1], 0, ()
        ))

    total, work = rest_sum(grad_parts[0], a, b, beside_back)
    grad_gate[1], grad_up[1], opened = work[0][0], work[0][1], work[0][2:]
    grad_normed_mlp.append(total)
    grad_parts += clock.sync(*back_input(1, 1, opened))
    a, b = first_sum(grad_parts[1])
    a, b, *work = clock.sync(a, b, *back_branch(0))
    keep_branch(work)
    total, work = rest_sum(
        grad_parts[1],
        a,
        b,
        lambda step: () if step else (weight_sum(hidden_rows, grad_group),),
    )
    down_grad = work[0][0]
    grad_normed_mlp.append(total)

    def attend_back(s):
        dq, *dkv = attn_backward(
            class_info,
            queries[s],
            pairs[s],
            clock.hold(grad_heads[s]),
            exact[s],
            lse[s],
            class_rows,
            rows,
        )
        return [dq.reshape(wide, class_rows, head_cols)] + dkv

    def class_sum(dkv):
        total = dkv[1 % classes]
        for step in range(2, classes + 1):
            total = low_sum(dkv[step % classes], class_ring(total))
        return total

    def far_start(grad):
        split = grad.reshape(2, 2, grad.shape[1] // 2, model_dim)
        return split[:, 0], swap(clock.hold(split[:, 1]), "seq", seq_bits[1])

    def far_end(kept, moved):
        grad = low_sum(kept, moved)
        for bit in seq_bits[2:]:
            grad = part_sum(grad, bit)
        return grad

    grad_heads, grad_attend = [], []
    query_back, pair_back = [], []

    def heads_of(value):
        return value.reshape(wide * class_rows, head_cols)

    back = all_to_all(clock.hold(grad_send[0]))
    down_grad = part_sum(down_grad, 1)
    back, down_grad, *work = clock.sync(back, down_grad, *back_branch(1))
    keep_branch(work)
    grad_heads.append(heads_of(back))
    all_normed = jnp.concatenate(normed, axis=0)
    all_attended = jnp.concatenate(attended, axis=0)
    all_branch = jnp.concatenate(grad_branch, axis=0)

    def half_dot(left, right, which, size):
        return dot(left, lax.dynamic_slice_in_dim(right, which * size, size, 1), TN)

    down_keep, down_move = far_start(down_grad)
    back = all_to_all(clock.hold(grad_send[1]))
    out_send = half_dot(all_branch, clock.hold(all_attended), 1 - side, half_out).astype(bf16)
    back, out_send, *work = clock.sync(back, out_send, *attend_back(0))
    grad_heads.append(heads_of(back))
    grad_attend.append(work)

    dq, *dkv = grad_attend[0]
    parts_of_pair = [two_parts(v) for v in dkv]
    out_sent = swap(out_send, "seq", 1)
    query = all_to_all(clock.hold(dq))
    pair_a = class_sum([v[0] for v in parts_of_pair])
    out_part = low_sum(
        half_dot(all_branch, clock.hold(all_attended), side, half_out), out_sent
    )
    query, pair_a, out_part, down_move, *work = clock.sync(
        query, pair_a, out_part, down_move, *attend_back(1)
    )
    down_grad = far_end(down_keep, down_move)
    query_back.append(query)
    grad_attend.append(work)
    dq, *dkv = grad_attend[1]
    query = all_to_all(clock.hold(dq))
    pair_b = class_sum([clock.hold(v[1]) for v in parts_of_pair])
    up_grad = weight_sum(grad_up, gathered)
    query, pair_b, up_grad = clock.sync(query, pair_b, up_grad)
    query_back.append(query)

    out_pieces = {
        t: lax.dynamic_slice_in_dim(
            out_part, jnp.bitwise_xor(member, t) * split_out, split_out, 1
        )
        for t in range(members)
    }
    for bit in seq_bits[1:]:
        for t in sorted(out_pieces):
            if not t & (bit // 2) and t | (bit // 2) in out_pieces:
                out_pieces[t] = low_sum(
                    out_pieces[t], swap(out_pieces.pop(t | (bit // 2)), "seq", bit)
                )
    out_piece = out_pieces[0]

    pair = heads_all_to_all(clock.hold(jnp.concatenate([pair_a, pair_b], axis=0)))
    pair_sum = class_sum([clock.hold(v) for v in dkv])
    up_grad = part_sum(up_grad, 1)
    pair, pair_sum, up_grad, out_piece = clock.sync(pair, pair_sum, up_grad, out_piece)
    pair_back.append(pair)
    up_keep, up_move = far_start(up_grad)
    pair = heads_all_to_all(clock.hold(pair_sum))
    gate_grad = weight_sum(grad_gate, gathered)
    pair, gate_grad = clock.sync(pair, gate_grad)
    pair_back.append(pair)

    def owner_start(grad):
        return grad[0], swap(clock.hold(grad[1]), "wide", half_wide)

    down_own, down_other = owner_start(down_grad)
    grad_proj = turn_back(
        [v.reshape(KEY_VALUE_HEADS, rows, head_cols) for v in query_back], pair_back, cosine, sine
    )
    proj_sent = swap(half_dot(all_normed, grad_proj, 1 - side, half_proj).astype(bf16), "seq", 1)
    gate_grad = part_sum(gate_grad, 1)
    proj_part = low_sum(half_dot(all_normed, grad_proj, side, half_proj), proj_sent)
    down_other, proj_part, gate_grad, up_move = clock.sync(
        down_other, proj_part, gate_grad, up_move
    )
    up_grad = far_end(up_keep, up_move)
    gate_keep, gate_move = far_start(gate_grad)

    def part_of(o):
        first = index_at(o) * attn_rows
        return jnp.concatenate(
            [
                lax.dynamic_slice_in_dim(proj_part, first, attn_rows, 0),
                lax.dynamic_slice_in_dim(out_piece, first, attn_rows, 0),
            ],
            axis=1,
        )

    def spread_grad(grad, bits):
        for bit in bits:
            grad = jnp.concatenate([grad, swap(grad, "seq", bit)], axis=0)
        return grad

    grad_tokens, gain_first = [], 0.0

    def back_tokens(s):
        grad_normed = dot(clock.hold(grad_proj[s * rows : (s + 1) * rows]), proj_weights[s], NT)
        grad_normed = lax.optimization_barrier(grad_normed)
        grad, gain = norm_back(inputs[s], input_factor[s], gain_attn, grad_normed)
        return [(grad_middle[s] + grad).astype(bf16), gain]

    down_grad = low_sum(down_own, down_other)
    ring_work = {}

    def beside_ring(step):
        if step == 0:
            return back_tokens(0)
        if step == 1:
            return back_tokens(1)
        if step == 2:
            ring_work["down"] = spread_grad(clock.hold(down_grad), far_bits)
            return (gate_move,)
        if step == half_wide - 1:
            return (ring_work["down"],)
        return ()

    a, b = halves(clock.hold(part_of(wide // 2)))
    for k in range(wide // 2 - 1, -1, -1):
        step = wide // 2 - 1 - k
        work = beside_ring(step)
        a, b = hop(a, b, wide)
        a, b, *work = clock.sync(a, b, *work)
        if step < 2:
            grad_tokens.append(work[0])
            gain_first = gain_first + work[1]
        elif step == 2:
            gate_grad = far_end(gate_keep, work[0])
        elif step == half_wide - 1:
            down_grad = work[0]
        if step == 0:
            a, b = add_first(part_of(k), a), add_last(part_of(-k), b)
        elif k > 0:
            a, b = low_sum(part_of(k), a), low_sum(part_of(-k), b)
    total = low_sum(part_of(0), a, b)

    def add_swapped(gains, axis, bits):
        for bit in bits:
            gains = gains + swap(gains, axis, bit)
        return gains

    gains = jnp.stack([gain_first, gain_second, gain_third, gain_fourth])
    wide_bits = [1 << i for i in range(wide.bit_length() - 1)]
    (gains,) = clock.sync(add_swapped(clock.hold(gains), "wide", wide_bits[1:]))

    up_own, up_other = owner_start(up_grad)
    proj_total = total[:, :half_proj]
    out_totals = {0: total[:, half_proj:]}
    for bit in seq_bits[1:]:
        sent = jnp.concatenate([proj_total] + [out_totals[t] for t in sorted(out_totals)], axis=1)
        moved = swap(clock.hold(sent), "seq", bit)
        proj_total = low_sum(proj_total, moved[:, :half_proj])
        for i, t in enumerate(sorted(out_totals)):
            first = half_proj + i * split_out
            out_totals[t | (bit // 2)] = moved[:, first : first + split_out]
    out_totals = jnp.stack([out_totals[t] for t in range(members)])
    low = jnp.concatenate(
        [proj_total]
        + [
            lax.dynamic_index_in_dim(out_totals, jnp.bitwise_xor(member, j), 0, keepdims=False)
            for j in range(members)
        ],
        axis=1,
    )
    up_other, low = clock.sync(up_other, low)
    gains = add_swapped(add_swapped(clock.hold(gains), "wide", wide_bits[:1]), "seq", seq_bits)
    up_grad = low_sum(up_own, up_other)
    gate_own, gate_other = owner_start(gate_grad)
    up_grad = spread_grad(clock.hold(up_grad), far_bits)
    other = swap(low, "seq", 1)
    left, right = jnp.where(is_low, low, other), jnp.where(is_low, other, low)
    attn_grad = jnp.concatenate(
        [left[:, :half_proj], right[:, :half_proj], left[:, half_proj:], right[:, half_proj:]],
        axis=1,
    ).astype(f32)
    mlp_grad = unpack(spread_grad(clock.hold(down_grad), seq_bits[:1]), pieces, 2, [])
    gate_other, up_grad, attn_grad, mlp_grad, gains = clock.sync(
        gate_other, up_grad, attn_grad, mlp_grad, gains
    )
    gate_grad = spread_grad(low_sum(gate_own, gate_other), far_bits)
    mlp_grad = unpack(spread_grad(clock.hold(up_grad), seq_bits[:1]), pieces, 1, [mlp_grad])
    gate_grad, mlp_grad = clock.sync(gate_grad, mlp_grad)
    mlp_grad = unpack(spread_grad(gate_grad, seq_bits[:1]), pieces, 0, [mlp_grad])
    return (
        jnp.stack(layer_out),
        jnp.stack(grad_tokens),
        attn_grad,
        mlp_grad,
        gains[0],
        gains[1],
        gains[2],
        gains[3],
    )


def solution(mesh):
    placed = (
        P("seq", "wide", None),
        P("seq", "wide", None),
        P("seq"),
        P("wide", None),
        P(),
        P(),
        P(None, "wide", None),
        P(),
        P(),
        P(),
        P(),
        P(),
        P(),
    )
    return jax.shard_map(
        per_device,
        mesh=mesh,
        in_specs=placed,
        out_specs=(
            P("seq", "wide", None),
            P("seq", "wide", None),
            P("wide", None),
            P(None, "wide", None),
            P(),
            P(),
            P(),
            P(),
        ),
        check_vma=False,
    )
```

```python
import functools
import math

import jax
import jax.numpy as jnp
from jax import lax
from jax.experimental import pallas as pl
from jax.experimental.pallas import tpu as pltpu
from jax.sharding import PartitionSpec as P

QUERY_HEADS = 8
KEY_VALUE_HEADS = 4
HEAD_SIZE = 256
PAIRED = QUERY_HEADS // KEY_VALUE_HEADS

eps_norm = 1e-06
soft_cap = 50.0
rope_base = 10000.0
gelu_coeff = math.sqrt(2.0 / math.pi)
f32 = jnp.float32
bf16 = jnp.bfloat16
VMEM_LIMIT = 56 * 1024 * 1024


def dot(a, b, dims):
    return lax.dot_general(a, b, (dims, ((), ())), preferred_element_type=f32)


NN = ((1,), (0,))
NT = ((1,), (1,))
TN = ((0,), (0,))


def inverse_powers(exponents):
    return 1.0 / jnp.left_shift(jnp.ones_like(exponents), exponents).astype(f32)


def norm_factor(values):
    return lax.rsqrt(jnp.mean(values * values, axis=-1, keepdims=True) + eps_norm)


def norm_back(values, factor, gain, grad):
    scaled = grad * gain
    inner = jnp.mean(values * scaled, axis=-1, keepdims=True)
    grad_values = factor * scaled - values * (factor * factor * factor * inner)
    return grad_values, jnp.sum(grad * values * factor, axis=0)


def gelu_parts(values):
    inner = gelu_coeff * (values + 0.044715 * values * values * values)
    return jnp.tanh(inner)


def rotary_rows(positions):
    half_dim = HEAD_SIZE // 2
    frequency = jnp.exp(
        jnp.arange(half_dim, dtype=f32) * (-2.0 * math.log(rope_base) / HEAD_SIZE)
    )
    angles = positions.astype(f32)[:, None] * frequency[None, :]
    return jnp.cos(angles), jnp.sin(angles)


def ring_place(index, size):
    return jnp.where(index % 2 == 0, index // 2, size - 1 - index // 2)


def ring_index(place, size):
    return jnp.where(place < size // 2, 2 * place, 2 * (size - 1 - place) + 1)


def ring_perms(size):
    order = list(range(0, size, 2)) + list(range(size - 1, 0, -2))
    up = [
        (base + order[i], base + order[(i + 1) % size])
        for base in range(0, lax.axis_size("wide"), size)
        for i in range(size)
    ]
    return up, [(b, a) for a, b in up]


def ring_offsets(size):
    out = [0]
    for k in range(1, size // 2):
        out += [-k, k]
    return out + [size // 2]


class Clock:
    def __init__(self, token):
        self.token = token

    def sync(self, *arrays):
        *arrays, self.token = lax.optimization_barrier(tuple(arrays) + (self.token,))
        return arrays

    def hold(self, value):
        return lax.optimization_barrier((value, self.token))[0]


def hop(a, b, size):
    up, down = ring_perms(size)
    return lax.ppermute(a, "wide", up), lax.ppermute(b, "wide", down)


def low_sum(*terms):
    return sum(t.astype(f32) for t in terms).astype(bf16)


def halves(value):
    half = value.shape[0] // 2
    return value[:half], value[half:]


def add_first(whole, part):
    count = part.shape[0]
    return jnp.concatenate([low_sum(whole[:count], part), whole[count:].astype(bf16)], axis=0)


def add_last(whole, part):
    count = whole.shape[0] - part.shape[0]
    return jnp.concatenate([whole[:count].astype(bf16), low_sum(whole[count:], part)], axis=0)


def ring_gather(clock, value, size, beside=lambda step: ()):
    a = b = clock.hold(value)
    out, other = [a], []
    for k in range(1, size // 2 + 1):
        if k == size // 2:
            a, b = halves(a)[0], halves(b)[1]
        work = beside(k - 1)
        a, b = hop(a, b, size)
        a, b, *work = clock.sync(a, b, *work)
        out += [a, b]
        other.append(work)
    return out, other


def ring_scatter(clock, part_of, rows, size, beside=lambda step: ()):
    a, b = halves(clock.hold(part_of(size // 2).astype(bf16)))
    other = []
    for k in range(size // 2 - 1, -1, -1):
        work = beside(size // 2 - 1 - k)
        a, b = hop(a, b, size)
        a, b, *work = clock.sync(a, b, *work)
        other.append(work)
        if k == size // 2 - 1 and k > 0:
            a = add_first(part_of(k), a)
            b = add_last(part_of(-k), b)
        elif k > 0:
            a = low_sum(part_of(k), a)
            b = low_sum(part_of(-k), b)
    return part_of(0).astype(f32) + a.astype(f32) + b.astype(f32), other


def swap(value, axis, bit):
    size = lax.axis_size(axis)
    return lax.ppermute(value, axis, [(i, i ^ bit) for i in range(size)])


def all_to_all(value):
    return lax.all_to_all(value, "wide", split_axis=0, concat_axis=0, tiled=True)


def heads_all_to_all(value):
    size = lax.axis_size("wide")
    classes = size // KEY_VALUE_HEADS
    groups = [list(range(c, size, classes)) for c in range(classes)]
    return lax.all_to_all(
        value, "wide", split_axis=0, concat_axis=0, axis_index_groups=groups, tiled=True
    )


def class_ring(value):
    size = lax.axis_size("wide")
    classes = size // KEY_VALUE_HEADS
    perm = [(i, i // classes * classes + (i + 1) % classes) for i in range(size)]
    return lax.ppermute(value, "wide", perm)


def slice_values(codes, width):
    lift = jnp.where(width == 0, 0.0, 0.5).astype(bf16)
    large = jnp.where(width == 0, 0.0, jnp.where(width == 1, 1.5 * 2**11, 1.5 * 2**13)).astype(bf16)
    top = jnp.where(width == 0, 127.0, jnp.where(width == 1, 112.0, 64.0)).astype(bf16)
    return jnp.minimum(((codes + lift) + large) - large, top)


def proj_slice_kernel(places, info, *refs, blocks, count):
    code_refs, scale_ref, out_refs = refs[: 2 * blocks], refs[2 * blocks], refs[len(refs) - count :]
    mine = pl.program_id(1) == info[0]

    def write(code_ref):
        codes = code_ref[...]
        scale = scale_ref[...].astype(bf16)
        for s, out_ref in enumerate(out_refs):
            out_ref[...] = slice_values(codes, info[1 + s]) * scale

    for k in range(blocks):
        here = pl.program_id(0) == k
        pl.when(jnp.logical_and(here, mine))(functools.partial(write, code_refs[2 * k]))
        pl.when(jnp.logical_and(here, jnp.logical_not(mine)))(
            functools.partial(write, code_refs[2 * k + 1])
        )


def proj_slices(own, other, places, info, scale, width, weights, total, count):
    blocks = len(own)
    rows = own[0].shape[0]
    inputs = [block for pair in zip(own, other) for block in pair] + [scale]
    grid_spec = pltpu.PrefetchScalarGridSpec(
        num_scalar_prefetch=2,
        grid=(blocks, 2),
        in_specs=[pl.BlockSpec((rows, width), lambda k, j, p, i: (0, 0))] * (2 * blocks)
        + [pl.BlockSpec((1, width), lambda k, j, p, i: (0, j))]
        + [pl.BlockSpec(memory_space=pl.ANY)] * len(weights),
        out_specs=[pl.BlockSpec((rows, width), lambda k, j, p, i: (p[k], j))] * count,
    )
    return pl.pallas_call(
        functools.partial(proj_slice_kernel, blocks=blocks, count=count),
        grid_spec=grid_spec,
        out_shape=[jax.ShapeDtypeStruct((total * rows, 2 * width), bf16)] * count,
        input_output_aliases={2 + len(inputs) + s: s for s in range(len(weights))},
        compiler_params=pltpu.CompilerParams(vmem_limit_bytes=VMEM_LIMIT),
        cost_estimate=pl.CostEstimate(
            flops=20 * count * blocks * rows * width,
            bytes_accessed=4 * blocks * rows * width * (1 + count),
            transcendentals=0,
        ),
        name="proj_slices",
    )(places, info, *inputs, *weights)


def out_slice_kernel(places, info, *refs, split, count):
    inputs, scale_ref, out_refs = refs[: -1 - count], refs[-1 - count], refs[-count:]
    members = len(inputs) // 2
    member = info[1 + count]
    mine = pl.program_id(1) == info[0]

    def write(code_refs):
        scale = scale_ref[...].astype(bf16)
        for t, code_ref in enumerate(code_refs):
            first = pl.multiple_of(jnp.bitwise_xor(member, t) * split, 128)
            for s, out_ref in enumerate(out_refs):
                out_ref[:, pl.ds(first, split)] = slice_values(code_ref[0], info[1 + s]) * scale

    pl.when(mine)(lambda: write(inputs[:members]))
    pl.when(jnp.logical_not(mine))(lambda: write(inputs[members:]))


def out_slices(own, other, places, info, scale, count):
    blocks, rows, split = own[0].shape
    width = split * len(own)
    inputs = list(own) + list(other)
    grid_spec = pltpu.PrefetchScalarGridSpec(
        num_scalar_prefetch=2,
        grid=(blocks, 2),
        in_specs=[pl.BlockSpec((1, rows, split), lambda k, j, p, i: (k, 0, 0))] * len(inputs)
        + [pl.BlockSpec((rows, 1), lambda k, j, p, i: (p[k], 0))],
        out_specs=[pl.BlockSpec((rows, width), lambda k, j, p, i: (p[k], j))] * count,
    )
    return pl.pallas_call(
        functools.partial(out_slice_kernel, split=split, count=count),
        grid_spec=grid_spec,
        out_shape=[jax.ShapeDtypeStruct((blocks * rows, 2 * width), bf16)] * count,
        compiler_params=pltpu.CompilerParams(vmem_limit_bytes=VMEM_LIMIT),
        cost_estimate=pl.CostEstimate(
            flops=20 * count * blocks * rows * width,
            bytes_accessed=4 * blocks * rows * width * (1 + count),
            transcendentals=0,
        ),
        name="out_slices",
    )(places, info, *inputs, scale)


def own_slice_kernel(pieces, info, code_ref, row_ref, col_ref, *out_refs):
    count = len(out_refs) // 3
    for m in range(3):
        codes = code_ref[m].astype(f32).astype(bf16)
        scale = (row_ref[m] if m < 2 else col_ref[...]).astype(bf16)
        for s in range(count):
            out_refs[m * count + s][...] = slice_values(codes, info[1 + s]) * scale


def own_slices(codes, pieces, info, row_scale, col_scale, count):
    three, rows, cols = codes.shape
    steps = pieces.shape[0]
    piece = rows // steps
    grid_spec = pltpu.PrefetchScalarGridSpec(
        num_scalar_prefetch=2,
        grid=(steps,),
        in_specs=[
            pl.BlockSpec((three, piece, cols), lambda j, p, i: (0, p[j], 0)),
            pl.BlockSpec((2, piece, 1), lambda j, p, i: (0, j, 0)),
            pl.BlockSpec((1, cols), lambda j, p, i: (0, 0)),
        ],
        out_specs=[pl.BlockSpec((piece, cols), lambda j, p, i: (j, 0))] * (three * count),
    )
    return pl.pallas_call(
        own_slice_kernel,
        grid_spec=grid_spec,
        out_shape=[jax.ShapeDtypeStruct((2 * rows, cols), bf16)] * (three * count),
        compiler_params=pltpu.CompilerParams(vmem_limit_bytes=VMEM_LIMIT),
        cost_estimate=pl.CostEstimate(
            flops=10 * count * codes.size,
            bytes_accessed=codes.size * (4 + 2 * count),
            transcendentals=0,
        ),
        name="own_slices",
    )(pieces, info, codes, row_scale, col_scale)


def partner_slice_kernel(info, *refs, steps, count):
    piece_refs, scale_ref, out_refs = refs[:steps], refs[steps], refs[steps + 1 + count :]
    for j in range(steps):

        @pl.when(pl.program_id(0) == j)
        def _():
            codes = piece_refs[j][...]
            scale = scale_ref[...].astype(bf16)
            for s, out_ref in enumerate(out_refs):
                out_ref[...] = slice_values(codes, info[1 + s]) * scale


def partner_slices(pieces, info, scale, by_column, weights):
    steps = len(pieces)
    count = len(weights)
    piece, cols = pieces[0].shape
    if by_column:
        scale_spec = pl.BlockSpec((1, cols), lambda j, i: (0, 0))
    else:
        scale_spec = pl.BlockSpec((piece, 1), lambda j, i: (steps + j, 0))
    grid_spec = pltpu.PrefetchScalarGridSpec(
        num_scalar_prefetch=1,
        grid=(steps,),
        in_specs=[pl.BlockSpec((piece, cols), lambda j, i: (0, 0))] * steps
        + [scale_spec]
        + [pl.BlockSpec(memory_space=pl.ANY)] * count,
        out_specs=[pl.BlockSpec((piece, cols), lambda j, i: (steps + j, 0))] * count,
    )
    return pl.pallas_call(
        functools.partial(partner_slice_kernel, steps=steps, count=count),
        grid_spec=grid_spec,
        out_shape=[jax.ShapeDtypeStruct(w.shape, bf16) for w in weights],
        input_output_aliases={2 + steps + s: s for s in range(count)},
        compiler_params=pltpu.CompilerParams(vmem_limit_bytes=VMEM_LIMIT),
        cost_estimate=pl.CostEstimate(
            flops=10 * count * steps * piece * cols,
            bytes_accessed=2 * (1 + count) * steps * piece * cols,
            transcendentals=0,
        ),
        name="partner_slices",
    )(info, *pieces, scale, *weights)


def unpack_kernel(pieces, *refs, parts):
    first = 0
    for ref in refs[:parts]:
        width = ref.shape[1]
        refs[-1][0, :, first : first + width] = ref[...].astype(f32)
        first += width


def unpack(grads, pieces, matrix, held):
    steps = pieces.shape[0]
    rows = grads[0].shape[0]
    cols = sum(g.shape[1] for g in grads)
    piece = rows // steps
    grid_spec = pltpu.PrefetchScalarGridSpec(
        num_scalar_prefetch=1,
        grid=(steps,),
        in_specs=[pl.BlockSpec((piece, g.shape[1]), lambda j, p: (j, 0)) for g in grads]
        + [pl.BlockSpec(memory_space=pl.ANY)] * len(held),
        out_specs=pl.BlockSpec((1, piece, cols), lambda j, p: (matrix, p[j], 0)),
    )
    return pl.pallas_call(
        functools.partial(unpack_kernel, parts=len(grads)),
        grid_spec=grid_spec,
        out_shape=jax.ShapeDtypeStruct((3, rows, cols), f32),
        input_output_aliases={1 + len(grads): 0} if held else {},
        compiler_params=pltpu.CompilerParams(vmem_limit_bytes=VMEM_LIMIT),
        cost_estimate=pl.CostEstimate(
            flops=rows * cols, bytes_accessed=6 * rows * cols, transcendentals=0
        ),
        name="unpack",
    )(pieces, *grads, *held)


def tile_of(size):
    return 256 if size % 256 == 0 else size


def tiles_of(size, part):
    tile = tile_of(size)
    tiles = size // tile
    first_part = (tiles + 1) // 2
    if part is None or tiles == 1:
        return tile, 0, tiles
    return (tile, 0, first_part) if part == 0 else (tile, first_part, tiles - first_part)


def whole_spec(shape):
    return pl.BlockSpec(shape, lambda i: (0, 0))


def column_spec(rows, tile, first=0):
    return pl.BlockSpec((rows, tile), lambda i: (0, first + i))


def row_spec(tile, cols, first=0):
    return pl.BlockSpec((tile, cols), lambda i: (first + i, 0))


def kernel_call(kernel, grid, in_specs, out_specs, out_shape, flops, moved, name, held=()):
    inputs = len(in_specs)
    return pl.pallas_call(
        lambda *refs: kernel(*refs[:inputs], *refs[inputs + len(held) :]),
        grid=(grid,),
        in_specs=in_specs + [pl.BlockSpec(memory_space=pl.ANY)] * len(held),
        out_specs=out_specs,
        out_shape=out_shape,
        input_output_aliases={inputs + i: i for i in range(len(held))},
        compiler_params=pltpu.CompilerParams(vmem_limit_bytes=VMEM_LIMIT),
        cost_estimate=pl.CostEstimate(flops=flops, bytes_accessed=moved, transcendentals=0),
        name=name,
    )


def row_parts(rows):
    part = 512 if rows % 512 == 0 else rows
    return [slice(first, first + part) for first in range(0, rows, part)]


def open_kernel(x_ref, wg_ref, wu_ref, gate_ref, up_ref, hidden_ref):
    for part in row_parts(x_ref.shape[0]):
        x = x_ref[part]
        gate = dot(x, wg_ref[...], NT)
        up = dot(x, wu_ref[...], NT)
        gate_ref[part] = gate
        up_ref[part] = up
        hidden_ref[part] = (gate * (0.5 + 0.5 * gelu_parts(gate)) * up).astype(bf16)


def open_forward(x, gate_weights, up_weights, part, held=()):
    rows, depth = x.shape
    hidden = gate_weights.shape[0]
    tile, first, tiles = tiles_of(hidden, part)
    if held and tiles * tile == hidden:
        return list(held)
    return kernel_call(
        open_kernel,
        tiles,
        [whole_spec(x.shape)] + [row_spec(tile, depth, first)] * 2,
        [column_spec(rows, tile, first)] * 3,
        [jax.ShapeDtypeStruct((rows, hidden), t) for t in (f32, f32, bf16)],
        4 * rows * depth * tile * tiles,
        2 * rows * depth + tiles * tile * (4 * depth + 10 * rows),
        "open_forward",
        held,
    )(x, gate_weights, up_weights, *held)


def open_back_kernel(x_ref, wd_ref, gate_ref, up_ref, grad_gate_ref, grad_up_ref):
    for part in row_parts(x_ref.shape[0]):
        grad = dot(x_ref[part], wd_ref[...], NT)
        gate = gate_ref[part]
        square = gate * gate
        bounded = jnp.tanh(gate * (gelu_coeff + (0.044715 * gelu_coeff) * square))
        half = 0.5 + 0.5 * bounded
        steep = (0.5 * gelu_coeff) + (1.5 * 0.044715 * gelu_coeff) * square
        slope = half + gate * (1.0 - bounded * bounded) * steep
        grad_gate_ref[part] = (grad * up_ref[part] * slope).astype(bf16)
        grad_up_ref[part] = (grad * (gate * half)).astype(bf16)


def open_back(x, down_weights, gate, up, part, held=()):
    rows, depth = x.shape
    hidden = down_weights.shape[0]
    tile, first, tiles = tiles_of(hidden, part)
    if held and tiles * tile == hidden:
        return list(held)
    return kernel_call(
        open_back_kernel,
        tiles,
        [whole_spec(x.shape), row_spec(tile, depth, first)] + [column_spec(rows, tile, first)] * 2,
        [column_spec(rows, tile, first)] * 2,
        [jax.ShapeDtypeStruct((rows, hidden), bf16)] * 2,
        2 * rows * depth * tile * tiles,
        2 * rows * depth + tiles * tile * (2 * depth + 12 * rows),
        "open_back",
        held,
    )(x, down_weights, gate, up, *held)


def input_back_kernel(gate_ref, up_ref, wg_ref, wu_ref, out_ref):
    out_ref[...] = (
        dot(gate_ref[...], wg_ref[...], NN) + dot(up_ref[...], wu_ref[...], NN)
    ).astype(bf16)


def input_back(grad_gate, grad_up, gate_weights, up_weights, part, held=()):
    rows, hidden = grad_gate.shape
    depth = gate_weights.shape[1]
    tile, first, tiles = tiles_of(depth, part)
    if held and tiles * tile == depth:
        return list(held)
    return kernel_call(
        input_back_kernel,
        tiles,
        [whole_spec(grad_gate.shape)] * 2 + [column_spec(hidden, tile, first)] * 2,
        [column_spec(rows, tile, first)],
        [jax.ShapeDtypeStruct((rows, depth), bf16)],
        4 * rows * hidden * tile * tiles,
        4 * rows * hidden + tiles * tile * (4 * hidden + 2 * rows),
        "input_back",
        held,
    )(grad_gate, grad_up, gate_weights, up_weights, *held)


def weight_kernel(*refs, count):
    out_ref = refs[-1]
    total = dot(refs[0][...], refs[count][...], TN)
    for s in range(1, count):
        total = total + dot(refs[s][...], refs[count + s][...], TN)
    out_ref[...] = total.astype(bf16)


def weight_back(lefts, rights):
    count = len(lefts)
    rows, hidden = lefts[0].shape
    depth = rights[0].shape[1]
    tile = tile_of(hidden)
    return kernel_call(
        functools.partial(weight_kernel, count=count),
        hidden // tile,
        [column_spec(rows, tile)] * count + [whole_spec((rows, depth))] * count,
        row_spec(tile, depth),
        jax.ShapeDtypeStruct((hidden, depth), bf16),
        2 * count * rows * depth * hidden,
        2 * count * rows * (hidden + depth) + 2 * hidden * depth,
        "weight_back",
    )(*lefts, *rights)


def turn(values, cosine, sine):
    half = HEAD_SIZE // 2
    out = []
    for j in range(values.shape[1] // HEAD_SIZE):
        a = values[:, j * HEAD_SIZE : j * HEAD_SIZE + half]
        b = values[:, j * HEAD_SIZE + half : (j + 1) * HEAD_SIZE]
        out += [a * cosine - b * sine, b * cosine + a * sine]
    return jnp.concatenate(out, axis=1)


def project_kernel(x_ref, wq_ref, wk_ref, wv_ref, cos_ref, sin_ref, q_ref, kv_ref):
    x = x_ref[...]
    cosine, sine = cos_ref[...], sin_ref[...]
    scale = HEAD_SIZE ** (-0.5)
    q_ref[0] = (turn(dot(x, wq_ref[...], NN), cosine, sine) * scale).astype(bf16)
    kv_ref[0, :, :HEAD_SIZE] = turn(dot(x, wk_ref[...], NN), cosine, sine).astype(bf16)
    kv_ref[0, :, HEAD_SIZE:] = dot(x, wv_ref[...], NN).astype(bf16)


def project(normed, weights, cosine, sine):
    rows, depth = normed.shape
    cols = PAIRED * HEAD_SIZE
    first_key = QUERY_HEADS
    first_value = QUERY_HEADS + KEY_VALUE_HEADS
    whole = lambda shape: pl.BlockSpec(shape, lambda h: (0, 0))
    return pl.pallas_call(
        project_kernel,
        grid=(KEY_VALUE_HEADS,),
        in_specs=[
            whole((rows, depth)),
            pl.BlockSpec((depth, cols), lambda h: (0, h)),
            pl.BlockSpec((depth, HEAD_SIZE), lambda h: (0, first_key + h)),
            pl.BlockSpec((depth, HEAD_SIZE), lambda h: (0, first_value + h)),
            whole(cosine.shape),
            whole(sine.shape),
        ],
        out_specs=[
            pl.BlockSpec((1, rows, cols), lambda h: (h, 0, 0)),
            pl.BlockSpec((1, rows, 2 * HEAD_SIZE), lambda h: (h, 0, 0)),
        ],
        out_shape=[
            jax.ShapeDtypeStruct((KEY_VALUE_HEADS, rows, cols), bf16),
            jax.ShapeDtypeStruct((KEY_VALUE_HEADS, rows, 2 * HEAD_SIZE), bf16),
        ],
        compiler_params=pltpu.CompilerParams(vmem_limit_bytes=VMEM_LIMIT),
        cost_estimate=pl.CostEstimate(
            flops=2 * rows * weights.size, bytes_accessed=2 * weights.size, transcendentals=0
        ),
        name="project",
    )(normed, weights, weights, weights, cosine, sine)


def turn_back_kernel(*refs, count):
    q_refs, kv_refs = refs[:count], refs[count : 2 * count]
    cos_ref, sin_ref, out_ref = refs[2 * count :]
    j = pl.program_id(1)
    scale = HEAD_SIZE ** (-0.5)
    keys = KEY_VALUE_HEADS // PAIRED
    for s in range(count):
        here = pl.program_id(0) == s

        @pl.when(jnp.logical_and(here, j < KEY_VALUE_HEADS))
        def _():
            grad = q_refs[s][0].astype(f32) * scale
            out_ref[...] = turn(grad, cos_ref[...], -sin_ref[...]).astype(bf16)

        @pl.when(jnp.logical_and(here, jnp.logical_and(j >= KEY_VALUE_HEADS, j < KEY_VALUE_HEADS + keys)))
        def _():
            grad = jnp.concatenate([kv_refs[s][i, :, :HEAD_SIZE] for i in range(PAIRED)], axis=1)
            out_ref[...] = turn(grad.astype(f32), cos_ref[...], -sin_ref[...]).astype(bf16)

        @pl.when(jnp.logical_and(here, j >= KEY_VALUE_HEADS + keys))
        def _():
            out_ref[...] = jnp.concatenate(
                [kv_refs[s][i, :, HEAD_SIZE:] for i in range(PAIRED)], axis=1
            )


def turn_back(queries, pairs, cosine, sine):
    count = len(queries)
    heads, rows, cols = queries[0].shape
    keys = heads // PAIRED
    grid = (count, heads + 2 * keys)
    whole = pl.BlockSpec(cosine.shape, lambda s, j: (0, 0))
    return pl.pallas_call(
        functools.partial(turn_back_kernel, count=count),
        grid=grid,
        in_specs=[
            pl.BlockSpec((1, rows, cols), lambda s, j: (jnp.minimum(j, heads - 1), 0, 0))
        ]
        * count
        + [
            pl.BlockSpec(
                (PAIRED, rows, cols), lambda s, j: (jnp.maximum(j - heads, 0) % keys, 0, 0)
            )
        ]
        * count
        + [whole, whole],
        out_specs=pl.BlockSpec((rows, cols), lambda s, j: (s, j)),
        out_shape=jax.ShapeDtypeStruct((count * rows, grid[1] * cols), bf16),
        compiler_params=pltpu.CompilerParams(vmem_limit_bytes=VMEM_LIMIT),
        cost_estimate=pl.CostEstimate(
            flops=4 * count * rows * grid[1] * cols,
            bytes_accessed=4 * count * rows * grid[1] * cols,
            transcendentals=0,
        ),
        name="turn_back",
    )(*queries, *pairs, cosine, sine)


def tile_positions(tile, count, start, class_index, class_rows, rows):
    index = lax.broadcasted_iota(jnp.int32, (count, 1), 0)
    place = start + jnp.bitwise_and(index, tile - 1)
    shift = class_rows.bit_length() - 1
    return (
        jnp.right_shift(place, shift) * rows
        + class_index * class_rows
        + jnp.bitwise_and(place, class_rows - 1)
    )


def stack_heads(block):
    return jnp.concatenate(
        [block[:, j * HEAD_SIZE : (j + 1) * HEAD_SIZE] for j in range(PAIRED)], axis=0
    )


def key_places(group, class_index, classes, rows):
    index = lax.broadcasted_iota(jnp.int32, (1, classes * rows), 1)
    shift = rows.bit_length() - 1
    back = jnp.bitwise_and(class_index - jnp.right_shift(index, shift), classes - 1)
    return (group * classes + back) * rows + jnp.bitwise_and(index, rows - 1)


def held_block(refs, group, cols):
    return jnp.concatenate([ref[group, :, cols] for ref in refs], axis=0)


def group_range(start, tile, class_rows, classes):
    return start // class_rows // classes, (start + tile - 1) // class_rows // classes + 1


def attn_forward_kernel(info, q_ref, *refs, tile, class_rows, rows, classes):
    kv_refs = refs[:classes]
    att_ref, exact_ref, lse_ref = refs[classes:]
    start = pl.program_id(0) * tile
    free, total = group_range(start, tile, class_rows, classes)
    queries = stack_heads(q_ref[...])
    count = queries.shape[0]
    position = tile_positions(tile, count, start, info[0], class_rows, rows)

    def step(group, carry, masked):
        acc, row_sum = carry
        keys = held_block(kv_refs, group, slice(0, HEAD_SIZE))
        values = held_block(kv_refs, group, slice(HEAD_SIZE, 2 * HEAD_SIZE))
        raw = dot(queries, keys, NT)
        weight = jnp.exp(soft_cap * jnp.tanh(raw * (1.0 / soft_cap)))
        if masked:
            weight = jnp.where(
                key_places(group, info[0], classes, rows) <= position, weight, 0.0
            )
        row_sum = row_sum + jnp.sum(weight, axis=-1, keepdims=True)
        acc = acc + dot(weight.astype(bf16), values, NN)
        return acc, row_sum

    carry = (jnp.zeros((count, HEAD_SIZE), f32), jnp.zeros((count, 1), f32))
    carry = lax.fori_loop(0, free, functools.partial(step, masked=False), carry)
    acc, row_sum = lax.fori_loop(free, total, functools.partial(step, masked=True), carry)
    exact = acc / row_sum
    lse = jnp.log(row_sum)
    for j in range(PAIRED):
        cols = slice(j * HEAD_SIZE, (j + 1) * HEAD_SIZE)
        exact_ref[:, cols] = exact[j * tile : (j + 1) * tile]
        att_ref[:, cols] = exact[j * tile : (j + 1) * tile].astype(bf16)
        lse_ref[:, j * 128 : (j + 1) * 128] = jnp.broadcast_to(
            lse[j * tile : (j + 1) * tile], (tile, 128)
        )


def attn_forward(info, queries, pairs, class_rows, rows):
    count, cols = queries.shape
    classes = len(pairs)
    length = classes * pairs[0].shape[0] * rows
    tile = min(256, count)
    grid_spec = pltpu.PrefetchScalarGridSpec(
        num_scalar_prefetch=1,
        grid=(count // tile,),
        in_specs=[pl.BlockSpec((tile, cols), lambda i, c: (i, 0))]
        + [pl.BlockSpec(p.shape, lambda i, c: (0, 0, 0)) for p in pairs],
        out_specs=[
            pl.BlockSpec((tile, cols), lambda i, c: (i, 0)),
            pl.BlockSpec((tile, cols), lambda i, c: (i, 0)),
            pl.BlockSpec((tile, PAIRED * 128), lambda i, c: (i, 0)),
        ],
    )
    return pl.pallas_call(
        functools.partial(
            attn_forward_kernel, tile=tile, class_rows=class_rows, rows=rows, classes=classes
        ),
        grid_spec=grid_spec,
        out_shape=[
            jax.ShapeDtypeStruct((count, cols), bf16),
            jax.ShapeDtypeStruct((count, cols), f32),
            jax.ShapeDtypeStruct((count, PAIRED * 128), f32),
        ],
        compiler_params=pltpu.CompilerParams(vmem_limit_bytes=VMEM_LIMIT),
        cost_estimate=pl.CostEstimate(
            flops=2 * count * PAIRED * length * 2 * HEAD_SIZE,
            bytes_accessed=8 * count * cols + 4 * length * HEAD_SIZE,
            transcendentals=2 * count * PAIRED * length,
        ),
        name="attn_forward",
    )(info, queries, *pairs)


def attn_backward_kernel(info, q_ref, grad_ref, exact_ref, lse_ref, *refs, tile, class_rows, rows, classes):
    kv_refs, dq_ref = refs[:classes], refs[classes]
    dkv_refs, sum_ref = refs[classes + 1 : 2 * classes + 1], refs[2 * classes + 1]

    @pl.when(pl.program_id(0) == 0)
    def _():
        sum_ref[...] = jnp.zeros_like(sum_ref)

    start = pl.program_id(0) * tile
    free, total = group_range(start, tile, class_rows, classes)
    queries = stack_heads(q_ref[...])
    grads = stack_heads(grad_ref[...])
    count = queries.shape[0]
    delta = jnp.sum(grads.astype(f32) * stack_heads(exact_ref[...]), axis=-1, keepdims=True)
    lse = jnp.concatenate([lse_ref[:, j * 128 : j * 128 + 1] for j in range(PAIRED)], axis=0)
    position = tile_positions(tile, count, start, info[0], class_rows, rows)

    def step(group, acc, masked):
        keys = held_block(kv_refs, group, slice(0, HEAD_SIZE))
        values = held_block(kv_refs, group, slice(HEAD_SIZE, 2 * HEAD_SIZE))
        bounded = jnp.tanh(dot(queries, keys, NT) * (1.0 / soft_cap))
        probs = jnp.exp(soft_cap * bounded - lse)
        if masked:
            probs = jnp.where(key_places(group, info[0], classes, rows) <= position, probs, 0.0)
        grad_probs = dot(grads, values, NT)
        grad_raw = (probs * (grad_probs - delta) * (1.0 - bounded * bounded)).astype(bf16)
        sum_ref[group, :, HEAD_SIZE:] += dot(probs.astype(bf16), grads, TN)
        sum_ref[group, :, :HEAD_SIZE] += dot(grad_raw, queries, TN)
        return acc + dot(grad_raw, keys, NN)

    acc = jnp.zeros((count, HEAD_SIZE), f32)
    acc = lax.fori_loop(0, free, functools.partial(step, masked=False), acc)
    acc = lax.fori_loop(free, total, functools.partial(step, masked=True), acc)
    for j in range(PAIRED):
        dq_ref[:, j * HEAD_SIZE : (j + 1) * HEAD_SIZE] = acc[j * tile : (j + 1) * tile].astype(bf16)

    @pl.when(pl.program_id(0) == pl.num_programs(0) - 1)
    def _():
        for h, ref in enumerate(dkv_refs):
            ref[...] = sum_ref[:, h * rows : (h + 1) * rows, :].astype(bf16)


def attn_backward(info, queries, pairs, grads, exact, lse, class_rows, rows):
    count, cols = queries.shape
    classes = len(pairs)
    groups = pairs[0].shape[0]
    length = classes * groups * rows
    tile = min(256, count)
    row_spec = pl.BlockSpec((tile, cols), lambda i, c: (i, 0))
    pair_specs = [pl.BlockSpec(p.shape, lambda i, c: (0, 0, 0)) for p in pairs]
    grid_spec = pltpu.PrefetchScalarGridSpec(
        num_scalar_prefetch=1,
        grid=(count // tile,),
        in_specs=[
            row_spec,
            row_spec,
            row_spec,
            pl.BlockSpec((tile, PAIRED * 128), lambda i, c: (i, 0)),
        ]
        + pair_specs,
        out_specs=[row_spec] + pair_specs,
        scratch_shapes=[pltpu.VMEM((groups, classes * rows, 2 * HEAD_SIZE), f32)],
    )
    return pl.pallas_call(
        functools.partial(
            attn_backward_kernel, tile=tile, class_rows=class_rows, rows=rows, classes=classes
        ),
        grid_spec=grid_spec,
        out_shape=[jax.ShapeDtypeStruct((count, cols), bf16)]
        + [jax.ShapeDtypeStruct(p.shape, bf16) for p in pairs],
        compiler_params=pltpu.CompilerParams(vmem_limit_bytes=VMEM_LIMIT),
        cost_estimate=pl.CostEstimate(
            flops=5 * count * PAIRED * length * 2 * HEAD_SIZE,
            bytes_accessed=10 * count * cols + 8 * length * HEAD_SIZE,
            transcendentals=2 * count * PAIRED * length,
        ),
        name="attn_backward",
    )(info, queries, grads, exact, lse, *pairs)


def per_device(
    tokens,
    cotangent,
    widths,
    attn_codes,
    attn_exps,
    out_exps,
    mlp_codes,
    gate_exps,
    down_exps,
    gain_attn,
    gain_post_attn,
    gain_mlp,
    gain_post_mlp,
):
    wide = lax.axis_size("wide")
    seq_size = lax.axis_size("seq")
    wide_index = lax.axis_index("wide")
    seq_index = lax.axis_index("seq")
    side = seq_index % 2
    is_low = side == 0
    members = seq_size // 2
    member = seq_index // 2
    half_wide = wide // 2
    place = ring_place(wide_index, wide)
    count, rows, model_dim = tokens.shape
    classes = wide // KEY_VALUE_HEADS
    class_rows = rows // classes
    class_index = wide_index % classes
    head_cols = PAIRED * HEAD_SIZE
    proj_cols = attn_exps.shape[0]
    half_proj = proj_cols // 2
    half_out = (attn_codes.shape[1] - proj_cols) // 2
    split_out = half_out // members
    attn_rows = attn_codes.shape[0]
    hidden = mlp_codes.shape[1]
    offsets = ring_offsets(wide)
    order = {o: i for i, o in enumerate(ring_offsets(half_wide))}
    seqs = range(count)
    seq_bits = [1 << i for i in range(seq_size.bit_length() - 1)]
    far_bits = list(reversed(seq_bits[1:]))
    clock = Clock(widths)

    def index_at(offset):
        return ring_index(jnp.mod(place + offset, wide), wide)

    places = jnp.stack([index_at(o) for o in offsets]).astype(jnp.int32)
    info = jnp.concatenate(
        [side[None].astype(jnp.int32), widths, member[None].astype(jnp.int32)]
    )
    class_info = class_index[None].astype(jnp.int32)
    column_scale = inverse_powers(attn_exps)[None, :]
    output_scale = inverse_powers(out_exps)[:, None]

    relative = [0]
    for bit in reversed(seq_bits):
        relative = relative + [r | bit for r in relative]
    pieces = jnp.stack([jnp.bitwise_xor(seq_index, r) for r in relative]).astype(jnp.int32)
    piece_rows = hidden // seq_size
    partner = jnp.bitwise_xor(wide_index, half_wide)
    gate_scale = inverse_powers(gate_exps)
    row_scale = jnp.concatenate(
        [
            lax.dynamic_slice_in_dim(
                gate_scale, block * hidden + pieces[j] * piece_rows, piece_rows, 1
            )
            for block in (wide_index, partner)
            for j in range(seq_size)
        ],
        axis=1,
    )[:, :, None]
    down_scale = inverse_powers(down_exps)[None, :]

    def columns(first, size):
        return lax.dynamic_slice_in_dim(attn_codes, first, size, 1)

    payload = jnp.concatenate(
        [
            columns(side * half_proj, half_proj),
            columns(proj_cols + side * half_out + member * split_out, split_out),
        ],
        axis=1,
    ).astype(bf16)
    piece_codes = lax.dynamic_slice_in_dim(mlp_codes, seq_index * piece_rows, piece_rows, 1)
    inputs = [tokens[s].astype(f32) for s in seqs]
    grad_out = [cotangent[s].astype(f32) for s in seqs]
    cosine, sine = rotary_rows(wide_index * rows + jnp.arange(rows))

    blocks, others = [clock.hold(payload)], []
    proj_weights = []

    def slice_more(first, last):
        return proj_slices(
            blocks[first:last],
            others[first:last],
            places[first:last],
            info,
            column_scale,
            half_proj,
            proj_weights,
            wide,
            count,
        )

    a = b = blocks[0]
    sliced = 0
    steps = half_wide
    for k in range(1, steps + 1):
        if k == steps:
            a, b = halves(a)[0], halves(b)[1]
        passed = [swap(v, "seq", 1) for v in blocks[len(others) :]]
        a, b = hop(a, b, wide)
        work = []
        if k == 1:
            work = own_slices(mlp_codes, pieces, info, row_scale, down_scale, count)
            a, b, *work = clock.sync(a, b, *passed, *work)
            passed, own_weights = work[: len(passed)], work[len(passed) :]
        elif k == 2:
            work = [piece_codes[m].astype(bf16) for m in range(3)]
            for s in seqs:
                factor = norm_factor(clock.hold(inputs[s]))
                work += [factor, (inputs[s] * factor * gain_attn).astype(bf16)]
            a, b, *work = clock.sync(a, b, *passed, *work)
            passed, work = work[: len(passed)], work[len(passed) :]
            sends, work = work[:3], work[3:]
            input_factor, normed = work[0::2], work[1::2]
        else:
            more = len(others)
            work = slice_more(sliced, more) if more > sliced else []
            a, b, *work = clock.sync(a, b, *passed, *work)
            passed, work = work[: len(passed)], work[len(passed) :]
            if work:
                proj_weights, sliced = list(work), more
        others += passed
        blocks += [a, b] if k < steps else [jnp.concatenate([a, b], axis=0)]

    def exchange(m):
        return swap(clock.hold(sends[m]), "wide", half_wide)

    def share(held, bits):
        for bit in bits:
            held = held + [swap(value, "seq", bit) for value in held]
        return held

    def partner_weights(m, held):
        scale = row_scale[m] if m < 2 else down_scale
        return partner_slices(
            held, info, scale, m == 2, own_weights[m * count : (m + 1) * count]
        )

    received = exchange(0)
    others += [swap(clock.hold(v), "seq", 1) for v in blocks[len(others) :]]
    proj_weights = slice_more(sliced, wide)
    query_send, pair_send = [], []
    for s in seqs:
        query, pair = project(normed[s], proj_weights[s], cosine, sine)
        query_send.append(query.reshape(wide, class_rows, head_cols))
        pair_send.append(pair)
    sent = clock.sync(received, *query_send, *pair_send)
    received, sent = sent[0], sent[1:]
    query_send, pair_send = sent[:count], sent[count:]

    def spread(pair):
        held = [pair]
        for _ in range(classes - 1):
            held.append(class_ring(held[-1]))
        return held[1:]

    def two_parts(value):
        cut = value.shape[0] // 2
        return value[:cut], value[cut:]

    attended_send, exact, lse, queries, pairs = [], [], [], [], []

    def attend(s):
        out, full, log_sum = attn_forward(class_info, queries[s], pairs[s], class_rows, rows)
        return [out.reshape(wide, class_rows, head_cols), full, log_sum]

    def keep_attend(work):
        attended_send.append(work[0])
        exact.append(work[1])
        lse.append(work[2])

    pair_first = heads_all_to_all(clock.hold(pair_send[0]))
    own_out = jnp.stack([clock.hold(v)[:, half_proj:] for v in blocks])
    other_out = jnp.stack([clock.hold(v)[:, half_proj:] for v in others])
    pair_first, own_out, other_out = clock.sync(pair_first, own_out, other_out)
    out_own = share([clock.hold(own_out)], far_bits)
    moved = spread(pair_first)
    pair_last, *work = clock.sync(heads_all_to_all(clock.hold(pair_send[1])), *moved)
    pairs.append([pair_first] + work)
    part_a, part_b = two_parts(pair_last)
    query = all_to_all(clock.hold(query_send[0]))
    query, *work = clock.sync(query, *spread(part_a), *out_own)
    moved_a, out_own = work[: classes - 1], work[classes - 1 :]
    queries.append(query.reshape(wide * class_rows, head_cols))
    moved_b = spread(clock.hold(part_b))
    query = all_to_all(clock.hold(query_send[1]))
    out_other = [swap(v, "seq", 1) for v in out_own[1:]]
    gate_held = share([clock.hold(received)], far_bits)
    query, *work = clock.sync(query, *moved_b, *out_other, *attend(0))
    moved_b, work = work[: classes - 1], work[classes - 1 :]
    out_other, work = [other_out] + work[: len(out_other)], work[len(out_other) :]
    keep_attend(work)
    queries.append(query.reshape(wide * class_rows, head_cols))
    pairs.append(
        [pair_last] + [jnp.concatenate([x, y], axis=0) for x, y in zip(moved_a, moved_b)]
    )

    attended, branch, branch_factor, middle, middle_factor, normed_mlp = [], [], [], [], [], []

    def heads_to_rows(values):
        split = values.reshape(KEY_VALUE_HEADS, rows, head_cols)
        return jnp.transpose(split, (1, 0, 2)).reshape(rows, KEY_VALUE_HEADS * head_cols)

    def join(s):
        value = dot(attended[s], out_weights[s], NT)
        factor = norm_factor(value)
        mid = inputs[s] + value * factor * gain_post_attn
        mid_factor = norm_factor(mid)
        return [value, factor, mid, mid_factor, (mid * mid_factor * gain_mlp).astype(bf16)]

    def keep_join(work):
        for held, value in zip((branch, branch_factor, middle, middle_factor, normed_mlp), work):
            held.append(value)

    for s in seqs:
        back = all_to_all(clock.hold(attended_send[s]))
        if s == 0:
            out_weights = out_slices(out_own, out_other, places, info, output_scale, count)
            back, *work = clock.sync(back, *gate_held, *out_weights, *attend(count - 1))
            gate_held, work = work[: len(gate_held)], work[len(gate_held) :]
            out_weights, work = work[:count], work[count:]
            keep_attend(work)
        else:
            gate_held = share(gate_held, seq_bits[:1])
            back, *work = clock.sync(back, *gate_held, *join(s - 1))
            gate_held, work = work[: len(gate_held)], work[len(gate_held) :]
            keep_join(work)
        attended.append(heads_to_rows(back))

    received = exchange(1)
    gate_weights = partner_weights(0, [clock.hold(v) for v in gate_held])
    received, *work = clock.sync(received, *gate_weights, *join(count - 1))
    gate_weights, work = work[:count], work[count:]
    keep_join(work)

    def blocks_of(part):
        return lambda o: part[order[o] * rows : (order[o] + 1) * rows]

    gathered, gate, up, hidden_rows, mixed, parts = [], [], [], [], [], []

    def open_part(s, part, held=()):
        group = clock.hold(gathered[s])
        return open_forward(group, gate_weights[s], up_weights[s], part, held)

    def keep_open(work):
        gate.append(work[0])
        up.append(work[1])
        hidden_rows.append(work[2])

    def mix(s):
        return dot(clock.hold(hidden_rows[s]), down_weights[s], NN).astype(bf16)

    up_held = share([clock.hold(received)], far_bits)
    received, *up_held = clock.sync(exchange(2), *up_held)

    def beside_first(step):
        nonlocal up_held
        if step == 0:
            up_held = share(up_held, seq_bits[:1])
            return tuple(up_held) + tuple(share([clock.hold(received)], far_bits))
        if step == 1:
            return tuple(partner_weights(1, [clock.hold(v) for v in up_held]))
        return ()

    a = b = clock.hold(normed_mlp[0])
    blocks = [a]
    for k in range(1, half_wide // 2 + 1):
        if k == half_wide // 2:
            a, b = halves(a)[0], halves(b)[1]
        if k == 2:
            down_held = share(down_held, seq_bits[:1])
        work = beside_first(k - 1) + (tuple(down_held) if k == 2 else ())
        a, b = hop(a, b, half_wide)
        a, b, *work = clock.sync(a, b, *work)
        if k == 1:
            up_held, down_held = work[: len(up_held)], work[len(up_held) :]
        elif k == 2:
            up_weights, down_held = work[:count], work[count:]
        blocks += [a, b]
    gathered.append(jnp.concatenate(blocks, axis=0))

    def beside_second(step):
        if step == 0:
            return open_part(0, None)
        if step == 1:
            return partner_weights(2, [clock.hold(v) for v in down_held])
        return ()

    a = b = clock.hold(normed_mlp[1])
    blocks = [a]
    for k in range(1, half_wide // 2 + 1):
        if k == half_wide // 2:
            a, b = halves(a)[0], halves(b)[1]
        work = beside_second(k - 1)
        a, b = hop(a, b, half_wide)
        a, b, *work = clock.sync(a, b, *work)
        if k == 1:
            keep_open(work)
        elif k == 2:
            down_weights = work
        blocks += [a, b]
    gathered.append(jnp.concatenate(blocks, axis=0))
    parts.append(clock.sync(mix(0))[0])

    layer_out, grad_mixed, gain_fourth = [], [], 0.0

    def finish(s):
        nonlocal gain_fourth
        factor = norm_factor(mixed[s])
        layer_out.append((middle[s] + mixed[s] * factor * gain_post_mlp).astype(bf16))
        grad, gain = norm_back(mixed[s], factor, gain_post_mlp, grad_out[s])
        grad_mixed.append(grad.astype(bf16))
        gain_fourth = gain_fourth + gain

    grad_group, grad_gate, grad_up, grad_parts, grad_normed_mlp = [], [], [], [], []

    def back_hidden(s, part, held=()):
        group = clock.hold(grad_group[s])
        return open_back(group, down_weights[s], gate[s], up[s], part, held)

    def back_input(s, part, held=()):
        grad = clock.hold(grad_gate[s])
        return input_back(grad, grad_up[s], gate_weights[s], up_weights[s], part, held)

    def keep_back(work):
        grad_gate.append(work[0])
        grad_up.append(work[1])

    def first_sum(part):
        a, b = hop(*halves(clock.hold(blocks_of(part)(half_wide // 2))), half_wide)
        return a, b

    def rest_sum(part, a, b, beside=lambda step: ()):
        part_of = blocks_of(part)
        other = []
        for k in range(half_wide // 2 - 1, 0, -1):
            if k == half_wide // 2 - 1:
                a = add_first(part_of(k), a)
                b = add_last(part_of(-k), b)
            else:
                a = low_sum(part_of(k), a)
                b = low_sum(part_of(-k), b)
            work = beside(half_wide // 2 - 1 - k)
            a, b = hop(a, b, half_wide)
            a, b, *work = clock.sync(a, b, *work)
            other.append(work)
        return part_of(0).astype(f32) + a.astype(f32) + b.astype(f32), other

    a, b = first_sum(parts[0])
    a, b, *opened = clock.sync(a, b, *open_part(1, 0))
    total, work = rest_sum(
        parts[0], a, b, lambda step: () if step else tuple(open_part(1, 1, opened))
    )
    keep_open(work[0])
    mixed.append(total)
    finish(0)
    parts.append(mix(1))
    blocks, work = ring_gather(
        clock, grad_mixed[0], half_wide, lambda k: (parts[1],) if k == 0 else ()
    )
    parts[1] = work[0][0]
    grad_group.append(jnp.concatenate(blocks, axis=0))
    a, b = first_sum(parts[1])
    a, b, *opened = clock.sync(a, b, *back_hidden(0, 0))

    def beside_last(step):
        if step:
            return ()
        keep_back(back_hidden(0, 1, opened))
        return (grad_gate[0], grad_up[0], *input_back(
            grad_gate[0], grad_up[0], gate_weights[0], up_weights[0], 0, ()
        ))

    total, work = rest_sum(parts[1], a, b, beside_last)
    grad_gate[0], grad_up[0], opened = work[0][0], work[0][1], work[0][2:]
    mixed.append(total)
    finish(1)
    blocks, work = ring_gather(
        clock, grad_mixed[1], half_wide, lambda k: () if k else tuple(back_input(0, 1, opened))
    )
    grad_parts.append(work[0][0])
    grad_group.append(jnp.concatenate(blocks, axis=0))

    def weight_sum(lefts, rights):
        lefts = [clock.hold(v) for v in lefts]
        return weight_back(lefts, rights).reshape(2, hidden, model_dim)

    def part_sum(grad, bit):
        split = grad.reshape(2, 2, grad.shape[1] // 2, model_dim)
        return low_sum(split[:, 0], swap(split[:, 1], "seq", bit))

    grad_middle, grad_branch, grad_send = [], [], []
    gain_third = gain_second = 0.0

    def back_branch(s):
        nonlocal gain_third, gain_second
        grad, gain = norm_back(middle[s], middle_factor[s], gain_mlp, grad_normed_mlp[s])
        gain_third = gain_third + gain
        grad_mid = grad_out[s] + grad
        grad, gain = norm_back(branch[s], branch_factor[s], gain_post_attn, grad_mid)
        gain_second = gain_second + gain
        grad = grad.astype(bf16)
        send = dot(grad, out_weights[s], NN).astype(bf16)
        send = jnp.transpose(send.reshape(rows, KEY_VALUE_HEADS, head_cols), (1, 0, 2))
        return [grad_mid, grad, send.reshape(wide, class_rows, head_cols)]

    def keep_branch(work):
        grad_middle.append(work[0])
        grad_branch.append(work[1])
        grad_send.append(work[2])

    a, b = first_sum(grad_parts[0])
    a, b, *opened = clock.sync(a, b, *back_hidden(1, 0))

    def beside_back(step):
        if step:
            return ()
        keep_back(back_hidden(1, 1, opened))
        return (grad_gate[1], grad_up[1], *input_back(
            grad_gate[1], grad_up[1], gate_weights[1], up_weights[1], 0, ()
        ))

    total, work = rest_sum(grad_parts[0], a, b, beside_back)
    grad_gate[1], grad_up[1], opened = work[0][0], work[0][1], work[0][2:]
    grad_normed_mlp.append(total)
    grad_parts += clock.sync(*back_input(1, 1, opened))
    a, b = first_sum(grad_parts[1])
    a, b, *work = clock.sync(a, b, *back_branch(0))
    keep_branch(work)
    total, work = rest_sum(
        grad_parts[1],
        a,
        b,
        lambda step: () if step else (weight_sum(hidden_rows, grad_group),),
    )
    down_grad = work[0][0]
    grad_normed_mlp.append(total)

    def attend_back(s):
        dq, *dkv = attn_backward(
            class_info,
            queries[s],
            pairs[s],
            clock.hold(grad_heads[s]),
            exact[s],
            lse[s],
            class_rows,
            rows,
        )
        return [dq.reshape(wide, class_rows, head_cols)] + dkv

    def class_sum(dkv):
        total = dkv[1 % classes]
        for step in range(2, classes + 1):
            total = low_sum(dkv[step % classes], class_ring(total))
        return total

    def far_start(grad):
        split = grad.reshape(2, 2, grad.shape[1] // 2, model_dim)
        return split[:, 0], swap(clock.hold(split[:, 1]), "seq", seq_bits[1])

    def far_end(kept, moved):
        grad = low_sum(kept, moved)
        for bit in seq_bits[2:]:
            grad = part_sum(grad, bit)
        return grad

    grad_heads, grad_attend = [], []
    query_back, pair_back = [], []

    def heads_of(value):
        return value.reshape(wide * class_rows, head_cols)

    back = all_to_all(clock.hold(grad_send[0]))
    down_grad = part_sum(down_grad, 1)
    back, down_grad, *work = clock.sync(back, down_grad, *back_branch(1))
    keep_branch(work)
    grad_heads.append(heads_of(back))
    all_normed = jnp.concatenate(normed, axis=0)
    all_attended = jnp.concatenate(attended, axis=0)
    all_branch = jnp.concatenate(grad_branch, axis=0)

    def half_dot(left, right, which, size):
        return dot(left, lax.dynamic_slice_in_dim(right, which * size, size, 1), TN)

    down_keep, down_move = far_start(down_grad)
    back = all_to_all(clock.hold(grad_send[1]))
    out_send = half_dot(all_branch, clock.hold(all_attended), 1 - side, half_out).astype(bf16)
    back, out_send, *work = clock.sync(back, out_send, *attend_back(0))
    grad_heads.append(heads_of(back))
    grad_attend.append(work)

    dq, *dkv = grad_attend[0]
    parts_of_pair = [two_parts(v) for v in dkv]
    out_sent = swap(out_send, "seq", 1)
    query = all_to_all(clock.hold(dq))
    pair_a = class_sum([v[0] for v in parts_of_pair])
    out_part = low_sum(
        half_dot(all_branch, clock.hold(all_attended), side, half_out), out_sent
    )
    query, pair_a, out_part, *work = clock.sync(query, pair_a, out_part, *attend_back(1))
    query_back.append(query)
    grad_attend.append(work)
    dq, *dkv = grad_attend[1]
    query = all_to_all(clock.hold(dq))
    pair_b = class_sum([clock.hold(v[1]) for v in parts_of_pair])
    up_grad = weight_sum(grad_up, gathered)
    query, pair_b, down_move, up_grad = clock.sync(query, pair_b, down_move, up_grad)
    query_back.append(query)

    out_pieces = {
        t: lax.dynamic_slice_in_dim(
            clock.hold(out_part), jnp.bitwise_xor(member, t) * split_out, split_out, 1
        )
        for t in range(members)
    }
    for bit in seq_bits[1:]:
        for t in sorted(out_pieces):
            if not t & (bit // 2) and t | (bit // 2) in out_pieces:
                out_pieces[t] = low_sum(
                    out_pieces[t], swap(out_pieces.pop(t | (bit // 2)), "seq", bit)
                )
    out_piece = out_pieces[0]

    pair = heads_all_to_all(clock.hold(jnp.concatenate([pair_a, pair_b], axis=0)))
    pair_sum = class_sum([clock.hold(v) for v in dkv])
    up_grad = part_sum(up_grad, 1)
    down_grad = far_end(down_keep, down_move)
    pair, pair_sum, up_grad, down_grad = clock.sync(pair, pair_sum, up_grad, down_grad)
    pair_back.append(pair)
    up_keep, up_move = far_start(up_grad)
    pair = heads_all_to_all(clock.hold(pair_sum))
    gate_grad = weight_sum(grad_gate, gathered)
    pair, out_piece, gate_grad = clock.sync(pair, out_piece, gate_grad)
    pair_back.append(pair)

    def column_parts(value, count):
        width = value.shape[1] // count
        return [value[:, i * width : (i + 1) * width] for i in range(count)]

    def exchange_grad(part):
        return swap(clock.hold(part), "wide", half_wide)

    def half_sum(grad):
        split = grad.reshape(2, 2, grad.shape[1] // 2, model_dim)
        return split[:, 0], split[:, 1]

    down_own = column_parts(down_grad[0], 3)
    down_send = column_parts(down_grad[1], 3)
    gate_keep, gate_send = half_sum(gate_grad)
    gate_moved = swap(gate_send, "seq", 1)
    moved, grad_proj = clock.sync(
        exchange_grad(down_send[0]),
        turn_back(
            [v.reshape(KEY_VALUE_HEADS, rows, head_cols) for v in query_back],
            pair_back,
            cosine,
            sine,
        ),
    )
    down_other = [moved]
    moved = exchange_grad(down_send[1])
    proj_send = half_dot(all_normed, clock.hold(grad_proj), 1 - side, half_proj).astype(bf16)
    moved, gate_moved, proj_send = clock.sync(moved, gate_moved, proj_send)
    down_other.append(moved)
    moved = exchange_grad(down_send[2])
    proj_sent = swap(proj_send, "seq", 1)
    gate_grad = low_sum(gate_keep, gate_moved)
    moved, proj_sent, up_move, gate_grad = clock.sync(moved, proj_sent, up_move, gate_grad)
    down_other.append(moved)
    proj_part = low_sum(half_dot(all_normed, clock.hold(grad_proj), side, half_proj), proj_sent)
    (proj_part,) = clock.sync(proj_part)
    gate_keep, gate_move = far_start(gate_grad)

    def part_of(o):
        first = index_at(o) * attn_rows
        return jnp.concatenate(
            [
                lax.dynamic_slice_in_dim(proj_part, first, attn_rows, 0),
                lax.dynamic_slice_in_dim(out_piece, first, attn_rows, 0),
            ],
            axis=1,
        )

    def spread_grad(grads, bits):
        for bit in bits:
            grads = [jnp.concatenate([g, swap(g, "seq", bit)], axis=0) for g in grads]
        return grads

    a, b = halves(clock.hold(part_of(wide // 2)))
    for k in range(wide // 2 - 1, -1, -1):
        step = wide // 2 - 1 - k
        a, b = hop(a, b, wide)
        work = []
        if step == 2:
            work = [gate_move]
        elif step == half_wide - 1:
            down_grad = spread_grad(
                [low_sum(clock.hold(x), y) for x, y in zip(down_own, down_other)], far_bits
            )
            work = down_grad
        a, b, *work = clock.sync(a, b, *work)
        if step == 2:
            gate_move = work[0]
        elif step == half_wide - 1:
            down_grad = work
        if step == 0:
            a, b = add_first(part_of(k), a), add_last(part_of(-k), b)
        elif k > 0:
            a, b = low_sum(part_of(k), a), low_sum(part_of(-k), b)
    total = low_sum(part_of(0), a, b)
    up_grad = far_end(up_keep, up_move)
    up_own, up_send = column_parts(up_grad[0], 2), column_parts(up_grad[1], 2)
    total, *up_send = clock.sync(total, *up_send)

    def input_grad(s):
        return dot(clock.hold(grad_proj[s * rows : (s + 1) * rows]), proj_weights[s], NT)

    def back_tokens(s, grad_normed):
        grad, gain = norm_back(inputs[s], input_factor[s], gain_attn, grad_normed)
        return (grad_middle[s] + grad).astype(bf16), gain

    def add_swapped(gains, axis, bits):
        for bit in bits:
            gains = gains + swap(gains, axis, bit)
        return gains

    proj_total = total[:, :half_proj]
    out_totals = {0: total[:, half_proj:]}
    for bit in seq_bits[1:]:
        sent = jnp.concatenate([proj_total] + [out_totals[t] for t in sorted(out_totals)], axis=1)
        moved = swap(sent, "seq", bit)
        proj_total = low_sum(proj_total, moved[:, :half_proj])
        for i, t in enumerate(sorted(out_totals)):
            first = half_proj + i * split_out
            out_totals[t | (bit // 2)] = moved[:, first : first + split_out]
    out_totals = jnp.stack([out_totals[t] for t in range(members)])
    low = jnp.concatenate(
        [proj_total]
        + [
            lax.dynamic_index_in_dim(out_totals, jnp.bitwise_xor(member, j), 0, keepdims=False)
            for j in range(members)
        ],
        axis=1,
    )
    moved, grad_first = clock.sync(exchange_grad(up_send[0]), input_grad(0))
    up_grad = [low_sum(up_own[0], moved)]
    moved, low, grad_last = clock.sync(exchange_grad(up_send[1]), low, input_grad(1))
    up_grad.append(low_sum(up_own[1], moved))
    gate_grad = far_end(gate_keep, gate_move)
    gate_own, gate_send = column_parts(gate_grad[0], 2), column_parts(gate_grad[1], 2)
    first_tokens, gain_first = back_tokens(0, grad_first)
    last_tokens, gain = back_tokens(1, grad_last)
    gains = jnp.stack([gain_first + gain, gain_second, gain_third, gain_fourth])
    wide_bits = [1 << i for i in range(wide.bit_length() - 1)]
    gains, *gate_send = clock.sync(add_swapped(gains, "wide", wide_bits[1:]), *gate_send)
    moved = exchange_grad(gate_send[0])
    up_grad = spread_grad([clock.hold(v) for v in up_grad], far_bits)
    other = swap(clock.hold(low), "seq", 1)
    moved, other, *up_grad = clock.sync(moved, other, *up_grad)
    gate_grad = [low_sum(gate_own[0], moved)]
    moved = exchange_grad(gate_send[1])
    gate_grad = spread_grad([clock.hold(v) for v in gate_grad], far_bits)
    gains = add_swapped(add_swapped(gains, "wide", wide_bits[:1]), "seq", seq_bits)
    left, right = jnp.where(is_low, low, other), jnp.where(is_low, other, low)
    attn_grad = jnp.concatenate(
        [left[:, :half_proj], right[:, :half_proj], left[:, half_proj:], right[:, half_proj:]],
        axis=1,
    ).astype(f32)
    down_grad = spread_grad([clock.hold(v) for v in down_grad], seq_bits[:1])
    mlp_grad = unpack(down_grad, pieces, 2, [])
    moved, attn_grad, mlp_grad, gains, *gate_grad = clock.sync(
        moved, attn_grad, mlp_grad, gains, *gate_grad
    )
    last = spread_grad([low_sum(gate_own[1], moved)], far_bits)
    up_grad = spread_grad([clock.hold(v) for v in up_grad], seq_bits[:1])
    mlp_grad = unpack(up_grad, pieces, 1, [mlp_grad])
    gate_grad = spread_grad([clock.hold(v) for v in gate_grad], seq_bits[:1])
    mlp_grad, *gate_grad = clock.sync(mlp_grad, *gate_grad, *last)
    gate_grad[1:] = spread_grad(gate_grad[1:], seq_bits[:1])
    mlp_grad = unpack(gate_grad, pieces, 0, [mlp_grad])
    grad_tokens = [first_tokens, last_tokens]
    return (
        jnp.stack(layer_out),
        jnp.stack(grad_tokens),
        attn_grad,
        mlp_grad,
        gains[0],
        gains[1],
        gains[2],
        gains[3],
    )


def solution(mesh):
    placed = (
        P("seq", "wide", None),
        P("seq", "wide", None),
        P("seq"),
        P("wide", None),
        P(),
        P(),
        P(None, "wide", None),
        P(),
        P(),
        P(),
        P(),
        P(),
        P(),
    )
    return jax.shard_map(
        per_device,
        mesh=mesh,
        in_specs=placed,
        out_specs=(
            P("seq", "wide", None),
            P("seq", "wide", None),
            P("wide", None),
            P(None, "wide", None),
            P(),
            P(),
            P(),
            P(),
        ),
        check_vma=False,
    )
```

```python
import functools
import math

import jax
import jax.numpy as jnp
from jax import lax
from jax.experimental import pallas as pl
from jax.experimental.pallas import tpu as pltpu
from jax.sharding import PartitionSpec as P

QUERY_HEADS = 8
KEY_VALUE_HEADS = 4
HEAD_SIZE = 256
PAIRED = QUERY_HEADS // KEY_VALUE_HEADS

eps_norm = 1e-06
soft_cap = 50.0
rope_base = 10000.0
gelu_coeff = math.sqrt(2.0 / math.pi)
f32 = jnp.float32
bf16 = jnp.bfloat16
VMEM_LIMIT = 56 * 1024 * 1024


def dot(a, b, dims):
    return lax.dot_general(a, b, (dims, ((), ())), preferred_element_type=f32)


NN = ((1,), (0,))
NT = ((1,), (1,))
TN = ((0,), (0,))


def inverse_powers(exponents):
    return 1.0 / jnp.left_shift(jnp.ones_like(exponents), exponents).astype(f32)


def norm_factor(values):
    return lax.rsqrt(jnp.mean(values * values, axis=-1, keepdims=True) + eps_norm)


def norm_back(values, factor, gain, grad):
    scaled = grad * gain
    inner = jnp.mean(values * scaled, axis=-1, keepdims=True)
    grad_values = factor * scaled - values * (factor * factor * factor * inner)
    return grad_values, jnp.sum(grad * values * factor, axis=0)


def gelu_parts(values):
    inner = gelu_coeff * (values + 0.044715 * values * values * values)
    return jnp.tanh(inner)


def rotary_rows(positions):
    half_dim = HEAD_SIZE // 2
    frequency = jnp.exp(
        jnp.arange(half_dim, dtype=f32) * (-2.0 * math.log(rope_base) / HEAD_SIZE)
    )
    angles = positions.astype(f32)[:, None] * frequency[None, :]
    return jnp.cos(angles), jnp.sin(angles)


def ring_place(index, size):
    return jnp.where(index % 2 == 0, index // 2, size - 1 - index // 2)


def ring_index(place, size):
    return jnp.where(place < size // 2, 2 * place, 2 * (size - 1 - place) + 1)


def ring_perms(size):
    order = list(range(0, size, 2)) + list(range(size - 1, 0, -2))
    up = [
        (base + order[i], base + order[(i + 1) % size])
        for base in range(0, lax.axis_size("wide"), size)
        for i in range(size)
    ]
    return up, [(b, a) for a, b in up]


def ring_offsets(size):
    out = [0]
    for k in range(1, size // 2):
        out += [-k, k]
    return out + [size // 2]


class Clock:
    def __init__(self, token):
        self.token = token

    def sync(self, *arrays):
        *arrays, self.token = lax.optimization_barrier(tuple(arrays) + (self.token,))
        return arrays

    def hold(self, value):
        return lax.optimization_barrier((value, self.token))[0]


def hop(a, b, size):
    up, down = ring_perms(size)
    return lax.ppermute(a, "wide", up), lax.ppermute(b, "wide", down)


def low_sum(*terms):
    return sum(t.astype(f32) for t in terms).astype(bf16)


def halves(value):
    half = value.shape[0] // 2
    return value[:half], value[half:]


def add_first(whole, part):
    count = part.shape[0]
    return jnp.concatenate([low_sum(whole[:count], part), whole[count:].astype(bf16)], axis=0)


def add_last(whole, part):
    count = whole.shape[0] - part.shape[0]
    return jnp.concatenate([whole[:count].astype(bf16), low_sum(whole[count:], part)], axis=0)


def ring_gather(clock, value, size, beside=lambda step: ()):
    a = b = clock.hold(value)
    out, other = [a], []
    for k in range(1, size // 2 + 1):
        if k == size // 2:
            a, b = halves(a)[0], halves(b)[1]
        work = beside(k - 1)
        a, b = hop(a, b, size)
        a, b, *work = clock.sync(a, b, *work)
        out += [a, b]
        other.append(work)
    return out, other


def ring_scatter(clock, part_of, rows, size, beside=lambda step: ()):
    a, b = halves(clock.hold(part_of(size // 2).astype(bf16)))
    other = []
    for k in range(size // 2 - 1, -1, -1):
        work = beside(size // 2 - 1 - k)
        a, b = hop(a, b, size)
        a, b, *work = clock.sync(a, b, *work)
        other.append(work)
        if k == size // 2 - 1 and k > 0:
            a = add_first(part_of(k), a)
            b = add_last(part_of(-k), b)
        elif k > 0:
            a = low_sum(part_of(k), a)
            b = low_sum(part_of(-k), b)
    return part_of(0).astype(f32) + a.astype(f32) + b.astype(f32), other


def swap(value, axis, bit):
    size = lax.axis_size(axis)
    return lax.ppermute(value, axis, [(i, i ^ bit) for i in range(size)])


def all_to_all(value):
    return lax.all_to_all(value, "wide", split_axis=0, concat_axis=0, tiled=True)


def heads_all_to_all(value):
    size = lax.axis_size("wide")
    classes = size // KEY_VALUE_HEADS
    groups = [list(range(c, size, classes)) for c in range(classes)]
    return lax.all_to_all(
        value, "wide", split_axis=0, concat_axis=0, axis_index_groups=groups, tiled=True
    )


def class_ring(value):
    size = lax.axis_size("wide")
    classes = size // KEY_VALUE_HEADS
    perm = [(i, i // classes * classes + (i + 1) % classes) for i in range(size)]
    return lax.ppermute(value, "wide", perm)


def slice_values(codes, width):
    lift = jnp.where(width == 0, 0.0, 0.5).astype(bf16)
    large = jnp.where(width == 0, 0.0, jnp.where(width == 1, 1.5 * 2**11, 1.5 * 2**13)).astype(bf16)
    top = jnp.where(width == 0, 127.0, jnp.where(width == 1, 112.0, 64.0)).astype(bf16)
    return jnp.minimum(((codes + lift) + large) - large, top)


def proj_slice_kernel(places, info, *refs, blocks, count):
    code_refs, scale_ref, out_refs = refs[: 2 * blocks], refs[2 * blocks], refs[len(refs) - count :]
    mine = pl.program_id(1) == info[0]

    def write(code_ref):
        codes = code_ref[...]
        scale = scale_ref[...].astype(bf16)
        for s, out_ref in enumerate(out_refs):
            out_ref[...] = slice_values(codes, info[1 + s]) * scale

    for k in range(blocks):
        here = pl.program_id(0) == k
        pl.when(jnp.logical_and(here, mine))(functools.partial(write, code_refs[2 * k]))
        pl.when(jnp.logical_and(here, jnp.logical_not(mine)))(
            functools.partial(write, code_refs[2 * k + 1])
        )


def proj_slices(own, other, places, info, scale, width, weights, total, count):
    blocks = len(own)
    rows = own[0].shape[0]
    inputs = [block for pair in zip(own, other) for block in pair] + [scale]
    grid_spec = pltpu.PrefetchScalarGridSpec(
        num_scalar_prefetch=2,
        grid=(blocks, 2),
        in_specs=[pl.BlockSpec((rows, width), lambda k, j, p, i: (0, 0))] * (2 * blocks)
        + [pl.BlockSpec((1, width), lambda k, j, p, i: (0, j))]
        + [pl.BlockSpec(memory_space=pl.ANY)] * len(weights),
        out_specs=[pl.BlockSpec((rows, width), lambda k, j, p, i: (p[k], j))] * count,
    )
    return pl.pallas_call(
        functools.partial(proj_slice_kernel, blocks=blocks, count=count),
        grid_spec=grid_spec,
        out_shape=[jax.ShapeDtypeStruct((total * rows, 2 * width), bf16)] * count,
        input_output_aliases={2 + len(inputs) + s: s for s in range(len(weights))},
        compiler_params=pltpu.CompilerParams(vmem_limit_bytes=VMEM_LIMIT),
        cost_estimate=pl.CostEstimate(
            flops=20 * count * blocks * rows * width,
            bytes_accessed=4 * blocks * rows * width * (1 + count),
            transcendentals=0,
        ),
        name="proj_slices",
    )(places, info, *inputs, *weights)


def out_slice_kernel(places, info, *refs, split, count):
    inputs, scale_ref, out_refs = refs[: -1 - count], refs[-1 - count], refs[-count:]
    members = len(inputs) // 2
    member = info[1 + count]
    mine = pl.program_id(1) == info[0]

    def write(code_refs):
        scale = scale_ref[...].astype(bf16)
        for t, code_ref in enumerate(code_refs):
            first = pl.multiple_of(jnp.bitwise_xor(member, t) * split, 128)
            for s, out_ref in enumerate(out_refs):
                out_ref[:, pl.ds(first, split)] = slice_values(code_ref[0], info[1 + s]) * scale

    pl.when(mine)(lambda: write(inputs[:members]))
    pl.when(jnp.logical_not(mine))(lambda: write(inputs[members:]))


def out_slices(own, other, places, info, scale, count):
    blocks, rows, split = own[0].shape
    width = split * len(own)
    inputs = list(own) + list(other)
    grid_spec = pltpu.PrefetchScalarGridSpec(
        num_scalar_prefetch=2,
        grid=(blocks, 2),
        in_specs=[pl.BlockSpec((1, rows, split), lambda k, j, p, i: (k, 0, 0))] * len(inputs)
        + [pl.BlockSpec((rows, 1), lambda k, j, p, i: (p[k], 0))],
        out_specs=[pl.BlockSpec((rows, width), lambda k, j, p, i: (p[k], j))] * count,
    )
    return pl.pallas_call(
        functools.partial(out_slice_kernel, split=split, count=count),
        grid_spec=grid_spec,
        out_shape=[jax.ShapeDtypeStruct((blocks * rows, 2 * width), bf16)] * count,
        compiler_params=pltpu.CompilerParams(vmem_limit_bytes=VMEM_LIMIT),
        cost_estimate=pl.CostEstimate(
            flops=20 * count * blocks * rows * width,
            bytes_accessed=4 * blocks * rows * width * (1 + count),
            transcendentals=0,
        ),
        name="out_slices",
    )(places, info, *inputs, scale)


def own_slice_kernel(pieces, info, code_ref, row_ref, col_ref, *out_refs):
    count = len(out_refs) // 3
    for m in range(3):
        codes = code_ref[m].astype(f32).astype(bf16)
        scale = (row_ref[m] if m < 2 else col_ref[...]).astype(bf16)
        for s in range(count):
            out_refs[m * count + s][...] = slice_values(codes, info[1 + s]) * scale


def own_slices(codes, pieces, info, row_scale, col_scale, count):
    three, rows, cols = codes.shape
    steps = pieces.shape[0]
    piece = rows // steps
    grid_spec = pltpu.PrefetchScalarGridSpec(
        num_scalar_prefetch=2,
        grid=(steps,),
        in_specs=[
            pl.BlockSpec((three, piece, cols), lambda j, p, i: (0, p[j], 0)),
            pl.BlockSpec((2, piece, 1), lambda j, p, i: (0, j, 0)),
            pl.BlockSpec((1, cols), lambda j, p, i: (0, 0)),
        ],
        out_specs=[pl.BlockSpec((piece, cols), lambda j, p, i: (j, 0))] * (three * count),
    )
    return pl.pallas_call(
        own_slice_kernel,
        grid_spec=grid_spec,
        out_shape=[jax.ShapeDtypeStruct((2 * rows, cols), bf16)] * (three * count),
        compiler_params=pltpu.CompilerParams(vmem_limit_bytes=VMEM_LIMIT),
        cost_estimate=pl.CostEstimate(
            flops=10 * count * codes.size,
            bytes_accessed=codes.size * (4 + 2 * count),
            transcendentals=0,
        ),
        name="own_slices",
    )(pieces, info, codes, row_scale, col_scale)


def partner_slice_kernel(info, *refs, steps, count):
    piece_refs, scale_ref, out_refs = refs[:steps], refs[steps], refs[steps + 1 + count :]
    for j in range(steps):

        @pl.when(pl.program_id(0) == j)
        def _():
            codes = piece_refs[j][...]
            scale = scale_ref[...].astype(bf16)
            for s, out_ref in enumerate(out_refs):
                out_ref[...] = slice_values(codes, info[1 + s]) * scale


def partner_slices(pieces, info, scale, by_column, weights):
    steps = len(pieces)
    count = len(weights)
    piece, cols = pieces[0].shape
    if by_column:
        scale_spec = pl.BlockSpec((1, cols), lambda j, i: (0, 0))
    else:
        scale_spec = pl.BlockSpec((piece, 1), lambda j, i: (steps + j, 0))
    grid_spec = pltpu.PrefetchScalarGridSpec(
        num_scalar_prefetch=1,
        grid=(steps,),
        in_specs=[pl.BlockSpec((piece, cols), lambda j, i: (0, 0))] * steps
        + [scale_spec]
        + [pl.BlockSpec(memory_space=pl.ANY)] * count,
        out_specs=[pl.BlockSpec((piece, cols), lambda j, i: (steps + j, 0))] * count,
    )
    return pl.pallas_call(
        functools.partial(partner_slice_kernel, steps=steps, count=count),
        grid_spec=grid_spec,
        out_shape=[jax.ShapeDtypeStruct(w.shape, bf16) for w in weights],
        input_output_aliases={2 + steps + s: s for s in range(count)},
        compiler_params=pltpu.CompilerParams(vmem_limit_bytes=VMEM_LIMIT),
        cost_estimate=pl.CostEstimate(
            flops=10 * count * steps * piece * cols,
            bytes_accessed=2 * (1 + count) * steps * piece * cols,
            transcendentals=0,
        ),
        name="partner_slices",
    )(info, *pieces, scale, *weights)


def unpack_kernel(pieces, *refs, parts):
    first = 0
    for ref in refs[:parts]:
        width = ref.shape[1]
        refs[-1][0, :, first : first + width] = ref[...].astype(f32)
        first += width


def unpack(grads, pieces, matrix, held):
    steps = pieces.shape[0]
    rows = grads[0].shape[0]
    cols = sum(g.shape[1] for g in grads)
    piece = rows // steps
    grid_spec = pltpu.PrefetchScalarGridSpec(
        num_scalar_prefetch=1,
        grid=(steps,),
        in_specs=[pl.BlockSpec((piece, g.shape[1]), lambda j, p: (j, 0)) for g in grads]
        + [pl.BlockSpec(memory_space=pl.ANY)] * len(held),
        out_specs=pl.BlockSpec((1, piece, cols), lambda j, p: (matrix, p[j], 0)),
    )
    return pl.pallas_call(
        functools.partial(unpack_kernel, parts=len(grads)),
        grid_spec=grid_spec,
        out_shape=jax.ShapeDtypeStruct((3, rows, cols), f32),
        input_output_aliases={1 + len(grads): 0} if held else {},
        compiler_params=pltpu.CompilerParams(vmem_limit_bytes=VMEM_LIMIT),
        cost_estimate=pl.CostEstimate(
            flops=rows * cols, bytes_accessed=6 * rows * cols, transcendentals=0
        ),
        name="unpack",
    )(pieces, *grads, *held)


def tile_of(size):
    return 256 if size % 256 == 0 else size


def tiles_of(size, part):
    tile = tile_of(size)
    tiles = size // tile
    first_part = (tiles + 1) // 2
    if part is None or tiles == 1:
        return tile, 0, tiles
    return (tile, 0, first_part) if part == 0 else (tile, first_part, tiles - first_part)


def whole_spec(shape):
    return pl.BlockSpec(shape, lambda i: (0, 0))


def column_spec(rows, tile, first=0):
    return pl.BlockSpec((rows, tile), lambda i: (0, first + i))


def row_spec(tile, cols, first=0):
    return pl.BlockSpec((tile, cols), lambda i: (first + i, 0))


def kernel_call(kernel, grid, in_specs, out_specs, out_shape, flops, moved, name, held=()):
    inputs = len(in_specs)
    return pl.pallas_call(
        lambda *refs: kernel(*refs[:inputs], *refs[inputs + len(held) :]),
        grid=(grid,),
        in_specs=in_specs + [pl.BlockSpec(memory_space=pl.ANY)] * len(held),
        out_specs=out_specs,
        out_shape=out_shape,
        input_output_aliases={inputs + i: i for i in range(len(held))},
        compiler_params=pltpu.CompilerParams(vmem_limit_bytes=VMEM_LIMIT),
        cost_estimate=pl.CostEstimate(flops=flops, bytes_accessed=moved, transcendentals=0),
        name=name,
    )


def row_parts(rows):
    part = 512 if rows % 512 == 0 else rows
    return [slice(first, first + part) for first in range(0, rows, part)]


def open_kernel(x_ref, wg_ref, wu_ref, gate_ref, up_ref, hidden_ref):
    for part in row_parts(x_ref.shape[0]):
        x = x_ref[part]
        gate = dot(x, wg_ref[...], NT)
        up = dot(x, wu_ref[...], NT)
        gate_ref[part] = gate
        up_ref[part] = up
        hidden_ref[part] = (gate * (0.5 + 0.5 * gelu_parts(gate)) * up).astype(bf16)


def open_forward(x, gate_weights, up_weights, part, held=()):
    rows, depth = x.shape
    hidden = gate_weights.shape[0]
    tile, first, tiles = tiles_of(hidden, part)
    if held and tiles * tile == hidden:
        return list(held)
    return kernel_call(
        open_kernel,
        tiles,
        [whole_spec(x.shape)] + [row_spec(tile, depth, first)] * 2,
        [column_spec(rows, tile, first)] * 3,
        [jax.ShapeDtypeStruct((rows, hidden), t) for t in (f32, f32, bf16)],
        4 * rows * depth * tile * tiles,
        2 * rows * depth + tiles * tile * (4 * depth + 10 * rows),
        "open_forward",
        held,
    )(x, gate_weights, up_weights, *held)


def open_back_kernel(x_ref, wd_ref, gate_ref, up_ref, grad_gate_ref, grad_up_ref):
    for part in row_parts(x_ref.shape[0]):
        grad = dot(x_ref[part], wd_ref[...], NT)
        gate = gate_ref[part]
        square = gate * gate
        bounded = jnp.tanh(gate * (gelu_coeff + (0.044715 * gelu_coeff) * square))
        half = 0.5 + 0.5 * bounded
        steep = (0.5 * gelu_coeff) + (1.5 * 0.044715 * gelu_coeff) * square
        slope = half + gate * (1.0 - bounded * bounded) * steep
        grad_gate_ref[part] = (grad * up_ref[part] * slope).astype(bf16)
        grad_up_ref[part] = (grad * (gate * half)).astype(bf16)


def open_back(x, down_weights, gate, up, part, held=()):
    rows, depth = x.shape
    hidden = down_weights.shape[0]
    tile, first, tiles = tiles_of(hidden, part)
    if held and tiles * tile == hidden:
        return list(held)
    return kernel_call(
        open_back_kernel,
        tiles,
        [whole_spec(x.shape), row_spec(tile, depth, first)] + [column_spec(rows, tile, first)] * 2,
        [column_spec(rows, tile, first)] * 2,
        [jax.ShapeDtypeStruct((rows, hidden), bf16)] * 2,
        2 * rows * depth * tile * tiles,
        2 * rows * depth + tiles * tile * (2 * depth + 12 * rows),
        "open_back",
        held,
    )(x, down_weights, gate, up, *held)


def input_back_kernel(gate_ref, up_ref, wg_ref, wu_ref, out_ref):
    out_ref[...] = (
        dot(gate_ref[...], wg_ref[...], NN) + dot(up_ref[...], wu_ref[...], NN)
    ).astype(bf16)


def input_back(grad_gate, grad_up, gate_weights, up_weights, part, held=()):
    rows, hidden = grad_gate.shape
    depth = gate_weights.shape[1]
    tile, first, tiles = tiles_of(depth, part)
    if held and tiles * tile == depth:
        return list(held)
    return kernel_call(
        input_back_kernel,
        tiles,
        [whole_spec(grad_gate.shape)] * 2 + [column_spec(hidden, tile, first)] * 2,
        [column_spec(rows, tile, first)],
        [jax.ShapeDtypeStruct((rows, depth), bf16)],
        4 * rows * hidden * tile * tiles,
        4 * rows * hidden + tiles * tile * (4 * hidden + 2 * rows),
        "input_back",
        held,
    )(grad_gate, grad_up, gate_weights, up_weights, *held)


def weight_kernel(*refs, count):
    out_ref = refs[-1]
    total = dot(refs[0][...], refs[count][...], TN)
    for s in range(1, count):
        total = total + dot(refs[s][...], refs[count + s][...], TN)
    out_ref[...] = total.astype(bf16)


def weight_back(lefts, rights):
    count = len(lefts)
    rows, hidden = lefts[0].shape
    depth = rights[0].shape[1]
    tile = tile_of(hidden)
    return kernel_call(
        functools.partial(weight_kernel, count=count),
        hidden // tile,
        [column_spec(rows, tile)] * count + [whole_spec((rows, depth))] * count,
        row_spec(tile, depth),
        jax.ShapeDtypeStruct((hidden, depth), bf16),
        2 * count * rows * depth * hidden,
        2 * count * rows * (hidden + depth) + 2 * hidden * depth,
        "weight_back",
    )(*lefts, *rights)


def turn(values, cosine, sine):
    half = HEAD_SIZE // 2
    out = []
    for j in range(values.shape[1] // HEAD_SIZE):
        a = values[:, j * HEAD_SIZE : j * HEAD_SIZE + half]
        b = values[:, j * HEAD_SIZE + half : (j + 1) * HEAD_SIZE]
        out += [a * cosine - b * sine, b * cosine + a * sine]
    return jnp.concatenate(out, axis=1)


def project_kernel(x_ref, wq_ref, wk_ref, wv_ref, cos_ref, sin_ref, q_ref, kv_ref):
    x = x_ref[...]
    cosine, sine = cos_ref[...], sin_ref[...]
    scale = HEAD_SIZE ** (-0.5)
    q_ref[0] = (turn(dot(x, wq_ref[...], NN), cosine, sine) * scale).astype(bf16)
    kv_ref[0, :, :HEAD_SIZE] = turn(dot(x, wk_ref[...], NN), cosine, sine).astype(bf16)
    kv_ref[0, :, HEAD_SIZE:] = dot(x, wv_ref[...], NN).astype(bf16)


def project(normed, weights, cosine, sine):
    rows, depth = normed.shape
    cols = PAIRED * HEAD_SIZE
    first_key = QUERY_HEADS
    first_value = QUERY_HEADS + KEY_VALUE_HEADS
    whole = lambda shape: pl.BlockSpec(shape, lambda h: (0, 0))
    return pl.pallas_call(
        project_kernel,
        grid=(KEY_VALUE_HEADS,),
        in_specs=[
            whole((rows, depth)),
            pl.BlockSpec((depth, cols), lambda h: (0, h)),
            pl.BlockSpec((depth, HEAD_SIZE), lambda h: (0, first_key + h)),
            pl.BlockSpec((depth, HEAD_SIZE), lambda h: (0, first_value + h)),
            whole(cosine.shape),
            whole(sine.shape),
        ],
        out_specs=[
            pl.BlockSpec((1, rows, cols), lambda h: (h, 0, 0)),
            pl.BlockSpec((1, rows, 2 * HEAD_SIZE), lambda h: (h, 0, 0)),
        ],
        out_shape=[
            jax.ShapeDtypeStruct((KEY_VALUE_HEADS, rows, cols), bf16),
            jax.ShapeDtypeStruct((KEY_VALUE_HEADS, rows, 2 * HEAD_SIZE), bf16),
        ],
        compiler_params=pltpu.CompilerParams(vmem_limit_bytes=VMEM_LIMIT),
        cost_estimate=pl.CostEstimate(
            flops=2 * rows * weights.size, bytes_accessed=2 * weights.size, transcendentals=0
        ),
        name="project",
    )(normed, weights, weights, weights, cosine, sine)


def turn_back_kernel(*refs, count):
    q_refs, kv_refs = refs[:count], refs[count : 2 * count]
    cos_ref, sin_ref, out_ref = refs[2 * count :]
    j = pl.program_id(1)
    scale = HEAD_SIZE ** (-0.5)
    keys = KEY_VALUE_HEADS // PAIRED
    for s in range(count):
        here = pl.program_id(0) == s

        @pl.when(jnp.logical_and(here, j < KEY_VALUE_HEADS))
        def _():
            grad = q_refs[s][0].astype(f32) * scale
            out_ref[...] = turn(grad, cos_ref[...], -sin_ref[...]).astype(bf16)

        @pl.when(jnp.logical_and(here, jnp.logical_and(j >= KEY_VALUE_HEADS, j < KEY_VALUE_HEADS + keys)))
        def _():
            grad = jnp.concatenate([kv_refs[s][i, :, :HEAD_SIZE] for i in range(PAIRED)], axis=1)
            out_ref[...] = turn(grad.astype(f32), cos_ref[...], -sin_ref[...]).astype(bf16)

        @pl.when(jnp.logical_and(here, j >= KEY_VALUE_HEADS + keys))
        def _():
            out_ref[...] = jnp.concatenate(
                [kv_refs[s][i, :, HEAD_SIZE:] for i in range(PAIRED)], axis=1
            )


def turn_back(queries, pairs, cosine, sine):
    count = len(queries)
    heads, rows, cols = queries[0].shape
    keys = heads // PAIRED
    grid = (count, heads + 2 * keys)
    whole = pl.BlockSpec(cosine.shape, lambda s, j: (0, 0))
    return pl.pallas_call(
        functools.partial(turn_back_kernel, count=count),
        grid=grid,
        in_specs=[
            pl.BlockSpec((1, rows, cols), lambda s, j: (jnp.minimum(j, heads - 1), 0, 0))
        ]
        * count
        + [
            pl.BlockSpec(
                (PAIRED, rows, cols), lambda s, j: (jnp.maximum(j - heads, 0) % keys, 0, 0)
            )
        ]
        * count
        + [whole, whole],
        out_specs=pl.BlockSpec((rows, cols), lambda s, j: (s, j)),
        out_shape=jax.ShapeDtypeStruct((count * rows, grid[1] * cols), bf16),
        compiler_params=pltpu.CompilerParams(vmem_limit_bytes=VMEM_LIMIT),
        cost_estimate=pl.CostEstimate(
            flops=4 * count * rows * grid[1] * cols,
            bytes_accessed=4 * count * rows * grid[1] * cols,
            transcendentals=0,
        ),
        name="turn_back",
    )(*queries, *pairs, cosine, sine)


def tile_positions(tile, count, start, class_index, class_rows, rows):
    index = lax.broadcasted_iota(jnp.int32, (count, 1), 0)
    place = start + jnp.bitwise_and(index, tile - 1)
    shift = class_rows.bit_length() - 1
    return (
        jnp.right_shift(place, shift) * rows
        + class_index * class_rows
        + jnp.bitwise_and(place, class_rows - 1)
    )


def stack_heads(block):
    return jnp.concatenate(
        [block[:, j * HEAD_SIZE : (j + 1) * HEAD_SIZE] for j in range(PAIRED)], axis=0
    )


def key_places(group, class_index, classes, rows):
    index = lax.broadcasted_iota(jnp.int32, (1, classes * rows), 1)
    shift = rows.bit_length() - 1
    back = jnp.bitwise_and(class_index - jnp.right_shift(index, shift), classes - 1)
    return (group * classes + back) * rows + jnp.bitwise_and(index, rows - 1)


def held_block(refs, group, cols):
    return jnp.concatenate([ref[group, :, cols] for ref in refs], axis=0)


def group_range(start, tile, class_rows, classes):
    return start // class_rows // classes, (start + tile - 1) // class_rows // classes + 1


def attn_forward_kernel(info, q_ref, *refs, tile, class_rows, rows, classes):
    kv_refs = refs[:classes]
    att_ref, exact_ref, lse_ref = refs[classes:]
    start = pl.program_id(0) * tile
    free, total = group_range(start, tile, class_rows, classes)
    queries = stack_heads(q_ref[...])
    count = queries.shape[0]
    position = tile_positions(tile, count, start, info[0], class_rows, rows)

    def step(group, carry, masked):
        acc, row_sum = carry
        keys = held_block(kv_refs, group, slice(0, HEAD_SIZE))
        values = held_block(kv_refs, group, slice(HEAD_SIZE, 2 * HEAD_SIZE))
        raw = dot(queries, keys, NT)
        weight = jnp.exp(soft_cap * jnp.tanh(raw * (1.0 / soft_cap)))
        if masked:
            weight = jnp.where(
                key_places(group, info[0], classes, rows) <= position, weight, 0.0
            )
        row_sum = row_sum + jnp.sum(weight, axis=-1, keepdims=True)
        acc = acc + dot(weight.astype(bf16), values, NN)
        return acc, row_sum

    carry = (jnp.zeros((count, HEAD_SIZE), f32), jnp.zeros((count, 1), f32))
    carry = lax.fori_loop(0, free, functools.partial(step, masked=False), carry)
    acc, row_sum = lax.fori_loop(free, total, functools.partial(step, masked=True), carry)
    exact = acc / row_sum
    lse = jnp.log(row_sum)
    for j in range(PAIRED):
        cols = slice(j * HEAD_SIZE, (j + 1) * HEAD_SIZE)
        exact_ref[:, cols] = exact[j * tile : (j + 1) * tile]
        att_ref[:, cols] = exact[j * tile : (j + 1) * tile].astype(bf16)
        lse_ref[:, j * 128 : (j + 1) * 128] = jnp.broadcast_to(
            lse[j * tile : (j + 1) * tile], (tile, 128)
        )


def attn_forward(info, queries, pairs, class_rows, rows):
    count, cols = queries.shape
    classes = len(pairs)
    length = classes * pairs[0].shape[0] * rows
    tile = min(256, count)
    grid_spec = pltpu.PrefetchScalarGridSpec(
        num_scalar_prefetch=1,
        grid=(count // tile,),
        in_specs=[pl.BlockSpec((tile, cols), lambda i, c: (i, 0))]
        + [pl.BlockSpec(p.shape, lambda i, c: (0, 0, 0)) for p in pairs],
        out_specs=[
            pl.BlockSpec((tile, cols), lambda i, c: (i, 0)),
            pl.BlockSpec((tile, cols), lambda i, c: (i, 0)),
            pl.BlockSpec((tile, PAIRED * 128), lambda i, c: (i, 0)),
        ],
    )
    return pl.pallas_call(
        functools.partial(
            attn_forward_kernel, tile=tile, class_rows=class_rows, rows=rows, classes=classes
        ),
        grid_spec=grid_spec,
        out_shape=[
            jax.ShapeDtypeStruct((count, cols), bf16),
            jax.ShapeDtypeStruct((count, cols), f32),
            jax.ShapeDtypeStruct((count, PAIRED * 128), f32),
        ],
        compiler_params=pltpu.CompilerParams(vmem_limit_bytes=VMEM_LIMIT),
        cost_estimate=pl.CostEstimate(
            flops=2 * count * PAIRED * length * 2 * HEAD_SIZE,
            bytes_accessed=8 * count * cols + 4 * length * HEAD_SIZE,
            transcendentals=2 * count * PAIRED * length,
        ),
        name="attn_forward",
    )(info, queries, *pairs)


def attn_backward_kernel(info, q_ref, grad_ref, exact_ref, lse_ref, *refs, tile, class_rows, rows, classes):
    kv_refs, dq_ref = refs[:classes], refs[classes]
    dkv_refs, sum_ref = refs[classes + 1 : 2 * classes + 1], refs[2 * classes + 1]

    @pl.when(pl.program_id(0) == 0)
    def _():
        sum_ref[...] = jnp.zeros_like(sum_ref)

    start = pl.program_id(0) * tile
    free, total = group_range(start, tile, class_rows, classes)
    queries = stack_heads(q_ref[...])
    grads = stack_heads(grad_ref[...])
    count = queries.shape[0]
    delta = jnp.sum(grads.astype(f32) * stack_heads(exact_ref[...]), axis=-1, keepdims=True)
    lse = jnp.concatenate([lse_ref[:, j * 128 : j * 128 + 1] for j in range(PAIRED)], axis=0)
    position = tile_positions(tile, count, start, info[0], class_rows, rows)

    def step(group, acc, masked):
        keys = held_block(kv_refs, group, slice(0, HEAD_SIZE))
        values = held_block(kv_refs, group, slice(HEAD_SIZE, 2 * HEAD_SIZE))
        bounded = jnp.tanh(dot(queries, keys, NT) * (1.0 / soft_cap))
        probs = jnp.exp(soft_cap * bounded - lse)
        if masked:
            probs = jnp.where(key_places(group, info[0], classes, rows) <= position, probs, 0.0)
        grad_probs = dot(grads, values, NT)
        grad_raw = (probs * (grad_probs - delta) * (1.0 - bounded * bounded)).astype(bf16)
        sum_ref[group, :, HEAD_SIZE:] += dot(probs.astype(bf16), grads, TN)
        sum_ref[group, :, :HEAD_SIZE] += dot(grad_raw, queries, TN)
        return acc + dot(grad_raw, keys, NN)

    acc = jnp.zeros((count, HEAD_SIZE), f32)
    acc = lax.fori_loop(0, free, functools.partial(step, masked=False), acc)
    acc = lax.fori_loop(free, total, functools.partial(step, masked=True), acc)
    for j in range(PAIRED):
        dq_ref[:, j * HEAD_SIZE : (j + 1) * HEAD_SIZE] = acc[j * tile : (j + 1) * tile].astype(bf16)

    @pl.when(pl.program_id(0) == pl.num_programs(0) - 1)
    def _():
        for h, ref in enumerate(dkv_refs):
            ref[...] = sum_ref[:, h * rows : (h + 1) * rows, :].astype(bf16)


def attn_backward(info, queries, pairs, grads, exact, lse, class_rows, rows):
    count, cols = queries.shape
    classes = len(pairs)
    groups = pairs[0].shape[0]
    length = classes * groups * rows
    tile = min(256, count)
    row_spec = pl.BlockSpec((tile, cols), lambda i, c: (i, 0))
    pair_specs = [pl.BlockSpec(p.shape, lambda i, c: (0, 0, 0)) for p in pairs]
    grid_spec = pltpu.PrefetchScalarGridSpec(
        num_scalar_prefetch=1,
        grid=(count // tile,),
        in_specs=[
            row_spec,
            row_spec,
            row_spec,
            pl.BlockSpec((tile, PAIRED * 128), lambda i, c: (i, 0)),
        ]
        + pair_specs,
        out_specs=[row_spec] + pair_specs,
        scratch_shapes=[pltpu.VMEM((groups, classes * rows, 2 * HEAD_SIZE), f32)],
    )
    return pl.pallas_call(
        functools.partial(
            attn_backward_kernel, tile=tile, class_rows=class_rows, rows=rows, classes=classes
        ),
        grid_spec=grid_spec,
        out_shape=[jax.ShapeDtypeStruct((count, cols), bf16)]
        + [jax.ShapeDtypeStruct(p.shape, bf16) for p in pairs],
        compiler_params=pltpu.CompilerParams(vmem_limit_bytes=VMEM_LIMIT),
        cost_estimate=pl.CostEstimate(
            flops=5 * count * PAIRED * length * 2 * HEAD_SIZE,
            bytes_accessed=10 * count * cols + 8 * length * HEAD_SIZE,
            transcendentals=2 * count * PAIRED * length,
        ),
        name="attn_backward",
    )(info, queries, grads, exact, lse, *pairs)


def per_device(
    tokens,
    cotangent,
    widths,
    attn_codes,
    attn_exps,
    out_exps,
    mlp_codes,
    gate_exps,
    down_exps,
    gain_attn,
    gain_post_attn,
    gain_mlp,
    gain_post_mlp,
):
    wide = lax.axis_size("wide")
    seq_size = lax.axis_size("seq")
    wide_index = lax.axis_index("wide")
    seq_index = lax.axis_index("seq")
    side = seq_index % 2
    is_low = side == 0
    members = seq_size // 2
    member = seq_index // 2
    half_wide = wide // 2
    place = ring_place(wide_index, wide)
    count, rows, model_dim = tokens.shape
    classes = wide // KEY_VALUE_HEADS
    class_rows = rows // classes
    class_index = wide_index % classes
    head_cols = PAIRED * HEAD_SIZE
    proj_cols = attn_exps.shape[0]
    half_proj = proj_cols // 2
    half_out = (attn_codes.shape[1] - proj_cols) // 2
    split_out = half_out // members
    attn_rows = attn_codes.shape[0]
    hidden = mlp_codes.shape[1]
    offsets = ring_offsets(wide)
    order = {o: i for i, o in enumerate(ring_offsets(half_wide))}
    seqs = range(count)
    seq_bits = [1 << i for i in range(seq_size.bit_length() - 1)]
    far_bits = list(reversed(seq_bits[1:]))
    clock = Clock(widths)

    def index_at(offset):
        return ring_index(jnp.mod(place + offset, wide), wide)

    places = jnp.stack([index_at(o) for o in offsets]).astype(jnp.int32)
    info = jnp.concatenate(
        [side[None].astype(jnp.int32), widths, member[None].astype(jnp.int32)]
    )
    class_info = class_index[None].astype(jnp.int32)
    column_scale = inverse_powers(attn_exps)[None, :]
    output_scale = inverse_powers(out_exps)[:, None]

    relative = [0]
    for bit in reversed(seq_bits):
        relative = relative + [r | bit for r in relative]
    pieces = jnp.stack([jnp.bitwise_xor(seq_index, r) for r in relative]).astype(jnp.int32)
    piece_rows = hidden // seq_size
    partner = jnp.bitwise_xor(wide_index, half_wide)
    gate_scale = inverse_powers(gate_exps)
    row_scale = jnp.concatenate(
        [
            lax.dynamic_slice_in_dim(
                gate_scale, block * hidden + pieces[j] * piece_rows, piece_rows, 1
            )
            for block in (wide_index, partner)
            for j in range(seq_size)
        ],
        axis=1,
    )[:, :, None]
    down_scale = inverse_powers(down_exps)[None, :]

    def columns(first, size):
        return lax.dynamic_slice_in_dim(attn_codes, first, size, 1)

    payload = jnp.concatenate(
        [
            columns(side * half_proj, half_proj),
            columns(proj_cols + side * half_out + member * split_out, split_out),
        ],
        axis=1,
    ).astype(bf16)
    piece_codes = lax.dynamic_slice_in_dim(mlp_codes, seq_index * piece_rows, piece_rows, 1)
    inputs = [tokens[s].astype(f32) for s in seqs]
    grad_out = [cotangent[s].astype(f32) for s in seqs]
    cosine, sine = rotary_rows(wide_index * rows + jnp.arange(rows))

    blocks, others = [clock.hold(payload)], []
    proj_weights = []

    def slice_more(first, last):
        return proj_slices(
            blocks[first:last],
            others[first:last],
            places[first:last],
            info,
            column_scale,
            half_proj,
            proj_weights,
            wide,
            count,
        )

    a = b = blocks[0]
    sliced = 0
    steps = half_wide
    for k in range(1, steps + 1):
        if k == steps:
            a, b = halves(a)[0], halves(b)[1]
        passed = [swap(v, "seq", 1) for v in blocks[len(others) :]]
        a, b = hop(a, b, wide)
        work = []
        if k == 1:
            work = own_slices(mlp_codes, pieces, info, row_scale, down_scale, count)
            a, b, *work = clock.sync(a, b, *passed, *work)
            passed, own_weights = work[: len(passed)], work[len(passed) :]
        elif k == 2:
            work = [piece_codes[m].astype(bf16) for m in range(3)]
            for s in seqs:
                factor = norm_factor(clock.hold(inputs[s]))
                work += [factor, (inputs[s] * factor * gain_attn).astype(bf16)]
            a, b, *work = clock.sync(a, b, *passed, *work)
            passed, work = work[: len(passed)], work[len(passed) :]
            sends, work = work[:3], work[3:]
            input_factor, normed = work[0::2], work[1::2]
        else:
            more = len(others)
            work = slice_more(sliced, more) if more > sliced else []
            a, b, *work = clock.sync(a, b, *passed, *work)
            passed, work = work[: len(passed)], work[len(passed) :]
            if work:
                proj_weights, sliced = list(work), more
        others += passed
        blocks += [a, b] if k < steps else [jnp.concatenate([a, b], axis=0)]

    def exchange(m):
        return swap(clock.hold(sends[m]), "wide", half_wide)

    def share(held, bits):
        for bit in bits:
            held = held + [swap(value, "seq", bit) for value in held]
        return held

    def partner_weights(m, held):
        scale = row_scale[m] if m < 2 else down_scale
        return partner_slices(
            held, info, scale, m == 2, own_weights[m * count : (m + 1) * count]
        )

    received = exchange(0)
    others += [swap(clock.hold(v), "seq", 1) for v in blocks[len(others) :]]
    proj_weights = slice_more(sliced, wide)
    query_send, pair_send = [], []
    for s in seqs:
        query, pair = project(normed[s], proj_weights[s], cosine, sine)
        query_send.append(query.reshape(wide, class_rows, head_cols))
        pair_send.append(pair)
    sent = clock.sync(received, *query_send, *pair_send)
    received, sent = sent[0], sent[1:]
    query_send, pair_send = sent[:count], sent[count:]

    def spread(pair):
        held = [pair]
        for _ in range(classes - 1):
            held.append(class_ring(held[-1]))
        return held[1:]

    def two_parts(value):
        cut = value.shape[0] // 2
        return value[:cut], value[cut:]

    attended_send, exact, lse, queries, pairs = [], [], [], [], []

    def attend(s):
        out, full, log_sum = attn_forward(class_info, queries[s], pairs[s], class_rows, rows)
        return [out.reshape(wide, class_rows, head_cols), full, log_sum]

    def keep_attend(work):
        attended_send.append(work[0])
        exact.append(work[1])
        lse.append(work[2])

    pair_first = heads_all_to_all(clock.hold(pair_send[0]))
    own_out = jnp.stack([clock.hold(v)[:, half_proj:] for v in blocks])
    other_out = jnp.stack([clock.hold(v)[:, half_proj:] for v in others])
    pair_first, own_out, other_out = clock.sync(pair_first, own_out, other_out)
    out_own = share([clock.hold(own_out)], far_bits)
    moved = spread(pair_first)
    pair_last, *work = clock.sync(heads_all_to_all(clock.hold(pair_send[1])), *moved)
    pairs.append([pair_first] + work)
    part_a, part_b = two_parts(pair_last)
    query = all_to_all(clock.hold(query_send[0]))
    query, *work = clock.sync(query, *spread(part_a), *out_own)
    moved_a, out_own = work[: classes - 1], work[classes - 1 :]
    queries.append(query.reshape(wide * class_rows, head_cols))
    moved_b = spread(clock.hold(part_b))
    query = all_to_all(clock.hold(query_send[1]))
    out_other = [swap(v, "seq", 1) for v in out_own[1:]]
    gate_held = share([clock.hold(received)], far_bits)
    query, *work = clock.sync(query, *moved_b, *out_other, *attend(0))
    moved_b, work = work[: classes - 1], work[classes - 1 :]
    out_other, work = [other_out] + work[: len(out_other)], work[len(out_other) :]
    keep_attend(work)
    queries.append(query.reshape(wide * class_rows, head_cols))
    pairs.append(
        [pair_last] + [jnp.concatenate([x, y], axis=0) for x, y in zip(moved_a, moved_b)]
    )

    attended, branch, branch_factor, middle, middle_factor, normed_mlp = [], [], [], [], [], []

    def heads_to_rows(values):
        split = values.reshape(KEY_VALUE_HEADS, rows, head_cols)
        return jnp.transpose(split, (1, 0, 2)).reshape(rows, KEY_VALUE_HEADS * head_cols)

    def join(s):
        value = dot(attended[s], out_weights[s], NT)
        factor = norm_factor(value)
        mid = inputs[s] + value * factor * gain_post_attn
        mid_factor = norm_factor(mid)
        return [value, factor, mid, mid_factor, (mid * mid_factor * gain_mlp).astype(bf16)]

    def keep_join(work):
        for held, value in zip((branch, branch_factor, middle, middle_factor, normed_mlp), work):
            held.append(value)

    for s in seqs:
        back = all_to_all(clock.hold(attended_send[s]))
        if s == 0:
            out_weights = out_slices(out_own, out_other, places, info, output_scale, count)
            back, *work = clock.sync(back, *gate_held, *out_weights, *attend(count - 1))
            gate_held, work = work[: len(gate_held)], work[len(gate_held) :]
            out_weights, work = work[:count], work[count:]
            keep_attend(work)
        else:
            gate_held = share(gate_held, seq_bits[:1])
            back, *work = clock.sync(back, *gate_held, *join(s - 1))
            gate_held, work = work[: len(gate_held)], work[len(gate_held) :]
            keep_join(work)
        attended.append(heads_to_rows(back))

    received = exchange(1)
    gate_weights = partner_weights(0, [clock.hold(v) for v in gate_held])
    received, *work = clock.sync(received, *gate_weights, *join(count - 1))
    gate_weights, work = work[:count], work[count:]
    keep_join(work)

    def blocks_of(part):
        return lambda o: part[order[o] * rows : (order[o] + 1) * rows]

    gathered, gate, up, hidden_rows, mixed, parts = [], [], [], [], [], []

    def open_part(s, part, held=()):
        group = clock.hold(gathered[s])
        return open_forward(group, gate_weights[s], up_weights[s], part, held)

    def keep_open(work):
        gate.append(work[0])
        up.append(work[1])
        hidden_rows.append(work[2])

    def mix(s):
        return dot(clock.hold(hidden_rows[s]), down_weights[s], NN).astype(bf16)

    up_held = share([clock.hold(received)], far_bits)
    received, *up_held = clock.sync(exchange(2), *up_held)

    def beside_first(step):
        nonlocal up_held
        if step == 0:
            up_held = share(up_held, seq_bits[:1])
            return tuple(up_held) + tuple(share([clock.hold(received)], far_bits))
        if step == 1:
            return tuple(partner_weights(1, [clock.hold(v) for v in up_held]))
        return ()

    a = b = clock.hold(normed_mlp[0])
    blocks = [a]
    for k in range(1, half_wide // 2 + 1):
        if k == half_wide // 2:
            a, b = halves(a)[0], halves(b)[1]
        if k == 2:
            down_held = share(down_held, seq_bits[:1])
        work = beside_first(k - 1) + (tuple(down_held) if k == 2 else ())
        a, b = hop(a, b, half_wide)
        a, b, *work = clock.sync(a, b, *work)
        if k == 1:
            up_held, down_held = work[: len(up_held)], work[len(up_held) :]
        elif k == 2:
            up_weights, down_held = work[:count], work[count:]
        blocks += [a, b]
    gathered.append(jnp.concatenate(blocks, axis=0))

    def beside_second(step):
        if step == 0:
            return open_part(0, None)
        if step == 1:
            return partner_weights(2, [clock.hold(v) for v in down_held])
        return ()

    a = b = clock.hold(normed_mlp[1])
    blocks = [a]
    for k in range(1, half_wide // 2 + 1):
        if k == half_wide // 2:
            a, b = halves(a)[0], halves(b)[1]
        work = beside_second(k - 1)
        a, b = hop(a, b, half_wide)
        a, b, *work = clock.sync(a, b, *work)
        if k == 1:
            keep_open(work)
        elif k == 2:
            down_weights = work
        blocks += [a, b]
    gathered.append(jnp.concatenate(blocks, axis=0))
    parts.append(clock.sync(mix(0))[0])

    layer_out, grad_mixed, gain_fourth = [], [], 0.0

    def finish(s):
        nonlocal gain_fourth
        factor = norm_factor(mixed[s])
        layer_out.append((middle[s] + mixed[s] * factor * gain_post_mlp).astype(bf16))
        grad, gain = norm_back(mixed[s], factor, gain_post_mlp, grad_out[s])
        grad_mixed.append(grad.astype(bf16))
        gain_fourth = gain_fourth + gain

    grad_group, grad_gate, grad_up, grad_parts, grad_normed_mlp = [], [], [], [], []

    def back_hidden(s, part, held=()):
        group = clock.hold(grad_group[s])
        return open_back(group, down_weights[s], gate[s], up[s], part, held)

    def back_input(s, part, held=()):
        grad = clock.hold(grad_gate[s])
        return input_back(grad, grad_up[s], gate_weights[s], up_weights[s], part, held)

    def keep_back(work):
        grad_gate.append(work[0])
        grad_up.append(work[1])

    def first_sum(part):
        a, b = hop(*halves(clock.hold(blocks_of(part)(half_wide // 2))), half_wide)
        return a, b

    def rest_sum(part, a, b, beside=lambda step: ()):
        part_of = blocks_of(part)
        other = []
        for k in range(half_wide // 2 - 1, 0, -1):
            if k == half_wide // 2 - 1:
                a = add_first(part_of(k), a)
                b = add_last(part_of(-k), b)
            else:
                a = low_sum(part_of(k), a)
                b = low_sum(part_of(-k), b)
            work = beside(half_wide // 2 - 1 - k)
            a, b = hop(a, b, half_wide)
            a, b, *work = clock.sync(a, b, *work)
            other.append(work)
        return part_of(0).astype(f32) + a.astype(f32) + b.astype(f32), other

    a, b = first_sum(parts[0])
    a, b, *opened = clock.sync(a, b, *open_part(1, 0))
    total, work = rest_sum(
        parts[0], a, b, lambda step: () if step else tuple(open_part(1, 1, opened))
    )
    keep_open(work[0])
    mixed.append(total)
    finish(0)
    parts.append(mix(1))
    blocks, work = ring_gather(
        clock, grad_mixed[0], half_wide, lambda k: (parts[1],) if k == 0 else ()
    )
    parts[1] = work[0][0]
    grad_group.append(jnp.concatenate(blocks, axis=0))
    a, b = first_sum(parts[1])
    a, b, *opened = clock.sync(a, b, *back_hidden(0, 0))

    def beside_last(step):
        if step:
            return ()
        keep_back(back_hidden(0, 1, opened))
        return (grad_gate[0], grad_up[0], *input_back(
            grad_gate[0], grad_up[0], gate_weights[0], up_weights[0], 0, ()
        ))

    total, work = rest_sum(parts[1], a, b, beside_last)
    grad_gate[0], grad_up[0], opened = work[0][0], work[0][1], work[0][2:]
    mixed.append(total)
    finish(1)
    blocks, work = ring_gather(
        clock, grad_mixed[1], half_wide, lambda k: () if k else tuple(back_input(0, 1, opened))
    )
    grad_parts.append(work[0][0])
    grad_group.append(jnp.concatenate(blocks, axis=0))

    def weight_sum(lefts, rights):
        lefts = [clock.hold(v) for v in lefts]
        return weight_back(lefts, rights).reshape(2, hidden, model_dim)

    def part_sum(grad, bit):
        split = grad.reshape(2, 2, grad.shape[1] // 2, model_dim)
        return low_sum(split[:, 0], swap(split[:, 1], "seq", bit))

    grad_middle, grad_branch, grad_send = [], [], []
    gain_third = gain_second = 0.0

    def back_branch(s):
        nonlocal gain_third, gain_second
        grad, gain = norm_back(middle[s], middle_factor[s], gain_mlp, grad_normed_mlp[s])
        gain_third = gain_third + gain
        grad_mid = grad_out[s] + grad
        grad, gain = norm_back(branch[s], branch_factor[s], gain_post_attn, grad_mid)
        gain_second = gain_second + gain
        grad = grad.astype(bf16)
        send = dot(grad, out_weights[s], NN).astype(bf16)
        send = jnp.transpose(send.reshape(rows, KEY_VALUE_HEADS, head_cols), (1, 0, 2))
        return [grad_mid, grad, send.reshape(wide, class_rows, head_cols)]

    def keep_branch(work):
        grad_middle.append(work[0])
        grad_branch.append(work[1])
        grad_send.append(work[2])

    a, b = first_sum(grad_parts[0])
    a, b, *opened = clock.sync(a, b, *back_hidden(1, 0))

    def beside_back(step):
        if step:
            return ()
        keep_back(back_hidden(1, 1, opened))
        return (grad_gate[1], grad_up[1], *input_back(
            grad_gate[1], grad_up[1], gate_weights[1], up_weights[1], 0, ()
        ))

    total, work = rest_sum(grad_parts[0], a, b, beside_back)
    grad_gate[1], grad_up[1], opened = work[0][0], work[0][1], work[0][2:]
    grad_normed_mlp.append(total)
    grad_parts += clock.sync(*back_input(1, 1, opened))
    a, b = first_sum(grad_parts[1])
    a, b, *work = clock.sync(a, b, *back_branch(0))
    keep_branch(work)
    total, work = rest_sum(
        grad_parts[1],
        a,
        b,
        lambda step: () if step else (weight_sum(hidden_rows, grad_group),),
    )
    down_grad = work[0][0]
    grad_normed_mlp.append(total)

    def attend_back(s):
        dq, *dkv = attn_backward(
            class_info,
            queries[s],
            pairs[s],
            clock.hold(grad_heads[s]),
            exact[s],
            lse[s],
            class_rows,
            rows,
        )
        return [dq.reshape(wide, class_rows, head_cols)] + dkv

    def class_sum(dkv):
        total = dkv[1 % classes]
        for step in range(2, classes + 1):
            total = low_sum(dkv[step % classes], class_ring(total))
        return total

    def far_parts(grad):
        split = grad.reshape(2, 2, grad.shape[1] // 2, model_dim)
        send = split[:, 1]
        return split[:, 0], [send[:, :, : model_dim // 2], send[:, :, model_dim // 2 :]]

    def far_move(part):
        return swap(clock.hold(part), "seq", seq_bits[1])

    def far_join(kept, moved):
        grad = low_sum(kept, jnp.concatenate(moved, axis=2))
        for bit in seq_bits[2:]:
            grad = part_sum(grad, bit)
        return grad

    grad_heads, grad_attend = [], []
    query_back, pair_back = [], []

    def heads_of(value):
        return value.reshape(wide * class_rows, head_cols)

    back = all_to_all(clock.hold(grad_send[0]))
    down_grad = part_sum(down_grad, 1)
    back, down_grad, *work = clock.sync(back, down_grad, *back_branch(1))
    keep_branch(work)
    grad_heads.append(heads_of(back))
    all_normed = jnp.concatenate(normed, axis=0)
    all_attended = jnp.concatenate(attended, axis=0)
    all_branch = jnp.concatenate(grad_branch, axis=0)

    def half_dot(left, right, which, size):
        return dot(left, lax.dynamic_slice_in_dim(right, which * size, size, 1), TN)

    down_keep, down_parts = far_parts(down_grad)
    down_moved = [far_move(down_parts[0])]
    back = all_to_all(clock.hold(grad_send[1]))
    out_send = half_dot(all_branch, clock.hold(all_attended), 1 - side, half_out).astype(bf16)
    back, down_moved[0], out_send, *work = clock.sync(
        back, down_moved[0], out_send, *attend_back(0)
    )
    down_moved.append(far_move(down_parts[1]))
    grad_heads.append(heads_of(back))
    grad_attend.append(work)

    dq, *dkv = grad_attend[0]
    parts_of_pair = [two_parts(v) for v in dkv]
    out_sent = swap(out_send, "seq", 1)
    query = all_to_all(clock.hold(dq))
    pair_a = class_sum([v[0] for v in parts_of_pair])
    out_part = low_sum(
        half_dot(all_branch, clock.hold(all_attended), side, half_out), out_sent
    )
    query, pair_a, down_moved[1], out_part, *work = clock.sync(
        query, pair_a, down_moved[1], out_part, *attend_back(1)
    )
    down_grad = far_join(down_keep, down_moved)
    query_back.append(query)
    grad_attend.append(work)
    dq, *dkv = grad_attend[1]
    query = all_to_all(clock.hold(dq))
    pair_b = class_sum([clock.hold(v[1]) for v in parts_of_pair])
    out_pieces = {
        t: lax.dynamic_slice_in_dim(
            clock.hold(out_part), jnp.bitwise_xor(member, t) * split_out, split_out, 1
        )
        for t in range(members)
    }
    out_moved = []
    if members == 2:
        out_parts = [out_pieces[1][:, : split_out // 2], out_pieces[1][:, split_out // 2 :]]
        out_moved.append(swap(out_parts[0], "seq", seq_bits[1]))
    else:
        for bit in seq_bits[1:]:
            for t in sorted(out_pieces):
                if not t & (bit // 2) and t | (bit // 2) in out_pieces:
                    out_pieces[t] = low_sum(
                        out_pieces[t], swap(out_pieces.pop(t | (bit // 2)), "seq", bit)
                    )
    up_grad = weight_sum(grad_up, gathered)
    query, pair_b, down_grad, up_grad, *out_moved = clock.sync(
        query, pair_b, down_grad, up_grad, *out_moved
    )
    query_back.append(query)

    pair = heads_all_to_all(clock.hold(jnp.concatenate([pair_a, pair_b], axis=0)))
    pair_sum = class_sum([clock.hold(v) for v in dkv])
    up_grad = part_sum(up_grad, 1)
    if members == 2:
        out_moved.append(swap(clock.hold(out_parts[1]), "seq", seq_bits[1]))
    pair, pair_sum, up_grad, *out_moved = clock.sync(pair, pair_sum, up_grad, *out_moved)
    out_piece = out_pieces[0]
    if out_moved:
        out_piece = low_sum(out_piece, jnp.concatenate(out_moved, axis=1))
    pair_back.append(pair)
    up_keep, up_parts = far_parts(up_grad)
    up_moved = [far_move(up_parts[0])]
    pair = heads_all_to_all(clock.hold(pair_sum))
    gate_grad = weight_sum(grad_gate, gathered)
    pair, up_moved[0], gate_grad = clock.sync(pair, up_moved[0], gate_grad)
    up_moved.append(far_move(up_parts[1]))
    pair_back.append(pair)

    def column_parts(value, count):
        width = value.shape[1] // count
        return [value[:, i * width : (i + 1) * width] for i in range(count)]

    def exchange_grad(part):
        return swap(clock.hold(part), "wide", half_wide)

    def half_sum(grad):
        split = grad.reshape(2, 2, grad.shape[1] // 2, model_dim)
        return split[:, 0], split[:, 1]

    down_own = column_parts(down_grad[0], 3)
    down_send = column_parts(down_grad[1], 3)
    gate_keep, gate_send = half_sum(gate_grad)
    gate_moved = swap(gate_send, "seq", 1)
    moved, grad_proj = clock.sync(
        exchange_grad(down_send[0]),
        turn_back(
            [v.reshape(KEY_VALUE_HEADS, rows, head_cols) for v in query_back],
            pair_back,
            cosine,
            sine,
        ),
    )
    down_other = [moved]
    moved = exchange_grad(down_send[1])
    proj_send = half_dot(all_normed, clock.hold(grad_proj), 1 - side, half_proj).astype(bf16)
    moved, gate_moved, up_moved[1], proj_send = clock.sync(
        moved, gate_moved, up_moved[1], proj_send
    )
    down_other.append(moved)
    up_grad = far_join(up_keep, up_moved)
    moved = exchange_grad(down_send[2])
    proj_sent = swap(proj_send, "seq", 1)
    gate_grad = low_sum(gate_keep, gate_moved)
    moved, proj_sent, up_grad, gate_grad = clock.sync(moved, proj_sent, up_grad, gate_grad)
    down_other.append(moved)
    gate_keep, gate_parts = far_parts(gate_grad)
    down_grad = [low_sum(x, y) for x, y in zip(down_own, down_other)]
    proj_part = low_sum(half_dot(all_normed, clock.hold(grad_proj), side, half_proj), proj_sent)
    (proj_part,) = clock.sync(proj_part)
    def part_of(o):
        first = index_at(o) * attn_rows
        return jnp.concatenate(
            [
                lax.dynamic_slice_in_dim(proj_part, first, attn_rows, 0),
                lax.dynamic_slice_in_dim(out_piece, first, attn_rows, 0),
            ],
            axis=1,
        )

    def spread_grad(grads, bits):
        for bit in bits:
            grads = [jnp.concatenate([g, swap(g, "seq", bit)], axis=0) for g in grads]
        return grads

    a, b = halves(clock.hold(part_of(wide // 2)))
    gate_moved = []
    for k in range(wide // 2 - 1, -1, -1):
        step = wide // 2 - 1 - k
        a, b = hop(a, b, wide)
        work = []
        if step in (1, 2):
            work = [far_move(gate_parts[step - 1])]
        elif step == half_wide - 1:
            work = spread_grad([clock.hold(v) for v in down_grad], far_bits)
        a, b, *work = clock.sync(a, b, *work)
        if step in (1, 2):
            gate_moved += work
        elif step == half_wide - 1:
            down_grad = work
        if step == 0:
            a, b = add_first(part_of(k), a), add_last(part_of(-k), b)
        elif k > 0:
            a, b = low_sum(part_of(k), a), low_sum(part_of(-k), b)
    total = low_sum(part_of(0), a, b)
    gate_grad = far_join(gate_keep, gate_moved)
    up_own, up_send = column_parts(up_grad[0], 2), column_parts(up_grad[1], 2)
    total, gate_grad, *up_send = clock.sync(total, gate_grad, *up_send)

    def input_grad(s):
        return dot(clock.hold(grad_proj[s * rows : (s + 1) * rows]), proj_weights[s], NT)

    def back_tokens(s, grad_normed):
        grad, gain = norm_back(inputs[s], input_factor[s], gain_attn, grad_normed)
        return (grad_middle[s] + grad).astype(bf16), gain

    def add_swapped(gains, axis, bits):
        for bit in bits:
            gains = gains + swap(gains, axis, bit)
        return gains

    proj_total = total[:, :half_proj]
    out_totals = {0: total[:, half_proj:]}
    for bit in seq_bits[1:]:
        sent = jnp.concatenate([proj_total] + [out_totals[t] for t in sorted(out_totals)], axis=1)
        moved = swap(sent, "seq", bit)
        proj_total = low_sum(proj_total, moved[:, :half_proj])
        for i, t in enumerate(sorted(out_totals)):
            first = half_proj + i * split_out
            out_totals[t | (bit // 2)] = moved[:, first : first + split_out]
    out_totals = jnp.stack([out_totals[t] for t in range(members)])
    low = jnp.concatenate(
        [proj_total]
        + [
            lax.dynamic_index_in_dim(out_totals, jnp.bitwise_xor(member, j), 0, keepdims=False)
            for j in range(members)
        ],
        axis=1,
    )
    moved, grad_first = clock.sync(exchange_grad(up_send[0]), input_grad(0))
    up_grad = [low_sum(up_own[0], moved)]
    moved, low, grad_last = clock.sync(exchange_grad(up_send[1]), low, input_grad(1))
    up_grad.append(low_sum(up_own[1], moved))
    gate_own, gate_send = column_parts(gate_grad[0], 2), column_parts(gate_grad[1], 2)
    first_tokens, gain_first = back_tokens(0, grad_first)
    last_tokens, gain = back_tokens(1, grad_last)
    gains = jnp.stack([gain_first + gain, gain_second, gain_third, gain_fourth])
    wide_bits = [1 << i for i in range(wide.bit_length() - 1)]
    gains, *gate_send = clock.sync(add_swapped(gains, "wide", wide_bits[1:]), *gate_send)
    moved = exchange_grad(gate_send[0])
    up_grad = spread_grad([clock.hold(v) for v in up_grad], far_bits)
    other = swap(clock.hold(low), "seq", 1)
    moved, other, *up_grad = clock.sync(moved, other, *up_grad)
    gate_grad = [low_sum(gate_own[0], moved)]
    moved = exchange_grad(gate_send[1])
    gate_grad = spread_grad([clock.hold(v) for v in gate_grad], far_bits)
    left, right = jnp.where(is_low, low, other), jnp.where(is_low, other, low)
    attn_grad = jnp.concatenate(
        [left[:, :half_proj], right[:, :half_proj], left[:, half_proj:], right[:, half_proj:]],
        axis=1,
    ).astype(f32)
    down_grad = spread_grad([clock.hold(v) for v in down_grad], seq_bits[:1])
    mlp_grad = unpack(down_grad, pieces, 2, [])
    moved, attn_grad, mlp_grad, *gate_grad = clock.sync(moved, attn_grad, mlp_grad, *gate_grad)
    last = spread_grad([low_sum(gate_own[1], moved)], far_bits)
    up_grad = spread_grad([clock.hold(v) for v in up_grad], seq_bits[:1])
    mlp_grad = unpack(up_grad, pieces, 1, [mlp_grad])
    gate_grad = spread_grad([clock.hold(v) for v in gate_grad], seq_bits[:1])
    gains = add_swapped(clock.hold(gains), "wide", wide_bits[:1])
    gains = add_swapped(add_swapped(gains, "seq", seq_bits[:1]), "seq", seq_bits[1:])
    mlp_grad, gains, *gate_grad = clock.sync(mlp_grad, gains, *gate_grad, *last)
    gate_grad[1:] = spread_grad(gate_grad[1:], seq_bits[:1])
    mlp_grad = unpack(gate_grad, pieces, 0, [mlp_grad])
    grad_tokens = [first_tokens, last_tokens]
    return (
        jnp.stack(layer_out),
        jnp.stack(grad_tokens),
        attn_grad,
        mlp_grad,
        gains[0],
        gains[1],
        gains[2],
        gains[3],
    )


def solution(mesh):
    placed = (
        P("seq", "wide", None),
        P("seq", "wide", None),
        P("seq"),
        P("wide", None),
        P(),
        P(),
        P(None, "wide", None),
        P(),
        P(),
        P(),
        P(),
        P(),
        P(),
    )
    return jax.shard_map(
        per_device,
        mesh=mesh,
        in_specs=placed,
        out_specs=(
            P("seq", "wide", None),
            P("seq", "wide", None),
            P("wide", None),
            P(None, "wide", None),
            P(),
            P(),
            P(),
            P(),
        ),
        check_vma=False,
    )
```

```python
import functools
import math

import jax
import jax.numpy as jnp
from jax import lax
from jax.experimental import pallas as pl
from jax.experimental.pallas import tpu as pltpu
from jax.sharding import PartitionSpec as P

QUERY_HEADS = 8
KEY_VALUE_HEADS = 4
HEAD_SIZE = 256
PAIRED = QUERY_HEADS // KEY_VALUE_HEADS

eps_norm = 1e-06
soft_cap = 50.0
rope_base = 10000.0
gelu_coeff = math.sqrt(2.0 / math.pi)
f32 = jnp.float32
bf16 = jnp.bfloat16
VMEM_LIMIT = 56 * 1024 * 1024


def dot(a, b, dims):
    return lax.dot_general(a, b, (dims, ((), ())), preferred_element_type=f32)


NN = ((1,), (0,))
NT = ((1,), (1,))
TN = ((0,), (0,))


def inverse_powers(exponents):
    return 1.0 / jnp.left_shift(jnp.ones_like(exponents), exponents).astype(f32)


def norm_factor(values):
    return lax.rsqrt(jnp.mean(values * values, axis=-1, keepdims=True) + eps_norm)


def norm_back(values, factor, gain, grad):
    scaled = grad * gain
    inner = jnp.mean(values * scaled, axis=-1, keepdims=True)
    grad_values = factor * scaled - values * (factor * factor * factor * inner)
    return grad_values, jnp.sum(grad * values * factor, axis=0)


def gelu_parts(values):
    inner = gelu_coeff * (values + 0.044715 * values * values * values)
    return jnp.tanh(inner)


def rotary_rows(positions):
    half_dim = HEAD_SIZE // 2
    frequency = jnp.exp(
        jnp.arange(half_dim, dtype=f32) * (-2.0 * math.log(rope_base) / HEAD_SIZE)
    )
    angles = positions.astype(f32)[:, None] * frequency[None, :]
    return jnp.cos(angles), jnp.sin(angles)


def ring_place(index, size):
    return jnp.where(index % 2 == 0, index // 2, size - 1 - index // 2)


def ring_index(place, size):
    return jnp.where(place < size // 2, 2 * place, 2 * (size - 1 - place) + 1)


def ring_perms(size):
    order = list(range(0, size, 2)) + list(range(size - 1, 0, -2))
    up = [
        (base + order[i], base + order[(i + 1) % size])
        for base in range(0, lax.axis_size("wide"), size)
        for i in range(size)
    ]
    return up, [(b, a) for a, b in up]


def ring_offsets(size):
    out = [0]
    for k in range(1, size // 2):
        out += [-k, k]
    return out + [size // 2]


class Clock:
    def __init__(self, token):
        self.token = token

    def sync(self, *arrays):
        *arrays, self.token = lax.optimization_barrier(tuple(arrays) + (self.token,))
        return arrays

    def hold(self, value):
        return lax.optimization_barrier((value, self.token))[0]


def hop(a, b, size):
    up, down = ring_perms(size)
    return lax.ppermute(a, "wide", up), lax.ppermute(b, "wide", down)


def low_sum(*terms):
    return sum(t.astype(f32) for t in terms).astype(bf16)


def halves(value):
    half = value.shape[0] // 2
    return value[:half], value[half:]


def add_first(whole, part):
    count = part.shape[0]
    return jnp.concatenate([low_sum(whole[:count], part), whole[count:].astype(bf16)], axis=0)


def add_last(whole, part):
    count = whole.shape[0] - part.shape[0]
    return jnp.concatenate([whole[:count].astype(bf16), low_sum(whole[count:], part)], axis=0)


def ring_gather(clock, value, size, beside=lambda step: ()):
    a = b = clock.hold(value)
    out, other = [a], []
    for k in range(1, size // 2 + 1):
        if k == size // 2:
            a, b = halves(a)[0], halves(b)[1]
        work = beside(k - 1)
        a, b = hop(a, b, size)
        a, b, *work = clock.sync(a, b, *work)
        out += [a, b]
        other.append(work)
    return out, other


def ring_scatter(clock, part_of, rows, size, beside=lambda step: ()):
    a, b = halves(clock.hold(part_of(size // 2).astype(bf16)))
    other = []
    for k in range(size // 2 - 1, -1, -1):
        work = beside(size // 2 - 1 - k)
        a, b = hop(a, b, size)
        a, b, *work = clock.sync(a, b, *work)
        other.append(work)
        if k == size // 2 - 1 and k > 0:
            a = add_first(part_of(k), a)
            b = add_last(part_of(-k), b)
        elif k > 0:
            a = low_sum(part_of(k), a)
            b = low_sum(part_of(-k), b)
    return part_of(0).astype(f32) + a.astype(f32) + b.astype(f32), other


def swap(value, axis, bit):
    size = lax.axis_size(axis)
    return lax.ppermute(value, axis, [(i, i ^ bit) for i in range(size)])


def all_to_all(value):
    return lax.all_to_all(value, "wide", split_axis=0, concat_axis=0, tiled=True)


def heads_all_to_all(value):
    size = lax.axis_size("wide")
    classes = size // KEY_VALUE_HEADS
    groups = [list(range(c, size, classes)) for c in range(classes)]
    return lax.all_to_all(
        value, "wide", split_axis=0, concat_axis=0, axis_index_groups=groups, tiled=True
    )


def class_ring(value):
    size = lax.axis_size("wide")
    classes = size // KEY_VALUE_HEADS
    perm = [(i, i // classes * classes + (i + 1) % classes) for i in range(size)]
    return lax.ppermute(value, "wide", perm)


def slice_values(codes, width):
    lift = jnp.where(width == 0, 0.0, 0.5).astype(bf16)
    large = jnp.where(width == 0, 0.0, jnp.where(width == 1, 1.5 * 2**11, 1.5 * 2**13)).astype(bf16)
    top = jnp.where(width == 0, 127.0, jnp.where(width == 1, 112.0, 64.0)).astype(bf16)
    return jnp.minimum(((codes + lift) + large) - large, top)


def proj_slice_kernel(places, info, *refs, blocks, count):
    code_refs, scale_ref, out_refs = refs[: 2 * blocks], refs[2 * blocks], refs[len(refs) - count :]
    mine = pl.program_id(1) == info[0]

    def write(code_ref):
        codes = code_ref[...]
        scale = scale_ref[...].astype(bf16)
        for s, out_ref in enumerate(out_refs):
            out_ref[...] = slice_values(codes, info[1 + s]) * scale

    for k in range(blocks):
        here = pl.program_id(0) == k
        pl.when(jnp.logical_and(here, mine))(functools.partial(write, code_refs[2 * k]))
        pl.when(jnp.logical_and(here, jnp.logical_not(mine)))(
            functools.partial(write, code_refs[2 * k + 1])
        )


def proj_slices(own, other, places, info, scale, width, weights, total, count):
    blocks = len(own)
    rows = own[0].shape[0]
    inputs = [block for pair in zip(own, other) for block in pair] + [scale]
    grid_spec = pltpu.PrefetchScalarGridSpec(
        num_scalar_prefetch=2,
        grid=(blocks, 2),
        in_specs=[pl.BlockSpec((rows, width), lambda k, j, p, i: (0, 0))] * (2 * blocks)
        + [pl.BlockSpec((1, width), lambda k, j, p, i: (0, j))]
        + [pl.BlockSpec(memory_space=pl.ANY)] * len(weights),
        out_specs=[pl.BlockSpec((rows, width), lambda k, j, p, i: (p[k], j))] * count,
    )
    return pl.pallas_call(
        functools.partial(proj_slice_kernel, blocks=blocks, count=count),
        grid_spec=grid_spec,
        out_shape=[jax.ShapeDtypeStruct((total * rows, 2 * width), bf16)] * count,
        input_output_aliases={2 + len(inputs) + s: s for s in range(len(weights))},
        compiler_params=pltpu.CompilerParams(vmem_limit_bytes=VMEM_LIMIT),
        cost_estimate=pl.CostEstimate(
            flops=20 * count * blocks * rows * width,
            bytes_accessed=4 * blocks * rows * width * (1 + count),
            transcendentals=0,
        ),
        name="proj_slices",
    )(places, info, *inputs, *weights)


def out_slice_kernel(places, info, *refs, split, count):
    inputs, scale_ref, out_refs = refs[: -1 - count], refs[-1 - count], refs[-count:]
    members = len(inputs) // 2
    member = info[1 + count]
    mine = pl.program_id(1) == info[0]

    def write(code_refs):
        scale = scale_ref[...].astype(bf16)
        for t, code_ref in enumerate(code_refs):
            first = pl.multiple_of(jnp.bitwise_xor(member, t) * split, 128)
            for s, out_ref in enumerate(out_refs):
                out_ref[:, pl.ds(first, split)] = slice_values(code_ref[0], info[1 + s]) * scale

    pl.when(mine)(lambda: write(inputs[:members]))
    pl.when(jnp.logical_not(mine))(lambda: write(inputs[members:]))


def out_slices(own, other, places, info, scale, count):
    blocks, rows, split = own[0].shape
    width = split * len(own)
    inputs = list(own) + list(other)
    grid_spec = pltpu.PrefetchScalarGridSpec(
        num_scalar_prefetch=2,
        grid=(blocks, 2),
        in_specs=[pl.BlockSpec((1, rows, split), lambda k, j, p, i: (k, 0, 0))] * len(inputs)
        + [pl.BlockSpec((rows, 1), lambda k, j, p, i: (p[k], 0))],
        out_specs=[pl.BlockSpec((rows, width), lambda k, j, p, i: (p[k], j))] * count,
    )
    return pl.pallas_call(
        functools.partial(out_slice_kernel, split=split, count=count),
        grid_spec=grid_spec,
        out_shape=[jax.ShapeDtypeStruct((blocks * rows, 2 * width), bf16)] * count,
        compiler_params=pltpu.CompilerParams(vmem_limit_bytes=VMEM_LIMIT),
        cost_estimate=pl.CostEstimate(
            flops=20 * count * blocks * rows * width,
            bytes_accessed=4 * blocks * rows * width * (1 + count),
            transcendentals=0,
        ),
        name="out_slices",
    )(places, info, *inputs, scale)


def own_slice_kernel(pieces, info, code_ref, row_ref, col_ref, *out_refs):
    count = len(out_refs) // 3
    for m in range(3):
        codes = code_ref[m].astype(f32).astype(bf16)
        scale = (row_ref[m] if m < 2 else col_ref[...]).astype(bf16)
        for s in range(count):
            out_refs[m * count + s][...] = slice_values(codes, info[1 + s]) * scale


def own_slices(codes, pieces, info, row_scale, col_scale, count):
    three, rows, cols = codes.shape
    steps = pieces.shape[0]
    piece = rows // steps
    grid_spec = pltpu.PrefetchScalarGridSpec(
        num_scalar_prefetch=2,
        grid=(steps,),
        in_specs=[
            pl.BlockSpec((three, piece, cols), lambda j, p, i: (0, p[j], 0)),
            pl.BlockSpec((2, piece, 1), lambda j, p, i: (0, j, 0)),
            pl.BlockSpec((1, cols), lambda j, p, i: (0, 0)),
        ],
        out_specs=[pl.BlockSpec((piece, cols), lambda j, p, i: (j, 0))] * (three * count),
    )
    return pl.pallas_call(
        own_slice_kernel,
        grid_spec=grid_spec,
        out_shape=[jax.ShapeDtypeStruct((2 * rows, cols), bf16)] * (three * count),
        compiler_params=pltpu.CompilerParams(vmem_limit_bytes=VMEM_LIMIT),
        cost_estimate=pl.CostEstimate(
            flops=10 * count * codes.size,
            bytes_accessed=codes.size * (4 + 2 * count),
            transcendentals=0,
        ),
        name="own_slices",
    )(pieces, info, codes, row_scale, col_scale)


def partner_slice_kernel(info, *refs, steps, count):
    piece_refs, scale_ref, out_refs = refs[:steps], refs[steps], refs[steps + 1 + count :]
    for j in range(steps):

        @pl.when(pl.program_id(0) == j)
        def _():
            codes = piece_refs[j][...]
            scale = scale_ref[...].astype(bf16)
            for s, out_ref in enumerate(out_refs):
                out_ref[...] = slice_values(codes, info[1 + s]) * scale


def partner_slices(pieces, info, scale, by_column, weights):
    steps = len(pieces)
    count = len(weights)
    piece, cols = pieces[0].shape
    if by_column:
        scale_spec = pl.BlockSpec((1, cols), lambda j, i: (0, 0))
    else:
        scale_spec = pl.BlockSpec((piece, 1), lambda j, i: (steps + j, 0))
    grid_spec = pltpu.PrefetchScalarGridSpec(
        num_scalar_prefetch=1,
        grid=(steps,),
        in_specs=[pl.BlockSpec((piece, cols), lambda j, i: (0, 0))] * steps
        + [scale_spec]
        + [pl.BlockSpec(memory_space=pl.ANY)] * count,
        out_specs=[pl.BlockSpec((piece, cols), lambda j, i: (steps + j, 0))] * count,
    )
    return pl.pallas_call(
        functools.partial(partner_slice_kernel, steps=steps, count=count),
        grid_spec=grid_spec,
        out_shape=[jax.ShapeDtypeStruct(w.shape, bf16) for w in weights],
        input_output_aliases={2 + steps + s: s for s in range(count)},
        compiler_params=pltpu.CompilerParams(vmem_limit_bytes=VMEM_LIMIT),
        cost_estimate=pl.CostEstimate(
            flops=10 * count * steps * piece * cols,
            bytes_accessed=2 * (1 + count) * steps * piece * cols,
            transcendentals=0,
        ),
        name="partner_slices",
    )(info, *pieces, scale, *weights)


def unpack_kernel(pieces, *refs, parts):
    first = 0
    for ref in refs[:parts]:
        width = ref.shape[1]
        refs[-1][0, :, first : first + width] = ref[...].astype(f32)
        first += width


def unpack(grads, pieces, matrix, held, column=None):
    steps = pieces.shape[0]
    rows = grads[0].shape[0]
    cols = sum(g.shape[1] for g in grads)
    total = held[0].shape[2] if held else cols
    first = column or 0
    piece = rows // steps
    grid_spec = pltpu.PrefetchScalarGridSpec(
        num_scalar_prefetch=1,
        grid=(steps,),
        in_specs=[pl.BlockSpec((piece, g.shape[1]), lambda j, p: (j, 0)) for g in grads]
        + [pl.BlockSpec(memory_space=pl.ANY)] * len(held),
        out_specs=pl.BlockSpec((1, piece, cols), lambda j, p: (matrix, p[j], first)),
    )
    return pl.pallas_call(
        functools.partial(unpack_kernel, parts=len(grads)),
        grid_spec=grid_spec,
        out_shape=jax.ShapeDtypeStruct((3, rows, total), f32),
        input_output_aliases={1 + len(grads): 0} if held else {},
        compiler_params=pltpu.CompilerParams(vmem_limit_bytes=VMEM_LIMIT),
        cost_estimate=pl.CostEstimate(
            flops=rows * cols, bytes_accessed=6 * rows * cols, transcendentals=0
        ),
        name="unpack",
    )(pieces, *grads, *held)


def tile_of(size):
    return 256 if size % 256 == 0 else size


def tiles_of(size, part):
    tile = tile_of(size)
    tiles = size // tile
    first_part = (tiles + 1) // 2
    if part is None or tiles == 1:
        return tile, 0, tiles
    return (tile, 0, first_part) if part == 0 else (tile, first_part, tiles - first_part)


def whole_spec(shape):
    return pl.BlockSpec(shape, lambda i: (0, 0))


def column_spec(rows, tile, first=0):
    return pl.BlockSpec((rows, tile), lambda i: (0, first + i))


def row_spec(tile, cols, first=0):
    return pl.BlockSpec((tile, cols), lambda i: (first + i, 0))


def kernel_call(kernel, grid, in_specs, out_specs, out_shape, flops, moved, name, held=()):
    inputs = len(in_specs)
    return pl.pallas_call(
        lambda *refs: kernel(*refs[:inputs], *refs[inputs + len(held) :]),
        grid=(grid,),
        in_specs=in_specs + [pl.BlockSpec(memory_space=pl.ANY)] * len(held),
        out_specs=out_specs,
        out_shape=out_shape,
        input_output_aliases={inputs + i: i for i in range(len(held))},
        compiler_params=pltpu.CompilerParams(vmem_limit_bytes=VMEM_LIMIT),
        cost_estimate=pl.CostEstimate(flops=flops, bytes_accessed=moved, transcendentals=0),
        name=name,
    )


def row_parts(rows):
    part = 512 if rows % 512 == 0 else rows
    return [slice(first, first + part) for first in range(0, rows, part)]


def open_kernel(x_ref, wg_ref, wu_ref, gate_ref, up_ref, hidden_ref):
    for part in row_parts(x_ref.shape[0]):
        x = x_ref[part]
        gate = dot(x, wg_ref[...], NT)
        up = dot(x, wu_ref[...], NT)
        gate_ref[part] = gate
        up_ref[part] = up
        hidden_ref[part] = (gate * (0.5 + 0.5 * gelu_parts(gate)) * up).astype(bf16)


def open_forward(x, gate_weights, up_weights, part, held=()):
    rows, depth = x.shape
    hidden = gate_weights.shape[0]
    tile, first, tiles = tiles_of(hidden, part)
    if held and tiles * tile == hidden:
        return list(held)
    return kernel_call(
        open_kernel,
        tiles,
        [whole_spec(x.shape)] + [row_spec(tile, depth, first)] * 2,
        [column_spec(rows, tile, first)] * 3,
        [jax.ShapeDtypeStruct((rows, hidden), t) for t in (f32, f32, bf16)],
        4 * rows * depth * tile * tiles,
        2 * rows * depth + tiles * tile * (4 * depth + 10 * rows),
        "open_forward",
        held,
    )(x, gate_weights, up_weights, *held)


def open_back_kernel(x_ref, wd_ref, gate_ref, up_ref, grad_gate_ref, grad_up_ref):
    for part in row_parts(x_ref.shape[0]):
        grad = dot(x_ref[part], wd_ref[...], NT)
        gate = gate_ref[part]
        square = gate * gate
        bounded = jnp.tanh(gate * (gelu_coeff + (0.044715 * gelu_coeff) * square))
        half = 0.5 + 0.5 * bounded
        steep = (0.5 * gelu_coeff) + (1.5 * 0.044715 * gelu_coeff) * square
        slope = half + gate * (1.0 - bounded * bounded) * steep
        grad_gate_ref[part] = (grad * up_ref[part] * slope).astype(bf16)
        grad_up_ref[part] = (grad * (gate * half)).astype(bf16)


def open_back(x, down_weights, gate, up, part, held=()):
    rows, depth = x.shape
    hidden = down_weights.shape[0]
    tile, first, tiles = tiles_of(hidden, part)
    if held and tiles * tile == hidden:
        return list(held)
    return kernel_call(
        open_back_kernel,
        tiles,
        [whole_spec(x.shape), row_spec(tile, depth, first)] + [column_spec(rows, tile, first)] * 2,
        [column_spec(rows, tile, first)] * 2,
        [jax.ShapeDtypeStruct((rows, hidden), bf16)] * 2,
        2 * rows * depth * tile * tiles,
        2 * rows * depth + tiles * tile * (2 * depth + 12 * rows),
        "open_back",
        held,
    )(x, down_weights, gate, up, *held)


def input_back_kernel(gate_ref, up_ref, wg_ref, wu_ref, out_ref):
    out_ref[...] = (
        dot(gate_ref[...], wg_ref[...], NN) + dot(up_ref[...], wu_ref[...], NN)
    ).astype(bf16)


def input_back(grad_gate, grad_up, gate_weights, up_weights, part, held=()):
    rows, hidden = grad_gate.shape
    depth = gate_weights.shape[1]
    tile, first, tiles = tiles_of(depth, part)
    if held and tiles * tile == depth:
        return list(held)
    return kernel_call(
        input_back_kernel,
        tiles,
        [whole_spec(grad_gate.shape)] * 2 + [column_spec(hidden, tile, first)] * 2,
        [column_spec(rows, tile, first)],
        [jax.ShapeDtypeStruct((rows, depth), bf16)],
        4 * rows * hidden * tile * tiles,
        4 * rows * hidden + tiles * tile * (4 * hidden + 2 * rows),
        "input_back",
        held,
    )(grad_gate, grad_up, gate_weights, up_weights, *held)


def weight_kernel(*refs, count):
    out_ref = refs[-1]
    total = dot(refs[0][...], refs[count][...], TN)
    for s in range(1, count):
        total = total + dot(refs[s][...], refs[count + s][...], TN)
    out_ref[...] = total.astype(bf16)


def weight_back(lefts, rights):
    count = len(lefts)
    rows, hidden = lefts[0].shape
    depth = rights[0].shape[1]
    tile = tile_of(hidden)
    return kernel_call(
        functools.partial(weight_kernel, count=count),
        hidden // tile,
        [column_spec(rows, tile)] * count + [whole_spec((rows, depth))] * count,
        row_spec(tile, depth),
        jax.ShapeDtypeStruct((hidden, depth), bf16),
        2 * count * rows * depth * hidden,
        2 * count * rows * (hidden + depth) + 2 * hidden * depth,
        "weight_back",
    )(*lefts, *rights)


def turn(values, cosine, sine):
    half = HEAD_SIZE // 2
    out = []
    for j in range(values.shape[1] // HEAD_SIZE):
        a = values[:, j * HEAD_SIZE : j * HEAD_SIZE + half]
        b = values[:, j * HEAD_SIZE + half : (j + 1) * HEAD_SIZE]
        out += [a * cosine - b * sine, b * cosine + a * sine]
    return jnp.concatenate(out, axis=1)


def project_kernel(x_ref, wq_ref, wk_ref, wv_ref, cos_ref, sin_ref, q_ref, kv_ref):
    x = x_ref[...]
    cosine, sine = cos_ref[...], sin_ref[...]
    scale = HEAD_SIZE ** (-0.5)
    q_ref[0] = (turn(dot(x, wq_ref[...], NN), cosine, sine) * scale).astype(bf16)
    kv_ref[0, :, :HEAD_SIZE] = turn(dot(x, wk_ref[...], NN), cosine, sine).astype(bf16)
    kv_ref[0, :, HEAD_SIZE:] = dot(x, wv_ref[...], NN).astype(bf16)


def project(normed, weights, cosine, sine):
    rows, depth = normed.shape
    cols = PAIRED * HEAD_SIZE
    first_key = QUERY_HEADS
    first_value = QUERY_HEADS + KEY_VALUE_HEADS
    whole = lambda shape: pl.BlockSpec(shape, lambda h: (0, 0))
    return pl.pallas_call(
        project_kernel,
        grid=(KEY_VALUE_HEADS,),
        in_specs=[
            whole((rows, depth)),
            pl.BlockSpec((depth, cols), lambda h: (0, h)),
            pl.BlockSpec((depth, HEAD_SIZE), lambda h: (0, first_key + h)),
            pl.BlockSpec((depth, HEAD_SIZE), lambda h: (0, first_value + h)),
            whole(cosine.shape),
            whole(sine.shape),
        ],
        out_specs=[
            pl.BlockSpec((1, rows, cols), lambda h: (h, 0, 0)),
            pl.BlockSpec((1, rows, 2 * HEAD_SIZE), lambda h: (h, 0, 0)),
        ],
        out_shape=[
            jax.ShapeDtypeStruct((KEY_VALUE_HEADS, rows, cols), bf16),
            jax.ShapeDtypeStruct((KEY_VALUE_HEADS, rows, 2 * HEAD_SIZE), bf16),
        ],
        compiler_params=pltpu.CompilerParams(vmem_limit_bytes=VMEM_LIMIT),
        cost_estimate=pl.CostEstimate(
            flops=2 * rows * weights.size, bytes_accessed=2 * weights.size, transcendentals=0
        ),
        name="project",
    )(normed, weights, weights, weights, cosine, sine)


def turn_back_kernel(*refs, count):
    q_refs, kv_refs = refs[:count], refs[count : 2 * count]
    cos_ref, sin_ref, out_ref = refs[2 * count :]
    j = pl.program_id(1)
    scale = HEAD_SIZE ** (-0.5)
    keys = KEY_VALUE_HEADS // PAIRED
    for s in range(count):
        here = pl.program_id(0) == s

        @pl.when(jnp.logical_and(here, j < KEY_VALUE_HEADS))
        def _():
            grad = q_refs[s][0].astype(f32) * scale
            out_ref[...] = turn(grad, cos_ref[...], -sin_ref[...]).astype(bf16)

        @pl.when(jnp.logical_and(here, jnp.logical_and(j >= KEY_VALUE_HEADS, j < KEY_VALUE_HEADS + keys)))
        def _():
            grad = jnp.concatenate([kv_refs[s][i, :, :HEAD_SIZE] for i in range(PAIRED)], axis=1)
            out_ref[...] = turn(grad.astype(f32), cos_ref[...], -sin_ref[...]).astype(bf16)

        @pl.when(jnp.logical_and(here, j >= KEY_VALUE_HEADS + keys))
        def _():
            out_ref[...] = jnp.concatenate(
                [kv_refs[s][i, :, HEAD_SIZE:] for i in range(PAIRED)], axis=1
            )


def turn_back(queries, pairs, cosine, sine):
    count = len(queries)
    heads, rows, cols = queries[0].shape
    keys = heads // PAIRED
    grid = (count, heads + 2 * keys)
    whole = pl.BlockSpec(cosine.shape, lambda s, j: (0, 0))
    return pl.pallas_call(
        functools.partial(turn_back_kernel, count=count),
        grid=grid,
        in_specs=[
            pl.BlockSpec((1, rows, cols), lambda s, j: (jnp.minimum(j, heads - 1), 0, 0))
        ]
        * count
        + [
            pl.BlockSpec(
                (PAIRED, rows, cols), lambda s, j: (jnp.maximum(j - heads, 0) % keys, 0, 0)
            )
        ]
        * count
        + [whole, whole],
        out_specs=pl.BlockSpec((rows, cols), lambda s, j: (s, j)),
        out_shape=jax.ShapeDtypeStruct((count * rows, grid[1] * cols), bf16),
        compiler_params=pltpu.CompilerParams(vmem_limit_bytes=VMEM_LIMIT),
        cost_estimate=pl.CostEstimate(
            flops=4 * count * rows * grid[1] * cols,
            bytes_accessed=4 * count * rows * grid[1] * cols,
            transcendentals=0,
        ),
        name="turn_back",
    )(*queries, *pairs, cosine, sine)


def tile_positions(tile, count, start, class_index, class_rows, rows):
    index = lax.broadcasted_iota(jnp.int32, (count, 1), 0)
    place = start + jnp.bitwise_and(index, tile - 1)
    shift = class_rows.bit_length() - 1
    return (
        jnp.right_shift(place, shift) * rows
        + class_index * class_rows
        + jnp.bitwise_and(place, class_rows - 1)
    )


def stack_heads(block):
    return jnp.concatenate(
        [block[:, j * HEAD_SIZE : (j + 1) * HEAD_SIZE] for j in range(PAIRED)], axis=0
    )


def key_places(group, class_index, classes, rows):
    index = lax.broadcasted_iota(jnp.int32, (1, classes * rows), 1)
    shift = rows.bit_length() - 1
    back = jnp.bitwise_and(class_index - jnp.right_shift(index, shift), classes - 1)
    return (group * classes + back) * rows + jnp.bitwise_and(index, rows - 1)


def held_block(refs, group, cols):
    return jnp.concatenate([ref[group, :, cols] for ref in refs], axis=0)


def group_range(start, tile, class_rows, classes):
    return start // class_rows // classes, (start + tile - 1) // class_rows // classes + 1


def attn_forward_kernel(info, q_ref, *refs, tile, class_rows, rows, classes):
    kv_refs = refs[:classes]
    att_ref, exact_ref, lse_ref = refs[classes:]
    start = pl.program_id(0) * tile
    free, total = group_range(start, tile, class_rows, classes)
    queries = stack_heads(q_ref[...])
    count = queries.shape[0]
    position = tile_positions(tile, count, start, info[0], class_rows, rows)

    def step(group, carry, masked):
        acc, row_sum = carry
        keys = held_block(kv_refs, group, slice(0, HEAD_SIZE))
        values = held_block(kv_refs, group, slice(HEAD_SIZE, 2 * HEAD_SIZE))
        raw = dot(queries, keys, NT)
        weight = jnp.exp(soft_cap * jnp.tanh(raw * (1.0 / soft_cap)))
        if masked:
            weight = jnp.where(
                key_places(group, info[0], classes, rows) <= position, weight, 0.0
            )
        row_sum = row_sum + jnp.sum(weight, axis=-1, keepdims=True)
        acc = acc + dot(weight.astype(bf16), values, NN)
        return acc, row_sum

    carry = (jnp.zeros((count, HEAD_SIZE), f32), jnp.zeros((count, 1), f32))
    carry = lax.fori_loop(0, free, functools.partial(step, masked=False), carry)
    acc, row_sum = lax.fori_loop(free, total, functools.partial(step, masked=True), carry)
    exact = acc / row_sum
    lse = jnp.log(row_sum)
    for j in range(PAIRED):
        cols = slice(j * HEAD_SIZE, (j + 1) * HEAD_SIZE)
        exact_ref[:, cols] = exact[j * tile : (j + 1) * tile]
        att_ref[:, cols] = exact[j * tile : (j + 1) * tile].astype(bf16)
        lse_ref[:, j * 128 : (j + 1) * 128] = jnp.broadcast_to(
            lse[j * tile : (j + 1) * tile], (tile, 128)
        )


def attn_forward(info, queries, pairs, class_rows, rows):
    count, cols = queries.shape
    classes = len(pairs)
    length = classes * pairs[0].shape[0] * rows
    tile = min(256, count)
    grid_spec = pltpu.PrefetchScalarGridSpec(
        num_scalar_prefetch=1,
        grid=(count // tile,),
        in_specs=[pl.BlockSpec((tile, cols), lambda i, c: (i, 0))]
        + [pl.BlockSpec(p.shape, lambda i, c: (0, 0, 0)) for p in pairs],
        out_specs=[
            pl.BlockSpec((tile, cols), lambda i, c: (i, 0)),
            pl.BlockSpec((tile, cols), lambda i, c: (i, 0)),
            pl.BlockSpec((tile, PAIRED * 128), lambda i, c: (i, 0)),
        ],
    )
    return pl.pallas_call(
        functools.partial(
            attn_forward_kernel, tile=tile, class_rows=class_rows, rows=rows, classes=classes
        ),
        grid_spec=grid_spec,
        out_shape=[
            jax.ShapeDtypeStruct((count, cols), bf16),
            jax.ShapeDtypeStruct((count, cols), f32),
            jax.ShapeDtypeStruct((count, PAIRED * 128), f32),
        ],
        compiler_params=pltpu.CompilerParams(vmem_limit_bytes=VMEM_LIMIT),
        cost_estimate=pl.CostEstimate(
            flops=2 * count * PAIRED * length * 2 * HEAD_SIZE,
            bytes_accessed=8 * count * cols + 4 * length * HEAD_SIZE,
            transcendentals=2 * count * PAIRED * length,
        ),
        name="attn_forward",
    )(info, queries, *pairs)


def attn_backward_kernel(info, q_ref, grad_ref, exact_ref, lse_ref, *refs, tile, class_rows, rows, classes):
    kv_refs, dq_ref = refs[:classes], refs[classes]
    dkv_refs, sum_ref = refs[classes + 1 : 2 * classes + 1], refs[2 * classes + 1]

    @pl.when(pl.program_id(0) == 0)
    def _():
        sum_ref[...] = jnp.zeros_like(sum_ref)

    start = pl.program_id(0) * tile
    free, total = group_range(start, tile, class_rows, classes)
    queries = stack_heads(q_ref[...])
    grads = stack_heads(grad_ref[...])
    count = queries.shape[0]
    delta = jnp.sum(grads.astype(f32) * stack_heads(exact_ref[...]), axis=-1, keepdims=True)
    lse = jnp.concatenate([lse_ref[:, j * 128 : j * 128 + 1] for j in range(PAIRED)], axis=0)
    position = tile_positions(tile, count, start, info[0], class_rows, rows)

    def step(group, acc, masked):
        keys = held_block(kv_refs, group, slice(0, HEAD_SIZE))
        values = held_block(kv_refs, group, slice(HEAD_SIZE, 2 * HEAD_SIZE))
        bounded = jnp.tanh(dot(queries, keys, NT) * (1.0 / soft_cap))
        probs = jnp.exp(soft_cap * bounded - lse)
        if masked:
            probs = jnp.where(key_places(group, info[0], classes, rows) <= position, probs, 0.0)
        grad_probs = dot(grads, values, NT)
        grad_raw = (probs * (grad_probs - delta) * (1.0 - bounded * bounded)).astype(bf16)
        sum_ref[group, :, HEAD_SIZE:] += dot(probs.astype(bf16), grads, TN)
        sum_ref[group, :, :HEAD_SIZE] += dot(grad_raw, queries, TN)
        return acc + dot(grad_raw, keys, NN)

    acc = jnp.zeros((count, HEAD_SIZE), f32)
    acc = lax.fori_loop(0, free, functools.partial(step, masked=False), acc)
    acc = lax.fori_loop(free, total, functools.partial(step, masked=True), acc)
    for j in range(PAIRED):
        dq_ref[:, j * HEAD_SIZE : (j + 1) * HEAD_SIZE] = acc[j * tile : (j + 1) * tile].astype(bf16)

    @pl.when(pl.program_id(0) == pl.num_programs(0) - 1)
    def _():
        for h, ref in enumerate(dkv_refs):
            ref[...] = sum_ref[:, h * rows : (h + 1) * rows, :].astype(bf16)


def attn_backward(info, queries, pairs, grads, exact, lse, class_rows, rows):
    count, cols = queries.shape
    classes = len(pairs)
    groups = pairs[0].shape[0]
    length = classes * groups * rows
    tile = min(256, count)
    row_spec = pl.BlockSpec((tile, cols), lambda i, c: (i, 0))
    pair_specs = [pl.BlockSpec(p.shape, lambda i, c: (0, 0, 0)) for p in pairs]
    grid_spec = pltpu.PrefetchScalarGridSpec(
        num_scalar_prefetch=1,
        grid=(count // tile,),
        in_specs=[
            row_spec,
            row_spec,
            row_spec,
            pl.BlockSpec((tile, PAIRED * 128), lambda i, c: (i, 0)),
        ]
        + pair_specs,
        out_specs=[row_spec] + pair_specs,
        scratch_shapes=[pltpu.VMEM((groups, classes * rows, 2 * HEAD_SIZE), f32)],
    )
    return pl.pallas_call(
        functools.partial(
            attn_backward_kernel, tile=tile, class_rows=class_rows, rows=rows, classes=classes
        ),
        grid_spec=grid_spec,
        out_shape=[jax.ShapeDtypeStruct((count, cols), bf16)]
        + [jax.ShapeDtypeStruct(p.shape, bf16) for p in pairs],
        compiler_params=pltpu.CompilerParams(vmem_limit_bytes=VMEM_LIMIT),
        cost_estimate=pl.CostEstimate(
            flops=5 * count * PAIRED * length * 2 * HEAD_SIZE,
            bytes_accessed=10 * count * cols + 8 * length * HEAD_SIZE,
            transcendentals=2 * count * PAIRED * length,
        ),
        name="attn_backward",
    )(info, queries, grads, exact, lse, *pairs)


def per_device(
    tokens,
    cotangent,
    widths,
    attn_codes,
    attn_exps,
    out_exps,
    mlp_codes,
    gate_exps,
    down_exps,
    gain_attn,
    gain_post_attn,
    gain_mlp,
    gain_post_mlp,
):
    wide = lax.axis_size("wide")
    seq_size = lax.axis_size("seq")
    wide_index = lax.axis_index("wide")
    seq_index = lax.axis_index("seq")
    side = seq_index % 2
    is_low = side == 0
    members = seq_size // 2
    member = seq_index // 2
    half_wide = wide // 2
    place = ring_place(wide_index, wide)
    count, rows, model_dim = tokens.shape
    classes = wide // KEY_VALUE_HEADS
    class_rows = rows // classes
    class_index = wide_index % classes
    head_cols = PAIRED * HEAD_SIZE
    proj_cols = attn_exps.shape[0]
    half_proj = proj_cols // 2
    half_out = (attn_codes.shape[1] - proj_cols) // 2
    split_out = half_out // members
    attn_rows = attn_codes.shape[0]
    hidden = mlp_codes.shape[1]
    offsets = ring_offsets(wide)
    order = {o: i for i, o in enumerate(ring_offsets(half_wide))}
    seqs = range(count)
    seq_bits = [1 << i for i in range(seq_size.bit_length() - 1)]
    far_bits = list(reversed(seq_bits[1:]))
    clock = Clock(widths)

    def index_at(offset):
        return ring_index(jnp.mod(place + offset, wide), wide)

    places = jnp.stack([index_at(o) for o in offsets]).astype(jnp.int32)
    info = jnp.concatenate(
        [side[None].astype(jnp.int32), widths, member[None].astype(jnp.int32)]
    )
    class_info = class_index[None].astype(jnp.int32)
    column_scale = inverse_powers(attn_exps)[None, :]
    output_scale = inverse_powers(out_exps)[:, None]

    relative = [0]
    for bit in reversed(seq_bits):
        relative = relative + [r | bit for r in relative]
    pieces = jnp.stack([jnp.bitwise_xor(seq_index, r) for r in relative]).astype(jnp.int32)
    piece_rows = hidden // seq_size
    partner = jnp.bitwise_xor(wide_index, half_wide)
    gate_scale = inverse_powers(gate_exps)
    row_scale = jnp.concatenate(
        [
            lax.dynamic_slice_in_dim(
                gate_scale, block * hidden + pieces[j] * piece_rows, piece_rows, 1
            )
            for block in (wide_index, partner)
            for j in range(seq_size)
        ],
        axis=1,
    )[:, :, None]
    down_scale = inverse_powers(down_exps)[None, :]

    def columns(first, size):
        return lax.dynamic_slice_in_dim(attn_codes, first, size, 1)

    payload = jnp.concatenate(
        [
            columns(side * half_proj, half_proj),
            columns(proj_cols + side * half_out + member * split_out, split_out),
        ],
        axis=1,
    ).astype(bf16)
    piece_codes = lax.dynamic_slice_in_dim(mlp_codes, seq_index * piece_rows, piece_rows, 1)
    inputs = [tokens[s].astype(f32) for s in seqs]
    grad_out = [cotangent[s].astype(f32) for s in seqs]
    cosine, sine = rotary_rows(wide_index * rows + jnp.arange(rows))

    blocks, others = [clock.hold(payload)], []
    proj_weights = []

    def slice_more(first, last):
        return proj_slices(
            blocks[first:last],
            others[first:last],
            places[first:last],
            info,
            column_scale,
            half_proj,
            proj_weights,
            wide,
            count,
        )

    a = b = blocks[0]
    sliced = 0
    steps = half_wide
    for k in range(1, steps + 1):
        if k == steps:
            a, b = halves(a)[0], halves(b)[1]
        passed = [swap(v, "seq", 1) for v in blocks[len(others) :]]
        a, b = hop(a, b, wide)
        work = []
        if k == 1:
            work = own_slices(mlp_codes, pieces, info, row_scale, down_scale, count)
            a, b, *work = clock.sync(a, b, *passed, *work)
            passed, own_weights = work[: len(passed)], work[len(passed) :]
        elif k == 2:
            work = [piece_codes[m].astype(bf16) for m in range(3)]
            for s in seqs:
                factor = norm_factor(clock.hold(inputs[s]))
                work += [factor, (inputs[s] * factor * gain_attn).astype(bf16)]
            a, b, *work = clock.sync(a, b, *passed, *work)
            passed, work = work[: len(passed)], work[len(passed) :]
            sends, work = work[:3], work[3:]
            input_factor, normed = work[0::2], work[1::2]
        else:
            more = len(others)
            work = slice_more(sliced, more) if more > sliced else []
            a, b, *work = clock.sync(a, b, *passed, *work)
            passed, work = work[: len(passed)], work[len(passed) :]
            if work:
                proj_weights, sliced = list(work), more
        others += passed
        blocks += [a, b] if k < steps else [jnp.concatenate([a, b], axis=0)]

    def exchange(m):
        return swap(clock.hold(sends[m]), "wide", half_wide)

    def share(held, bits):
        for bit in bits:
            held = held + [swap(value, "seq", bit) for value in held]
        return held

    def partner_weights(m, held):
        scale = row_scale[m] if m < 2 else down_scale
        return partner_slices(
            held, info, scale, m == 2, own_weights[m * count : (m + 1) * count]
        )

    received = exchange(0)
    others += [swap(clock.hold(v), "seq", 1) for v in blocks[len(others) :]]
    proj_weights = slice_more(sliced, wide)
    query_send, pair_send = [], []
    for s in seqs:
        query, pair = project(normed[s], proj_weights[s], cosine, sine)
        query_send.append(query.reshape(wide, class_rows, head_cols))
        pair_send.append(pair)
    sent = clock.sync(received, *query_send, *pair_send)
    received, sent = sent[0], sent[1:]
    query_send, pair_send = sent[:count], sent[count:]

    def spread(pair):
        held = [pair]
        for _ in range(classes - 1):
            held.append(class_ring(held[-1]))
        return held[1:]

    def two_parts(value):
        cut = value.shape[0] // 2
        return value[:cut], value[cut:]

    attended_send, exact, lse, queries, pairs = [], [], [], [], []

    def attend(s):
        out, full, log_sum = attn_forward(class_info, queries[s], pairs[s], class_rows, rows)
        return [out.reshape(wide, class_rows, head_cols), full, log_sum]

    def keep_attend(work):
        attended_send.append(work[0])
        exact.append(work[1])
        lse.append(work[2])

    pair_first = heads_all_to_all(clock.hold(pair_send[0]))
    own_out = jnp.stack([clock.hold(v)[:, half_proj:] for v in blocks])
    other_out = jnp.stack([clock.hold(v)[:, half_proj:] for v in others])
    pair_first, own_out, other_out = clock.sync(pair_first, own_out, other_out)
    out_own = share([clock.hold(own_out)], far_bits)
    moved = spread(pair_first)
    pair_last, *work = clock.sync(heads_all_to_all(clock.hold(pair_send[1])), *moved)
    pairs.append([pair_first] + work)
    part_a, part_b = two_parts(pair_last)
    query = all_to_all(clock.hold(query_send[0]))
    query, *work = clock.sync(query, *spread(part_a), *out_own)
    moved_a, out_own = work[: classes - 1], work[classes - 1 :]
    queries.append(query.reshape(wide * class_rows, head_cols))
    moved_b = spread(clock.hold(part_b))
    query = all_to_all(clock.hold(query_send[1]))
    out_other = [swap(v, "seq", 1) for v in out_own[1:]]
    gate_held = share([clock.hold(received)], far_bits)
    query, *work = clock.sync(query, *moved_b, *out_other, *attend(0))
    moved_b, work = work[: classes - 1], work[classes - 1 :]
    out_other, work = [other_out] + work[: len(out_other)], work[len(out_other) :]
    keep_attend(work)
    queries.append(query.reshape(wide * class_rows, head_cols))
    pairs.append(
        [pair_last] + [jnp.concatenate([x, y], axis=0) for x, y in zip(moved_a, moved_b)]
    )

    attended, branch, branch_factor, middle, middle_factor, normed_mlp = [], [], [], [], [], []

    def heads_to_rows(values):
        split = values.reshape(KEY_VALUE_HEADS, rows, head_cols)
        return jnp.transpose(split, (1, 0, 2)).reshape(rows, KEY_VALUE_HEADS * head_cols)

    def join(s):
        value = dot(attended[s], out_weights[s], NT)
        factor = norm_factor(value)
        mid = inputs[s] + value * factor * gain_post_attn
        mid_factor = norm_factor(mid)
        return [value, factor, mid, mid_factor, (mid * mid_factor * gain_mlp).astype(bf16)]

    def keep_join(work):
        for held, value in zip((branch, branch_factor, middle, middle_factor, normed_mlp), work):
            held.append(value)

    for s in seqs:
        back = all_to_all(clock.hold(attended_send[s]))
        if s == 0:
            out_weights = out_slices(out_own, out_other, places, info, output_scale, count)
            back, *work = clock.sync(back, *gate_held, *out_weights, *attend(count - 1))
            gate_held, work = work[: len(gate_held)], work[len(gate_held) :]
            out_weights, work = work[:count], work[count:]
            keep_attend(work)
        else:
            gate_held = share(gate_held, seq_bits[:1])
            back, *work = clock.sync(back, *gate_held, *join(s - 1))
            gate_held, work = work[: len(gate_held)], work[len(gate_held) :]
            keep_join(work)
        attended.append(heads_to_rows(back))

    received = exchange(1)
    gate_weights = partner_weights(0, [clock.hold(v) for v in gate_held])
    received, *work = clock.sync(received, *gate_weights, *join(count - 1))
    gate_weights, work = work[:count], work[count:]
    keep_join(work)

    def blocks_of(part):
        return lambda o: part[order[o] * rows : (order[o] + 1) * rows]

    gathered, gate, up, hidden_rows, mixed, parts = [], [], [], [], [], []

    def open_part(s, part, held=()):
        group = clock.hold(gathered[s])
        return open_forward(group, gate_weights[s], up_weights[s], part, held)

    def keep_open(work):
        gate.append(work[0])
        up.append(work[1])
        hidden_rows.append(work[2])

    def mix(s):
        return dot(clock.hold(hidden_rows[s]), down_weights[s], NN).astype(bf16)

    up_held = share([clock.hold(received)], far_bits)
    received, *up_held = clock.sync(exchange(2), *up_held)

    def beside_first(step):
        nonlocal up_held
        if step == 0:
            up_held = share(up_held, seq_bits[:1])
            return tuple(up_held) + tuple(share([clock.hold(received)], far_bits))
        if step == 1:
            return tuple(partner_weights(1, [clock.hold(v) for v in up_held]))
        return ()

    a = b = clock.hold(normed_mlp[0])
    blocks = [a]
    for k in range(1, half_wide // 2 + 1):
        if k == half_wide // 2:
            a, b = halves(a)[0], halves(b)[1]
        if k == 2:
            down_held = share(down_held, seq_bits[:1])
        work = beside_first(k - 1) + (tuple(down_held) if k == 2 else ())
        a, b = hop(a, b, half_wide)
        a, b, *work = clock.sync(a, b, *work)
        if k == 1:
            up_held, down_held = work[: len(up_held)], work[len(up_held) :]
        elif k == 2:
            up_weights, down_held = work[:count], work[count:]
        blocks += [a, b]
    gathered.append(jnp.concatenate(blocks, axis=0))

    def beside_second(step):
        if step == 0:
            return open_part(0, None)
        if step == 1:
            weights = partner_weights(2, [clock.hold(v) for v in down_held])
            return [dot(clock.hold(hidden_rows[0]), weights[0], NN).astype(bf16)] + list(weights)
        return ()

    a = b = clock.hold(normed_mlp[1])
    blocks = [a]
    for k in range(1, half_wide // 2 + 1):
        if k == half_wide // 2:
            a, b = halves(a)[0], halves(b)[1]
        work = beside_second(k - 1)
        a, b = hop(a, b, half_wide)
        a, b, *work = clock.sync(a, b, *work)
        if k == 1:
            keep_open(work)
        elif k == 2:
            parts.append(work[0])
            down_weights = work[1:]
        blocks += [a, b]
    gathered.append(jnp.concatenate(blocks, axis=0))

    layer_out, grad_mixed, gain_fourth = [], [], 0.0

    def finish(s):
        nonlocal gain_fourth
        factor = norm_factor(mixed[s])
        layer_out.append((middle[s] + mixed[s] * factor * gain_post_mlp).astype(bf16))
        grad, gain = norm_back(mixed[s], factor, gain_post_mlp, grad_out[s])
        grad_mixed.append(grad.astype(bf16))
        gain_fourth = gain_fourth + gain

    grad_group, grad_gate, grad_up, grad_parts, grad_normed_mlp = [], [], [], [], []

    def back_hidden(s, part, held=()):
        group = clock.hold(grad_group[s])
        return open_back(group, down_weights[s], gate[s], up[s], part, held)

    def back_input(s, part, held=()):
        grad = clock.hold(grad_gate[s])
        return input_back(grad, grad_up[s], gate_weights[s], up_weights[s], part, held)

    def keep_back(work):
        grad_gate.append(work[0])
        grad_up.append(work[1])

    def first_sum(part):
        a, b = hop(*halves(clock.hold(blocks_of(part)(half_wide // 2))), half_wide)
        return a, b

    def rest_sum(part, a, b, beside=lambda step: ()):
        part_of = blocks_of(part)
        other = []
        for k in range(half_wide // 2 - 1, 0, -1):
            if k == half_wide // 2 - 1:
                a = add_first(part_of(k), a)
                b = add_last(part_of(-k), b)
            else:
                a = low_sum(part_of(k), a)
                b = low_sum(part_of(-k), b)
            work = beside(half_wide // 2 - 1 - k)
            a, b = hop(a, b, half_wide)
            a, b, *work = clock.sync(a, b, *work)
            other.append(work)
        return part_of(0).astype(f32) + a.astype(f32) + b.astype(f32), other

    a, b = first_sum(parts[0])
    a, b, *opened = clock.sync(a, b, *open_part(1, 0))
    total, work = rest_sum(
        parts[0], a, b, lambda step: () if step else tuple(open_part(1, 1, opened))
    )
    keep_open(work[0])
    mixed.append(total)
    finish(0)
    parts.append(mix(1))
    blocks, work = ring_gather(
        clock, grad_mixed[0], half_wide, lambda k: (parts[1],) if k == 0 else ()
    )
    parts[1] = work[0][0]
    grad_group.append(jnp.concatenate(blocks, axis=0))
    a, b = first_sum(parts[1])
    a, b, *opened = clock.sync(a, b, *back_hidden(0, 0))

    def beside_last(step):
        if step:
            return ()
        keep_back(back_hidden(0, 1, opened))
        return (grad_gate[0], grad_up[0], *input_back(
            grad_gate[0], grad_up[0], gate_weights[0], up_weights[0], 0, ()
        ))

    total, work = rest_sum(parts[1], a, b, beside_last)
    grad_gate[0], grad_up[0], opened = work[0][0], work[0][1], work[0][2:]
    mixed.append(total)
    finish(1)
    blocks, work = ring_gather(
        clock, grad_mixed[1], half_wide, lambda k: () if k else tuple(back_input(0, 1, opened))
    )
    grad_parts.append(work[0][0])
    grad_group.append(jnp.concatenate(blocks, axis=0))

    def weight_sum(lefts, rights):
        lefts = [clock.hold(v) for v in lefts]
        return weight_back(lefts, rights).reshape(2, hidden, model_dim)

    def part_sum(grad, bit):
        split = grad.reshape(2, 2, grad.shape[1] // 2, model_dim)
        return low_sum(split[:, 0], swap(split[:, 1], "seq", bit))

    grad_middle, grad_branch, grad_send = [], [], []
    gain_third = gain_second = 0.0

    def back_branch(s):
        nonlocal gain_third, gain_second
        grad_normed = clock.hold(grad_normed_mlp[s])
        grad, gain = norm_back(middle[s], middle_factor[s], gain_mlp, grad_normed)
        gain_third = gain_third + gain
        grad_mid = grad_out[s] + grad
        grad, gain = norm_back(branch[s], branch_factor[s], gain_post_attn, grad_mid)
        gain_second = gain_second + gain
        grad = grad.astype(bf16)
        send = dot(grad, out_weights[s], NN).astype(bf16)
        send = jnp.transpose(send.reshape(rows, KEY_VALUE_HEADS, head_cols), (1, 0, 2))
        return [grad_mid, grad, send.reshape(wide, class_rows, head_cols)]

    def keep_branch(work):
        grad_middle.append(work[0])
        grad_branch.append(work[1])
        grad_send.append(work[2])

    a, b = first_sum(grad_parts[0])
    a, b, *opened = clock.sync(a, b, *back_hidden(1, 0))

    def beside_back(step):
        if step:
            return ()
        keep_back(back_hidden(1, 1, opened))
        return (grad_gate[1], grad_up[1], *input_back(
            grad_gate[1], grad_up[1], gate_weights[1], up_weights[1], 0, ()
        ))

    total, work = rest_sum(grad_parts[0], a, b, beside_back)
    grad_gate[1], grad_up[1], opened = work[0][0], work[0][1], work[0][2:]
    grad_normed_mlp.append(total)
    grad_parts += clock.sync(*back_input(1, 1, opened))
    a, b = first_sum(grad_parts[1])
    a, b, *work = clock.sync(a, b, *back_branch(0))
    keep_branch(work)
    total, work = rest_sum(
        grad_parts[1],
        a,
        b,
        lambda step: () if step else (weight_sum(hidden_rows, grad_group),),
    )
    down_grad = work[0][0]
    grad_normed_mlp.append(total)

    def attend_back(s):
        dq, *dkv = attn_backward(
            class_info,
            queries[s],
            pairs[s],
            clock.hold(grad_heads[s]),
            exact[s],
            lse[s],
            class_rows,
            rows,
        )
        return [dq.reshape(wide, class_rows, head_cols)] + dkv

    def class_sum(dkv):
        total = dkv[1 % classes]
        for step in range(2, classes + 1):
            total = low_sum(dkv[step % classes], class_ring(total))
        return total

    def far_parts(grad):
        split = grad.reshape(2, 2, grad.shape[1] // 2, model_dim)
        send = split[:, 1]
        return split[:, 0], [send[:, :, : model_dim // 2], send[:, :, model_dim // 2 :]]

    def far_move(part):
        return swap(clock.hold(part), "seq", seq_bits[1])

    def far_join(kept, moved):
        grad = low_sum(kept, jnp.concatenate(moved, axis=2))
        for bit in seq_bits[2:]:
            grad = part_sum(grad, bit)
        return grad

    grad_heads, grad_attend = [], []
    query_back, pair_back = [], []

    def heads_of(value):
        return value.reshape(wide * class_rows, head_cols)

    back = all_to_all(clock.hold(grad_send[0]))
    down_grad = part_sum(down_grad, 1)
    back, down_grad, *work = clock.sync(back, down_grad, *back_branch(1))
    keep_branch(work)
    grad_heads.append(heads_of(back))
    all_normed = jnp.concatenate(normed, axis=0)
    all_attended = jnp.concatenate(attended, axis=0)
    all_branch = jnp.concatenate(grad_branch, axis=0)

    def half_dot(left, right, which, size):
        return dot(left, lax.dynamic_slice_in_dim(right, which * size, size, 1), TN)

    down_keep, down_parts = far_parts(down_grad)
    down_moved = [far_move(down_parts[0])]
    back = all_to_all(clock.hold(grad_send[1]))
    out_send = half_dot(all_branch, clock.hold(all_attended), 1 - side, half_out).astype(bf16)
    back, down_moved[0], out_send, *work = clock.sync(
        back, down_moved[0], out_send, *attend_back(0)
    )
    down_moved.append(far_move(down_parts[1]))
    grad_heads.append(heads_of(back))
    grad_attend.append(work)

    dq, *dkv = grad_attend[0]
    parts_of_pair = [two_parts(v) for v in dkv]
    out_sent = swap(out_send, "seq", 1)
    query = all_to_all(clock.hold(dq))
    pair_a = class_sum([v[0] for v in parts_of_pair])
    query, pair_a, down_moved[1], out_sent, *work = clock.sync(
        query, pair_a, down_moved[1], out_sent, *attend_back(1)
    )
    down_grad = far_join(down_keep, down_moved)
    query_back.append(query)
    grad_attend.append(work)
    dq, *dkv = grad_attend[1]
    query = all_to_all(clock.hold(dq))
    pair_b = class_sum([clock.hold(v[1]) for v in parts_of_pair])
    up_grad = weight_sum(grad_up, gathered)
    query, pair_b, down_grad, up_grad = clock.sync(query, pair_b, down_grad, up_grad)
    query_back.append(query)

    pair = heads_all_to_all(clock.hold(jnp.concatenate([pair_a, pair_b], axis=0)))
    pair_sum = class_sum([clock.hold(v) for v in dkv])
    up_grad = part_sum(up_grad, 1)
    out_part = low_sum(
        half_dot(all_branch, clock.hold(all_attended), side, half_out), out_sent
    )
    pair, pair_sum, up_grad, out_part = clock.sync(pair, pair_sum, up_grad, out_part)
    out_pieces = {
        t: lax.dynamic_slice_in_dim(out_part, jnp.bitwise_xor(member, t) * split_out, split_out, 1)
        for t in range(members)
    }
    out_parts = None
    if members == 2:
        out_parts = [out_pieces[1][:, : split_out // 2], out_pieces[1][:, split_out // 2 :]]
    else:
        for bit in seq_bits[1:]:
            for t in sorted(out_pieces):
                if not t & (bit // 2) and t | (bit // 2) in out_pieces:
                    out_pieces[t] = low_sum(
                        out_pieces[t], swap(out_pieces.pop(t | (bit // 2)), "seq", bit)
                    )

    def out_move(part):
        return [swap(clock.hold(out_parts[part]), "seq", seq_bits[1])] if out_parts else []

    pair_back.append(pair)
    up_keep, up_parts = far_parts(up_grad)
    up_moved = [far_move(up_parts[0])]
    pair = heads_all_to_all(clock.hold(pair_sum))
    gate_grad = weight_sum(grad_gate, gathered)
    pair, up_moved[0], gate_grad = clock.sync(pair, up_moved[0], gate_grad)
    pair_back.append(pair)

    def column_parts(value, count):
        width = value.shape[1] // count
        return [value[:, i * width : (i + 1) * width] for i in range(count)]

    def exchange_grad(part):
        return swap(clock.hold(part), "wide", half_wide)

    def half_sum(grad):
        split = grad.reshape(2, 2, grad.shape[1] // 2, model_dim)
        return split[:, 0], split[:, 1]

    down_own = column_parts(down_grad[0], 3)
    down_send = column_parts(down_grad[1], 3)
    gate_keep, gate_send = half_sum(gate_grad)
    gate_moved = swap(gate_send, "seq", 1)
    out_moved = out_move(0)
    moved, grad_proj, *out_moved = clock.sync(
        exchange_grad(down_send[0]),
        turn_back(
            [v.reshape(KEY_VALUE_HEADS, rows, head_cols) for v in query_back],
            pair_back,
            cosine,
            sine,
        ),
        *out_moved,
    )
    down_other = [moved]
    up_moved.append(far_move(up_parts[1]))
    moved = exchange_grad(down_send[1])
    proj_send = half_dot(all_normed, clock.hold(grad_proj), 1 - side, half_proj).astype(bf16)
    moved, gate_moved, up_moved[1], proj_send = clock.sync(
        moved, gate_moved, up_moved[1], proj_send
    )
    down_other.append(moved)
    up_grad = far_join(up_keep, up_moved)
    moved = exchange_grad(down_send[2])
    proj_sent = swap(proj_send, "seq", 1)
    gate_grad = low_sum(gate_keep, gate_moved)
    out_moved += out_move(1)
    moved, proj_sent, up_grad, gate_grad, *out_moved = clock.sync(
        moved, proj_sent, up_grad, gate_grad, *out_moved
    )
    out_piece = out_pieces[0]
    if out_moved:
        out_piece = low_sum(out_piece, jnp.concatenate(out_moved, axis=1))
    down_other.append(moved)
    gate_keep, gate_parts = far_parts(gate_grad)
    down_grad = [low_sum(x, y) for x, y in zip(down_own, down_other)]
    proj_part = low_sum(half_dot(all_normed, clock.hold(grad_proj), side, half_proj), proj_sent)
    (proj_part,) = clock.sync(proj_part)
    def part_of(o):
        first = index_at(o) * attn_rows
        return jnp.concatenate(
            [
                lax.dynamic_slice_in_dim(proj_part, first, attn_rows, 0),
                lax.dynamic_slice_in_dim(out_piece, first, attn_rows, 0),
            ],
            axis=1,
        )

    def spread_grad(grads, bits):
        for bit in bits:
            grads = [jnp.concatenate([g, swap(g, "seq", bit)], axis=0) for g in grads]
        return grads

    a, b = halves(clock.hold(part_of(wide // 2)))
    gate_moved = []
    for k in range(wide // 2 - 1, -1, -1):
        step = wide // 2 - 1 - k
        a, b = hop(a, b, wide)
        work = []
        if step in (1, 2):
            work = [far_move(gate_parts[step - 1])]
        elif step == half_wide - 1:
            work = spread_grad([clock.hold(v) for v in down_grad], far_bits)
        a, b, *work = clock.sync(a, b, *work)
        if step in (1, 2):
            gate_moved += work
        elif step == half_wide - 1:
            down_grad = work
        if step == 0:
            a, b = add_first(part_of(k), a), add_last(part_of(-k), b)
        elif k > 0:
            a, b = low_sum(part_of(k), a), low_sum(part_of(-k), b)
    total = low_sum(part_of(0), a, b)
    gate_grad = far_join(gate_keep, gate_moved)
    up_own, up_send = column_parts(up_grad[0], 2), column_parts(up_grad[1], 2)
    total, gate_grad, *up_send = clock.sync(total, gate_grad, *up_send)

    def input_grad(s):
        return dot(clock.hold(grad_proj[s * rows : (s + 1) * rows]), proj_weights[s], NT)

    def back_tokens(s, grad_normed):
        grad, gain = norm_back(inputs[s], input_factor[s], gain_attn, grad_normed)
        return (grad_middle[s] + grad).astype(bf16), gain

    def add_swapped(gains, axis, bits):
        for bit in bits:
            gains = gains + swap(gains, axis, bit)
        return gains

    proj_total = total[:, :half_proj]
    out_totals = {0: total[:, half_proj:]}
    for bit in seq_bits[1:]:
        sent = jnp.concatenate([proj_total] + [out_totals[t] for t in sorted(out_totals)], axis=1)
        moved = swap(sent, "seq", bit)
        proj_total = low_sum(proj_total, moved[:, :half_proj])
        for i, t in enumerate(sorted(out_totals)):
            first = half_proj + i * split_out
            out_totals[t | (bit // 2)] = moved[:, first : first + split_out]
    out_totals = jnp.stack([out_totals[t] for t in range(members)])
    low = jnp.concatenate(
        [proj_total]
        + [
            lax.dynamic_index_in_dim(out_totals, jnp.bitwise_xor(member, j), 0, keepdims=False)
            for j in range(members)
        ],
        axis=1,
    )
    moved, grad_first = clock.sync(exchange_grad(up_send[0]), input_grad(0))
    up_grad = [low_sum(up_own[0], moved)]
    moved, low, grad_last = clock.sync(exchange_grad(up_send[1]), low, input_grad(1))
    up_grad.append(low_sum(up_own[1], moved))
    gate_own, gate_send = column_parts(gate_grad[0], 2), column_parts(gate_grad[1], 2)
    first_tokens, gain_first = back_tokens(0, grad_first)
    last_tokens, gain = back_tokens(1, grad_last)
    gains = jnp.stack([gain_first + gain, gain_second, gain_third, gain_fourth])
    wide_bits = [1 << i for i in range(wide.bit_length() - 1)]
    gains, *gate_send = clock.sync(add_swapped(gains, "wide", wide_bits[1:]), *gate_send)
    moved = exchange_grad(gate_send[0])
    up_grad = spread_grad([clock.hold(v) for v in up_grad], far_bits)
    other = swap(clock.hold(low), "seq", 1)
    moved, other, *up_grad = clock.sync(moved, other, *up_grad)
    gate_grad = [low_sum(gate_own[0], moved)]
    moved = exchange_grad(gate_send[1])
    gate_grad = spread_grad([clock.hold(v) for v in gate_grad], far_bits)
    left, right = jnp.where(is_low, low, other), jnp.where(is_low, other, low)
    attn_grad = jnp.concatenate(
        [left[:, :half_proj], right[:, :half_proj], left[:, half_proj:], right[:, half_proj:]],
        axis=1,
    ).astype(f32)
    down_grad = spread_grad([clock.hold(v) for v in down_grad], seq_bits[:1])
    up_grad = spread_grad([clock.hold(v) for v in up_grad], seq_bits[:1])
    mlp_grad = unpack(down_grad, pieces, 2, [])
    mlp_grad = unpack(up_grad, pieces, 1, [mlp_grad])
    moved, attn_grad, mlp_grad, *gate_grad = clock.sync(moved, attn_grad, mlp_grad, *gate_grad)
    last = spread_grad([low_sum(gate_own[1], moved)], far_bits)
    gains = add_swapped(clock.hold(gains), "wide", wide_bits[:1])
    gains = add_swapped(add_swapped(gains, "seq", seq_bits[:1]), "seq", seq_bits[1:])
    gate_grad = spread_grad([clock.hold(v) for v in gate_grad], seq_bits[:1])
    mlp_grad = unpack(gate_grad, pieces, 0, [mlp_grad], 0)
    mlp_grad, gains, *last = clock.sync(mlp_grad, gains, *last)
    mlp_grad = unpack(spread_grad(last, seq_bits[:1]), pieces, 0, [mlp_grad], 1)
    grad_tokens = [first_tokens, last_tokens]
    return (
        jnp.stack(layer_out),
        jnp.stack(grad_tokens),
        attn_grad,
        mlp_grad,
        gains[0],
        gains[1],
        gains[2],
        gains[3],
    )


def solution(mesh):
    placed = (
        P("seq", "wide", None),
        P("seq", "wide", None),
        P("seq"),
        P("wide", None),
        P(),
        P(),
        P(None, "wide", None),
        P(),
        P(),
        P(),
        P(),
        P(),
        P(),
    )
    return jax.shard_map(
        per_device,
        mesh=mesh,
        in_specs=placed,
        out_specs=(
            P("seq", "wide", None),
            P("seq", "wide", None),
            P("wide", None),
            P(None, "wide", None),
            P(),
            P(),
            P(),
            P(),
        ),
        check_vma=False,
    )
```

```python
import functools
import math

import jax
import jax.numpy as jnp
from jax import lax
from jax.experimental import pallas as pl
from jax.experimental.pallas import tpu as pltpu
from jax.sharding import PartitionSpec as P

QUERY_HEADS = 8
KEY_VALUE_HEADS = 4
HEAD_SIZE = 256
PAIRED = QUERY_HEADS // KEY_VALUE_HEADS

eps_norm = 1e-06
soft_cap = 50.0
rope_base = 10000.0
gelu_coeff = math.sqrt(2.0 / math.pi)
f32 = jnp.float32
bf16 = jnp.bfloat16
VMEM_LIMIT = 56 * 1024 * 1024


def dot(a, b, dims):
    return lax.dot_general(a, b, (dims, ((), ())), preferred_element_type=f32)


NN = ((1,), (0,))
NT = ((1,), (1,))
TN = ((0,), (0,))


def inverse_powers(exponents):
    return 1.0 / jnp.left_shift(jnp.ones_like(exponents), exponents).astype(f32)


def norm_factor(values):
    return lax.rsqrt(jnp.mean(values * values, axis=-1, keepdims=True) + eps_norm)


def norm_back(values, factor, gain, grad):
    scaled = grad * gain
    inner = jnp.mean(values * scaled, axis=-1, keepdims=True)
    grad_values = factor * scaled - values * (factor * factor * factor * inner)
    return grad_values, jnp.sum(grad * values * factor, axis=0)


def gelu_parts(values):
    inner = gelu_coeff * (values + 0.044715 * values * values * values)
    return jnp.tanh(inner)


def rotary_rows(positions):
    half_dim = HEAD_SIZE // 2
    frequency = jnp.exp(
        jnp.arange(half_dim, dtype=f32) * (-2.0 * math.log(rope_base) / HEAD_SIZE)
    )
    angles = positions.astype(f32)[:, None] * frequency[None, :]
    return jnp.cos(angles), jnp.sin(angles)


def ring_place(index, size):
    return jnp.where(index % 2 == 0, index // 2, size - 1 - index // 2)


def ring_index(place, size):
    return jnp.where(place < size // 2, 2 * place, 2 * (size - 1 - place) + 1)


def ring_perms(size):
    order = list(range(0, size, 2)) + list(range(size - 1, 0, -2))
    up = [
        (base + order[i], base + order[(i + 1) % size])
        for base in range(0, lax.axis_size("wide"), size)
        for i in range(size)
    ]
    return up, [(b, a) for a, b in up]


def ring_offsets(size):
    out = [0]
    for k in range(1, size // 2):
        out += [-k, k]
    return out + [size // 2]


class Clock:
    def __init__(self, token):
        self.token = token

    def sync(self, *arrays):
        *arrays, self.token = lax.optimization_barrier(tuple(arrays) + (self.token,))
        return arrays

    def hold(self, value):
        return lax.optimization_barrier((value, self.token))[0]


def hop(a, b, size):
    up, down = ring_perms(size)
    return lax.ppermute(a, "wide", up), lax.ppermute(b, "wide", down)


def low_sum(*terms):
    return sum(t.astype(f32) for t in terms).astype(bf16)


def halves(value):
    half = value.shape[0] // 2
    return value[:half], value[half:]


def add_first(whole, part):
    count = part.shape[0]
    return jnp.concatenate([low_sum(whole[:count], part), whole[count:].astype(bf16)], axis=0)


def add_last(whole, part):
    count = whole.shape[0] - part.shape[0]
    return jnp.concatenate([whole[:count].astype(bf16), low_sum(whole[count:], part)], axis=0)


def ring_gather(clock, value, size, beside=lambda step: ()):
    a = b = clock.hold(value)
    out, other = [a], []
    for k in range(1, size // 2 + 1):
        if k == size // 2:
            a, b = halves(a)[0], halves(b)[1]
        work = beside(k - 1)
        a, b = hop(a, b, size)
        a, b, *work = clock.sync(a, b, *work)
        out += [a, b]
        other.append(work)
    return out, other


def ring_scatter(clock, part_of, rows, size, beside=lambda step: ()):
    a, b = halves(clock.hold(part_of(size // 2).astype(bf16)))
    other = []
    for k in range(size // 2 - 1, -1, -1):
        work = beside(size // 2 - 1 - k)
        a, b = hop(a, b, size)
        a, b, *work = clock.sync(a, b, *work)
        other.append(work)
        if k == size // 2 - 1 and k > 0:
            a = add_first(part_of(k), a)
            b = add_last(part_of(-k), b)
        elif k > 0:
            a = low_sum(part_of(k), a)
            b = low_sum(part_of(-k), b)
    return part_of(0).astype(f32) + a.astype(f32) + b.astype(f32), other


def swap(value, axis, bit):
    size = lax.axis_size(axis)
    return lax.ppermute(value, axis, [(i, i ^ bit) for i in range(size)])


def all_to_all(value):
    return lax.all_to_all(value, "wide", split_axis=0, concat_axis=0, tiled=True)


def heads_all_to_all(value):
    size = lax.axis_size("wide")
    classes = size // KEY_VALUE_HEADS
    groups = [list(range(c, size, classes)) for c in range(classes)]
    return lax.all_to_all(
        value, "wide", split_axis=0, concat_axis=0, axis_index_groups=groups, tiled=True
    )


def class_ring(value):
    size = lax.axis_size("wide")
    classes = size // KEY_VALUE_HEADS
    perm = [(i, i // classes * classes + (i + 1) % classes) for i in range(size)]
    return lax.ppermute(value, "wide", perm)


def slice_values(codes, width):
    lift = jnp.where(width == 0, 0.0, 0.5).astype(bf16)
    large = jnp.where(width == 0, 0.0, jnp.where(width == 1, 1.5 * 2**11, 1.5 * 2**13)).astype(bf16)
    top = jnp.where(width == 0, 127.0, jnp.where(width == 1, 112.0, 64.0)).astype(bf16)
    return jnp.minimum(((codes + lift) + large) - large, top)


def proj_slice_kernel(places, info, *refs, blocks, count):
    code_refs, scale_ref, out_refs = refs[: 2 * blocks], refs[2 * blocks], refs[len(refs) - count :]
    mine = pl.program_id(1) == info[0]

    def write(code_ref):
        codes = code_ref[...]
        scale = scale_ref[...].astype(bf16)
        for s, out_ref in enumerate(out_refs):
            out_ref[...] = slice_values(codes, info[1 + s]) * scale

    for k in range(blocks):
        here = pl.program_id(0) == k
        pl.when(jnp.logical_and(here, mine))(functools.partial(write, code_refs[2 * k]))
        pl.when(jnp.logical_and(here, jnp.logical_not(mine)))(
            functools.partial(write, code_refs[2 * k + 1])
        )


def proj_slices(own, other, places, info, scale, width, weights, total, count):
    blocks = len(own)
    rows = own[0].shape[0]
    inputs = [block for pair in zip(own, other) for block in pair] + [scale]
    grid_spec = pltpu.PrefetchScalarGridSpec(
        num_scalar_prefetch=2,
        grid=(blocks, 2),
        in_specs=[pl.BlockSpec((rows, width), lambda k, j, p, i: (0, 0))] * (2 * blocks)
        + [pl.BlockSpec((1, width), lambda k, j, p, i: (0, j))]
        + [pl.BlockSpec(memory_space=pl.ANY)] * len(weights),
        out_specs=[pl.BlockSpec((rows, width), lambda k, j, p, i: (p[k], j))] * count,
    )
    return pl.pallas_call(
        functools.partial(proj_slice_kernel, blocks=blocks, count=count),
        grid_spec=grid_spec,
        out_shape=[jax.ShapeDtypeStruct((total * rows, 2 * width), bf16)] * count,
        input_output_aliases={2 + len(inputs) + s: s for s in range(len(weights))},
        compiler_params=pltpu.CompilerParams(vmem_limit_bytes=VMEM_LIMIT),
        cost_estimate=pl.CostEstimate(
            flops=20 * count * blocks * rows * width,
            bytes_accessed=4 * blocks * rows * width * (1 + count),
            transcendentals=0,
        ),
        name="proj_slices",
    )(places, info, *inputs, *weights)


def out_slice_kernel(places, info, *refs, split, count):
    inputs, scale_ref, out_refs = refs[: -1 - count], refs[-1 - count], refs[-count:]
    members = len(inputs) // 2
    member = info[1 + count]
    mine = pl.program_id(1) == info[0]

    def write(code_refs):
        scale = scale_ref[...].astype(bf16)
        for t, code_ref in enumerate(code_refs):
            first = pl.multiple_of(jnp.bitwise_xor(member, t) * split, 128)
            for s, out_ref in enumerate(out_refs):
                out_ref[:, pl.ds(first, split)] = slice_values(code_ref[0], info[1 + s]) * scale

    pl.when(mine)(lambda: write(inputs[:members]))
    pl.when(jnp.logical_not(mine))(lambda: write(inputs[members:]))


def out_slices(own, other, places, info, scale, count):
    blocks, rows, split = own[0].shape
    width = split * len(own)
    inputs = list(own) + list(other)
    grid_spec = pltpu.PrefetchScalarGridSpec(
        num_scalar_prefetch=2,
        grid=(blocks, 2),
        in_specs=[pl.BlockSpec((1, rows, split), lambda k, j, p, i: (k, 0, 0))] * len(inputs)
        + [pl.BlockSpec((rows, 1), lambda k, j, p, i: (p[k], 0))],
        out_specs=[pl.BlockSpec((rows, width), lambda k, j, p, i: (p[k], j))] * count,
    )
    return pl.pallas_call(
        functools.partial(out_slice_kernel, split=split, count=count),
        grid_spec=grid_spec,
        out_shape=[jax.ShapeDtypeStruct((blocks * rows, 2 * width), bf16)] * count,
        compiler_params=pltpu.CompilerParams(vmem_limit_bytes=VMEM_LIMIT),
        cost_estimate=pl.CostEstimate(
            flops=20 * count * blocks * rows * width,
            bytes_accessed=4 * blocks * rows * width * (1 + count),
            transcendentals=0,
        ),
        name="out_slices",
    )(places, info, *inputs, scale)


def own_slice_kernel(pieces, info, code_ref, row_ref, col_ref, *out_refs):
    count = len(out_refs) // 3
    for m in range(3):
        codes = code_ref[m].astype(f32).astype(bf16)
        scale = (row_ref[m] if m < 2 else col_ref[...]).astype(bf16)
        for s in range(count):
            out_refs[m * count + s][...] = slice_values(codes, info[1 + s]) * scale


def own_slices(codes, pieces, info, row_scale, col_scale, count):
    three, rows, cols = codes.shape
    steps = pieces.shape[0]
    piece = rows // steps
    grid_spec = pltpu.PrefetchScalarGridSpec(
        num_scalar_prefetch=2,
        grid=(steps,),
        in_specs=[
            pl.BlockSpec((three, piece, cols), lambda j, p, i: (0, p[j], 0)),
            pl.BlockSpec((2, piece, 1), lambda j, p, i: (0, j, 0)),
            pl.BlockSpec((1, cols), lambda j, p, i: (0, 0)),
        ],
        out_specs=[pl.BlockSpec((piece, cols), lambda j, p, i: (j, 0))] * (three * count),
    )
    return pl.pallas_call(
        own_slice_kernel,
        grid_spec=grid_spec,
        out_shape=[jax.ShapeDtypeStruct((2 * rows, cols), bf16)] * (three * count),
        compiler_params=pltpu.CompilerParams(vmem_limit_bytes=VMEM_LIMIT),
        cost_estimate=pl.CostEstimate(
            flops=10 * count * codes.size,
            bytes_accessed=codes.size * (4 + 2 * count),
            transcendentals=0,
        ),
        name="own_slices",
    )(pieces, info, codes, row_scale, col_scale)


def partner_slice_kernel(info, *refs, steps, count):
    piece_refs, scale_ref, out_refs = refs[:steps], refs[steps], refs[steps + 1 + count :]
    for j in range(steps):

        @pl.when(pl.program_id(0) == j)
        def _():
            codes = piece_refs[j][...]
            scale = scale_ref[...].astype(bf16)
            for s, out_ref in enumerate(out_refs):
                out_ref[...] = slice_values(codes, info[1 + s]) * scale


def partner_slices(pieces, info, scale, by_column, weights):
    steps = len(pieces)
    count = len(weights)
    piece, cols = pieces[0].shape
    if by_column:
        scale_spec = pl.BlockSpec((1, cols), lambda j, i: (0, 0))
    else:
        scale_spec = pl.BlockSpec((piece, 1), lambda j, i: (steps + j, 0))
    grid_spec = pltpu.PrefetchScalarGridSpec(
        num_scalar_prefetch=1,
        grid=(steps,),
        in_specs=[pl.BlockSpec((piece, cols), lambda j, i: (0, 0))] * steps
        + [scale_spec]
        + [pl.BlockSpec(memory_space=pl.ANY)] * count,
        out_specs=[pl.BlockSpec((piece, cols), lambda j, i: (steps + j, 0))] * count,
    )
    return pl.pallas_call(
        functools.partial(partner_slice_kernel, steps=steps, count=count),
        grid_spec=grid_spec,
        out_shape=[jax.ShapeDtypeStruct(w.shape, bf16) for w in weights],
        input_output_aliases={2 + steps + s: s for s in range(count)},
        compiler_params=pltpu.CompilerParams(vmem_limit_bytes=VMEM_LIMIT),
        cost_estimate=pl.CostEstimate(
            flops=10 * count * steps * piece * cols,
            bytes_accessed=2 * (1 + count) * steps * piece * cols,
            transcendentals=0,
        ),
        name="partner_slices",
    )(info, *pieces, scale, *weights)


def unpack_kernel(pieces, *refs, parts):
    first = 0
    for ref in refs[:parts]:
        width = ref.shape[1]
        refs[-1][0, :, first : first + width] = ref[...].astype(f32)
        first += width


def unpack(grads, pieces, matrix, held):
    steps = pieces.shape[0]
    rows = grads[0].shape[0]
    cols = sum(g.shape[1] for g in grads)
    piece = rows // steps
    grid_spec = pltpu.PrefetchScalarGridSpec(
        num_scalar_prefetch=1,
        grid=(steps,),
        in_specs=[pl.BlockSpec((piece, g.shape[1]), lambda j, p: (j, 0)) for g in grads]
        + [pl.BlockSpec(memory_space=pl.ANY)] * len(held),
        out_specs=pl.BlockSpec((1, piece, cols), lambda j, p: (matrix, p[j], 0)),
    )
    return pl.pallas_call(
        functools.partial(unpack_kernel, parts=len(grads)),
        grid_spec=grid_spec,
        out_shape=jax.ShapeDtypeStruct((3, rows, cols), f32),
        input_output_aliases={1 + len(grads): 0} if held else {},
        compiler_params=pltpu.CompilerParams(vmem_limit_bytes=VMEM_LIMIT),
        cost_estimate=pl.CostEstimate(
            flops=rows * cols, bytes_accessed=6 * rows * cols, transcendentals=0
        ),
        name="unpack",
    )(pieces, *grads, *held)


def tile_of(size):
    return 256 if size % 256 == 0 else size


def tiles_of(size, part):
    tile = tile_of(size)
    tiles = size // tile
    first_part = (tiles + 1) // 2
    if part is None or tiles == 1:
        return tile, 0, tiles
    return (tile, 0, first_part) if part == 0 else (tile, first_part, tiles - first_part)


def whole_spec(shape):
    return pl.BlockSpec(shape, lambda i: (0, 0))


def column_spec(rows, tile, first=0):
    return pl.BlockSpec((rows, tile), lambda i: (0, first + i))


def row_spec(tile, cols, first=0):
    return pl.BlockSpec((tile, cols), lambda i: (first + i, 0))


def kernel_call(kernel, grid, in_specs, out_specs, out_shape, flops, moved, name, held=()):
    inputs = len(in_specs)
    return pl.pallas_call(
        lambda *refs: kernel(*refs[:inputs], *refs[inputs + len(held) :]),
        grid=(grid,),
        in_specs=in_specs + [pl.BlockSpec(memory_space=pl.ANY)] * len(held),
        out_specs=out_specs,
        out_shape=out_shape,
        input_output_aliases={inputs + i: i for i in range(len(held))},
        compiler_params=pltpu.CompilerParams(vmem_limit_bytes=VMEM_LIMIT),
        cost_estimate=pl.CostEstimate(flops=flops, bytes_accessed=moved, transcendentals=0),
        name=name,
    )


def row_parts(rows):
    part = 512 if rows % 512 == 0 else rows
    return [slice(first, first + part) for first in range(0, rows, part)]


def open_kernel(x_ref, wg_ref, wu_ref, gate_ref, up_ref, hidden_ref):
    for part in row_parts(x_ref.shape[0]):
        x = x_ref[part]
        gate = dot(x, wg_ref[...], NT)
        up = dot(x, wu_ref[...], NT)
        gate_ref[part] = gate
        up_ref[part] = up
        hidden_ref[part] = (gate * (0.5 + 0.5 * gelu_parts(gate)) * up).astype(bf16)


def open_forward(x, gate_weights, up_weights, part, held=()):
    rows, depth = x.shape
    hidden = gate_weights.shape[0]
    tile, first, tiles = tiles_of(hidden, part)
    if held and tiles * tile == hidden:
        return list(held)
    return kernel_call(
        open_kernel,
        tiles,
        [whole_spec(x.shape)] + [row_spec(tile, depth, first)] * 2,
        [column_spec(rows, tile, first)] * 3,
        [jax.ShapeDtypeStruct((rows, hidden), t) for t in (f32, f32, bf16)],
        4 * rows * depth * tile * tiles,
        2 * rows * depth + tiles * tile * (4 * depth + 10 * rows),
        "open_forward",
        held,
    )(x, gate_weights, up_weights, *held)


def open_back_kernel(x_ref, wd_ref, gate_ref, up_ref, grad_gate_ref, grad_up_ref):
    for part in row_parts(x_ref.shape[0]):
        grad = dot(x_ref[part], wd_ref[...], NT)
        gate = gate_ref[part]
        square = gate * gate
        bounded = jnp.tanh(gate * (gelu_coeff + (0.044715 * gelu_coeff) * square))
        half = 0.5 + 0.5 * bounded
        steep = (0.5 * gelu_coeff) + (1.5 * 0.044715 * gelu_coeff) * square
        slope = half + gate * (1.0 - bounded * bounded) * steep
        grad_gate_ref[part] = (grad * up_ref[part] * slope).astype(bf16)
        grad_up_ref[part] = (grad * (gate * half)).astype(bf16)


def open_back(x, down_weights, gate, up, part, held=()):
    rows, depth = x.shape
    hidden = down_weights.shape[0]
    tile, first, tiles = tiles_of(hidden, part)
    if held and tiles * tile == hidden:
        return list(held)
    return kernel_call(
        open_back_kernel,
        tiles,
        [whole_spec(x.shape), row_spec(tile, depth, first)] + [column_spec(rows, tile, first)] * 2,
        [column_spec(rows, tile, first)] * 2,
        [jax.ShapeDtypeStruct((rows, hidden), bf16)] * 2,
        2 * rows * depth * tile * tiles,
        2 * rows * depth + tiles * tile * (2 * depth + 12 * rows),
        "open_back",
        held,
    )(x, down_weights, gate, up, *held)


def input_back_kernel(gate_ref, up_ref, wg_ref, wu_ref, out_ref):
    out_ref[...] = (
        dot(gate_ref[...], wg_ref[...], NN) + dot(up_ref[...], wu_ref[...], NN)
    ).astype(bf16)


def input_back(grad_gate, grad_up, gate_weights, up_weights, part, held=()):
    rows, hidden = grad_gate.shape
    depth = gate_weights.shape[1]
    tile, first, tiles = tiles_of(depth, part)
    if held and tiles * tile == depth:
        return list(held)
    return kernel_call(
        input_back_kernel,
        tiles,
        [whole_spec(grad_gate.shape)] * 2 + [column_spec(hidden, tile, first)] * 2,
        [column_spec(rows, tile, first)],
        [jax.ShapeDtypeStruct((rows, depth), bf16)],
        4 * rows * hidden * tile * tiles,
        4 * rows * hidden + tiles * tile * (4 * hidden + 2 * rows),
        "input_back",
        held,
    )(grad_gate, grad_up, gate_weights, up_weights, *held)


def weight_kernel(*refs, count):
    out_ref = refs[-1]
    total = dot(refs[0][...], refs[count][...], TN)
    for s in range(1, count):
        total = total + dot(refs[s][...], refs[count + s][...], TN)
    out_ref[...] = total.astype(bf16)


def weight_back(lefts, rights):
    count = len(lefts)
    rows, hidden = lefts[0].shape
    depth = rights[0].shape[1]
    tile = tile_of(hidden)
    return kernel_call(
        functools.partial(weight_kernel, count=count),
        hidden // tile,
        [column_spec(rows, tile)] * count + [whole_spec((rows, depth))] * count,
        row_spec(tile, depth),
        jax.ShapeDtypeStruct((hidden, depth), bf16),
        2 * count * rows * depth * hidden,
        2 * count * rows * (hidden + depth) + 2 * hidden * depth,
        "weight_back",
    )(*lefts, *rights)


def turn(values, cosine, sine):
    half = HEAD_SIZE // 2
    out = []
    for j in range(values.shape[1] // HEAD_SIZE):
        a = values[:, j * HEAD_SIZE : j * HEAD_SIZE + half]
        b = values[:, j * HEAD_SIZE + half : (j + 1) * HEAD_SIZE]
        out += [a * cosine - b * sine, b * cosine + a * sine]
    return jnp.concatenate(out, axis=1)


def project_kernel(x_ref, wq_ref, wk_ref, wv_ref, cos_ref, sin_ref, q_ref, kv_ref):
    x = x_ref[...]
    cosine, sine = cos_ref[...], sin_ref[...]
    scale = HEAD_SIZE ** (-0.5)
    q_ref[0] = (turn(dot(x, wq_ref[...], NN), cosine, sine) * scale).astype(bf16)
    kv_ref[0, :, :HEAD_SIZE] = turn(dot(x, wk_ref[...], NN), cosine, sine).astype(bf16)
    kv_ref[0, :, HEAD_SIZE:] = dot(x, wv_ref[...], NN).astype(bf16)


def project(normed, weights, cosine, sine):
    rows, depth = normed.shape
    cols = PAIRED * HEAD_SIZE
    first_key = QUERY_HEADS
    first_value = QUERY_HEADS + KEY_VALUE_HEADS
    whole = lambda shape: pl.BlockSpec(shape, lambda h: (0, 0))
    return pl.pallas_call(
        project_kernel,
        grid=(KEY_VALUE_HEADS,),
        in_specs=[
            whole((rows, depth)),
            pl.BlockSpec((depth, cols), lambda h: (0, h)),
            pl.BlockSpec((depth, HEAD_SIZE), lambda h: (0, first_key + h)),
            pl.BlockSpec((depth, HEAD_SIZE), lambda h: (0, first_value + h)),
            whole(cosine.shape),
            whole(sine.shape),
        ],
        out_specs=[
            pl.BlockSpec((1, rows, cols), lambda h: (h, 0, 0)),
            pl.BlockSpec((1, rows, 2 * HEAD_SIZE), lambda h: (h, 0, 0)),
        ],
        out_shape=[
            jax.ShapeDtypeStruct((KEY_VALUE_HEADS, rows, cols), bf16),
            jax.ShapeDtypeStruct((KEY_VALUE_HEADS, rows, 2 * HEAD_SIZE), bf16),
        ],
        compiler_params=pltpu.CompilerParams(vmem_limit_bytes=VMEM_LIMIT),
        cost_estimate=pl.CostEstimate(
            flops=2 * rows * weights.size, bytes_accessed=2 * weights.size, transcendentals=0
        ),
        name="project",
    )(normed, weights, weights, weights, cosine, sine)


def turn_back_kernel(*refs, count):
    q_refs, kv_refs = refs[:count], refs[count : 2 * count]
    cos_ref, sin_ref, out_ref = refs[2 * count :]
    j = pl.program_id(1)
    scale = HEAD_SIZE ** (-0.5)
    keys = KEY_VALUE_HEADS // PAIRED
    for s in range(count):
        here = pl.program_id(0) == s

        @pl.when(jnp.logical_and(here, j < KEY_VALUE_HEADS))
        def _():
            grad = q_refs[s][0].astype(f32) * scale
            out_ref[...] = turn(grad, cos_ref[...], -sin_ref[...]).astype(bf16)

        @pl.when(jnp.logical_and(here, jnp.logical_and(j >= KEY_VALUE_HEADS, j < KEY_VALUE_HEADS + keys)))
        def _():
            grad = jnp.concatenate([kv_refs[s][i, :, :HEAD_SIZE] for i in range(PAIRED)], axis=1)
            out_ref[...] = turn(grad.astype(f32), cos_ref[...], -sin_ref[...]).astype(bf16)

        @pl.when(jnp.logical_and(here, j >= KEY_VALUE_HEADS + keys))
        def _():
            out_ref[...] = jnp.concatenate(
                [kv_refs[s][i, :, HEAD_SIZE:] for i in range(PAIRED)], axis=1
            )


def turn_back(queries, pairs, cosine, sine):
    count = len(queries)
    heads, rows, cols = queries[0].shape
    keys = heads // PAIRED
    grid = (count, heads + 2 * keys)
    whole = pl.BlockSpec(cosine.shape, lambda s, j: (0, 0))
    return pl.pallas_call(
        functools.partial(turn_back_kernel, count=count),
        grid=grid,
        in_specs=[
            pl.BlockSpec((1, rows, cols), lambda s, j: (jnp.minimum(j, heads - 1), 0, 0))
        ]
        * count
        + [
            pl.BlockSpec(
                (PAIRED, rows, cols), lambda s, j: (jnp.maximum(j - heads, 0) % keys, 0, 0)
            )
        ]
        * count
        + [whole, whole],
        out_specs=pl.BlockSpec((rows, cols), lambda s, j: (s, j)),
        out_shape=jax.ShapeDtypeStruct((count * rows, grid[1] * cols), bf16),
        compiler_params=pltpu.CompilerParams(vmem_limit_bytes=VMEM_LIMIT),
        cost_estimate=pl.CostEstimate(
            flops=4 * count * rows * grid[1] * cols,
            bytes_accessed=4 * count * rows * grid[1] * cols,
            transcendentals=0,
        ),
        name="turn_back",
    )(*queries, *pairs, cosine, sine)


def tile_positions(tile, count, start, class_index, class_rows, rows):
    index = lax.broadcasted_iota(jnp.int32, (count, 1), 0)
    place = start + jnp.bitwise_and(index, tile - 1)
    shift = class_rows.bit_length() - 1
    return (
        jnp.right_shift(place, shift) * rows
        + class_index * class_rows
        + jnp.bitwise_and(place, class_rows - 1)
    )


def stack_heads(block):
    return jnp.concatenate(
        [block[:, j * HEAD_SIZE : (j + 1) * HEAD_SIZE] for j in range(PAIRED)], axis=0
    )


def key_places(group, class_index, classes, rows):
    index = lax.broadcasted_iota(jnp.int32, (1, classes * rows), 1)
    shift = rows.bit_length() - 1
    back = jnp.bitwise_and(class_index - jnp.right_shift(index, shift), classes - 1)
    return (group * classes + back) * rows + jnp.bitwise_and(index, rows - 1)


def held_block(refs, group, cols):
    return jnp.concatenate([ref[group, :, cols] for ref in refs], axis=0)


def group_range(start, tile, class_rows, classes):
    return start // class_rows // classes, (start + tile - 1) // class_rows // classes + 1


def attn_forward_kernel(info, q_ref, *refs, tile, class_rows, rows, classes):
    kv_refs = refs[:classes]
    att_ref, exact_ref, lse_ref = refs[classes:]
    start = pl.program_id(0) * tile
    free, total = group_range(start, tile, class_rows, classes)
    queries = stack_heads(q_ref[...])
    count = queries.shape[0]
    position = tile_positions(tile, count, start, info[0], class_rows, rows)

    def step(group, carry, masked):
        acc, row_sum = carry
        keys = held_block(kv_refs, group, slice(0, HEAD_SIZE))
        values = held_block(kv_refs, group, slice(HEAD_SIZE, 2 * HEAD_SIZE))
        raw = dot(queries, keys, NT)
        weight = jnp.exp(soft_cap * jnp.tanh(raw * (1.0 / soft_cap)))
        if masked:
            weight = jnp.where(
                key_places(group, info[0], classes, rows) <= position, weight, 0.0
            )
        row_sum = row_sum + jnp.sum(weight, axis=-1, keepdims=True)
        acc = acc + dot(weight.astype(bf16), values, NN)
        return acc, row_sum

    carry = (jnp.zeros((count, HEAD_SIZE), f32), jnp.zeros((count, 1), f32))
    carry = lax.fori_loop(0, free, functools.partial(step, masked=False), carry)
    acc, row_sum = lax.fori_loop(free, total, functools.partial(step, masked=True), carry)
    exact = acc / row_sum
    lse = jnp.log(row_sum)
    for j in range(PAIRED):
        cols = slice(j * HEAD_SIZE, (j + 1) * HEAD_SIZE)
        exact_ref[:, cols] = exact[j * tile : (j + 1) * tile]
        att_ref[:, cols] = exact[j * tile : (j + 1) * tile].astype(bf16)
        lse_ref[:, j * 128 : (j + 1) * 128] = jnp.broadcast_to(
            lse[j * tile : (j + 1) * tile], (tile, 128)
        )


def attn_forward(info, queries, pairs, class_rows, rows):
    count, cols = queries.shape
    classes = len(pairs)
    length = classes * pairs[0].shape[0] * rows
    tile = min(256, count)
    grid_spec = pltpu.PrefetchScalarGridSpec(
        num_scalar_prefetch=1,
        grid=(count // tile,),
        in_specs=[pl.BlockSpec((tile, cols), lambda i, c: (i, 0))]
        + [pl.BlockSpec(p.shape, lambda i, c: (0, 0, 0)) for p in pairs],
        out_specs=[
            pl.BlockSpec((tile, cols), lambda i, c: (i, 0)),
            pl.BlockSpec((tile, cols), lambda i, c: (i, 0)),
            pl.BlockSpec((tile, PAIRED * 128), lambda i, c: (i, 0)),
        ],
    )
    return pl.pallas_call(
        functools.partial(
            attn_forward_kernel, tile=tile, class_rows=class_rows, rows=rows, classes=classes
        ),
        grid_spec=grid_spec,
        out_shape=[
            jax.ShapeDtypeStruct((count, cols), bf16),
            jax.ShapeDtypeStruct((count, cols), f32),
            jax.ShapeDtypeStruct((count, PAIRED * 128), f32),
        ],
        compiler_params=pltpu.CompilerParams(vmem_limit_bytes=VMEM_LIMIT),
        cost_estimate=pl.CostEstimate(
            flops=2 * count * PAIRED * length * 2 * HEAD_SIZE,
            bytes_accessed=8 * count * cols + 4 * length * HEAD_SIZE,
            transcendentals=2 * count * PAIRED * length,
        ),
        name="attn_forward",
    )(info, queries, *pairs)


def attn_backward_kernel(info, q_ref, grad_ref, exact_ref, lse_ref, *refs, tile, class_rows, rows, classes):
    kv_refs, dq_ref = refs[:classes], refs[classes]
    dkv_refs, sum_ref = refs[classes + 1 : 2 * classes + 1], refs[2 * classes + 1]

    @pl.when(pl.program_id(0) == 0)
    def _():
        sum_ref[...] = jnp.zeros_like(sum_ref)

    start = pl.program_id(0) * tile
    free, total = group_range(start, tile, class_rows, classes)
    queries = stack_heads(q_ref[...])
    grads = stack_heads(grad_ref[...])
    count = queries.shape[0]
    delta = jnp.sum(grads.astype(f32) * stack_heads(exact_ref[...]), axis=-1, keepdims=True)
    lse = jnp.concatenate([lse_ref[:, j * 128 : j * 128 + 1] for j in range(PAIRED)], axis=0)
    position = tile_positions(tile, count, start, info[0], class_rows, rows)

    def step(group, acc, masked):
        keys = held_block(kv_refs, group, slice(0, HEAD_SIZE))
        values = held_block(kv_refs, group, slice(HEAD_SIZE, 2 * HEAD_SIZE))
        bounded = jnp.tanh(dot(queries, keys, NT) * (1.0 / soft_cap))
        probs = jnp.exp(soft_cap * bounded - lse)
        if masked:
            probs = jnp.where(key_places(group, info[0], classes, rows) <= position, probs, 0.0)
        grad_probs = dot(grads, values, NT)
        grad_raw = (probs * (grad_probs - delta) * (1.0 - bounded * bounded)).astype(bf16)
        sum_ref[group, :, HEAD_SIZE:] += dot(probs.astype(bf16), grads, TN)
        sum_ref[group, :, :HEAD_SIZE] += dot(grad_raw, queries, TN)
        return acc + dot(grad_raw, keys, NN)

    acc = jnp.zeros((count, HEAD_SIZE), f32)
    acc = lax.fori_loop(0, free, functools.partial(step, masked=False), acc)
    acc = lax.fori_loop(free, total, functools.partial(step, masked=True), acc)
    for j in range(PAIRED):
        dq_ref[:, j * HEAD_SIZE : (j + 1) * HEAD_SIZE] = acc[j * tile : (j + 1) * tile].astype(bf16)

    @pl.when(pl.program_id(0) == pl.num_programs(0) - 1)
    def _():
        for h, ref in enumerate(dkv_refs):
            ref[...] = sum_ref[:, h * rows : (h + 1) * rows, :].astype(bf16)


def attn_backward(info, queries, pairs, grads, exact, lse, class_rows, rows):
    count, cols = queries.shape
    classes = len(pairs)
    groups = pairs[0].shape[0]
    length = classes * groups * rows
    tile = min(256, count)
    row_spec = pl.BlockSpec((tile, cols), lambda i, c: (i, 0))
    pair_specs = [pl.BlockSpec(p.shape, lambda i, c: (0, 0, 0)) for p in pairs]
    grid_spec = pltpu.PrefetchScalarGridSpec(
        num_scalar_prefetch=1,
        grid=(count // tile,),
        in_specs=[
            row_spec,
            row_spec,
            row_spec,
            pl.BlockSpec((tile, PAIRED * 128), lambda i, c: (i, 0)),
        ]
        + pair_specs,
        out_specs=[row_spec] + pair_specs,
        scratch_shapes=[pltpu.VMEM((groups, classes * rows, 2 * HEAD_SIZE), f32)],
    )
    return pl.pallas_call(
        functools.partial(
            attn_backward_kernel, tile=tile, class_rows=class_rows, rows=rows, classes=classes
        ),
        grid_spec=grid_spec,
        out_shape=[jax.ShapeDtypeStruct((count, cols), bf16)]
        + [jax.ShapeDtypeStruct(p.shape, bf16) for p in pairs],
        compiler_params=pltpu.CompilerParams(vmem_limit_bytes=VMEM_LIMIT),
        cost_estimate=pl.CostEstimate(
            flops=5 * count * PAIRED * length * 2 * HEAD_SIZE,
            bytes_accessed=10 * count * cols + 8 * length * HEAD_SIZE,
            transcendentals=2 * count * PAIRED * length,
        ),
        name="attn_backward",
    )(info, queries, grads, exact, lse, *pairs)


def per_device(
    tokens,
    cotangent,
    widths,
    attn_codes,
    attn_exps,
    out_exps,
    mlp_codes,
    gate_exps,
    down_exps,
    gain_attn,
    gain_post_attn,
    gain_mlp,
    gain_post_mlp,
):
    wide = lax.axis_size("wide")
    seq_size = lax.axis_size("seq")
    wide_index = lax.axis_index("wide")
    seq_index = lax.axis_index("seq")
    side = seq_index % 2
    is_low = side == 0
    members = seq_size // 2
    member = seq_index // 2
    half_wide = wide // 2
    place = ring_place(wide_index, wide)
    count, rows, model_dim = tokens.shape
    classes = wide // KEY_VALUE_HEADS
    class_rows = rows // classes
    class_index = wide_index % classes
    head_cols = PAIRED * HEAD_SIZE
    proj_cols = attn_exps.shape[0]
    half_proj = proj_cols // 2
    half_out = (attn_codes.shape[1] - proj_cols) // 2
    split_out = half_out // members
    attn_rows = attn_codes.shape[0]
    hidden = mlp_codes.shape[1]
    offsets = ring_offsets(wide)
    order = {o: i for i, o in enumerate(ring_offsets(half_wide))}
    seqs = range(count)
    seq_bits = [1 << i for i in range(seq_size.bit_length() - 1)]
    far_bits = list(reversed(seq_bits[1:]))
    clock = Clock(widths)

    def index_at(offset):
        return ring_index(jnp.mod(place + offset, wide), wide)

    places = jnp.stack([index_at(o) for o in offsets]).astype(jnp.int32)
    info = jnp.concatenate(
        [side[None].astype(jnp.int32), widths, member[None].astype(jnp.int32)]
    )
    class_info = class_index[None].astype(jnp.int32)
    column_scale = inverse_powers(attn_exps)[None, :]
    output_scale = inverse_powers(out_exps)[:, None]

    relative = [0]
    for bit in reversed(seq_bits):
        relative = relative + [r | bit for r in relative]
    pieces = jnp.stack([jnp.bitwise_xor(seq_index, r) for r in relative]).astype(jnp.int32)
    piece_rows = hidden // seq_size
    partner = jnp.bitwise_xor(wide_index, half_wide)
    gate_scale = inverse_powers(gate_exps)
    row_scale = jnp.concatenate(
        [
            lax.dynamic_slice_in_dim(
                gate_scale, block * hidden + pieces[j] * piece_rows, piece_rows, 1
            )
            for block in (wide_index, partner)
            for j in range(seq_size)
        ],
        axis=1,
    )[:, :, None]
    down_scale = inverse_powers(down_exps)[None, :]

    def columns(first, size):
        return lax.dynamic_slice_in_dim(attn_codes, first, size, 1)

    payload = jnp.concatenate(
        [
            columns(side * half_proj, half_proj),
            columns(proj_cols + side * half_out + member * split_out, split_out),
        ],
        axis=1,
    ).astype(bf16)
    piece_codes = lax.dynamic_slice_in_dim(mlp_codes, seq_index * piece_rows, piece_rows, 1)
    inputs = [tokens[s].astype(f32) for s in seqs]
    grad_out = [cotangent[s].astype(f32) for s in seqs]
    cosine, sine = rotary_rows(wide_index * rows + jnp.arange(rows))

    blocks, others = [clock.hold(payload)], []
    proj_weights = []

    def slice_more(first, last):
        return proj_slices(
            blocks[first:last],
            others[first:last],
            places[first:last],
            info,
            column_scale,
            half_proj,
            proj_weights,
            wide,
            count,
        )

    a = b = blocks[0]
    sliced = 0
    steps = half_wide
    for k in range(1, steps + 1):
        if k == steps:
            a, b = halves(a)[0], halves(b)[1]
        passed = [swap(v, "seq", 1) for v in blocks[len(others) :]]
        a, b = hop(a, b, wide)
        work = []
        if k == 1:
            work = own_slices(mlp_codes, pieces, info, row_scale, down_scale, count)
            a, b, *work = clock.sync(a, b, *passed, *work)
            passed, own_weights = work[: len(passed)], work[len(passed) :]
        elif k == 2:
            work = [piece_codes[m].astype(bf16) for m in range(3)]
            for s in seqs:
                factor = norm_factor(clock.hold(inputs[s]))
                work += [factor, (inputs[s] * factor * gain_attn).astype(bf16)]
            a, b, *work = clock.sync(a, b, *passed, *work)
            passed, work = work[: len(passed)], work[len(passed) :]
            sends, work = work[:3], work[3:]
            input_factor, normed = work[0::2], work[1::2]
        else:
            more = len(others)
            work = slice_more(sliced, more) if more > sliced else []
            a, b, *work = clock.sync(a, b, *passed, *work)
            passed, work = work[: len(passed)], work[len(passed) :]
            if work:
                proj_weights, sliced = list(work), more
        others += passed
        blocks += [a, b] if k < steps else [jnp.concatenate([a, b], axis=0)]

    def exchange(m):
        return swap(clock.hold(sends[m]), "wide", half_wide)

    def share(held, bits):
        for bit in bits:
            held = held + [swap(value, "seq", bit) for value in held]
        return held

    def partner_weights(m, held):
        scale = row_scale[m] if m < 2 else down_scale
        return partner_slices(
            held, info, scale, m == 2, own_weights[m * count : (m + 1) * count]
        )

    received = exchange(0)
    others += [swap(clock.hold(v), "seq", 1) for v in blocks[len(others) :]]
    proj_weights = slice_more(sliced, wide)
    query_send, pair_send = [], []
    for s in seqs:
        query, pair = project(normed[s], proj_weights[s], cosine, sine)
        query_send.append(query.reshape(wide, class_rows, head_cols))
        pair_send.append(pair)
    sent = clock.sync(received, *query_send, *pair_send)
    received, sent = sent[0], sent[1:]
    query_send, pair_send = sent[:count], sent[count:]

    def spread(pair):
        held = [pair]
        for _ in range(classes - 1):
            held.append(class_ring(held[-1]))
        return held[1:]

    def two_parts(value):
        cut = value.shape[0] // 2
        return value[:cut], value[cut:]

    attended_send, exact, lse, queries, pairs = [], [], [], [], []

    def attend(s):
        out, full, log_sum = attn_forward(class_info, queries[s], pairs[s], class_rows, rows)
        return [out.reshape(wide, class_rows, head_cols), full, log_sum]

    def keep_attend(work):
        attended_send.append(work[0])
        exact.append(work[1])
        lse.append(work[2])

    pair_first = heads_all_to_all(clock.hold(pair_send[0]))
    own_out = jnp.stack([clock.hold(v)[:, half_proj:] for v in blocks])
    other_out = jnp.stack([clock.hold(v)[:, half_proj:] for v in others])
    pair_first, own_out, other_out = clock.sync(pair_first, own_out, other_out)
    out_own = share([clock.hold(own_out)], far_bits)
    moved = spread(pair_first)
    pair_last, *work = clock.sync(heads_all_to_all(clock.hold(pair_send[1])), *moved)
    pairs.append([pair_first] + work)
    part_a, part_b = two_parts(pair_last)
    query = all_to_all(clock.hold(query_send[0]))
    query, *work = clock.sync(query, *spread(part_a), *out_own)
    moved_a, out_own = work[: classes - 1], work[classes - 1 :]
    queries.append(query.reshape(wide * class_rows, head_cols))
    moved_b = spread(clock.hold(part_b))
    query = all_to_all(clock.hold(query_send[1]))
    out_other = [swap(v, "seq", 1) for v in out_own[1:]]
    gate_held = share([clock.hold(received)], far_bits)
    query, *work = clock.sync(query, *moved_b, *out_other, *attend(0))
    moved_b, work = work[: classes - 1], work[classes - 1 :]
    out_other, work = [other_out] + work[: len(out_other)], work[len(out_other) :]
    keep_attend(work)
    queries.append(query.reshape(wide * class_rows, head_cols))
    pairs.append(
        [pair_last] + [jnp.concatenate([x, y], axis=0) for x, y in zip(moved_a, moved_b)]
    )

    attended, branch, branch_factor, middle, middle_factor, normed_mlp = [], [], [], [], [], []

    def heads_to_rows(values):
        split = values.reshape(KEY_VALUE_HEADS, rows, head_cols)
        return jnp.transpose(split, (1, 0, 2)).reshape(rows, KEY_VALUE_HEADS * head_cols)

    def join(s):
        value = dot(attended[s], out_weights[s], NT)
        factor = norm_factor(value)
        mid = inputs[s] + value * factor * gain_post_attn
        mid_factor = norm_factor(mid)
        return [value, factor, mid, mid_factor, (mid * mid_factor * gain_mlp).astype(bf16)]

    def keep_join(work):
        for held, value in zip((branch, branch_factor, middle, middle_factor, normed_mlp), work):
            held.append(value)

    for s in seqs:
        back = all_to_all(clock.hold(attended_send[s]))
        if s == 0:
            out_weights = out_slices(out_own, out_other, places, info, output_scale, count)
            back, *work = clock.sync(back, *gate_held, *out_weights, *attend(count - 1))
            gate_held, work = work[: len(gate_held)], work[len(gate_held) :]
            out_weights, work = work[:count], work[count:]
            keep_attend(work)
        else:
            gate_held = share(gate_held, seq_bits[:1])
            back, *work = clock.sync(back, *gate_held, *join(s - 1))
            gate_held, work = work[: len(gate_held)], work[len(gate_held) :]
            keep_join(work)
        attended.append(heads_to_rows(back))

    received = exchange(1)
    gate_weights = partner_weights(0, [clock.hold(v) for v in gate_held])
    received, *work = clock.sync(received, *gate_weights, *join(count - 1))
    gate_weights, work = work[:count], work[count:]
    keep_join(work)

    def blocks_of(part):
        return lambda o: part[order[o] * rows : (order[o] + 1) * rows]

    gathered, gate, up, hidden_rows, mixed, parts = [], [], [], [], [], []

    def open_part(s, part, held=()):
        group = clock.hold(gathered[s])
        return open_forward(group, gate_weights[s], up_weights[s], part, held)

    def keep_open(work):
        gate.append(work[0])
        up.append(work[1])
        hidden_rows.append(work[2])

    def mix(s):
        return dot(clock.hold(hidden_rows[s]), down_weights[s], NN).astype(bf16)

    up_held = share([clock.hold(received)], far_bits)
    received, *up_held = clock.sync(exchange(2), *up_held)

    def beside_first(step):
        nonlocal up_held
        if step == 0:
            up_held = share(up_held, seq_bits[:1])
            return tuple(up_held) + tuple(share([clock.hold(received)], far_bits))
        if step == 1:
            return tuple(partner_weights(1, [clock.hold(v) for v in up_held]))
        return ()

    a = b = clock.hold(normed_mlp[0])
    blocks = [a]
    for k in range(1, half_wide // 2 + 1):
        if k == half_wide // 2:
            a, b = halves(a)[0], halves(b)[1]
        if k == 2:
            down_held = share(down_held, seq_bits[:1])
        work = beside_first(k - 1) + (tuple(down_held) if k == 2 else ())
        a, b = hop(a, b, half_wide)
        a, b, *work = clock.sync(a, b, *work)
        if k == 1:
            up_held, down_held = work[: len(up_held)], work[len(up_held) :]
        elif k == 2:
            up_weights, down_held = work[:count], work[count:]
        blocks += [a, b]
    gathered.append(jnp.concatenate(blocks, axis=0))

    def beside_second(step):
        if step == 0:
            return open_part(0, None)
        if step == 1:
            return partner_weights(2, [clock.hold(v) for v in down_held])
        return ()

    a = b = clock.hold(normed_mlp[1])
    blocks = [a]
    for k in range(1, half_wide // 2 + 1):
        if k == half_wide // 2:
            a, b = halves(a)[0], halves(b)[1]
        work = beside_second(k - 1)
        a, b = hop(a, b, half_wide)
        a, b, *work = clock.sync(a, b, *work)
        if k == 1:
            keep_open(work)
        elif k == 2:
            down_weights = work
        blocks += [a, b]
    gathered.append(jnp.concatenate(blocks, axis=0))
    parts.append(clock.sync(mix(0))[0])

    layer_out, grad_mixed, gain_fourth = [], [], 0.0

    def finish(s):
        nonlocal gain_fourth
        factor = norm_factor(mixed[s])
        layer_out.append((middle[s] + mixed[s] * factor * gain_post_mlp).astype(bf16))
        grad, gain = norm_back(mixed[s], factor, gain_post_mlp, grad_out[s])
        grad_mixed.append(grad.astype(bf16))
        gain_fourth = gain_fourth + gain

    grad_group, grad_gate, grad_up, grad_parts, grad_normed_mlp = [], [], [], [], []

    def back_hidden(s, part, held=()):
        group = clock.hold(grad_group[s])
        return open_back(group, down_weights[s], gate[s], up[s], part, held)

    def back_input(s, part, held=()):
        grad = clock.hold(grad_gate[s])
        return input_back(grad, grad_up[s], gate_weights[s], up_weights[s], part, held)

    def keep_back(work):
        grad_gate.append(work[0])
        grad_up.append(work[1])

    def first_sum(part):
        a, b = hop(*halves(clock.hold(blocks_of(part)(half_wide // 2))), half_wide)
        return a, b

    def rest_sum(part, a, b, beside=lambda step: ()):
        part_of = blocks_of(part)
        other = []
        for k in range(half_wide // 2 - 1, 0, -1):
            if k == half_wide // 2 - 1:
                a = add_first(part_of(k), a)
                b = add_last(part_of(-k), b)
            else:
                a = low_sum(part_of(k), a)
                b = low_sum(part_of(-k), b)
            work = beside(half_wide // 2 - 1 - k)
            a, b = hop(a, b, half_wide)
            a, b, *work = clock.sync(a, b, *work)
            other.append(work)
        return part_of(0).astype(f32) + a.astype(f32) + b.astype(f32), other

    a, b = first_sum(parts[0])
    a, b, *opened = clock.sync(a, b, *open_part(1, 0))
    total, work = rest_sum(
        parts[0], a, b, lambda step: () if step else tuple(open_part(1, 1, opened))
    )
    keep_open(work[0])
    mixed.append(total)
    finish(0)
    parts.append(mix(1))
    blocks, work = ring_gather(
        clock, grad_mixed[0], half_wide, lambda k: (parts[1],) if k == 0 else ()
    )
    parts[1] = work[0][0]
    grad_group.append(jnp.concatenate(blocks, axis=0))
    a, b = first_sum(parts[1])
    a, b, *opened = clock.sync(a, b, *back_hidden(0, 0))

    def beside_last(step):
        if step:
            return ()
        keep_back(back_hidden(0, 1, opened))
        return (grad_gate[0], grad_up[0], *input_back(
            grad_gate[0], grad_up[0], gate_weights[0], up_weights[0], 0, ()
        ))

    total, work = rest_sum(parts[1], a, b, beside_last)
    grad_gate[0], grad_up[0], opened = work[0][0], work[0][1], work[0][2:]
    mixed.append(total)
    finish(1)
    blocks, work = ring_gather(
        clock, grad_mixed[1], half_wide, lambda k: () if k else tuple(back_input(0, 1, opened))
    )
    grad_parts.append(work[0][0])
    grad_group.append(jnp.concatenate(blocks, axis=0))

    def weight_sum(lefts, rights):
        lefts = [clock.hold(v) for v in lefts]
        return weight_back(lefts, rights).reshape(2, hidden, model_dim)

    def part_sum(grad, bit):
        split = grad.reshape(2, 2, grad.shape[1] // 2, model_dim)
        return low_sum(split[:, 0], swap(split[:, 1], "seq", bit))

    grad_middle, grad_branch, grad_send = [], [], []
    gain_third = gain_second = 0.0

    def back_branch(s):
        nonlocal gain_third, gain_second
        grad, gain = norm_back(middle[s], middle_factor[s], gain_mlp, grad_normed_mlp[s])
        gain_third = gain_third + gain
        grad_mid = grad_out[s] + grad
        grad, gain = norm_back(branch[s], branch_factor[s], gain_post_attn, grad_mid)
        gain_second = gain_second + gain
        grad = grad.astype(bf16)
        send = dot(grad, out_weights[s], NN).astype(bf16)
        send = jnp.transpose(send.reshape(rows, KEY_VALUE_HEADS, head_cols), (1, 0, 2))
        return [grad_mid, grad, send.reshape(wide, class_rows, head_cols)]

    def keep_branch(work):
        grad_middle.append(work[0])
        grad_branch.append(work[1])
        grad_send.append(work[2])

    a, b = first_sum(grad_parts[0])
    a, b, *opened = clock.sync(a, b, *back_hidden(1, 0))

    def beside_back(step):
        if step:
            return ()
        keep_back(back_hidden(1, 1, opened))
        return (grad_gate[1], grad_up[1], *input_back(
            grad_gate[1], grad_up[1], gate_weights[1], up_weights[1], 0, ()
        ))

    total, work = rest_sum(grad_parts[0], a, b, beside_back)
    grad_gate[1], grad_up[1], opened = work[0][0], work[0][1], work[0][2:]
    grad_normed_mlp.append(total)
    grad_parts += clock.sync(*back_input(1, 1, opened))
    a, b = first_sum(grad_parts[1])
    a, b, *work = clock.sync(a, b, *back_branch(0))
    keep_branch(work)
    total, work = rest_sum(
        grad_parts[1],
        a,
        b,
        lambda step: () if step else (weight_sum(hidden_rows, grad_group),),
    )
    down_grad = work[0][0]
    grad_normed_mlp.append(total)

    def attend_back(s):
        dq, *dkv = attn_backward(
            class_info,
            queries[s],
            pairs[s],
            clock.hold(grad_heads[s]),
            exact[s],
            lse[s],
            class_rows,
            rows,
        )
        return [dq.reshape(wide, class_rows, head_cols)] + dkv

    def class_sum(dkv):
        total = dkv[1 % classes]
        for step in range(2, classes + 1):
            total = low_sum(dkv[step % classes], class_ring(total))
        return total

    def far_parts(grad):
        split = grad.reshape(2, 2, grad.shape[1] // 2, model_dim)
        send = split[:, 1]
        return split[:, 0], [send[:, :, : model_dim // 2], send[:, :, model_dim // 2 :]]

    def far_move(part):
        return swap(clock.hold(part), "seq", seq_bits[1])

    def far_join(kept, moved):
        grad = low_sum(kept, jnp.concatenate(moved, axis=2))
        for bit in seq_bits[2:]:
            grad = part_sum(grad, bit)
        return grad

    grad_heads, grad_attend = [], []
    query_back, pair_back = [], []

    def heads_of(value):
        return value.reshape(wide * class_rows, head_cols)

    back = all_to_all(clock.hold(grad_send[0]))
    down_grad = part_sum(down_grad, 1)
    back, down_grad, *work = clock.sync(back, down_grad, *back_branch(1))
    keep_branch(work)
    grad_heads.append(heads_of(back))
    all_normed = jnp.concatenate(normed, axis=0)
    all_attended = jnp.concatenate(attended, axis=0)
    all_branch = jnp.concatenate(grad_branch, axis=0)

    def half_dot(left, right, which, size):
        return dot(left, lax.dynamic_slice_in_dim(right, which * size, size, 1), TN)

    down_keep, down_parts = far_parts(down_grad)
    down_moved = [far_move(down_parts[0])]
    back = all_to_all(clock.hold(grad_send[1]))
    out_send = half_dot(all_branch, clock.hold(all_attended), 1 - side, half_out).astype(bf16)
    back, down_moved[0], out_send, *work = clock.sync(
        back, down_moved[0], out_send, *attend_back(0)
    )
    down_moved.append(far_move(down_parts[1]))
    grad_heads.append(heads_of(back))
    grad_attend.append(work)

    dq, *dkv = grad_attend[0]
    parts_of_pair = [two_parts(v) for v in dkv]
    out_sent = swap(out_send, "seq", 1)
    query = all_to_all(clock.hold(dq))
    pair_a = class_sum([v[0] for v in parts_of_pair])
    query, pair_a, down_moved[1], out_sent, *work = clock.sync(
        query, pair_a, down_moved[1], out_sent, *attend_back(1)
    )
    down_grad = far_join(down_keep, down_moved)
    query_back.append(query)
    grad_attend.append(work)
    dq, *dkv = grad_attend[1]
    query = all_to_all(clock.hold(dq))
    pair_b = class_sum([clock.hold(v[1]) for v in parts_of_pair])
    out_part = low_sum(
        half_dot(all_branch, clock.hold(all_attended), side, half_out), out_sent
    )
    query, pair_b, down_grad, out_part = clock.sync(query, pair_b, down_grad, out_part)
    query_back.append(query)
    out_pieces = {
        t: lax.dynamic_slice_in_dim(out_part, jnp.bitwise_xor(member, t) * split_out, split_out, 1)
        for t in range(members)
    }
    out_parts = None
    if members == 2:
        out_parts = [out_pieces[1][:, : split_out // 2], out_pieces[1][:, split_out // 2 :]]
    else:
        for bit in seq_bits[1:]:
            for t in sorted(out_pieces):
                if not t & (bit // 2) and t | (bit // 2) in out_pieces:
                    out_pieces[t] = low_sum(
                        out_pieces[t], swap(out_pieces.pop(t | (bit // 2)), "seq", bit)
                    )

    def out_move(part):
        return [swap(clock.hold(out_parts[part]), "seq", seq_bits[1])] if out_parts else []

    pair = heads_all_to_all(clock.hold(jnp.concatenate([pair_a, pair_b], axis=0)))
    pair_sum = class_sum([clock.hold(v) for v in dkv])
    pair, pair_sum, *out_moved = clock.sync(pair, pair_sum, *out_move(0))
    pair_back.append(pair)
    out_moved += out_move(1)
    pair = heads_all_to_all(clock.hold(pair_sum))
    up_grad = weight_sum(grad_up, gathered)
    pair, up_grad, *out_moved = clock.sync(pair, up_grad, *out_moved)
    pair_back.append(pair)
    out_piece = out_pieces[0]
    if out_moved:
        out_piece = low_sum(out_piece, jnp.concatenate(out_moved, axis=1))

    def column_parts(value, count):
        width = value.shape[1] // count
        return [value[:, i * width : (i + 1) * width] for i in range(count)]

    def exchange_grad(part):
        return swap(clock.hold(part), "wide", half_wide)

    def half_sum(grad):
        split = grad.reshape(2, 2, grad.shape[1] // 2, model_dim)
        return split[:, 0], split[:, 1]

    down_own = column_parts(down_grad[0], 3)
    down_send = column_parts(down_grad[1], 3)
    up_keep, up_send = half_sum(up_grad)
    up_moved = swap(up_send, "seq", 1)
    moved, grad_proj = clock.sync(
        exchange_grad(down_send[0]),
        turn_back(
            [v.reshape(KEY_VALUE_HEADS, rows, head_cols) for v in query_back],
            pair_back,
            cosine,
            sine,
        ),
    )
    down_other = [moved]
    moved = exchange_grad(down_send[1])
    proj_send = half_dot(all_normed, clock.hold(grad_proj), 1 - side, half_proj).astype(bf16)
    moved, up_moved, proj_send = clock.sync(moved, up_moved, proj_send)
    down_other.append(moved)
    moved = exchange_grad(down_send[2])
    proj_sent = swap(proj_send, "seq", 1)
    up_grad = low_sum(up_keep, up_moved)
    moved, proj_sent, up_grad = clock.sync(moved, proj_sent, up_grad)
    down_other.append(moved)
    up_keep, up_parts = far_parts(up_grad)
    down_grad = [low_sum(x, y) for x, y in zip(down_own, down_other)]
    far_down = [swap(clock.hold(v), "seq", far_bits[0]) for v in down_grad]
    proj_part = low_sum(half_dot(all_normed, clock.hold(grad_proj), side, half_proj), proj_sent)
    (proj_part,) = clock.sync(proj_part)
    def part_of(o):
        first = index_at(o) * attn_rows
        return jnp.concatenate(
            [
                lax.dynamic_slice_in_dim(proj_part, first, attn_rows, 0),
                lax.dynamic_slice_in_dim(out_piece, first, attn_rows, 0),
            ],
            axis=1,
        )

    def spread_grad(grads, bits):
        for bit in bits:
            grads = [jnp.concatenate([g, swap(g, "seq", bit)], axis=0) for g in grads]
        return grads

    a, b = halves(clock.hold(part_of(wide // 2)))
    up_moved = []
    for k in range(wide // 2 - 1, -1, -1):
        step = wide // 2 - 1 - k
        a, b = hop(a, b, wide)
        work = []
        if step == 0:
            work = far_down
        elif step == 1:
            work = [far_move(up_parts[0]), weight_sum(grad_gate, gathered)]
        elif step == 2:
            gate_keep, gate_send = half_sum(gate_grad)
            work = [far_move(up_parts[1]), swap(clock.hold(gate_send), "seq", 1)]
        elif step == half_wide - 1:
            gate_keep, gate_parts = far_parts(low_sum(gate_keep, gate_moved))
            work = [far_move(gate_parts[0])]
        a, b, *work = clock.sync(a, b, *work)
        if step == 0:
            down_grad = [jnp.concatenate(v, axis=0) for v in zip(down_grad, work)]
            down_grad = spread_grad(down_grad, far_bits[1:])
        elif step == 1:
            up_moved.append(work[0])
            gate_grad = work[1]
        elif step == 2:
            up_moved.append(work[0])
            gate_moved = work[1]
        elif step == half_wide - 1:
            gate_moved = work
        if step == 0:
            a, b = add_first(part_of(k), a), add_last(part_of(-k), b)
        elif k > 0:
            a, b = low_sum(part_of(k), a), low_sum(part_of(-k), b)
    total = low_sum(part_of(0), a, b)
    up_grad = far_join(up_keep, up_moved)
    up_own, up_send = column_parts(up_grad[0], 2), column_parts(up_grad[1], 2)
    total, *up_send = clock.sync(total, *up_send)

    def input_grad(s):
        return dot(clock.hold(grad_proj[s * rows : (s + 1) * rows]), proj_weights[s], NT)

    def back_tokens(s, grad_normed):
        grad, gain = norm_back(inputs[s], input_factor[s], gain_attn, grad_normed)
        return (grad_middle[s] + grad).astype(bf16), gain

    def add_swapped(gains, axis, bits):
        for bit in bits:
            gains = gains + swap(gains, axis, bit)
        return gains

    moved, grad_first, last = clock.sync(
        exchange_grad(up_send[0]), input_grad(0), far_move(gate_parts[1])
    )
    gate_grad = far_join(gate_keep, gate_moved + [last])
    up_grad = [low_sum(up_own[0], moved)]
    proj_total = total[:, :half_proj]
    out_totals = {0: total[:, half_proj:]}
    for bit in seq_bits[1:]:
        sent = jnp.concatenate([proj_total] + [out_totals[t] for t in sorted(out_totals)], axis=1)
        moved = swap(clock.hold(sent), "seq", bit)
        proj_total = low_sum(proj_total, moved[:, :half_proj])
        for i, t in enumerate(sorted(out_totals)):
            first = half_proj + i * split_out
            out_totals[t | (bit // 2)] = moved[:, first : first + split_out]
    out_totals = jnp.stack([out_totals[t] for t in range(members)])
    low = jnp.concatenate(
        [proj_total]
        + [
            lax.dynamic_index_in_dim(out_totals, jnp.bitwise_xor(member, j), 0, keepdims=False)
            for j in range(members)
        ],
        axis=1,
    )
    moved, low, grad_last = clock.sync(exchange_grad(up_send[1]), low, input_grad(1))
    up_grad.append(low_sum(up_own[1], moved))
    gate_own, gate_send = column_parts(gate_grad[0], 2), column_parts(gate_grad[1], 2)
    first_tokens, gain_first = back_tokens(0, grad_first)
    last_tokens, gain = back_tokens(1, grad_last)
    gains = jnp.stack([gain_first + gain, gain_second, gain_third, gain_fourth])
    wide_bits = [1 << i for i in range(wide.bit_length() - 1)]
    gains, *gate_send = clock.sync(add_swapped(gains, "wide", wide_bits[1:]), *gate_send)
    moved = exchange_grad(gate_send[0])
    up_grad = spread_grad([clock.hold(v) for v in up_grad], far_bits)
    other = swap(clock.hold(low), "seq", 1)
    down_grad = spread_grad([clock.hold(v) for v in down_grad], seq_bits[:1])
    mlp_grad = unpack(down_grad, pieces, 2, [])
    moved, other, mlp_grad, *up_grad = clock.sync(moved, other, mlp_grad, *up_grad)
    gate_grad = [low_sum(gate_own[0], moved)]
    moved = exchange_grad(gate_send[1])
    gate_grad = spread_grad([clock.hold(v) for v in gate_grad], far_bits)
    left, right = jnp.where(is_low, low, other), jnp.where(is_low, other, low)
    attn_grad = jnp.concatenate(
        [left[:, :half_proj], right[:, :half_proj], left[:, half_proj:], right[:, half_proj:]],
        axis=1,
    ).astype(f32)
    up_grad = spread_grad([clock.hold(v) for v in up_grad], seq_bits[:1])
    mlp_grad = unpack(up_grad, pieces, 1, [mlp_grad])
    moved, attn_grad, mlp_grad, *gate_grad = clock.sync(moved, attn_grad, mlp_grad, *gate_grad)
    last = spread_grad([low_sum(gate_own[1], moved)], far_bits)
    gate_grad = spread_grad([clock.hold(v) for v in gate_grad], seq_bits[:1])
    gains = add_swapped(clock.hold(gains), "wide", wide_bits[:1])
    gains = add_swapped(add_swapped(gains, "seq", seq_bits[:1]), "seq", seq_bits[1:])
    mlp_grad, gains, *gate_grad = clock.sync(mlp_grad, gains, *gate_grad, *last)
    gate_grad[1:] = spread_grad(gate_grad[1:], seq_bits[:1])
    mlp_grad = unpack(gate_grad, pieces, 0, [mlp_grad])
    grad_tokens = [first_tokens, last_tokens]
    return (
        jnp.stack(layer_out),
        jnp.stack(grad_tokens),
        attn_grad,
        mlp_grad,
        gains[0],
        gains[1],
        gains[2],
        gains[3],
    )


def solution(mesh):
    placed = (
        P("seq", "wide", None),
        P("seq", "wide", None),
        P("seq"),
        P("wide", None),
        P(),
        P(),
        P(None, "wide", None),
        P(),
        P(),
        P(),
        P(),
        P(),
        P(),
    )
    return jax.shard_map(
        per_device,
        mesh=mesh,
        in_specs=placed,
        out_specs=(
            P("seq", "wide", None),
            P("seq", "wide", None),
            P("wide", None),
            P(None, "wide", None),
            P(),
            P(),
            P(),
            P(),
        ),
        check_vma=False,
    )
```

```python
import functools
import math

import jax
import jax.numpy as jnp
from jax import lax
from jax.experimental import pallas as pl
from jax.experimental.pallas import tpu as pltpu
from jax.sharding import PartitionSpec as P

QUERY_HEADS = 8
KEY_VALUE_HEADS = 4
HEAD_SIZE = 256
PAIRED = QUERY_HEADS // KEY_VALUE_HEADS

eps_norm = 1e-06
soft_cap = 50.0
rope_base = 10000.0
gelu_coeff = math.sqrt(2.0 / math.pi)
f32 = jnp.float32
bf16 = jnp.bfloat16
VMEM_LIMIT = 56 * 1024 * 1024


def dot(a, b, dims):
    return lax.dot_general(a, b, (dims, ((), ())), preferred_element_type=f32)


NN = ((1,), (0,))
NT = ((1,), (1,))
TN = ((0,), (0,))


def inverse_powers(exponents):
    return 1.0 / jnp.left_shift(jnp.ones_like(exponents), exponents).astype(f32)


def norm_factor(values):
    return lax.rsqrt(jnp.mean(values * values, axis=-1, keepdims=True) + eps_norm)


def norm_back(values, factor, gain, grad):
    scaled = grad * gain
    inner = jnp.mean(values * scaled, axis=-1, keepdims=True)
    grad_values = factor * scaled - values * (factor * factor * factor * inner)
    return grad_values, jnp.sum(grad * values * factor, axis=0, keepdims=True)


def gelu_parts(values):
    inner = gelu_coeff * (values + 0.044715 * values * values * values)
    return jnp.tanh(inner)


def rotary_rows(positions):
    half_dim = HEAD_SIZE // 2
    frequency = jnp.exp(
        jnp.arange(half_dim, dtype=f32) * (-2.0 * math.log(rope_base) / HEAD_SIZE)
    )
    angles = positions.astype(f32)[:, None] * frequency[None, :]
    return jnp.cos(angles), jnp.sin(angles)


def ring_place(index, size):
    return jnp.where(index % 2 == 0, index // 2, size - 1 - index // 2)


def ring_index(place, size):
    return jnp.where(place < size // 2, 2 * place, 2 * (size - 1 - place) + 1)


def ring_perms(size):
    order = list(range(0, size, 2)) + list(range(size - 1, 0, -2))
    up = [
        (base + order[i], base + order[(i + 1) % size])
        for base in range(0, lax.axis_size("wide"), size)
        for i in range(size)
    ]
    return up, [(b, a) for a, b in up]


def ring_offsets(size):
    out = [0]
    for k in range(1, size // 2):
        out += [-k, k]
    return out + [size // 2]


class Clock:
    def __init__(self, token):
        self.token = token

    def sync(self, *arrays):
        *arrays, self.token = lax.optimization_barrier(tuple(arrays) + (self.token,))
        return arrays

    def hold(self, value):
        return lax.optimization_barrier((value, self.token))[0]


def hop(a, b, size):
    up, down = ring_perms(size)
    return lax.ppermute(a, "wide", up), lax.ppermute(b, "wide", down)


def low_sum(*terms):
    return sum(t.astype(f32) for t in terms).astype(bf16)


def halves(value):
    half = value.shape[0] // 2
    return value[:half], value[half:]


def add_first(whole, part):
    count = part.shape[0]
    return jnp.concatenate([low_sum(whole[:count], part), whole[count:].astype(bf16)], axis=0)


def add_last(whole, part):
    count = whole.shape[0] - part.shape[0]
    return jnp.concatenate([whole[:count].astype(bf16), low_sum(whole[count:], part)], axis=0)


def ring_gather(clock, value, size, beside=lambda step: ()):
    a = b = clock.hold(value)
    out, other = [a], []
    for k in range(1, size // 2 + 1):
        if k == size // 2:
            a, b = halves(a)[0], halves(b)[1]
        work = beside(k - 1)
        a, b = hop(a, b, size)
        a, b, *work = clock.sync(a, b, *work)
        out += [a, b]
        other.append(work)
    return out, other


def ring_scatter(clock, part_of, rows, size, beside=lambda step: ()):
    a, b = halves(clock.hold(part_of(size // 2).astype(bf16)))
    other = []
    for k in range(size // 2 - 1, -1, -1):
        work = beside(size // 2 - 1 - k)
        a, b = hop(a, b, size)
        a, b, *work = clock.sync(a, b, *work)
        other.append(work)
        if k == size // 2 - 1 and k > 0:
            a = add_first(part_of(k), a)
            b = add_last(part_of(-k), b)
        elif k > 0:
            a = low_sum(part_of(k), a)
            b = low_sum(part_of(-k), b)
    return part_of(0).astype(f32) + a.astype(f32) + b.astype(f32), other


def swap(value, axis, bit):
    size = lax.axis_size(axis)
    return lax.ppermute(value, axis, [(i, i ^ bit) for i in range(size)])


def all_to_all(value):
    return lax.all_to_all(value, "wide", split_axis=0, concat_axis=0, tiled=True)


def heads_all_to_all(value):
    size = lax.axis_size("wide")
    classes = size // KEY_VALUE_HEADS
    groups = [list(range(c, size, classes)) for c in range(classes)]
    return lax.all_to_all(
        value, "wide", split_axis=0, concat_axis=0, axis_index_groups=groups, tiled=True
    )


def class_ring(value):
    size = lax.axis_size("wide")
    classes = size // KEY_VALUE_HEADS
    perm = [(i, i // classes * classes + (i + 1) % classes) for i in range(size)]
    return lax.ppermute(value, "wide", perm)


def slice_values(codes, width):
    lift = jnp.where(width == 0, 0.0, 0.5).astype(bf16)
    large = jnp.where(width == 0, 0.0, jnp.where(width == 1, 1.5 * 2**11, 1.5 * 2**13)).astype(bf16)
    top = jnp.where(width == 0, 127.0, jnp.where(width == 1, 112.0, 64.0)).astype(bf16)
    return jnp.minimum(((codes + lift) + large) - large, top)


def proj_slice_kernel(places, info, *refs, blocks, count):
    code_refs, scale_ref, out_refs = refs[: 2 * blocks], refs[2 * blocks], refs[len(refs) - count :]
    mine = pl.program_id(1) == info[0]

    def write(code_ref):
        codes = code_ref[...]
        scale = scale_ref[...].astype(bf16)
        for s, out_ref in enumerate(out_refs):
            out_ref[...] = slice_values(codes, info[1 + s]) * scale

    for k in range(blocks):
        here = pl.program_id(0) == k
        pl.when(jnp.logical_and(here, mine))(functools.partial(write, code_refs[2 * k]))
        pl.when(jnp.logical_and(here, jnp.logical_not(mine)))(
            functools.partial(write, code_refs[2 * k + 1])
        )


def proj_slices(own, other, places, info, scale, width, weights, total, count):
    blocks = len(own)
    rows = own[0].shape[0]
    inputs = [block for pair in zip(own, other) for block in pair] + [scale]
    grid_spec = pltpu.PrefetchScalarGridSpec(
        num_scalar_prefetch=2,
        grid=(blocks, 2),
        in_specs=[pl.BlockSpec((rows, width), lambda k, j, p, i: (0, 0))] * (2 * blocks)
        + [pl.BlockSpec((1, width), lambda k, j, p, i: (0, j))]
        + [pl.BlockSpec(memory_space=pl.ANY)] * len(weights),
        out_specs=[pl.BlockSpec((rows, width), lambda k, j, p, i: (p[k], j))] * count,
    )
    return pl.pallas_call(
        functools.partial(proj_slice_kernel, blocks=blocks, count=count),
        grid_spec=grid_spec,
        out_shape=[jax.ShapeDtypeStruct((total * rows, 2 * width), bf16)] * count,
        input_output_aliases={2 + len(inputs) + s: s for s in range(len(weights))},
        compiler_params=pltpu.CompilerParams(vmem_limit_bytes=VMEM_LIMIT),
        cost_estimate=pl.CostEstimate(
            flops=20 * count * blocks * rows * width,
            bytes_accessed=4 * blocks * rows * width * (1 + count),
            transcendentals=0,
        ),
        name="proj_slices",
    )(places, info, *inputs, *weights)


def out_slice_kernel(places, info, *refs, split, count):
    inputs, scale_ref, out_refs = refs[: -1 - count], refs[-1 - count], refs[-count:]
    members = len(inputs) // 2
    member = info[1 + count]
    mine = pl.program_id(1) == info[0]

    def write(code_refs):
        scale = scale_ref[...].astype(bf16)
        for t, code_ref in enumerate(code_refs):
            first = pl.multiple_of(jnp.bitwise_xor(member, t) * split, 128)
            for s, out_ref in enumerate(out_refs):
                out_ref[:, pl.ds(first, split)] = slice_values(code_ref[0], info[1 + s]) * scale

    pl.when(mine)(lambda: write(inputs[:members]))
    pl.when(jnp.logical_not(mine))(lambda: write(inputs[members:]))


def out_slices(own, other, places, info, scale, count):
    blocks, rows, split = own[0].shape
    width = split * len(own)
    inputs = list(own) + list(other)
    grid_spec = pltpu.PrefetchScalarGridSpec(
        num_scalar_prefetch=2,
        grid=(blocks, 2),
        in_specs=[pl.BlockSpec((1, rows, split), lambda k, j, p, i: (k, 0, 0))] * len(inputs)
        + [pl.BlockSpec((rows, 1), lambda k, j, p, i: (p[k], 0))],
        out_specs=[pl.BlockSpec((rows, width), lambda k, j, p, i: (p[k], j))] * count,
    )
    return pl.pallas_call(
        functools.partial(out_slice_kernel, split=split, count=count),
        grid_spec=grid_spec,
        out_shape=[jax.ShapeDtypeStruct((blocks * rows, 2 * width), bf16)] * count,
        compiler_params=pltpu.CompilerParams(vmem_limit_bytes=VMEM_LIMIT),
        cost_estimate=pl.CostEstimate(
            flops=20 * count * blocks * rows * width,
            bytes_accessed=4 * blocks * rows * width * (1 + count),
            transcendentals=0,
        ),
        name="out_slices",
    )(places, info, *inputs, scale)


def own_slice_kernel(pieces, info, code_ref, row_ref, col_ref, *out_refs):
    count = len(out_refs) // 3
    for m in range(3):
        codes = code_ref[m].astype(f32).astype(bf16)
        scale = (row_ref[m] if m < 2 else col_ref[...]).astype(bf16)
        for s in range(count):
            out_refs[m * count + s][...] = slice_values(codes, info[1 + s]) * scale


def own_slices(codes, pieces, info, row_scale, col_scale, count):
    three, rows, cols = codes.shape
    steps = pieces.shape[0]
    piece = rows // steps
    grid_spec = pltpu.PrefetchScalarGridSpec(
        num_scalar_prefetch=2,
        grid=(steps,),
        in_specs=[
            pl.BlockSpec((three, piece, cols), lambda j, p, i: (0, p[j], 0)),
            pl.BlockSpec((2, piece, 1), lambda j, p, i: (0, j, 0)),
            pl.BlockSpec((1, cols), lambda j, p, i: (0, 0)),
        ],
        out_specs=[pl.BlockSpec((piece, cols), lambda j, p, i: (j, 0))] * (three * count),
    )
    return pl.pallas_call(
        own_slice_kernel,
        grid_spec=grid_spec,
        out_shape=[jax.ShapeDtypeStruct((2 * rows, cols), bf16)] * (three * count),
        compiler_params=pltpu.CompilerParams(vmem_limit_bytes=VMEM_LIMIT),
        cost_estimate=pl.CostEstimate(
            flops=10 * count * codes.size,
            bytes_accessed=codes.size * (4 + 2 * count),
            transcendentals=0,
        ),
        name="own_slices",
    )(pieces, info, codes, row_scale, col_scale)


def partner_slice_kernel(info, *refs, steps, count):
    piece_refs, scale_ref, out_refs = refs[:steps], refs[steps], refs[steps + 1 + count :]
    for j in range(steps):

        @pl.when(pl.program_id(0) == j)
        def _():
            codes = piece_refs[j][...]
            scale = scale_ref[...].astype(bf16)
            for s, out_ref in enumerate(out_refs):
                out_ref[...] = slice_values(codes, info[1 + s]) * scale


def partner_slices(pieces, info, scale, by_column, weights):
    steps = len(pieces)
    count = len(weights)
    piece, cols = pieces[0].shape
    if by_column:
        scale_spec = pl.BlockSpec((1, cols), lambda j, i: (0, 0))
    else:
        scale_spec = pl.BlockSpec((piece, 1), lambda j, i: (steps + j, 0))
    grid_spec = pltpu.PrefetchScalarGridSpec(
        num_scalar_prefetch=1,
        grid=(steps,),
        in_specs=[pl.BlockSpec((piece, cols), lambda j, i: (0, 0))] * steps
        + [scale_spec]
        + [pl.BlockSpec(memory_space=pl.ANY)] * count,
        out_specs=[pl.BlockSpec((piece, cols), lambda j, i: (steps + j, 0))] * count,
    )
    return pl.pallas_call(
        functools.partial(partner_slice_kernel, steps=steps, count=count),
        grid_spec=grid_spec,
        out_shape=[jax.ShapeDtypeStruct(w.shape, bf16) for w in weights],
        input_output_aliases={2 + steps + s: s for s in range(count)},
        compiler_params=pltpu.CompilerParams(vmem_limit_bytes=VMEM_LIMIT),
        cost_estimate=pl.CostEstimate(
            flops=10 * count * steps * piece * cols,
            bytes_accessed=2 * (1 + count) * steps * piece * cols,
            transcendentals=0,
        ),
        name="partner_slices",
    )(info, *pieces, scale, *weights)


def unpack_kernel(pieces, *refs, parts):
    first = 0
    for ref in refs[:parts]:
        width = ref.shape[1]
        refs[-1][0, :, first : first + width] = ref[...].astype(f32)
        first += width


def unpack(grads, pieces, matrix, held):
    steps = pieces.shape[0]
    rows = grads[0].shape[0]
    cols = sum(g.shape[1] for g in grads)
    piece = rows // steps
    grid_spec = pltpu.PrefetchScalarGridSpec(
        num_scalar_prefetch=1,
        grid=(steps,),
        in_specs=[pl.BlockSpec((piece, g.shape[1]), lambda j, p: (j, 0)) for g in grads]
        + [pl.BlockSpec(memory_space=pl.ANY)] * len(held),
        out_specs=pl.BlockSpec((1, piece, cols), lambda j, p: (matrix, p[j], 0)),
    )
    return pl.pallas_call(
        functools.partial(unpack_kernel, parts=len(grads)),
        grid_spec=grid_spec,
        out_shape=jax.ShapeDtypeStruct((3, rows, cols), f32),
        input_output_aliases={1 + len(grads): 0} if held else {},
        compiler_params=pltpu.CompilerParams(vmem_limit_bytes=VMEM_LIMIT),
        cost_estimate=pl.CostEstimate(
            flops=rows * cols, bytes_accessed=6 * rows * cols, transcendentals=0
        ),
        name="unpack",
    )(pieces, *grads, *held)


def tile_of(size):
    return 256 if size % 256 == 0 else size


def tiles_of(size, part):
    tile = tile_of(size)
    tiles = size // tile
    first_part = (tiles + 1) // 2
    if part is None or tiles == 1:
        return tile, 0, tiles
    return (tile, 0, first_part) if part == 0 else (tile, first_part, tiles - first_part)


def whole_spec(shape):
    return pl.BlockSpec(shape, lambda i: (0, 0))


def column_spec(rows, tile, first=0):
    return pl.BlockSpec((rows, tile), lambda i: (0, first + i))


def row_spec(tile, cols, first=0):
    return pl.BlockSpec((tile, cols), lambda i: (first + i, 0))


def kernel_call(kernel, grid, in_specs, out_specs, out_shape, flops, moved, name, held=()):
    inputs = len(in_specs)
    return pl.pallas_call(
        lambda *refs: kernel(*refs[:inputs], *refs[inputs + len(held) :]),
        grid=(grid,),
        in_specs=in_specs + [pl.BlockSpec(memory_space=pl.ANY)] * len(held),
        out_specs=out_specs,
        out_shape=out_shape,
        input_output_aliases={inputs + i: i for i in range(len(held))},
        compiler_params=pltpu.CompilerParams(vmem_limit_bytes=VMEM_LIMIT),
        cost_estimate=pl.CostEstimate(flops=flops, bytes_accessed=moved, transcendentals=0),
        name=name,
    )


def row_parts(rows):
    part = 512 if rows % 512 == 0 else rows
    return [slice(first, first + part) for first in range(0, rows, part)]


def open_kernel(x_ref, wg_ref, wu_ref, gate_ref, up_ref, hidden_ref):
    for part in row_parts(x_ref.shape[0]):
        x = x_ref[part]
        gate = dot(x, wg_ref[...], NT)
        up = dot(x, wu_ref[...], NT)
        gate_ref[part] = gate
        up_ref[part] = up
        hidden_ref[part] = (gate * (0.5 + 0.5 * gelu_parts(gate)) * up).astype(bf16)


def open_forward(x, gate_weights, up_weights, part, held=()):
    rows, depth = x.shape
    hidden = gate_weights.shape[0]
    tile, first, tiles = tiles_of(hidden, part)
    if held and tiles * tile == hidden:
        return list(held)
    return kernel_call(
        open_kernel,
        tiles,
        [whole_spec(x.shape)] + [row_spec(tile, depth, first)] * 2,
        [column_spec(rows, tile, first)] * 3,
        [jax.ShapeDtypeStruct((rows, hidden), t) for t in (f32, f32, bf16)],
        4 * rows * depth * tile * tiles,
        2 * rows * depth + tiles * tile * (4 * depth + 10 * rows),
        "open_forward",
        held,
    )(x, gate_weights, up_weights, *held)


def open_back_kernel(x_ref, wd_ref, gate_ref, up_ref, grad_gate_ref, grad_up_ref):
    for part in row_parts(x_ref.shape[0]):
        grad = dot(x_ref[part], wd_ref[...], NT)
        gate = gate_ref[part]
        square = gate * gate
        bounded = jnp.tanh(gate * (gelu_coeff + (0.044715 * gelu_coeff) * square))
        half = 0.5 + 0.5 * bounded
        steep = (0.5 * gelu_coeff) + (1.5 * 0.044715 * gelu_coeff) * square
        slope = half + gate * (1.0 - bounded * bounded) * steep
        grad_gate_ref[part] = (grad * up_ref[part] * slope).astype(bf16)
        grad_up_ref[part] = (grad * (gate * half)).astype(bf16)


def open_back(x, down_weights, gate, up, part, held=()):
    rows, depth = x.shape
    hidden = down_weights.shape[0]
    tile, first, tiles = tiles_of(hidden, part)
    if held and tiles * tile == hidden:
        return list(held)
    return kernel_call(
        open_back_kernel,
        tiles,
        [whole_spec(x.shape), row_spec(tile, depth, first)] + [column_spec(rows, tile, first)] * 2,
        [column_spec(rows, tile, first)] * 2,
        [jax.ShapeDtypeStruct((rows, hidden), bf16)] * 2,
        2 * rows * depth * tile * tiles,
        2 * rows * depth + tiles * tile * (2 * depth + 12 * rows),
        "open_back",
        held,
    )(x, down_weights, gate, up, *held)


def input_back_kernel(gate_ref, up_ref, wg_ref, wu_ref, out_ref):
    out_ref[...] = (
        dot(gate_ref[...], wg_ref[...], NN) + dot(up_ref[...], wu_ref[...], NN)
    ).astype(bf16)


def input_back(grad_gate, grad_up, gate_weights, up_weights, part, held=()):
    rows, hidden = grad_gate.shape
    depth = gate_weights.shape[1]
    tile, first, tiles = tiles_of(depth, part)
    if held and tiles * tile == depth:
        return list(held)
    return kernel_call(
        input_back_kernel,
        tiles,
        [whole_spec(grad_gate.shape)] * 2 + [column_spec(hidden, tile, first)] * 2,
        [column_spec(rows, tile, first)],
        [jax.ShapeDtypeStruct((rows, depth), bf16)],
        4 * rows * hidden * tile * tiles,
        4 * rows * hidden + tiles * tile * (4 * hidden + 2 * rows),
        "input_back",
        held,
    )(grad_gate, grad_up, gate_weights, up_weights, *held)


def weight_kernel(*refs, count):
    out_ref = refs[-1]
    total = dot(refs[0][...], refs[count][...], TN)
    for s in range(1, count):
        total = total + dot(refs[s][...], refs[count + s][...], TN)
    out_ref[...] = total.astype(bf16)


def weight_back(lefts, rights):
    count = len(lefts)
    rows, hidden = lefts[0].shape
    depth = rights[0].shape[1]
    tile = tile_of(hidden)
    return kernel_call(
        functools.partial(weight_kernel, count=count),
        hidden // tile,
        [column_spec(rows, tile)] * count + [whole_spec((rows, depth))] * count,
        row_spec(tile, depth),
        jax.ShapeDtypeStruct((hidden, depth), bf16),
        2 * count * rows * depth * hidden,
        2 * count * rows * (hidden + depth) + 2 * hidden * depth,
        "weight_back",
    )(*lefts, *rights)


def fixed_spec(shape):
    return pl.BlockSpec(shape, lambda i: (0,) * len(shape))


def join_kernel(att_ref, w_ref, x_ref, gain_ref, next_ref, branch_ref, mid_ref, normed_ref, sum_ref):
    step = pl.program_id(0)
    heads, _, cols = att_ref.shape
    tile = w_ref.shape[0]
    total = dot(att_ref[0], w_ref[:, :cols], NT)
    for h in range(1, heads):
        total = total + dot(att_ref[h], w_ref[:, h * cols : (h + 1) * cols], NT)
    sum_ref[:, pl.ds(pl.multiple_of(step * tile, 128), tile)] = total

    @pl.when(step == pl.num_programs(0) - 1)
    def _():
        value = sum_ref[...]
        mid = x_ref[...].astype(f32) + value * norm_factor(value) * gain_ref[...]
        branch_ref[...] = value
        mid_ref[...] = mid
        normed_ref[...] = (mid * norm_factor(mid) * next_ref[...]).astype(bf16)


def join_rows(attended, weights, x, gain, next_gain):
    rows, depth = x.shape
    tile = tile_of(depth)
    return pl.pallas_call(
        join_kernel,
        grid=(depth // tile,),
        in_specs=[
            fixed_spec(attended.shape),
            row_spec(tile, weights.shape[1]),
            fixed_spec(x.shape),
            fixed_spec((1, depth)),
            fixed_spec((1, depth)),
        ],
        out_specs=[fixed_spec((rows, depth))] * 3,
        out_shape=[jax.ShapeDtypeStruct((rows, depth), t) for t in (f32, f32, bf16)],
        scratch_shapes=[pltpu.VMEM((rows, depth), f32)],
        compiler_params=pltpu.CompilerParams(vmem_limit_bytes=VMEM_LIMIT),
        cost_estimate=pl.CostEstimate(
            flops=2 * rows * weights.size,
            bytes_accessed=2 * weights.size + 12 * rows * depth,
            transcendentals=0,
        ),
        name="join_rows",
    )(attended, weights, x, gain[None], next_gain[None])


def finish_kernel(part_ref, a_ref, b_ref, mid_ref, cot_ref, gain_ref, out_ref, grad_ref, dg_ref):
    value = part_ref[...].astype(f32) + a_ref[...].astype(f32) + b_ref[...].astype(f32)
    factor = norm_factor(value)
    gain = gain_ref[...]
    out_ref[...] = (mid_ref[...] + value * factor * gain).astype(bf16)
    grad, dg = norm_back(value, factor, gain, cot_ref[...].astype(f32))
    grad_ref[...] = grad.astype(bf16)
    dg_ref[...] = dg


def finish_rows(part, a, b, mid, cotangent, gain):
    rows, depth = mid.shape
    spec = fixed_spec((rows, depth))
    return pl.pallas_call(
        finish_kernel,
        grid=(1,),
        in_specs=[spec] * 5 + [fixed_spec((1, depth))],
        out_specs=[spec, spec, fixed_spec((1, depth))],
        out_shape=[
            jax.ShapeDtypeStruct((rows, depth), bf16),
            jax.ShapeDtypeStruct((rows, depth), bf16),
            jax.ShapeDtypeStruct((1, depth), f32),
        ],
        compiler_params=pltpu.CompilerParams(vmem_limit_bytes=VMEM_LIMIT),
        cost_estimate=pl.CostEstimate(
            flops=20 * rows * depth, bytes_accessed=16 * rows * depth, transcendentals=0
        ),
        name="finish_rows",
    )(part, a, b, mid, cotangent, gain[None])


def branch_back_kernel(
    part_ref,
    a_ref,
    b_ref,
    mid_ref,
    branch_ref,
    cot_ref,
    mlp_gain_ref,
    gain_ref,
    w_ref,
    grad_mid_ref,
    grad_ref,
    send_ref,
    mlp_dg_ref,
    dg_ref,
    held_ref,
):
    @pl.when(pl.program_id(0) == 0)
    def _():
        normed = part_ref[...].astype(f32) + a_ref[...].astype(f32) + b_ref[...].astype(f32)
        mid = mid_ref[...]
        grad, dg = norm_back(mid, norm_factor(mid), mlp_gain_ref[...], normed)
        mlp_dg_ref[...] = dg
        grad_mid = cot_ref[...].astype(f32) + grad
        grad_mid_ref[...] = grad_mid
        branch = branch_ref[...]
        grad, dg = norm_back(branch, norm_factor(branch), gain_ref[...], grad_mid)
        dg_ref[...] = dg
        held_ref[...] = grad.astype(bf16)
        grad_ref[...] = grad.astype(bf16)

    send_ref[0] = dot(held_ref[...], w_ref[...], NN).astype(bf16)


def branch_back(part, a, b, mid, branch, cotangent, mlp_gain, gain, weights):
    rows, depth = mid.shape
    cols = PAIRED * HEAD_SIZE
    spec = fixed_spec((rows, depth))
    line = fixed_spec((1, depth))
    return pl.pallas_call(
        branch_back_kernel,
        grid=(KEY_VALUE_HEADS,),
        in_specs=[spec] * 6 + [line] * 2 + [column_spec(depth, cols)],
        out_specs=[
            spec,
            spec,
            pl.BlockSpec((1, rows, cols), lambda i: (i, 0, 0)),
            line,
            line,
        ],
        out_shape=[
            jax.ShapeDtypeStruct((rows, depth), f32),
            jax.ShapeDtypeStruct((rows, depth), bf16),
            jax.ShapeDtypeStruct((KEY_VALUE_HEADS, rows, cols), bf16),
            jax.ShapeDtypeStruct((1, depth), f32),
            jax.ShapeDtypeStruct((1, depth), f32),
        ],
        scratch_shapes=[pltpu.VMEM((rows, depth), bf16)],
        compiler_params=pltpu.CompilerParams(vmem_limit_bytes=VMEM_LIMIT),
        cost_estimate=pl.CostEstimate(
            flops=2 * rows * weights.size,
            bytes_accessed=2 * weights.size + 22 * rows * depth,
            transcendentals=0,
        ),
        name="branch_back",
    )(part, a, b, mid, branch, cotangent, mlp_gain[None], gain[None], weights)


def turn(values, cosine, sine):
    half = HEAD_SIZE // 2
    out = []
    for j in range(values.shape[1] // HEAD_SIZE):
        a = values[:, j * HEAD_SIZE : j * HEAD_SIZE + half]
        b = values[:, j * HEAD_SIZE + half : (j + 1) * HEAD_SIZE]
        out += [a * cosine - b * sine, b * cosine + a * sine]
    return jnp.concatenate(out, axis=1)


def project_kernel(x_ref, wq_ref, wk_ref, wv_ref, cos_ref, sin_ref, q_ref, kv_ref):
    x = x_ref[...]
    cosine, sine = cos_ref[...], sin_ref[...]
    scale = HEAD_SIZE ** (-0.5)
    q_ref[0] = (turn(dot(x, wq_ref[...], NN), cosine, sine) * scale).astype(bf16)
    kv_ref[0, :, :HEAD_SIZE] = turn(dot(x, wk_ref[...], NN), cosine, sine).astype(bf16)
    kv_ref[0, :, HEAD_SIZE:] = dot(x, wv_ref[...], NN).astype(bf16)


def project(normed, weights, cosine, sine):
    rows, depth = normed.shape
    cols = PAIRED * HEAD_SIZE
    first_key = QUERY_HEADS
    first_value = QUERY_HEADS + KEY_VALUE_HEADS
    whole = lambda shape: pl.BlockSpec(shape, lambda h: (0, 0))
    return pl.pallas_call(
        project_kernel,
        grid=(KEY_VALUE_HEADS,),
        in_specs=[
            whole((rows, depth)),
            pl.BlockSpec((depth, cols), lambda h: (0, h)),
            pl.BlockSpec((depth, HEAD_SIZE), lambda h: (0, first_key + h)),
            pl.BlockSpec((depth, HEAD_SIZE), lambda h: (0, first_value + h)),
            whole(cosine.shape),
            whole(sine.shape),
        ],
        out_specs=[
            pl.BlockSpec((1, rows, cols), lambda h: (h, 0, 0)),
            pl.BlockSpec((1, rows, 2 * HEAD_SIZE), lambda h: (h, 0, 0)),
        ],
        out_shape=[
            jax.ShapeDtypeStruct((KEY_VALUE_HEADS, rows, cols), bf16),
            jax.ShapeDtypeStruct((KEY_VALUE_HEADS, rows, 2 * HEAD_SIZE), bf16),
        ],
        compiler_params=pltpu.CompilerParams(vmem_limit_bytes=VMEM_LIMIT),
        cost_estimate=pl.CostEstimate(
            flops=2 * rows * weights.size, bytes_accessed=2 * weights.size, transcendentals=0
        ),
        name="project",
    )(normed, weights, weights, weights, cosine, sine)


def turn_back_kernel(*refs, count):
    q_refs, kv_refs = refs[:count], refs[count : 2 * count]
    cos_ref, sin_ref, out_ref = refs[2 * count :]
    j = pl.program_id(1)
    scale = HEAD_SIZE ** (-0.5)
    keys = KEY_VALUE_HEADS // PAIRED
    for s in range(count):
        here = pl.program_id(0) == s

        @pl.when(jnp.logical_and(here, j < KEY_VALUE_HEADS))
        def _():
            grad = q_refs[s][0].astype(f32) * scale
            out_ref[...] = turn(grad, cos_ref[...], -sin_ref[...]).astype(bf16)

        @pl.when(jnp.logical_and(here, jnp.logical_and(j >= KEY_VALUE_HEADS, j < KEY_VALUE_HEADS + keys)))
        def _():
            grad = jnp.concatenate([kv_refs[s][i, :, :HEAD_SIZE] for i in range(PAIRED)], axis=1)
            out_ref[...] = turn(grad.astype(f32), cos_ref[...], -sin_ref[...]).astype(bf16)

        @pl.when(jnp.logical_and(here, j >= KEY_VALUE_HEADS + keys))
        def _():
            out_ref[...] = jnp.concatenate(
                [kv_refs[s][i, :, HEAD_SIZE:] for i in range(PAIRED)], axis=1
            )


def turn_back(queries, pairs, cosine, sine):
    count = len(queries)
    heads, rows, cols = queries[0].shape
    keys = heads // PAIRED
    grid = (count, heads + 2 * keys)
    whole = pl.BlockSpec(cosine.shape, lambda s, j: (0, 0))
    return pl.pallas_call(
        functools.partial(turn_back_kernel, count=count),
        grid=grid,
        in_specs=[
            pl.BlockSpec((1, rows, cols), lambda s, j: (jnp.minimum(j, heads - 1), 0, 0))
        ]
        * count
        + [
            pl.BlockSpec(
                (PAIRED, rows, cols), lambda s, j: (jnp.maximum(j - heads, 0) % keys, 0, 0)
            )
        ]
        * count
        + [whole, whole],
        out_specs=pl.BlockSpec((rows, cols), lambda s, j: (s, j)),
        out_shape=jax.ShapeDtypeStruct((count * rows, grid[1] * cols), bf16),
        compiler_params=pltpu.CompilerParams(vmem_limit_bytes=VMEM_LIMIT),
        cost_estimate=pl.CostEstimate(
            flops=4 * count * rows * grid[1] * cols,
            bytes_accessed=4 * count * rows * grid[1] * cols,
            transcendentals=0,
        ),
        name="turn_back",
    )(*queries, *pairs, cosine, sine)


def tile_positions(tile, count, start, class_index, class_rows, rows):
    index = lax.broadcasted_iota(jnp.int32, (count, 1), 0)
    place = start + jnp.bitwise_and(index, tile - 1)
    shift = class_rows.bit_length() - 1
    return (
        jnp.right_shift(place, shift) * rows
        + class_index * class_rows
        + jnp.bitwise_and(place, class_rows - 1)
    )


def stack_heads(block):
    return jnp.concatenate(
        [block[:, j * HEAD_SIZE : (j + 1) * HEAD_SIZE] for j in range(PAIRED)], axis=0
    )


def key_places(group, class_index, classes, rows):
    index = lax.broadcasted_iota(jnp.int32, (1, classes * rows), 1)
    shift = rows.bit_length() - 1
    back = jnp.bitwise_and(class_index - jnp.right_shift(index, shift), classes - 1)
    return (group * classes + back) * rows + jnp.bitwise_and(index, rows - 1)


def held_block(refs, group, cols):
    return jnp.concatenate([ref[group, :, cols] for ref in refs], axis=0)


def group_range(start, tile, class_rows, classes):
    return start // class_rows // classes, (start + tile - 1) // class_rows // classes + 1


def attn_forward_kernel(info, q_ref, *refs, tile, class_rows, rows, classes):
    kv_refs = refs[:classes]
    att_ref, exact_ref, lse_ref = refs[classes:]
    start = pl.program_id(0) * tile
    free, total = group_range(start, tile, class_rows, classes)
    queries = stack_heads(q_ref[...])
    count = queries.shape[0]
    position = tile_positions(tile, count, start, info[0], class_rows, rows)

    def step(group, carry, masked):
        acc, row_sum = carry
        keys = held_block(kv_refs, group, slice(0, HEAD_SIZE))
        values = held_block(kv_refs, group, slice(HEAD_SIZE, 2 * HEAD_SIZE))
        raw = dot(queries, keys, NT)
        weight = jnp.exp(soft_cap * jnp.tanh(raw * (1.0 / soft_cap)))
        if masked:
            weight = jnp.where(
                key_places(group, info[0], classes, rows) <= position, weight, 0.0
            )
        row_sum = row_sum + jnp.sum(weight, axis=-1, keepdims=True)
        acc = acc + dot(weight.astype(bf16), values, NN)
        return acc, row_sum

    carry = (jnp.zeros((count, HEAD_SIZE), f32), jnp.zeros((count, 1), f32))
    carry = lax.fori_loop(0, free, functools.partial(step, masked=False), carry)
    acc, row_sum = lax.fori_loop(free, total, functools.partial(step, masked=True), carry)
    exact = acc / row_sum
    lse = jnp.log(row_sum)
    for j in range(PAIRED):
        cols = slice(j * HEAD_SIZE, (j + 1) * HEAD_SIZE)
        exact_ref[:, cols] = exact[j * tile : (j + 1) * tile]
        att_ref[:, cols] = exact[j * tile : (j + 1) * tile].astype(bf16)
        lse_ref[:, j * 128 : (j + 1) * 128] = jnp.broadcast_to(
            lse[j * tile : (j + 1) * tile], (tile, 128)
        )


def attn_forward(info, queries, pairs, class_rows, rows):
    count, cols = queries.shape
    classes = len(pairs)
    length = classes * pairs[0].shape[0] * rows
    tile = min(256, count)
    grid_spec = pltpu.PrefetchScalarGridSpec(
        num_scalar_prefetch=1,
        grid=(count // tile,),
        in_specs=[pl.BlockSpec((tile, cols), lambda i, c: (i, 0))]
        + [pl.BlockSpec(p.shape, lambda i, c: (0, 0, 0)) for p in pairs],
        out_specs=[
            pl.BlockSpec((tile, cols), lambda i, c: (i, 0)),
            pl.BlockSpec((tile, cols), lambda i, c: (i, 0)),
            pl.BlockSpec((tile, PAIRED * 128), lambda i, c: (i, 0)),
        ],
    )
    return pl.pallas_call(
        functools.partial(
            attn_forward_kernel, tile=tile, class_rows=class_rows, rows=rows, classes=classes
        ),
        grid_spec=grid_spec,
        out_shape=[
            jax.ShapeDtypeStruct((count, cols), bf16),
            jax.ShapeDtypeStruct((count, cols), f32),
            jax.ShapeDtypeStruct((count, PAIRED * 128), f32),
        ],
        compiler_params=pltpu.CompilerParams(vmem_limit_bytes=VMEM_LIMIT),
        cost_estimate=pl.CostEstimate(
            flops=2 * count * PAIRED * length * 2 * HEAD_SIZE,
            bytes_accessed=8 * count * cols + 4 * length * HEAD_SIZE,
            transcendentals=2 * count * PAIRED * length,
        ),
        name="attn_forward",
    )(info, queries, *pairs)


def attn_backward_kernel(info, q_ref, grad_ref, exact_ref, lse_ref, *refs, tile, class_rows, rows, classes):
    kv_refs, dq_ref = refs[:classes], refs[classes]
    dkv_refs, sum_ref = refs[classes + 1 : 2 * classes + 1], refs[2 * classes + 1]

    @pl.when(pl.program_id(0) == 0)
    def _():
        sum_ref[...] = jnp.zeros_like(sum_ref)

    start = pl.program_id(0) * tile
    free, total = group_range(start, tile, class_rows, classes)
    queries = stack_heads(q_ref[...])
    grads = stack_heads(grad_ref[...])
    count = queries.shape[0]
    delta = jnp.sum(grads.astype(f32) * stack_heads(exact_ref[...]), axis=-1, keepdims=True)
    lse = jnp.concatenate([lse_ref[:, j * 128 : j * 128 + 1] for j in range(PAIRED)], axis=0)
    position = tile_positions(tile, count, start, info[0], class_rows, rows)

    def step(group, acc, masked):
        keys = held_block(kv_refs, group, slice(0, HEAD_SIZE))
        values = held_block(kv_refs, group, slice(HEAD_SIZE, 2 * HEAD_SIZE))
        bounded = jnp.tanh(dot(queries, keys, NT) * (1.0 / soft_cap))
        probs = jnp.exp(soft_cap * bounded - lse)
        if masked:
            probs = jnp.where(key_places(group, info[0], classes, rows) <= position, probs, 0.0)
        grad_probs = dot(grads, values, NT)
        grad_raw = (probs * (grad_probs - delta) * (1.0 - bounded * bounded)).astype(bf16)
        sum_ref[group, :, HEAD_SIZE:] += dot(probs.astype(bf16), grads, TN)
        sum_ref[group, :, :HEAD_SIZE] += dot(grad_raw, queries, TN)
        return acc + dot(grad_raw, keys, NN)

    acc = jnp.zeros((count, HEAD_SIZE), f32)
    acc = lax.fori_loop(0, free, functools.partial(step, masked=False), acc)
    acc = lax.fori_loop(free, total, functools.partial(step, masked=True), acc)
    for j in range(PAIRED):
        dq_ref[:, j * HEAD_SIZE : (j + 1) * HEAD_SIZE] = acc[j * tile : (j + 1) * tile].astype(bf16)

    @pl.when(pl.program_id(0) == pl.num_programs(0) - 1)
    def _():
        for h, ref in enumerate(dkv_refs):
            ref[...] = sum_ref[:, h * rows : (h + 1) * rows, :].astype(bf16)


def attn_backward(info, queries, pairs, grads, exact, lse, class_rows, rows):
    count, cols = queries.shape
    classes = len(pairs)
    groups = pairs[0].shape[0]
    length = classes * groups * rows
    tile = min(256, count)
    row_spec = pl.BlockSpec((tile, cols), lambda i, c: (i, 0))
    pair_specs = [pl.BlockSpec(p.shape, lambda i, c: (0, 0, 0)) for p in pairs]
    grid_spec = pltpu.PrefetchScalarGridSpec(
        num_scalar_prefetch=1,
        grid=(count // tile,),
        in_specs=[
            row_spec,
            row_spec,
            row_spec,
            pl.BlockSpec((tile, PAIRED * 128), lambda i, c: (i, 0)),
        ]
        + pair_specs,
        out_specs=[row_spec] + pair_specs,
        scratch_shapes=[pltpu.VMEM((groups, classes * rows, 2 * HEAD_SIZE), f32)],
    )
    return pl.pallas_call(
        functools.partial(
            attn_backward_kernel, tile=tile, class_rows=class_rows, rows=rows, classes=classes
        ),
        grid_spec=grid_spec,
        out_shape=[jax.ShapeDtypeStruct((count, cols), bf16)]
        + [jax.ShapeDtypeStruct(p.shape, bf16) for p in pairs],
        compiler_params=pltpu.CompilerParams(vmem_limit_bytes=VMEM_LIMIT),
        cost_estimate=pl.CostEstimate(
            flops=5 * count * PAIRED * length * 2 * HEAD_SIZE,
            bytes_accessed=10 * count * cols + 8 * length * HEAD_SIZE,
            transcendentals=2 * count * PAIRED * length,
        ),
        name="attn_backward",
    )(info, queries, grads, exact, lse, *pairs)


def per_device(
    tokens,
    cotangent,
    widths,
    attn_codes,
    attn_exps,
    out_exps,
    mlp_codes,
    gate_exps,
    down_exps,
    gain_attn,
    gain_post_attn,
    gain_mlp,
    gain_post_mlp,
):
    wide = lax.axis_size("wide")
    seq_size = lax.axis_size("seq")
    wide_index = lax.axis_index("wide")
    seq_index = lax.axis_index("seq")
    side = seq_index % 2
    is_low = side == 0
    members = seq_size // 2
    member = seq_index // 2
    half_wide = wide // 2
    place = ring_place(wide_index, wide)
    count, rows, model_dim = tokens.shape
    classes = wide // KEY_VALUE_HEADS
    class_rows = rows // classes
    class_index = wide_index % classes
    head_cols = PAIRED * HEAD_SIZE
    proj_cols = attn_exps.shape[0]
    half_proj = proj_cols // 2
    half_out = (attn_codes.shape[1] - proj_cols) // 2
    split_out = half_out // members
    attn_rows = attn_codes.shape[0]
    hidden = mlp_codes.shape[1]
    offsets = ring_offsets(wide)
    order = {o: i for i, o in enumerate(ring_offsets(half_wide))}
    seqs = range(count)
    seq_bits = [1 << i for i in range(seq_size.bit_length() - 1)]
    far_bits = list(reversed(seq_bits[1:]))
    clock = Clock(widths)

    def index_at(offset):
        return ring_index(jnp.mod(place + offset, wide), wide)

    places = jnp.stack([index_at(o) for o in offsets]).astype(jnp.int32)
    info = jnp.concatenate(
        [side[None].astype(jnp.int32), widths, member[None].astype(jnp.int32)]
    )
    class_info = class_index[None].astype(jnp.int32)
    column_scale = inverse_powers(attn_exps)[None, :]
    output_scale = inverse_powers(out_exps)[:, None]

    relative = [0]
    for bit in reversed(seq_bits):
        relative = relative + [r | bit for r in relative]
    pieces = jnp.stack([jnp.bitwise_xor(seq_index, r) for r in relative]).astype(jnp.int32)
    piece_rows = hidden // seq_size
    partner = jnp.bitwise_xor(wide_index, half_wide)
    gate_scale = inverse_powers(gate_exps)
    row_scale = jnp.concatenate(
        [
            lax.dynamic_slice_in_dim(
                gate_scale, block * hidden + pieces[j] * piece_rows, piece_rows, 1
            )
            for block in (wide_index, partner)
            for j in range(seq_size)
        ],
        axis=1,
    )[:, :, None]
    down_scale = inverse_powers(down_exps)[None, :]

    def columns(first, size):
        return lax.dynamic_slice_in_dim(attn_codes, first, size, 1)

    payload = jnp.concatenate(
        [
            columns(side * half_proj, half_proj),
            columns(proj_cols + side * half_out + member * split_out, split_out),
        ],
        axis=1,
    ).astype(bf16)
    piece_codes = lax.dynamic_slice_in_dim(mlp_codes, seq_index * piece_rows, piece_rows, 1)
    inputs = [tokens[s].astype(f32) for s in seqs]
    cosine, sine = rotary_rows(wide_index * rows + jnp.arange(rows))

    blocks, others = [clock.hold(payload)], []
    proj_weights = []

    def slice_more(first, last):
        return proj_slices(
            blocks[first:last],
            others[first:last],
            places[first:last],
            info,
            column_scale,
            half_proj,
            proj_weights,
            wide,
            count,
        )

    a = b = blocks[0]
    sliced = 0
    steps = half_wide
    for k in range(1, steps + 1):
        if k == steps:
            a, b = halves(a)[0], halves(b)[1]
        passed = [swap(v, "seq", 1) for v in blocks[len(others) :]]
        a, b = hop(a, b, wide)
        work = []
        if k == 1:
            work = own_slices(mlp_codes, pieces, info, row_scale, down_scale, count)
            a, b, *work = clock.sync(a, b, *passed, *work)
            passed, own_weights = work[: len(passed)], work[len(passed) :]
        elif k == 2:
            work = [piece_codes[m].astype(bf16) for m in range(3)]
            for s in seqs:
                factor = norm_factor(clock.hold(inputs[s]))
                work += [factor, (inputs[s] * factor * gain_attn).astype(bf16)]
            a, b, *work = clock.sync(a, b, *passed, *work)
            passed, work = work[: len(passed)], work[len(passed) :]
            sends, work = work[:3], work[3:]
            input_factor, normed = work[0::2], work[1::2]
        else:
            more = len(others)
            work = slice_more(sliced, more) if more > sliced else []
            a, b, *work = clock.sync(a, b, *passed, *work)
            passed, work = work[: len(passed)], work[len(passed) :]
            if work:
                proj_weights, sliced = list(work), more
        others += passed
        blocks += [a, b] if k < steps else [jnp.concatenate([a, b], axis=0)]

    def exchange(m):
        return swap(clock.hold(sends[m]), "wide", half_wide)

    def share(held, bits):
        for bit in bits:
            held = held + [swap(value, "seq", bit) for value in held]
        return held

    def partner_weights(m, held):
        scale = row_scale[m] if m < 2 else down_scale
        return partner_slices(
            held, info, scale, m == 2, own_weights[m * count : (m + 1) * count]
        )

    received = exchange(0)
    others += [swap(clock.hold(v), "seq", 1) for v in blocks[len(others) :]]
    proj_weights = slice_more(sliced, wide)
    query_send, pair_send = [], []
    for s in seqs:
        query, pair = project(normed[s], proj_weights[s], cosine, sine)
        query_send.append(query.reshape(wide, class_rows, head_cols))
        pair_send.append(pair)
    sent = clock.sync(received, *query_send, *pair_send)
    received, sent = sent[0], sent[1:]
    query_send, pair_send = sent[:count], sent[count:]

    def spread(pair):
        held = [pair]
        for _ in range(classes - 1):
            held.append(class_ring(held[-1]))
        return held[1:]

    def two_parts(value):
        cut = value.shape[0] // 2
        return value[:cut], value[cut:]

    attended_send, exact, lse, queries, pairs = [], [], [], [], []

    def attend(s):
        out, full, log_sum = attn_forward(class_info, queries[s], pairs[s], class_rows, rows)
        return [out.reshape(wide, class_rows, head_cols), full, log_sum]

    def keep_attend(work):
        attended_send.append(work[0])
        exact.append(work[1])
        lse.append(work[2])

    pair_first = heads_all_to_all(clock.hold(pair_send[0]))
    own_out = jnp.stack([clock.hold(v)[:, half_proj:] for v in blocks])
    other_out = jnp.stack([clock.hold(v)[:, half_proj:] for v in others])
    pair_first, own_out, other_out = clock.sync(pair_first, own_out, other_out)
    out_own = share([clock.hold(own_out)], far_bits)
    moved = spread(pair_first)
    pair_last, *work = clock.sync(heads_all_to_all(clock.hold(pair_send[1])), *moved)
    pairs.append([pair_first] + work)
    part_a, part_b = two_parts(pair_last)
    query = all_to_all(clock.hold(query_send[0]))
    query, *work = clock.sync(query, *spread(part_a), *out_own)
    moved_a, out_own = work[: classes - 1], work[classes - 1 :]
    queries.append(query.reshape(wide * class_rows, head_cols))
    moved_b = spread(clock.hold(part_b))
    query = all_to_all(clock.hold(query_send[1]))
    out_other = [swap(v, "seq", 1) for v in out_own[1:]]
    gate_held = share([clock.hold(received)], far_bits)
    query, *work = clock.sync(query, *moved_b, *out_other, *attend(0))
    moved_b, work = work[: classes - 1], work[classes - 1 :]
    out_other, work = [other_out] + work[: len(out_other)], work[len(out_other) :]
    keep_attend(work)
    queries.append(query.reshape(wide * class_rows, head_cols))
    pairs.append(
        [pair_last] + [jnp.concatenate([x, y], axis=0) for x, y in zip(moved_a, moved_b)]
    )

    attended, heads_back, branch, middle, normed_mlp = [], [], [], [], []

    def heads_to_rows(values):
        split = values.reshape(KEY_VALUE_HEADS, rows, head_cols)
        return jnp.transpose(split, (1, 0, 2)).reshape(rows, KEY_VALUE_HEADS * head_cols)

    def join(s):
        return join_rows(
            heads_back[s], out_weights[s], tokens[s], gain_post_attn, gain_mlp
        )

    def keep_join(work):
        for held, value in zip((branch, middle, normed_mlp), work):
            held.append(value)

    for s in seqs:
        back = all_to_all(clock.hold(attended_send[s]))
        if s == 0:
            out_weights = out_slices(out_own, out_other, places, info, output_scale, count)
            back, *work = clock.sync(back, *gate_held, *out_weights, *attend(count - 1))
            gate_held, work = work[: len(gate_held)], work[len(gate_held) :]
            out_weights, work = work[:count], work[count:]
            keep_attend(work)
        else:
            gate_held = share(gate_held, seq_bits[:1])
            back, *work = clock.sync(back, *gate_held, *join(s - 1))
            gate_held, work = work[: len(gate_held)], work[len(gate_held) :]
            keep_join(work)
        heads_back.append(back.reshape(KEY_VALUE_HEADS, rows, head_cols))
        attended.append(heads_to_rows(back))

    received = exchange(1)
    gate_weights = partner_weights(0, [clock.hold(v) for v in gate_held])
    received, *work = clock.sync(received, *gate_weights, *join(count - 1))
    gate_weights, work = work[:count], work[count:]
    keep_join(work)

    def blocks_of(part):
        return lambda o: part[order[o] * rows : (order[o] + 1) * rows]

    gathered, gate, up, hidden_rows, mixed, parts = [], [], [], [], [], []

    def open_part(s, part, held=()):
        group = clock.hold(gathered[s])
        return open_forward(group, gate_weights[s], up_weights[s], part, held)

    def keep_open(work):
        gate.append(work[0])
        up.append(work[1])
        hidden_rows.append(work[2])

    def mix(s):
        return dot(clock.hold(hidden_rows[s]), down_weights[s], NN).astype(bf16)

    up_held = share([clock.hold(received)], far_bits)
    received, *up_held = clock.sync(exchange(2), *up_held)

    def beside_first(step):
        nonlocal up_held
        if step == 0:
            up_held = share(up_held, seq_bits[:1])
            return tuple(up_held) + tuple(share([clock.hold(received)], far_bits))
        if step == 1:
            return tuple(partner_weights(1, [clock.hold(v) for v in up_held]))
        return ()

    a = b = clock.hold(normed_mlp[0])
    blocks = [a]
    for k in range(1, half_wide // 2 + 1):
        if k == half_wide // 2:
            a, b = halves(a)[0], halves(b)[1]
        if k == 2:
            down_held = share(down_held, seq_bits[:1])
        work = beside_first(k - 1) + (tuple(down_held) if k == 2 else ())
        a, b = hop(a, b, half_wide)
        a, b, *work = clock.sync(a, b, *work)
        if k == 1:
            up_held, down_held = work[: len(up_held)], work[len(up_held) :]
        elif k == 2:
            up_weights, down_held = work[:count], work[count:]
        blocks += [a, b]
    gathered.append(jnp.concatenate(blocks, axis=0))

    def beside_second(step):
        if step == 0:
            return open_part(0, None)
        if step == 1:
            return partner_weights(2, [clock.hold(v) for v in down_held])
        return ()

    a = b = clock.hold(normed_mlp[1])
    blocks = [a]
    for k in range(1, half_wide // 2 + 1):
        if k == half_wide // 2:
            a, b = halves(a)[0], halves(b)[1]
        work = beside_second(k - 1)
        a, b = hop(a, b, half_wide)
        a, b, *work = clock.sync(a, b, *work)
        if k == 1:
            keep_open(work)
        elif k == 2:
            down_weights = work
        blocks += [a, b]
    gathered.append(jnp.concatenate(blocks, axis=0))
    parts.append(clock.sync(mix(0))[0])

    layer_out, grad_mixed, gain_fourth = [], [], 0.0

    def finish(s):
        nonlocal gain_fourth
        out, grad, gain = finish_rows(*mixed[s], middle[s], cotangent[s], gain_post_mlp)
        layer_out.append(out)
        grad_mixed.append(grad)
        gain_fourth = gain_fourth + gain

    grad_group, grad_gate, grad_up, grad_parts, grad_normed_mlp = [], [], [], [], []

    def back_hidden(s, part, held=()):
        group = clock.hold(grad_group[s])
        return open_back(group, down_weights[s], gate[s], up[s], part, held)

    def back_input(s, part, held=()):
        grad = clock.hold(grad_gate[s])
        return input_back(grad, grad_up[s], gate_weights[s], up_weights[s], part, held)

    def keep_back(work):
        grad_gate.append(work[0])
        grad_up.append(work[1])

    def first_sum(part):
        a, b = hop(*halves(clock.hold(blocks_of(part)(half_wide // 2))), half_wide)
        return a, b

    def rest_sum(part, a, b, beside=lambda step: ()):
        part_of = blocks_of(part)
        other = []
        for k in range(half_wide // 2 - 1, 0, -1):
            if k == half_wide // 2 - 1:
                a = add_first(part_of(k), a)
                b = add_last(part_of(-k), b)
            else:
                a = low_sum(part_of(k), a)
                b = low_sum(part_of(-k), b)
            work = beside(half_wide // 2 - 1 - k)
            a, b = hop(a, b, half_wide)
            a, b, *work = clock.sync(a, b, *work)
            other.append(work)
        return (part, a, b), other

    a, b = first_sum(parts[0])
    a, b, *opened = clock.sync(a, b, *open_part(1, 0))
    total, work = rest_sum(
        parts[0], a, b, lambda step: () if step else tuple(open_part(1, 1, opened))
    )
    keep_open(work[0])
    mixed.append(total)
    finish(0)
    parts.append(mix(1))
    blocks, work = ring_gather(
        clock, grad_mixed[0], half_wide, lambda k: (parts[1],) if k == 0 else ()
    )
    parts[1] = work[0][0]
    grad_group.append(jnp.concatenate(blocks, axis=0))
    a, b = first_sum(parts[1])
    a, b, *opened = clock.sync(a, b, *back_hidden(0, 0))

    def beside_last(step):
        if step:
            return ()
        keep_back(back_hidden(0, 1, opened))
        return (grad_gate[0], grad_up[0], *input_back(
            grad_gate[0], grad_up[0], gate_weights[0], up_weights[0], 0, ()
        ))

    total, work = rest_sum(parts[1], a, b, beside_last)
    grad_gate[0], grad_up[0], opened = work[0][0], work[0][1], work[0][2:]
    mixed.append(total)
    finish(1)
    blocks, work = ring_gather(
        clock, grad_mixed[1], half_wide, lambda k: () if k else tuple(back_input(0, 1, opened))
    )
    grad_parts.append(work[0][0])
    grad_group.append(jnp.concatenate(blocks, axis=0))

    def weight_sum(lefts, rights):
        lefts = [clock.hold(v) for v in lefts]
        return weight_back(lefts, rights).reshape(2, hidden, model_dim)

    def part_sum(grad, bit):
        split = grad.reshape(2, 2, grad.shape[1] // 2, model_dim)
        return low_sum(split[:, 0], swap(split[:, 1], "seq", bit))

    grad_middle, grad_branch, grad_send = [], [], []
    gain_third = gain_second = 0.0

    def back_branch(s):
        nonlocal gain_third, gain_second
        grad_mid, grad, send, third, second = branch_back(
            *[clock.hold(v) for v in grad_normed_mlp[s]],
            middle[s],
            branch[s],
            cotangent[s],
            gain_mlp,
            gain_post_attn,
            out_weights[s],
        )
        gain_third = gain_third + third
        gain_second = gain_second + second
        return [grad_mid, grad, send.reshape(wide, class_rows, head_cols)]

    def keep_branch(work):
        grad_middle.append(work[0])
        grad_branch.append(work[1])
        grad_send.append(work[2])

    a, b = first_sum(grad_parts[0])
    a, b, *opened = clock.sync(a, b, *back_hidden(1, 0))

    def beside_back(step):
        if step:
            return ()
        keep_back(back_hidden(1, 1, opened))
        return (grad_gate[1], grad_up[1], *input_back(
            grad_gate[1], grad_up[1], gate_weights[1], up_weights[1], 0, ()
        ))

    total, work = rest_sum(grad_parts[0], a, b, beside_back)
    grad_gate[1], grad_up[1], opened = work[0][0], work[0][1], work[0][2:]
    grad_normed_mlp.append(total)
    grad_parts += clock.sync(*back_input(1, 1, opened))
    a, b = first_sum(grad_parts[1])
    a, b, *work = clock.sync(a, b, *back_branch(0))
    keep_branch(work)
    total, work = rest_sum(
        grad_parts[1],
        a,
        b,
        lambda step: () if step else (weight_sum(hidden_rows, grad_group),),
    )
    down_grad = work[0][0]
    grad_normed_mlp.append(total)

    def attend_back(s):
        dq, *dkv = attn_backward(
            class_info,
            queries[s],
            pairs[s],
            clock.hold(grad_heads[s]),
            exact[s],
            lse[s],
            class_rows,
            rows,
        )
        return [dq.reshape(wide, class_rows, head_cols)] + dkv

    def class_sum(dkv):
        total = dkv[1 % classes]
        for step in range(2, classes + 1):
            total = low_sum(dkv[step % classes], class_ring(total))
        return total

    def far_parts(grad):
        split = grad.reshape(2, 2, grad.shape[1] // 2, model_dim)
        send = split[:, 1]
        return split[:, 0], [send[:, :, : model_dim // 2], send[:, :, model_dim // 2 :]]

    def far_move(part):
        return swap(clock.hold(part), "seq", seq_bits[1])

    def far_join(kept, moved):
        grad = low_sum(kept, jnp.concatenate(moved, axis=2))
        for bit in seq_bits[2:]:
            grad = part_sum(grad, bit)
        return grad

    grad_heads, grad_attend = [], []
    query_back, pair_back = [], []

    def heads_of(value):
        return value.reshape(wide * class_rows, head_cols)

    back = all_to_all(clock.hold(grad_send[0]))
    down_grad = part_sum(down_grad, 1)
    back, down_grad, *work = clock.sync(back, down_grad, *back_branch(1))
    keep_branch(work)
    grad_heads.append(heads_of(back))
    all_normed = jnp.concatenate(normed, axis=0)
    all_attended = jnp.concatenate(attended, axis=0)
    all_branch = jnp.concatenate(grad_branch, axis=0)

    def half_dot(left, right, which, size):
        return dot(left, lax.dynamic_slice_in_dim(right, which * size, size, 1), TN)

    down_keep, down_parts = far_parts(down_grad)
    down_moved = [far_move(down_parts[0])]
    back = all_to_all(clock.hold(grad_send[1]))
    out_send = half_dot(all_branch, clock.hold(all_attended), 1 - side, half_out).astype(bf16)
    back, down_moved[0], out_send, *work = clock.sync(
        back, down_moved[0], out_send, *attend_back(0)
    )
    down_moved.append(far_move(down_parts[1]))
    grad_heads.append(heads_of(back))
    grad_attend.append(work)

    dq, *dkv = grad_attend[0]
    parts_of_pair = [two_parts(v) for v in dkv]
    out_sent = swap(out_send, "seq", 1)
    query = all_to_all(clock.hold(dq))
    pair_a = class_sum([v[0] for v in parts_of_pair])
    out_part = low_sum(
        half_dot(all_branch, clock.hold(all_attended), side, half_out), out_sent
    )
    query, pair_a, down_moved[1], out_part, *work = clock.sync(
        query, pair_a, down_moved[1], out_part, *attend_back(1)
    )
    down_grad = far_join(down_keep, down_moved)
    query_back.append(query)
    grad_attend.append(work)
    dq, *dkv = grad_attend[1]
    query = all_to_all(clock.hold(dq))
    pair_b = class_sum([clock.hold(v[1]) for v in parts_of_pair])
    out_pieces = {
        t: lax.dynamic_slice_in_dim(
            clock.hold(out_part), jnp.bitwise_xor(member, t) * split_out, split_out, 1
        )
        for t in range(members)
    }
    out_moved = []
    if members == 2:
        out_parts = [out_pieces[1][:, : split_out // 2], out_pieces[1][:, split_out // 2 :]]
        out_moved.append(swap(out_parts[0], "seq", seq_bits[1]))
    else:
        for bit in seq_bits[1:]:
            for t in sorted(out_pieces):
                if not t & (bit // 2) and t | (bit // 2) in out_pieces:
                    out_pieces[t] = low_sum(
                        out_pieces[t], swap(out_pieces.pop(t | (bit // 2)), "seq", bit)
                    )
    up_grad = weight_sum(grad_up, gathered)
    query, pair_b, down_grad, up_grad, *out_moved = clock.sync(
        query, pair_b, down_grad, up_grad, *out_moved
    )
    query_back.append(query)

    pair = heads_all_to_all(clock.hold(jnp.concatenate([pair_a, pair_b], axis=0)))
    pair_sum = class_sum([clock.hold(v) for v in dkv])
    up_grad = part_sum(up_grad, 1)
    if members == 2:
        out_moved.append(swap(clock.hold(out_parts[1]), "seq", seq_bits[1]))
    pair, pair_sum, up_grad, *out_moved = clock.sync(pair, pair_sum, up_grad, *out_moved)
    out_piece = out_pieces[0]
    if out_moved:
        out_piece = low_sum(out_piece, jnp.concatenate(out_moved, axis=1))
    pair_back.append(pair)
    up_keep, up_parts = far_parts(up_grad)
    up_moved = [far_move(up_parts[0])]
    pair = heads_all_to_all(clock.hold(pair_sum))
    gate_grad = weight_sum(grad_gate, gathered)
    pair, up_moved[0], gate_grad = clock.sync(pair, up_moved[0], gate_grad)
    up_moved.append(far_move(up_parts[1]))
    pair_back.append(pair)

    def column_parts(value, count):
        width = value.shape[1] // count
        return [value[:, i * width : (i + 1) * width] for i in range(count)]

    def exchange_grad(part):
        return swap(clock.hold(part), "wide", half_wide)

    def half_sum(grad):
        split = grad.reshape(2, 2, grad.shape[1] // 2, model_dim)
        return split[:, 0], split[:, 1]

    down_own = column_parts(down_grad[0], 3)
    down_send = column_parts(down_grad[1], 3)
    gate_keep, gate_send = half_sum(gate_grad)
    gate_moved = swap(gate_send, "seq", 1)
    moved, grad_proj = clock.sync(
        exchange_grad(down_send[0]),
        turn_back(
            [v.reshape(KEY_VALUE_HEADS, rows, head_cols) for v in query_back],
            pair_back,
            cosine,
            sine,
        ),
    )
    down_other = [moved]
    moved = exchange_grad(down_send[1])
    proj_send = half_dot(all_normed, clock.hold(grad_proj), 1 - side, half_proj).astype(bf16)
    moved, gate_moved, up_moved[1], proj_send = clock.sync(
        moved, gate_moved, up_moved[1], proj_send
    )
    down_other.append(moved)
    up_grad = far_join(up_keep, up_moved)
    moved = exchange_grad(down_send[2])
    proj_sent = swap(proj_send, "seq", 1)
    gate_grad = low_sum(gate_keep, gate_moved)
    moved, proj_sent, up_grad, gate_grad = clock.sync(moved, proj_sent, up_grad, gate_grad)
    down_other.append(moved)
    gate_keep, gate_parts = far_parts(gate_grad)
    down_grad = [low_sum(x, y) for x, y in zip(down_own, down_other)]
    proj_part = low_sum(half_dot(all_normed, clock.hold(grad_proj), side, half_proj), proj_sent)
    (proj_part,) = clock.sync(proj_part)
    def part_of(o):
        first = index_at(o) * attn_rows
        return jnp.concatenate(
            [
                lax.dynamic_slice_in_dim(proj_part, first, attn_rows, 0),
                lax.dynamic_slice_in_dim(out_piece, first, attn_rows, 0),
            ],
            axis=1,
        )

    def spread_grad(grads, bits):
        for bit in bits:
            grads = [jnp.concatenate([g, swap(g, "seq", bit)], axis=0) for g in grads]
        return grads

    a, b = halves(clock.hold(part_of(wide // 2)))
    gate_moved = []
    for k in range(wide // 2 - 1, -1, -1):
        step = wide // 2 - 1 - k
        a, b = hop(a, b, wide)
        work = []
        if step in (1, 2):
            work = [far_move(gate_parts[step - 1])]
        elif step == half_wide - 1:
            work = spread_grad([clock.hold(v) for v in down_grad], far_bits)
        a, b, *work = clock.sync(a, b, *work)
        if step in (1, 2):
            gate_moved += work
        elif step == half_wide - 1:
            down_grad = work
        if step == 0:
            a, b = add_first(part_of(k), a), add_last(part_of(-k), b)
        elif k > 0:
            a, b = low_sum(part_of(k), a), low_sum(part_of(-k), b)
    total = low_sum(part_of(0), a, b)
    gate_grad = far_join(gate_keep, gate_moved)
    up_own, up_send = column_parts(up_grad[0], 2), column_parts(up_grad[1], 2)
    total, gate_grad, *up_send = clock.sync(total, gate_grad, *up_send)

    def input_grad(s):
        return dot(clock.hold(grad_proj[s * rows : (s + 1) * rows]), proj_weights[s], NT)

    def back_tokens(s, grad_normed):
        grad, gain = norm_back(inputs[s], input_factor[s], gain_attn, grad_normed)
        return (grad_middle[s] + grad).astype(bf16), gain

    def add_swapped(gains, axis, bits):
        for bit in bits:
            gains = gains + swap(gains, axis, bit)
        return gains

    proj_total = total[:, :half_proj]
    out_totals = {0: total[:, half_proj:]}
    for bit in seq_bits[1:]:
        sent = jnp.concatenate([proj_total] + [out_totals[t] for t in sorted(out_totals)], axis=1)
        moved = swap(sent, "seq", bit)
        proj_total = low_sum(proj_total, moved[:, :half_proj])
        for i, t in enumerate(sorted(out_totals)):
            first = half_proj + i * split_out
            out_totals[t | (bit // 2)] = moved[:, first : first + split_out]
    out_totals = jnp.stack([out_totals[t] for t in range(members)])
    low = jnp.concatenate(
        [proj_total]
        + [
            lax.dynamic_index_in_dim(out_totals, jnp.bitwise_xor(member, j), 0, keepdims=False)
            for j in range(members)
        ],
        axis=1,
    )
    moved, grad_first = clock.sync(exchange_grad(up_send[0]), input_grad(0))
    up_grad = [low_sum(up_own[0], moved)]
    moved, low, grad_last = clock.sync(exchange_grad(up_send[1]), low, input_grad(1))
    up_grad.append(low_sum(up_own[1], moved))
    gate_own, gate_send = column_parts(gate_grad[0], 2), column_parts(gate_grad[1], 2)
    first_tokens, gain_first = back_tokens(0, grad_first)
    last_tokens, gain = back_tokens(1, grad_last)
    gains = jnp.concatenate([gain_first + gain, gain_second, gain_third, gain_fourth], axis=0)
    wide_bits = [1 << i for i in range(wide.bit_length() - 1)]
    gains, *gate_send = clock.sync(add_swapped(gains, "wide", wide_bits[1:]), *gate_send)
    moved = exchange_grad(gate_send[0])
    up_grad = spread_grad([clock.hold(v) for v in up_grad], far_bits)
    other = swap(clock.hold(low), "seq", 1)
    moved, other, *up_grad = clock.sync(moved, other, *up_grad)
    gate_grad = [low_sum(gate_own[0], moved)]
    moved = exchange_grad(gate_send[1])
    gate_grad = spread_grad([clock.hold(v) for v in gate_grad], far_bits)
    left, right = jnp.where(is_low, low, other), jnp.where(is_low, other, low)
    attn_grad = jnp.concatenate(
        [left[:, :half_proj], right[:, :half_proj], left[:, half_proj:], right[:, half_proj:]],
        axis=1,
    ).astype(f32)
    down_grad = spread_grad([clock.hold(v) for v in down_grad], seq_bits[:1])
    mlp_grad = unpack(down_grad, pieces, 2, [])
    moved, attn_grad, mlp_grad, *gate_grad = clock.sync(moved, attn_grad, mlp_grad, *gate_grad)
    last = spread_grad([low_sum(gate_own[1], moved)], far_bits)
    up_grad = spread_grad([clock.hold(v) for v in up_grad], seq_bits[:1])
    mlp_grad = unpack(up_grad, pieces, 1, [mlp_grad])
    gate_grad = spread_grad([clock.hold(v) for v in gate_grad], seq_bits[:1])
    gains = add_swapped(clock.hold(gains), "wide", wide_bits[:1])
    gains = add_swapped(add_swapped(gains, "seq", seq_bits[:1]), "seq", seq_bits[1:])
    mlp_grad, gains, *gate_grad = clock.sync(mlp_grad, gains, *gate_grad, *last)
    gate_grad[1:] = spread_grad(gate_grad[1:], seq_bits[:1])
    mlp_grad = unpack(gate_grad, pieces, 0, [mlp_grad])
    grad_tokens = [first_tokens, last_tokens]
    return (
        jnp.stack(layer_out),
        jnp.stack(grad_tokens),
        attn_grad,
        mlp_grad,
        gains[0],
        gains[1],
        gains[2],
        gains[3],
    )


def solution(mesh):
    placed = (
        P("seq", "wide", None),
        P("seq", "wide", None),
        P("seq"),
        P("wide", None),
        P(),
        P(),
        P(None, "wide", None),
        P(),
        P(),
        P(),
        P(),
        P(),
        P(),
    )
    return jax.shard_map(
        per_device,
        mesh=mesh,
        in_specs=placed,
        out_specs=(
            P("seq", "wide", None),
            P("seq", "wide", None),
            P("wide", None),
            P(None, "wide", None),
            P(),
            P(),
            P(),
            P(),
        ),
        check_vma=False,
    )
```

```python
import functools
import math

import jax
import jax.numpy as jnp
from jax import lax
from jax.experimental import pallas as pl
from jax.experimental.pallas import tpu as pltpu
from jax.sharding import PartitionSpec as P

QUERY_HEADS = 8
KEY_VALUE_HEADS = 4
HEAD_SIZE = 256
PAIRED = QUERY_HEADS // KEY_VALUE_HEADS

eps_norm = 1e-06
soft_cap = 50.0
rope_base = 10000.0
gelu_coeff = math.sqrt(2.0 / math.pi)
f32 = jnp.float32
bf16 = jnp.bfloat16
VMEM_LIMIT = 56 * 1024 * 1024


def dot(a, b, dims):
    return lax.dot_general(a, b, (dims, ((), ())), preferred_element_type=f32)


NN = ((1,), (0,))
NT = ((1,), (1,))
TN = ((0,), (0,))


def inverse_powers(exponents):
    return 1.0 / jnp.left_shift(jnp.ones_like(exponents), exponents).astype(f32)


def norm_factor(values):
    return lax.rsqrt(jnp.mean(values * values, axis=-1, keepdims=True) + eps_norm)


def norm_back(values, factor, gain, grad):
    scaled = grad * gain
    inner = jnp.mean(values * scaled, axis=-1, keepdims=True)
    grad_values = factor * scaled - values * (factor * factor * factor * inner)
    return grad_values, jnp.sum(grad * values * factor, axis=0, keepdims=True)


def gelu_parts(values):
    inner = gelu_coeff * (values + 0.044715 * values * values * values)
    return jnp.tanh(inner)


def rotary_rows(positions):
    half_dim = HEAD_SIZE // 2
    frequency = jnp.exp(
        jnp.arange(half_dim, dtype=f32) * (-2.0 * math.log(rope_base) / HEAD_SIZE)
    )
    angles = positions.astype(f32)[:, None] * frequency[None, :]
    return jnp.cos(angles), jnp.sin(angles)


def ring_place(index, size):
    return jnp.where(index % 2 == 0, index // 2, size - 1 - index // 2)


def ring_index(place, size):
    return jnp.where(place < size // 2, 2 * place, 2 * (size - 1 - place) + 1)


def ring_perms(size):
    order = list(range(0, size, 2)) + list(range(size - 1, 0, -2))
    up = [
        (base + order[i], base + order[(i + 1) % size])
        for base in range(0, lax.axis_size("wide"), size)
        for i in range(size)
    ]
    return up, [(b, a) for a, b in up]


def ring_offsets(size):
    out = [0]
    for k in range(1, size // 2):
        out += [-k, k]
    return out + [size // 2]


class Clock:
    def __init__(self, token):
        self.token = token

    def sync(self, *arrays):
        *arrays, self.token = lax.optimization_barrier(tuple(arrays) + (self.token,))
        return arrays

    def hold(self, value):
        return lax.optimization_barrier((value, self.token))[0]


def hop(a, b, size):
    up, down = ring_perms(size)
    return lax.ppermute(a, "wide", up), lax.ppermute(b, "wide", down)


def low_sum(*terms):
    return sum(t.astype(f32) for t in terms).astype(bf16)


def halves(value):
    half = value.shape[0] // 2
    return value[:half], value[half:]


def add_first(whole, part):
    count = part.shape[0]
    return jnp.concatenate([low_sum(whole[:count], part), whole[count:].astype(bf16)], axis=0)


def add_last(whole, part):
    count = whole.shape[0] - part.shape[0]
    return jnp.concatenate([whole[:count].astype(bf16), low_sum(whole[count:], part)], axis=0)


def ring_gather(clock, value, size, beside=lambda step: ()):
    a = b = clock.hold(value)
    out, other = [a], []
    for k in range(1, size // 2 + 1):
        if k == size // 2:
            a, b = halves(a)[0], halves(b)[1]
        work = beside(k - 1)
        a, b = hop(a, b, size)
        a, b, *work = clock.sync(a, b, *work)
        out += [a, b]
        other.append(work)
    return out, other


def ring_scatter(clock, part_of, rows, size, beside=lambda step: ()):
    a, b = halves(clock.hold(part_of(size // 2).astype(bf16)))
    other = []
    for k in range(size // 2 - 1, -1, -1):
        work = beside(size // 2 - 1 - k)
        a, b = hop(a, b, size)
        a, b, *work = clock.sync(a, b, *work)
        other.append(work)
        if k == size // 2 - 1 and k > 0:
            a = add_first(part_of(k), a)
            b = add_last(part_of(-k), b)
        elif k > 0:
            a = low_sum(part_of(k), a)
            b = low_sum(part_of(-k), b)
    return part_of(0).astype(f32) + a.astype(f32) + b.astype(f32), other


def swap(value, axis, bit):
    size = lax.axis_size(axis)
    return lax.ppermute(value, axis, [(i, i ^ bit) for i in range(size)])


def all_to_all(value):
    return lax.all_to_all(value, "wide", split_axis=0, concat_axis=0, tiled=True)


def heads_all_to_all(value):
    size = lax.axis_size("wide")
    classes = size // KEY_VALUE_HEADS
    groups = [list(range(c, size, classes)) for c in range(classes)]
    return lax.all_to_all(
        value, "wide", split_axis=0, concat_axis=0, axis_index_groups=groups, tiled=True
    )


def class_ring(value):
    size = lax.axis_size("wide")
    classes = size // KEY_VALUE_HEADS
    perm = [(i, i // classes * classes + (i + 1) % classes) for i in range(size)]
    return lax.ppermute(value, "wide", perm)


def slice_values(codes, width):
    lift = jnp.where(width == 0, 0.0, 0.5).astype(bf16)
    large = jnp.where(width == 0, 0.0, jnp.where(width == 1, 1.5 * 2**11, 1.5 * 2**13)).astype(bf16)
    top = jnp.where(width == 0, 127.0, jnp.where(width == 1, 112.0, 64.0)).astype(bf16)
    return jnp.minimum(((codes + lift) + large) - large, top)


def proj_slice_kernel(places, info, *refs, blocks, count):
    code_refs, scale_ref, out_refs = refs[: 2 * blocks], refs[2 * blocks], refs[len(refs) - count :]
    mine = pl.program_id(1) == info[0]

    def write(code_ref):
        codes = code_ref[...]
        scale = scale_ref[...].astype(bf16)
        for s, out_ref in enumerate(out_refs):
            out_ref[...] = slice_values(codes, info[1 + s]) * scale

    for k in range(blocks):
        here = pl.program_id(0) == k
        pl.when(jnp.logical_and(here, mine))(functools.partial(write, code_refs[2 * k]))
        pl.when(jnp.logical_and(here, jnp.logical_not(mine)))(
            functools.partial(write, code_refs[2 * k + 1])
        )


def proj_slices(own, other, places, info, scale, width, weights, total, count):
    blocks = len(own)
    rows = own[0].shape[0]
    inputs = [block for pair in zip(own, other) for block in pair] + [scale]
    grid_spec = pltpu.PrefetchScalarGridSpec(
        num_scalar_prefetch=2,
        grid=(blocks, 2),
        in_specs=[pl.BlockSpec((rows, width), lambda k, j, p, i: (0, 0))] * (2 * blocks)
        + [pl.BlockSpec((1, width), lambda k, j, p, i: (0, j))]
        + [pl.BlockSpec(memory_space=pl.ANY)] * len(weights),
        out_specs=[pl.BlockSpec((rows, width), lambda k, j, p, i: (p[k], j))] * count,
    )
    return pl.pallas_call(
        functools.partial(proj_slice_kernel, blocks=blocks, count=count),
        grid_spec=grid_spec,
        out_shape=[jax.ShapeDtypeStruct((total * rows, 2 * width), bf16)] * count,
        input_output_aliases={2 + len(inputs) + s: s for s in range(len(weights))},
        compiler_params=pltpu.CompilerParams(vmem_limit_bytes=VMEM_LIMIT),
        cost_estimate=pl.CostEstimate(
            flops=20 * count * blocks * rows * width,
            bytes_accessed=4 * blocks * rows * width * (1 + count),
            transcendentals=0,
        ),
        name="proj_slices",
    )(places, info, *inputs, *weights)


def out_slice_kernel(places, info, *refs, split, count):
    inputs, scale_ref, out_refs = refs[: -1 - count], refs[-1 - count], refs[-count:]
    members = len(inputs) // 2
    member = info[1 + count]
    mine = pl.program_id(1) == info[0]

    def write(code_refs):
        scale = scale_ref[...].astype(bf16)
        for t, code_ref in enumerate(code_refs):
            first = pl.multiple_of(jnp.bitwise_xor(member, t) * split, 128)
            for s, out_ref in enumerate(out_refs):
                out_ref[:, pl.ds(first, split)] = slice_values(code_ref[0], info[1 + s]) * scale

    pl.when(mine)(lambda: write(inputs[:members]))
    pl.when(jnp.logical_not(mine))(lambda: write(inputs[members:]))


def out_slices(own, other, places, info, scale, count):
    blocks, rows, split = own[0].shape
    width = split * len(own)
    inputs = list(own) + list(other)
    grid_spec = pltpu.PrefetchScalarGridSpec(
        num_scalar_prefetch=2,
        grid=(blocks, 2),
        in_specs=[pl.BlockSpec((1, rows, split), lambda k, j, p, i: (k, 0, 0))] * len(inputs)
        + [pl.BlockSpec((rows, 1), lambda k, j, p, i: (p[k], 0))],
        out_specs=[pl.BlockSpec((rows, width), lambda k, j, p, i: (p[k], j))] * count,
    )
    return pl.pallas_call(
        functools.partial(out_slice_kernel, split=split, count=count),
        grid_spec=grid_spec,
        out_shape=[jax.ShapeDtypeStruct((blocks * rows, 2 * width), bf16)] * count,
        compiler_params=pltpu.CompilerParams(vmem_limit_bytes=VMEM_LIMIT),
        cost_estimate=pl.CostEstimate(
            flops=20 * count * blocks * rows * width,
            bytes_accessed=4 * blocks * rows * width * (1 + count),
            transcendentals=0,
        ),
        name="out_slices",
    )(places, info, *inputs, scale)


def piece_at(j, steps, block):
    half = steps // 2
    return j + j // half * half + block * half


def own_slice_kernel(pieces, info, code_ref, row_ref, col_ref, *out_refs):
    count = len(out_refs) // 3
    for m in range(3):
        codes = code_ref[m].astype(f32).astype(bf16)
        scale = (row_ref[m] if m < 2 else col_ref[...]).astype(bf16)
        for s in range(count):
            out_refs[m * count + s][...] = slice_values(codes, info[1 + s]) * scale


def own_slices(codes, pieces, info, row_scale, col_scale, count):
    three, rows, cols = codes.shape
    steps = pieces.shape[0]
    piece = rows // steps
    grid_spec = pltpu.PrefetchScalarGridSpec(
        num_scalar_prefetch=2,
        grid=(steps,),
        in_specs=[
            pl.BlockSpec((three, piece, cols), lambda j, p, i: (0, p[j], 0)),
            pl.BlockSpec((2, piece, 1), lambda j, p, i: (0, piece_at(j, steps, 0), 0)),
            pl.BlockSpec((1, cols), lambda j, p, i: (0, 0)),
        ],
        out_specs=[pl.BlockSpec((piece, cols), lambda j, p, i: (piece_at(j, steps, 0), 0))]
        * (three * count),
    )
    return pl.pallas_call(
        own_slice_kernel,
        grid_spec=grid_spec,
        out_shape=[jax.ShapeDtypeStruct((2 * rows, cols), bf16)] * (three * count),
        compiler_params=pltpu.CompilerParams(vmem_limit_bytes=VMEM_LIMIT),
        cost_estimate=pl.CostEstimate(
            flops=10 * count * codes.size,
            bytes_accessed=codes.size * (4 + 2 * count),
            transcendentals=0,
        ),
        name="own_slices",
    )(pieces, info, codes, row_scale, col_scale)


def partner_slice_kernel(info, *refs, steps, count):
    piece_refs, scale_ref, out_refs = refs[:steps], refs[steps], refs[steps + 1 + count :]
    for j in range(steps):

        @pl.when(pl.program_id(0) == j)
        def _():
            codes = piece_refs[j][...]
            scale = scale_ref[...].astype(bf16)
            for s, out_ref in enumerate(out_refs):
                out_ref[...] = slice_values(codes, info[1 + s]) * scale


def partner_slices(pieces, info, scale, by_column, weights):
    steps = len(pieces)
    count = len(weights)
    piece, cols = pieces[0].shape
    if by_column:
        scale_spec = pl.BlockSpec((1, cols), lambda j, i: (0, 0))
    else:
        scale_spec = pl.BlockSpec((piece, 1), lambda j, i: (piece_at(j, steps, 1), 0))
    grid_spec = pltpu.PrefetchScalarGridSpec(
        num_scalar_prefetch=1,
        grid=(steps,),
        in_specs=[pl.BlockSpec((piece, cols), lambda j, i: (0, 0))] * steps
        + [scale_spec]
        + [pl.BlockSpec(memory_space=pl.ANY)] * count,
        out_specs=[pl.BlockSpec((piece, cols), lambda j, i: (piece_at(j, steps, 1), 0))] * count,
    )
    return pl.pallas_call(
        functools.partial(partner_slice_kernel, steps=steps, count=count),
        grid_spec=grid_spec,
        out_shape=[jax.ShapeDtypeStruct(w.shape, bf16) for w in weights],
        input_output_aliases={2 + steps + s: s for s in range(count)},
        compiler_params=pltpu.CompilerParams(vmem_limit_bytes=VMEM_LIMIT),
        cost_estimate=pl.CostEstimate(
            flops=10 * count * steps * piece * cols,
            bytes_accessed=2 * (1 + count) * steps * piece * cols,
            transcendentals=0,
        ),
        name="partner_slices",
    )(info, *pieces, scale, *weights)


def unpack_kernel(pieces, *refs, parts):
    first = 0
    for ref in refs[:parts]:
        width = ref.shape[1]
        refs[-1][0, :, first : first + width] = ref[...].astype(f32)
        first += width


def unpack(grads, pieces, matrix, held):
    steps = pieces.shape[0]
    rows = grads[0].shape[0]
    cols = sum(g.shape[1] for g in grads)
    piece = rows // steps
    grid_spec = pltpu.PrefetchScalarGridSpec(
        num_scalar_prefetch=1,
        grid=(steps,),
        in_specs=[pl.BlockSpec((piece, g.shape[1]), lambda j, p: (j, 0)) for g in grads]
        + [pl.BlockSpec(memory_space=pl.ANY)] * len(held),
        out_specs=pl.BlockSpec((1, piece, cols), lambda j, p: (matrix, p[j], 0)),
    )
    return pl.pallas_call(
        functools.partial(unpack_kernel, parts=len(grads)),
        grid_spec=grid_spec,
        out_shape=jax.ShapeDtypeStruct((3, rows, cols), f32),
        input_output_aliases={1 + len(grads): 0} if held else {},
        compiler_params=pltpu.CompilerParams(vmem_limit_bytes=VMEM_LIMIT),
        cost_estimate=pl.CostEstimate(
            flops=rows * cols, bytes_accessed=6 * rows * cols, transcendentals=0
        ),
        name="unpack",
    )(pieces, *grads, *held)


def tile_of(size):
    return 256 if size % 256 == 0 else size


def tiles_of(size, part):
    tile = tile_of(size)
    tiles = size // tile
    first_part = (tiles + 1) // 2
    if part is None or tiles == 1:
        return tile, 0, tiles
    return (tile, 0, first_part) if part == 0 else (tile, first_part, tiles - first_part)


def whole_spec(shape):
    return pl.BlockSpec(shape, lambda i: (0, 0))


def column_spec(rows, tile, first=0):
    return pl.BlockSpec((rows, tile), lambda i: (0, first + i))


def row_spec(tile, cols, first=0):
    return pl.BlockSpec((tile, cols), lambda i: (first + i, 0))


def kernel_call(kernel, grid, in_specs, out_specs, out_shape, flops, moved, name, held=()):
    inputs = len(in_specs)
    return pl.pallas_call(
        lambda *refs: kernel(*refs[:inputs], *refs[inputs + len(held) :]),
        grid=(grid,),
        in_specs=in_specs + [pl.BlockSpec(memory_space=pl.ANY)] * len(held),
        out_specs=out_specs,
        out_shape=out_shape,
        input_output_aliases={inputs + i: i for i in range(len(held))},
        compiler_params=pltpu.CompilerParams(vmem_limit_bytes=VMEM_LIMIT),
        cost_estimate=pl.CostEstimate(flops=flops, bytes_accessed=moved, transcendentals=0),
        name=name,
    )


def row_parts(rows):
    part = 512 if rows % 512 == 0 else rows
    return [slice(first, first + part) for first in range(0, rows, part)]


def open_kernel(x_ref, wg_ref, wu_ref, gate_ref, up_ref, hidden_ref):
    for part in row_parts(x_ref.shape[0]):
        x = x_ref[part]
        gate = dot(x, wg_ref[...], NT)
        up = dot(x, wu_ref[...], NT)
        gate_ref[part] = gate
        up_ref[part] = up
        hidden_ref[part] = (gate * (0.5 + 0.5 * gelu_parts(gate)) * up).astype(bf16)


def open_forward(x, gate_weights, up_weights, part, held=()):
    rows, depth = x.shape
    hidden = gate_weights.shape[0]
    tile, first, tiles = tiles_of(hidden, part)
    if held and tiles * tile == hidden:
        return list(held)
    return kernel_call(
        open_kernel,
        tiles,
        [whole_spec(x.shape)] + [row_spec(tile, depth, first)] * 2,
        [column_spec(rows, tile, first)] * 3,
        [jax.ShapeDtypeStruct((rows, hidden), t) for t in (f32, f32, bf16)],
        4 * rows * depth * tile * tiles,
        2 * rows * depth + tiles * tile * (4 * depth + 10 * rows),
        "open_forward",
        held,
    )(x, gate_weights, up_weights, *held)


def open_back_kernel(x_ref, wd_ref, gate_ref, up_ref, grad_gate_ref, grad_up_ref):
    for part in row_parts(x_ref.shape[0]):
        grad = dot(x_ref[part], wd_ref[...], NT)
        gate = gate_ref[part]
        square = gate * gate
        bounded = jnp.tanh(gate * (gelu_coeff + (0.044715 * gelu_coeff) * square))
        half = 0.5 + 0.5 * bounded
        steep = (0.5 * gelu_coeff) + (1.5 * 0.044715 * gelu_coeff) * square
        slope = half + gate * (1.0 - bounded * bounded) * steep
        grad_gate_ref[part] = (grad * up_ref[part] * slope).astype(bf16)
        grad_up_ref[part] = (grad * (gate * half)).astype(bf16)


def open_back(x, down_weights, gate, up, part, held=()):
    rows, depth = x.shape
    hidden = down_weights.shape[0]
    tile, first, tiles = tiles_of(hidden, part)
    if held and tiles * tile == hidden:
        return list(held)
    return kernel_call(
        open_back_kernel,
        tiles,
        [whole_spec(x.shape), row_spec(tile, depth, first)] + [column_spec(rows, tile, first)] * 2,
        [column_spec(rows, tile, first)] * 2,
        [jax.ShapeDtypeStruct((rows, hidden), bf16)] * 2,
        2 * rows * depth * tile * tiles,
        2 * rows * depth + tiles * tile * (2 * depth + 12 * rows),
        "open_back",
        held,
    )(x, down_weights, gate, up, *held)


def input_back_kernel(gate_ref, up_ref, wg_ref, wu_ref, out_ref):
    out_ref[...] = (
        dot(gate_ref[...], wg_ref[...], NN) + dot(up_ref[...], wu_ref[...], NN)
    ).astype(bf16)


def input_back(grad_gate, grad_up, gate_weights, up_weights, part, held=()):
    rows, hidden = grad_gate.shape
    depth = gate_weights.shape[1]
    tile, first, tiles = tiles_of(depth, part)
    if held and tiles * tile == depth:
        return list(held)
    return kernel_call(
        input_back_kernel,
        tiles,
        [whole_spec(grad_gate.shape)] * 2 + [column_spec(hidden, tile, first)] * 2,
        [column_spec(rows, tile, first)],
        [jax.ShapeDtypeStruct((rows, depth), bf16)],
        4 * rows * hidden * tile * tiles,
        4 * rows * hidden + tiles * tile * (4 * hidden + 2 * rows),
        "input_back",
        held,
    )(grad_gate, grad_up, gate_weights, up_weights, *held)


def weight_kernel(*refs, count, tiles):
    keep_ref, send_ref = refs[-2:]
    total = dot(refs[0][...], refs[count][...], TN)
    for s in range(1, count):
        total = total + dot(refs[s][...], refs[count + s][...], TN)
    total = total.astype(bf16)
    if tiles == 1:
        half = keep_ref.shape[0]
        keep_ref[...] = total[:half]
        send_ref[...] = total[half:]
        return
    step = pl.program_id(0)

    @pl.when(step < tiles // 2)
    def _():
        keep_ref[...] = total

    @pl.when(step >= tiles // 2)
    def _():
        send_ref[...] = total


def weight_back(lefts, rights):
    count = len(lefts)
    rows, hidden = lefts[0].shape
    depth = rights[0].shape[1]
    tile = 384 if hidden % 768 == 0 else hidden
    tiles = hidden // tile
    half = max(tiles // 2, 1)
    out = (tile if tiles > 1 else hidden // 2, depth)
    return kernel_call(
        functools.partial(weight_kernel, count=count, tiles=tiles),
        tiles,
        [column_spec(rows, tile)] * count + [whole_spec((rows, depth))] * count,
        [
            pl.BlockSpec(out, lambda i: (jnp.minimum(i, half - 1), 0)),
            pl.BlockSpec(out, lambda i: (jnp.maximum(i - half, 0), 0)),
        ],
        [jax.ShapeDtypeStruct((hidden // 2, depth), bf16)] * 2,
        2 * count * rows * depth * hidden,
        2 * count * rows * (hidden + depth) + 2 * hidden * depth,
        "weight_back",
    )(*lefts, *rights)


def fixed_spec(shape):
    return pl.BlockSpec(shape, lambda i: (0,) * len(shape))


def join_kernel(att_ref, w_ref, x_ref, gain_ref, next_ref, branch_ref, mid_ref, normed_ref, sum_ref):
    step = pl.program_id(0)
    heads, _, cols = att_ref.shape
    tile = w_ref.shape[0]
    total = dot(att_ref[0], w_ref[:, :cols], NT)
    for h in range(1, heads):
        total = total + dot(att_ref[h], w_ref[:, h * cols : (h + 1) * cols], NT)
    sum_ref[:, pl.ds(pl.multiple_of(step * tile, 128), tile)] = total

    @pl.when(step == pl.num_programs(0) - 1)
    def _():
        value = sum_ref[...]
        mid = x_ref[...].astype(f32) + value * norm_factor(value) * gain_ref[...]
        branch_ref[...] = value
        mid_ref[...] = mid
        normed_ref[...] = (mid * norm_factor(mid) * next_ref[...]).astype(bf16)


def join_rows(attended, weights, x, gain, next_gain):
    rows, depth = x.shape
    tile = tile_of(depth)
    return pl.pallas_call(
        join_kernel,
        grid=(depth // tile,),
        in_specs=[
            fixed_spec(attended.shape),
            row_spec(tile, weights.shape[1]),
            fixed_spec(x.shape),
            fixed_spec((1, depth)),
            fixed_spec((1, depth)),
        ],
        out_specs=[fixed_spec((rows, depth))] * 3,
        out_shape=[jax.ShapeDtypeStruct((rows, depth), t) for t in (f32, f32, bf16)],
        scratch_shapes=[pltpu.VMEM((rows, depth), f32)],
        compiler_params=pltpu.CompilerParams(vmem_limit_bytes=VMEM_LIMIT),
        cost_estimate=pl.CostEstimate(
            flops=2 * rows * weights.size,
            bytes_accessed=2 * weights.size + 12 * rows * depth,
            transcendentals=0,
        ),
        name="join_rows",
    )(attended, weights, x, gain[None], next_gain[None])


def finish_kernel(part_ref, a_ref, b_ref, mid_ref, cot_ref, gain_ref, out_ref, grad_ref, dg_ref):
    value = part_ref[...].astype(f32) + a_ref[...].astype(f32) + b_ref[...].astype(f32)
    factor = norm_factor(value)
    gain = gain_ref[...]
    out_ref[...] = (mid_ref[...] + value * factor * gain).astype(bf16)
    grad, dg = norm_back(value, factor, gain, cot_ref[...].astype(f32))
    grad_ref[...] = grad.astype(bf16)
    dg_ref[...] = dg


def finish_rows(part, a, b, mid, cotangent, gain):
    rows, depth = mid.shape
    spec = fixed_spec((rows, depth))
    return pl.pallas_call(
        finish_kernel,
        grid=(1,),
        in_specs=[spec] * 5 + [fixed_spec((1, depth))],
        out_specs=[spec, spec, fixed_spec((1, depth))],
        out_shape=[
            jax.ShapeDtypeStruct((rows, depth), bf16),
            jax.ShapeDtypeStruct((rows, depth), bf16),
            jax.ShapeDtypeStruct((1, depth), f32),
        ],
        compiler_params=pltpu.CompilerParams(vmem_limit_bytes=VMEM_LIMIT),
        cost_estimate=pl.CostEstimate(
            flops=20 * rows * depth, bytes_accessed=16 * rows * depth, transcendentals=0
        ),
        name="finish_rows",
    )(part, a, b, mid, cotangent, gain[None])


def branch_back_kernel(
    part_ref,
    a_ref,
    b_ref,
    mid_ref,
    branch_ref,
    cot_ref,
    mlp_gain_ref,
    gain_ref,
    w_ref,
    grad_mid_ref,
    grad_ref,
    send_ref,
    mlp_dg_ref,
    dg_ref,
    held_ref,
):
    @pl.when(pl.program_id(0) == 0)
    def _():
        normed = part_ref[...].astype(f32) + a_ref[...].astype(f32) + b_ref[...].astype(f32)
        mid = mid_ref[...]
        grad, dg = norm_back(mid, norm_factor(mid), mlp_gain_ref[...], normed)
        mlp_dg_ref[...] = dg
        grad_mid = cot_ref[...].astype(f32) + grad
        grad_mid_ref[...] = grad_mid
        branch = branch_ref[...]
        grad, dg = norm_back(branch, norm_factor(branch), gain_ref[...], grad_mid)
        dg_ref[...] = dg
        held_ref[...] = grad.astype(bf16)
        grad_ref[...] = grad.astype(bf16)

    send_ref[0] = dot(held_ref[...], w_ref[...], NN).astype(bf16)


def branch_back(part, a, b, mid, branch, cotangent, mlp_gain, gain, weights):
    rows, depth = mid.shape
    cols = PAIRED * HEAD_SIZE
    spec = fixed_spec((rows, depth))
    line = fixed_spec((1, depth))
    return pl.pallas_call(
        branch_back_kernel,
        grid=(KEY_VALUE_HEADS,),
        in_specs=[spec] * 6 + [line] * 2 + [column_spec(depth, cols)],
        out_specs=[
            spec,
            spec,
            pl.BlockSpec((1, rows, cols), lambda i: (i, 0, 0)),
            line,
            line,
        ],
        out_shape=[
            jax.ShapeDtypeStruct((rows, depth), f32),
            jax.ShapeDtypeStruct((rows, depth), bf16),
            jax.ShapeDtypeStruct((KEY_VALUE_HEADS, rows, cols), bf16),
            jax.ShapeDtypeStruct((1, depth), f32),
            jax.ShapeDtypeStruct((1, depth), f32),
        ],
        scratch_shapes=[pltpu.VMEM((rows, depth), bf16)],
        compiler_params=pltpu.CompilerParams(vmem_limit_bytes=VMEM_LIMIT),
        cost_estimate=pl.CostEstimate(
            flops=2 * rows * weights.size,
            bytes_accessed=2 * weights.size + 22 * rows * depth,
            transcendentals=0,
        ),
        name="branch_back",
    )(part, a, b, mid, branch, cotangent, mlp_gain[None], gain[None], weights)


def turn(values, cosine, sine):
    half = HEAD_SIZE // 2
    out = []
    for j in range(values.shape[1] // HEAD_SIZE):
        a = values[:, j * HEAD_SIZE : j * HEAD_SIZE + half]
        b = values[:, j * HEAD_SIZE + half : (j + 1) * HEAD_SIZE]
        out += [a * cosine - b * sine, b * cosine + a * sine]
    return jnp.concatenate(out, axis=1)


def project_kernel(x_ref, wq_ref, wk_ref, wv_ref, cos_ref, sin_ref, q_ref, kv_ref):
    x = x_ref[...]
    cosine, sine = cos_ref[...], sin_ref[...]
    scale = HEAD_SIZE ** (-0.5)
    q_ref[0] = (turn(dot(x, wq_ref[...], NN), cosine, sine) * scale).astype(bf16)
    kv_ref[0, :, :HEAD_SIZE] = turn(dot(x, wk_ref[...], NN), cosine, sine).astype(bf16)
    kv_ref[0, :, HEAD_SIZE:] = dot(x, wv_ref[...], NN).astype(bf16)


def project(normed, weights, cosine, sine):
    rows, depth = normed.shape
    cols = PAIRED * HEAD_SIZE
    first_key = QUERY_HEADS
    first_value = QUERY_HEADS + KEY_VALUE_HEADS
    whole = lambda shape: pl.BlockSpec(shape, lambda h: (0, 0))
    return pl.pallas_call(
        project_kernel,
        grid=(KEY_VALUE_HEADS,),
        in_specs=[
            whole((rows, depth)),
            pl.BlockSpec((depth, cols), lambda h: (0, h)),
            pl.BlockSpec((depth, HEAD_SIZE), lambda h: (0, first_key + h)),
            pl.BlockSpec((depth, HEAD_SIZE), lambda h: (0, first_value + h)),
            whole(cosine.shape),
            whole(sine.shape),
        ],
        out_specs=[
            pl.BlockSpec((1, rows, cols), lambda h: (h, 0, 0)),
            pl.BlockSpec((1, rows, 2 * HEAD_SIZE), lambda h: (h, 0, 0)),
        ],
        out_shape=[
            jax.ShapeDtypeStruct((KEY_VALUE_HEADS, rows, cols), bf16),
            jax.ShapeDtypeStruct((KEY_VALUE_HEADS, rows, 2 * HEAD_SIZE), bf16),
        ],
        compiler_params=pltpu.CompilerParams(vmem_limit_bytes=VMEM_LIMIT),
        cost_estimate=pl.CostEstimate(
            flops=2 * rows * weights.size, bytes_accessed=2 * weights.size, transcendentals=0
        ),
        name="project",
    )(normed, weights, weights, weights, cosine, sine)


def turn_back_kernel(*refs, count):
    q_refs, kv_refs = refs[:count], refs[count : 2 * count]
    cos_ref, sin_ref, out_ref = refs[2 * count :]
    j = pl.program_id(1)
    scale = HEAD_SIZE ** (-0.5)
    keys = KEY_VALUE_HEADS // PAIRED
    for s in range(count):
        here = pl.program_id(0) == s

        @pl.when(jnp.logical_and(here, j < KEY_VALUE_HEADS))
        def _():
            grad = q_refs[s][0].astype(f32) * scale
            out_ref[...] = turn(grad, cos_ref[...], -sin_ref[...]).astype(bf16)

        @pl.when(jnp.logical_and(here, jnp.logical_and(j >= KEY_VALUE_HEADS, j < KEY_VALUE_HEADS + keys)))
        def _():
            grad = jnp.concatenate([kv_refs[s][i, :, :HEAD_SIZE] for i in range(PAIRED)], axis=1)
            out_ref[...] = turn(grad.astype(f32), cos_ref[...], -sin_ref[...]).astype(bf16)

        @pl.when(jnp.logical_and(here, j >= KEY_VALUE_HEADS + keys))
        def _():
            out_ref[...] = jnp.concatenate(
                [kv_refs[s][i, :, HEAD_SIZE:] for i in range(PAIRED)], axis=1
            )


def turn_back(queries, pairs, cosine, sine):
    count = len(queries)
    heads, rows, cols = queries[0].shape
    keys = heads // PAIRED
    grid = (count, heads + 2 * keys)
    whole = pl.BlockSpec(cosine.shape, lambda s, j: (0, 0))
    return pl.pallas_call(
        functools.partial(turn_back_kernel, count=count),
        grid=grid,
        in_specs=[
            pl.BlockSpec((1, rows, cols), lambda s, j: (jnp.minimum(j, heads - 1), 0, 0))
        ]
        * count
        + [
            pl.BlockSpec(
                (PAIRED, rows, cols), lambda s, j: (jnp.maximum(j - heads, 0) % keys, 0, 0)
            )
        ]
        * count
        + [whole, whole],
        out_specs=pl.BlockSpec((rows, cols), lambda s, j: (s, j)),
        out_shape=jax.ShapeDtypeStruct((count * rows, grid[1] * cols), bf16),
        compiler_params=pltpu.CompilerParams(vmem_limit_bytes=VMEM_LIMIT),
        cost_estimate=pl.CostEstimate(
            flops=4 * count * rows * grid[1] * cols,
            bytes_accessed=4 * count * rows * grid[1] * cols,
            transcendentals=0,
        ),
        name="turn_back",
    )(*queries, *pairs, cosine, sine)


def tile_positions(tile, count, start, class_index, class_rows, rows):
    index = lax.broadcasted_iota(jnp.int32, (count, 1), 0)
    place = start + jnp.bitwise_and(index, tile - 1)
    shift = class_rows.bit_length() - 1
    return (
        jnp.right_shift(place, shift) * rows
        + class_index * class_rows
        + jnp.bitwise_and(place, class_rows - 1)
    )


def stack_heads(block):
    return jnp.concatenate(
        [block[:, j * HEAD_SIZE : (j + 1) * HEAD_SIZE] for j in range(PAIRED)], axis=0
    )


def key_places(group, class_index, classes, rows):
    index = lax.broadcasted_iota(jnp.int32, (1, classes * rows), 1)
    shift = rows.bit_length() - 1
    back = jnp.bitwise_and(class_index - jnp.right_shift(index, shift), classes - 1)
    return (group * classes + back) * rows + jnp.bitwise_and(index, rows - 1)


def held_block(refs, group, cols):
    return jnp.concatenate([ref[group, :, cols] for ref in refs], axis=0)


def group_range(start, tile, class_rows, classes):
    return start // class_rows // classes, (start + tile - 1) // class_rows // classes + 1


def attn_forward_kernel(info, q_ref, *refs, tile, class_rows, rows, classes):
    kv_refs = refs[:classes]
    att_ref, exact_ref, lse_ref = refs[classes:]
    start = pl.program_id(0) * tile
    free, total = group_range(start, tile, class_rows, classes)
    queries = stack_heads(q_ref[...])
    count = queries.shape[0]
    position = tile_positions(tile, count, start, info[0], class_rows, rows)

    def step(group, carry, masked):
        acc, row_sum = carry
        keys = held_block(kv_refs, group, slice(0, HEAD_SIZE))
        values = held_block(kv_refs, group, slice(HEAD_SIZE, 2 * HEAD_SIZE))
        raw = dot(queries, keys, NT)
        weight = jnp.exp(soft_cap * jnp.tanh(raw * (1.0 / soft_cap)))
        if masked:
            weight = jnp.where(
                key_places(group, info[0], classes, rows) <= position, weight, 0.0
            )
        row_sum = row_sum + jnp.sum(weight, axis=-1, keepdims=True)
        acc = acc + dot(weight.astype(bf16), values, NN)
        return acc, row_sum

    carry = (jnp.zeros((count, HEAD_SIZE), f32), jnp.zeros((count, 1), f32))
    carry = lax.fori_loop(0, free, functools.partial(step, masked=False), carry)
    acc, row_sum = lax.fori_loop(free, total, functools.partial(step, masked=True), carry)
    exact = acc / row_sum
    lse = jnp.log(row_sum)
    for j in range(PAIRED):
        cols = slice(j * HEAD_SIZE, (j + 1) * HEAD_SIZE)
        exact_ref[:, cols] = exact[j * tile : (j + 1) * tile]
        att_ref[:, cols] = exact[j * tile : (j + 1) * tile].astype(bf16)
        lse_ref[:, j * 128 : (j + 1) * 128] = jnp.broadcast_to(
            lse[j * tile : (j + 1) * tile], (tile, 128)
        )


def attn_forward(info, queries, pairs, class_rows, rows):
    count, cols = queries.shape
    classes = len(pairs)
    length = classes * pairs[0].shape[0] * rows
    tile = min(256, count)
    grid_spec = pltpu.PrefetchScalarGridSpec(
        num_scalar_prefetch=1,
        grid=(count // tile,),
        in_specs=[pl.BlockSpec((tile, cols), lambda i, c: (i, 0))]
        + [pl.BlockSpec(p.shape, lambda i, c: (0, 0, 0)) for p in pairs],
        out_specs=[
            pl.BlockSpec((tile, cols), lambda i, c: (i, 0)),
            pl.BlockSpec((tile, cols), lambda i, c: (i, 0)),
            pl.BlockSpec((tile, PAIRED * 128), lambda i, c: (i, 0)),
        ],
    )
    return pl.pallas_call(
        functools.partial(
            attn_forward_kernel, tile=tile, class_rows=class_rows, rows=rows, classes=classes
        ),
        grid_spec=grid_spec,
        out_shape=[
            jax.ShapeDtypeStruct((count, cols), bf16),
            jax.ShapeDtypeStruct((count, cols), f32),
            jax.ShapeDtypeStruct((count, PAIRED * 128), f32),
        ],
        compiler_params=pltpu.CompilerParams(vmem_limit_bytes=VMEM_LIMIT),
        cost_estimate=pl.CostEstimate(
            flops=2 * count * PAIRED * length * 2 * HEAD_SIZE,
            bytes_accessed=8 * count * cols + 4 * length * HEAD_SIZE,
            transcendentals=2 * count * PAIRED * length,
        ),
        name="attn_forward",
    )(info, queries, *pairs)


def attn_backward_kernel(info, q_ref, grad_ref, exact_ref, lse_ref, *refs, tile, class_rows, rows, classes):
    kv_refs, dq_ref = refs[:classes], refs[classes]
    dkv_refs, sum_ref = refs[classes + 1 : 2 * classes + 1], refs[2 * classes + 1]

    @pl.when(pl.program_id(0) == 0)
    def _():
        sum_ref[...] = jnp.zeros_like(sum_ref)

    start = pl.program_id(0) * tile
    free, total = group_range(start, tile, class_rows, classes)
    queries = stack_heads(q_ref[...])
    grads = stack_heads(grad_ref[...])
    count = queries.shape[0]
    delta = jnp.sum(grads.astype(f32) * stack_heads(exact_ref[...]), axis=-1, keepdims=True)
    lse = jnp.concatenate([lse_ref[:, j * 128 : j * 128 + 1] for j in range(PAIRED)], axis=0)
    position = tile_positions(tile, count, start, info[0], class_rows, rows)

    def step(group, acc, masked):
        keys = held_block(kv_refs, group, slice(0, HEAD_SIZE))
        values = held_block(kv_refs, group, slice(HEAD_SIZE, 2 * HEAD_SIZE))
        bounded = jnp.tanh(dot(queries, keys, NT) * (1.0 / soft_cap))
        probs = jnp.exp(soft_cap * bounded - lse)
        if masked:
            probs = jnp.where(key_places(group, info[0], classes, rows) <= position, probs, 0.0)
        grad_probs = dot(grads, values, NT)
        grad_raw = (probs * (grad_probs - delta) * (1.0 - bounded * bounded)).astype(bf16)
        sum_ref[group, :, HEAD_SIZE:] += dot(probs.astype(bf16), grads, TN)
        sum_ref[group, :, :HEAD_SIZE] += dot(grad_raw, queries, TN)
        return acc + dot(grad_raw, keys, NN)

    acc = jnp.zeros((count, HEAD_SIZE), f32)
    acc = lax.fori_loop(0, free, functools.partial(step, masked=False), acc)
    acc = lax.fori_loop(free, total, functools.partial(step, masked=True), acc)
    for j in range(PAIRED):
        dq_ref[:, j * HEAD_SIZE : (j + 1) * HEAD_SIZE] = acc[j * tile : (j + 1) * tile].astype(bf16)

    @pl.when(pl.program_id(0) == pl.num_programs(0) - 1)
    def _():
        for h, ref in enumerate(dkv_refs):
            ref[...] = sum_ref[:, h * rows : (h + 1) * rows, :].astype(bf16)


def attn_backward(info, queries, pairs, grads, exact, lse, class_rows, rows):
    count, cols = queries.shape
    classes = len(pairs)
    groups = pairs[0].shape[0]
    length = classes * groups * rows
    tile = min(256, count)
    row_spec = pl.BlockSpec((tile, cols), lambda i, c: (i, 0))
    pair_specs = [pl.BlockSpec(p.shape, lambda i, c: (0, 0, 0)) for p in pairs]
    grid_spec = pltpu.PrefetchScalarGridSpec(
        num_scalar_prefetch=1,
        grid=(count // tile,),
        in_specs=[
            row_spec,
            row_spec,
            row_spec,
            pl.BlockSpec((tile, PAIRED * 128), lambda i, c: (i, 0)),
        ]
        + pair_specs,
        out_specs=[row_spec] + pair_specs,
        scratch_shapes=[pltpu.VMEM((groups, classes * rows, 2 * HEAD_SIZE), f32)],
    )
    return pl.pallas_call(
        functools.partial(
            attn_backward_kernel, tile=tile, class_rows=class_rows, rows=rows, classes=classes
        ),
        grid_spec=grid_spec,
        out_shape=[jax.ShapeDtypeStruct((count, cols), bf16)]
        + [jax.ShapeDtypeStruct(p.shape, bf16) for p in pairs],
        compiler_params=pltpu.CompilerParams(vmem_limit_bytes=VMEM_LIMIT),
        cost_estimate=pl.CostEstimate(
            flops=5 * count * PAIRED * length * 2 * HEAD_SIZE,
            bytes_accessed=10 * count * cols + 8 * length * HEAD_SIZE,
            transcendentals=2 * count * PAIRED * length,
        ),
        name="attn_backward",
    )(info, queries, grads, exact, lse, *pairs)


def per_device(
    tokens,
    cotangent,
    widths,
    attn_codes,
    attn_exps,
    out_exps,
    mlp_codes,
    gate_exps,
    down_exps,
    gain_attn,
    gain_post_attn,
    gain_mlp,
    gain_post_mlp,
):
    wide = lax.axis_size("wide")
    seq_size = lax.axis_size("seq")
    wide_index = lax.axis_index("wide")
    seq_index = lax.axis_index("seq")
    side = seq_index % 2
    is_low = side == 0
    members = seq_size // 2
    member = seq_index // 2
    half_wide = wide // 2
    place = ring_place(wide_index, wide)
    count, rows, model_dim = tokens.shape
    classes = wide // KEY_VALUE_HEADS
    class_rows = rows // classes
    class_index = wide_index % classes
    head_cols = PAIRED * HEAD_SIZE
    proj_cols = attn_exps.shape[0]
    half_proj = proj_cols // 2
    half_out = (attn_codes.shape[1] - proj_cols) // 2
    split_out = half_out // members
    attn_rows = attn_codes.shape[0]
    hidden = mlp_codes.shape[1]
    offsets = ring_offsets(wide)
    order = {o: i for i, o in enumerate(ring_offsets(half_wide))}
    seqs = range(count)
    seq_bits = [1 << i for i in range(seq_size.bit_length() - 1)]
    far_bits = list(reversed(seq_bits[1:]))
    clock = Clock(widths)

    def index_at(offset):
        return ring_index(jnp.mod(place + offset, wide), wide)

    places = jnp.stack([index_at(o) for o in offsets]).astype(jnp.int32)
    info = jnp.concatenate(
        [side[None].astype(jnp.int32), widths, member[None].astype(jnp.int32)]
    )
    class_info = class_index[None].astype(jnp.int32)
    column_scale = inverse_powers(attn_exps)[None, :]
    output_scale = inverse_powers(out_exps)[:, None]

    relative = [0]
    for bit in reversed(seq_bits):
        relative = relative + [r | bit for r in relative]
    pieces = jnp.stack([jnp.bitwise_xor(seq_index, r) for r in relative]).astype(jnp.int32)
    piece_rows = hidden // seq_size
    partner = jnp.bitwise_xor(wide_index, half_wide)
    gate_scale = inverse_powers(gate_exps)
    row_scale = jnp.concatenate(
        [
            lax.dynamic_slice_in_dim(
                gate_scale, block * hidden + pieces[j] * piece_rows, piece_rows, 1
            )
            for group in (range(seq_size // 2), range(seq_size // 2, seq_size))
            for block in (wide_index, partner)
            for j in group
        ],
        axis=1,
    )[:, :, None]
    down_scale = inverse_powers(down_exps)[None, :]

    def columns(first, size):
        return lax.dynamic_slice_in_dim(attn_codes, first, size, 1)

    payload = jnp.concatenate(
        [
            columns(side * half_proj, half_proj),
            columns(proj_cols + side * half_out + member * split_out, split_out),
        ],
        axis=1,
    ).astype(bf16)
    piece_codes = lax.dynamic_slice_in_dim(mlp_codes, seq_index * piece_rows, piece_rows, 1)
    inputs = [tokens[s].astype(f32) for s in seqs]
    cosine, sine = rotary_rows(wide_index * rows + jnp.arange(rows))

    blocks, others = [clock.hold(payload)], []
    proj_weights = []

    def slice_more(first, last):
        return proj_slices(
            blocks[first:last],
            others[first:last],
            places[first:last],
            info,
            column_scale,
            half_proj,
            proj_weights,
            wide,
            count,
        )

    a = b = blocks[0]
    sliced = 0
    steps = half_wide
    for k in range(1, steps + 1):
        if k == steps:
            a, b = halves(a)[0], halves(b)[1]
        passed = [swap(v, "seq", 1) for v in blocks[len(others) :]]
        a, b = hop(a, b, wide)
        work = []
        if k == 1:
            work = own_slices(mlp_codes, pieces, info, row_scale, down_scale, count)
            a, b, *work = clock.sync(a, b, *passed, *work)
            passed, own_weights = work[: len(passed)], work[len(passed) :]
        elif k == 2:
            work = [piece_codes[m].astype(bf16) for m in range(3)]
            for s in seqs:
                factor = norm_factor(clock.hold(inputs[s]))
                work += [factor, (inputs[s] * factor * gain_attn).astype(bf16)]
            a, b, *work = clock.sync(a, b, *passed, *work)
            passed, work = work[: len(passed)], work[len(passed) :]
            sends, work = work[:3], work[3:]
            input_factor, normed = work[0::2], work[1::2]
        else:
            more = len(others)
            work = slice_more(sliced, more) if more > sliced else []
            a, b, *work = clock.sync(a, b, *passed, *work)
            passed, work = work[: len(passed)], work[len(passed) :]
            if work:
                proj_weights, sliced = list(work), more
        others += passed
        blocks += [a, b] if k < steps else [jnp.concatenate([a, b], axis=0)]

    def exchange(m):
        return swap(clock.hold(sends[m]), "wide", half_wide)

    def share(held, bits):
        for bit in bits:
            held = held + [swap(value, "seq", bit) for value in held]
        return held

    def partner_weights(m, held):
        scale = row_scale[m] if m < 2 else down_scale
        return partner_slices(
            held, info, scale, m == 2, own_weights[m * count : (m + 1) * count]
        )

    received = exchange(0)
    others += [swap(clock.hold(v), "seq", 1) for v in blocks[len(others) :]]
    proj_weights = slice_more(sliced, wide)
    query_send, pair_send = [], []
    for s in seqs:
        query, pair = project(normed[s], proj_weights[s], cosine, sine)
        query_send.append(query.reshape(wide, class_rows, head_cols))
        pair_send.append(pair)
    sent = clock.sync(received, *query_send, *pair_send)
    received, sent = sent[0], sent[1:]
    query_send, pair_send = sent[:count], sent[count:]

    def spread(pair):
        held = [pair]
        for _ in range(classes - 1):
            held.append(class_ring(held[-1]))
        return held[1:]

    def two_parts(value):
        cut = value.shape[0] // 2
        return value[:cut], value[cut:]

    attended_send, exact, lse, queries, pairs = [], [], [], [], []

    def attend(s):
        out, full, log_sum = attn_forward(class_info, queries[s], pairs[s], class_rows, rows)
        return [out.reshape(wide, class_rows, head_cols), full, log_sum]

    def keep_attend(work):
        attended_send.append(work[0])
        exact.append(work[1])
        lse.append(work[2])

    pair_first = heads_all_to_all(clock.hold(pair_send[0]))
    own_out = jnp.stack([clock.hold(v)[:, half_proj:] for v in blocks])
    other_out = jnp.stack([clock.hold(v)[:, half_proj:] for v in others])
    pair_first, own_out, other_out = clock.sync(pair_first, own_out, other_out)
    out_own = share([clock.hold(own_out)], far_bits)
    moved = spread(pair_first)
    pair_last, *work = clock.sync(heads_all_to_all(clock.hold(pair_send[1])), *moved)
    pairs.append([pair_first] + work)
    part_a, part_b = two_parts(pair_last)
    query = all_to_all(clock.hold(query_send[0]))
    query, *work = clock.sync(query, *spread(part_a), *out_own)
    moved_a, out_own = work[: classes - 1], work[classes - 1 :]
    queries.append(query.reshape(wide * class_rows, head_cols))
    moved_b = spread(clock.hold(part_b))
    query = all_to_all(clock.hold(query_send[1]))
    out_other = [swap(v, "seq", 1) for v in out_own[1:]]
    gate_held = share([clock.hold(received)], far_bits)
    query, *work = clock.sync(query, *moved_b, *out_other, *attend(0))
    moved_b, work = work[: classes - 1], work[classes - 1 :]
    out_other, work = [other_out] + work[: len(out_other)], work[len(out_other) :]
    keep_attend(work)
    queries.append(query.reshape(wide * class_rows, head_cols))
    pairs.append(
        [pair_last] + [jnp.concatenate([x, y], axis=0) for x, y in zip(moved_a, moved_b)]
    )

    attended, heads_back, branch, middle, normed_mlp = [], [], [], [], []

    def heads_to_rows(values):
        split = values.reshape(KEY_VALUE_HEADS, rows, head_cols)
        return jnp.transpose(split, (1, 0, 2)).reshape(rows, KEY_VALUE_HEADS * head_cols)

    def join(s):
        return join_rows(
            heads_back[s], out_weights[s], tokens[s], gain_post_attn, gain_mlp
        )

    def keep_join(work):
        for held, value in zip((branch, middle, normed_mlp), work):
            held.append(value)

    for s in seqs:
        back = all_to_all(clock.hold(attended_send[s]))
        if s == 0:
            out_weights = out_slices(out_own, out_other, places, info, output_scale, count)
            back, *work = clock.sync(back, *gate_held, *out_weights, *attend(count - 1))
            gate_held, work = work[: len(gate_held)], work[len(gate_held) :]
            out_weights, work = work[:count], work[count:]
            keep_attend(work)
        else:
            gate_held = share(gate_held, seq_bits[:1])
            back, *work = clock.sync(back, *gate_held, *join(s - 1))
            gate_held, work = work[: len(gate_held)], work[len(gate_held) :]
            keep_join(work)
        heads_back.append(back.reshape(KEY_VALUE_HEADS, rows, head_cols))
        attended.append(heads_to_rows(back))

    received = exchange(1)
    gate_weights = partner_weights(0, [clock.hold(v) for v in gate_held])
    received, *work = clock.sync(received, *gate_weights, *join(count - 1))
    gate_weights, work = work[:count], work[count:]
    keep_join(work)

    def blocks_of(part):
        return lambda o: part[order[o] * rows : (order[o] + 1) * rows]

    gathered, gate, up, hidden_rows, mixed, parts = [], [], [], [], [], []

    def open_part(s, part, held=()):
        group = clock.hold(gathered[s])
        return open_forward(group, gate_weights[s], up_weights[s], part, held)

    def keep_open(work):
        gate.append(work[0])
        up.append(work[1])
        hidden_rows.append(work[2])

    def mix(s):
        return dot(clock.hold(hidden_rows[s]), down_weights[s], NN).astype(bf16)

    up_held = share([clock.hold(received)], far_bits)
    received, *up_held = clock.sync(exchange(2), *up_held)

    def beside_first(step):
        nonlocal up_held
        if step == 0:
            up_held = share(up_held, seq_bits[:1])
            return tuple(up_held) + tuple(share([clock.hold(received)], far_bits))
        if step == 1:
            return tuple(partner_weights(1, [clock.hold(v) for v in up_held]))
        return ()

    a = b = clock.hold(normed_mlp[0])
    blocks = [a]
    for k in range(1, half_wide // 2 + 1):
        if k == half_wide // 2:
            a, b = halves(a)[0], halves(b)[1]
        if k == 2:
            down_held = share(down_held, seq_bits[:1])
        work = beside_first(k - 1) + (tuple(down_held) if k == 2 else ())
        a, b = hop(a, b, half_wide)
        a, b, *work = clock.sync(a, b, *work)
        if k == 1:
            up_held, down_held = work[: len(up_held)], work[len(up_held) :]
        elif k == 2:
            up_weights, down_held = work[:count], work[count:]
        blocks += [a, b]
    gathered.append(jnp.concatenate(blocks, axis=0))

    def beside_second(step):
        if step == 0:
            return open_part(0, None)
        if step == 1:
            return partner_weights(2, [clock.hold(v) for v in down_held])
        return ()

    a = b = clock.hold(normed_mlp[1])
    blocks = [a]
    for k in range(1, half_wide // 2 + 1):
        if k == half_wide // 2:
            a, b = halves(a)[0], halves(b)[1]
        work = beside_second(k - 1)
        a, b = hop(a, b, half_wide)
        a, b, *work = clock.sync(a, b, *work)
        if k == 1:
            keep_open(work)
        elif k == 2:
            down_weights = work
        blocks += [a, b]
    gathered.append(jnp.concatenate(blocks, axis=0))
    parts.append(clock.sync(mix(0))[0])

    layer_out, grad_mixed, gain_fourth = [], [], 0.0

    def finish(s):
        nonlocal gain_fourth
        out, grad, gain = finish_rows(*mixed[s], middle[s], cotangent[s], gain_post_mlp)
        layer_out.append(out)
        grad_mixed.append(grad)
        gain_fourth = gain_fourth + gain

    grad_group, grad_gate, grad_up, grad_parts, grad_normed_mlp = [], [], [], [], []

    def back_hidden(s, part, held=()):
        group = clock.hold(grad_group[s])
        return open_back(group, down_weights[s], gate[s], up[s], part, held)

    def back_input(s, part, held=()):
        grad = clock.hold(grad_gate[s])
        return input_back(grad, grad_up[s], gate_weights[s], up_weights[s], part, held)

    def keep_back(work):
        grad_gate.append(work[0])
        grad_up.append(work[1])

    def first_sum(part):
        a, b = hop(*halves(clock.hold(blocks_of(part)(half_wide // 2))), half_wide)
        return a, b

    def rest_sum(part, a, b, beside=lambda step: ()):
        part_of = blocks_of(part)
        other = []
        for k in range(half_wide // 2 - 1, 0, -1):
            if k == half_wide // 2 - 1:
                a = add_first(part_of(k), a)
                b = add_last(part_of(-k), b)
            else:
                a = low_sum(part_of(k), a)
                b = low_sum(part_of(-k), b)
            work = beside(half_wide // 2 - 1 - k)
            a, b = hop(a, b, half_wide)
            a, b, *work = clock.sync(a, b, *work)
            other.append(work)
        return (part, a, b), other

    a, b = first_sum(parts[0])
    a, b, *opened = clock.sync(a, b, *open_part(1, 0))
    total, work = rest_sum(
        parts[0], a, b, lambda step: () if step else tuple(open_part(1, 1, opened))
    )
    keep_open(work[0])
    mixed.append(total)
    finish(0)
    parts.append(mix(1))
    blocks, work = ring_gather(
        clock, grad_mixed[0], half_wide, lambda k: (parts[1],) if k == 0 else ()
    )
    parts[1] = work[0][0]
    grad_group.append(jnp.concatenate(blocks, axis=0))
    a, b = first_sum(parts[1])
    a, b, *opened = clock.sync(a, b, *back_hidden(0, 0))

    def beside_last(step):
        if step:
            return ()
        keep_back(back_hidden(0, 1, opened))
        return (grad_gate[0], grad_up[0], *input_back(
            grad_gate[0], grad_up[0], gate_weights[0], up_weights[0], 0, ()
        ))

    total, work = rest_sum(parts[1], a, b, beside_last)
    grad_gate[0], grad_up[0], opened = work[0][0], work[0][1], work[0][2:]
    mixed.append(total)
    finish(1)
    blocks, work = ring_gather(
        clock, grad_mixed[1], half_wide, lambda k: () if k else tuple(back_input(0, 1, opened))
    )
    grad_parts.append(work[0][0])
    grad_group.append(jnp.concatenate(blocks, axis=0))

    def weight_sum(lefts, rights):
        lefts = [clock.hold(v) for v in lefts]
        return [v.reshape(2, hidden // 2, model_dim) for v in weight_back(lefts, rights)]

    def part_sum(grad, bit):
        split = grad.reshape(2, 2, grad.shape[1] // 2, model_dim)
        return low_sum(split[:, 0], swap(split[:, 1], "seq", bit))

    grad_middle, grad_branch, grad_send = [], [], []
    gain_third = gain_second = 0.0

    def back_branch(s):
        nonlocal gain_third, gain_second
        grad_mid, grad, send, third, second = branch_back(
            *[clock.hold(v) for v in grad_normed_mlp[s]],
            middle[s],
            branch[s],
            cotangent[s],
            gain_mlp,
            gain_post_attn,
            out_weights[s],
        )
        gain_third = gain_third + third
        gain_second = gain_second + second
        return [grad_mid, grad, send.reshape(wide, class_rows, head_cols)]

    def keep_branch(work):
        grad_middle.append(work[0])
        grad_branch.append(work[1])
        grad_send.append(work[2])

    a, b = first_sum(grad_parts[0])
    a, b, *opened = clock.sync(a, b, *back_hidden(1, 0))

    def beside_back(step):
        if step:
            return ()
        keep_back(back_hidden(1, 1, opened))
        return (grad_gate[1], grad_up[1], *input_back(
            grad_gate[1], grad_up[1], gate_weights[1], up_weights[1], 0, ()
        ))

    total, work = rest_sum(grad_parts[0], a, b, beside_back)
    grad_gate[1], grad_up[1], opened = work[0][0], work[0][1], work[0][2:]
    grad_normed_mlp.append(total)
    grad_parts += clock.sync(*back_input(1, 1, opened))
    a, b = first_sum(grad_parts[1])
    a, b, *work = clock.sync(a, b, *back_branch(0))
    keep_branch(work)
    total, work = rest_sum(
        grad_parts[1],
        a,
        b,
        lambda step: () if step else tuple(weight_sum(hidden_rows, grad_group)),
    )
    down_keep, down_send = work[0]
    grad_normed_mlp.append(total)

    def attend_back(s):
        dq, *dkv = attn_backward(
            class_info,
            queries[s],
            pairs[s],
            clock.hold(grad_heads[s]),
            exact[s],
            lse[s],
            class_rows,
            rows,
        )
        return [dq.reshape(wide, class_rows, head_cols)] + dkv

    def class_sum(dkv):
        total = dkv[1 % classes]
        for step in range(2, classes + 1):
            total = low_sum(dkv[step % classes], class_ring(total))
        return total

    def far_parts(grad):
        split = grad.reshape(2, 2, grad.shape[1] // 2, model_dim)
        send = split[:, 1]
        return split[:, 0], [send[:, :, : model_dim // 2], send[:, :, model_dim // 2 :]]

    def far_move(part):
        return swap(clock.hold(part), "seq", seq_bits[1])

    def far_join(kept, moved):
        grad = low_sum(kept, jnp.concatenate(moved, axis=2))
        for bit in seq_bits[2:]:
            grad = part_sum(grad, bit)
        return grad

    grad_heads, grad_attend = [], []
    query_back, pair_back = [], []

    def heads_of(value):
        return value.reshape(wide * class_rows, head_cols)

    back = all_to_all(clock.hold(grad_send[0]))
    down_grad = low_sum(down_keep, swap(down_send, "seq", 1))
    back, down_grad, *work = clock.sync(back, down_grad, *back_branch(1))
    keep_branch(work)
    grad_heads.append(heads_of(back))
    all_normed = jnp.concatenate(normed, axis=0)
    all_attended = jnp.concatenate(attended, axis=0)
    all_branch = jnp.concatenate(grad_branch, axis=0)

    def half_dot(left, right, which, size):
        return dot(left, lax.dynamic_slice_in_dim(right, which * size, size, 1), TN)

    down_keep, down_parts = far_parts(down_grad)
    down_moved = [far_move(down_parts[0])]
    back = all_to_all(clock.hold(grad_send[1]))
    out_send = half_dot(all_branch, clock.hold(all_attended), 1 - side, half_out).astype(bf16)
    back, down_moved[0], out_send, *work = clock.sync(
        back, down_moved[0], out_send, *attend_back(0)
    )
    down_moved.append(far_move(down_parts[1]))
    grad_heads.append(heads_of(back))
    grad_attend.append(work)

    dq, *dkv = grad_attend[0]
    parts_of_pair = [two_parts(v) for v in dkv]
    out_sent = swap(out_send, "seq", 1)
    query = all_to_all(clock.hold(dq))
    pair_a = class_sum([v[0] for v in parts_of_pair])
    out_part = low_sum(
        half_dot(all_branch, clock.hold(all_attended), side, half_out), out_sent
    )
    query, pair_a, down_moved[1], out_part, *work = clock.sync(
        query, pair_a, down_moved[1], out_part, *attend_back(1)
    )
    down_grad = far_join(down_keep, down_moved)
    query_back.append(query)
    grad_attend.append(work)
    dq, *dkv = grad_attend[1]
    query = all_to_all(clock.hold(dq))
    pair_b = class_sum([clock.hold(v[1]) for v in parts_of_pair])
    out_pieces = {
        t: lax.dynamic_slice_in_dim(
            clock.hold(out_part), jnp.bitwise_xor(member, t) * split_out, split_out, 1
        )
        for t in range(members)
    }
    out_moved = []
    if members == 2:
        out_parts = [out_pieces[1][:, : split_out // 2], out_pieces[1][:, split_out // 2 :]]
        out_moved.append(swap(out_parts[0], "seq", seq_bits[1]))
    else:
        for bit in seq_bits[1:]:
            for t in sorted(out_pieces):
                if not t & (bit // 2) and t | (bit // 2) in out_pieces:
                    out_pieces[t] = low_sum(
                        out_pieces[t], swap(out_pieces.pop(t | (bit // 2)), "seq", bit)
                    )
    up_keep, up_send = weight_sum(grad_up, gathered)
    query, pair_b, down_grad, up_keep, up_send, *out_moved = clock.sync(
        query, pair_b, down_grad, up_keep, up_send, *out_moved
    )
    query_back.append(query)

    pair = heads_all_to_all(clock.hold(jnp.concatenate([pair_a, pair_b], axis=0)))
    pair_sum = class_sum([clock.hold(v) for v in dkv])
    up_grad = low_sum(up_keep, swap(up_send, "seq", 1))
    if members == 2:
        out_moved.append(swap(clock.hold(out_parts[1]), "seq", seq_bits[1]))
    pair, pair_sum, up_grad, *out_moved = clock.sync(pair, pair_sum, up_grad, *out_moved)
    out_piece = out_pieces[0]
    if out_moved:
        out_piece = low_sum(out_piece, jnp.concatenate(out_moved, axis=1))
    pair_back.append(pair)
    up_keep, up_parts = far_parts(up_grad)
    up_moved = [far_move(up_parts[0])]
    pair = heads_all_to_all(clock.hold(pair_sum))
    gate_keep, gate_send = weight_sum(grad_gate, gathered)
    pair, up_moved[0], gate_keep, gate_send = clock.sync(pair, up_moved[0], gate_keep, gate_send)
    up_moved.append(far_move(up_parts[1]))
    pair_back.append(pair)

    def column_parts(value, count):
        width = value.shape[1] // count
        return [value[:, i * width : (i + 1) * width] for i in range(count)]

    def exchange_grad(part):
        return swap(clock.hold(part), "wide", half_wide)

    down_own = column_parts(down_grad[0], 3)
    down_send = column_parts(down_grad[1], 3)
    gate_moved = swap(gate_send, "seq", 1)
    moved, grad_proj = clock.sync(
        exchange_grad(down_send[0]),
        turn_back(
            [v.reshape(KEY_VALUE_HEADS, rows, head_cols) for v in query_back],
            pair_back,
            cosine,
            sine,
        ),
    )
    down_other = [moved]
    moved = exchange_grad(down_send[1])
    proj_send = half_dot(all_normed, clock.hold(grad_proj), 1 - side, half_proj).astype(bf16)
    moved, gate_moved, up_moved[1], proj_send = clock.sync(
        moved, gate_moved, up_moved[1], proj_send
    )
    down_other.append(moved)
    up_grad = far_join(up_keep, up_moved)
    moved = exchange_grad(down_send[2])
    proj_sent = swap(proj_send, "seq", 1)
    gate_grad = low_sum(gate_keep, gate_moved)
    moved, proj_sent, up_grad, gate_grad = clock.sync(moved, proj_sent, up_grad, gate_grad)
    down_other.append(moved)
    gate_keep, gate_parts = far_parts(gate_grad)
    down_grad = [low_sum(x, y) for x, y in zip(down_own, down_other)]
    proj_part = low_sum(half_dot(all_normed, clock.hold(grad_proj), side, half_proj), proj_sent)
    (proj_part,) = clock.sync(proj_part)
    def part_of(o):
        first = index_at(o) * attn_rows
        return jnp.concatenate(
            [
                lax.dynamic_slice_in_dim(clock.hold(proj_part), first, attn_rows, 0),
                lax.dynamic_slice_in_dim(clock.hold(out_piece), first, attn_rows, 0),
            ],
            axis=1,
        )

    def spread_grad(grads, bits):
        for bit in bits:
            grads = [jnp.concatenate([g, swap(g, "seq", bit)], axis=0) for g in grads]
        return grads

    a, b = halves(clock.hold(part_of(wide // 2)))
    gate_moved = []
    for k in range(wide // 2 - 1, -1, -1):
        step = wide // 2 - 1 - k
        a, b = hop(a, b, wide)
        work = []
        if step in (1, 2):
            work = [far_move(gate_parts[step - 1])]
        elif step == half_wide - 1:
            work = spread_grad([clock.hold(v) for v in down_grad], far_bits)
        a, b, *work = clock.sync(a, b, *work)
        if step in (1, 2):
            gate_moved += work
        elif step == half_wide - 1:
            down_grad = work
        if step == 0:
            a, b = add_first(part_of(k), a), add_last(part_of(-k), b)
        elif k > 0:
            a, b = low_sum(part_of(k), a), low_sum(part_of(-k), b)
    total = low_sum(part_of(0), a, b)
    gate_grad = far_join(gate_keep, gate_moved)
    up_own, up_send = column_parts(up_grad[0], 2), column_parts(up_grad[1], 2)
    total, gate_grad, *up_send = clock.sync(total, gate_grad, *up_send)

    def input_grad(s):
        return dot(clock.hold(grad_proj[s * rows : (s + 1) * rows]), proj_weights[s], NT)

    def back_tokens(s, grad_normed):
        grad, gain = norm_back(inputs[s], input_factor[s], gain_attn, grad_normed)
        return (grad_middle[s] + grad).astype(bf16), gain

    def add_swapped(gains, axis, bits):
        for bit in bits:
            gains = gains + swap(gains, axis, bit)
        return gains

    proj_total = total[:, :half_proj]
    out_totals = {0: total[:, half_proj:]}
    for bit in seq_bits[1:]:
        sent = jnp.concatenate([proj_total] + [out_totals[t] for t in sorted(out_totals)], axis=1)
        moved = swap(sent, "seq", bit)
        proj_total = low_sum(proj_total, moved[:, :half_proj])
        for i, t in enumerate(sorted(out_totals)):
            first = half_proj + i * split_out
            out_totals[t | (bit // 2)] = moved[:, first : first + split_out]
    out_totals = jnp.stack([out_totals[t] for t in range(members)])
    low = jnp.concatenate(
        [proj_total]
        + [
            lax.dynamic_index_in_dim(out_totals, jnp.bitwise_xor(member, j), 0, keepdims=False)
            for j in range(members)
        ],
        axis=1,
    )
    moved, grad_first = clock.sync(exchange_grad(up_send[0]), input_grad(0))
    up_grad = [low_sum(up_own[0], moved)]
    moved, low, grad_last = clock.sync(exchange_grad(up_send[1]), low, input_grad(1))
    up_grad.append(low_sum(up_own[1], moved))
    gate_own, gate_send = column_parts(gate_grad[0], 2), column_parts(gate_grad[1], 2)
    first_tokens, gain_first = back_tokens(0, grad_first)
    last_tokens, gain = back_tokens(1, grad_last)
    gains = jnp.concatenate([gain_first + gain, gain_second, gain_third, gain_fourth], axis=0)
    wide_bits = [1 << i for i in range(wide.bit_length() - 1)]
    gains = add_swapped(add_swapped(gains, "wide", wide_bits), "seq", seq_bits)
    gains, *gate_send = clock.sync(gains, *gate_send)
    moved = exchange_grad(gate_send[0])
    up_grad = spread_grad([clock.hold(v) for v in up_grad], far_bits)
    other = swap(clock.hold(low), "seq", 1)
    moved, other, *up_grad = clock.sync(moved, other, *up_grad)
    gate_grad = [low_sum(gate_own[0], moved)]
    moved = exchange_grad(gate_send[1])
    gate_grad = spread_grad([clock.hold(v) for v in gate_grad], far_bits)
    left, right = jnp.where(is_low, low, other), jnp.where(is_low, other, low)
    attn_grad = jnp.concatenate(
        [left[:, :half_proj], right[:, :half_proj], left[:, half_proj:], right[:, half_proj:]],
        axis=1,
    ).astype(f32)
    down_grad = spread_grad([clock.hold(v) for v in down_grad], seq_bits[:1])
    mlp_grad = unpack(down_grad, pieces, 2, [])
    moved, attn_grad, mlp_grad, *gate_grad = clock.sync(moved, attn_grad, mlp_grad, *gate_grad)
    last = spread_grad([low_sum(gate_own[1], moved)], far_bits)
    up_grad = spread_grad([clock.hold(v) for v in up_grad], seq_bits[:1])
    mlp_grad = unpack(up_grad, pieces, 1, [mlp_grad])
    gate_grad = spread_grad([clock.hold(v) for v in gate_grad], seq_bits[:1])
    mlp_grad, *gate_grad = clock.sync(mlp_grad, *gate_grad, *last)
    gate_grad[1:] = spread_grad(gate_grad[1:], seq_bits[:1])
    mlp_grad = unpack(gate_grad, pieces, 0, [mlp_grad])
    grad_tokens = [first_tokens, last_tokens]
    return (
        jnp.stack(layer_out),
        jnp.stack(grad_tokens),
        attn_grad,
        mlp_grad,
        gains[0],
        gains[1],
        gains[2],
        gains[3],
    )


def solution(mesh):
    placed = (
        P("seq", "wide", None),
        P("seq", "wide", None),
        P("seq"),
        P("wide", None),
        P(),
        P(),
        P(None, "wide", None),
        P(),
        P(),
        P(),
        P(),
        P(),
        P(),
    )
    return jax.shard_map(
        per_device,
        mesh=mesh,
        in_specs=placed,
        out_specs=(
            P("seq", "wide", None),
            P("seq", "wide", None),
            P("wide", None),
            P(None, "wide", None),
            P(),
            P(),
            P(),
            P(),
        ),
        check_vma=False,
    )
```

```python
import functools
import math

import jax
import jax.numpy as jnp
from jax import lax
from jax.experimental import pallas as pl
from jax.experimental.pallas import tpu as pltpu
from jax.sharding import PartitionSpec as P

QUERY_HEADS = 8
KEY_VALUE_HEADS = 4
HEAD_SIZE = 256
PAIRED = QUERY_HEADS // KEY_VALUE_HEADS

eps_norm = 1e-06
soft_cap = 50.0
rope_base = 10000.0
gelu_coeff = math.sqrt(2.0 / math.pi)
f32 = jnp.float32
bf16 = jnp.bfloat16
VMEM_LIMIT = 56 * 1024 * 1024


def dot(a, b, dims):
    return lax.dot_general(a, b, (dims, ((), ())), preferred_element_type=f32)


NN = ((1,), (0,))
NT = ((1,), (1,))
TN = ((0,), (0,))


def inverse_powers(exponents):
    return 1.0 / jnp.left_shift(jnp.ones_like(exponents), exponents).astype(f32)


def norm_factor(values):
    return lax.rsqrt(jnp.mean(values * values, axis=-1, keepdims=True) + eps_norm)


def norm_back(values, factor, gain, grad):
    scaled = grad * gain
    inner = jnp.mean(values * scaled, axis=-1, keepdims=True)
    grad_values = factor * scaled - values * (factor * factor * factor * inner)
    return grad_values, jnp.sum(grad * values * factor, axis=0, keepdims=True)


def gelu_parts(values):
    inner = gelu_coeff * (values + 0.044715 * values * values * values)
    return jnp.tanh(inner)


def rotary_rows(positions):
    half_dim = HEAD_SIZE // 2
    frequency = jnp.exp(
        jnp.arange(half_dim, dtype=f32) * (-2.0 * math.log(rope_base) / HEAD_SIZE)
    )
    angles = positions.astype(f32)[:, None] * frequency[None, :]
    return jnp.cos(angles), jnp.sin(angles)


def ring_place(index, size):
    return jnp.where(index % 2 == 0, index // 2, size - 1 - index // 2)


def ring_index(place, size):
    return jnp.where(place < size // 2, 2 * place, 2 * (size - 1 - place) + 1)


def ring_perms(size):
    order = list(range(0, size, 2)) + list(range(size - 1, 0, -2))
    up = [
        (base + order[i], base + order[(i + 1) % size])
        for base in range(0, lax.axis_size("wide"), size)
        for i in range(size)
    ]
    return up, [(b, a) for a, b in up]


def ring_offsets(size):
    out = [0]
    for k in range(1, size // 2):
        out += [-k, k]
    return out + [size // 2]


class Clock:
    def __init__(self, token):
        self.token = token

    def sync(self, *arrays):
        *arrays, self.token = lax.optimization_barrier(tuple(arrays) + (self.token,))
        return arrays

    def hold(self, value):
        return lax.optimization_barrier((value, self.token))[0]


def hop(a, b, size):
    up, down = ring_perms(size)
    return lax.ppermute(a, "wide", up), lax.ppermute(b, "wide", down)


def low_sum(*terms):
    return sum(t.astype(f32) for t in terms).astype(bf16)


def halves(value):
    half = value.shape[0] // 2
    return value[:half], value[half:]


def add_first(whole, part):
    count = part.shape[0]
    return jnp.concatenate([low_sum(whole[:count], part), whole[count:].astype(bf16)], axis=0)


def add_last(whole, part):
    count = whole.shape[0] - part.shape[0]
    return jnp.concatenate([whole[:count].astype(bf16), low_sum(whole[count:], part)], axis=0)


def ring_gather(clock, value, size, beside=lambda step: ()):
    a = b = clock.hold(value)
    out, other = [a], []
    for k in range(1, size // 2 + 1):
        if k == size // 2:
            a, b = halves(a)[0], halves(b)[1]
        work = beside(k - 1)
        a, b = hop(a, b, size)
        a, b, *work = clock.sync(a, b, *work)
        out += [a, b]
        other.append(work)
    return out, other


def ring_scatter(clock, part_of, rows, size, beside=lambda step: ()):
    a, b = halves(clock.hold(part_of(size // 2).astype(bf16)))
    other = []
    for k in range(size // 2 - 1, -1, -1):
        work = beside(size // 2 - 1 - k)
        a, b = hop(a, b, size)
        a, b, *work = clock.sync(a, b, *work)
        other.append(work)
        if k == size // 2 - 1 and k > 0:
            a = add_first(part_of(k), a)
            b = add_last(part_of(-k), b)
        elif k > 0:
            a = low_sum(part_of(k), a)
            b = low_sum(part_of(-k), b)
    return part_of(0).astype(f32) + a.astype(f32) + b.astype(f32), other


def swap(value, axis, bit):
    size = lax.axis_size(axis)
    return lax.ppermute(value, axis, [(i, i ^ bit) for i in range(size)])


def all_to_all(value):
    return lax.all_to_all(value, "wide", split_axis=0, concat_axis=0, tiled=True)


def heads_all_to_all(value):
    size = lax.axis_size("wide")
    classes = size // KEY_VALUE_HEADS
    groups = [list(range(c, size, classes)) for c in range(classes)]
    return lax.all_to_all(
        value, "wide", split_axis=0, concat_axis=0, axis_index_groups=groups, tiled=True
    )


def class_ring(value):
    size = lax.axis_size("wide")
    classes = size // KEY_VALUE_HEADS
    perm = [(i, i // classes * classes + (i + 1) % classes) for i in range(size)]
    return lax.ppermute(value, "wide", perm)


def slice_values(codes, width):
    lift = jnp.where(width == 0, 0.0, 0.5).astype(bf16)
    large = jnp.where(width == 0, 0.0, jnp.where(width == 1, 1.5 * 2**11, 1.5 * 2**13)).astype(bf16)
    top = jnp.where(width == 0, 127.0, jnp.where(width == 1, 112.0, 64.0)).astype(bf16)
    return jnp.minimum(((codes + lift) + large) - large, top)


def proj_slice_kernel(places, info, *refs, blocks, count):
    code_refs, scale_ref, out_refs = refs[: 2 * blocks], refs[2 * blocks], refs[len(refs) - count :]
    mine = pl.program_id(1) == info[0]

    def write(code_ref):
        codes = code_ref[...]
        scale = scale_ref[...].astype(bf16)
        for s, out_ref in enumerate(out_refs):
            out_ref[...] = slice_values(codes, info[1 + s]) * scale

    for k in range(blocks):
        here = pl.program_id(0) == k
        pl.when(jnp.logical_and(here, mine))(functools.partial(write, code_refs[2 * k]))
        pl.when(jnp.logical_and(here, jnp.logical_not(mine)))(
            functools.partial(write, code_refs[2 * k + 1])
        )


def proj_slices(own, other, places, info, scale, width, weights, total, count):
    blocks = len(own)
    rows = own[0].shape[0]
    inputs = [block for pair in zip(own, other) for block in pair] + [scale]
    grid_spec = pltpu.PrefetchScalarGridSpec(
        num_scalar_prefetch=2,
        grid=(blocks, 2),
        in_specs=[pl.BlockSpec((rows, width), lambda k, j, p, i: (0, 0))] * (2 * blocks)
        + [pl.BlockSpec((1, width), lambda k, j, p, i: (0, j))]
        + [pl.BlockSpec(memory_space=pl.ANY)] * len(weights),
        out_specs=[pl.BlockSpec((rows, width), lambda k, j, p, i: (p[k], j))] * count,
    )
    return pl.pallas_call(
        functools.partial(proj_slice_kernel, blocks=blocks, count=count),
        grid_spec=grid_spec,
        out_shape=[jax.ShapeDtypeStruct((total * rows, 2 * width), bf16)] * count,
        input_output_aliases={2 + len(inputs) + s: s for s in range(len(weights))},
        compiler_params=pltpu.CompilerParams(vmem_limit_bytes=VMEM_LIMIT),
        cost_estimate=pl.CostEstimate(
            flops=20 * count * blocks * rows * width,
            bytes_accessed=4 * blocks * rows * width * (1 + count),
            transcendentals=0,
        ),
        name="proj_slices",
    )(places, info, *inputs, *weights)


def out_slice_kernel(places, info, *refs, split, count):
    inputs, scale_ref, out_refs = refs[: -1 - count], refs[-1 - count], refs[-count:]
    members = len(inputs) // 2
    member = info[1 + count]
    mine = pl.program_id(1) == info[0]

    def write(code_refs):
        scale = scale_ref[...].astype(bf16)
        for t, code_ref in enumerate(code_refs):
            first = pl.multiple_of(jnp.bitwise_xor(member, t) * split, 128)
            for s, out_ref in enumerate(out_refs):
                out_ref[:, pl.ds(first, split)] = slice_values(code_ref[0], info[1 + s]) * scale

    pl.when(mine)(lambda: write(inputs[:members]))
    pl.when(jnp.logical_not(mine))(lambda: write(inputs[members:]))


def out_slices(own, other, places, info, scale, count):
    blocks, rows, split = own[0].shape
    width = split * len(own)
    inputs = list(own) + list(other)
    grid_spec = pltpu.PrefetchScalarGridSpec(
        num_scalar_prefetch=2,
        grid=(blocks, 2),
        in_specs=[pl.BlockSpec((1, rows, split), lambda k, j, p, i: (k, 0, 0))] * len(inputs)
        + [pl.BlockSpec((rows, 1), lambda k, j, p, i: (p[k], 0))],
        out_specs=[pl.BlockSpec((rows, width), lambda k, j, p, i: (p[k], j))] * count,
    )
    return pl.pallas_call(
        functools.partial(out_slice_kernel, split=split, count=count),
        grid_spec=grid_spec,
        out_shape=[jax.ShapeDtypeStruct((blocks * rows, 2 * width), bf16)] * count,
        compiler_params=pltpu.CompilerParams(vmem_limit_bytes=VMEM_LIMIT),
        cost_estimate=pl.CostEstimate(
            flops=20 * count * blocks * rows * width,
            bytes_accessed=4 * blocks * rows * width * (1 + count),
            transcendentals=0,
        ),
        name="out_slices",
    )(places, info, *inputs, scale)


def piece_at(j, steps, block):
    half = steps // 2
    return j + j // half * half + block * half


def own_slice_kernel(pieces, info, code_ref, row_ref, col_ref, *out_refs):
    count = len(out_refs) // 3
    for m in range(3):
        codes = code_ref[m].astype(f32).astype(bf16)
        scale = (row_ref[m] if m < 2 else col_ref[...]).astype(bf16)
        for s in range(count):
            out_refs[m * count + s][...] = slice_values(codes, info[1 + s]) * scale


def own_slices(codes, pieces, info, row_scale, col_scale, count):
    three, rows, cols = codes.shape
    steps = pieces.shape[0]
    piece = rows // steps
    grid_spec = pltpu.PrefetchScalarGridSpec(
        num_scalar_prefetch=2,
        grid=(steps,),
        in_specs=[
            pl.BlockSpec((three, piece, cols), lambda j, p, i: (0, p[j], 0)),
            pl.BlockSpec((2, piece, 1), lambda j, p, i: (0, piece_at(j, steps, 0), 0)),
            pl.BlockSpec((1, cols), lambda j, p, i: (0, 0)),
        ],
        out_specs=[pl.BlockSpec((piece, cols), lambda j, p, i: (piece_at(j, steps, 0), 0))]
        * (three * count),
    )
    return pl.pallas_call(
        own_slice_kernel,
        grid_spec=grid_spec,
        out_shape=[jax.ShapeDtypeStruct((2 * rows, cols), bf16)] * (three * count),
        compiler_params=pltpu.CompilerParams(vmem_limit_bytes=VMEM_LIMIT),
        cost_estimate=pl.CostEstimate(
            flops=10 * count * codes.size,
            bytes_accessed=codes.size * (4 + 2 * count),
            transcendentals=0,
        ),
        name="own_slices",
    )(pieces, info, codes, row_scale, col_scale)


def partner_slice_kernel(info, *refs, steps, count):
    piece_refs, scale_ref, out_refs = refs[:steps], refs[steps], refs[steps + 1 + count :]
    for j in range(steps):

        @pl.when(pl.program_id(0) == j)
        def _():
            codes = piece_refs[j][...]
            scale = scale_ref[...].astype(bf16)
            for s, out_ref in enumerate(out_refs):
                out_ref[...] = slice_values(codes, info[1 + s]) * scale


def partner_slices(pieces, info, scale, by_column, weights):
    steps = len(pieces)
    count = len(weights)
    piece, cols = pieces[0].shape
    if by_column:
        scale_spec = pl.BlockSpec((1, cols), lambda j, i: (0, 0))
    else:
        scale_spec = pl.BlockSpec((piece, 1), lambda j, i: (piece_at(j, steps, 1), 0))
    grid_spec = pltpu.PrefetchScalarGridSpec(
        num_scalar_prefetch=1,
        grid=(steps,),
        in_specs=[pl.BlockSpec((piece, cols), lambda j, i: (0, 0))] * steps
        + [scale_spec]
        + [pl.BlockSpec(memory_space=pl.ANY)] * count,
        out_specs=[pl.BlockSpec((piece, cols), lambda j, i: (piece_at(j, steps, 1), 0))] * count,
    )
    return pl.pallas_call(
        functools.partial(partner_slice_kernel, steps=steps, count=count),
        grid_spec=grid_spec,
        out_shape=[jax.ShapeDtypeStruct(w.shape, bf16) for w in weights],
        input_output_aliases={2 + steps + s: s for s in range(count)},
        compiler_params=pltpu.CompilerParams(vmem_limit_bytes=VMEM_LIMIT),
        cost_estimate=pl.CostEstimate(
            flops=10 * count * steps * piece * cols,
            bytes_accessed=2 * (1 + count) * steps * piece * cols,
            transcendentals=0,
        ),
        name="partner_slices",
    )(info, *pieces, scale, *weights)


def unpack_kernel(pieces, *refs, parts):
    first = 0
    for ref in refs[:parts]:
        width = ref.shape[1]
        refs[-1][0, :, first : first + width] = ref[...].astype(f32)
        first += width


def unpack(grads, pieces, matrix, held):
    steps = pieces.shape[0]
    rows = grads[0].shape[0]
    cols = sum(g.shape[1] for g in grads)
    piece = rows // steps
    grid_spec = pltpu.PrefetchScalarGridSpec(
        num_scalar_prefetch=1,
        grid=(steps,),
        in_specs=[pl.BlockSpec((piece, g.shape[1]), lambda j, p: (j, 0)) for g in grads]
        + [pl.BlockSpec(memory_space=pl.ANY)] * len(held),
        out_specs=pl.BlockSpec((1, piece, cols), lambda j, p: (matrix, p[j], 0)),
    )
    return pl.pallas_call(
        functools.partial(unpack_kernel, parts=len(grads)),
        grid_spec=grid_spec,
        out_shape=jax.ShapeDtypeStruct((3, rows, cols), f32),
        input_output_aliases={1 + len(grads): 0} if held else {},
        compiler_params=pltpu.CompilerParams(vmem_limit_bytes=VMEM_LIMIT),
        cost_estimate=pl.CostEstimate(
            flops=rows * cols, bytes_accessed=6 * rows * cols, transcendentals=0
        ),
        name="unpack",
    )(pieces, *grads, *held)


def tile_of(size):
    return 256 if size % 256 == 0 else size


def tiles_of(size, part):
    tile = tile_of(size)
    tiles = size // tile
    first_part = (tiles + 1) // 2
    if part is None or tiles == 1:
        return tile, 0, tiles
    return (tile, 0, first_part) if part == 0 else (tile, first_part, tiles - first_part)


def whole_spec(shape):
    return pl.BlockSpec(shape, lambda i: (0, 0))


def column_spec(rows, tile, first=0):
    return pl.BlockSpec((rows, tile), lambda i: (0, first + i))


def row_spec(tile, cols, first=0):
    return pl.BlockSpec((tile, cols), lambda i: (first + i, 0))


def kernel_call(kernel, grid, in_specs, out_specs, out_shape, flops, moved, name, held=()):
    inputs = len(in_specs)
    return pl.pallas_call(
        lambda *refs: kernel(*refs[:inputs], *refs[inputs + len(held) :]),
        grid=(grid,),
        in_specs=in_specs + [pl.BlockSpec(memory_space=pl.ANY)] * len(held),
        out_specs=out_specs,
        out_shape=out_shape,
        input_output_aliases={inputs + i: i for i in range(len(held))},
        compiler_params=pltpu.CompilerParams(vmem_limit_bytes=VMEM_LIMIT),
        cost_estimate=pl.CostEstimate(flops=flops, bytes_accessed=moved, transcendentals=0),
        name=name,
    )


def row_parts(rows):
    part = 512 if rows % 512 == 0 else rows
    return [slice(first, first + part) for first in range(0, rows, part)]


def open_kernel(x_ref, wg_ref, wu_ref, gate_ref, up_ref, hidden_ref):
    for part in row_parts(x_ref.shape[0]):
        x = x_ref[part]
        gate = dot(x, wg_ref[...], NT)
        up = dot(x, wu_ref[...], NT)
        gate_ref[part] = gate
        up_ref[part] = up
        hidden_ref[part] = (gate * (0.5 + 0.5 * gelu_parts(gate)) * up).astype(bf16)


def open_forward(x, gate_weights, up_weights, part, held=()):
    rows, depth = x.shape
    hidden = gate_weights.shape[0]
    tile, first, tiles = tiles_of(hidden, part)
    if held and tiles * tile == hidden:
        return list(held)
    return kernel_call(
        open_kernel,
        tiles,
        [whole_spec(x.shape)] + [row_spec(tile, depth, first)] * 2,
        [column_spec(rows, tile, first)] * 3,
        [jax.ShapeDtypeStruct((rows, hidden), t) for t in (f32, f32, bf16)],
        4 * rows * depth * tile * tiles,
        2 * rows * depth + tiles * tile * (4 * depth + 10 * rows),
        "open_forward",
        held,
    )(x, gate_weights, up_weights, *held)


def open_back_kernel(x_ref, wd_ref, gate_ref, up_ref, grad_gate_ref, grad_up_ref):
    for part in row_parts(x_ref.shape[0]):
        grad = dot(x_ref[part], wd_ref[...], NT)
        gate = gate_ref[part]
        square = gate * gate
        bounded = jnp.tanh(gate * (gelu_coeff + (0.044715 * gelu_coeff) * square))
        half = 0.5 + 0.5 * bounded
        steep = (0.5 * gelu_coeff) + (1.5 * 0.044715 * gelu_coeff) * square
        slope = half + gate * (1.0 - bounded * bounded) * steep
        grad_gate_ref[part] = (grad * up_ref[part] * slope).astype(bf16)
        grad_up_ref[part] = (grad * (gate * half)).astype(bf16)


def open_back(x, down_weights, gate, up, part, held=()):
    rows, depth = x.shape
    hidden = down_weights.shape[0]
    tile, first, tiles = tiles_of(hidden, part)
    if held and tiles * tile == hidden:
        return list(held)
    return kernel_call(
        open_back_kernel,
        tiles,
        [whole_spec(x.shape), row_spec(tile, depth, first)] + [column_spec(rows, tile, first)] * 2,
        [column_spec(rows, tile, first)] * 2,
        [jax.ShapeDtypeStruct((rows, hidden), bf16)] * 2,
        2 * rows * depth * tile * tiles,
        2 * rows * depth + tiles * tile * (2 * depth + 12 * rows),
        "open_back",
        held,
    )(x, down_weights, gate, up, *held)


def input_back_kernel(gate_ref, up_ref, wg_ref, wu_ref, out_ref):
    out_ref[...] = (
        dot(gate_ref[...], wg_ref[...], NN) + dot(up_ref[...], wu_ref[...], NN)
    ).astype(bf16)


def input_back(grad_gate, grad_up, gate_weights, up_weights, part, held=()):
    rows, hidden = grad_gate.shape
    depth = gate_weights.shape[1]
    tile, first, tiles = tiles_of(depth, part)
    if held and tiles * tile == depth:
        return list(held)
    return kernel_call(
        input_back_kernel,
        tiles,
        [whole_spec(grad_gate.shape)] * 2 + [column_spec(hidden, tile, first)] * 2,
        [column_spec(rows, tile, first)],
        [jax.ShapeDtypeStruct((rows, depth), bf16)],
        4 * rows * hidden * tile * tiles,
        4 * rows * hidden + tiles * tile * (4 * hidden + 2 * rows),
        "input_back",
        held,
    )(grad_gate, grad_up, gate_weights, up_weights, *held)


def weight_kernel(*refs, count, tiles):
    keep_ref, send_ref = refs[-2:]
    total = dot(refs[0][...], refs[count][...], TN)
    for s in range(1, count):
        total = total + dot(refs[s][...], refs[count + s][...], TN)
    total = total.astype(bf16)
    if tiles == 1:
        half = keep_ref.shape[0]
        keep_ref[...] = total[:half]
        send_ref[...] = total[half:]
        return
    step = pl.program_id(0)

    @pl.when(step < tiles // 2)
    def _():
        keep_ref[...] = total

    @pl.when(step >= tiles // 2)
    def _():
        send_ref[...] = total


def weight_back(lefts, rights):
    count = len(lefts)
    rows, hidden = lefts[0].shape
    depth = rights[0].shape[1]
    tile = 384 if hidden % 768 == 0 else hidden
    tiles = hidden // tile
    half = max(tiles // 2, 1)
    out = (tile if tiles > 1 else hidden // 2, depth)
    return kernel_call(
        functools.partial(weight_kernel, count=count, tiles=tiles),
        tiles,
        [column_spec(rows, tile)] * count + [whole_spec((rows, depth))] * count,
        [
            pl.BlockSpec(out, lambda i: (jnp.minimum(i, half - 1), 0)),
            pl.BlockSpec(out, lambda i: (jnp.maximum(i - half, 0), 0)),
        ],
        [jax.ShapeDtypeStruct((hidden // 2, depth), bf16)] * 2,
        2 * count * rows * depth * hidden,
        2 * count * rows * (hidden + depth) + 2 * hidden * depth,
        "weight_back",
    )(*lefts, *rights)


def fixed_spec(shape):
    return pl.BlockSpec(shape, lambda i: (0,) * len(shape))


def join_kernel(att_ref, w_ref, x_ref, gain_ref, next_ref, branch_ref, mid_ref, normed_ref, sum_ref):
    step = pl.program_id(0)
    heads, _, cols = att_ref.shape
    tile = w_ref.shape[0]
    total = dot(att_ref[0], w_ref[:, :cols], NT)
    for h in range(1, heads):
        total = total + dot(att_ref[h], w_ref[:, h * cols : (h + 1) * cols], NT)
    sum_ref[:, pl.ds(pl.multiple_of(step * tile, 128), tile)] = total

    @pl.when(step == pl.num_programs(0) - 1)
    def _():
        value = sum_ref[...]
        mid = x_ref[...].astype(f32) + value * norm_factor(value) * gain_ref[...]
        branch_ref[...] = value
        mid_ref[...] = mid
        normed_ref[...] = (mid * norm_factor(mid) * next_ref[...]).astype(bf16)


def join_rows(attended, weights, x, gain, next_gain):
    rows, depth = x.shape
    tile = tile_of(depth)
    return pl.pallas_call(
        join_kernel,
        grid=(depth // tile,),
        in_specs=[
            fixed_spec(attended.shape),
            row_spec(tile, weights.shape[1]),
            fixed_spec(x.shape),
            fixed_spec((1, depth)),
            fixed_spec((1, depth)),
        ],
        out_specs=[fixed_spec((rows, depth))] * 3,
        out_shape=[jax.ShapeDtypeStruct((rows, depth), t) for t in (f32, f32, bf16)],
        scratch_shapes=[pltpu.VMEM((rows, depth), f32)],
        compiler_params=pltpu.CompilerParams(vmem_limit_bytes=VMEM_LIMIT),
        cost_estimate=pl.CostEstimate(
            flops=2 * rows * weights.size,
            bytes_accessed=2 * weights.size + 12 * rows * depth,
            transcendentals=0,
        ),
        name="join_rows",
    )(attended, weights, x, gain[None], next_gain[None])


def finish_kernel(part_ref, a_ref, b_ref, mid_ref, cot_ref, gain_ref, out_ref, grad_ref, dg_ref):
    value = part_ref[...].astype(f32) + a_ref[...].astype(f32) + b_ref[...].astype(f32)
    factor = norm_factor(value)
    gain = gain_ref[...]
    out_ref[...] = (mid_ref[...] + value * factor * gain).astype(bf16)
    grad, dg = norm_back(value, factor, gain, cot_ref[...].astype(f32))
    grad_ref[...] = grad.astype(bf16)
    dg_ref[...] = dg


def finish_rows(part, a, b, mid, cotangent, gain):
    rows, depth = mid.shape
    spec = fixed_spec((rows, depth))
    return pl.pallas_call(
        finish_kernel,
        grid=(1,),
        in_specs=[spec] * 5 + [fixed_spec((1, depth))],
        out_specs=[spec, spec, fixed_spec((1, depth))],
        out_shape=[
            jax.ShapeDtypeStruct((rows, depth), bf16),
            jax.ShapeDtypeStruct((rows, depth), bf16),
            jax.ShapeDtypeStruct((1, depth), f32),
        ],
        compiler_params=pltpu.CompilerParams(vmem_limit_bytes=VMEM_LIMIT),
        cost_estimate=pl.CostEstimate(
            flops=20 * rows * depth, bytes_accessed=16 * rows * depth, transcendentals=0
        ),
        name="finish_rows",
    )(part, a, b, mid, cotangent, gain[None])


def branch_back_kernel(
    part_ref,
    a_ref,
    b_ref,
    mid_ref,
    branch_ref,
    cot_ref,
    mlp_gain_ref,
    gain_ref,
    w_ref,
    grad_mid_ref,
    grad_ref,
    send_ref,
    mlp_dg_ref,
    dg_ref,
    held_ref,
):
    @pl.when(pl.program_id(0) == 0)
    def _():
        normed = part_ref[...].astype(f32) + a_ref[...].astype(f32) + b_ref[...].astype(f32)
        mid = mid_ref[...]
        grad, dg = norm_back(mid, norm_factor(mid), mlp_gain_ref[...], normed)
        mlp_dg_ref[...] = dg
        grad_mid = cot_ref[...].astype(f32) + grad
        grad_mid_ref[...] = grad_mid
        branch = branch_ref[...]
        grad, dg = norm_back(branch, norm_factor(branch), gain_ref[...], grad_mid)
        dg_ref[...] = dg
        held_ref[...] = grad.astype(bf16)
        grad_ref[...] = grad.astype(bf16)

    send_ref[0] = dot(held_ref[...], w_ref[...], NN).astype(bf16)


def branch_back(part, a, b, mid, branch, cotangent, mlp_gain, gain, weights):
    rows, depth = mid.shape
    cols = PAIRED * HEAD_SIZE
    spec = fixed_spec((rows, depth))
    line = fixed_spec((1, depth))
    return pl.pallas_call(
        branch_back_kernel,
        grid=(KEY_VALUE_HEADS,),
        in_specs=[spec] * 6 + [line] * 2 + [column_spec(depth, cols)],
        out_specs=[
            spec,
            spec,
            pl.BlockSpec((1, rows, cols), lambda i: (i, 0, 0)),
            line,
            line,
        ],
        out_shape=[
            jax.ShapeDtypeStruct((rows, depth), f32),
            jax.ShapeDtypeStruct((rows, depth), bf16),
            jax.ShapeDtypeStruct((KEY_VALUE_HEADS, rows, cols), bf16),
            jax.ShapeDtypeStruct((1, depth), f32),
            jax.ShapeDtypeStruct((1, depth), f32),
        ],
        scratch_shapes=[pltpu.VMEM((rows, depth), bf16)],
        compiler_params=pltpu.CompilerParams(vmem_limit_bytes=VMEM_LIMIT),
        cost_estimate=pl.CostEstimate(
            flops=2 * rows * weights.size,
            bytes_accessed=2 * weights.size + 22 * rows * depth,
            transcendentals=0,
        ),
        name="branch_back",
    )(part, a, b, mid, branch, cotangent, mlp_gain[None], gain[None], weights)


def out_product_kernel(info, branch_ref, att_ref, received_ref, own_ref, send_ref):
    total = dot(branch_ref[...], att_ref[...], TN) + received_ref[...].astype(f32)
    total = total.astype(bf16)
    width = own_ref.shape[1]
    first = info[1] == 0
    own_ref[...] = jnp.where(first, total[:, :width], total[:, width:])
    send_ref[...] = jnp.where(first, total[:, width:], total[:, :width])


def out_product(info, branch, attended, received):
    rows, depth = branch.shape
    cols = attended.shape[1] // 2
    tile = tile_of(depth)
    out = pl.BlockSpec((tile, cols // 2), lambda i, c: (i, 0))
    return pl.pallas_call(
        out_product_kernel,
        grid_spec=pltpu.PrefetchScalarGridSpec(
            num_scalar_prefetch=1,
            grid=(depth // tile,),
            in_specs=[
                pl.BlockSpec((rows, tile), lambda i, c: (0, i)),
                pl.BlockSpec((rows, cols), lambda i, c: (0, c[0])),
                pl.BlockSpec((tile, cols), lambda i, c: (i, 0)),
            ],
            out_specs=[out, out],
        ),
        out_shape=[jax.ShapeDtypeStruct((depth, cols // 2), bf16)] * 2,
        compiler_params=pltpu.CompilerParams(vmem_limit_bytes=VMEM_LIMIT),
        cost_estimate=pl.CostEstimate(
            flops=2 * rows * depth * cols, bytes_accessed=4 * depth * cols, transcendentals=0
        ),
        name="out_product",
    )(info, branch, attended, received)


def turn(values, cosine, sine):
    half = HEAD_SIZE // 2
    out = []
    for j in range(values.shape[1] // HEAD_SIZE):
        a = values[:, j * HEAD_SIZE : j * HEAD_SIZE + half]
        b = values[:, j * HEAD_SIZE + half : (j + 1) * HEAD_SIZE]
        out += [a * cosine - b * sine, b * cosine + a * sine]
    return jnp.concatenate(out, axis=1)


def project_kernel(x_ref, wq_ref, wk_ref, wv_ref, cos_ref, sin_ref, q_ref, kv_ref):
    x = x_ref[...]
    cosine, sine = cos_ref[...], sin_ref[...]
    scale = HEAD_SIZE ** (-0.5)
    q_ref[0] = (turn(dot(x, wq_ref[...], NN), cosine, sine) * scale).astype(bf16)
    kv_ref[0, :, :HEAD_SIZE] = turn(dot(x, wk_ref[...], NN), cosine, sine).astype(bf16)
    kv_ref[0, :, HEAD_SIZE:] = dot(x, wv_ref[...], NN).astype(bf16)


def project(normed, weights, cosine, sine):
    rows, depth = normed.shape
    cols = PAIRED * HEAD_SIZE
    first_key = QUERY_HEADS
    first_value = QUERY_HEADS + KEY_VALUE_HEADS
    whole = lambda shape: pl.BlockSpec(shape, lambda h: (0, 0))
    return pl.pallas_call(
        project_kernel,
        grid=(KEY_VALUE_HEADS,),
        in_specs=[
            whole((rows, depth)),
            pl.BlockSpec((depth, cols), lambda h: (0, h)),
            pl.BlockSpec((depth, HEAD_SIZE), lambda h: (0, first_key + h)),
            pl.BlockSpec((depth, HEAD_SIZE), lambda h: (0, first_value + h)),
            whole(cosine.shape),
            whole(sine.shape),
        ],
        out_specs=[
            pl.BlockSpec((1, rows, cols), lambda h: (h, 0, 0)),
            pl.BlockSpec((1, rows, 2 * HEAD_SIZE), lambda h: (h, 0, 0)),
        ],
        out_shape=[
            jax.ShapeDtypeStruct((KEY_VALUE_HEADS, rows, cols), bf16),
            jax.ShapeDtypeStruct((KEY_VALUE_HEADS, rows, 2 * HEAD_SIZE), bf16),
        ],
        compiler_params=pltpu.CompilerParams(vmem_limit_bytes=VMEM_LIMIT),
        cost_estimate=pl.CostEstimate(
            flops=2 * rows * weights.size, bytes_accessed=2 * weights.size, transcendentals=0
        ),
        name="project",
    )(normed, weights, weights, weights, cosine, sine)


def turn_back_kernel(*refs, count):
    q_refs, kv_refs = refs[:count], refs[count : 2 * count]
    cos_ref, sin_ref, out_ref = refs[2 * count :]
    j = pl.program_id(1)
    scale = HEAD_SIZE ** (-0.5)
    keys = KEY_VALUE_HEADS // PAIRED
    for s in range(count):
        here = pl.program_id(0) == s

        @pl.when(jnp.logical_and(here, j < KEY_VALUE_HEADS))
        def _():
            grad = q_refs[s][0].astype(f32) * scale
            out_ref[...] = turn(grad, cos_ref[...], -sin_ref[...]).astype(bf16)

        @pl.when(jnp.logical_and(here, jnp.logical_and(j >= KEY_VALUE_HEADS, j < KEY_VALUE_HEADS + keys)))
        def _():
            grad = jnp.concatenate([kv_refs[s][i, :, :HEAD_SIZE] for i in range(PAIRED)], axis=1)
            out_ref[...] = turn(grad.astype(f32), cos_ref[...], -sin_ref[...]).astype(bf16)

        @pl.when(jnp.logical_and(here, j >= KEY_VALUE_HEADS + keys))
        def _():
            out_ref[...] = jnp.concatenate(
                [kv_refs[s][i, :, HEAD_SIZE:] for i in range(PAIRED)], axis=1
            )


def turn_back(queries, pairs, cosine, sine):
    count = len(queries)
    heads, rows, cols = queries[0].shape
    keys = heads // PAIRED
    grid = (count, heads + 2 * keys)
    whole = pl.BlockSpec(cosine.shape, lambda s, j: (0, 0))
    return pl.pallas_call(
        functools.partial(turn_back_kernel, count=count),
        grid=grid,
        in_specs=[
            pl.BlockSpec((1, rows, cols), lambda s, j: (jnp.minimum(j, heads - 1), 0, 0))
        ]
        * count
        + [
            pl.BlockSpec(
                (PAIRED, rows, cols), lambda s, j: (jnp.maximum(j - heads, 0) % keys, 0, 0)
            )
        ]
        * count
        + [whole, whole],
        out_specs=pl.BlockSpec((rows, cols), lambda s, j: (s, j)),
        out_shape=jax.ShapeDtypeStruct((count * rows, grid[1] * cols), bf16),
        compiler_params=pltpu.CompilerParams(vmem_limit_bytes=VMEM_LIMIT),
        cost_estimate=pl.CostEstimate(
            flops=4 * count * rows * grid[1] * cols,
            bytes_accessed=4 * count * rows * grid[1] * cols,
            transcendentals=0,
        ),
        name="turn_back",
    )(*queries, *pairs, cosine, sine)


def tile_positions(tile, count, start, class_index, class_rows, rows):
    index = lax.broadcasted_iota(jnp.int32, (count, 1), 0)
    place = start + jnp.bitwise_and(index, tile - 1)
    shift = class_rows.bit_length() - 1
    return (
        jnp.right_shift(place, shift) * rows
        + class_index * class_rows
        + jnp.bitwise_and(place, class_rows - 1)
    )


def stack_heads(block):
    return jnp.concatenate(
        [block[:, j * HEAD_SIZE : (j + 1) * HEAD_SIZE] for j in range(PAIRED)], axis=0
    )


def key_places(group, class_index, classes, rows):
    index = lax.broadcasted_iota(jnp.int32, (1, classes * rows), 1)
    shift = rows.bit_length() - 1
    back = jnp.bitwise_and(class_index - jnp.right_shift(index, shift), classes - 1)
    return (group * classes + back) * rows + jnp.bitwise_and(index, rows - 1)


def held_block(refs, group, cols):
    return jnp.concatenate([ref[group, :, cols] for ref in refs], axis=0)


def group_range(start, tile, class_rows, classes):
    return start // class_rows // classes, (start + tile - 1) // class_rows // classes + 1


def attn_forward_kernel(info, q_ref, *refs, tile, class_rows, rows, classes):
    kv_refs = refs[:classes]
    att_ref, exact_ref, lse_ref = refs[classes:]
    start = pl.program_id(0) * tile
    free, total = group_range(start, tile, class_rows, classes)
    queries = stack_heads(q_ref[...])
    count = queries.shape[0]
    position = tile_positions(tile, count, start, info[0], class_rows, rows)

    def step(group, carry, masked):
        acc, row_sum = carry
        keys = held_block(kv_refs, group, slice(0, HEAD_SIZE))
        values = held_block(kv_refs, group, slice(HEAD_SIZE, 2 * HEAD_SIZE))
        raw = dot(queries, keys, NT)
        weight = jnp.exp(soft_cap * jnp.tanh(raw * (1.0 / soft_cap)))
        if masked:
            weight = jnp.where(
                key_places(group, info[0], classes, rows) <= position, weight, 0.0
            )
        row_sum = row_sum + jnp.sum(weight, axis=-1, keepdims=True)
        acc = acc + dot(weight.astype(bf16), values, NN)
        return acc, row_sum

    carry = (jnp.zeros((count, HEAD_SIZE), f32), jnp.zeros((count, 1), f32))
    carry = lax.fori_loop(0, free, functools.partial(step, masked=False), carry)
    acc, row_sum = lax.fori_loop(free, total, functools.partial(step, masked=True), carry)
    exact = acc / row_sum
    lse = jnp.log(row_sum)
    for j in range(PAIRED):
        cols = slice(j * HEAD_SIZE, (j + 1) * HEAD_SIZE)
        exact_ref[:, cols] = exact[j * tile : (j + 1) * tile]
        att_ref[:, cols] = exact[j * tile : (j + 1) * tile].astype(bf16)
        lse_ref[:, j * 128 : (j + 1) * 128] = jnp.broadcast_to(
            lse[j * tile : (j + 1) * tile], (tile, 128)
        )


def attn_forward(info, queries, pairs, class_rows, rows):
    count, cols = queries.shape
    classes = len(pairs)
    length = classes * pairs[0].shape[0] * rows
    tile = min(256, count)
    grid_spec = pltpu.PrefetchScalarGridSpec(
        num_scalar_prefetch=1,
        grid=(count // tile,),
        in_specs=[pl.BlockSpec((tile, cols), lambda i, c: (i, 0))]
        + [pl.BlockSpec(p.shape, lambda i, c: (0, 0, 0)) for p in pairs],
        out_specs=[
            pl.BlockSpec((tile, cols), lambda i, c: (i, 0)),
            pl.BlockSpec((tile, cols), lambda i, c: (i, 0)),
            pl.BlockSpec((tile, PAIRED * 128), lambda i, c: (i, 0)),
        ],
    )
    return pl.pallas_call(
        functools.partial(
            attn_forward_kernel, tile=tile, class_rows=class_rows, rows=rows, classes=classes
        ),
        grid_spec=grid_spec,
        out_shape=[
            jax.ShapeDtypeStruct((count, cols), bf16),
            jax.ShapeDtypeStruct((count, cols), f32),
            jax.ShapeDtypeStruct((count, PAIRED * 128), f32),
        ],
        compiler_params=pltpu.CompilerParams(vmem_limit_bytes=VMEM_LIMIT),
        cost_estimate=pl.CostEstimate(
            flops=2 * count * PAIRED * length * 2 * HEAD_SIZE,
            bytes_accessed=8 * count * cols + 4 * length * HEAD_SIZE,
            transcendentals=2 * count * PAIRED * length,
        ),
        name="attn_forward",
    )(info, queries, *pairs)


def attn_backward_kernel(info, q_ref, grad_ref, exact_ref, lse_ref, *refs, tile, class_rows, rows, classes):
    kv_refs, dq_ref = refs[:classes], refs[classes]
    dkv_refs, sum_ref = refs[classes + 1 : 2 * classes + 1], refs[2 * classes + 1]

    @pl.when(pl.program_id(0) == 0)
    def _():
        sum_ref[...] = jnp.zeros_like(sum_ref)

    start = pl.program_id(0) * tile
    free, total = group_range(start, tile, class_rows, classes)
    queries = stack_heads(q_ref[...])
    grads = stack_heads(grad_ref[...])
    count = queries.shape[0]
    delta = jnp.sum(grads.astype(f32) * stack_heads(exact_ref[...]), axis=-1, keepdims=True)
    lse = jnp.concatenate([lse_ref[:, j * 128 : j * 128 + 1] for j in range(PAIRED)], axis=0)
    position = tile_positions(tile, count, start, info[0], class_rows, rows)

    def step(group, acc, masked):
        keys = held_block(kv_refs, group, slice(0, HEAD_SIZE))
        values = held_block(kv_refs, group, slice(HEAD_SIZE, 2 * HEAD_SIZE))
        bounded = jnp.tanh(dot(queries, keys, NT) * (1.0 / soft_cap))
        probs = jnp.exp(soft_cap * bounded - lse)
        if masked:
            probs = jnp.where(key_places(group, info[0], classes, rows) <= position, probs, 0.0)
        grad_probs = dot(grads, values, NT)
        grad_raw = (probs * (grad_probs - delta) * (1.0 - bounded * bounded)).astype(bf16)
        sum_ref[group, :, HEAD_SIZE:] += dot(probs.astype(bf16), grads, TN)
        sum_ref[group, :, :HEAD_SIZE] += dot(grad_raw, queries, TN)
        return acc + dot(grad_raw, keys, NN)

    acc = jnp.zeros((count, HEAD_SIZE), f32)
    acc = lax.fori_loop(0, free, functools.partial(step, masked=False), acc)
    acc = lax.fori_loop(free, total, functools.partial(step, masked=True), acc)
    for j in range(PAIRED):
        dq_ref[:, j * HEAD_SIZE : (j + 1) * HEAD_SIZE] = acc[j * tile : (j + 1) * tile].astype(bf16)

    @pl.when(pl.program_id(0) == pl.num_programs(0) - 1)
    def _():
        for h, ref in enumerate(dkv_refs):
            ref[...] = sum_ref[:, h * rows : (h + 1) * rows, :].astype(bf16)


def attn_backward(info, queries, pairs, grads, exact, lse, class_rows, rows):
    count, cols = queries.shape
    classes = len(pairs)
    groups = pairs[0].shape[0]
    length = classes * groups * rows
    tile = min(256, count)
    row_spec = pl.BlockSpec((tile, cols), lambda i, c: (i, 0))
    pair_specs = [pl.BlockSpec(p.shape, lambda i, c: (0, 0, 0)) for p in pairs]
    grid_spec = pltpu.PrefetchScalarGridSpec(
        num_scalar_prefetch=1,
        grid=(count // tile,),
        in_specs=[
            row_spec,
            row_spec,
            row_spec,
            pl.BlockSpec((tile, PAIRED * 128), lambda i, c: (i, 0)),
        ]
        + pair_specs,
        out_specs=[row_spec] + pair_specs,
        scratch_shapes=[pltpu.VMEM((groups, classes * rows, 2 * HEAD_SIZE), f32)],
    )
    return pl.pallas_call(
        functools.partial(
            attn_backward_kernel, tile=tile, class_rows=class_rows, rows=rows, classes=classes
        ),
        grid_spec=grid_spec,
        out_shape=[jax.ShapeDtypeStruct((count, cols), bf16)]
        + [jax.ShapeDtypeStruct(p.shape, bf16) for p in pairs],
        compiler_params=pltpu.CompilerParams(vmem_limit_bytes=VMEM_LIMIT),
        cost_estimate=pl.CostEstimate(
            flops=5 * count * PAIRED * length * 2 * HEAD_SIZE,
            bytes_accessed=10 * count * cols + 8 * length * HEAD_SIZE,
            transcendentals=2 * count * PAIRED * length,
        ),
        name="attn_backward",
    )(info, queries, grads, exact, lse, *pairs)


def per_device(
    tokens,
    cotangent,
    widths,
    attn_codes,
    attn_exps,
    out_exps,
    mlp_codes,
    gate_exps,
    down_exps,
    gain_attn,
    gain_post_attn,
    gain_mlp,
    gain_post_mlp,
):
    wide = lax.axis_size("wide")
    seq_size = lax.axis_size("seq")
    wide_index = lax.axis_index("wide")
    seq_index = lax.axis_index("seq")
    side = seq_index % 2
    is_low = side == 0
    members = seq_size // 2
    member = seq_index // 2
    half_wide = wide // 2
    place = ring_place(wide_index, wide)
    count, rows, model_dim = tokens.shape
    classes = wide // KEY_VALUE_HEADS
    class_rows = rows // classes
    class_index = wide_index % classes
    head_cols = PAIRED * HEAD_SIZE
    proj_cols = attn_exps.shape[0]
    half_proj = proj_cols // 2
    half_out = (attn_codes.shape[1] - proj_cols) // 2
    split_out = half_out // members
    attn_rows = attn_codes.shape[0]
    hidden = mlp_codes.shape[1]
    offsets = ring_offsets(wide)
    order = {o: i for i, o in enumerate(ring_offsets(half_wide))}
    seqs = range(count)
    seq_bits = [1 << i for i in range(seq_size.bit_length() - 1)]
    far_bits = list(reversed(seq_bits[1:]))
    clock = Clock(widths)

    def index_at(offset):
        return ring_index(jnp.mod(place + offset, wide), wide)

    places = jnp.stack([index_at(o) for o in offsets]).astype(jnp.int32)
    info = jnp.concatenate(
        [side[None].astype(jnp.int32), widths, member[None].astype(jnp.int32)]
    )
    class_info = class_index[None].astype(jnp.int32)
    column_scale = inverse_powers(attn_exps)[None, :]
    output_scale = inverse_powers(out_exps)[:, None]

    relative = [0]
    for bit in reversed(seq_bits):
        relative = relative + [r | bit for r in relative]
    pieces = jnp.stack([jnp.bitwise_xor(seq_index, r) for r in relative]).astype(jnp.int32)
    piece_rows = hidden // seq_size
    partner = jnp.bitwise_xor(wide_index, half_wide)
    gate_scale = inverse_powers(gate_exps)
    row_scale = jnp.concatenate(
        [
            lax.dynamic_slice_in_dim(
                gate_scale, block * hidden + pieces[j] * piece_rows, piece_rows, 1
            )
            for group in (range(seq_size // 2), range(seq_size // 2, seq_size))
            for block in (wide_index, partner)
            for j in group
        ],
        axis=1,
    )[:, :, None]
    down_scale = inverse_powers(down_exps)[None, :]

    def columns(first, size):
        return lax.dynamic_slice_in_dim(attn_codes, first, size, 1)

    payload = jnp.concatenate(
        [
            columns(side * half_proj, half_proj),
            columns(proj_cols + side * half_out + member * split_out, split_out),
        ],
        axis=1,
    ).astype(bf16)
    piece_codes = lax.dynamic_slice_in_dim(mlp_codes, seq_index * piece_rows, piece_rows, 1)
    inputs = [tokens[s].astype(f32) for s in seqs]
    cosine, sine = rotary_rows(wide_index * rows + jnp.arange(rows))

    blocks, others = [clock.hold(payload)], []
    proj_weights = []

    def slice_more(first, last):
        return proj_slices(
            blocks[first:last],
            others[first:last],
            places[first:last],
            info,
            column_scale,
            half_proj,
            proj_weights,
            wide,
            count,
        )

    a = b = blocks[0]
    sliced = 0
    steps = half_wide
    for k in range(1, steps + 1):
        if k == steps:
            a, b = halves(a)[0], halves(b)[1]
        passed = [swap(v, "seq", 1) for v in blocks[len(others) :]]
        a, b = hop(a, b, wide)
        work = []
        if k == 1:
            work = own_slices(mlp_codes, pieces, info, row_scale, down_scale, count)
            a, b, *work = clock.sync(a, b, *passed, *work)
            passed, own_weights = work[: len(passed)], work[len(passed) :]
        elif k == 2:
            work = [piece_codes[m].astype(bf16) for m in range(3)]
            for s in seqs:
                factor = norm_factor(clock.hold(inputs[s]))
                work += [factor, (inputs[s] * factor * gain_attn).astype(bf16)]
            a, b, *work = clock.sync(a, b, *passed, *work)
            passed, work = work[: len(passed)], work[len(passed) :]
            sends, work = work[:3], work[3:]
            input_factor, normed = work[0::2], work[1::2]
        else:
            more = len(others)
            work = slice_more(sliced, more) if more > sliced else []
            a, b, *work = clock.sync(a, b, *passed, *work)
            passed, work = work[: len(passed)], work[len(passed) :]
            if work:
                proj_weights, sliced = list(work), more
        others += passed
        blocks += [a, b] if k < steps else [jnp.concatenate([a, b], axis=0)]

    def exchange(m):
        return swap(clock.hold(sends[m]), "wide", half_wide)

    def share(held, bits):
        for bit in bits:
            held = held + [swap(value, "seq", bit) for value in held]
        return held

    def partner_weights(m, held):
        scale = row_scale[m] if m < 2 else down_scale
        return partner_slices(
            held, info, scale, m == 2, own_weights[m * count : (m + 1) * count]
        )

    received = exchange(0)
    others += [swap(clock.hold(v), "seq", 1) for v in blocks[len(others) :]]
    proj_weights = slice_more(sliced, wide)
    query_send, pair_send = [], []
    for s in seqs:
        query, pair = project(normed[s], proj_weights[s], cosine, sine)
        query_send.append(query.reshape(wide, class_rows, head_cols))
        pair_send.append(pair)
    sent = clock.sync(received, *query_send, *pair_send)
    received, sent = sent[0], sent[1:]
    query_send, pair_send = sent[:count], sent[count:]

    def spread(pair):
        held = [pair]
        for _ in range(classes - 1):
            held.append(class_ring(held[-1]))
        return held[1:]

    def two_parts(value):
        cut = value.shape[0] // 2
        return value[:cut], value[cut:]

    attended_send, exact, lse, queries, pairs = [], [], [], [], []

    def attend(s):
        out, full, log_sum = attn_forward(class_info, queries[s], pairs[s], class_rows, rows)
        return [out.reshape(wide, class_rows, head_cols), full, log_sum]

    def keep_attend(work):
        attended_send.append(work[0])
        exact.append(work[1])
        lse.append(work[2])

    pair_first = heads_all_to_all(clock.hold(pair_send[0]))
    own_out = jnp.stack([clock.hold(v)[:, half_proj:] for v in blocks])
    other_out = jnp.stack([clock.hold(v)[:, half_proj:] for v in others])
    pair_first, own_out, other_out = clock.sync(pair_first, own_out, other_out)
    out_own = share([clock.hold(own_out)], far_bits)
    moved = spread(pair_first)
    pair_last, *work = clock.sync(heads_all_to_all(clock.hold(pair_send[1])), *moved)
    pairs.append([pair_first] + work)
    part_a, part_b = two_parts(pair_last)
    query = all_to_all(clock.hold(query_send[0]))
    query, *work = clock.sync(query, *spread(part_a), *out_own)
    moved_a, out_own = work[: classes - 1], work[classes - 1 :]
    queries.append(query.reshape(wide * class_rows, head_cols))
    moved_b = spread(clock.hold(part_b))
    query = all_to_all(clock.hold(query_send[1]))
    out_other = [swap(v, "seq", 1) for v in out_own[1:]]
    gate_held = share([clock.hold(received)], far_bits)
    query, *work = clock.sync(query, *moved_b, *out_other, *attend(0))
    moved_b, work = work[: classes - 1], work[classes - 1 :]
    out_other, work = [other_out] + work[: len(out_other)], work[len(out_other) :]
    keep_attend(work)
    queries.append(query.reshape(wide * class_rows, head_cols))
    pairs.append(
        [pair_last] + [jnp.concatenate([x, y], axis=0) for x, y in zip(moved_a, moved_b)]
    )

    attended, heads_back, branch, middle, normed_mlp = [], [], [], [], []

    def heads_to_rows(values):
        split = values.reshape(KEY_VALUE_HEADS, rows, head_cols)
        return jnp.transpose(split, (1, 0, 2)).reshape(rows, KEY_VALUE_HEADS * head_cols)

    def join(s):
        return join_rows(
            heads_back[s], out_weights[s], tokens[s], gain_post_attn, gain_mlp
        )

    def keep_join(work):
        for held, value in zip((branch, middle, normed_mlp), work):
            held.append(value)

    for s in seqs:
        back = all_to_all(clock.hold(attended_send[s]))
        if s == 0:
            out_weights = out_slices(out_own, out_other, places, info, output_scale, count)
            back, *work = clock.sync(back, *gate_held, *out_weights, *attend(count - 1))
            gate_held, work = work[: len(gate_held)], work[len(gate_held) :]
            out_weights, work = work[:count], work[count:]
            keep_attend(work)
        else:
            gate_held = share(gate_held, seq_bits[:1])
            back, *work = clock.sync(back, *gate_held, *join(s - 1))
            gate_held, work = work[: len(gate_held)], work[len(gate_held) :]
            keep_join(work)
        heads_back.append(back.reshape(KEY_VALUE_HEADS, rows, head_cols))
        attended.append(heads_to_rows(back))

    received = exchange(1)
    gate_weights = partner_weights(0, [clock.hold(v) for v in gate_held])
    received, *work = clock.sync(received, *gate_weights, *join(count - 1))
    gate_weights, work = work[:count], work[count:]
    keep_join(work)

    def blocks_of(part):
        return lambda o: part[order[o] * rows : (order[o] + 1) * rows]

    gathered, gate, up, hidden_rows, mixed, parts = [], [], [], [], [], []

    def open_part(s, part, held=()):
        group = clock.hold(gathered[s])
        return open_forward(group, gate_weights[s], up_weights[s], part, held)

    def keep_open(work):
        gate.append(work[0])
        up.append(work[1])
        hidden_rows.append(work[2])

    def mix(s):
        return dot(clock.hold(hidden_rows[s]), down_weights[s], NN).astype(bf16)

    up_held = share([clock.hold(received)], far_bits)
    received, *up_held = clock.sync(exchange(2), *up_held)

    def beside_first(step):
        nonlocal up_held
        if step == 0:
            up_held = share(up_held, seq_bits[:1])
            return tuple(up_held) + tuple(share([clock.hold(received)], far_bits))
        if step == 1:
            return tuple(partner_weights(1, [clock.hold(v) for v in up_held]))
        return ()

    a = b = clock.hold(normed_mlp[0])
    blocks = [a]
    for k in range(1, half_wide // 2 + 1):
        if k == half_wide // 2:
            a, b = halves(a)[0], halves(b)[1]
        if k == 2:
            down_held = share(down_held, seq_bits[:1])
        work = beside_first(k - 1) + (tuple(down_held) if k == 2 else ())
        a, b = hop(a, b, half_wide)
        a, b, *work = clock.sync(a, b, *work)
        if k == 1:
            up_held, down_held = work[: len(up_held)], work[len(up_held) :]
        elif k == 2:
            up_weights, down_held = work[:count], work[count:]
        blocks += [a, b]
    gathered.append(jnp.concatenate(blocks, axis=0))

    def beside_second(step):
        if step == 0:
            return open_part(0, None)
        if step == 1:
            return partner_weights(2, [clock.hold(v) for v in down_held])
        return ()

    a = b = clock.hold(normed_mlp[1])
    blocks = [a]
    for k in range(1, half_wide // 2 + 1):
        if k == half_wide // 2:
            a, b = halves(a)[0], halves(b)[1]
        work = beside_second(k - 1)
        a, b = hop(a, b, half_wide)
        a, b, *work = clock.sync(a, b, *work)
        if k == 1:
            keep_open(work)
        elif k == 2:
            down_weights = work
        blocks += [a, b]
    gathered.append(jnp.concatenate(blocks, axis=0))
    parts.append(clock.sync(mix(0))[0])

    layer_out, grad_mixed, gain_fourth = [], [], 0.0

    def finish(s):
        nonlocal gain_fourth
        out, grad, gain = finish_rows(*mixed[s], middle[s], cotangent[s], gain_post_mlp)
        layer_out.append(out)
        grad_mixed.append(grad)
        gain_fourth = gain_fourth + gain

    grad_group, grad_gate, grad_up, grad_parts, grad_normed_mlp = [], [], [], [], []

    def back_hidden(s, part, held=()):
        group = clock.hold(grad_group[s])
        return open_back(group, down_weights[s], gate[s], up[s], part, held)

    def back_input(s, part, held=()):
        grad = clock.hold(grad_gate[s])
        return input_back(grad, grad_up[s], gate_weights[s], up_weights[s], part, held)

    def keep_back(work):
        grad_gate.append(work[0])
        grad_up.append(work[1])

    def first_sum(part):
        a, b = hop(*halves(clock.hold(blocks_of(part)(half_wide // 2))), half_wide)
        return a, b

    def rest_sum(part, a, b, beside=lambda step: ()):
        part_of = blocks_of(part)
        other = []
        for k in range(half_wide // 2 - 1, 0, -1):
            if k == half_wide // 2 - 1:
                a = add_first(part_of(k), a)
                b = add_last(part_of(-k), b)
            else:
                a = low_sum(part_of(k), a)
                b = low_sum(part_of(-k), b)
            work = beside(half_wide // 2 - 1 - k)
            a, b = hop(a, b, half_wide)
            a, b, *work = clock.sync(a, b, *work)
            other.append(work)
        return (part, a, b), other

    a, b = first_sum(parts[0])
    a, b, *opened = clock.sync(a, b, *open_part(1, 0))
    total, work = rest_sum(
        parts[0], a, b, lambda step: () if step else tuple(open_part(1, 1, opened))
    )
    keep_open(work[0])
    mixed.append(total)
    finish(0)
    parts.append(mix(1))
    blocks, work = ring_gather(
        clock, grad_mixed[0], half_wide, lambda k: (parts[1],) if k == 0 else ()
    )
    parts[1] = work[0][0]
    grad_group.append(jnp.concatenate(blocks, axis=0))
    a, b = first_sum(parts[1])
    a, b, *opened = clock.sync(a, b, *back_hidden(0, 0))

    def beside_last(step):
        if step:
            return ()
        keep_back(back_hidden(0, 1, opened))
        return (grad_gate[0], grad_up[0], *input_back(
            grad_gate[0], grad_up[0], gate_weights[0], up_weights[0], 0, ()
        ))

    total, work = rest_sum(parts[1], a, b, beside_last)
    grad_gate[0], grad_up[0], opened = work[0][0], work[0][1], work[0][2:]
    mixed.append(total)
    finish(1)
    blocks, work = ring_gather(
        clock, grad_mixed[1], half_wide, lambda k: () if k else tuple(back_input(0, 1, opened))
    )
    grad_parts.append(work[0][0])
    grad_group.append(jnp.concatenate(blocks, axis=0))

    def weight_sum(lefts, rights):
        lefts = [clock.hold(v) for v in lefts]
        return [v.reshape(2, hidden // 2, model_dim) for v in weight_back(lefts, rights)]

    def part_sum(grad, bit):
        split = grad.reshape(2, 2, grad.shape[1] // 2, model_dim)
        return low_sum(split[:, 0], swap(split[:, 1], "seq", bit))

    grad_middle, grad_branch, grad_send = [], [], []
    gain_third = gain_second = 0.0

    def back_branch(s):
        nonlocal gain_third, gain_second
        grad_mid, grad, send, third, second = branch_back(
            *[clock.hold(v) for v in grad_normed_mlp[s]],
            middle[s],
            branch[s],
            cotangent[s],
            gain_mlp,
            gain_post_attn,
            out_weights[s],
        )
        gain_third = gain_third + third
        gain_second = gain_second + second
        return [grad_mid, grad, send.reshape(wide, class_rows, head_cols)]

    def keep_branch(work):
        grad_middle.append(work[0])
        grad_branch.append(work[1])
        grad_send.append(work[2])

    a, b = first_sum(grad_parts[0])
    a, b, *opened = clock.sync(a, b, *back_hidden(1, 0))

    def beside_back(step):
        if step:
            return ()
        keep_back(back_hidden(1, 1, opened))
        return (grad_gate[1], grad_up[1], *input_back(
            grad_gate[1], grad_up[1], gate_weights[1], up_weights[1], 0, ()
        ))

    total, work = rest_sum(grad_parts[0], a, b, beside_back)
    grad_gate[1], grad_up[1], opened = work[0][0], work[0][1], work[0][2:]
    grad_normed_mlp.append(total)
    grad_parts += clock.sync(*back_input(1, 1, opened))
    a, b = first_sum(grad_parts[1])
    a, b, *work = clock.sync(a, b, *back_branch(0))
    keep_branch(work)
    total, work = rest_sum(
        grad_parts[1],
        a,
        b,
        lambda step: () if step else tuple(weight_sum(hidden_rows, grad_group)),
    )
    down_keep, down_send = work[0]
    grad_normed_mlp.append(total)

    def attend_back(s):
        dq, *dkv = attn_backward(
            class_info,
            queries[s],
            pairs[s],
            clock.hold(grad_heads[s]),
            exact[s],
            lse[s],
            class_rows,
            rows,
        )
        return [dq.reshape(wide, class_rows, head_cols)] + dkv

    def class_sum(dkv):
        total = dkv[1 % classes]
        for step in range(2, classes + 1):
            total = low_sum(dkv[step % classes], class_ring(total))
        return total

    def far_parts(grad):
        split = grad.reshape(2, 2, grad.shape[1] // 2, model_dim)
        send = split[:, 1]
        return split[:, 0], [send[:, :, : model_dim // 2], send[:, :, model_dim // 2 :]]

    def far_move(part):
        return swap(clock.hold(part), "seq", seq_bits[1])

    def far_join(kept, moved):
        grad = low_sum(kept, jnp.concatenate(moved, axis=2))
        for bit in seq_bits[2:]:
            grad = part_sum(grad, bit)
        return grad

    grad_heads, grad_attend = [], []
    query_back, pair_back = [], []

    def heads_of(value):
        return value.reshape(wide * class_rows, head_cols)

    back = all_to_all(clock.hold(grad_send[0]))
    down_grad = low_sum(down_keep, swap(down_send, "seq", 1))
    back, down_grad, *work = clock.sync(back, down_grad, *back_branch(1))
    keep_branch(work)
    grad_heads.append(heads_of(back))
    all_normed = jnp.concatenate(normed, axis=0)
    all_attended = jnp.concatenate(attended, axis=0)
    all_branch = jnp.concatenate(grad_branch, axis=0)

    def half_dot(left, right, which, size):
        return dot(left, lax.dynamic_slice_in_dim(right, which * size, size, 1), TN)

    down_keep, down_parts = far_parts(down_grad)
    down_moved = [far_move(down_parts[0])]
    back = all_to_all(clock.hold(grad_send[1]))
    out_send = half_dot(all_branch, clock.hold(all_attended), 1 - side, half_out).astype(bf16)
    back, down_moved[0], out_send, *work = clock.sync(
        back, down_moved[0], out_send, *attend_back(0)
    )
    down_moved.append(far_move(down_parts[1]))
    grad_heads.append(heads_of(back))
    grad_attend.append(work)

    dq, *dkv = grad_attend[0]
    parts_of_pair = [two_parts(v) for v in dkv]
    out_sent = swap(out_send, "seq", 1)
    query = all_to_all(clock.hold(dq))
    pair_a = class_sum([v[0] for v in parts_of_pair])
    if members == 2:
        out_pair = out_product(
            jnp.stack([side, member]).astype(jnp.int32),
            all_branch,
            clock.hold(all_attended),
            out_sent,
        )
    else:
        out_pair = [
            low_sum(half_dot(all_branch, clock.hold(all_attended), side, half_out), out_sent)
        ]
    query, pair_a, down_moved[1], *work = clock.sync(
        query, pair_a, down_moved[1], *out_pair, *attend_back(1)
    )
    out_pair, work = work[: len(out_pair)], work[len(out_pair) :]
    down_grad = far_join(down_keep, down_moved)
    query_back.append(query)
    grad_attend.append(work)
    dq, *dkv = grad_attend[1]
    query = all_to_all(clock.hold(dq))
    pair_b = class_sum([clock.hold(v[1]) for v in parts_of_pair])
    out_moved = []
    if members == 2:
        out_piece = out_pair[0]
        out_parts = [
            clock.hold(out_pair[1])[:, : split_out // 2],
            out_pair[1][:, split_out // 2 :],
        ]
        out_moved.append(swap(out_parts[0], "seq", seq_bits[1]))
    else:
        out_pieces = {
            t: lax.dynamic_slice_in_dim(
                clock.hold(out_pair[0]), jnp.bitwise_xor(member, t) * split_out, split_out, 1
            )
            for t in range(members)
        }
        for bit in seq_bits[1:]:
            for t in sorted(out_pieces):
                if not t & (bit // 2) and t | (bit // 2) in out_pieces:
                    out_pieces[t] = low_sum(
                        out_pieces[t], swap(out_pieces.pop(t | (bit // 2)), "seq", bit)
                    )
        out_piece = out_pieces[0]
    up_keep, up_send = weight_sum(grad_up, gathered)
    query, pair_b, down_grad, up_keep, up_send, *out_moved = clock.sync(
        query, pair_b, down_grad, up_keep, up_send, *out_moved
    )
    query_back.append(query)

    pair = heads_all_to_all(clock.hold(jnp.concatenate([pair_a, pair_b], axis=0)))
    pair_sum = class_sum([clock.hold(v) for v in dkv])
    up_grad = low_sum(up_keep, swap(up_send, "seq", 1))
    if members == 2:
        out_moved.append(swap(clock.hold(out_parts[1]), "seq", seq_bits[1]))
    pair, pair_sum, up_grad, *out_moved = clock.sync(pair, pair_sum, up_grad, *out_moved)
    if out_moved:
        out_piece = low_sum(out_piece, jnp.concatenate(out_moved, axis=1))
    pair_back.append(pair)
    up_keep, up_parts = far_parts(up_grad)
    up_moved = [far_move(up_parts[0])]
    pair = heads_all_to_all(clock.hold(pair_sum))
    gate_keep, gate_send = weight_sum(grad_gate, gathered)
    pair, up_moved[0], gate_keep, gate_send = clock.sync(pair, up_moved[0], gate_keep, gate_send)
    up_moved.append(far_move(up_parts[1]))
    pair_back.append(pair)

    def column_parts(value, count):
        width = value.shape[1] // count
        return [value[:, i * width : (i + 1) * width] for i in range(count)]

    def exchange_grad(part):
        return swap(clock.hold(part), "wide", half_wide)

    down_own = column_parts(down_grad[0], 3)
    down_send = column_parts(down_grad[1], 3)
    gate_moved = swap(gate_send, "seq", 1)
    moved, grad_proj = clock.sync(
        exchange_grad(down_send[0]),
        turn_back(
            [v.reshape(KEY_VALUE_HEADS, rows, head_cols) for v in query_back],
            pair_back,
            cosine,
            sine,
        ),
    )
    down_other = [moved]
    moved = exchange_grad(down_send[1])
    proj_send = half_dot(all_normed, clock.hold(grad_proj), 1 - side, half_proj).astype(bf16)
    moved, gate_moved, up_moved[1], proj_send = clock.sync(
        moved, gate_moved, up_moved[1], proj_send
    )
    down_other.append(moved)
    up_grad = far_join(up_keep, up_moved)
    moved = exchange_grad(down_send[2])
    proj_sent = swap(proj_send, "seq", 1)
    gate_grad = low_sum(gate_keep, gate_moved)
    moved, proj_sent, up_grad, gate_grad = clock.sync(moved, proj_sent, up_grad, gate_grad)
    down_other.append(moved)
    gate_keep, gate_parts = far_parts(gate_grad)
    down_grad = [low_sum(x, y) for x, y in zip(down_own, down_other)]
    proj_part = low_sum(half_dot(all_normed, clock.hold(grad_proj), side, half_proj), proj_sent)
    (proj_part,) = clock.sync(proj_part)
    def part_of(o):
        first = index_at(o) * attn_rows
        return jnp.concatenate(
            [
                lax.dynamic_slice_in_dim(clock.hold(proj_part), first, attn_rows, 0),
                lax.dynamic_slice_in_dim(clock.hold(out_piece), first, attn_rows, 0),
            ],
            axis=1,
        )

    def spread_grad(grads, bits):
        for bit in bits:
            grads = [jnp.concatenate([g, swap(g, "seq", bit)], axis=0) for g in grads]
        return grads

    rows_out = jnp.stack(layer_out)
    a, b = halves(clock.hold(part_of(wide // 2)))
    gate_moved = []
    for k in range(wide // 2 - 1, -1, -1):
        step = wide // 2 - 1 - k
        a, b = hop(a, b, wide)
        work = []
        if step == 0:
            work = [clock.hold(rows_out)]
        elif step in (1, 2):
            work = [far_move(gate_parts[step - 1])]
        elif step == half_wide - 1:
            work = spread_grad([clock.hold(v) for v in down_grad], far_bits)
        a, b, *work = clock.sync(a, b, *work)
        if step == 0:
            rows_out = work[0]
        elif step in (1, 2):
            gate_moved += work
        elif step == half_wide - 1:
            down_grad = work
        if step == 0:
            a, b = add_first(part_of(k), a), add_last(part_of(-k), b)
        elif k > 0:
            a, b = low_sum(part_of(k), a), low_sum(part_of(-k), b)
    total = low_sum(part_of(0), a, b)
    gate_grad = far_join(gate_keep, gate_moved)
    up_own, up_send = column_parts(up_grad[0], 2), column_parts(up_grad[1], 2)
    total, gate_grad, *up_send = clock.sync(total, gate_grad, *up_send)

    def input_grad(s):
        return dot(clock.hold(grad_proj[s * rows : (s + 1) * rows]), proj_weights[s], NT)

    def back_tokens(s, grad_normed):
        grad, gain = norm_back(inputs[s], input_factor[s], gain_attn, grad_normed)
        return (grad_middle[s] + grad).astype(bf16), gain

    def add_swapped(gains, axis, bits):
        for bit in bits:
            gains = gains + swap(gains, axis, bit)
        return gains

    proj_total = total[:, :half_proj]
    out_totals = {0: total[:, half_proj:]}
    for bit in seq_bits[1:]:
        sent = jnp.concatenate([proj_total] + [out_totals[t] for t in sorted(out_totals)], axis=1)
        moved = swap(sent, "seq", bit)
        proj_total = low_sum(proj_total, moved[:, :half_proj])
        for i, t in enumerate(sorted(out_totals)):
            first = half_proj + i * split_out
            out_totals[t | (bit // 2)] = moved[:, first : first + split_out]
    out_totals = jnp.stack([out_totals[t] for t in range(members)])
    low = jnp.concatenate(
        [proj_total]
        + [
            lax.dynamic_index_in_dim(out_totals, jnp.bitwise_xor(member, j), 0, keepdims=False)
            for j in range(members)
        ],
        axis=1,
    )
    moved, grad_first = clock.sync(exchange_grad(up_send[0]), input_grad(0))
    up_grad = [low_sum(up_own[0], moved)]
    moved, low, grad_last = clock.sync(exchange_grad(up_send[1]), low, input_grad(1))
    up_grad.append(low_sum(up_own[1], moved))
    gate_own, gate_send = column_parts(gate_grad[0], 2), column_parts(gate_grad[1], 2)
    first_tokens, gain_first = back_tokens(0, grad_first)
    last_tokens, gain = back_tokens(1, grad_last)
    gains = jnp.concatenate([gain_first + gain, gain_second, gain_third, gain_fourth], axis=0)
    wide_bits = [1 << i for i in range(wide.bit_length() - 1)]
    gains = add_swapped(add_swapped(gains, "wide", wide_bits), "seq", seq_bits)
    gains, *gate_send = clock.sync(gains, *gate_send)
    moved = exchange_grad(gate_send[0])
    up_grad = spread_grad([clock.hold(v) for v in up_grad], far_bits)
    other = swap(clock.hold(low), "seq", 1)
    moved, other, *up_grad = clock.sync(moved, other, *up_grad)
    gate_grad = [low_sum(gate_own[0], moved)]
    moved = exchange_grad(gate_send[1])
    gate_grad = spread_grad([clock.hold(v) for v in gate_grad], far_bits)
    left, right = jnp.where(is_low, low, other), jnp.where(is_low, other, low)
    attn_grad = jnp.concatenate(
        [left[:, :half_proj], right[:, :half_proj], left[:, half_proj:], right[:, half_proj:]],
        axis=1,
    ).astype(f32)
    down_grad = spread_grad([clock.hold(v) for v in down_grad], seq_bits[:1])
    mlp_grad = unpack(down_grad, pieces, 2, [])
    up_grad = spread_grad([clock.hold(v) for v in up_grad], seq_bits[:1])
    tokens_out = jnp.stack([first_tokens, last_tokens])
    parts_up = len(up_grad)
    moved, attn_grad, mlp_grad, tokens_out, *work = clock.sync(
        moved, attn_grad, mlp_grad, tokens_out, *up_grad, *gate_grad
    )
    up_grad, gate_grad = work[:parts_up], work[parts_up:]
    last = spread_grad([low_sum(gate_own[1], moved)], far_bits)
    mlp_grad = unpack(up_grad, pieces, 1, [clock.hold(mlp_grad)])
    gate_grad = spread_grad([clock.hold(v) for v in gate_grad], seq_bits[:1])
    mlp_grad, *gate_grad = clock.sync(mlp_grad, *gate_grad, *last)
    gate_grad[1:] = spread_grad(gate_grad[1:], seq_bits[:1])
    mlp_grad = unpack(gate_grad, pieces, 0, [mlp_grad])
    return (
        rows_out,
        tokens_out,
        attn_grad,
        mlp_grad,
        gains[0],
        gains[1],
        gains[2],
        gains[3],
    )


def solution(mesh):
    placed = (
        P("seq", "wide", None),
        P("seq", "wide", None),
        P("seq"),
        P("wide", None),
        P(),
        P(),
        P(None, "wide", None),
        P(),
        P(),
        P(),
        P(),
        P(),
        P(),
    )
    return jax.shard_map(
        per_device,
        mesh=mesh,
        in_specs=placed,
        out_specs=(
            P("seq", "wide", None),
            P("seq", "wide", None),
            P("wide", None),
            P(None, "wide", None),
            P(),
            P(),
            P(),
            P(),
        ),
        check_vma=False,
    )
```

```python
import functools
import math

import jax
import jax.numpy as jnp
from jax import lax
from jax.experimental import pallas as pl
from jax.experimental.pallas import tpu as pltpu
from jax.sharding import PartitionSpec as P

QUERY_HEADS = 8
KEY_VALUE_HEADS = 4
HEAD_SIZE = 256
PAIRED = QUERY_HEADS // KEY_VALUE_HEADS

eps_norm = 1e-06
soft_cap = 50.0
rope_base = 10000.0
gelu_coeff = math.sqrt(2.0 / math.pi)
f32 = jnp.float32
bf16 = jnp.bfloat16
VMEM_LIMIT = 56 * 1024 * 1024


def dot(a, b, dims):
    return lax.dot_general(a, b, (dims, ((), ())), preferred_element_type=f32)


NN = ((1,), (0,))
NT = ((1,), (1,))
TN = ((0,), (0,))


def inverse_powers(exponents):
    return 1.0 / jnp.left_shift(jnp.ones_like(exponents), exponents).astype(f32)


def norm_factor(values):
    return lax.rsqrt(jnp.mean(values * values, axis=-1, keepdims=True) + eps_norm)


def norm_back(values, factor, gain, grad):
    scaled = grad * gain
    inner = jnp.mean(values * scaled, axis=-1, keepdims=True)
    grad_values = factor * scaled - values * (factor * factor * factor * inner)
    return grad_values, jnp.sum(grad * values * factor, axis=0, keepdims=True)


def gelu_parts(values):
    inner = gelu_coeff * (values + 0.044715 * values * values * values)
    return jnp.tanh(inner)


def rotary_rows(positions):
    half_dim = HEAD_SIZE // 2
    frequency = jnp.exp(
        jnp.arange(half_dim, dtype=f32) * (-2.0 * math.log(rope_base) / HEAD_SIZE)
    )
    angles = positions.astype(f32)[:, None] * frequency[None, :]
    return jnp.cos(angles), jnp.sin(angles)


def ring_place(index, size):
    return jnp.where(index % 2 == 0, index // 2, size - 1 - index // 2)


def ring_index(place, size):
    return jnp.where(place < size // 2, 2 * place, 2 * (size - 1 - place) + 1)


def ring_perms(size):
    order = list(range(0, size, 2)) + list(range(size - 1, 0, -2))
    up = [
        (base + order[i], base + order[(i + 1) % size])
        for base in range(0, lax.axis_size("wide"), size)
        for i in range(size)
    ]
    return up, [(b, a) for a, b in up]


def ring_offsets(size):
    out = [0]
    for k in range(1, size // 2):
        out += [-k, k]
    return out + [size // 2]


class Clock:
    def __init__(self, token):
        self.token = token

    def sync(self, *arrays):
        *arrays, self.token = lax.optimization_barrier(tuple(arrays) + (self.token,))
        return arrays

    def hold(self, value):
        return lax.optimization_barrier((value, self.token))[0]


def hop(a, b, size):
    up, down = ring_perms(size)
    return lax.ppermute(a, "wide", up), lax.ppermute(b, "wide", down)


def low_sum(*terms):
    return sum(t.astype(f32) for t in terms).astype(bf16)


def halves(value):
    half = value.shape[0] // 2
    return value[:half], value[half:]


def add_first(whole, part):
    count = part.shape[0]
    return jnp.concatenate([low_sum(whole[:count], part), whole[count:].astype(bf16)], axis=0)


def add_last(whole, part):
    count = whole.shape[0] - part.shape[0]
    return jnp.concatenate([whole[:count].astype(bf16), low_sum(whole[count:], part)], axis=0)


def ring_gather(clock, value, size, beside=lambda step: ()):
    a = b = clock.hold(value)
    out, other = [a], []
    for k in range(1, size // 2 + 1):
        if k == size // 2:
            a, b = halves(a)[0], halves(b)[1]
        work = beside(k - 1)
        a, b = hop(a, b, size)
        a, b, *work = clock.sync(a, b, *work)
        out += [a, b]
        other.append(work)
    return out, other


def ring_scatter(clock, part_of, rows, size, beside=lambda step: ()):
    a, b = halves(clock.hold(part_of(size // 2).astype(bf16)))
    other = []
    for k in range(size // 2 - 1, -1, -1):
        work = beside(size // 2 - 1 - k)
        a, b = hop(a, b, size)
        a, b, *work = clock.sync(a, b, *work)
        other.append(work)
        if k == size // 2 - 1 and k > 0:
            a = add_first(part_of(k), a)
            b = add_last(part_of(-k), b)
        elif k > 0:
            a = low_sum(part_of(k), a)
            b = low_sum(part_of(-k), b)
    return part_of(0).astype(f32) + a.astype(f32) + b.astype(f32), other


def swap(value, axis, bit):
    size = lax.axis_size(axis)
    return lax.ppermute(value, axis, [(i, i ^ bit) for i in range(size)])


def all_to_all(value):
    return lax.all_to_all(value, "wide", split_axis=0, concat_axis=0, tiled=True)


def heads_all_to_all(value):
    size = lax.axis_size("wide")
    classes = size // KEY_VALUE_HEADS
    groups = [list(range(c, size, classes)) for c in range(classes)]
    return lax.all_to_all(
        value, "wide", split_axis=0, concat_axis=0, axis_index_groups=groups, tiled=True
    )


def class_ring(value):
    size = lax.axis_size("wide")
    classes = size // KEY_VALUE_HEADS
    perm = [(i, i // classes * classes + (i + 1) % classes) for i in range(size)]
    return lax.ppermute(value, "wide", perm)


def slice_values(codes, width):
    lift = jnp.where(width == 0, 0.0, 0.5).astype(bf16)
    large = jnp.where(width == 0, 0.0, jnp.where(width == 1, 1.5 * 2**11, 1.5 * 2**13)).astype(bf16)
    top = jnp.where(width == 0, 127.0, jnp.where(width == 1, 112.0, 64.0)).astype(bf16)
    return jnp.minimum(((codes + lift) + large) - large, top)


def proj_slice_kernel(places, info, *refs, blocks, count):
    code_refs, scale_ref, out_refs = refs[: 2 * blocks], refs[2 * blocks], refs[len(refs) - count :]
    mine = pl.program_id(1) == info[0]

    def write(code_ref):
        codes = code_ref[...]
        scale = scale_ref[...].astype(bf16)
        for s, out_ref in enumerate(out_refs):
            out_ref[...] = slice_values(codes, info[1 + s]) * scale

    for k in range(blocks):
        here = pl.program_id(0) == k
        pl.when(jnp.logical_and(here, mine))(functools.partial(write, code_refs[2 * k]))
        pl.when(jnp.logical_and(here, jnp.logical_not(mine)))(
            functools.partial(write, code_refs[2 * k + 1])
        )


def proj_slices(own, other, places, info, scale, width, weights, total, count):
    blocks = len(own)
    rows = own[0].shape[0]
    inputs = [block for pair in zip(own, other) for block in pair] + [scale]
    grid_spec = pltpu.PrefetchScalarGridSpec(
        num_scalar_prefetch=2,
        grid=(blocks, 2),
        in_specs=[pl.BlockSpec((rows, width), lambda k, j, p, i: (0, 0))] * (2 * blocks)
        + [pl.BlockSpec((1, width), lambda k, j, p, i: (0, j))]
        + [pl.BlockSpec(memory_space=pl.ANY)] * len(weights),
        out_specs=[pl.BlockSpec((rows, width), lambda k, j, p, i: (p[k], j))] * count,
    )
    return pl.pallas_call(
        functools.partial(proj_slice_kernel, blocks=blocks, count=count),
        grid_spec=grid_spec,
        out_shape=[jax.ShapeDtypeStruct((total * rows, 2 * width), bf16)] * count,
        input_output_aliases={2 + len(inputs) + s: s for s in range(len(weights))},
        compiler_params=pltpu.CompilerParams(vmem_limit_bytes=VMEM_LIMIT),
        cost_estimate=pl.CostEstimate(
            flops=20 * count * blocks * rows * width,
            bytes_accessed=4 * blocks * rows * width * (1 + count),
            transcendentals=0,
        ),
        name="proj_slices",
    )(places, info, *inputs, *weights)


def out_slice_kernel(places, info, *refs, split, count):
    inputs, scale_ref, out_refs = refs[: -1 - count], refs[-1 - count], refs[-count:]
    members = len(inputs) // 2
    member = info[1 + count]
    mine = pl.program_id(1) == info[0]

    def write(code_refs):
        scale = scale_ref[...].astype(bf16)
        for t, code_ref in enumerate(code_refs):
            first = pl.multiple_of(jnp.bitwise_xor(member, t) * split, 128)
            for s, out_ref in enumerate(out_refs):
                out_ref[:, pl.ds(first, split)] = slice_values(code_ref[0], info[1 + s]) * scale

    pl.when(mine)(lambda: write(inputs[:members]))
    pl.when(jnp.logical_not(mine))(lambda: write(inputs[members:]))


def out_slices(own, other, places, info, scale, count):
    blocks, rows, split = own[0].shape
    width = split * len(own)
    inputs = list(own) + list(other)
    grid_spec = pltpu.PrefetchScalarGridSpec(
        num_scalar_prefetch=2,
        grid=(blocks, 2),
        in_specs=[pl.BlockSpec((1, rows, split), lambda k, j, p, i: (k, 0, 0))] * len(inputs)
        + [pl.BlockSpec((rows, 1), lambda k, j, p, i: (p[k], 0))],
        out_specs=[pl.BlockSpec((rows, width), lambda k, j, p, i: (p[k], j))] * count,
    )
    return pl.pallas_call(
        functools.partial(out_slice_kernel, split=split, count=count),
        grid_spec=grid_spec,
        out_shape=[jax.ShapeDtypeStruct((blocks * rows, 2 * width), bf16)] * count,
        compiler_params=pltpu.CompilerParams(vmem_limit_bytes=VMEM_LIMIT),
        cost_estimate=pl.CostEstimate(
            flops=20 * count * blocks * rows * width,
            bytes_accessed=4 * blocks * rows * width * (1 + count),
            transcendentals=0,
        ),
        name="out_slices",
    )(places, info, *inputs, scale)


def piece_at(j, steps, block):
    half = steps // 2
    return j + j // half * half + block * half


def own_slice_kernel(pieces, info, code_ref, row_ref, col_ref, *out_refs):
    count = len(out_refs) // 3
    for m in range(3):
        codes = code_ref[m].astype(f32).astype(bf16)
        scale = (row_ref[m] if m < 2 else col_ref[...]).astype(bf16)
        for s in range(count):
            out_refs[m * count + s][...] = slice_values(codes, info[1 + s]) * scale


def own_slices(codes, pieces, info, row_scale, col_scale, count):
    three, rows, cols = codes.shape
    steps = pieces.shape[0]
    piece = rows // steps
    grid_spec = pltpu.PrefetchScalarGridSpec(
        num_scalar_prefetch=2,
        grid=(steps,),
        in_specs=[
            pl.BlockSpec((three, piece, cols), lambda j, p, i: (0, p[j], 0)),
            pl.BlockSpec((2, piece, 1), lambda j, p, i: (0, piece_at(j, steps, 0), 0)),
            pl.BlockSpec((1, cols), lambda j, p, i: (0, 0)),
        ],
        out_specs=[pl.BlockSpec((piece, cols), lambda j, p, i: (piece_at(j, steps, 0), 0))]
        * (three * count),
    )
    return pl.pallas_call(
        own_slice_kernel,
        grid_spec=grid_spec,
        out_shape=[jax.ShapeDtypeStruct((2 * rows, cols), bf16)] * (three * count),
        compiler_params=pltpu.CompilerParams(vmem_limit_bytes=VMEM_LIMIT),
        cost_estimate=pl.CostEstimate(
            flops=10 * count * codes.size,
            bytes_accessed=codes.size * (4 + 2 * count),
            transcendentals=0,
        ),
        name="own_slices",
    )(pieces, info, codes, row_scale, col_scale)


def partner_slice_kernel(info, *refs, steps, count):
    piece_refs, scale_ref, out_refs = refs[:steps], refs[steps], refs[steps + 1 + count :]
    for j in range(steps):

        @pl.when(pl.program_id(0) == j)
        def _():
            codes = piece_refs[j][...]
            scale = scale_ref[...].astype(bf16)
            for s, out_ref in enumerate(out_refs):
                out_ref[...] = slice_values(codes, info[1 + s]) * scale


def partner_slices(pieces, info, scale, by_column, weights):
    steps = len(pieces)
    count = len(weights)
    piece, cols = pieces[0].shape
    if by_column:
        scale_spec = pl.BlockSpec((1, cols), lambda j, i: (0, 0))
    else:
        scale_spec = pl.BlockSpec((piece, 1), lambda j, i: (piece_at(j, steps, 1), 0))
    grid_spec = pltpu.PrefetchScalarGridSpec(
        num_scalar_prefetch=1,
        grid=(steps,),
        in_specs=[pl.BlockSpec((piece, cols), lambda j, i: (0, 0))] * steps
        + [scale_spec]
        + [pl.BlockSpec(memory_space=pl.ANY)] * count,
        out_specs=[pl.BlockSpec((piece, cols), lambda j, i: (piece_at(j, steps, 1), 0))] * count,
    )
    return pl.pallas_call(
        functools.partial(partner_slice_kernel, steps=steps, count=count),
        grid_spec=grid_spec,
        out_shape=[jax.ShapeDtypeStruct(w.shape, bf16) for w in weights],
        input_output_aliases={2 + steps + s: s for s in range(count)},
        compiler_params=pltpu.CompilerParams(vmem_limit_bytes=VMEM_LIMIT),
        cost_estimate=pl.CostEstimate(
            flops=10 * count * steps * piece * cols,
            bytes_accessed=2 * (1 + count) * steps * piece * cols,
            transcendentals=0,
        ),
        name="partner_slices",
    )(info, *pieces, scale, *weights)


def unpack_kernel(pieces, *refs, parts):
    first = 0
    for ref in refs[:parts]:
        width = ref.shape[1]
        refs[-1][0, :, first : first + width] = ref[...].astype(f32)
        first += width


def unpack(grads, pieces, matrix, held):
    steps = pieces.shape[0]
    rows = grads[0].shape[0]
    cols = sum(g.shape[1] for g in grads)
    piece = rows // steps
    grid_spec = pltpu.PrefetchScalarGridSpec(
        num_scalar_prefetch=1,
        grid=(steps,),
        in_specs=[pl.BlockSpec((piece, g.shape[1]), lambda j, p: (j, 0)) for g in grads]
        + [pl.BlockSpec(memory_space=pl.ANY)] * len(held),
        out_specs=pl.BlockSpec((1, piece, cols), lambda j, p: (matrix, p[j], 0)),
    )
    return pl.pallas_call(
        functools.partial(unpack_kernel, parts=len(grads)),
        grid_spec=grid_spec,
        out_shape=jax.ShapeDtypeStruct((3, rows, cols), f32),
        input_output_aliases={1 + len(grads): 0} if held else {},
        compiler_params=pltpu.CompilerParams(vmem_limit_bytes=VMEM_LIMIT),
        cost_estimate=pl.CostEstimate(
            flops=rows * cols, bytes_accessed=6 * rows * cols, transcendentals=0
        ),
        name="unpack",
    )(pieces, *grads, *held)


def tile_of(size):
    return 256 if size % 256 == 0 else size


def tiles_of(size, part):
    tile = tile_of(size)
    tiles = size // tile
    first_part = (tiles + 1) // 2
    if part is None or tiles == 1:
        return tile, 0, tiles
    return (tile, 0, first_part) if part == 0 else (tile, first_part, tiles - first_part)


def whole_spec(shape):
    return pl.BlockSpec(shape, lambda i: (0, 0))


def column_spec(rows, tile, first=0):
    return pl.BlockSpec((rows, tile), lambda i: (0, first + i))


def row_spec(tile, cols, first=0):
    return pl.BlockSpec((tile, cols), lambda i: (first + i, 0))


def kernel_call(kernel, grid, in_specs, out_specs, out_shape, flops, moved, name, held=()):
    inputs = len(in_specs)
    return pl.pallas_call(
        lambda *refs: kernel(*refs[:inputs], *refs[inputs + len(held) :]),
        grid=(grid,),
        in_specs=in_specs + [pl.BlockSpec(memory_space=pl.ANY)] * len(held),
        out_specs=out_specs,
        out_shape=out_shape,
        input_output_aliases={inputs + i: i for i in range(len(held))},
        compiler_params=pltpu.CompilerParams(vmem_limit_bytes=VMEM_LIMIT),
        cost_estimate=pl.CostEstimate(flops=flops, bytes_accessed=moved, transcendentals=0),
        name=name,
    )


def row_parts(rows):
    part = 512 if rows % 512 == 0 else rows
    return [slice(first, first + part) for first in range(0, rows, part)]


def open_kernel(x_ref, wg_ref, wu_ref, gate_ref, up_ref, hidden_ref):
    for part in row_parts(x_ref.shape[0]):
        x = x_ref[part]
        gate = dot(x, wg_ref[...], NT)
        up = dot(x, wu_ref[...], NT)
        gate_ref[part] = gate
        up_ref[part] = up
        hidden_ref[part] = (gate * (0.5 + 0.5 * gelu_parts(gate)) * up).astype(bf16)


def open_forward(x, gate_weights, up_weights, part, held=()):
    rows, depth = x.shape
    hidden = gate_weights.shape[0]
    tile, first, tiles = tiles_of(hidden, part)
    if held and tiles * tile == hidden:
        return list(held)
    return kernel_call(
        open_kernel,
        tiles,
        [whole_spec(x.shape)] + [row_spec(tile, depth, first)] * 2,
        [column_spec(rows, tile, first)] * 3,
        [jax.ShapeDtypeStruct((rows, hidden), t) for t in (f32, f32, bf16)],
        4 * rows * depth * tile * tiles,
        2 * rows * depth + tiles * tile * (4 * depth + 10 * rows),
        "open_forward",
        held,
    )(x, gate_weights, up_weights, *held)


def open_back_kernel(x_ref, wd_ref, gate_ref, up_ref, grad_gate_ref, grad_up_ref):
    for part in row_parts(x_ref.shape[0]):
        grad = dot(x_ref[part], wd_ref[...], NT)
        gate = gate_ref[part]
        square = gate * gate
        bounded = jnp.tanh(gate * (gelu_coeff + (0.044715 * gelu_coeff) * square))
        half = 0.5 + 0.5 * bounded
        steep = (0.5 * gelu_coeff) + (1.5 * 0.044715 * gelu_coeff) * square
        slope = half + gate * (1.0 - bounded * bounded) * steep
        grad_gate_ref[part] = (grad * up_ref[part] * slope).astype(bf16)
        grad_up_ref[part] = (grad * (gate * half)).astype(bf16)


def open_back(x, down_weights, gate, up, part, held=()):
    rows, depth = x.shape
    hidden = down_weights.shape[0]
    tile, first, tiles = tiles_of(hidden, part)
    if held and tiles * tile == hidden:
        return list(held)
    return kernel_call(
        open_back_kernel,
        tiles,
        [whole_spec(x.shape), row_spec(tile, depth, first)] + [column_spec(rows, tile, first)] * 2,
        [column_spec(rows, tile, first)] * 2,
        [jax.ShapeDtypeStruct((rows, hidden), bf16)] * 2,
        2 * rows * depth * tile * tiles,
        2 * rows * depth + tiles * tile * (2 * depth + 12 * rows),
        "open_back",
        held,
    )(x, down_weights, gate, up, *held)


def input_back_kernel(gate_ref, up_ref, wg_ref, wu_ref, out_ref):
    out_ref[...] = (
        dot(gate_ref[...], wg_ref[...], NN) + dot(up_ref[...], wu_ref[...], NN)
    ).astype(bf16)


def input_back(grad_gate, grad_up, gate_weights, up_weights, part, held=()):
    rows, hidden = grad_gate.shape
    depth = gate_weights.shape[1]
    tile, first, tiles = tiles_of(depth, part)
    if held and tiles * tile == depth:
        return list(held)
    return kernel_call(
        input_back_kernel,
        tiles,
        [whole_spec(grad_gate.shape)] * 2 + [column_spec(hidden, tile, first)] * 2,
        [column_spec(rows, tile, first)],
        [jax.ShapeDtypeStruct((rows, depth), bf16)],
        4 * rows * hidden * tile * tiles,
        4 * rows * hidden + tiles * tile * (4 * hidden + 2 * rows),
        "input_back",
        held,
    )(grad_gate, grad_up, gate_weights, up_weights, *held)


def weight_kernel(*refs, count, tiles):
    keep_ref, send_ref = refs[-2:]
    total = dot(refs[0][...], refs[count][...], TN)
    for s in range(1, count):
        total = total + dot(refs[s][...], refs[count + s][...], TN)
    total = total.astype(bf16)
    if tiles == 1:
        half = keep_ref.shape[0]
        keep_ref[...] = total[:half]
        send_ref[...] = total[half:]
        return
    step = pl.program_id(0)

    @pl.when(step < tiles // 2)
    def _():
        keep_ref[...] = total

    @pl.when(step >= tiles // 2)
    def _():
        send_ref[...] = total


def weight_back(lefts, rights):
    count = len(lefts)
    rows, hidden = lefts[0].shape
    depth = rights[0].shape[1]
    tile = 384 if hidden % 768 == 0 else hidden
    tiles = hidden // tile
    half = max(tiles // 2, 1)
    out = (tile if tiles > 1 else hidden // 2, depth)
    return kernel_call(
        functools.partial(weight_kernel, count=count, tiles=tiles),
        tiles,
        [column_spec(rows, tile)] * count + [whole_spec((rows, depth))] * count,
        [
            pl.BlockSpec(out, lambda i: (jnp.minimum(i, half - 1), 0)),
            pl.BlockSpec(out, lambda i: (jnp.maximum(i - half, 0), 0)),
        ],
        [jax.ShapeDtypeStruct((hidden // 2, depth), bf16)] * 2,
        2 * count * rows * depth * hidden,
        2 * count * rows * (hidden + depth) + 2 * hidden * depth,
        "weight_back",
    )(*lefts, *rights)


def fixed_spec(shape):
    return pl.BlockSpec(shape, lambda i: (0,) * len(shape))


def join_kernel(att_ref, w_ref, x_ref, gain_ref, next_ref, branch_ref, mid_ref, normed_ref, sum_ref):
    step = pl.program_id(0)
    heads, _, cols = att_ref.shape
    tile = w_ref.shape[0]
    total = dot(att_ref[0], w_ref[:, :cols], NT)
    for h in range(1, heads):
        total = total + dot(att_ref[h], w_ref[:, h * cols : (h + 1) * cols], NT)
    sum_ref[:, pl.ds(pl.multiple_of(step * tile, 128), tile)] = total

    @pl.when(step == pl.num_programs(0) - 1)
    def _():
        value = sum_ref[...]
        mid = x_ref[...].astype(f32) + value * norm_factor(value) * gain_ref[...]
        branch_ref[...] = value
        mid_ref[...] = mid
        normed_ref[...] = (mid * norm_factor(mid) * next_ref[...]).astype(bf16)


def join_rows(attended, weights, x, gain, next_gain):
    rows, depth = x.shape
    tile = tile_of(depth)
    return pl.pallas_call(
        join_kernel,
        grid=(depth // tile,),
        in_specs=[
            fixed_spec(attended.shape),
            row_spec(tile, weights.shape[1]),
            fixed_spec(x.shape),
            fixed_spec((1, depth)),
            fixed_spec((1, depth)),
        ],
        out_specs=[fixed_spec((rows, depth))] * 3,
        out_shape=[jax.ShapeDtypeStruct((rows, depth), t) for t in (f32, f32, bf16)],
        scratch_shapes=[pltpu.VMEM((rows, depth), f32)],
        compiler_params=pltpu.CompilerParams(vmem_limit_bytes=VMEM_LIMIT),
        cost_estimate=pl.CostEstimate(
            flops=2 * rows * weights.size,
            bytes_accessed=2 * weights.size + 12 * rows * depth,
            transcendentals=0,
        ),
        name="join_rows",
    )(attended, weights, x, gain[None], next_gain[None])


def finish_kernel(part_ref, a_ref, b_ref, mid_ref, cot_ref, gain_ref, out_ref, grad_ref, dg_ref):
    value = part_ref[...].astype(f32) + a_ref[...].astype(f32) + b_ref[...].astype(f32)
    factor = norm_factor(value)
    gain = gain_ref[...]
    out_ref[...] = (mid_ref[...] + value * factor * gain).astype(bf16)
    grad, dg = norm_back(value, factor, gain, cot_ref[...].astype(f32))
    grad_ref[...] = grad.astype(bf16)
    dg_ref[...] = dg


def finish_rows(part, a, b, mid, cotangent, gain):
    rows, depth = mid.shape
    spec = fixed_spec((rows, depth))
    return pl.pallas_call(
        finish_kernel,
        grid=(1,),
        in_specs=[spec] * 5 + [fixed_spec((1, depth))],
        out_specs=[spec, spec, fixed_spec((1, depth))],
        out_shape=[
            jax.ShapeDtypeStruct((rows, depth), bf16),
            jax.ShapeDtypeStruct((rows, depth), bf16),
            jax.ShapeDtypeStruct((1, depth), f32),
        ],
        compiler_params=pltpu.CompilerParams(vmem_limit_bytes=VMEM_LIMIT),
        cost_estimate=pl.CostEstimate(
            flops=20 * rows * depth, bytes_accessed=16 * rows * depth, transcendentals=0
        ),
        name="finish_rows",
    )(part, a, b, mid, cotangent, gain[None])


def branch_back_kernel(
    part_ref,
    a_ref,
    b_ref,
    mid_ref,
    branch_ref,
    cot_ref,
    mlp_gain_ref,
    gain_ref,
    w_ref,
    grad_mid_ref,
    grad_ref,
    send_ref,
    mlp_dg_ref,
    dg_ref,
    held_ref,
):
    @pl.when(pl.program_id(0) == 0)
    def _():
        normed = part_ref[...].astype(f32) + a_ref[...].astype(f32) + b_ref[...].astype(f32)
        mid = mid_ref[...]
        grad, dg = norm_back(mid, norm_factor(mid), mlp_gain_ref[...], normed)
        mlp_dg_ref[...] = dg
        grad_mid = cot_ref[...].astype(f32) + grad
        grad_mid_ref[...] = grad_mid
        branch = branch_ref[...]
        grad, dg = norm_back(branch, norm_factor(branch), gain_ref[...], grad_mid)
        dg_ref[...] = dg
        held_ref[...] = grad.astype(bf16)
        grad_ref[...] = grad.astype(bf16)

    send_ref[0] = dot(held_ref[...], w_ref[...], NN).astype(bf16)


def branch_back(part, a, b, mid, branch, cotangent, mlp_gain, gain, weights):
    rows, depth = mid.shape
    cols = PAIRED * HEAD_SIZE
    spec = fixed_spec((rows, depth))
    line = fixed_spec((1, depth))
    return pl.pallas_call(
        branch_back_kernel,
        grid=(KEY_VALUE_HEADS,),
        in_specs=[spec] * 6 + [line] * 2 + [column_spec(depth, cols)],
        out_specs=[
            spec,
            spec,
            pl.BlockSpec((1, rows, cols), lambda i: (i, 0, 0)),
            line,
            line,
        ],
        out_shape=[
            jax.ShapeDtypeStruct((rows, depth), f32),
            jax.ShapeDtypeStruct((rows, depth), bf16),
            jax.ShapeDtypeStruct((KEY_VALUE_HEADS, rows, cols), bf16),
            jax.ShapeDtypeStruct((1, depth), f32),
            jax.ShapeDtypeStruct((1, depth), f32),
        ],
        scratch_shapes=[pltpu.VMEM((rows, depth), bf16)],
        compiler_params=pltpu.CompilerParams(vmem_limit_bytes=VMEM_LIMIT),
        cost_estimate=pl.CostEstimate(
            flops=2 * rows * weights.size,
            bytes_accessed=2 * weights.size + 22 * rows * depth,
            transcendentals=0,
        ),
        name="branch_back",
    )(part, a, b, mid, branch, cotangent, mlp_gain[None], gain[None], weights)


def turn(values, cosine, sine):
    half = HEAD_SIZE // 2
    out = []
    for j in range(values.shape[1] // HEAD_SIZE):
        a = values[:, j * HEAD_SIZE : j * HEAD_SIZE + half]
        b = values[:, j * HEAD_SIZE + half : (j + 1) * HEAD_SIZE]
        out += [a * cosine - b * sine, b * cosine + a * sine]
    return jnp.concatenate(out, axis=1)


def project_kernel(x_ref, wq_ref, wk_ref, wv_ref, cos_ref, sin_ref, q_ref, kv_ref):
    x = x_ref[...]
    cosine, sine = cos_ref[...], sin_ref[...]
    scale = HEAD_SIZE ** (-0.5)
    q_ref[0] = (turn(dot(x, wq_ref[...], NN), cosine, sine) * scale).astype(bf16)
    kv_ref[0, :, :HEAD_SIZE] = turn(dot(x, wk_ref[...], NN), cosine, sine).astype(bf16)
    kv_ref[0, :, HEAD_SIZE:] = dot(x, wv_ref[...], NN).astype(bf16)


def project(normed, weights, cosine, sine):
    rows, depth = normed.shape
    cols = PAIRED * HEAD_SIZE
    first_key = QUERY_HEADS
    first_value = QUERY_HEADS + KEY_VALUE_HEADS
    whole = lambda shape: pl.BlockSpec(shape, lambda h: (0, 0))
    return pl.pallas_call(
        project_kernel,
        grid=(KEY_VALUE_HEADS,),
        in_specs=[
            whole((rows, depth)),
            pl.BlockSpec((depth, cols), lambda h: (0, h)),
            pl.BlockSpec((depth, HEAD_SIZE), lambda h: (0, first_key + h)),
            pl.BlockSpec((depth, HEAD_SIZE), lambda h: (0, first_value + h)),
            whole(cosine.shape),
            whole(sine.shape),
        ],
        out_specs=[
            pl.BlockSpec((1, rows, cols), lambda h: (h, 0, 0)),
            pl.BlockSpec((1, rows, 2 * HEAD_SIZE), lambda h: (h, 0, 0)),
        ],
        out_shape=[
            jax.ShapeDtypeStruct((KEY_VALUE_HEADS, rows, cols), bf16),
            jax.ShapeDtypeStruct((KEY_VALUE_HEADS, rows, 2 * HEAD_SIZE), bf16),
        ],
        compiler_params=pltpu.CompilerParams(vmem_limit_bytes=VMEM_LIMIT),
        cost_estimate=pl.CostEstimate(
            flops=2 * rows * weights.size, bytes_accessed=2 * weights.size, transcendentals=0
        ),
        name="project",
    )(normed, weights, weights, weights, cosine, sine)


def turn_back_kernel(*refs, count):
    q_refs, kv_refs = refs[:count], refs[count : 2 * count]
    cos_ref, sin_ref, out_ref = refs[2 * count :]
    j = pl.program_id(1)
    scale = HEAD_SIZE ** (-0.5)
    keys = KEY_VALUE_HEADS // PAIRED
    for s in range(count):
        here = pl.program_id(0) == s

        @pl.when(jnp.logical_and(here, j < KEY_VALUE_HEADS))
        def _():
            grad = q_refs[s][0].astype(f32) * scale
            out_ref[...] = turn(grad, cos_ref[...], -sin_ref[...]).astype(bf16)

        @pl.when(jnp.logical_and(here, jnp.logical_and(j >= KEY_VALUE_HEADS, j < KEY_VALUE_HEADS + keys)))
        def _():
            grad = jnp.concatenate([kv_refs[s][i, :, :HEAD_SIZE] for i in range(PAIRED)], axis=1)
            out_ref[...] = turn(grad.astype(f32), cos_ref[...], -sin_ref[...]).astype(bf16)

        @pl.when(jnp.logical_and(here, j >= KEY_VALUE_HEADS + keys))
        def _():
            out_ref[...] = jnp.concatenate(
                [kv_refs[s][i, :, HEAD_SIZE:] for i in range(PAIRED)], axis=1
            )


def turn_back(queries, pairs, cosine, sine):
    count = len(queries)
    heads, rows, cols = queries[0].shape
    keys = heads // PAIRED
    grid = (count, heads + 2 * keys)
    whole = pl.BlockSpec(cosine.shape, lambda s, j: (0, 0))
    return pl.pallas_call(
        functools.partial(turn_back_kernel, count=count),
        grid=grid,
        in_specs=[
            pl.BlockSpec((1, rows, cols), lambda s, j: (jnp.minimum(j, heads - 1), 0, 0))
        ]
        * count
        + [
            pl.BlockSpec(
                (PAIRED, rows, cols), lambda s, j: (jnp.maximum(j - heads, 0) % keys, 0, 0)
            )
        ]
        * count
        + [whole, whole],
        out_specs=pl.BlockSpec((rows, cols), lambda s, j: (s, j)),
        out_shape=jax.ShapeDtypeStruct((count * rows, grid[1] * cols), bf16),
        compiler_params=pltpu.CompilerParams(vmem_limit_bytes=VMEM_LIMIT),
        cost_estimate=pl.CostEstimate(
            flops=4 * count * rows * grid[1] * cols,
            bytes_accessed=4 * count * rows * grid[1] * cols,
            transcendentals=0,
        ),
        name="turn_back",
    )(*queries, *pairs, cosine, sine)


def tile_positions(tile, count, start, class_index, class_rows, rows):
    index = lax.broadcasted_iota(jnp.int32, (count, 1), 0)
    place = start + jnp.bitwise_and(index, tile - 1)
    shift = class_rows.bit_length() - 1
    return (
        jnp.right_shift(place, shift) * rows
        + class_index * class_rows
        + jnp.bitwise_and(place, class_rows - 1)
    )


def stack_heads(block):
    return jnp.concatenate(
        [block[:, j * HEAD_SIZE : (j + 1) * HEAD_SIZE] for j in range(PAIRED)], axis=0
    )


def key_places(group, class_index, classes, rows):
    index = lax.broadcasted_iota(jnp.int32, (1, classes * rows), 1)
    shift = rows.bit_length() - 1
    back = jnp.bitwise_and(class_index - jnp.right_shift(index, shift), classes - 1)
    return (group * classes + back) * rows + jnp.bitwise_and(index, rows - 1)


def held_block(refs, group, cols):
    return jnp.concatenate([ref[group, :, cols] for ref in refs], axis=0)


def group_range(start, tile, class_rows, classes):
    return start // class_rows // classes, (start + tile - 1) // class_rows // classes + 1


def attn_forward_kernel(info, q_ref, *refs, tile, class_rows, rows, classes):
    kv_refs = refs[:classes]
    att_ref, exact_ref, lse_ref = refs[classes:]
    start = pl.program_id(0) * tile
    free, total = group_range(start, tile, class_rows, classes)
    queries = stack_heads(q_ref[...])
    count = queries.shape[0]
    position = tile_positions(tile, count, start, info[0], class_rows, rows)

    def step(group, carry, masked):
        acc, row_sum = carry
        keys = held_block(kv_refs, group, slice(0, HEAD_SIZE))
        values = held_block(kv_refs, group, slice(HEAD_SIZE, 2 * HEAD_SIZE))
        raw = dot(queries, keys, NT)
        weight = jnp.exp(soft_cap * jnp.tanh(raw * (1.0 / soft_cap)))
        if masked:
            weight = jnp.where(
                key_places(group, info[0], classes, rows) <= position, weight, 0.0
            )
        row_sum = row_sum + jnp.sum(weight, axis=-1, keepdims=True)
        acc = acc + dot(weight.astype(bf16), values, NN)
        return acc, row_sum

    carry = (jnp.zeros((count, HEAD_SIZE), f32), jnp.zeros((count, 1), f32))
    carry = lax.fori_loop(0, free, functools.partial(step, masked=False), carry)
    acc, row_sum = lax.fori_loop(free, total, functools.partial(step, masked=True), carry)
    exact = acc / row_sum
    lse = jnp.log(row_sum)
    for j in range(PAIRED):
        cols = slice(j * HEAD_SIZE, (j + 1) * HEAD_SIZE)
        exact_ref[:, cols] = exact[j * tile : (j + 1) * tile]
        att_ref[:, cols] = exact[j * tile : (j + 1) * tile].astype(bf16)
        lse_ref[:, j * 128 : (j + 1) * 128] = jnp.broadcast_to(
            lse[j * tile : (j + 1) * tile], (tile, 128)
        )


def attn_forward(info, queries, pairs, class_rows, rows):
    count, cols = queries.shape
    classes = len(pairs)
    length = classes * pairs[0].shape[0] * rows
    tile = min(256, count)
    grid_spec = pltpu.PrefetchScalarGridSpec(
        num_scalar_prefetch=1,
        grid=(count // tile,),
        in_specs=[pl.BlockSpec((tile, cols), lambda i, c: (i, 0))]
        + [pl.BlockSpec(p.shape, lambda i, c: (0, 0, 0)) for p in pairs],
        out_specs=[
            pl.BlockSpec((tile, cols), lambda i, c: (i, 0)),
            pl.BlockSpec((tile, cols), lambda i, c: (i, 0)),
            pl.BlockSpec((tile, PAIRED * 128), lambda i, c: (i, 0)),
        ],
    )
    return pl.pallas_call(
        functools.partial(
            attn_forward_kernel, tile=tile, class_rows=class_rows, rows=rows, classes=classes
        ),
        grid_spec=grid_spec,
        out_shape=[
            jax.ShapeDtypeStruct((count, cols), bf16),
            jax.ShapeDtypeStruct((count, cols), f32),
            jax.ShapeDtypeStruct((count, PAIRED * 128), f32),
        ],
        compiler_params=pltpu.CompilerParams(vmem_limit_bytes=VMEM_LIMIT),
        cost_estimate=pl.CostEstimate(
            flops=2 * count * PAIRED * length * 2 * HEAD_SIZE,
            bytes_accessed=8 * count * cols + 4 * length * HEAD_SIZE,
            transcendentals=2 * count * PAIRED * length,
        ),
        name="attn_forward",
    )(info, queries, *pairs)


def attn_backward_kernel(info, q_ref, grad_ref, exact_ref, lse_ref, *refs, tile, class_rows, rows, classes):
    kv_refs, dq_ref = refs[:classes], refs[classes]
    dkv_refs, sum_ref = refs[classes + 1 : 2 * classes + 1], refs[2 * classes + 1]

    @pl.when(pl.program_id(0) == 0)
    def _():
        sum_ref[...] = jnp.zeros_like(sum_ref)

    start = pl.program_id(0) * tile
    free, total = group_range(start, tile, class_rows, classes)
    queries = stack_heads(q_ref[...])
    grads = stack_heads(grad_ref[...])
    count = queries.shape[0]
    delta = jnp.sum(grads.astype(f32) * stack_heads(exact_ref[...]), axis=-1, keepdims=True)
    lse = jnp.concatenate([lse_ref[:, j * 128 : j * 128 + 1] for j in range(PAIRED)], axis=0)
    position = tile_positions(tile, count, start, info[0], class_rows, rows)

    def step(group, acc, masked):
        keys = held_block(kv_refs, group, slice(0, HEAD_SIZE))
        values = held_block(kv_refs, group, slice(HEAD_SIZE, 2 * HEAD_SIZE))
        bounded = jnp.tanh(dot(queries, keys, NT) * (1.0 / soft_cap))
        probs = jnp.exp(soft_cap * bounded - lse)
        if masked:
            probs = jnp.where(key_places(group, info[0], classes, rows) <= position, probs, 0.0)
        grad_probs = dot(grads, values, NT)
        grad_raw = (probs * (grad_probs - delta) * (1.0 - bounded * bounded)).astype(bf16)
        sum_ref[group, :, HEAD_SIZE:] += dot(probs.astype(bf16), grads, TN)
        sum_ref[group, :, :HEAD_SIZE] += dot(grad_raw, queries, TN)
        return acc + dot(grad_raw, keys, NN)

    acc = jnp.zeros((count, HEAD_SIZE), f32)
    acc = lax.fori_loop(0, free, functools.partial(step, masked=False), acc)
    acc = lax.fori_loop(free, total, functools.partial(step, masked=True), acc)
    for j in range(PAIRED):
        dq_ref[:, j * HEAD_SIZE : (j + 1) * HEAD_SIZE] = acc[j * tile : (j + 1) * tile].astype(bf16)

    @pl.when(pl.program_id(0) == pl.num_programs(0) - 1)
    def _():
        for h, ref in enumerate(dkv_refs):
            ref[...] = sum_ref[:, h * rows : (h + 1) * rows, :].astype(bf16)


def attn_backward(info, queries, pairs, grads, exact, lse, class_rows, rows):
    count, cols = queries.shape
    classes = len(pairs)
    groups = pairs[0].shape[0]
    length = classes * groups * rows
    tile = min(256, count)
    row_spec = pl.BlockSpec((tile, cols), lambda i, c: (i, 0))
    pair_specs = [pl.BlockSpec(p.shape, lambda i, c: (0, 0, 0)) for p in pairs]
    grid_spec = pltpu.PrefetchScalarGridSpec(
        num_scalar_prefetch=1,
        grid=(count // tile,),
        in_specs=[
            row_spec,
            row_spec,
            row_spec,
            pl.BlockSpec((tile, PAIRED * 128), lambda i, c: (i, 0)),
        ]
        + pair_specs,
        out_specs=[row_spec] + pair_specs,
        scratch_shapes=[pltpu.VMEM((groups, classes * rows, 2 * HEAD_SIZE), f32)],
    )
    return pl.pallas_call(
        functools.partial(
            attn_backward_kernel, tile=tile, class_rows=class_rows, rows=rows, classes=classes
        ),
        grid_spec=grid_spec,
        out_shape=[jax.ShapeDtypeStruct((count, cols), bf16)]
        + [jax.ShapeDtypeStruct(p.shape, bf16) for p in pairs],
        compiler_params=pltpu.CompilerParams(vmem_limit_bytes=VMEM_LIMIT),
        cost_estimate=pl.CostEstimate(
            flops=5 * count * PAIRED * length * 2 * HEAD_SIZE,
            bytes_accessed=10 * count * cols + 8 * length * HEAD_SIZE,
            transcendentals=2 * count * PAIRED * length,
        ),
        name="attn_backward",
    )(info, queries, grads, exact, lse, *pairs)


def per_device(
    tokens,
    cotangent,
    widths,
    attn_codes,
    attn_exps,
    out_exps,
    mlp_codes,
    gate_exps,
    down_exps,
    gain_attn,
    gain_post_attn,
    gain_mlp,
    gain_post_mlp,
):
    wide = lax.axis_size("wide")
    seq_size = lax.axis_size("seq")
    wide_index = lax.axis_index("wide")
    seq_index = lax.axis_index("seq")
    side = seq_index % 2
    is_low = side == 0
    members = seq_size // 2
    member = seq_index // 2
    half_wide = wide // 2
    place = ring_place(wide_index, wide)
    count, rows, model_dim = tokens.shape
    classes = wide // KEY_VALUE_HEADS
    class_rows = rows // classes
    class_index = wide_index % classes
    head_cols = PAIRED * HEAD_SIZE
    proj_cols = attn_exps.shape[0]
    half_proj = proj_cols // 2
    half_out = (attn_codes.shape[1] - proj_cols) // 2
    split_out = half_out // members
    attn_rows = attn_codes.shape[0]
    hidden = mlp_codes.shape[1]
    offsets = ring_offsets(wide)
    order = {o: i for i, o in enumerate(ring_offsets(half_wide))}
    seqs = range(count)
    seq_bits = [1 << i for i in range(seq_size.bit_length() - 1)]
    far_bits = list(reversed(seq_bits[1:]))
    clock = Clock(widths)

    def index_at(offset):
        return ring_index(jnp.mod(place + offset, wide), wide)

    places = jnp.stack([index_at(o) for o in offsets]).astype(jnp.int32)
    info = jnp.concatenate(
        [side[None].astype(jnp.int32), widths, member[None].astype(jnp.int32)]
    )
    class_info = class_index[None].astype(jnp.int32)
    column_scale = inverse_powers(attn_exps)[None, :]
    output_scale = inverse_powers(out_exps)[:, None]

    relative = [0]
    for bit in reversed(seq_bits):
        relative = relative + [r | bit for r in relative]
    pieces = jnp.stack([jnp.bitwise_xor(seq_index, r) for r in relative]).astype(jnp.int32)
    piece_rows = hidden // seq_size
    partner = jnp.bitwise_xor(wide_index, half_wide)
    gate_scale = inverse_powers(gate_exps)
    row_scale = jnp.concatenate(
        [
            lax.dynamic_slice_in_dim(
                gate_scale, block * hidden + pieces[j] * piece_rows, piece_rows, 1
            )
            for group in (range(seq_size // 2), range(seq_size // 2, seq_size))
            for block in (wide_index, partner)
            for j in group
        ],
        axis=1,
    )[:, :, None]
    down_scale = inverse_powers(down_exps)[None, :]

    def columns(first, size):
        return lax.dynamic_slice_in_dim(attn_codes, first, size, 1)

    payload = jnp.concatenate(
        [
            columns(side * half_proj, half_proj),
            columns(proj_cols + side * half_out + member * split_out, split_out),
        ],
        axis=1,
    ).astype(bf16)
    piece_codes = lax.dynamic_slice_in_dim(mlp_codes, seq_index * piece_rows, piece_rows, 1)
    inputs = [tokens[s].astype(f32) for s in seqs]
    cosine, sine = rotary_rows(wide_index * rows + jnp.arange(rows))

    blocks, others = [clock.hold(payload)], []
    proj_weights = []

    def slice_more(first, last):
        return proj_slices(
            blocks[first:last],
            others[first:last],
            places[first:last],
            info,
            column_scale,
            half_proj,
            proj_weights,
            wide,
            count,
        )

    a = b = blocks[0]
    sliced = 0
    steps = half_wide
    for k in range(1, steps + 1):
        if k == steps:
            a, b = halves(a)[0], halves(b)[1]
        passed = [swap(v, "seq", 1) for v in blocks[len(others) :]]
        a, b = hop(a, b, wide)
        work = []
        if k == 1:
            work = own_slices(mlp_codes, pieces, info, row_scale, down_scale, count)
            a, b, *work = clock.sync(a, b, *passed, *work)
            passed, own_weights = work[: len(passed)], work[len(passed) :]
        elif k == 2:
            work = [piece_codes[m].astype(bf16) for m in range(3)]
            for s in seqs:
                factor = norm_factor(clock.hold(inputs[s]))
                work += [factor, (inputs[s] * factor * gain_attn).astype(bf16)]
            a, b, *work = clock.sync(a, b, *passed, *work)
            passed, work = work[: len(passed)], work[len(passed) :]
            sends, work = work[:3], work[3:]
            input_factor, normed = work[0::2], work[1::2]
        else:
            more = len(others)
            work = slice_more(sliced, more) if more > sliced else []
            a, b, *work = clock.sync(a, b, *passed, *work)
            passed, work = work[: len(passed)], work[len(passed) :]
            if work:
                proj_weights, sliced = list(work), more
        others += passed
        blocks += [a, b] if k < steps else [jnp.concatenate([a, b], axis=0)]

    def exchange(m):
        return swap(clock.hold(sends[m]), "wide", half_wide)

    def share(held, bits):
        for bit in bits:
            held = held + [swap(value, "seq", bit) for value in held]
        return held

    def partner_weights(m, held):
        scale = row_scale[m] if m < 2 else down_scale
        return partner_slices(
            held, info, scale, m == 2, own_weights[m * count : (m + 1) * count]
        )

    received = exchange(0)
    others += [swap(clock.hold(v), "seq", 1) for v in blocks[len(others) :]]
    proj_weights = slice_more(sliced, wide)
    query_send, pair_send = [], []
    for s in seqs:
        query, pair = project(normed[s], proj_weights[s], cosine, sine)
        query_send.append(query.reshape(wide, class_rows, head_cols))
        pair_send.append(pair)
    sent = clock.sync(received, *query_send, *pair_send)
    received, sent = sent[0], sent[1:]
    query_send, pair_send = sent[:count], sent[count:]

    def spread(pair):
        held = [pair]
        for _ in range(classes - 1):
            held.append(class_ring(held[-1]))
        return held[1:]

    def two_parts(value):
        cut = value.shape[0] // 2
        return value[:cut], value[cut:]

    attended_send, exact, lse, queries, pairs = [], [], [], [], []

    def attend(s):
        out, full, log_sum = attn_forward(class_info, queries[s], pairs[s], class_rows, rows)
        return [out.reshape(wide, class_rows, head_cols), full, log_sum]

    def keep_attend(work):
        attended_send.append(work[0])
        exact.append(work[1])
        lse.append(work[2])

    pair_first = heads_all_to_all(clock.hold(pair_send[0]))
    own_out = jnp.stack([clock.hold(v)[:, half_proj:] for v in blocks])
    other_out = jnp.stack([clock.hold(v)[:, half_proj:] for v in others])
    pair_first, own_out, other_out = clock.sync(pair_first, own_out, other_out)
    out_own = share([clock.hold(own_out)], far_bits)
    moved = spread(pair_first)
    pair_last, *work = clock.sync(heads_all_to_all(clock.hold(pair_send[1])), *moved)
    pairs.append([pair_first] + work)
    part_a, part_b = two_parts(pair_last)
    query = all_to_all(clock.hold(query_send[0]))
    query, *work = clock.sync(query, *spread(part_a), *out_own)
    moved_a, out_own = work[: classes - 1], work[classes - 1 :]
    queries.append(query.reshape(wide * class_rows, head_cols))
    moved_b = spread(clock.hold(part_b))
    query = all_to_all(clock.hold(query_send[1]))
    out_other = [swap(v, "seq", 1) for v in out_own[1:]]
    gate_held = share([clock.hold(received)], far_bits)
    query, *work = clock.sync(query, *moved_b, *out_other, *attend(0))
    moved_b, work = work[: classes - 1], work[classes - 1 :]
    out_other, work = [other_out] + work[: len(out_other)], work[len(out_other) :]
    keep_attend(work)
    queries.append(query.reshape(wide * class_rows, head_cols))
    pairs.append(
        [pair_last] + [jnp.concatenate([x, y], axis=0) for x, y in zip(moved_a, moved_b)]
    )

    attended, heads_back, branch, middle, normed_mlp = [], [], [], [], []

    def heads_to_rows(values):
        split = values.reshape(KEY_VALUE_HEADS, rows, head_cols)
        return jnp.transpose(split, (1, 0, 2)).reshape(rows, KEY_VALUE_HEADS * head_cols)

    def join(s):
        return join_rows(
            heads_back[s], out_weights[s], tokens[s], gain_post_attn, gain_mlp
        )

    def keep_join(work):
        for held, value in zip((branch, middle, normed_mlp), work):
            held.append(value)

    for s in seqs:
        back = all_to_all(clock.hold(attended_send[s]))
        if s == 0:
            out_weights = out_slices(out_own, out_other, places, info, output_scale, count)
            back, *work = clock.sync(back, *gate_held, *out_weights, *attend(count - 1))
            gate_held, work = work[: len(gate_held)], work[len(gate_held) :]
            out_weights, work = work[:count], work[count:]
            keep_attend(work)
        else:
            gate_held = share(gate_held, seq_bits[:1])
            back, *work = clock.sync(back, *gate_held, *join(s - 1))
            gate_held, work = work[: len(gate_held)], work[len(gate_held) :]
            keep_join(work)
        heads_back.append(back.reshape(KEY_VALUE_HEADS, rows, head_cols))
        attended.append(heads_to_rows(back))

    received = exchange(1)
    gate_weights = partner_weights(0, [clock.hold(v) for v in gate_held])
    received, *work = clock.sync(received, *gate_weights, *join(count - 1))
    gate_weights, work = work[:count], work[count:]
    keep_join(work)

    def blocks_of(part):
        return lambda o: part[order[o] * rows : (order[o] + 1) * rows]

    gathered, gate, up, hidden_rows, mixed, parts = [], [], [], [], [], []

    def open_part(s, part, held=()):
        group = clock.hold(gathered[s])
        return open_forward(group, gate_weights[s], up_weights[s], part, held)

    def keep_open(work):
        gate.append(work[0])
        up.append(work[1])
        hidden_rows.append(work[2])

    def mix(s):
        return dot(clock.hold(hidden_rows[s]), down_weights[s], NN).astype(bf16)

    up_held = share([clock.hold(received)], far_bits)
    received, *up_held = clock.sync(exchange(2), *up_held)

    def beside_first(step):
        nonlocal up_held
        if step == 0:
            up_held = share(up_held, seq_bits[:1])
            return tuple(up_held) + tuple(share([clock.hold(received)], far_bits))
        if step == 1:
            return tuple(partner_weights(1, [clock.hold(v) for v in up_held]))
        return ()

    a = b = clock.hold(normed_mlp[0])
    blocks = [a]
    for k in range(1, half_wide // 2 + 1):
        if k == half_wide // 2:
            a, b = halves(a)[0], halves(b)[1]
        if k == 2:
            down_held = share(down_held, seq_bits[:1])
        work = beside_first(k - 1) + (tuple(down_held) if k == 2 else ())
        a, b = hop(a, b, half_wide)
        a, b, *work = clock.sync(a, b, *work)
        if k == 1:
            up_held, down_held = work[: len(up_held)], work[len(up_held) :]
        elif k == 2:
            up_weights, down_held = work[:count], work[count:]
        blocks += [a, b]
    gathered.append(jnp.concatenate(blocks, axis=0))

    def beside_second(step):
        if step == 0:
            return open_part(0, None)
        if step == 1:
            return partner_weights(2, [clock.hold(v) for v in down_held])
        return ()

    a = b = clock.hold(normed_mlp[1])
    blocks = [a]
    for k in range(1, half_wide // 2 + 1):
        if k == half_wide // 2:
            a, b = halves(a)[0], halves(b)[1]
        work = beside_second(k - 1)
        a, b = hop(a, b, half_wide)
        a, b, *work = clock.sync(a, b, *work)
        if k == 1:
            keep_open(work)
        elif k == 2:
            down_weights = work
        blocks += [a, b]
    gathered.append(jnp.concatenate(blocks, axis=0))
    parts.append(clock.sync(mix(0))[0])

    layer_out, grad_mixed, gain_fourth = [], [], 0.0

    def finish(s):
        nonlocal gain_fourth
        out, grad, gain = finish_rows(*mixed[s], middle[s], cotangent[s], gain_post_mlp)
        layer_out.append(out)
        grad_mixed.append(grad)
        gain_fourth = gain_fourth + gain

    grad_group, grad_gate, grad_up, grad_parts, grad_normed_mlp = [], [], [], [], []

    def back_hidden(s, part, held=()):
        group = clock.hold(grad_group[s])
        return open_back(group, down_weights[s], gate[s], up[s], part, held)

    def back_input(s, part, held=()):
        grad = clock.hold(grad_gate[s])
        return input_back(grad, grad_up[s], gate_weights[s], up_weights[s], part, held)

    def keep_back(work):
        grad_gate.append(work[0])
        grad_up.append(work[1])

    def first_sum(part):
        a, b = hop(*halves(clock.hold(blocks_of(part)(half_wide // 2))), half_wide)
        return a, b

    def rest_sum(part, a, b, beside=lambda step: ()):
        part_of = blocks_of(part)
        other = []
        for k in range(half_wide // 2 - 1, 0, -1):
            if k == half_wide // 2 - 1:
                a = add_first(part_of(k), a)
                b = add_last(part_of(-k), b)
            else:
                a = low_sum(part_of(k), a)
                b = low_sum(part_of(-k), b)
            work = beside(half_wide // 2 - 1 - k)
            a, b = hop(a, b, half_wide)
            a, b, *work = clock.sync(a, b, *work)
            other.append(work)
        return (part, a, b), other

    a, b = first_sum(parts[0])
    a, b, *opened = clock.sync(a, b, *open_part(1, 0))
    total, work = rest_sum(
        parts[0], a, b, lambda step: () if step else tuple(open_part(1, 1, opened))
    )
    keep_open(work[0])
    mixed.append(total)
    finish(0)
    parts.append(mix(1))
    blocks, work = ring_gather(
        clock, grad_mixed[0], half_wide, lambda k: (parts[1],) if k == 0 else ()
    )
    parts[1] = work[0][0]
    grad_group.append(jnp.concatenate(blocks, axis=0))
    a, b = first_sum(parts[1])
    a, b, *opened = clock.sync(a, b, *back_hidden(0, 0))

    def beside_last(step):
        if step:
            return ()
        keep_back(back_hidden(0, 1, opened))
        return (grad_gate[0], grad_up[0], *input_back(
            grad_gate[0], grad_up[0], gate_weights[0], up_weights[0], 0, ()
        ))

    total, work = rest_sum(parts[1], a, b, beside_last)
    grad_gate[0], grad_up[0], opened = work[0][0], work[0][1], work[0][2:]
    mixed.append(total)
    finish(1)
    blocks, work = ring_gather(
        clock, grad_mixed[1], half_wide, lambda k: () if k else tuple(back_input(0, 1, opened))
    )
    grad_parts.append(work[0][0])
    grad_group.append(jnp.concatenate(blocks, axis=0))

    def weight_sum(lefts, rights):
        lefts = [clock.hold(v) for v in lefts]
        return [v.reshape(2, hidden // 2, model_dim) for v in weight_back(lefts, rights)]

    def part_sum(grad, bit):
        split = grad.reshape(2, 2, grad.shape[1] // 2, model_dim)
        return low_sum(split[:, 0], swap(split[:, 1], "seq", bit))

    grad_middle, grad_branch, grad_send = [], [], []
    gain_third = gain_second = 0.0

    def back_branch(s):
        nonlocal gain_third, gain_second
        grad_mid, grad, send, third, second = branch_back(
            *[clock.hold(v) for v in grad_normed_mlp[s]],
            middle[s],
            branch[s],
            cotangent[s],
            gain_mlp,
            gain_post_attn,
            out_weights[s],
        )
        gain_third = gain_third + third
        gain_second = gain_second + second
        return [grad_mid, grad, send.reshape(wide, class_rows, head_cols)]

    def keep_branch(work):
        grad_middle.append(work[0])
        grad_branch.append(work[1])
        grad_send.append(work[2])

    a, b = first_sum(grad_parts[0])
    a, b, *opened = clock.sync(a, b, *back_hidden(1, 0))

    def beside_back(step):
        if step:
            return ()
        keep_back(back_hidden(1, 1, opened))
        return (grad_gate[1], grad_up[1], *input_back(
            grad_gate[1], grad_up[1], gate_weights[1], up_weights[1], 0, ()
        ))

    total, work = rest_sum(grad_parts[0], a, b, beside_back)
    grad_gate[1], grad_up[1], opened = work[0][0], work[0][1], work[0][2:]
    grad_normed_mlp.append(total)
    grad_parts += clock.sync(*back_input(1, 1, opened))
    a, b = first_sum(grad_parts[1])
    a, b, *work = clock.sync(a, b, *back_branch(0))
    keep_branch(work)
    total, work = rest_sum(
        grad_parts[1],
        a,
        b,
        lambda step: () if step else tuple(weight_sum(hidden_rows, grad_group)),
    )
    down_keep, down_send = work[0]
    grad_normed_mlp.append(total)

    def attend_back(s):
        dq, *dkv = attn_backward(
            class_info,
            queries[s],
            pairs[s],
            clock.hold(grad_heads[s]),
            exact[s],
            lse[s],
            class_rows,
            rows,
        )
        return [dq.reshape(wide, class_rows, head_cols)] + dkv

    def class_sum(dkv):
        total = dkv[1 % classes]
        for step in range(2, classes + 1):
            total = low_sum(dkv[step % classes], class_ring(total))
        return total

    def far_parts(grad):
        split = grad.reshape(2, 2, grad.shape[1] // 2, model_dim)
        send = split[:, 1]
        return split[:, 0], [send[:, :, : model_dim // 2], send[:, :, model_dim // 2 :]]

    def far_move(part):
        return swap(clock.hold(part), "seq", seq_bits[1])

    def far_join(kept, moved):
        grad = low_sum(kept, jnp.concatenate(moved, axis=2))
        for bit in seq_bits[2:]:
            grad = part_sum(grad, bit)
        return grad

    grad_heads, grad_attend = [], []
    query_back, pair_back = [], []

    def heads_of(value):
        return value.reshape(wide * class_rows, head_cols)

    back = all_to_all(clock.hold(grad_send[0]))
    down_grad = low_sum(down_keep, swap(down_send, "seq", 1))
    back, down_grad, *work = clock.sync(back, down_grad, *back_branch(1))
    keep_branch(work)
    grad_heads.append(heads_of(back))
    all_normed = jnp.concatenate(normed, axis=0)
    all_attended = jnp.concatenate(attended, axis=0)
    all_branch = jnp.concatenate(grad_branch, axis=0)

    def half_dot(left, right, which, size):
        return dot(left, lax.dynamic_slice_in_dim(right, which * size, size, 1), TN)

    down_keep, down_parts = far_parts(down_grad)
    down_moved = [far_move(down_parts[0])]
    back = all_to_all(clock.hold(grad_send[1]))
    out_send = half_dot(all_branch, clock.hold(all_attended), 1 - side, half_out).astype(bf16)
    back, down_moved[0], out_send, *work = clock.sync(
        back, down_moved[0], out_send, *attend_back(0)
    )
    down_moved.append(far_move(down_parts[1]))
    grad_heads.append(heads_of(back))
    grad_attend.append(work)

    dq, *dkv = grad_attend[0]
    parts_of_pair = [two_parts(v) for v in dkv]
    out_sent = swap(out_send, "seq", 1)
    query = all_to_all(clock.hold(dq))
    pair_a = class_sum([v[0] for v in parts_of_pair])
    out_part = low_sum(
        half_dot(all_branch, clock.hold(all_attended), side, half_out), out_sent
    )
    query, pair_a, down_moved[1], out_part, *work = clock.sync(
        query, pair_a, down_moved[1], out_part, *attend_back(1)
    )
    down_grad = far_join(down_keep, down_moved)
    query_back.append(query)
    grad_attend.append(work)
    dq, *dkv = grad_attend[1]
    query = all_to_all(clock.hold(dq))
    pair_b = class_sum([clock.hold(v[1]) for v in parts_of_pair])
    out_pieces = {
        t: lax.dynamic_slice_in_dim(
            clock.hold(out_part), jnp.bitwise_xor(member, t) * split_out, split_out, 1
        )
        for t in range(members)
    }
    out_moved = []
    if members == 2:
        out_parts = [out_pieces[1][:, : split_out // 2], out_pieces[1][:, split_out // 2 :]]
        out_moved.append(swap(out_parts[0], "seq", seq_bits[1]))
    else:
        for bit in seq_bits[1:]:
            for t in sorted(out_pieces):
                if not t & (bit // 2) and t | (bit // 2) in out_pieces:
                    out_pieces[t] = low_sum(
                        out_pieces[t], swap(out_pieces.pop(t | (bit // 2)), "seq", bit)
                    )
    up_keep, up_send = weight_sum(grad_up, gathered)
    query, pair_b, down_grad, up_keep, up_send, *out_moved = clock.sync(
        query, pair_b, down_grad, up_keep, up_send, *out_moved
    )
    query_back.append(query)

    pair = heads_all_to_all(clock.hold(jnp.concatenate([pair_a, pair_b], axis=0)))
    pair_sum = class_sum([clock.hold(v) for v in dkv])
    up_grad = low_sum(up_keep, swap(up_send, "seq", 1))
    if members == 2:
        out_moved.append(swap(clock.hold(out_parts[1]), "seq", seq_bits[1]))
    pair, pair_sum, up_grad, *out_moved = clock.sync(pair, pair_sum, up_grad, *out_moved)
    out_piece = out_pieces[0]
    if out_moved:
        out_piece = low_sum(out_piece, jnp.concatenate(out_moved, axis=1))
    pair_back.append(pair)
    up_keep, up_parts = far_parts(up_grad)
    up_moved = [far_move(up_parts[0])]
    pair = heads_all_to_all(clock.hold(pair_sum))
    gate_keep, gate_send = weight_sum(grad_gate, gathered)
    pair, up_moved[0], gate_keep, gate_send = clock.sync(pair, up_moved[0], gate_keep, gate_send)
    up_moved.append(far_move(up_parts[1]))
    pair_back.append(pair)

    def column_parts(value, count):
        width = value.shape[1] // count
        return [value[:, i * width : (i + 1) * width] for i in range(count)]

    def exchange_grad(part):
        return swap(clock.hold(part), "wide", half_wide)

    down_own = column_parts(down_grad[0], 3)
    down_send = column_parts(down_grad[1], 3)
    gate_moved = swap(gate_send, "seq", 1)
    moved, grad_proj = clock.sync(
        exchange_grad(down_send[0]),
        turn_back(
            [v.reshape(KEY_VALUE_HEADS, rows, head_cols) for v in query_back],
            pair_back,
            cosine,
            sine,
        ),
    )
    down_other = [moved]
    moved = exchange_grad(down_send[1])
    proj_send = half_dot(all_normed, clock.hold(grad_proj), 1 - side, half_proj).astype(bf16)
    moved, gate_moved, up_moved[1], proj_send = clock.sync(
        moved, gate_moved, up_moved[1], proj_send
    )
    down_other.append(moved)
    up_grad = far_join(up_keep, up_moved)
    moved = exchange_grad(down_send[2])
    proj_sent = swap(proj_send, "seq", 1)
    gate_grad = low_sum(gate_keep, gate_moved)
    moved, proj_sent, up_grad, gate_grad = clock.sync(moved, proj_sent, up_grad, gate_grad)
    down_other.append(moved)
    gate_keep, gate_parts = far_parts(gate_grad)
    down_grad = [low_sum(x, y) for x, y in zip(down_own, down_other)]
    proj_part = low_sum(half_dot(all_normed, clock.hold(grad_proj), side, half_proj), proj_sent)
    (proj_part,) = clock.sync(proj_part)
    def part_of(o):
        first = index_at(o) * attn_rows
        return jnp.concatenate(
            [
                lax.dynamic_slice_in_dim(clock.hold(proj_part), first, attn_rows, 0),
                lax.dynamic_slice_in_dim(clock.hold(out_piece), first, attn_rows, 0),
            ],
            axis=1,
        )

    def spread_grad(grads, bits):
        for bit in bits:
            grads = [jnp.concatenate([g, swap(g, "seq", bit)], axis=0) for g in grads]
        return grads

    rows_out = jnp.stack(layer_out)
    far_down = [swap(clock.hold(v), "seq", far_bits[0]) for v in down_grad]
    a, b = halves(clock.hold(part_of(wide // 2)))
    gate_moved = []
    for k in range(wide // 2 - 1, -1, -1):
        step = wide // 2 - 1 - k
        a, b = hop(a, b, wide)
        work = []
        if step == 0:
            work = far_down
        elif step == 1:
            near_down = [swap(clock.hold(v), "seq", 1) for v in down_grad]
            work = [far_move(gate_parts[0]), *near_down]
        elif step == 2:
            work = [far_move(gate_parts[1]), unpack(down_grad, pieces, 2, [])]
        a, b, *work = clock.sync(a, b, *work)
        if step == 0:
            down_grad = [jnp.concatenate(v, axis=0) for v in zip(down_grad, work)]
            down_grad = spread_grad(down_grad, far_bits[1:])
        elif step == 1:
            gate_moved.append(work[0])
            down_grad = [jnp.concatenate(v, axis=0) for v in zip(down_grad, work[1:])]
        elif step == 2:
            gate_moved.append(work[0])
            mlp_grad = work[1]
        if step == 0:
            a, b = add_first(part_of(k), a), add_last(part_of(-k), b)
        elif k > 0:
            a, b = low_sum(part_of(k), a), low_sum(part_of(-k), b)
    total = low_sum(part_of(0), a, b)
    gate_grad = far_join(gate_keep, gate_moved)
    up_own, up_send = column_parts(up_grad[0], 2), column_parts(up_grad[1], 2)
    total, gate_grad, *up_send = clock.sync(total, gate_grad, *up_send)

    def input_grad(s):
        return dot(clock.hold(grad_proj[s * rows : (s + 1) * rows]), proj_weights[s], NT)

    def back_tokens(s, grad_normed):
        grad, gain = norm_back(inputs[s], input_factor[s], gain_attn, grad_normed)
        return (grad_middle[s] + grad).astype(bf16), gain

    def add_swapped(gains, axis, bits):
        for bit in bits:
            gains = gains + swap(gains, axis, bit)
        return gains

    proj_total = total[:, :half_proj]
    out_totals = {0: total[:, half_proj:]}
    for bit in seq_bits[1:]:
        sent = jnp.concatenate([proj_total] + [out_totals[t] for t in sorted(out_totals)], axis=1)
        moved = swap(sent, "seq", bit)
        proj_total = low_sum(proj_total, moved[:, :half_proj])
        for i, t in enumerate(sorted(out_totals)):
            first = half_proj + i * split_out
            out_totals[t | (bit // 2)] = moved[:, first : first + split_out]
    out_totals = jnp.stack([out_totals[t] for t in range(members)])
    low = jnp.concatenate(
        [proj_total]
        + [
            lax.dynamic_index_in_dim(out_totals, jnp.bitwise_xor(member, j), 0, keepdims=False)
            for j in range(members)
        ],
        axis=1,
    )
    moved, grad_first = clock.sync(exchange_grad(up_send[0]), input_grad(0))
    up_grad = [low_sum(up_own[0], moved)]
    moved, low, grad_last = clock.sync(exchange_grad(up_send[1]), low, input_grad(1))
    up_grad.append(low_sum(up_own[1], moved))
    gate_own, gate_send = column_parts(gate_grad[0], 2), column_parts(gate_grad[1], 2)
    first_tokens, gain_first = back_tokens(0, grad_first)
    last_tokens, gain = back_tokens(1, grad_last)
    gains = jnp.concatenate([gain_first + gain, gain_second, gain_third, gain_fourth], axis=0)
    wide_bits = [1 << i for i in range(wide.bit_length() - 1)]
    gains = add_swapped(add_swapped(gains, "wide", wide_bits), "seq", seq_bits)
    gains, *gate_send = clock.sync(gains, *gate_send)
    moved = exchange_grad(gate_send[0])
    up_grad = spread_grad([clock.hold(v) for v in up_grad], far_bits)
    other = swap(clock.hold(low), "seq", 1)
    moved, other, *up_grad = clock.sync(moved, other, *up_grad)
    gate_grad = [low_sum(gate_own[0], moved)]
    moved = exchange_grad(gate_send[1])
    gate_grad = spread_grad([clock.hold(v) for v in gate_grad], far_bits)
    left, right = jnp.where(is_low, low, other), jnp.where(is_low, other, low)
    attn_grad = jnp.concatenate(
        [left[:, :half_proj], right[:, :half_proj], left[:, half_proj:], right[:, half_proj:]],
        axis=1,
    ).astype(f32)
    up_other = [swap(clock.hold(v), "seq", 1) for v in up_grad]
    parts_up = len(up_other)
    moved, attn_grad, *work = clock.sync(moved, attn_grad, *up_other, *gate_grad)
    up_other, gate_grad = work[:parts_up], work[parts_up:]
    last = spread_grad([low_sum(gate_own[1], moved)], far_bits)
    up_grad = [jnp.concatenate(v, axis=0) for v in zip(up_grad, up_other)]
    mlp_grad = unpack([clock.hold(v) for v in up_grad], pieces, 1, [mlp_grad])
    gate_grad = spread_grad([clock.hold(v) for v in gate_grad], seq_bits[:1])
    mlp_grad, *gate_grad = clock.sync(mlp_grad, *gate_grad, *last)
    gate_grad[1:] = spread_grad(gate_grad[1:], seq_bits[:1])
    mlp_grad = unpack(gate_grad, pieces, 0, [mlp_grad])
    grad_tokens = [first_tokens, last_tokens]
    return (
        rows_out,
        jnp.stack(grad_tokens),
        attn_grad,
        mlp_grad,
        gains[0],
        gains[1],
        gains[2],
        gains[3],
    )


def solution(mesh):
    placed = (
        P("seq", "wide", None),
        P("seq", "wide", None),
        P("seq"),
        P("wide", None),
        P(),
        P(),
        P(None, "wide", None),
        P(),
        P(),
        P(),
        P(),
        P(),
        P(),
    )
    return jax.shard_map(
        per_device,
        mesh=mesh,
        in_specs=placed,
        out_specs=(
            P("seq", "wide", None),
            P("seq", "wide", None),
            P("wide", None),
            P(None, "wide", None),
            P(),
            P(),
            P(),
            P(),
        ),
        check_vma=False,
    )
```
